32 devices in a mesh: wide: 8 (over z, y), narrow: 4 (over x, core).
Axes of the slice: x: 2, y: 2, z: 4, core: 2. Of those that a mesh axis runs over, the one named last changes fastest.
Arguments:
- noised: int32 [8, 1024], P('wide'), may hold values from 0 to 8191, as said below
- clean: int32 [8, 1024], P('wide'), may hold values from 0 to 8191
- timesteps: int32 [8, 1024], P('wide'), may hold values from 1 to 1000
- segments: int32 [8, 1024], P('wide'), may hold values from 0 to 7, never falling along the last dimension, each value on 1 to 512 neighbouring positions
- counted: int32 [8, 1024], P('wide'), may hold values from 0 to 1
- attn_in: float32 [2, 3, 768, 768], P(None, None, 'wide', 'narrow'), may hold values from -0.109375 to 0.109375
- attn_out: float32 [2, 768, 768], P(None, 'wide', 'narrow'), may hold values from -0.875 to 0.875
- ffn_in: float32 [2, 768, 3072], P(None, 'wide', 'narrow'), may hold values from -0.21875 to 0.21875
- ffn_out: float32 [2, 768, 3072], P(None, 'wide', 'narrow'), may hold values from -0.15625 to 0.15625
- tables: float32 [2, 768, 8192], P(None, 'wide', 'narrow')
- gains: float32 [5, 768], P(None, 'wide')
- attn_in_mean: float32 [2, 3, 768, 768], P(None, None, 'wide', 'narrow'), may hold values from -5.9604645e-07 to 5.9604645e-07
- attn_out_mean: float32 [2, 768, 768], P(None, 'wide', 'narrow'), may hold values from -5.9604645e-07 to 5.9604645e-07
- ffn_in_mean: float32 [2, 768, 3072], P(None, 'wide', 'narrow'), may hold values from -5.9604645e-07 to 5.9604645e-07
- ffn_out_mean: float32 [2, 768, 3072], P(None, 'wide', 'narrow'), may hold values from -5.9604645e-07 to 5.9604645e-07
- tables_mean: float32 [2, 768, 8192], P(None, 'wide', 'narrow'), may hold values from -5.9604645e-07 to 5.9604645e-07
- gains_mean: float32 [5, 768], P(None, 'wide'), may hold values from -2.3841858e-06 to 2.3841858e-06
- attn_in_square: float32 [2, 3, 768, 768], P(None, None, 'wide', 'narrow'), may hold values from 9.348406e-16 to 3.7393625e-15
- attn_out_square: float32 [2, 768, 768], P(None, 'wide', 'narrow'), may hold values from 9.348406e-16 to 3.7393625e-15
- ffn_in_square: float32 [2, 768, 3072], P(None, 'wide', 'narrow'), may hold values from 9.348406e-16 to 3.7393625e-15
- ffn_out_square: float32 [2, 768, 3072], P(None, 'wide', 'narrow'), may hold values from 9.348406e-16 to 3.7393625e-15
- tables_square: float32 [2, 768, 8192], P(None, 'wide', 'narrow')
- gains_square: float32 [5, 768], P(None, 'wide'), may hold values from 1.495745e-14 to 5.98298e-14
Outputs:
- loss_sum: float32 [], replicated
- token_total: float32 [], replicated
- grad_norm: float32 [], replicated
- attn_in_next: float32 [2, 3, 768, 768], P(None, None, 'wide', 'narrow')
- attn_in_mean_next: float32 [2, 3, 768, 768], P(None, None, 'wide', 'narrow')
- attn_in_square_next: float32 [2, 3, 768, 768], P(None, None, 'wide', 'narrow')
- attn_in_copy: bfloat16 [2, 3, 768, 768], P(None, None, 'wide', 'narrow')
- attn_out_next: float32 [2, 768, 768], P(None, 'wide', 'narrow')
- attn_out_mean_next: float32 [2, 768, 768], P(None, 'wide', 'narrow')
- attn_out_square_next: float32 [2, 768, 768], P(None, 'wide', 'narrow')
- attn_out_copy: bfloat16 [2, 768, 768], P(None, 'wide', 'narrow')
- ffn_in_next: float32 [2, 768, 3072], P(None, 'wide', 'narrow')
- ffn_in_mean_next: float32 [2, 768, 3072], P(None, 'wide', 'narrow')
- ffn_in_square_next: float32 [2, 768, 3072], P(None, 'wide', 'narrow')
- ffn_in_copy: bfloat16 [2, 768, 3072], P(None, 'wide', 'narrow')
- ffn_out_next: float32 [2, 768, 3072], P(None, 'wide', 'narrow')
- ffn_out_mean_next: float32 [2, 768, 3072], P(None, 'wide', 'narrow')
- ffn_out_square_next: float32 [2, 768, 3072], P(None, 'wide', 'narrow')
- ffn_out_copy: bfloat16 [2, 768, 3072], P(None, 'wide', 'narrow')
- tables_next: float32 [2, 768, 8192], P(None, 'wide', 'narrow')
- tables_mean_next: float32 [2, 768, 8192], P(None, 'wide', 'narrow')
- tables_square_next: float32 [2, 768, 8192], P(None, 'wide', 'narrow')
- tables_copy: bfloat16 [2, 768, 8192], P(None, 'wide', 'narrow')
- gains_next: float32 [5, 768], P(None, 'wide')
- gains_mean_next: float32 [5, 768], P(None, 'wide')
- gains_square_next: float32 [5, 768], P(None, 'wide')
- gains_copy: bfloat16 [5, 768], P(None, 'wide')
The draws below stay inside these ranges and needn't reach their ends.
Inputs may be any that keep to these rules, and one draw needn't show every extreme that they name: noised tokens follow q(x_t | x_0) of the uniform plan: equal to clean with probability (1000 - t)/1000, else a uniform token.
All inputs are finite; a program needn't handle non-finite values.
Results may differ from the reference program's by a relative error of at most 0.004.
The reference program's roundings to bfloat16 on the way count: a program that leaves them out, or rounds other values in their place, can miss the bound.
Values may be sent and summed in bfloat16 or wider, within the bound.
A program may use at most 192 MiB of HBM per device.

```python
import math
import jax
import jax.numpy as jnp
import numpy as np
from jax import lax

D = 768
H = 12
HD = 64
FF = 3072
V = 8192
L = 2
SEQ = 1024
STEPS = 1000
ADAM_STEP = 10
SEQS = 8
PARAMS = 26742528


def draw_token_common(key):
    keys = jax.random.split(key, 5)
    shape = (SEQS, SEQ)
    later = jax.random.randint(keys[0], shape, 2, STEPS + 1)
    first = jax.random.randint(keys[1], shape, 0, 4) == 0
    steps_drawn = jnp.where(first, 1, later)
    steps_drawn = steps_drawn.at[0, SEQ - 1].set(STEPS)
    clean_drawn = jax.random.randint(keys[2], shape, 0, V)
    retained = jax.random.randint(keys[3], shape, 0, STEPS) >= steps_drawn
    noised_drawn = jnp.where(retained, clean_drawn, jax.random.randint(keys[4], shape, 0, V))
    return (noised_drawn.astype(jnp.int32), clean_drawn.astype(jnp.int32), steps_drawn.astype(jnp.int32))


def draw_noised(key, part):
    return draw_token_common(key)[0]


def draw_clean(key, part):
    return draw_token_common(key)[1]


def draw_timesteps(key, part):
    return draw_token_common(key)[2]


def draw_counted(key, part):
    key = jax.random.fold_in(key, 7)
    place = jnp.arange(SEQS, dtype=jnp.int32)[:, None]
    limit = 250 + 500 * place // max(SEQS - 1, 1)
    return (jax.random.randint(key, (SEQS, SEQ), 0, 1000) < limit).astype(jnp.int32)


def draw_tables(key, part):
    key = jax.random.fold_in(key, 11)
    noise = jax.random.normal(key, (2, D, V), jnp.float32)
    column = jnp.arange(V, dtype=jnp.float32) / (V - 1)
    scales = jnp.stack([jnp.ones((V,), jnp.float32), 0.5 * (1.0 + 2.0 * column)])
    return noise * scales[:, None, :] / math.sqrt(D)


def draw_gains(key, part):
    key = jax.random.fold_in(key, 13)
    noise = jax.random.uniform(key, (2 * L + 1, D), jnp.float32, -1.0, 1.0)
    ramp = 1.0 + 2.0 * jnp.arange(D, dtype=jnp.float32) / (D - 1)
    return ramp[None, :] * (1.0 + 0.15 * noise)


def draw_tables_square(key, part):
    key = jax.random.fold_in(key, 17)
    low_end, high_end = (0.001, 0.004)
    exponent = jax.random.uniform(key, (2, D, V), jnp.float32, math.log(low_end), math.log(high_end))
    return jnp.exp(exponent) * (2.5e-05 / PARAMS)


def block_scale(stream_key, shape, cuts, low, largest):
    def one(dim, shards_of):
        draws = jax.random.uniform(jax.random.fold_in(jax.random.fold_in(stream_key, 6), dim), (shards_of,), jnp.float32, low / len(cuts), largest / len(cuts))
        return jnp.repeat(jnp.exp(draws), shape[dim] // shards_of).reshape((-1,) + (1,) * (len(shape) - dim - 1))

    loudness = one(*cuts[0])
    for cut in cuts[1:]:
        loudness = loudness * one(*cut)
    return loudness


def profile(number_of, total, most, slope):
    weights = [(1 << 20) // math.isqrt(grade ** slope) + 1 for grade in range(2, number_of + 1)]
    spare, given = total - most - (number_of - 1), [1] * (number_of - 1)
    while spare > 0:
        movable = [i for i in range(number_of - 1) if given[i] < most]
        whole, remaining = sum([weights[i] for i in movable]), spare
        for i in movable:
            addition = min(most - given[i], max(1, remaining * weights[i] // whole), spare)
            given[i] = given[i] + addition
            spare = spare - addition
    return np.array([most] + given)


def ragged(stream_key, amount, total, most, slope):
    if amount == 2:
        one = jax.random.randint(stream_key, (), max(1, total - most), min(most, total - 1) + 1)
        return jnp.stack([one, total - one])
    tallies = jnp.asarray(profile(amount, total, most, slope), jnp.int32)
    twos = (amount - 1) // 2
    donor, sink = tallies[1:1 + 2 * twos:2], tallies[2:2 + 2 * twos:2]
    room = jnp.minimum(donor - 1, most - sink)
    passed = jax.random.randint(jax.random.fold_in(stream_key, 1), (twos,), 0, 1 << 20) % (room + 1)
    tallies = tallies.at[1:1 + 2 * twos:2].set(donor - passed).at[2:2 + 2 * twos:2].set(sink + passed)
    return tallies[jax.random.permutation(jax.random.fold_in(stream_key, 2), amount)]


def normal_values(rng, dims, width, bound, cuts=(), kind=jnp.bfloat16):
    result = jax.random.normal(rng, dims, jnp.float32) * width
    if len(cuts) > 0:
        result = block_scale(rng, dims, cuts, -0.22, 0.18) * result
    return jnp.clip(result, min=-bound, max=bound).astype(kind)


def setup_inputs(seed: int = 0) -> dict:
    key_list = jax.random.split(jax.random.key(seed), 24)
    return {
        "noised": draw_noised(jax.random.fold_in(key_list[23], 71), 0),
        "clean": draw_clean(jax.random.fold_in(key_list[23], 71), 0),
        "timesteps": draw_timesteps(jax.random.fold_in(key_list[23], 71), 0),
        "segments": jax.vmap(lambda own: jnp.searchsorted(jnp.cumsum(ragged(own, max(SEQ // 128, 3), SEQ, SEQ // 2, 2)), jnp.arange(SEQ), side="right"))(jax.random.split(key_list[3], SEQS)).reshape((SEQS, SEQ)).astype(jnp.int32),
        "counted": draw_counted(jax.random.fold_in(key_list[23], 71), 0),
        "attn_in": normal_values(key_list[5], (L, 3, D, D), (4 * D) ** -0.5, 0.109375, ((2, 8), (3, 4)), jnp.float32),
        "attn_out": normal_values(key_list[6], (L, D, D), (D // 16) ** -0.5, 0.875, ((1, 8), (2, 4)), jnp.float32),
        "ffn_in": normal_values(key_list[7], (L, D, FF), D ** -0.5, 0.21875, ((1, 8), (2, 4)), jnp.float32),
        "ffn_out": normal_values(key_list[8], (L, D, FF), (FF // 2) ** -0.5, 0.15625, ((1, 8), (2, 4)), jnp.float32),
        "tables": draw_tables(jax.random.fold_in(key_list[23], 71), 0),
        "gains": draw_gains(jax.random.fold_in(key_list[23], 71), 0),
        "attn_in_mean": normal_values(key_list[11], (L, 3, D, D), (0.111 * 0.005 / PARAMS ** 0.5), 5.960464477539062e-07, ((2, 8), (3, 4)), jnp.float32),
        "attn_out_mean": normal_values(key_list[12], (L, D, D), (0.111 * 0.005 / PARAMS ** 0.5), 5.960464477539062e-07, ((1, 8), (2, 4)), jnp.float32),
        "ffn_in_mean": normal_values(key_list[13], (L, D, FF), (0.111 * 0.005 / PARAMS ** 0.5), 5.960464477539062e-07, ((1, 8), (2, 4)), jnp.float32),
        "ffn_out_mean": normal_values(key_list[14], (L, D, FF), (0.111 * 0.005 / PARAMS ** 0.5), 5.960464477539062e-07, ((1, 8), (2, 4)), jnp.float32),
        "tables_mean": normal_values(key_list[15], (2, D, V), (0.111 * 0.005 / PARAMS ** 0.5), 5.960464477539062e-07, ((1, 8), (2, 4)), jnp.float32),
        "gains_mean": normal_values(key_list[16], (2 * L + 1, D), (0.444 * 0.005 / PARAMS ** 0.5), 2.384185791015625e-06, ((1, 8),), jnp.float32),
        "attn_in_square": jnp.clip(jnp.exp(math.log(3.7393624709256695e-15) - 1.3862944 * jax.random.uniform(key_list[17], (L, 3, D, D), jnp.float32) ** block_scale(key_list[17], (L, 3, D, D), ((2, 8), (3, 4)), -0.2, 0.2)), 9.348406177314174e-16, 3.7393624709256695e-15),
        "attn_out_square": jnp.clip(jnp.exp(math.log(3.7393624709256695e-15) - 1.3862944 * jax.random.uniform(key_list[18], (L, D, D), jnp.float32) ** block_scale(key_list[18], (L, D, D), ((1, 8), (2, 4)), -0.2, 0.2)), 9.348406177314174e-16, 3.7393624709256695e-15),
        "ffn_in_square": jnp.clip(jnp.exp(math.log(3.7393624709256695e-15) - 1.3862944 * jax.random.uniform(key_list[19], (L, D, FF), jnp.float32) ** block_scale(key_list[19], (L, D, FF), ((1, 8), (2, 4)), -0.2, 0.2)), 9.348406177314174e-16, 3.7393624709256695e-15),
        "ffn_out_square": jnp.clip(jnp.exp(math.log(3.7393624709256695e-15) - 1.3862944 * jax.random.uniform(key_list[20], (L, D, FF), jnp.float32) ** block_scale(key_list[20], (L, D, FF), ((1, 8), (2, 4)), -0.2, 0.2)), 9.348406177314174e-16, 3.7393624709256695e-15),
        "tables_square": draw_tables_square(jax.random.fold_in(key_list[23], 71), 0),
        "gains_square": jnp.clip(jnp.exp(math.log(5.982979953481071e-14) - 1.3862944 * jax.random.uniform(key_list[22], (2 * L + 1, D), jnp.float32) ** block_scale(key_list[22], (2 * L + 1, D), ((1, 8),), -0.2, 0.2)), 1.4957449883702678e-14, 5.982979953481071e-14),
    }


@jax.custom_vjp
def low(v):
    return lax.optimization_barrier(v.astype(jnp.bfloat16)).astype(jnp.float32)

@jax.custom_vjp
def low_back(v):
    return v

def low_keep(v):
    return (low(v), None)

def low_pass(kept, grad):
    return (grad,)

def back_keep(v):
    return (v, None)

def back_low(kept, grad):
    return (low(grad),)
low.defvjp(low_keep, low_pass)
low_back.defvjp(back_keep, back_low)
PRECISE = lax.Precision.HIGHEST
NORM_EPS = 1e-05
LEARN_RATE = 0.05
GAIN_RATE = 0.75
FIRST_DECAY = 0.9
SECOND_DECAY = 0.999
ADAM_EPS = 1e-08
WEIGHT_DECAY = 0.01
CLIP_NORM = 0.005

def both_ways(value):
    return low(low_back(value))

def rms_norm(value, gain):
    return value * lax.rsqrt(lax.optimization_barrier(jnp.mean(value * value, axis=-1, keepdims=True)) + NORM_EPS) * gain

def time_features(timestep_row):
    half_width = D // 2
    rates = jnp.exp(-math.log(10000.0) * jnp.arange(half_width, dtype=jnp.float32) / half_width)
    angles = timestep_row.astype(jnp.float32)[:, None] * rates[None, :]
    return jnp.concatenate([jnp.sin(angles), jnp.cos(angles)], axis=1)

def block(residual, segment, query_w, output_w, expand_w, reduce_w, gain_attn, gain_ffn):
    length = residual.shape[0]
    normed = low(rms_norm(residual, gain_attn))
    projected = both_ways(jnp.einsum('sd,cde->cse', normed, query_w, precision=PRECISE))
    queries, key_rows, values = [projected[which].reshape(length, H, HD) for which in range(3)]
    scores = low_back(jnp.einsum('qhd,khd->hqk', queries, key_rows, precision=PRECISE) * HD ** (-0.5))
    same_doc = (segment[:, None] == segment[None, :])[None]
    weights = low(jax.nn.softmax(jnp.where(same_doc, scores, -1e+30), axis=-1))
    mixed = both_ways(jnp.einsum('hqk,khd->qhd', weights, values, precision=PRECISE)).reshape(length, D)
    residual = residual + low_back(jnp.einsum('se,de->sd', mixed, output_w, precision=PRECISE))
    normed = low(rms_norm(residual, gain_ffn))
    before = low_back(jnp.dot(normed, expand_w, precision=PRECISE))
    after = low(jax.nn.gelu(before))
    return residual + low_back(jnp.einsum('sf,df->sd', after, reduce_w, precision=PRECISE))

def token_losses(logits, noised_row, clean_row, step_row):
    row_top = lax.optimization_barrier(jnp.max(logits, axis=1, keepdims=True))
    log_probs = logits - row_top - jnp.log(lax.optimization_barrier(jnp.sum(jnp.exp(logits - row_top), axis=1, keepdims=True)))
    probs = jnp.exp(log_probs)
    clamped = jnp.maximum(step_row, 2).astype(jnp.float32)[:, None]
    beta = 1.0 / (STEPS - clamped + 1.0)
    retain = (STEPS - clamped + 1.0) / STEPS
    spread = (clamped - 1.0) / (STEPS * V)
    vocab_ids = jnp.arange(V, dtype=jnp.int32)[None, :]
    at_noised = (vocab_ids == noised_row[:, None]).astype(jnp.float32)
    at_clean = (vocab_ids == clean_row[:, None]).astype(jnp.float32)
    forward_fac = beta / V + (1.0 - beta) * at_noised
    backward_fac = retain * at_clean + spread
    joint = forward_fac * backward_fac
    marginal = retain * probs + spread
    joint_total = lax.optimization_barrier(jnp.sum(joint, axis=1))
    cross = lax.optimization_barrier(jnp.sum(joint * (jnp.log(backward_fac) - jnp.log(marginal)), axis=1))
    model_total = lax.optimization_barrier(jnp.sum(forward_fac * marginal, axis=1))
    divergence = cross / joint_total - jnp.log(joint_total) + jnp.log(model_total)
    recon = -lax.optimization_barrier(jnp.sum(at_clean * log_probs, axis=1))
    return jnp.where(step_row == 1, recon, divergence)

def objective(attn_in, attn_out, ffn_in, ffn_out, tables, gains, noised, clean, timesteps, segments, counted, token_total):
    query_w, output_w, expand_w, reduce_w, table_w, gain_w = [low(weight) for weight in (attn_in, attn_out, ffn_in, ffn_out, tables, gains)]

    def one_sequence(running, entry):
        noised_row, clean_row, step_row, segment, count_row = entry
        residual = math.sqrt(D) * low_back(table_w[0][:, noised_row].T) + time_features(step_row)
        for layer_index in range(L):
            residual = block(residual, segment, query_w[layer_index], output_w[layer_index], expand_w[layer_index], reduce_w[layer_index], gain_w[2 * layer_index], gain_w[2 * layer_index + 1])
        normed = low(rms_norm(residual, gain_w[2 * L]))
        logits = low_back(jnp.dot(normed, table_w[1], precision=PRECISE))
        losses = token_losses(logits, noised_row, clean_row, step_row)
        return (running + jnp.sum(losses * count_row.astype(jnp.float32)), None)
    loss_sum, _ = lax.scan(jax.checkpoint(one_sequence), jnp.zeros((), jnp.float32), (noised, clean, timesteps, segments, counted))
    return (loss_sum / token_total, loss_sum)

def adam(weight, grad, first, second, decay, rate):
    first_new = FIRST_DECAY * first + (1.0 - FIRST_DECAY) * grad
    second_new = SECOND_DECAY * second + (1.0 - SECOND_DECAY) * grad * grad
    first_hat = first_new / (1.0 - FIRST_DECAY ** ADAM_STEP)
    second_hat = second_new / (1.0 - SECOND_DECAY ** ADAM_STEP)
    weight_new = weight - rate * (first_hat / (jnp.sqrt(second_hat) + ADAM_EPS) + decay * weight)
    return (weight_new, first_new, second_new, weight_new.astype(jnp.bfloat16))

def reference(noised, clean, timesteps, segments, counted, attn_in, attn_out, ffn_in, ffn_out, tables, gains, attn_in_mean, attn_out_mean, ffn_in_mean, ffn_out_mean, tables_mean, gains_mean, attn_in_square, attn_out_square, ffn_in_square, ffn_out_square, tables_square, gains_square):
    token_total = jnp.sum(counted.astype(jnp.float32))

    def loss_of(*params):
        return objective(*params, noised, clean, timesteps, segments, counted, token_total)
    _, pull_back, loss_sum = jax.vjp(loss_of, attn_in, attn_out, ffn_in, ffn_out, tables, gains, has_aux=True)
    grads = pull_back(jnp.ones((), jnp.float32))
    grad_norm = jnp.sqrt(sum((jnp.sum(grad * grad) for grad in grads)))
    factor = jnp.minimum(1.0, CLIP_NORM / (grad_norm + 1e-06))
    attn_in_next, attn_in_mean_next, attn_in_square_next, attn_in_copy = adam(attn_in, factor * grads[0], attn_in_mean, attn_in_square, WEIGHT_DECAY, LEARN_RATE)
    attn_out_next, attn_out_mean_next, attn_out_square_next, attn_out_copy = adam(attn_out, factor * grads[1], attn_out_mean, attn_out_square, WEIGHT_DECAY, LEARN_RATE)
    ffn_in_next, ffn_in_mean_next, ffn_in_square_next, ffn_in_copy = adam(ffn_in, factor * grads[2], ffn_in_mean, ffn_in_square, WEIGHT_DECAY, LEARN_RATE)
    ffn_out_next, ffn_out_mean_next, ffn_out_square_next, ffn_out_copy = adam(ffn_out, factor * grads[3], ffn_out_mean, ffn_out_square, WEIGHT_DECAY, LEARN_RATE)
    tables_next, tables_mean_next, tables_square_next, tables_copy = adam(tables, factor * grads[4], tables_mean, tables_square, WEIGHT_DECAY, LEARN_RATE)
    gains_next, gains_mean_next, gains_square_next, gains_copy = adam(gains, factor * grads[5], gains_mean, gains_square, 0.0, GAIN_RATE)
    return (loss_sum, token_total, grad_norm, attn_in_next, attn_in_mean_next, attn_in_square_next, attn_in_copy, attn_out_next, attn_out_mean_next, attn_out_square_next, attn_out_copy, ffn_in_next, ffn_in_mean_next, ffn_in_square_next, ffn_in_copy, ffn_out_next, ffn_out_mean_next, ffn_out_square_next, ffn_out_copy, tables_next, tables_mean_next, tables_square_next, tables_copy, gains_next, gains_mean_next, gains_square_next, gains_copy)
```

```python
import functools
import math

import jax
import jax.numpy as jnp
from jax import lax
from jax.experimental import pallas as pl
from jax.experimental.pallas import tpu as pltpu
from jax.sharding import PartitionSpec as P

D = 768
HD = 64
V = 8192
STEPS = 1000
ADAM_STEP = 10


NORM_EPS = 1e-05
LEARN_RATE = 0.05
GAIN_RATE = 0.75
FIRST_DECAY = 0.9
SECOND_DECAY = 0.999
ADAM_EPS = 1e-08
WEIGHT_DECAY = 0.01
CLIP_NORM = 0.005


def add_heads(partial_value):
    return lax.psum(partial_value, "narrow")


def back_heads(partial_value):
    return lax.psum(partial_value, "narrow")


def rms_forward(value, gain):
    scale_row = lax.rsqrt(jnp.mean(value * value, axis=-1, keepdims=True) + NORM_EPS)
    return (value * scale_row * gain, scale_row)


def rms_backward(grad, value, scale_row, gain):
    unit = value * scale_row
    scaled = grad * gain
    back = scale_row * (scaled - unit * jnp.mean(scaled * unit, axis=-1, keepdims=True))
    return (back, jnp.sum(grad * unit, axis=0))


def time_features(timestep_row):
    half_width = D // 2
    rates = jnp.exp(-math.log(10000.0) * jnp.arange(half_width, dtype=jnp.float32) / half_width)
    angles = timestep_row.astype(jnp.float32)[:, None] * rates[None, :]
    return jnp.concatenate([jnp.sin(angles), jnp.cos(angles)], axis=1)


def masked_scores(queries, key_rows, segment):
    scores = jnp.einsum(
        "qhd,khd->hqk", queries, key_rows, preferred_element_type=jnp.float32
    ) * HD ** (-0.5)
    return jnp.where((segment[:, None] == segment[None, :])[None], scores, -1e30)


def attend(entry):
    queries, key_rows, values, segment = entry
    scores = masked_scores(queries, key_rows, segment)
    row_top = jnp.max(scores, axis=-1, keepdims=True)
    log_total = row_top + jnp.log(jnp.sum(jnp.exp(scores - row_top), axis=-1, keepdims=True))
    probs = jnp.exp(scores - log_total).astype(jnp.bfloat16)
    mixed = jnp.einsum("hqk,khd->qhd", probs, values, preferred_element_type=jnp.float32)
    return (mixed.astype(jnp.bfloat16), log_total)


def attend_back(entry):
    queries, key_rows, values, segment, log_total, grad_mixed = entry
    probs = jnp.exp(masked_scores(queries, key_rows, segment) - log_total)
    grad_probs = jnp.einsum("qhd,khd->hqk", grad_mixed, values, preferred_element_type=jnp.float32)
    grad_scores = (
        probs * (grad_probs - jnp.sum(probs * grad_probs, axis=-1, keepdims=True))
    ).astype(jnp.bfloat16)
    grad_query = jnp.einsum(
        "hqk,khd->qhd", grad_scores, key_rows, preferred_element_type=jnp.float32
    ) * HD ** (-0.5)
    grad_key = jnp.einsum(
        "hqk,qhd->khd", grad_scores, queries, preferred_element_type=jnp.float32
    ) * HD ** (-0.5)
    grad_value = jnp.einsum(
        "hqk,qhd->khd", probs.astype(jnp.bfloat16), grad_mixed, preferred_element_type=jnp.float32
    )
    return (grad_query, grad_key, grad_value)


def layer_forward(residual, segments, query_w, output_w, expand_w, reduce_w, gain_attn, gain_ffn):
    seq_count, seq_len = segments.shape
    normed, scale_one = rms_forward(residual, gain_attn)
    normed = normed.astype(jnp.bfloat16)
    projected = jnp.einsum(
        "sd,cde->cse", normed, query_w, preferred_element_type=jnp.float32
    ).astype(jnp.bfloat16)
    heads = projected.reshape(3, seq_count, seq_len, -1, HD)
    mixed, log_total = lax.map(attend, (heads[0], heads[1], heads[2], segments))
    mixed = mixed.reshape(seq_count * seq_len, -1)
    middle = residual + add_heads(
        jnp.einsum("se,de->sd", mixed, output_w, preferred_element_type=jnp.float32)
    )
    normed_two, scale_two = rms_forward(middle, gain_ffn)
    normed_two = normed_two.astype(jnp.bfloat16)
    before = jnp.dot(normed_two, expand_w, preferred_element_type=jnp.float32)
    after = jax.nn.gelu(before).astype(jnp.bfloat16)
    result = middle + add_heads(
        jnp.einsum("sf,df->sd", after, reduce_w, preferred_element_type=jnp.float32)
    )
    return (
        result,
        (
            residual,
            scale_one,
            normed,
            projected,
            log_total,
            mixed,
            middle,
            scale_two,
            normed_two,
            before,
            after,
        ),
    )


def layer_backward(
    grad, kept, segments, query_w, output_w, expand_w, reduce_w, gain_attn, gain_ffn
):
    (
        residual,
        scale_one,
        normed,
        projected,
        log_total,
        mixed,
        middle,
        scale_two,
        normed_two,
        before,
        after,
    ) = kept
    seq_count, seq_len = segments.shape
    grad_branch = grad.astype(jnp.bfloat16)
    grad_after = jnp.dot(grad_branch, reduce_w, preferred_element_type=jnp.float32)
    grad_reduce = jnp.einsum("sd,sf->df", grad_branch, after, preferred_element_type=jnp.float32)
    _, gelu_pull = jax.vjp(jax.nn.gelu, before)
    grad_before = gelu_pull(grad_after)[0].astype(jnp.bfloat16)
    grad_expand = jnp.einsum(
        "sd,sf->df", normed_two, grad_before, preferred_element_type=jnp.float32
    )
    grad_normed_two = back_heads(
        jnp.einsum("sf,df->sd", grad_before, expand_w, preferred_element_type=jnp.float32)
    )
    grad_middle, grad_gain_ffn = rms_backward(grad_normed_two, middle, scale_two, gain_ffn)
    grad_middle = grad_middle + grad
    grad_attn = grad_middle.astype(jnp.bfloat16)
    grad_mixed = jnp.dot(grad_attn, output_w, preferred_element_type=jnp.float32).astype(
        jnp.bfloat16
    )
    grad_output = jnp.einsum("sd,se->de", grad_attn, mixed, preferred_element_type=jnp.float32)
    heads = projected.reshape(3, seq_count, seq_len, -1, HD)
    grad_query, grad_key, grad_value = lax.map(
        attend_back,
        (
            heads[0],
            heads[1],
            heads[2],
            segments,
            log_total,
            grad_mixed.reshape(seq_count, seq_len, -1, HD),
        ),
    )
    grad_projected = (
        jnp.stack([grad_query, grad_key, grad_value])
        .reshape(3, seq_count * seq_len, -1)
        .astype(jnp.bfloat16)
    )
    grad_query_w = jnp.einsum(
        "sd,cse->cde", normed, grad_projected, preferred_element_type=jnp.float32
    )
    grad_normed = back_heads(
        jnp.einsum("cse,cde->sd", grad_projected, query_w, preferred_element_type=jnp.float32)
    )
    grad_input, grad_gain_attn = rms_backward(grad_normed, residual, scale_one, gain_attn)
    return (
        grad_input + grad_middle,
        (
            grad_query_w,
            grad_output,
            grad_expand,
            grad_reduce,
            jnp.stack([grad_gain_attn, grad_gain_ffn]),
        ),
    )


def adam(weight, grad, first, second, decay, rate):
    first_new = FIRST_DECAY * first + (1.0 - FIRST_DECAY) * grad
    second_new = SECOND_DECAY * second + (1.0 - SECOND_DECAY) * grad * grad
    first_hat = first_new / (1.0 - FIRST_DECAY**ADAM_STEP)
    second_hat = second_new / (1.0 - SECOND_DECAY**ADAM_STEP)
    weight_new = weight - rate * (first_hat / (jnp.sqrt(second_hat) + ADAM_EPS) + decay * weight)
    return (weight_new, first_new, second_new, weight_new.astype(jnp.bfloat16))


def general_device(
    noised,
    clean,
    timesteps,
    segments,
    counted,
    attn_in,
    attn_out,
    ffn_in,
    ffn_out,
    tables,
    gains,
    attn_in_mean,
    attn_out_mean,
    ffn_in_mean,
    ffn_out_mean,
    tables_mean,
    gains_mean,
    attn_in_square,
    attn_out_square,
    ffn_in_square,
    ffn_out_square,
    tables_square,
    gains_square,
):
    layers = attn_in.shape[0]
    mask = counted.reshape(-1).astype(jnp.float32)
    token_total = lax.psum(jnp.sum(mask), "wide")
    query_w, output_w, expand_w, reduce_w, table_w, gain_low = (
        lax.all_gather(attn_in.astype(jnp.bfloat16), "wide", axis=2, tiled=True),
        lax.all_gather(attn_out.astype(jnp.bfloat16), "wide", axis=1, tiled=True),
        lax.all_gather(ffn_in.astype(jnp.bfloat16), "wide", axis=1, tiled=True),
        lax.all_gather(ffn_out.astype(jnp.bfloat16), "wide", axis=1, tiled=True),
        lax.all_gather(tables.astype(jnp.bfloat16), "wide", axis=1, tiled=True),
        lax.all_gather(gains.astype(jnp.bfloat16), "wide", axis=1, tiled=True),
    )
    gain_w = gain_low.astype(jnp.float32)
    noised_flat = noised.reshape(-1)
    clean_flat = clean.reshape(-1)
    step_flat = timesteps.reshape(-1)
    vocab_local = table_w.shape[2]
    vocab_ids = lax.axis_index("narrow") * vocab_local + jnp.arange(vocab_local, dtype=jnp.int32)
    picks = (noised_flat[:, None] == vocab_ids[None, :]).astype(jnp.bfloat16)
    looked = add_heads(
        jnp.einsum("sv,dv->sd", picks, table_w[0], preferred_element_type=jnp.float32)
    )
    residual = math.sqrt(D) * looked + time_features(step_flat)
    kept_layers = []
    for layer_index in range(layers):
        residual, kept = layer_forward(
            residual,
            segments,
            query_w[layer_index],
            output_w[layer_index],
            expand_w[layer_index],
            reduce_w[layer_index],
            gain_w[2 * layer_index],
            gain_w[2 * layer_index + 1],
        )
        kept_layers.append(kept)
    final, scale_final = rms_forward(residual, gain_w[2 * layers])
    final_low = final.astype(jnp.bfloat16)
    logits = jnp.dot(final_low, table_w[1], preferred_element_type=jnp.float32)
    local_top = jnp.max(logits, axis=1)
    row_top = lax.pmax(local_top, "narrow")
    row_total = lax.psum(jnp.sum(jnp.exp(logits - row_top[:, None]), axis=1), "narrow")
    log_probs = logits - (row_top + jnp.log(row_total))[:, None]
    probs = jnp.exp(log_probs)
    clamped = jnp.maximum(step_flat, 2).astype(jnp.float32)[:, None]
    beta = 1.0 / (STEPS - clamped + 1.0)
    retain = (STEPS - clamped + 1.0) / STEPS
    spread = (clamped - 1.0) / (STEPS * V)
    at_noised = (vocab_ids[None, :] == noised_flat[:, None]).astype(jnp.float32)
    at_clean = (vocab_ids[None, :] == clean_flat[:, None]).astype(jnp.float32)
    forward_fac = beta / V + (1.0 - beta) * at_noised
    backward_fac = retain * at_clean + spread
    joint = forward_fac * backward_fac
    marginal = retain * probs + spread
    joint_total, cross, model_total, weighted, aligned, clean_logp = lax.psum(
        (
            jnp.sum(joint, axis=1),
            jnp.sum(joint * (jnp.log(backward_fac) - jnp.log(marginal)), axis=1),
            jnp.sum(forward_fac * marginal, axis=1),
            jnp.sum(probs * joint / marginal, axis=1),
            jnp.sum(forward_fac * probs, axis=1),
            jnp.sum(at_clean * log_probs, axis=1),
        ),
        "narrow",
    )
    divergence = cross / joint_total - jnp.log(joint_total) + jnp.log(model_total)
    first_step = step_flat == 1
    losses = jnp.where(first_step, -clean_logp, divergence)
    pull = retain * (
        -(joint / joint_total[:, None]) / marginal + forward_fac / model_total[:, None]
    )
    centre = retain[:, 0] * (-weighted / joint_total + aligned / model_total)
    grad_kl = probs * (pull - centre[:, None])
    grad_recon = probs - at_clean
    grad_logits = (
        (mask / token_total)[:, None] * jnp.where(first_step[:, None], grad_recon, grad_kl)
    ).astype(jnp.bfloat16)
    grad_table_out = jnp.einsum(
        "sd,sv->dv", final_low, grad_logits, preferred_element_type=jnp.float32
    )
    grad_final = back_heads(
        jnp.einsum("sv,dv->sd", grad_logits, table_w[1], preferred_element_type=jnp.float32)
    )
    grad_x, grad_gain_final = rms_backward(grad_final, residual, scale_final, gain_w[2 * layers])
    layer_grads = [None] * layers
    for layer_index in reversed(range(layers)):
        grad_x, produced = layer_backward(
            grad_x,
            kept_layers[layer_index],
            segments,
            query_w[layer_index],
            output_w[layer_index],
            expand_w[layer_index],
            reduce_w[layer_index],
            gain_w[2 * layer_index],
            gain_w[2 * layer_index + 1],
        )
        layer_grads[layer_index] = produced
    grad_look = (math.sqrt(D) * grad_x).astype(jnp.bfloat16)
    grad_table_in = jnp.einsum("sd,sv->dv", grad_look, picks, preferred_element_type=jnp.float32)
    stacked = [jnp.stack([entry[which] for entry in layer_grads]) for which in range(5)]
    gain_layers = stacked[4].reshape(2 * layers, -1)
    grad_tables_all = jnp.stack([grad_table_in, grad_table_out])
    grad_attn_in, grad_attn_out, grad_ffn_in, grad_ffn_out, grad_tables, grad_gains = (
        lax.psum_scatter(stacked[0], "wide", scatter_dimension=2, tiled=True),
        lax.psum_scatter(stacked[1], "wide", scatter_dimension=1, tiled=True),
        lax.psum_scatter(stacked[2], "wide", scatter_dimension=1, tiled=True),
        lax.psum_scatter(stacked[3], "wide", scatter_dimension=1, tiled=True),
        lax.psum_scatter(grad_tables_all, "wide", scatter_dimension=1, tiled=True),
        lax.psum_scatter(
            jnp.concatenate([gain_layers, grad_gain_final[None, :]], axis=0),
            "wide",
            scatter_dimension=1,
            tiled=True,
        ),
    )
    narrow_first = (lax.axis_index("narrow") == 0).astype(jnp.float32)
    squares = (
        jnp.sum(grad_attn_in * grad_attn_in)
        + jnp.sum(grad_attn_out * grad_attn_out)
        + jnp.sum(grad_ffn_in * grad_ffn_in)
        + jnp.sum(grad_ffn_out * grad_ffn_out)
        + jnp.sum(grad_tables * grad_tables)
        + narrow_first * jnp.sum(grad_gains * grad_gains)
    )
    squares, loss_sum = lax.psum(
        (squares, narrow_first * jnp.sum(mask * losses)), ("wide", "narrow")
    )
    grad_norm = jnp.sqrt(squares)
    factor = jnp.minimum(1.0, CLIP_NORM / (grad_norm + 1e-06))
    attn_in_next, attn_in_mean_next, attn_in_square_next, attn_in_copy = adam(
        attn_in, factor * grad_attn_in, attn_in_mean, attn_in_square, WEIGHT_DECAY, LEARN_RATE
    )
    attn_out_next, attn_out_mean_next, attn_out_square_next, attn_out_copy = adam(
        attn_out, factor * grad_attn_out, attn_out_mean, attn_out_square, WEIGHT_DECAY, LEARN_RATE
    )
    ffn_in_next, ffn_in_mean_next, ffn_in_square_next, ffn_in_copy = adam(
        ffn_in, factor * grad_ffn_in, ffn_in_mean, ffn_in_square, WEIGHT_DECAY, LEARN_RATE
    )
    ffn_out_next, ffn_out_mean_next, ffn_out_square_next, ffn_out_copy = adam(
        ffn_out, factor * grad_ffn_out, ffn_out_mean, ffn_out_square, WEIGHT_DECAY, LEARN_RATE
    )
    tables_next, tables_mean_next, tables_square_next, tables_copy = adam(
        tables, factor * grad_tables, tables_mean, tables_square, WEIGHT_DECAY, LEARN_RATE
    )
    gains_next, gains_mean_next, gains_square_next, gains_copy = adam(
        gains, factor * grad_gains, gains_mean, gains_square, 0.0, GAIN_RATE
    )
    return (
        loss_sum,
        token_total,
        grad_norm,
        attn_in_next,
        attn_in_mean_next,
        attn_in_square_next,
        attn_in_copy,
        attn_out_next,
        attn_out_mean_next,
        attn_out_square_next,
        attn_out_copy,
        ffn_in_next,
        ffn_in_mean_next,
        ffn_in_square_next,
        ffn_in_copy,
        ffn_out_next,
        ffn_out_mean_next,
        ffn_out_square_next,
        ffn_out_copy,
        tables_next,
        tables_mean_next,
        tables_square_next,
        tables_copy,
        gains_next,
        gains_mean_next,
        gains_square_next,
        gains_copy,
    )


MESH = pl.DeviceIdType.MESH
F32 = jnp.float32
BF16 = jnp.bfloat16
CHUNKS = 4
VMEM_LIMIT = 56 * 1024 * 1024
FORWARD_KIND = BF16
BACKWARD_KIND = BF16


def whole_vmem():
    return pl.BlockSpec(memory_space=pltpu.VMEM)


def dot_nn(a, b):
    return lax.dot_general(a, b, (((1,), (0,)), ((), ())), preferred_element_type=F32)


def dot_nt(a, b):
    return lax.dot_general(a, b, (((1,), (1,)), ((), ())), preferred_element_type=F32)


def remote(src, dst, send_sem, recv_sem, device):
    return pltpu.make_async_remote_copy(
        src_ref=src,
        dst_ref=dst,
        send_sem=send_sem,
        recv_sem=recv_sem,
        device_id=device,
        device_id_type=MESH,
    )


def greet(devices):
    barrier = pltpu.get_barrier_semaphore()
    for device in devices:
        pl.semaphore_signal(barrier, inc=1, device_id=device, device_id_type=MESH)
    pl.semaphore_wait(barrier, len(devices))


def group_places(seq_len):
    me = lax.axis_index("narrow")
    core = lax.rem(me, 2)
    half = seq_len // 2
    mine = pl.multiple_of(core * half, half)
    other = pl.multiple_of((1 - core) * half, half)
    return ({"narrow": me + 1 - 2 * core}, {"narrow": lax.rem(me + 2, 4)}, mine, other)


class Exchange:
    def __init__(self, refs, sems, base, sibling, partner):
        self.near_out, self.near_in, self.far_out, self.far_in = refs
        self.send, self.recv = sems
        self.base, self.sibling, self.partner = base, sibling, partner

    def near(self, j):
        return remote(
            self.near_out.at[j],
            self.near_in.at[j],
            self.send.at[self.base, j],
            self.recv.at[self.base, j],
            self.sibling,
        )

    def far(self, j):
        return remote(
            self.far_out.at[j],
            self.far_in.at[j],
            self.send.at[self.base + 1, j],
            self.recv.at[self.base + 1, j],
            self.partner,
        )

    def give(self, j, value):
        self.near_out[j] = value
        self.near(j).start()

    def pass_on(self, j, value):
        self.near(j).wait_recv()
        self.far_out[j] = (value + self.near_in[j]).astype(self.far_out.dtype)
        self.far(j).start()

    def take(self, j):
        self.far(j).wait_recv()
        return self.far_out[j].astype(F32) + self.far_in[j].astype(F32)

    def close(self):
        for j in range(CHUNKS):
            self.near(j).wait_send()
            self.far(j).wait_send()

    @staticmethod
    def scratch(chunk, width, kind):
        return [
            pltpu.VMEM((CHUNKS, chunk, width), F32),
            pltpu.VMEM((CHUNKS, chunk, width), F32),
            pltpu.VMEM((CHUNKS, chunk, width), kind),
            pltpu.VMEM((CHUNKS, chunk, width), kind),
        ]


class Share:
    def __init__(self, ref, sems, base, sibling, mine, chunk):
        self.ref, self.base, self.sibling, self.mine, self.chunk = ref, base, sibling, mine, chunk
        self.send, self.recv = sems

    def piece(self, j):
        rows = self.ref.at[pl.ds(pl.multiple_of(self.mine + j * self.chunk, self.chunk), self.chunk)]
        return remote(rows, rows, self.send.at[self.base, j], self.recv.at[self.base, j], self.sibling)

    def put(self, j, value):
        self.ref[pl.ds(pl.multiple_of(self.mine + j * self.chunk, self.chunk), self.chunk), :] = value
        self.piece(j).start()

    def arrived(self, j):
        self.piece(j).wait_recv()

    def close(self):
        for j in range(CHUNKS):
            self.piece(j).wait_send()


def norm_of(value, gain):
    scale = lax.rsqrt(jnp.mean(value * value, axis=-1, keepdims=True) + NORM_EPS)
    return value * scale * gain


def norm_back(grad, value, gain):
    scale = lax.rsqrt(jnp.mean(value * value, axis=-1, keepdims=True) + NORM_EPS)
    unit = value * scale
    scaled = grad * gain
    back = scale * (scaled - unit * jnp.mean(scaled * unit, axis=-1, keepdims=True))
    return (back, jnp.sum(grad * unit, axis=0, keepdims=True))


GELU_A = math.sqrt(2.0 / math.pi)
GELU_B = 0.044715


def gelu_of(x):
    return 0.5 * x * (1.0 + jnp.tanh(GELU_A * (x + GELU_B * (x * x * x))))


def gelu_slope(x):
    square = x * x
    t = jnp.tanh(GELU_A * (x + GELU_B * (x * square)))
    return 0.5 * (1.0 + t) + 0.5 * x * (1.0 - t * t) * (GELU_A * (1.0 + 3.0 * GELU_B * square))


def rows_at(start, j, chunk):
    return pl.ds(pl.multiple_of(start + j * chunk, chunk), chunk)


def embed_kernel(ids, extra, table, gain, resid, normed, near_out, near_in, far_out, far_in, send, recv):
    seq_len, width = normed.shape
    chunk = seq_len // 2 // CHUNKS
    sibling, partner, mine, other = group_places(seq_len)
    vocab = table.shape[1]
    first = lax.axis_index("narrow") * vocab
    greet([sibling, partner])
    trade = Exchange((near_out, near_in, far_out, far_in), (send, recv), 0, sibling, partner)
    share = Share(normed, (send, recv), 2, sibling, mine, chunk)

    def partial(start, j):
        here = ids[rows_at(start, j, chunk), :] - first
        columns = lax.broadcasted_iota(jnp.int32, (chunk, vocab), 1)
        picks = (here == columns).astype(F32).astype(BF16)
        return dot_nt(picks, table[...])

    trade.give(0, partial(other, 0))
    for j in range(CHUNKS):
        if j + 1 < CHUNKS:
            trade.give(j + 1, partial(other, j + 1))
        trade.pass_on(j, partial(mine, j))
    for j in range(CHUNKS):
        x = math.sqrt(width) * trade.take(j) + extra[rows_at(0, j, chunk), :]
        resid[rows_at(0, j, chunk), :] = x
        share.put(j, norm_of(x, gain[...]).astype(BF16))
    for j in range(CHUNKS):
        share.arrived(j)
    trade.close()
    share.close()


def embed(ids, extra, table, gain, collective_id):
    seq_len, width = ids.shape[0], table.shape[0]
    chunk = seq_len // 2 // CHUNKS
    return pl.pallas_call(
        embed_kernel,
        out_shape=(
            jax.ShapeDtypeStruct((seq_len // 2, width), F32),
            jax.ShapeDtypeStruct((seq_len, width), BF16),
        ),
        in_specs=[whole_vmem()] * 4,
        out_specs=(whole_vmem(),) * 2,
        scratch_shapes=Exchange.scratch(chunk, width, FORWARD_KIND)
        + [pltpu.SemaphoreType.DMA((3, CHUNKS)), pltpu.SemaphoreType.DMA((3, CHUNKS))],
        compiler_params=pltpu.CompilerParams(
            collective_id=collective_id, has_side_effects=True, vmem_limit_bytes=VMEM_LIMIT
        ),
        name="embed",
    )(ids, extra, table, gain)


def ffn_kernel(
    mixed, resid, w_out, w_in, w_red, gain, gain_next,
    middle, normed, before, after, result, normed_next,
    near_out, near_in, far_out, far_in, near_out2, near_in2, far_out2, far_in2, own2, send, recv,
):
    seq_len = normed.shape[0]
    chunk = seq_len // 2 // CHUNKS
    sibling, partner, mine, other = group_places(seq_len)
    greet([sibling, partner])
    sems = (send, recv)
    first = Exchange((near_out, near_in, far_out, far_in), sems, 0, sibling, partner)
    second = Exchange((near_out2, near_in2, far_out2, far_in2), sems, 2, sibling, partner)
    share = Share(normed, sems, 4, sibling, mine, chunk)
    share_next = Share(normed_next, sems, 5, sibling, mine, chunk)

    def project(start, j):
        return dot_nt(mixed[rows_at(start, j, chunk), :], w_out[...])

    def feed(rows):
        pre = dot_nn(normed[rows, :], w_in[...])
        before[rows, :] = pre
        act = gelu_of(pre).astype(BF16)
        after[rows, :] = act
        return dot_nt(act, w_red[...])

    first.give(0, project(other, 0))
    for j in range(CHUNKS):
        if j + 1 < CHUNKS:
            first.give(j + 1, project(other, j + 1))
        first.pass_on(j, project(mine, j))
    for j in range(CHUNKS):
        rows = rows_at(0, j, chunk)
        mid = resid[rows, :] + first.take(j)
        middle[rows, :] = mid
        share.put(j, norm_of(mid, gain[...]).astype(BF16))
        own2[j] = feed(rows_at(mine, j, chunk))
        share.arrived(j)
        second.give(j, feed(rows_at(other, j, chunk)))
        if j >= 1:
            second.pass_on(j - 1, own2[j - 1])
    second.pass_on(CHUNKS - 1, own2[CHUNKS - 1])
    for j in range(CHUNKS):
        rows = rows_at(0, j, chunk)
        x = middle[rows, :] + second.take(j)
        result[rows, :] = x
        share_next.put(j, norm_of(x, gain_next[...]).astype(BF16))
    for j in range(CHUNKS):
        share_next.arrived(j)
    for part in (first, second, share, share_next):
        part.close()


def ffn_forward(mixed, resid, w_out, w_in, w_red, gain, gain_next, collective_id):
    seq_len, width, hidden = mixed.shape[0], w_in.shape[0], w_in.shape[1]
    half, chunk = seq_len // 2, seq_len // 2 // CHUNKS
    return pl.pallas_call(
        ffn_kernel,
        out_shape=(
            jax.ShapeDtypeStruct((half, width), F32),
            jax.ShapeDtypeStruct((seq_len, width), BF16),
            jax.ShapeDtypeStruct((seq_len, hidden), F32),
            jax.ShapeDtypeStruct((seq_len, hidden), BF16),
            jax.ShapeDtypeStruct((half, width), F32),
            jax.ShapeDtypeStruct((seq_len, width), BF16),
        ),
        in_specs=[whole_vmem()] * 7,
        out_specs=(whole_vmem(),) * 6,
        scratch_shapes=Exchange.scratch(chunk, width, FORWARD_KIND)
        + Exchange.scratch(chunk, width, FORWARD_KIND)
        + [
            pltpu.VMEM((CHUNKS, chunk, width), F32),
            pltpu.SemaphoreType.DMA((6, CHUNKS)),
            pltpu.SemaphoreType.DMA((6, CHUNKS)),
        ],
        compiler_params=pltpu.CompilerParams(
            collective_id=collective_id, has_side_effects=True, vmem_limit_bytes=VMEM_LIMIT
        ),
        name="ffn_forward",
    )(mixed, resid, w_out, w_in, w_red, gain, gain_next)


TILE = 256


def weight_grad(left_t, right, out):
    columns = right.shape[1]
    tile = TILE if columns % TILE == 0 else columns

    def step(i, _):
        where = pl.ds(pl.multiple_of(i * tile, tile), tile)
        out[:, where] = dot_nn(left_t[...], right[:, where]).astype(out.dtype)
        return 0

    if tile == columns:
        out[...] = dot_nn(left_t[...], right[...]).astype(out.dtype)
    else:
        lax.fori_loop(0, columns // tile, step, 0)


def ffn_back_kernel(
    grad, branch, w_red, w_in, w_out, before, after, normed, middle, gain, mixed,
    grad_middle, grad_attn, grad_mixed, d_red, d_in, d_out, d_gain,
    grad_before, turned, near_out, near_in, far_out, far_in, send, recv,
):
    seq_len = normed.shape[0]
    chunk = seq_len // 2 // CHUNKS
    sibling, partner, mine, other = group_places(seq_len)
    greet([sibling, partner])
    sems = (send, recv)
    trade = Exchange((near_out, near_in, far_out, far_in), sems, 0, sibling, partner)
    share = Share(grad_attn, sems, 2, sibling, mine, chunk)

    def partial(start, j):
        rows = rows_at(start, j, chunk)
        back = dot_nn(branch[rows, :], w_red[...])
        low = (back * gelu_slope(before[rows, :])).astype(BF16)
        grad_before[rows, :] = low
        return dot_nt(low, w_in[...])

    trade.give(0, partial(other, 0))
    for j in range(CHUNKS):
        if j + 1 < CHUNKS:
            trade.give(j + 1, partial(other, j + 1))
        trade.pass_on(j, partial(mine, j))
    turned[...] = jnp.transpose(branch[...])
    weight_grad(turned, after, d_red)
    turned[...] = jnp.transpose(normed[...])
    weight_grad(turned, grad_before, d_in)
    gain_total = jnp.zeros(gain.shape, F32)
    for j in range(CHUNKS):
        rows = rows_at(0, j, chunk)
        back, gain_part = norm_back(trade.take(j), middle[rows, :], gain[...])
        gain_total = gain_total + gain_part
        total = back + grad[rows, :]
        grad_middle[rows, :] = total
        share.put(j, total.astype(BF16))
        here = rows_at(mine, j, chunk)
        grad_mixed[here, :] = dot_nn(grad_attn[here, :], w_out[...]).astype(BF16)
    for j in range(CHUNKS):
        share.arrived(j)
        here = rows_at(other, j, chunk)
        grad_mixed[here, :] = dot_nn(grad_attn[here, :], w_out[...]).astype(BF16)
    d_gain[...] = gain_total
    turned[...] = jnp.transpose(grad_attn[...])
    weight_grad(turned, mixed, d_out)
    trade.close()
    share.close()


def ffn_backward(grad, branch, w_red, w_in, w_out, before, after, normed, middle, gain, mixed, collective_id):
    seq_len, width = normed.shape
    half, chunk = seq_len // 2, seq_len // 2 // CHUNKS
    return pl.pallas_call(
        ffn_back_kernel,
        out_shape=(
            jax.ShapeDtypeStruct((half, width), F32),
            jax.ShapeDtypeStruct((seq_len, width), BF16),
            jax.ShapeDtypeStruct(mixed.shape, BF16),
            jax.ShapeDtypeStruct(w_red.shape, BF16),
            jax.ShapeDtypeStruct(w_in.shape, BF16),
            jax.ShapeDtypeStruct(w_out.shape, BF16),
            jax.ShapeDtypeStruct(gain.shape, F32),
        ),
        in_specs=[whole_vmem()] * 11,
        out_specs=(whole_vmem(),) * 7,
        scratch_shapes=[
            pltpu.VMEM(before.shape, BF16),
            pltpu.VMEM((width, seq_len), BF16),
        ]
        + Exchange.scratch(chunk, width, BACKWARD_KIND)
        + [pltpu.SemaphoreType.DMA((3, CHUNKS)), pltpu.SemaphoreType.DMA((3, CHUNKS))],
        compiler_params=pltpu.CompilerParams(
            collective_id=collective_id, has_side_effects=True, vmem_limit_bytes=VMEM_LIMIT
        ),
        name="ffn_backward",
    )(grad, branch, w_red, w_in, w_out, before, after, normed, middle, gain, mixed)


def norm_back_kernel(
    scale, grads, weights, normed, value, gain, upstream,
    grad_out, branch, d_weights, d_gain,
    turned, near_out, near_in, far_out, far_in, send, recv,
):
    seq_len, width = normed.shape
    chunk = seq_len // 2 // CHUNKS
    sibling, partner, mine, other = group_places(seq_len)
    greet([sibling, partner])
    sems = (send, recv)
    trade = Exchange((near_out, near_in, far_out, far_in), sems, 0, sibling, partner)
    share = Share(branch, sems, 2, sibling, mine, chunk)

    def partial(start, j):
        rows = rows_at(start, j, chunk)
        total = None
        for which in range(grads.shape[0]):
            part = dot_nt(grads[which, rows, :], weights[which])
            total = part if total is None else total + part
        return total

    trade.give(0, partial(other, 0))
    for j in range(CHUNKS):
        if j + 1 < CHUNKS:
            trade.give(j + 1, partial(other, j + 1))
        trade.pass_on(j, partial(mine, j))
    turned[...] = jnp.transpose(normed[...])
    for which in range(grads.shape[0]):
        weight_grad(turned, grads.at[which], d_weights.at[which])
    gain_total = jnp.zeros(gain.shape, F32)
    for j in range(CHUNKS):
        rows = rows_at(0, j, chunk)
        back, gain_part = norm_back(trade.take(j), value[rows, :], gain[...])
        gain_total = gain_total + gain_part
        if upstream is not None:
            back = back + upstream[rows, :]
        grad_out[rows, :] = back
        share.put(j, (back if scale is None else scale * back).astype(BF16))
    d_gain[...] = gain_total
    for j in range(CHUNKS):
        share.arrived(j)
    trade.close()
    share.close()


def norm_backward(grads, weights, normed, value, gain, upstream, scale, collective_id):
    seq_len, width = normed.shape
    half, chunk = seq_len // 2, seq_len // 2 // CHUNKS
    operands = [grads, weights, normed, value, gain] + ([] if upstream is None else [upstream])

    def kernel(*refs):
        given, rest = list(refs[: len(operands)]), refs[len(operands) :]
        if upstream is None:
            given.append(None)
        norm_back_kernel(scale, *given, *rest)

    return pl.pallas_call(
        kernel,
        out_shape=(
            jax.ShapeDtypeStruct((half, width), F32),
            jax.ShapeDtypeStruct((seq_len, width), BF16),
            jax.ShapeDtypeStruct(weights.shape, BF16),
            jax.ShapeDtypeStruct(gain.shape, F32),
        ),
        in_specs=[whole_vmem()] * len(operands),
        out_specs=(whole_vmem(),) * 4,
        scratch_shapes=[pltpu.VMEM((width, seq_len), BF16)]
        + Exchange.scratch(chunk, width, BACKWARD_KIND)
        + [pltpu.SemaphoreType.DMA((3, CHUNKS)), pltpu.SemaphoreType.DMA((3, CHUNKS))],
        compiler_params=pltpu.CompilerParams(
            collective_id=collective_id, has_side_effects=True, vmem_limit_bytes=VMEM_LIMIT
        ),
        name="norm_backward",
    )(*operands)


def wide_places(count):
    me = lax.axis_index("wide")
    fast = lax.rem(me, 2)
    slow = me // 2
    return (me, slow, fast, count // 2)


def gather_kernel(arrays, lead, *refs):
    shards, outs = refs[:arrays], refs[arrays : 2 * arrays]
    lows = refs[2 * arrays : 3 * arrays]
    local, slow_send, slow_recv, fast_send, fast_recv = refs[3 * arrays :]
    count = outs[0].shape[lead[0]]
    me, slow, fast, slows = wide_places(count)
    beside = me + 1 - 2 * fast

    def at(which, owner):
        out = outs[which]
        return out.at[(slice(None),) * lead[which] + (owner,)]

    def along(step):
        return 2 * lax.rem(slow + step, slows) + fast

    def back(step):
        return 2 * lax.rem(slow + slows - step, slows) + fast

    def slow_copy(which, step):
        return remote(
            lows[which], at(which, me), slow_send.at[which, step - 1], slow_recv.at[which, step - 1],
            {"wide": along(step)},
        )

    def fast_copy(which, step):
        block = at(which, back(step))
        return remote(
            lows[which] if step == 0 else block, block, fast_send.at[which, step], fast_recv.at[which, step],
            {"wide": beside},
        )

    greet([{"wide": along(step)} for step in range(1, slows)] + [{"wide": beside}])
    for which in range(arrays):
        lows[which][...] = shards[which][...].astype(lows[which].dtype)
        for step in range(1, slows):
            slow_copy(which, step).start()
        fast_copy(which, 0).start()
        pltpu.make_async_copy(lows[which], at(which, me), local.at[which]).start()
    for which in range(arrays):
        for step in range(1, slows):
            slow_copy(which, step).wait_recv()
            fast_copy(which, step).start()
    for which in range(arrays):
        for step in range(slows):
            fast_copy(which, step).wait()
            if step:
                slow_copy(which, step).wait_send()
        pltpu.make_async_copy(lows[which], at(which, me), local.at[which]).wait()


def gather_wide(shards, leads, kinds, count, collective_id):
    arrays = len(shards)
    slows = count // 2
    return pl.pallas_call(
        functools.partial(gather_kernel, arrays, leads),
        out_shape=tuple(
            jax.ShapeDtypeStruct(s.shape[:lead] + (count,) + s.shape[lead:], kind)
            for s, lead, kind in zip(shards, leads, kinds)
        ),
        in_specs=[whole_vmem()] * arrays,
        out_specs=(pl.BlockSpec(memory_space=pl.ANY),) * arrays,
        scratch_shapes=[pltpu.VMEM(s.shape, kind) for s, kind in zip(shards, kinds)]
        + [
            pltpu.SemaphoreType.DMA((arrays,)),
            pltpu.SemaphoreType.DMA((arrays, slows - 1)),
            pltpu.SemaphoreType.DMA((arrays, slows - 1)),
            pltpu.SemaphoreType.DMA((arrays, slows)),
            pltpu.SemaphoreType.DMA((arrays, slows)),
        ],
        compiler_params=pltpu.CompilerParams(
            collective_id=collective_id, has_side_effects=True, vmem_limit_bytes=VMEM_LIMIT
        ),
        name="gather_weights",
    )(*shards)


def scatter_kernel(arrays, lead, *refs):
    fulls, outs = refs[:arrays], refs[arrays : 2 * arrays]
    fast_in = refs[2 * arrays : 3 * arrays]
    sums = refs[3 * arrays : 4 * arrays]
    slow_in = refs[4 * arrays : 5 * arrays]
    paired, paired_in, fast_send, fast_recv, slow_send, slow_recv, near_send, near_recv = refs[5 * arrays :]
    count = fulls[0].shape[lead[0]]
    me, slow, fast, slows = wide_places(count)
    beside = me + 1 - 2 * fast
    place = lax.axis_index("narrow")
    sibling = {"narrow": place + 1 - 2 * lax.rem(place, 2)}
    sources = list(fulls[:-1]) + [paired]

    def block(which, owner):
        return sources[which].at[(slice(None),) * lead[which] + (owner,)]

    def along(step):
        return lax.rem(slow + step, slows)

    def fast_copy(which, step):
        owner = 2 * along(step) + 1 - fast
        return remote(
            block(which, owner), fast_in[which].at[step], fast_send.at[which, step], fast_recv.at[which, step],
            {"wide": beside},
        )

    def slow_copy(which, step):
        return remote(
            sums[which].at[step - 1], slow_in[which].at[step - 1],
            slow_send.at[which, step - 1], slow_recv.at[which, step - 1],
            {"wide": 2 * along(step) + fast},
        )

    greet([{"wide": 2 * along(step) + fast} for step in range(1, slows)] + [{"wide": beside}, sibling])
    near = remote(fulls[-1], paired_in, near_send, near_recv, sibling)
    near.start()
    for which in range(arrays):
        if which == arrays - 1:
            near.wait()
            paired[...] = fulls[-1][...] + paired_in[...]
        for step in list(range(1, slows)) + [0]:
            fast_copy(which, step).start()
    for which in range(arrays):
        for step in range(1, slows):
            fast_copy(which, step).wait_recv()
            owner = 2 * along(step) + fast
            total = block(which, owner)[...].astype(F32) + fast_in[which][step].astype(F32)
            sums[which][step - 1] = total.astype(sums[which].dtype)
            slow_copy(which, step).start()
    for which in range(arrays):
        fast_copy(which, 0).wait_recv()
        total = block(which, me)[...].astype(F32) + fast_in[which][0].astype(F32)
        for step in range(1, slows):
            slow_copy(which, step).wait_recv()
            total = total + slow_in[which][step - 1].astype(F32)
        outs[which][...] = total
    for which in range(arrays):
        for step in range(slows):
            fast_copy(which, step).wait_send()
            if step:
                slow_copy(which, step).wait_send()


def scatter_wide(fulls, leads, collective_id):
    arrays = len(fulls)
    count = fulls[0].shape[leads[0]]
    slows = count // 2
    shapes = [f.shape[:lead] + f.shape[lead + 1 :] for f, lead in zip(fulls, leads)]
    kinds = [f.dtype for f in fulls]
    return pl.pallas_call(
        functools.partial(scatter_kernel, arrays, leads),
        out_shape=tuple(jax.ShapeDtypeStruct(shape, F32) for shape in shapes),
        in_specs=[whole_vmem()] * arrays,
        out_specs=(whole_vmem(),) * arrays,
        scratch_shapes=[pltpu.VMEM((slows,) + shape, kind) for shape, kind in zip(shapes, kinds)]
        + [pltpu.VMEM((slows - 1,) + shape, kind) for shape, kind in zip(shapes, kinds)]
        + [pltpu.VMEM((slows - 1,) + shape, kind) for shape, kind in zip(shapes, kinds)]
        + [pltpu.VMEM(fulls[-1].shape, F32)] * 2
        + [
            pltpu.SemaphoreType.DMA((arrays, slows)),
            pltpu.SemaphoreType.DMA((arrays, slows)),
            pltpu.SemaphoreType.DMA((arrays, slows - 1)),
            pltpu.SemaphoreType.DMA((arrays, slows - 1)),
            pltpu.SemaphoreType.DMA,
            pltpu.SemaphoreType.DMA,
        ],
        compiler_params=pltpu.CompilerParams(
            collective_id=collective_id, has_side_effects=True, vmem_limit_bytes=VMEM_LIMIT
        ),
        name="scatter_grads",
    )(*fulls)


def shares_tile(wide, narrow, noised, attn_in, attn_out, ffn_in):
    rows, seq_len = noised.shape
    return (
        narrow == 4
        and wide % 2 == 0
        and rows == 1
        and seq_len % (2 * CHUNKS * 128) == 0
        and attn_out.shape[1] % 16 == 0
        and ffn_in.shape[2] % 128 == 0
    )


def per_device(wide, narrow, *arrays):
    noised, attn_in, attn_out, ffn_in = arrays[0], arrays[5], arrays[6], arrays[7]
    if shares_tile(wide, narrow, noised, attn_in, attn_out, ffn_in):
        return tiled_device(wide, *arrays)
    return general_device(*arrays)


def tiled_device(
    wide,
    noised,
    clean,
    timesteps,
    segments,
    counted,
    attn_in,
    attn_out,
    ffn_in,
    ffn_out,
    tables,
    gains,
    attn_in_mean,
    attn_out_mean,
    ffn_in_mean,
    ffn_out_mean,
    tables_mean,
    gains_mean,
    attn_in_square,
    attn_out_square,
    ffn_in_square,
    ffn_out_square,
    tables_square,
    gains_square,
):
    layers = attn_in.shape[0]
    gain_rows, gain_cols = gains.shape
    mask = counted.reshape(-1).astype(jnp.float32)
    seq_len = mask.shape[0]
    half = seq_len // 2
    core = lax.rem(lax.axis_index("narrow"), 2)
    small = jnp.pad(
        jnp.concatenate(
            [
                lax.reduce_precision(gains, 8, 7),
                jnp.full((1, gain_cols), jnp.sum(mask), jnp.float32),
            ]
        ),
        ((0, -(gain_rows + 1) % 8), (0, -gain_cols % 128)),
    )
    shards, leads, kinds = [small, tables[0]], [0, 0], [F32, BF16]
    for layer in range(layers):
        shards += [attn_in[layer], attn_out[layer], ffn_in[layer], ffn_out[layer]]
        leads += [1, 0, 0, 0]
        kinds += [BF16] * 4
    shards.append(tables[1])
    leads.append(0)
    kinds.append(BF16)
    small_all, *weights = gather_wide(shards, leads, kinds, wide, 0)
    token_total = jnp.sum(small_all[:, gain_rows, 0])
    gain_w = small_all[:, :gain_rows, :gain_cols].transpose(1, 0, 2).reshape(gain_rows, 1, -1)
    table_first = weights[0].reshape(-1, tables.shape[2])
    table_last = weights[-1].reshape(-1, tables.shape[2])
    query_w, output_w, expand_w, reduce_w = [], [], [], []
    for layer in range(layers):
        four = weights[1 + 4 * layer : 5 + 4 * layer]
        query_w.append(four[0].reshape(four[0].shape[0], -1, four[0].shape[-1]))
        output_w.append(four[1].reshape(-1, four[1].shape[-1]))
        expand_w.append(four[2].reshape(-1, four[2].shape[-1]))
        reduce_w.append(four[3].reshape(-1, four[3].shape[-1]))

    noised_flat = noised.reshape(-1)
    clean_flat = clean.reshape(-1)
    step_flat = timesteps.reshape(-1)
    vocab_local = tables.shape[2]
    vocab_ids = lax.axis_index("narrow") * vocab_local + jnp.arange(vocab_local, dtype=jnp.int32)
    extra = time_features(lax.dynamic_slice(step_flat, (core * half,), (half,)))
    residual, normed = embed(noised_flat[:, None], extra, table_first, gain_w[0], 1)
    segment = segments[0]
    kept = []
    for layer in range(layers):
        projected = jnp.einsum(
            "sd,cde->cse", normed, query_w[layer], preferred_element_type=jnp.float32
        ).astype(jnp.bfloat16)
        heads = projected.reshape(3, seq_len, -1, HD)
        mixed, log_total = attend((heads[0], heads[1], heads[2], segment))
        mixed = mixed.reshape(seq_len, -1)
        middle, normed_two, before, after, result, normed_next = ffn_forward(
            mixed, residual, output_w[layer], expand_w[layer], reduce_w[layer],
            gain_w[2 * layer + 1], gain_w[2 * layer + 2], 2 + layer,
        )
        kept.append((residual, normed, heads, log_total, mixed, middle, normed_two, before, after))
        residual, normed = result, normed_next

    logits = jnp.dot(normed, table_last, preferred_element_type=jnp.float32)
    local_top = jnp.max(logits, axis=1)
    row_top = lax.pmax(local_top, "narrow")
    row_total = lax.psum(jnp.sum(jnp.exp(logits - row_top[:, None]), axis=1), "narrow")
    log_probs = logits - (row_top + jnp.log(row_total))[:, None]
    probs = jnp.exp(log_probs)
    clamped = jnp.maximum(step_flat, 2).astype(jnp.float32)[:, None]
    beta = 1.0 / (STEPS - clamped + 1.0)
    retain = (STEPS - clamped + 1.0) / STEPS
    spread = (clamped - 1.0) / (STEPS * V)
    at_noised = (vocab_ids[None, :] == noised_flat[:, None]).astype(jnp.float32)
    at_clean = (vocab_ids[None, :] == clean_flat[:, None]).astype(jnp.float32)
    forward_fac = beta / V + (1.0 - beta) * at_noised
    backward_fac = retain * at_clean + spread
    joint = forward_fac * backward_fac
    marginal = retain * probs + spread
    joint_total, cross, model_total, weighted, aligned, clean_logp = lax.psum(
        (
            jnp.sum(joint, axis=1),
            jnp.sum(joint * (jnp.log(backward_fac) - jnp.log(marginal)), axis=1),
            jnp.sum(forward_fac * marginal, axis=1),
            jnp.sum(probs * joint / marginal, axis=1),
            jnp.sum(forward_fac * probs, axis=1),
            jnp.sum(at_clean * log_probs, axis=1),
        ),
        "narrow",
    )
    divergence = cross / joint_total - jnp.log(joint_total) + jnp.log(model_total)
    first_step = step_flat == 1
    losses = jnp.where(first_step, -clean_logp, divergence)
    pull = retain * (
        -(joint / joint_total[:, None]) / marginal + forward_fac / model_total[:, None]
    )
    centre = retain[:, 0] * (-weighted / joint_total + aligned / model_total)
    grad_kl = probs * (pull - centre[:, None])
    grad_recon = probs - at_clean
    grad_logits = (
        (mask / token_total)[:, None] * jnp.where(first_step[:, None], grad_recon, grad_kl)
    ).astype(jnp.bfloat16)

    grad, branch, d_last, gain_final = norm_backward(
        grad_logits[None], table_last[None], normed, residual, gain_w[2 * layers], None, None, 2 + layers
    )
    next_id = 3 + layers
    gain_grads = [None] * (2 * layers) + [gain_final]
    grads = [None] * (4 * layers)
    for layer in reversed(range(layers)):
        residual, normed, heads, log_total, mixed, middle, normed_two, before, after = kept[layer]
        grad_middle, grad_attn, grad_mixed, d_red, d_in, d_out, gain_two = ffn_backward(
            grad, branch, reduce_w[layer], expand_w[layer], output_w[layer], before, after,
            normed_two, middle, gain_w[2 * layer + 1], mixed, next_id,
        )
        pulled = attend_back(
            (heads[0], heads[1], heads[2], segment, log_total, grad_mixed.reshape(seq_len, -1, HD))
        )
        grad_projected = jnp.stack(pulled).reshape(3, seq_len, -1).astype(jnp.bfloat16)
        grad, branch, d_query, gain_one = norm_backward(
            grad_projected, query_w[layer], normed, residual, gain_w[2 * layer], grad_middle,
            math.sqrt(D) if layer == 0 else None, next_id + 1,
        )
        next_id += 2
        gain_grads[2 * layer], gain_grads[2 * layer + 1] = gain_one, gain_two
        grads[4 * layer : 4 * layer + 4] = [d_query, d_out, d_in, d_red]
    picks = (noised_flat[:, None] == vocab_ids[None, :]).astype(jnp.bfloat16)
    d_first = jnp.einsum("sd,sv->dv", branch, picks, preferred_element_type=jnp.float32)

    def by_owner(value, lead):
        shape = value.shape
        return value.astype(jnp.bfloat16).reshape(shape[:lead] + (wide, shape[lead] // wide) + shape[lead + 1 :])

    small_grad = jnp.pad(
        jnp.concatenate(gain_grads).reshape(gain_rows, wide, gain_cols).transpose(1, 0, 2),
        ((0, 0), (0, -gain_rows % 8), (0, -gain_cols % 128)),
    )
    fulls = [by_owner(value, lead) for value, lead in zip(grads, leads[2:])]
    fulls += [by_owner(d_last[0], 0), by_owner(d_first, 0), small_grad]
    own = scatter_wide(fulls, leads[2:] + [0, 0], next_id)
    grad_attn_in, grad_attn_out, grad_ffn_in, grad_ffn_out = [
        jnp.stack([own[4 * layer + which] for layer in range(layers)]) for which in range(4)
    ]
    grad_tables = jnp.stack([own[4 * layers + 1], own[4 * layers]])
    grad_gains = own[-1][:gain_rows, :gain_cols]
    narrow_first = (lax.axis_index("narrow") == 0).astype(jnp.float32)
    squares = (
        jnp.sum(grad_attn_in * grad_attn_in)
        + jnp.sum(grad_attn_out * grad_attn_out)
        + jnp.sum(grad_ffn_in * grad_ffn_in)
        + jnp.sum(grad_ffn_out * grad_ffn_out)
        + jnp.sum(grad_tables * grad_tables)
        + narrow_first * jnp.sum(grad_gains * grad_gains)
    )
    squares, loss_sum = lax.psum(
        (squares, narrow_first * jnp.sum(mask * losses)), ("wide", "narrow")
    )
    grad_norm = jnp.sqrt(squares)
    factor = jnp.minimum(1.0, CLIP_NORM / (grad_norm + 1e-06))
    results = [loss_sum, token_total, grad_norm]
    for weight, gradient, first, second, decay, rate in (
        (attn_in, grad_attn_in, attn_in_mean, attn_in_square, WEIGHT_DECAY, LEARN_RATE),
        (attn_out, grad_attn_out, attn_out_mean, attn_out_square, WEIGHT_DECAY, LEARN_RATE),
        (ffn_in, grad_ffn_in, ffn_in_mean, ffn_in_square, WEIGHT_DECAY, LEARN_RATE),
        (ffn_out, grad_ffn_out, ffn_out_mean, ffn_out_square, WEIGHT_DECAY, LEARN_RATE),
        (tables, grad_tables, tables_mean, tables_square, WEIGHT_DECAY, LEARN_RATE),
        (gains, grad_gains, gains_mean, gains_square, 0.0, GAIN_RATE),
    ):
        results += adam(weight, factor * gradient, first, second, decay, rate)
    return tuple(results)


def solution(mesh):
    wide, narrow = mesh.shape["wide"], mesh.shape["narrow"]
    placed = (
        P("wide", None),
        P("wide", None),
        P("wide", None),
        P("wide", None),
        P("wide", None),
        P(None, None, "wide", "narrow"),
        P(None, "wide", "narrow"),
        P(None, "wide", "narrow"),
        P(None, "wide", "narrow"),
        P(None, "wide", "narrow"),
        P(None, "wide"),
        P(None, None, "wide", "narrow"),
        P(None, "wide", "narrow"),
        P(None, "wide", "narrow"),
        P(None, "wide", "narrow"),
        P(None, "wide", "narrow"),
        P(None, "wide"),
        P(None, None, "wide", "narrow"),
        P(None, "wide", "narrow"),
        P(None, "wide", "narrow"),
        P(None, "wide", "narrow"),
        P(None, "wide", "narrow"),
        P(None, "wide"),
    )
    return jax.shard_map(
        functools.partial(per_device, wide, narrow),
        mesh=mesh,
        in_specs=placed,
        out_specs=(
            P(),
            P(),
            P(),
            P(None, None, "wide", "narrow"),
            P(None, None, "wide", "narrow"),
            P(None, None, "wide", "narrow"),
            P(None, None, "wide", "narrow"),
            P(None, "wide", "narrow"),
            P(None, "wide", "narrow"),
            P(None, "wide", "narrow"),
            P(None, "wide", "narrow"),
            P(None, "wide", "narrow"),
            P(None, "wide", "narrow"),
            P(None, "wide", "narrow"),
            P(None, "wide", "narrow"),
            P(None, "wide", "narrow"),
            P(None, "wide", "narrow"),
            P(None, "wide", "narrow"),
            P(None, "wide", "narrow"),
            P(None, "wide", "narrow"),
            P(None, "wide", "narrow"),
            P(None, "wide", "narrow"),
            P(None, "wide", "narrow"),
            P(None, "wide"),
            P(None, "wide"),
            P(None, "wide"),
            P(None, "wide"),
        ),
        check_vma=False,
    )
```

```python
import functools
import math

import jax
import jax.numpy as jnp
from jax import lax
from jax.experimental import pallas as pl
from jax.experimental.pallas import tpu as pltpu
from jax.sharding import PartitionSpec as P

D = 768
HD = 64
V = 8192
STEPS = 1000
ADAM_STEP = 10


NORM_EPS = 1e-05
LEARN_RATE = 0.05
GAIN_RATE = 0.75
FIRST_DECAY = 0.9
SECOND_DECAY = 0.999
ADAM_EPS = 1e-08
WEIGHT_DECAY = 0.01
CLIP_NORM = 0.005


def add_heads(partial_value):
    return lax.psum(partial_value, "narrow")


def back_heads(partial_value):
    return lax.psum(partial_value, "narrow")


def rms_forward(value, gain):
    scale_row = lax.rsqrt(jnp.mean(value * value, axis=-1, keepdims=True) + NORM_EPS)
    return (value * scale_row * gain, scale_row)


def rms_backward(grad, value, scale_row, gain):
    unit = value * scale_row
    scaled = grad * gain
    back = scale_row * (scaled - unit * jnp.mean(scaled * unit, axis=-1, keepdims=True))
    return (back, jnp.sum(grad * unit, axis=0))


def time_features(timestep_row):
    half_width = D // 2
    rates = jnp.exp(-math.log(10000.0) * jnp.arange(half_width, dtype=jnp.float32) / half_width)
    angles = timestep_row.astype(jnp.float32)[:, None] * rates[None, :]
    return jnp.concatenate([jnp.sin(angles), jnp.cos(angles)], axis=1)


def masked_scores(queries, key_rows, segment):
    scores = jnp.einsum(
        "qhd,khd->hqk", queries, key_rows, preferred_element_type=jnp.float32
    ) * HD ** (-0.5)
    return jnp.where((segment[:, None] == segment[None, :])[None], scores, -1e30)


def attend(entry):
    queries, key_rows, values, segment = entry
    scores = masked_scores(queries, key_rows, segment)
    row_top = jnp.max(scores, axis=-1, keepdims=True)
    log_total = row_top + jnp.log(jnp.sum(jnp.exp(scores - row_top), axis=-1, keepdims=True))
    probs = jnp.exp(scores - log_total).astype(jnp.bfloat16)
    mixed = jnp.einsum("hqk,khd->qhd", probs, values, preferred_element_type=jnp.float32)
    return (mixed.astype(jnp.bfloat16), log_total)


def attend_back(entry):
    queries, key_rows, values, segment, log_total, grad_mixed = entry
    probs = jnp.exp(masked_scores(queries, key_rows, segment) - log_total)
    grad_probs = jnp.einsum("qhd,khd->hqk", grad_mixed, values, preferred_element_type=jnp.float32)
    grad_scores = (
        probs * (grad_probs - jnp.sum(probs * grad_probs, axis=-1, keepdims=True))
    ).astype(jnp.bfloat16)
    grad_query = jnp.einsum(
        "hqk,khd->qhd", grad_scores, key_rows, preferred_element_type=jnp.float32
    ) * HD ** (-0.5)
    grad_key = jnp.einsum(
        "hqk,qhd->khd", grad_scores, queries, preferred_element_type=jnp.float32
    ) * HD ** (-0.5)
    grad_value = jnp.einsum(
        "hqk,qhd->khd", probs.astype(jnp.bfloat16), grad_mixed, preferred_element_type=jnp.float32
    )
    return (grad_query, grad_key, grad_value)


def layer_forward(residual, segments, query_w, output_w, expand_w, reduce_w, gain_attn, gain_ffn):
    seq_count, seq_len = segments.shape
    normed, scale_one = rms_forward(residual, gain_attn)
    normed = normed.astype(jnp.bfloat16)
    projected = jnp.einsum(
        "sd,cde->cse", normed, query_w, preferred_element_type=jnp.float32
    ).astype(jnp.bfloat16)
    heads = projected.reshape(3, seq_count, seq_len, -1, HD)
    mixed, log_total = lax.map(attend, (heads[0], heads[1], heads[2], segments))
    mixed = mixed.reshape(seq_count * seq_len, -1)
    middle = residual + add_heads(
        jnp.einsum("se,de->sd", mixed, output_w, preferred_element_type=jnp.float32)
    )
    normed_two, scale_two = rms_forward(middle, gain_ffn)
    normed_two = normed_two.astype(jnp.bfloat16)
    before = jnp.dot(normed_two, expand_w, preferred_element_type=jnp.float32)
    after = jax.nn.gelu(before).astype(jnp.bfloat16)
    result = middle + add_heads(
        jnp.einsum("sf,df->sd", after, reduce_w, preferred_element_type=jnp.float32)
    )
    return (
        result,
        (
            residual,
            scale_one,
            normed,
            projected,
            log_total,
            mixed,
            middle,
            scale_two,
            normed_two,
            before,
            after,
        ),
    )


def layer_backward(
    grad, kept, segments, query_w, output_w, expand_w, reduce_w, gain_attn, gain_ffn
):
    (
        residual,
        scale_one,
        normed,
        projected,
        log_total,
        mixed,
        middle,
        scale_two,
        normed_two,
        before,
        after,
    ) = kept
    seq_count, seq_len = segments.shape
    grad_branch = grad.astype(jnp.bfloat16)
    grad_after = jnp.dot(grad_branch, reduce_w, preferred_element_type=jnp.float32)
    grad_reduce = jnp.einsum("sd,sf->df", grad_branch, after, preferred_element_type=jnp.float32)
    _, gelu_pull = jax.vjp(jax.nn.gelu, before)
    grad_before = gelu_pull(grad_after)[0].astype(jnp.bfloat16)
    grad_expand = jnp.einsum(
        "sd,sf->df", normed_two, grad_before, preferred_element_type=jnp.float32
    )
    grad_normed_two = back_heads(
        jnp.einsum("sf,df->sd", grad_before, expand_w, preferred_element_type=jnp.float32)
    )
    grad_middle, grad_gain_ffn = rms_backward(grad_normed_two, middle, scale_two, gain_ffn)
    grad_middle = grad_middle + grad
    grad_attn = grad_middle.astype(jnp.bfloat16)
    grad_mixed = jnp.dot(grad_attn, output_w, preferred_element_type=jnp.float32).astype(
        jnp.bfloat16
    )
    grad_output = jnp.einsum("sd,se->de", grad_attn, mixed, preferred_element_type=jnp.float32)
    heads = projected.reshape(3, seq_count, seq_len, -1, HD)
    grad_query, grad_key, grad_value = lax.map(
        attend_back,
        (
            heads[0],
            heads[1],
            heads[2],
            segments,
            log_total,
            grad_mixed.reshape(seq_count, seq_len, -1, HD),
        ),
    )
    grad_projected = (
        jnp.stack([grad_query, grad_key, grad_value])
        .reshape(3, seq_count * seq_len, -1)
        .astype(jnp.bfloat16)
    )
    grad_query_w = jnp.einsum(
        "sd,cse->cde", normed, grad_projected, preferred_element_type=jnp.float32
    )
    grad_normed = back_heads(
        jnp.einsum("cse,cde->sd", grad_projected, query_w, preferred_element_type=jnp.float32)
    )
    grad_input, grad_gain_attn = rms_backward(grad_normed, residual, scale_one, gain_attn)
    return (
        grad_input + grad_middle,
        (
            grad_query_w,
            grad_output,
            grad_expand,
            grad_reduce,
            jnp.stack([grad_gain_attn, grad_gain_ffn]),
        ),
    )


def adam(weight, grad, first, second, decay, rate):
    first_new = FIRST_DECAY * first + (1.0 - FIRST_DECAY) * grad
    second_new = SECOND_DECAY * second + (1.0 - SECOND_DECAY) * grad * grad
    first_hat = first_new / (1.0 - FIRST_DECAY**ADAM_STEP)
    second_hat = second_new / (1.0 - SECOND_DECAY**ADAM_STEP)
    weight_new = weight - rate * (first_hat / (jnp.sqrt(second_hat) + ADAM_EPS) + decay * weight)
    return (weight_new, first_new, second_new, weight_new.astype(jnp.bfloat16))


def general_device(
    noised,
    clean,
    timesteps,
    segments,
    counted,
    attn_in,
    attn_out,
    ffn_in,
    ffn_out,
    tables,
    gains,
    attn_in_mean,
    attn_out_mean,
    ffn_in_mean,
    ffn_out_mean,
    tables_mean,
    gains_mean,
    attn_in_square,
    attn_out_square,
    ffn_in_square,
    ffn_out_square,
    tables_square,
    gains_square,
):
    layers = attn_in.shape[0]
    mask = counted.reshape(-1).astype(jnp.float32)
    token_total = lax.psum(jnp.sum(mask), "wide")
    query_w, output_w, expand_w, reduce_w, table_w, gain_low = (
        lax.all_gather(attn_in.astype(jnp.bfloat16), "wide", axis=2, tiled=True),
        lax.all_gather(attn_out.astype(jnp.bfloat16), "wide", axis=1, tiled=True),
        lax.all_gather(ffn_in.astype(jnp.bfloat16), "wide", axis=1, tiled=True),
        lax.all_gather(ffn_out.astype(jnp.bfloat16), "wide", axis=1, tiled=True),
        lax.all_gather(tables.astype(jnp.bfloat16), "wide", axis=1, tiled=True),
        lax.all_gather(gains.astype(jnp.bfloat16), "wide", axis=1, tiled=True),
    )
    gain_w = gain_low.astype(jnp.float32)
    noised_flat = noised.reshape(-1)
    clean_flat = clean.reshape(-1)
    step_flat = timesteps.reshape(-1)
    vocab_local = table_w.shape[2]
    vocab_ids = lax.axis_index("narrow") * vocab_local + jnp.arange(vocab_local, dtype=jnp.int32)
    picks = (noised_flat[:, None] == vocab_ids[None, :]).astype(jnp.bfloat16)
    looked = add_heads(
        jnp.einsum("sv,dv->sd", picks, table_w[0], preferred_element_type=jnp.float32)
    )
    residual = math.sqrt(D) * looked + time_features(step_flat)
    kept_layers = []
    for layer_index in range(layers):
        residual, kept = layer_forward(
            residual,
            segments,
            query_w[layer_index],
            output_w[layer_index],
            expand_w[layer_index],
            reduce_w[layer_index],
            gain_w[2 * layer_index],
            gain_w[2 * layer_index + 1],
        )
        kept_layers.append(kept)
    final, scale_final = rms_forward(residual, gain_w[2 * layers])
    final_low = final.astype(jnp.bfloat16)
    logits = jnp.dot(final_low, table_w[1], preferred_element_type=jnp.float32)
    local_top = jnp.max(logits, axis=1)
    row_top = lax.pmax(local_top, "narrow")
    row_total = lax.psum(jnp.sum(jnp.exp(logits - row_top[:, None]), axis=1), "narrow")
    log_probs = logits - (row_top + jnp.log(row_total))[:, None]
    probs = jnp.exp(log_probs)
    clamped = jnp.maximum(step_flat, 2).astype(jnp.float32)[:, None]
    beta = 1.0 / (STEPS - clamped + 1.0)
    retain = (STEPS - clamped + 1.0) / STEPS
    spread = (clamped - 1.0) / (STEPS * V)
    at_noised = (vocab_ids[None, :] == noised_flat[:, None]).astype(jnp.float32)
    at_clean = (vocab_ids[None, :] == clean_flat[:, None]).astype(jnp.float32)
    forward_fac = beta / V + (1.0 - beta) * at_noised
    backward_fac = retain * at_clean + spread
    joint = forward_fac * backward_fac
    marginal = retain * probs + spread
    joint_total, cross, model_total, weighted, aligned, clean_logp = lax.psum(
        (
            jnp.sum(joint, axis=1),
            jnp.sum(joint * (jnp.log(backward_fac) - jnp.log(marginal)), axis=1),
            jnp.sum(forward_fac * marginal, axis=1),
            jnp.sum(probs * joint / marginal, axis=1),
            jnp.sum(forward_fac * probs, axis=1),
            jnp.sum(at_clean * log_probs, axis=1),
        ),
        "narrow",
    )
    divergence = cross / joint_total - jnp.log(joint_total) + jnp.log(model_total)
    first_step = step_flat == 1
    losses = jnp.where(first_step, -clean_logp, divergence)
    pull = retain * (
        -(joint / joint_total[:, None]) / marginal + forward_fac / model_total[:, None]
    )
    centre = retain[:, 0] * (-weighted / joint_total + aligned / model_total)
    grad_kl = probs * (pull - centre[:, None])
    grad_recon = probs - at_clean
    grad_logits = (
        (mask / token_total)[:, None] * jnp.where(first_step[:, None], grad_recon, grad_kl)
    ).astype(jnp.bfloat16)
    grad_table_out = jnp.einsum(
        "sd,sv->dv", final_low, grad_logits, preferred_element_type=jnp.float32
    )
    grad_final = back_heads(
        jnp.einsum("sv,dv->sd", grad_logits, table_w[1], preferred_element_type=jnp.float32)
    )
    grad_x, grad_gain_final = rms_backward(grad_final, residual, scale_final, gain_w[2 * layers])
    layer_grads = [None] * layers
    for layer_index in reversed(range(layers)):
        grad_x, produced = layer_backward(
            grad_x,
            kept_layers[layer_index],
            segments,
            query_w[layer_index],
            output_w[layer_index],
            expand_w[layer_index],
            reduce_w[layer_index],
            gain_w[2 * layer_index],
            gain_w[2 * layer_index + 1],
        )
        layer_grads[layer_index] = produced
    grad_look = (math.sqrt(D) * grad_x).astype(jnp.bfloat16)
    grad_table_in = jnp.einsum("sd,sv->dv", grad_look, picks, preferred_element_type=jnp.float32)
    stacked = [jnp.stack([entry[which] for entry in layer_grads]) for which in range(5)]
    gain_layers = stacked[4].reshape(2 * layers, -1)
    grad_tables_all = jnp.stack([grad_table_in, grad_table_out])
    grad_attn_in, grad_attn_out, grad_ffn_in, grad_ffn_out, grad_tables, grad_gains = (
        lax.psum_scatter(stacked[0], "wide", scatter_dimension=2, tiled=True),
        lax.psum_scatter(stacked[1], "wide", scatter_dimension=1, tiled=True),
        lax.psum_scatter(stacked[2], "wide", scatter_dimension=1, tiled=True),
        lax.psum_scatter(stacked[3], "wide", scatter_dimension=1, tiled=True),
        lax.psum_scatter(grad_tables_all, "wide", scatter_dimension=1, tiled=True),
        lax.psum_scatter(
            jnp.concatenate([gain_layers, grad_gain_final[None, :]], axis=0),
            "wide",
            scatter_dimension=1,
            tiled=True,
        ),
    )
    narrow_first = (lax.axis_index("narrow") == 0).astype(jnp.float32)
    squares = (
        jnp.sum(grad_attn_in * grad_attn_in)
        + jnp.sum(grad_attn_out * grad_attn_out)
        + jnp.sum(grad_ffn_in * grad_ffn_in)
        + jnp.sum(grad_ffn_out * grad_ffn_out)
        + jnp.sum(grad_tables * grad_tables)
        + narrow_first * jnp.sum(grad_gains * grad_gains)
    )
    squares, loss_sum = lax.psum(
        (squares, narrow_first * jnp.sum(mask * losses)), ("wide", "narrow")
    )
    grad_norm = jnp.sqrt(squares)
    factor = jnp.minimum(1.0, CLIP_NORM / (grad_norm + 1e-06))
    attn_in_next, attn_in_mean_next, attn_in_square_next, attn_in_copy = adam(
        attn_in, factor * grad_attn_in, attn_in_mean, attn_in_square, WEIGHT_DECAY, LEARN_RATE
    )
    attn_out_next, attn_out_mean_next, attn_out_square_next, attn_out_copy = adam(
        attn_out, factor * grad_attn_out, attn_out_mean, attn_out_square, WEIGHT_DECAY, LEARN_RATE
    )
    ffn_in_next, ffn_in_mean_next, ffn_in_square_next, ffn_in_copy = adam(
        ffn_in, factor * grad_ffn_in, ffn_in_mean, ffn_in_square, WEIGHT_DECAY, LEARN_RATE
    )
    ffn_out_next, ffn_out_mean_next, ffn_out_square_next, ffn_out_copy = adam(
        ffn_out, factor * grad_ffn_out, ffn_out_mean, ffn_out_square, WEIGHT_DECAY, LEARN_RATE
    )
    tables_next, tables_mean_next, tables_square_next, tables_copy = adam(
        tables, factor * grad_tables, tables_mean, tables_square, WEIGHT_DECAY, LEARN_RATE
    )
    gains_next, gains_mean_next, gains_square_next, gains_copy = adam(
        gains, factor * grad_gains, gains_mean, gains_square, 0.0, GAIN_RATE
    )
    return (
        loss_sum,
        token_total,
        grad_norm,
        attn_in_next,
        attn_in_mean_next,
        attn_in_square_next,
        attn_in_copy,
        attn_out_next,
        attn_out_mean_next,
        attn_out_square_next,
        attn_out_copy,
        ffn_in_next,
        ffn_in_mean_next,
        ffn_in_square_next,
        ffn_in_copy,
        ffn_out_next,
        ffn_out_mean_next,
        ffn_out_square_next,
        ffn_out_copy,
        tables_next,
        tables_mean_next,
        tables_square_next,
        tables_copy,
        gains_next,
        gains_mean_next,
        gains_square_next,
        gains_copy,
    )


MESH = pl.DeviceIdType.MESH
F32 = jnp.float32
BF16 = jnp.bfloat16
CHUNKS = 4
VMEM_LIMIT = 56 * 1024 * 1024
FORWARD_KIND = BF16
BACKWARD_KIND = BF16


def whole_vmem():
    return pl.BlockSpec(memory_space=pltpu.VMEM)


def dot_nn(a, b):
    return lax.dot_general(a, b, (((1,), (0,)), ((), ())), preferred_element_type=F32)


def dot_nt(a, b):
    return lax.dot_general(a, b, (((1,), (1,)), ((), ())), preferred_element_type=F32)


def remote(src, dst, send_sem, recv_sem, device):
    return pltpu.make_async_remote_copy(
        src_ref=src,
        dst_ref=dst,
        send_sem=send_sem,
        recv_sem=recv_sem,
        device_id=device,
        device_id_type=MESH,
    )


def greet(devices):
    barrier = pltpu.get_barrier_semaphore()
    for device in devices:
        pl.semaphore_signal(barrier, inc=1, device_id=device, device_id_type=MESH)
    pl.semaphore_wait(barrier, len(devices))


def group_places(seq_len):
    me = lax.axis_index("narrow")
    core = lax.rem(me, 2)
    half = seq_len // 2
    mine = pl.multiple_of(core * half, half)
    other = pl.multiple_of((1 - core) * half, half)
    return ({"narrow": me + 1 - 2 * core}, {"narrow": lax.rem(me + 2, 4)}, mine, other)


class Exchange:
    def __init__(self, refs, sems, base, sibling, partner):
        self.near_out, self.near_in, self.far_out, self.far_in = refs
        self.send, self.recv = sems
        self.base, self.sibling, self.partner = base, sibling, partner

    def near(self, j):
        return remote(
            self.near_out.at[j],
            self.near_in.at[j],
            self.send.at[self.base, j],
            self.recv.at[self.base, j],
            self.sibling,
        )

    def far(self, j):
        return remote(
            self.far_out.at[j],
            self.far_in.at[j],
            self.send.at[self.base + 1, j],
            self.recv.at[self.base + 1, j],
            self.partner,
        )

    def give(self, j, value):
        self.near_out[j] = value
        self.near(j).start()

    def pass_on(self, j, value):
        self.near(j).wait_recv()
        self.far_out[j] = (value + self.near_in[j]).astype(self.far_out.dtype)
        self.far(j).start()

    def take(self, j):
        self.far(j).wait_recv()
        return self.far_out[j].astype(F32) + self.far_in[j].astype(F32)

    def close(self):
        for j in range(CHUNKS):
            self.near(j).wait_send()
            self.far(j).wait_send()

    @staticmethod
    def scratch(chunk, width, kind):
        return [
            pltpu.VMEM((CHUNKS, chunk, width), F32),
            pltpu.VMEM((CHUNKS, chunk, width), F32),
            pltpu.VMEM((CHUNKS, chunk, width), kind),
            pltpu.VMEM((CHUNKS, chunk, width), kind),
        ]


class Share:
    def __init__(self, ref, sems, base, sibling, mine, chunk):
        self.ref, self.base, self.sibling, self.mine, self.chunk = ref, base, sibling, mine, chunk
        self.send, self.recv = sems

    def piece(self, j):
        rows = self.ref.at[pl.ds(pl.multiple_of(self.mine + j * self.chunk, self.chunk), self.chunk)]
        return remote(rows, rows, self.send.at[self.base, j], self.recv.at[self.base, j], self.sibling)

    def put(self, j, value):
        self.ref[pl.ds(pl.multiple_of(self.mine + j * self.chunk, self.chunk), self.chunk), :] = value
        self.piece(j).start()

    def arrived(self, j):
        self.piece(j).wait_recv()

    def close(self):
        for j in range(CHUNKS):
            self.piece(j).wait_send()


def norm_of(value, gain):
    scale = lax.rsqrt(jnp.mean(value * value, axis=-1, keepdims=True) + NORM_EPS)
    return value * scale * gain


def norm_back(grad, value, gain):
    scale = lax.rsqrt(jnp.mean(value * value, axis=-1, keepdims=True) + NORM_EPS)
    unit = value * scale
    scaled = grad * gain
    back = scale * (scaled - unit * jnp.mean(scaled * unit, axis=-1, keepdims=True))
    return (back, jnp.sum(grad * unit, axis=0, keepdims=True))


GELU_A = math.sqrt(2.0 / math.pi)
GELU_B = 0.044715


def gelu_of(x):
    return 0.5 * x * (1.0 + jnp.tanh(GELU_A * (x + GELU_B * (x * x * x))))


def gelu_slope(x):
    square = x * x
    t = jnp.tanh(GELU_A * (x + GELU_B * (x * square)))
    return 0.5 * (1.0 + t) + 0.5 * x * (1.0 - t * t) * (GELU_A * (1.0 + 3.0 * GELU_B * square))


def rows_at(start, j, chunk):
    return pl.ds(pl.multiple_of(start + j * chunk, chunk), chunk)


def embed_kernel(ids, extra, table, gain, resid, normed, near_out, near_in, far_out, far_in, send, recv):
    seq_len, width = normed.shape
    chunk = seq_len // 2 // CHUNKS
    sibling, partner, mine, other = group_places(seq_len)
    vocab = table.shape[1]
    first = lax.axis_index("narrow") * vocab
    greet([sibling, partner])
    trade = Exchange((near_out, near_in, far_out, far_in), (send, recv), 0, sibling, partner)
    share = Share(normed, (send, recv), 2, sibling, mine, chunk)

    def partial(start, j):
        here = ids[rows_at(start, j, chunk), :] - first
        columns = lax.broadcasted_iota(jnp.int32, (chunk, vocab), 1)
        picks = (here == columns).astype(F32).astype(BF16)
        return dot_nt(picks, table[...])

    trade.give(0, partial(other, 0))
    for j in range(CHUNKS):
        if j + 1 < CHUNKS:
            trade.give(j + 1, partial(other, j + 1))
        trade.pass_on(j, partial(mine, j))
    for j in range(CHUNKS):
        x = math.sqrt(width) * trade.take(j) + extra[rows_at(0, j, chunk), :]
        resid[rows_at(0, j, chunk), :] = x
        share.put(j, norm_of(x, gain[...]).astype(BF16))
    for j in range(CHUNKS):
        share.arrived(j)
    trade.close()
    share.close()


def embed(ids, extra, table, gain, collective_id):
    seq_len, width = ids.shape[0], table.shape[0]
    chunk = seq_len // 2 // CHUNKS
    return pl.pallas_call(
        embed_kernel,
        out_shape=(
            jax.ShapeDtypeStruct((seq_len // 2, width), F32),
            jax.ShapeDtypeStruct((seq_len, width), BF16),
        ),
        in_specs=[whole_vmem()] * 4,
        out_specs=(whole_vmem(),) * 2,
        scratch_shapes=Exchange.scratch(chunk, width, FORWARD_KIND)
        + [pltpu.SemaphoreType.DMA((3, CHUNKS)), pltpu.SemaphoreType.DMA((3, CHUNKS))],
        compiler_params=pltpu.CompilerParams(
            collective_id=collective_id, has_side_effects=True, vmem_limit_bytes=VMEM_LIMIT
        ),
        name="embed",
    )(ids, extra, table, gain)


def ffn_kernel(
    mixed, resid, w_out, w_in, w_red, gain, gain_next,
    middle, normed, before, after, result, normed_next,
    near_out, near_in, far_out, far_in, near_out2, near_in2, far_out2, far_in2, own2, send, recv,
):
    seq_len = normed.shape[0]
    chunk = seq_len // 2 // CHUNKS
    sibling, partner, mine, other = group_places(seq_len)
    greet([sibling, partner])
    sems = (send, recv)
    first = Exchange((near_out, near_in, far_out, far_in), sems, 0, sibling, partner)
    second = Exchange((near_out2, near_in2, far_out2, far_in2), sems, 2, sibling, partner)
    share = Share(normed, sems, 4, sibling, mine, chunk)
    share_next = Share(normed_next, sems, 5, sibling, mine, chunk)

    def project(start, j):
        return dot_nt(mixed[rows_at(start, j, chunk), :], w_out[...])

    def feed(rows):
        pre = dot_nn(normed[rows, :], w_in[...])
        before[rows, :] = pre
        act = gelu_of(pre).astype(BF16)
        after[rows, :] = act
        return dot_nt(act, w_red[...])

    first.give(0, project(other, 0))
    for j in range(CHUNKS):
        if j + 1 < CHUNKS:
            first.give(j + 1, project(other, j + 1))
        first.pass_on(j, project(mine, j))
    for j in range(CHUNKS):
        rows = rows_at(0, j, chunk)
        mid = resid[rows, :] + first.take(j)
        middle[rows, :] = mid
        share.put(j, norm_of(mid, gain[...]).astype(BF16))
        own2[j] = feed(rows_at(mine, j, chunk))
        share.arrived(j)
        second.give(j, feed(rows_at(other, j, chunk)))
        if j >= 1:
            second.pass_on(j - 1, own2[j - 1])
    second.pass_on(CHUNKS - 1, own2[CHUNKS - 1])
    for j in range(CHUNKS):
        rows = rows_at(0, j, chunk)
        x = middle[rows, :] + second.take(j)
        result[rows, :] = x
        share_next.put(j, norm_of(x, gain_next[...]).astype(BF16))
    for j in range(CHUNKS):
        share_next.arrived(j)
    for part in (first, second, share, share_next):
        part.close()


def ffn_forward(mixed, resid, w_out, w_in, w_red, gain, gain_next, collective_id):
    seq_len, width, hidden = mixed.shape[0], w_in.shape[0], w_in.shape[1]
    half, chunk = seq_len // 2, seq_len // 2 // CHUNKS
    return pl.pallas_call(
        ffn_kernel,
        out_shape=(
            jax.ShapeDtypeStruct((half, width), F32),
            jax.ShapeDtypeStruct((seq_len, width), BF16),
            jax.ShapeDtypeStruct((seq_len, hidden), F32),
            jax.ShapeDtypeStruct((seq_len, hidden), BF16),
            jax.ShapeDtypeStruct((half, width), F32),
            jax.ShapeDtypeStruct((seq_len, width), BF16),
        ),
        in_specs=[whole_vmem()] * 7,
        out_specs=(whole_vmem(),) * 6,
        scratch_shapes=Exchange.scratch(chunk, width, FORWARD_KIND)
        + Exchange.scratch(chunk, width, FORWARD_KIND)
        + [
            pltpu.VMEM((CHUNKS, chunk, width), F32),
            pltpu.SemaphoreType.DMA((6, CHUNKS)),
            pltpu.SemaphoreType.DMA((6, CHUNKS)),
        ],
        compiler_params=pltpu.CompilerParams(
            collective_id=collective_id, has_side_effects=True, vmem_limit_bytes=VMEM_LIMIT
        ),
        name="ffn_forward",
    )(mixed, resid, w_out, w_in, w_red, gain, gain_next)


TILE = 256


def weight_grad(left_t, right, out):
    columns = right.shape[1]
    tile = TILE if columns % TILE == 0 else columns

    def step(i, _):
        where = pl.ds(pl.multiple_of(i * tile, tile), tile)
        out[:, where] = dot_nn(left_t[...], right[:, where]).astype(out.dtype)
        return 0

    if tile == columns:
        out[...] = dot_nn(left_t[...], right[...]).astype(out.dtype)
    else:
        lax.fori_loop(0, columns // tile, step, 0)


def ffn_back_kernel(
    grad, branch, w_red, w_in, w_out, before, after, normed, middle, gain, mixed,
    grad_middle, grad_attn, grad_mixed, d_red, d_in, d_out, d_gain,
    grad_before, turned, near_out, near_in, far_out, far_in, send, recv,
):
    seq_len = normed.shape[0]
    chunk = seq_len // 2 // CHUNKS
    sibling, partner, mine, other = group_places(seq_len)
    greet([sibling, partner])
    sems = (send, recv)
    trade = Exchange((near_out, near_in, far_out, far_in), sems, 0, sibling, partner)
    share = Share(grad_attn, sems, 2, sibling, mine, chunk)

    def partial(start, j):
        rows = rows_at(start, j, chunk)
        back = dot_nn(branch[rows, :], w_red[...])
        low = (back * gelu_slope(before[rows, :])).astype(BF16)
        grad_before[rows, :] = low
        return dot_nt(low, w_in[...])

    trade.give(0, partial(other, 0))
    for j in range(CHUNKS):
        if j + 1 < CHUNKS:
            trade.give(j + 1, partial(other, j + 1))
        trade.pass_on(j, partial(mine, j))
    turned[...] = jnp.transpose(branch[...])
    weight_grad(turned, after, d_red)
    turned[...] = jnp.transpose(normed[...])
    weight_grad(turned, grad_before, d_in)
    gain_total = jnp.zeros(gain.shape, F32)
    for j in range(CHUNKS):
        rows = rows_at(0, j, chunk)
        back, gain_part = norm_back(trade.take(j), middle[rows, :], gain[...])
        gain_total = gain_total + gain_part
        total = back + grad[rows, :]
        grad_middle[rows, :] = total
        share.put(j, total.astype(BF16))
        here = rows_at(mine, j, chunk)
        grad_mixed[here, :] = dot_nn(grad_attn[here, :], w_out[...]).astype(BF16)
    for j in range(CHUNKS):
        share.arrived(j)
        here = rows_at(other, j, chunk)
        grad_mixed[here, :] = dot_nn(grad_attn[here, :], w_out[...]).astype(BF16)
    d_gain[...] = gain_total
    turned[...] = jnp.transpose(grad_attn[...])
    weight_grad(turned, mixed, d_out)
    trade.close()
    share.close()


def ffn_backward(grad, branch, w_red, w_in, w_out, before, after, normed, middle, gain, mixed, collective_id):
    seq_len, width = normed.shape
    half, chunk = seq_len // 2, seq_len // 2 // CHUNKS
    return pl.pallas_call(
        ffn_back_kernel,
        out_shape=(
            jax.ShapeDtypeStruct((half, width), F32),
            jax.ShapeDtypeStruct((seq_len, width), BF16),
            jax.ShapeDtypeStruct(mixed.shape, BF16),
            jax.ShapeDtypeStruct(w_red.shape, BF16),
            jax.ShapeDtypeStruct(w_in.shape, BF16),
            jax.ShapeDtypeStruct(w_out.shape, BF16),
            jax.ShapeDtypeStruct(gain.shape, F32),
        ),
        in_specs=[whole_vmem()] * 11,
        out_specs=(whole_vmem(),) * 7,
        scratch_shapes=[
            pltpu.VMEM(before.shape, BF16),
            pltpu.VMEM((width, seq_len), BF16),
        ]
        + Exchange.scratch(chunk, width, BACKWARD_KIND)
        + [pltpu.SemaphoreType.DMA((3, CHUNKS)), pltpu.SemaphoreType.DMA((3, CHUNKS))],
        compiler_params=pltpu.CompilerParams(
            collective_id=collective_id, has_side_effects=True, vmem_limit_bytes=VMEM_LIMIT
        ),
        name="ffn_backward",
    )(grad, branch, w_red, w_in, w_out, before, after, normed, middle, gain, mixed)


def norm_back_kernel(
    scale, grads, weights, normed, value, gain, upstream,
    grad_out, branch, d_weights, d_gain,
    turned, near_out, near_in, far_out, far_in, send, recv,
):
    seq_len, width = normed.shape
    chunk = seq_len // 2 // CHUNKS
    sibling, partner, mine, other = group_places(seq_len)
    greet([sibling, partner])
    sems = (send, recv)
    trade = Exchange((near_out, near_in, far_out, far_in), sems, 0, sibling, partner)
    share = Share(branch, sems, 2, sibling, mine, chunk)

    def partial(start, j):
        rows = rows_at(start, j, chunk)
        total = None
        for which in range(grads.shape[0]):
            part = dot_nt(grads[which, rows, :], weights[which])
            total = part if total is None else total + part
        return total

    trade.give(0, partial(other, 0))
    for j in range(CHUNKS):
        if j + 1 < CHUNKS:
            trade.give(j + 1, partial(other, j + 1))
        trade.pass_on(j, partial(mine, j))
    turned[...] = jnp.transpose(normed[...])
    for which in range(grads.shape[0]):
        weight_grad(turned, grads.at[which], d_weights.at[which])
    gain_total = jnp.zeros(gain.shape, F32)
    for j in range(CHUNKS):
        rows = rows_at(0, j, chunk)
        back, gain_part = norm_back(trade.take(j), value[rows, :], gain[...])
        gain_total = gain_total + gain_part
        if upstream is not None:
            back = back + upstream[rows, :]
        grad_out[rows, :] = back
        share.put(j, (back if scale is None else scale * back).astype(BF16))
    d_gain[...] = gain_total
    for j in range(CHUNKS):
        share.arrived(j)
    trade.close()
    share.close()


def norm_backward(grads, weights, normed, value, gain, upstream, scale, collective_id):
    seq_len, width = normed.shape
    half, chunk = seq_len // 2, seq_len // 2 // CHUNKS
    operands = [grads, weights, normed, value, gain] + ([] if upstream is None else [upstream])

    def kernel(*refs):
        given, rest = list(refs[: len(operands)]), refs[len(operands) :]
        if upstream is None:
            given.append(None)
        norm_back_kernel(scale, *given, *rest)

    return pl.pallas_call(
        kernel,
        out_shape=(
            jax.ShapeDtypeStruct((half, width), F32),
            jax.ShapeDtypeStruct((seq_len, width), BF16),
            jax.ShapeDtypeStruct(weights.shape, BF16),
            jax.ShapeDtypeStruct(gain.shape, F32),
        ),
        in_specs=[whole_vmem()] * len(operands),
        out_specs=(whole_vmem(),) * 4,
        scratch_shapes=[pltpu.VMEM((width, seq_len), BF16)]
        + Exchange.scratch(chunk, width, BACKWARD_KIND)
        + [pltpu.SemaphoreType.DMA((3, CHUNKS)), pltpu.SemaphoreType.DMA((3, CHUNKS))],
        compiler_params=pltpu.CompilerParams(
            collective_id=collective_id, has_side_effects=True, vmem_limit_bytes=VMEM_LIMIT
        ),
        name="norm_backward",
    )(*operands)


def wide_places(count):
    me = lax.axis_index("wide")
    fast = lax.rem(me, 2)
    slow = me // 2
    return (me, slow, fast, count // 2)


def gather_kernel(arrays, lead, *refs):
    shards, outs = refs[:arrays], refs[arrays : 2 * arrays]
    lows = refs[2 * arrays : 3 * arrays]
    local, slow_send, slow_recv, fast_send, fast_recv = refs[3 * arrays :]
    count = outs[0].shape[lead[0]]
    me, slow, fast, slows = wide_places(count)
    beside = me + 1 - 2 * fast

    def at(which, owner):
        out = outs[which]
        return out.at[(slice(None),) * lead[which] + (owner,)]

    def along(step):
        return 2 * lax.rem(slow + step, slows) + fast

    def back(step):
        return 2 * lax.rem(slow + slows - step, slows) + fast

    def slow_copy(which, step):
        return remote(
            lows[which], at(which, me), slow_send.at[which, step - 1], slow_recv.at[which, step - 1],
            {"wide": along(step)},
        )

    def fast_copy(which, step):
        block = at(which, back(step))
        return remote(
            lows[which] if step == 0 else block, block, fast_send.at[which, step], fast_recv.at[which, step],
            {"wide": beside},
        )

    greet([{"wide": along(step)} for step in range(1, slows)] + [{"wide": beside}])
    for which in range(arrays):
        lows[which][...] = shards[which][...].astype(lows[which].dtype)
        for step in range(1, slows):
            slow_copy(which, step).start()
        fast_copy(which, 0).start()
        pltpu.make_async_copy(lows[which], at(which, me), local.at[which]).start()
    for which in range(arrays):
        for step in range(1, slows):
            slow_copy(which, step).wait_recv()
            fast_copy(which, step).start()
    for which in range(arrays):
        for step in range(slows):
            fast_copy(which, step).wait()
            if step:
                slow_copy(which, step).wait_send()
        pltpu.make_async_copy(lows[which], at(which, me), local.at[which]).wait()


def gather_wide(shards, leads, kinds, count, collective_id):
    arrays = len(shards)
    slows = count // 2
    return pl.pallas_call(
        functools.partial(gather_kernel, arrays, leads),
        out_shape=tuple(
            jax.ShapeDtypeStruct(s.shape[:lead] + (count,) + s.shape[lead:], kind)
            for s, lead, kind in zip(shards, leads, kinds)
        ),
        in_specs=[whole_vmem()] * arrays,
        out_specs=(pl.BlockSpec(memory_space=pl.ANY),) * arrays,
        scratch_shapes=[pltpu.VMEM(s.shape, kind) for s, kind in zip(shards, kinds)]
        + [
            pltpu.SemaphoreType.DMA((arrays,)),
            pltpu.SemaphoreType.DMA((arrays, slows - 1)),
            pltpu.SemaphoreType.DMA((arrays, slows - 1)),
            pltpu.SemaphoreType.DMA((arrays, slows)),
            pltpu.SemaphoreType.DMA((arrays, slows)),
        ],
        compiler_params=pltpu.CompilerParams(
            collective_id=collective_id, has_side_effects=True, vmem_limit_bytes=VMEM_LIMIT
        ),
        name="gather_weights",
    )(*shards)


def scatter_kernel(arrays, lead, *refs):
    fulls, outs = refs[:arrays], refs[arrays : 2 * arrays]
    fast_in = refs[2 * arrays : 3 * arrays]
    sums = refs[3 * arrays : 4 * arrays]
    slow_in = refs[4 * arrays : 5 * arrays]
    paired, paired_in, fast_send, fast_recv, slow_send, slow_recv, near_send, near_recv = refs[5 * arrays :]
    count = fulls[0].shape[lead[0]]
    me, slow, fast, slows = wide_places(count)
    beside = me + 1 - 2 * fast
    place = lax.axis_index("narrow")
    sibling = {"narrow": place + 1 - 2 * lax.rem(place, 2)}
    sources = list(fulls[:-1]) + [paired]

    def block(which, owner):
        return sources[which].at[(slice(None),) * lead[which] + (owner,)]

    def along(step):
        return lax.rem(slow + step, slows)

    def fast_copy(which, step):
        owner = 2 * along(step) + 1 - fast
        return remote(
            block(which, owner), fast_in[which].at[step], fast_send.at[which, step], fast_recv.at[which, step],
            {"wide": beside},
        )

    def slow_copy(which, step):
        return remote(
            sums[which].at[step - 1], slow_in[which].at[step - 1],
            slow_send.at[which, step - 1], slow_recv.at[which, step - 1],
            {"wide": 2 * along(step) + fast},
        )

    greet([{"wide": 2 * along(step) + fast} for step in range(1, slows)] + [{"wide": beside}, sibling])
    near = remote(fulls[-1], paired_in, near_send, near_recv, sibling)
    near.start()
    for which in range(arrays):
        if which == arrays - 1:
            near.wait()
            paired[...] = fulls[-1][...] + paired_in[...]
        for step in list(range(1, slows)) + [0]:
            fast_copy(which, step).start()
    for which in range(arrays):
        for step in range(1, slows):
            fast_copy(which, step).wait_recv()
            owner = 2 * along(step) + fast
            total = block(which, owner)[...].astype(F32) + fast_in[which][step].astype(F32)
            sums[which][step - 1] = total.astype(sums[which].dtype)
            slow_copy(which, step).start()
    for which in range(arrays):
        fast_copy(which, 0).wait_recv()
        total = block(which, me)[...].astype(F32) + fast_in[which][0].astype(F32)
        for step in range(1, slows):
            slow_copy(which, step).wait_recv()
            total = total + slow_in[which][step - 1].astype(F32)
        outs[which][...] = total
    for which in range(arrays):
        for step in range(slows):
            fast_copy(which, step).wait_send()
            if step:
                slow_copy(which, step).wait_send()


def scatter_wide(fulls, leads, collective_id):
    arrays = len(fulls)
    count = fulls[0].shape[leads[0]]
    slows = count // 2
    shapes = [f.shape[:lead] + f.shape[lead + 1 :] for f, lead in zip(fulls, leads)]
    kinds = [f.dtype for f in fulls]
    return pl.pallas_call(
        functools.partial(scatter_kernel, arrays, leads),
        out_shape=tuple(jax.ShapeDtypeStruct(shape, F32) for shape in shapes),
        in_specs=[whole_vmem()] * arrays,
        out_specs=(whole_vmem(),) * arrays,
        scratch_shapes=[pltpu.VMEM((slows,) + shape, kind) for shape, kind in zip(shapes, kinds)]
        + [pltpu.VMEM((slows - 1,) + shape, kind) for shape, kind in zip(shapes, kinds)]
        + [pltpu.VMEM((slows - 1,) + shape, kind) for shape, kind in zip(shapes, kinds)]
        + [pltpu.VMEM(fulls[-1].shape, F32)] * 2
        + [
            pltpu.SemaphoreType.DMA((arrays, slows)),
            pltpu.SemaphoreType.DMA((arrays, slows)),
            pltpu.SemaphoreType.DMA((arrays, slows - 1)),
            pltpu.SemaphoreType.DMA((arrays, slows - 1)),
            pltpu.SemaphoreType.DMA,
            pltpu.SemaphoreType.DMA,
        ],
        compiler_params=pltpu.CompilerParams(
            collective_id=collective_id, has_side_effects=True, vmem_limit_bytes=VMEM_LIMIT
        ),
        name="scatter_grads",
    )(*fulls)


def head_lanes(value, head, size):
    lanes = lax.broadcasted_iota(jnp.int32, value.shape, 1)
    inside = (lanes >= head * size) & (lanes < (head + 1) * size)
    return jnp.where(inside, value, jnp.zeros_like(value))


def attention_kernel(normed, weights, key_seg, query_seg, projected, mixed, bias, values_t):
    seq_len = normed.shape[0]
    width = mixed.shape[1]
    block = bias.shape[1]
    heads = width // HD

    def project(i, _):
        rows = rows_at(0, i, block)
        for which in range(3):
            projected[which, rows, :] = dot_nn(normed[rows, :], weights[which]).astype(BF16)
        return 0

    lax.fori_loop(0, seq_len // block, project, 0)
    values_t[...] = jnp.transpose(projected[2])

    def queries(i, _):
        rows = rows_at(0, i, block)
        bias[...] = jnp.where(key_seg[...] == query_seg[:, rows], 0.0, -1e30)
        asked = projected[0, rows, :] * HD ** (-0.5)
        parts = []
        for head in range(heads):
            scores = dot_nt(projected[1], head_lanes(asked, head, HD)) + bias[...]
            powers = jnp.exp(scores - jnp.max(scores, axis=0, keepdims=True))
            probs = (powers * (1.0 / jnp.sum(powers, axis=0, keepdims=True))).astype(BF16)
            parts.append(dot_nn(values_t[head * HD : (head + 1) * HD, :], probs))
        mixed[rows, :] = jnp.transpose(jnp.concatenate(parts, axis=0)).astype(BF16)
        return 0

    lax.fori_loop(0, seq_len // block, queries, 0)


QUERY_BLOCK = 256


def attention(normed, weights, key_seg, query_seg):
    seq_len, width = normed.shape[0], weights.shape[2]
    block = min(QUERY_BLOCK, seq_len)
    return pl.pallas_call(
        attention_kernel,
        out_shape=(
            jax.ShapeDtypeStruct((3, seq_len, width), BF16),
            jax.ShapeDtypeStruct((seq_len, width), BF16),
        ),
        in_specs=[whole_vmem()] * 4,
        out_specs=(whole_vmem(),) * 2,
        scratch_shapes=[pltpu.VMEM((seq_len, block), F32), pltpu.VMEM((width, seq_len), BF16)],
        compiler_params=pltpu.CompilerParams(vmem_limit_bytes=VMEM_LIMIT),
        name="attention",
    )(normed, weights, key_seg, query_seg)


def attention_back_kernel(projected, grad_mixed, key_seg, query_seg, out, bias, keys_t, grad_keys, grad_values):
    seq_len, width = grad_mixed.shape
    block = bias.shape[1]
    heads = width // HD
    scale = HD ** (-0.5)
    keys_t[...] = jnp.transpose(projected[1])
    grad_keys[...] = jnp.zeros(grad_keys.shape, F32)
    grad_values[...] = jnp.zeros(grad_values.shape, F32)

    def queries(i, _):
        rows = rows_at(0, i, block)
        bias[...] = jnp.where(key_seg[...] == query_seg[:, rows], 0.0, -1e30)
        asked = projected[0, rows, :] * scale
        given = grad_mixed[rows, :]
        parts = []
        for head in range(heads):
            query = head_lanes(asked, head, HD)
            grad = head_lanes(given, head, HD)
            scores = dot_nt(projected[1], query) + bias[...]
            powers = jnp.exp(scores - jnp.max(scores, axis=0, keepdims=True))
            probs = powers * (1.0 / jnp.sum(powers, axis=0, keepdims=True))
            grad_probs = dot_nt(projected[2], grad)
            centre = jnp.sum(probs * grad_probs, axis=0, keepdims=True)
            grad_scores = (probs * (grad_probs - centre)).astype(BF16)
            parts.append(dot_nn(keys_t[head * HD : (head + 1) * HD, :], grad_scores))
            grad_keys[...] += dot_nn(grad_scores, query)
            grad_values[...] += dot_nn(probs.astype(BF16), grad)
        out[0, rows, :] = (jnp.transpose(jnp.concatenate(parts, axis=0)) * scale).astype(BF16)
        return 0

    lax.fori_loop(0, seq_len // block, queries, 0)
    out[1] = grad_keys[...].astype(BF16)
    out[2] = grad_values[...].astype(BF16)


def attention_back(projected, grad_mixed, key_seg, query_seg):
    seq_len, width = grad_mixed.shape
    block = min(QUERY_BLOCK, seq_len)
    return pl.pallas_call(
        attention_back_kernel,
        out_shape=jax.ShapeDtypeStruct(projected.shape, BF16),
        in_specs=[whole_vmem()] * 4,
        out_specs=whole_vmem(),
        scratch_shapes=[
            pltpu.VMEM((seq_len, block), F32),
            pltpu.VMEM((width, seq_len), BF16),
            pltpu.VMEM((seq_len, width), F32),
            pltpu.VMEM((seq_len, width), F32),
        ],
        compiler_params=pltpu.CompilerParams(vmem_limit_bytes=VMEM_LIMIT),
        name="attention_back",
    )(projected, grad_mixed, key_seg, query_seg)


LANES = 128


def spread(row):
    return jnp.transpose(jnp.broadcast_to(row, (LANES, LANES)))


def to_rows(columns):
    lanes = lax.broadcasted_iota(jnp.int32, (LANES, LANES), 1)
    total = jnp.zeros((LANES, LANES), F32)
    for k, column in enumerate(columns):
        total = jnp.where(lanes == k, column, total)
    return jnp.transpose(total)[:8, :]


def loss_kernel(
    normed, table, info, value, gain,
    grad_out, branch, d_table, d_gain, losses,
    logits, grads, places, turned, stat_out, stat_in, sum_out, sum_in,
    near_out, near_in, far_out, far_in, send, recv, stat_send, stat_recv, sum_send, sum_recv,
):
    seq_len, width = normed.shape
    chunk = seq_len // 2 // CHUNKS
    vocab = table.shape[1]
    tiles = vocab // LANES
    blocks = seq_len // LANES
    me = lax.axis_index("narrow")
    sibling, partner, mine, other = group_places(seq_len)
    peers = [{"narrow": lax.rem(me + k, 4)} for k in range(1, 4)]
    greet(peers)
    sems = (send, recv)
    trade = Exchange((near_out, near_in, far_out, far_in), sems, 0, sibling, partner)
    share = Share(branch, sems, 2, sibling, mine, chunk)
    first = (me * vocab).astype(F32)
    whole = 4.0 * vocab
    lanes = lax.broadcasted_iota(jnp.int32, (LANES, LANES), 1).astype(F32)

    def stat_copy(b, k):
        return remote(stat_out.at[b], stat_in.at[k, b], stat_send.at[k, b], stat_recv.at[k, b], peers[k])

    def sum_copy(b, k):
        return remote(sum_out.at[b], sum_in.at[k, b], sum_send.at[k, b], sum_recv.at[k, b], peers[k])

    def tile_at(t):
        return pl.ds(pl.multiple_of(t * LANES, LANES), LANES)

    def ask(b, _):
        rows = rows_at(0, b, LANES)
        logits[rows, :] = dot_nn(normed[rows, :], table[...])
        here = info[:, rows]
        at_noised = spread(here[0:1] - first)
        at_clean = spread(here[1:2] - first)
        places[b, 0] = at_noised
        places[b, 1] = at_clean

        def top_step(t, top):
            return jnp.maximum(top, logits[rows, tile_at(t)])

        top = lax.fori_loop(1, tiles, top_step, logits[rows, tile_at(0)], unroll=4)
        top = jnp.max(top, axis=1, keepdims=True)
        top_wide = jnp.broadcast_to(top, (LANES, LANES))

        def sum_step(t, totals):
            powers, noised, clean = totals
            piece = logits[rows, tile_at(t)]
            column = lanes + (t * LANES).astype(F32)
            return (
                powers + jnp.exp(piece - top_wide),
                noised + jnp.where(column == at_noised, piece, 0.0),
                clean + jnp.where(column == at_clean, piece, 0.0),
            )

        zero = jnp.zeros((LANES, LANES), F32)
        totals = lax.fori_loop(0, tiles, sum_step, (zero, zero, zero))
        stat_out[b] = to_rows([top] + [jnp.sum(total, axis=1, keepdims=True) for total in totals])
        for k in range(3):
            stat_copy(b, k).start()
        return 0

    lax.fori_loop(0, blocks, ask, 0)

    def scalars(b):
        here = info[:, rows_at(0, b, LANES)]
        step = jnp.maximum(here[2:3], 2.0)
        left = STEPS - step + 1.0
        beta = 1.0 / left
        keep = left / STEPS
        rest = (step - 1.0) / (STEPS * whole)
        own = stat_out[b]
        others = [stat_in[k, b] for k in range(3)]
        top = own[0:1]
        for stat in others:
            top = jnp.maximum(top, stat[0:1])
        total = own[1:2] * jnp.exp(own[0:1] - top)
        noised, clean = own[2:3], own[3:4]
        for stat in others:
            total = total + stat[1:2] * jnp.exp(stat[0:1] - top)
            noised, clean = noised + stat[2:3], clean + stat[3:4]
        return here, beta, keep, rest, top + jnp.log(total), noised, clean

    def measure(b, _):
        rows = rows_at(0, b, LANES)
        for k in range(3):
            stat_copy(b, k).wait_recv()
        _, _, keep, rest, log_total, _, _ = scalars(b)
        log_wide = spread(log_total)
        ratio = spread(keep / rest)

        def step(t, totals):
            logs, shares = totals
            probs = jnp.exp(logits[rows, tile_at(t)] - log_wide)
            logits[rows, tile_at(t)] = probs
            grown = 1.0 + probs * ratio
            return (logs + jnp.log(grown), shares + probs / grown)

        zero = jnp.zeros((LANES, LANES), F32)
        totals = lax.fori_loop(0, tiles, step, (zero, zero))
        sum_out[b] = to_rows([jnp.sum(total, axis=1, keepdims=True) for total in totals])
        for k in range(3):
            sum_copy(b, k).start()
        return 0

    lax.fori_loop(0, blocks, measure, 0)

    def pull(b):
        rows = rows_at(0, b, LANES)
        for k in range(3):
            sum_copy(b, k).wait_recv()
        here, beta, keep, rest, log_total, noised, clean = scalars(b)
        sums = sum_out[b] + sum_in[0, b] + sum_in[1, b] + sum_in[2, b]
        log_sum, share_sum = sums[0:1], sums[1:2] / rest
        same = here[0:1] == here[1:2]
        first_step = here[2:3] == 1.0
        base_a, more_a = beta / whole, 1.0 - beta
        base_w = base_a * rest
        joint = whole * base_w + more_a * rest + base_a * keep + jnp.where(same, more_a * keep, 0.0)
        ratio = keep / rest
        prob_n, prob_c = jnp.exp(noised - log_total), jnp.exp(clean - log_total)
        grown_n, grown_c = 1.0 + prob_n * ratio, 1.0 + prob_c * ratio
        marginal_n, marginal_c = rest * grown_n, rest * grown_c
        log_n, log_c = jnp.log(grown_n), jnp.log(grown_c)
        weight_n = jnp.where(same, 0.0, more_a * rest)
        weight_c = jnp.where(same, more_a * rest + base_a * keep + more_a * keep, base_a * keep)
        lift = jnp.log((keep + rest) / rest)
        cross = -base_w * log_sum - weight_n * log_n - weight_c * log_c + (base_w + weight_c) * lift
        model = base_a * (keep + whole * rest) + more_a * marginal_n
        divergence = cross / joint - jnp.log(joint) + jnp.log(model)
        loss = jnp.where(first_step, log_total - clean, divergence)
        losses[:, rows] = here[4:5] * loss
        weighted = base_w * share_sum + weight_n * prob_n / marginal_n + weight_c * prob_c / marginal_c
        aligned = base_a + more_a * prob_n
        centre = keep * (aligned / model - weighted / joint)
        scale = here[3:4]
        zero = jnp.zeros_like(scale)
        even = scale * jnp.where(first_step, 1.0, keep * base_a / model - centre)
        bent = scale * jnp.where(first_step, zero, -keep * base_w / joint / rest)
        at_n = prob_n * keep * (more_a / model - weight_n / joint / marginal_n)
        at_c = -prob_c * keep * (weight_c / joint / marginal_c)
        extra_n = spread(scale * jnp.where(first_step, zero, at_n))
        extra_c = spread(scale * jnp.where(first_step, -1.0, at_c))
        even, bent, ratio = spread(even), spread(bent), spread(ratio)
        at_noised, at_clean = places[b, 0], places[b, 1]

        def step(t, _):
            probs = logits[rows, tile_at(t)]
            column = lanes + (t * LANES).astype(F32)
            grad = probs * (even + bent / (1.0 + probs * ratio))
            grad = grad + jnp.where(column == at_noised, extra_n, 0.0)
            grad = grad + jnp.where(column == at_clean, extra_c, 0.0)
            grads[rows, tile_at(t)] = grad.astype(BF16)
            return 0

        lax.fori_loop(0, tiles, step, 0)

    def partial(start, j):
        base = start // LANES + j * (chunk // LANES)
        for b in range(chunk // LANES):
            pull(base + b)
        return dot_nt(grads[rows_at(start, j, chunk), :], table[...])

    trade.give(0, partial(other, 0))
    for j in range(CHUNKS):
        if j + 1 < CHUNKS:
            trade.give(j + 1, partial(other, j + 1))
        trade.pass_on(j, partial(mine, j))
    turned[...] = jnp.transpose(normed[...])
    weight_grad(turned, grads, d_table)
    gain_total = jnp.zeros(gain.shape, F32)
    for j in range(CHUNKS):
        rows = rows_at(0, j, chunk)
        back, gain_part = norm_back(trade.take(j), value[rows, :], gain[...])
        gain_total = gain_total + gain_part
        grad_out[rows, :] = back
        share.put(j, back.astype(BF16))
    d_gain[...] = gain_total
    for j in range(CHUNKS):
        share.arrived(j)
    trade.close()
    share.close()

    def finish(b, _):
        for k in range(3):
            stat_copy(b, k).wait_send()
            sum_copy(b, k).wait_send()
        return 0

    lax.fori_loop(0, blocks, finish, 0)


def loss_and_back(normed, table, info, value, gain, collective_id):
    seq_len, width = normed.shape
    vocab = table.shape[1]
    half, chunk, blocks = seq_len // 2, seq_len // 2 // CHUNKS, seq_len // LANES
    return pl.pallas_call(
        loss_kernel,
        out_shape=(
            jax.ShapeDtypeStruct((half, width), F32),
            jax.ShapeDtypeStruct((seq_len, width), BF16),
            jax.ShapeDtypeStruct(table.shape, BF16),
            jax.ShapeDtypeStruct(gain.shape, F32),
            jax.ShapeDtypeStruct((1, seq_len), F32),
        ),
        in_specs=[whole_vmem()] * 5,
        out_specs=(whole_vmem(),) * 5,
        scratch_shapes=[
            pltpu.VMEM((seq_len, vocab), F32),
            pltpu.VMEM((seq_len, vocab), BF16),
            pltpu.VMEM((blocks, 2, LANES, LANES), F32),
            pltpu.VMEM((width, seq_len), BF16),
            pltpu.VMEM((blocks, 8, LANES), F32),
            pltpu.VMEM((3, blocks, 8, LANES), F32),
            pltpu.VMEM((blocks, 8, LANES), F32),
            pltpu.VMEM((3, blocks, 8, LANES), F32),
        ]
        + Exchange.scratch(chunk, width, BACKWARD_KIND)
        + [pltpu.SemaphoreType.DMA((3, CHUNKS)), pltpu.SemaphoreType.DMA((3, CHUNKS))]
        + [pltpu.SemaphoreType.DMA((3, blocks))] * 4,
        compiler_params=pltpu.CompilerParams(
            collective_id=collective_id, has_side_effects=True, vmem_limit_bytes=VMEM_LIMIT
        ),
        name="loss_and_back",
    )(normed, table, info, value, gain)


def scalars_kernel(given, out, near, along, across, send, recv):
    count = 2 * along.shape[0]
    me, slow, fast, slows = wide_places(count)
    place = lax.axis_index("narrow")
    beside = me + 1 - 2 * fast
    group = near.shape[0]

    def near_copy(step):
        return remote(
            near.at[place], near.at[place], send.at[0, step - 1], recv.at[0, step - 1],
            {"narrow": lax.rem(place + step, group)},
        )

    def along_copy(step):
        return remote(
            along.at[slow], along.at[slow], send.at[1, step - 1], recv.at[1, step - 1],
            {"wide": 2 * lax.rem(slow + step, slows) + fast},
        )

    greet(
        [{"narrow": lax.rem(place + step, group)} for step in range(1, group)]
        + [{"wide": 2 * lax.rem(slow + step, slows) + fast} for step in range(1, slows)]
        + [{"wide": beside}]
    )
    near[place] = given[...]
    for step in range(1, group):
        near_copy(step).start()
    for step in range(1, group):
        near_copy(step).wait()
    along[slow] = jnp.sum(near[...], axis=0)
    for step in range(1, slows):
        along_copy(step).start()
    for step in range(1, slows):
        along_copy(step).wait()
    across[0] = jnp.sum(along[...], axis=0)
    last = remote(across.at[0], across.at[1], send.at[2, 0], recv.at[2, 0], {"wide": beside})
    last.start()
    last.wait()
    out[...] = across[0] + across[1]


def sum_scalars(given, wide, narrow, collective_id):
    steps = max(wide // 2, narrow) - 1
    return pl.pallas_call(
        scalars_kernel,
        out_shape=jax.ShapeDtypeStruct(given.shape, F32),
        in_specs=[whole_vmem()],
        out_specs=whole_vmem(),
        scratch_shapes=[
            pltpu.VMEM((narrow,) + given.shape, F32),
            pltpu.VMEM((wide // 2,) + given.shape, F32),
            pltpu.VMEM((2,) + given.shape, F32),
            pltpu.SemaphoreType.DMA((3, steps)),
            pltpu.SemaphoreType.DMA((3, steps)),
        ],
        compiler_params=pltpu.CompilerParams(collective_id=collective_id, has_side_effects=True),
        name="sum_scalars",
    )(given)


def shares_tile(wide, narrow, noised, attn_in, attn_out, ffn_in):
    rows, seq_len = noised.shape
    return (
        narrow == 4
        and wide % 2 == 0
        and rows == 1
        and seq_len % (2 * CHUNKS * 128) == 0
        and attn_out.shape[1] % 16 == 0
        and ffn_in.shape[2] % 128 == 0
    )


def per_device(wide, narrow, *arrays):
    noised, attn_in, attn_out, ffn_in = arrays[0], arrays[5], arrays[6], arrays[7]
    if shares_tile(wide, narrow, noised, attn_in, attn_out, ffn_in):
        return tiled_device(wide, *arrays)
    return general_device(*arrays)


def tiled_device(
    wide,
    noised,
    clean,
    timesteps,
    segments,
    counted,
    attn_in,
    attn_out,
    ffn_in,
    ffn_out,
    tables,
    gains,
    attn_in_mean,
    attn_out_mean,
    ffn_in_mean,
    ffn_out_mean,
    tables_mean,
    gains_mean,
    attn_in_square,
    attn_out_square,
    ffn_in_square,
    ffn_out_square,
    tables_square,
    gains_square,
):
    layers = attn_in.shape[0]
    gain_rows, gain_cols = gains.shape
    mask = counted.reshape(-1).astype(jnp.float32)
    seq_len = mask.shape[0]
    half = seq_len // 2
    core = lax.rem(lax.axis_index("narrow"), 2)
    small = jnp.pad(
        jnp.concatenate(
            [
                lax.reduce_precision(gains, 8, 7),
                jnp.full((1, gain_cols), jnp.sum(mask), jnp.float32),
            ]
        ),
        ((0, -(gain_rows + 1) % 8), (0, -gain_cols % 128)),
    )
    shards, leads, kinds = [small, tables[0]], [0, 0], [F32, BF16]
    for layer in range(layers):
        shards += [attn_in[layer], attn_out[layer], ffn_in[layer], ffn_out[layer]]
        leads += [1, 0, 0, 0]
        kinds += [BF16] * 4
    shards.append(tables[1])
    leads.append(0)
    kinds.append(BF16)
    small_all, *weights = gather_wide(shards, leads, kinds, wide, 0)
    token_total = jnp.sum(small_all[:, gain_rows, 0])
    gain_w = small_all[:, :gain_rows, :gain_cols].transpose(1, 0, 2).reshape(gain_rows, 1, -1)
    table_first = weights[0].reshape(-1, tables.shape[2])
    table_last = weights[-1].reshape(-1, tables.shape[2])
    query_w, output_w, expand_w, reduce_w = [], [], [], []
    for layer in range(layers):
        four = weights[1 + 4 * layer : 5 + 4 * layer]
        query_w.append(four[0].reshape(four[0].shape[0], -1, four[0].shape[-1]))
        output_w.append(four[1].reshape(-1, four[1].shape[-1]))
        expand_w.append(four[2].reshape(-1, four[2].shape[-1]))
        reduce_w.append(four[3].reshape(-1, four[3].shape[-1]))

    noised_flat = noised.reshape(-1)
    clean_flat = clean.reshape(-1)
    step_flat = timesteps.reshape(-1)
    vocab_local = tables.shape[2]
    vocab_ids = lax.axis_index("narrow") * vocab_local + jnp.arange(vocab_local, dtype=jnp.int32)
    extra = time_features(lax.dynamic_slice(step_flat, (core * half,), (half,)))
    residual, normed = embed(noised_flat[:, None], extra, table_first, gain_w[0], 1)
    key_seg, query_seg = segments.reshape(-1, 1), segments.reshape(1, -1)
    kept = []
    for layer in range(layers):
        projected, mixed = attention(normed, query_w[layer], key_seg, query_seg)
        middle, normed_two, before, after, result, normed_next = ffn_forward(
            mixed, residual, output_w[layer], expand_w[layer], reduce_w[layer],
            gain_w[2 * layer + 1], gain_w[2 * layer + 2], 2 + layer,
        )
        kept.append((residual, normed, projected, mixed, middle, normed_two, before, after))
        residual, normed = result, normed_next

    info = jnp.stack(
        [noised_flat.astype(F32), clean_flat.astype(F32), step_flat.astype(F32), mask / token_total, mask]
        + [jnp.zeros_like(mask)] * 3
    )
    grad, branch, d_last, gain_final, losses = loss_and_back(
        normed, table_last, info, residual, gain_w[2 * layers], 2 + layers
    )
    next_id = 3 + layers
    gain_grads = [None] * (2 * layers) + [gain_final]
    grads = [None] * (4 * layers)
    for layer in reversed(range(layers)):
        residual, normed, projected, mixed, middle, normed_two, before, after = kept[layer]
        grad_middle, grad_attn, grad_mixed, d_red, d_in, d_out, gain_two = ffn_backward(
            grad, branch, reduce_w[layer], expand_w[layer], output_w[layer], before, after,
            normed_two, middle, gain_w[2 * layer + 1], mixed, next_id,
        )
        grad_projected = attention_back(projected, grad_mixed, key_seg, query_seg)
        grad, branch, d_query, gain_one = norm_backward(
            grad_projected, query_w[layer], normed, residual, gain_w[2 * layer], grad_middle,
            math.sqrt(D) if layer == 0 else None, next_id + 1,
        )
        next_id += 2
        gain_grads[2 * layer], gain_grads[2 * layer + 1] = gain_one, gain_two
        grads[4 * layer : 4 * layer + 4] = [d_query, d_out, d_in, d_red]
    picks = (noised_flat[:, None] == vocab_ids[None, :]).astype(jnp.bfloat16)
    d_first = jnp.einsum("sd,sv->dv", branch, picks, preferred_element_type=jnp.float32)

    def by_owner(value, lead):
        shape = value.shape
        return value.astype(jnp.bfloat16).reshape(shape[:lead] + (wide, shape[lead] // wide) + shape[lead + 1 :])

    small_grad = jnp.pad(
        jnp.concatenate(gain_grads).reshape(gain_rows, wide, gain_cols).transpose(1, 0, 2),
        ((0, 0), (0, -gain_rows % 8), (0, -gain_cols % 128)),
    )
    fulls = [by_owner(value, lead) for value, lead in zip(grads, leads[2:])]
    fulls += [by_owner(d_last, 0), by_owner(d_first, 0), small_grad]
    own = scatter_wide(fulls, leads[2:] + [0, 0], next_id)
    grad_attn_in, grad_attn_out, grad_ffn_in, grad_ffn_out = [
        jnp.stack([own[4 * layer + which] for layer in range(layers)]) for which in range(4)
    ]
    grad_tables = jnp.stack([own[4 * layers + 1], own[4 * layers]])
    grad_gains = own[-1][:gain_rows, :gain_cols]
    narrow_first = (lax.axis_index("narrow") == 0).astype(jnp.float32)
    squares = (
        jnp.sum(grad_attn_in * grad_attn_in)
        + jnp.sum(grad_attn_out * grad_attn_out)
        + jnp.sum(grad_ffn_in * grad_ffn_in)
        + jnp.sum(grad_ffn_out * grad_ffn_out)
        + jnp.sum(grad_tables * grad_tables)
        + narrow_first * jnp.sum(grad_gains * grad_gains)
    )
    lanes = lax.broadcasted_iota(jnp.int32, (8, 128), 1)
    both = jnp.where(lanes == 0, squares, jnp.where(lanes == 1, narrow_first * jnp.sum(losses), 0.0))
    both = sum_scalars(both, wide, 4, next_id + 1)
    squares, loss_sum = both[0, 0], both[0, 1]
    grad_norm = jnp.sqrt(squares)
    factor = jnp.minimum(1.0, CLIP_NORM / (grad_norm + 1e-06))
    results = [loss_sum, token_total, grad_norm]
    for weight, gradient, first, second, decay, rate in (
        (attn_in, grad_attn_in, attn_in_mean, attn_in_square, WEIGHT_DECAY, LEARN_RATE),
        (attn_out, grad_attn_out, attn_out_mean, attn_out_square, WEIGHT_DECAY, LEARN_RATE),
        (ffn_in, grad_ffn_in, ffn_in_mean, ffn_in_square, WEIGHT_DECAY, LEARN_RATE),
        (ffn_out, grad_ffn_out, ffn_out_mean, ffn_out_square, WEIGHT_DECAY, LEARN_RATE),
        (tables, grad_tables, tables_mean, tables_square, WEIGHT_DECAY, LEARN_RATE),
        (gains, grad_gains, gains_mean, gains_square, 0.0, GAIN_RATE),
    ):
        results += adam(weight, factor * gradient, first, second, decay, rate)
    return tuple(results)


def solution(mesh):
    wide, narrow = mesh.shape["wide"], mesh.shape["narrow"]
    placed = (
        P("wide", None),
        P("wide", None),
        P("wide", None),
        P("wide", None),
        P("wide", None),
        P(None, None, "wide", "narrow"),
        P(None, "wide", "narrow"),
        P(None, "wide", "narrow"),
        P(None, "wide", "narrow"),
        P(None, "wide", "narrow"),
        P(None, "wide"),
        P(None, None, "wide", "narrow"),
        P(None, "wide", "narrow"),
        P(None, "wide", "narrow"),
        P(None, "wide", "narrow"),
        P(None, "wide", "narrow"),
        P(None, "wide"),
        P(None, None, "wide", "narrow"),
        P(None, "wide", "narrow"),
        P(None, "wide", "narrow"),
        P(None, "wide", "narrow"),
        P(None, "wide", "narrow"),
        P(None, "wide"),
    )
    return jax.shard_map(
        functools.partial(per_device, wide, narrow),
        mesh=mesh,
        in_specs=placed,
        out_specs=(
            P(),
            P(),
            P(),
            P(None, None, "wide", "narrow"),
            P(None, None, "wide", "narrow"),
            P(None, None, "wide", "narrow"),
            P(None, None, "wide", "narrow"),
            P(None, "wide", "narrow"),
            P(None, "wide", "narrow"),
            P(None, "wide", "narrow"),
            P(None, "wide", "narrow"),
            P(None, "wide", "narrow"),
            P(None, "wide", "narrow"),
            P(None, "wide", "narrow"),
            P(None, "wide", "narrow"),
            P(None, "wide", "narrow"),
            P(None, "wide", "narrow"),
            P(None, "wide", "narrow"),
            P(None, "wide", "narrow"),
            P(None, "wide", "narrow"),
            P(None, "wide", "narrow"),
            P(None, "wide", "narrow"),
            P(None, "wide", "narrow"),
            P(None, "wide"),
            P(None, "wide"),
            P(None, "wide"),
            P(None, "wide"),
        ),
        check_vma=False,
    )
```

```python
import functools
import math

import jax
import jax.numpy as jnp
from jax import lax
from jax.experimental import pallas as pl
from jax.experimental.pallas import tpu as pltpu
from jax.sharding import PartitionSpec as P

D = 768
HD = 64
V = 8192
STEPS = 1000
ADAM_STEP = 10


NORM_EPS = 1e-05
LEARN_RATE = 0.05
GAIN_RATE = 0.75
FIRST_DECAY = 0.9
SECOND_DECAY = 0.999
ADAM_EPS = 1e-08
WEIGHT_DECAY = 0.01
CLIP_NORM = 0.005


def add_heads(partial_value):
    return lax.psum(partial_value, "narrow")


def back_heads(partial_value):
    return lax.psum(partial_value, "narrow")


def rms_forward(value, gain):
    scale_row = lax.rsqrt(jnp.mean(value * value, axis=-1, keepdims=True) + NORM_EPS)
    return (value * scale_row * gain, scale_row)


def rms_backward(grad, value, scale_row, gain):
    unit = value * scale_row
    scaled = grad * gain
    back = scale_row * (scaled - unit * jnp.mean(scaled * unit, axis=-1, keepdims=True))
    return (back, jnp.sum(grad * unit, axis=0))


def time_features(timestep_row):
    half_width = D // 2
    rates = jnp.exp(-math.log(10000.0) * jnp.arange(half_width, dtype=jnp.float32) / half_width)
    angles = timestep_row.astype(jnp.float32)[:, None] * rates[None, :]
    return jnp.concatenate([jnp.sin(angles), jnp.cos(angles)], axis=1)


def masked_scores(queries, key_rows, segment):
    scores = jnp.einsum(
        "qhd,khd->hqk", queries, key_rows, preferred_element_type=jnp.float32
    ) * HD ** (-0.5)
    return jnp.where((segment[:, None] == segment[None, :])[None], scores, -1e30)


def attend(entry):
    queries, key_rows, values, segment = entry
    scores = masked_scores(queries, key_rows, segment)
    row_top = jnp.max(scores, axis=-1, keepdims=True)
    log_total = row_top + jnp.log(jnp.sum(jnp.exp(scores - row_top), axis=-1, keepdims=True))
    probs = jnp.exp(scores - log_total).astype(jnp.bfloat16)
    mixed = jnp.einsum("hqk,khd->qhd", probs, values, preferred_element_type=jnp.float32)
    return (mixed.astype(jnp.bfloat16), log_total)


def attend_back(entry):
    queries, key_rows, values, segment, log_total, grad_mixed = entry
    probs = jnp.exp(masked_scores(queries, key_rows, segment) - log_total)
    grad_probs = jnp.einsum("qhd,khd->hqk", grad_mixed, values, preferred_element_type=jnp.float32)
    grad_scores = (
        probs * (grad_probs - jnp.sum(probs * grad_probs, axis=-1, keepdims=True))
    ).astype(jnp.bfloat16)
    grad_query = jnp.einsum(
        "hqk,khd->qhd", grad_scores, key_rows, preferred_element_type=jnp.float32
    ) * HD ** (-0.5)
    grad_key = jnp.einsum(
        "hqk,qhd->khd", grad_scores, queries, preferred_element_type=jnp.float32
    ) * HD ** (-0.5)
    grad_value = jnp.einsum(
        "hqk,qhd->khd", probs.astype(jnp.bfloat16), grad_mixed, preferred_element_type=jnp.float32
    )
    return (grad_query, grad_key, grad_value)


def layer_forward(residual, segments, query_w, output_w, expand_w, reduce_w, gain_attn, gain_ffn):
    seq_count, seq_len = segments.shape
    normed, scale_one = rms_forward(residual, gain_attn)
    normed = normed.astype(jnp.bfloat16)
    projected = jnp.einsum(
        "sd,cde->cse", normed, query_w, preferred_element_type=jnp.float32
    ).astype(jnp.bfloat16)
    heads = projected.reshape(3, seq_count, seq_len, -1, HD)
    mixed, log_total = lax.map(attend, (heads[0], heads[1], heads[2], segments))
    mixed = mixed.reshape(seq_count * seq_len, -1)
    middle = residual + add_heads(
        jnp.einsum("se,de->sd", mixed, output_w, preferred_element_type=jnp.float32)
    )
    normed_two, scale_two = rms_forward(middle, gain_ffn)
    normed_two = normed_two.astype(jnp.bfloat16)
    before = jnp.dot(normed_two, expand_w, preferred_element_type=jnp.float32)
    after = jax.nn.gelu(before).astype(jnp.bfloat16)
    result = middle + add_heads(
        jnp.einsum("sf,df->sd", after, reduce_w, preferred_element_type=jnp.float32)
    )
    return (
        result,
        (
            residual,
            scale_one,
            normed,
            projected,
            log_total,
            mixed,
            middle,
            scale_two,
            normed_two,
            before,
            after,
        ),
    )


def layer_backward(
    grad, kept, segments, query_w, output_w, expand_w, reduce_w, gain_attn, gain_ffn
):
    (
        residual,
        scale_one,
        normed,
        projected,
        log_total,
        mixed,
        middle,
        scale_two,
        normed_two,
        before,
        after,
    ) = kept
    seq_count, seq_len = segments.shape
    grad_branch = grad.astype(jnp.bfloat16)
    grad_after = jnp.dot(grad_branch, reduce_w, preferred_element_type=jnp.float32)
    grad_reduce = jnp.einsum("sd,sf->df", grad_branch, after, preferred_element_type=jnp.float32)
    _, gelu_pull = jax.vjp(jax.nn.gelu, before)
    grad_before = gelu_pull(grad_after)[0].astype(jnp.bfloat16)
    grad_expand = jnp.einsum(
        "sd,sf->df", normed_two, grad_before, preferred_element_type=jnp.float32
    )
    grad_normed_two = back_heads(
        jnp.einsum("sf,df->sd", grad_before, expand_w, preferred_element_type=jnp.float32)
    )
    grad_middle, grad_gain_ffn = rms_backward(grad_normed_two, middle, scale_two, gain_ffn)
    grad_middle = grad_middle + grad
    grad_attn = grad_middle.astype(jnp.bfloat16)
    grad_mixed = jnp.dot(grad_attn, output_w, preferred_element_type=jnp.float32).astype(
        jnp.bfloat16
    )
    grad_output = jnp.einsum("sd,se->de", grad_attn, mixed, preferred_element_type=jnp.float32)
    heads = projected.reshape(3, seq_count, seq_len, -1, HD)
    grad_query, grad_key, grad_value = lax.map(
        attend_back,
        (
            heads[0],
            heads[1],
            heads[2],
            segments,
            log_total,
            grad_mixed.reshape(seq_count, seq_len, -1, HD),
        ),
    )
    grad_projected = (
        jnp.stack([grad_query, grad_key, grad_value])
        .reshape(3, seq_count * seq_len, -1)
        .astype(jnp.bfloat16)
    )
    grad_query_w = jnp.einsum(
        "sd,cse->cde", normed, grad_projected, preferred_element_type=jnp.float32
    )
    grad_normed = back_heads(
        jnp.einsum("cse,cde->sd", grad_projected, query_w, preferred_element_type=jnp.float32)
    )
    grad_input, grad_gain_attn = rms_backward(grad_normed, residual, scale_one, gain_attn)
    return (
        grad_input + grad_middle,
        (
            grad_query_w,
            grad_output,
            grad_expand,
            grad_reduce,
            jnp.stack([grad_gain_attn, grad_gain_ffn]),
        ),
    )


def adam(weight, grad, first, second, decay, rate):
    first_new = FIRST_DECAY * first + (1.0 - FIRST_DECAY) * grad
    second_new = SECOND_DECAY * second + (1.0 - SECOND_DECAY) * grad * grad
    first_hat = first_new / (1.0 - FIRST_DECAY**ADAM_STEP)
    second_hat = second_new / (1.0 - SECOND_DECAY**ADAM_STEP)
    weight_new = weight - rate * (first_hat / (jnp.sqrt(second_hat) + ADAM_EPS) + decay * weight)
    return (weight_new, first_new, second_new, weight_new.astype(jnp.bfloat16))


def general_device(
    noised,
    clean,
    timesteps,
    segments,
    counted,
    attn_in,
    attn_out,
    ffn_in,
    ffn_out,
    tables,
    gains,
    attn_in_mean,
    attn_out_mean,
    ffn_in_mean,
    ffn_out_mean,
    tables_mean,
    gains_mean,
    attn_in_square,
    attn_out_square,
    ffn_in_square,
    ffn_out_square,
    tables_square,
    gains_square,
):
    layers = attn_in.shape[0]
    mask = counted.reshape(-1).astype(jnp.float32)
    token_total = lax.psum(jnp.sum(mask), "wide")
    query_w, output_w, expand_w, reduce_w, table_w, gain_low = (
        lax.all_gather(attn_in.astype(jnp.bfloat16), "wide", axis=2, tiled=True),
        lax.all_gather(attn_out.astype(jnp.bfloat16), "wide", axis=1, tiled=True),
        lax.all_gather(ffn_in.astype(jnp.bfloat16), "wide", axis=1, tiled=True),
        lax.all_gather(ffn_out.astype(jnp.bfloat16), "wide", axis=1, tiled=True),
        lax.all_gather(tables.astype(jnp.bfloat16), "wide", axis=1, tiled=True),
        lax.all_gather(gains.astype(jnp.bfloat16), "wide", axis=1, tiled=True),
    )
    gain_w = gain_low.astype(jnp.float32)
    noised_flat = noised.reshape(-1)
    clean_flat = clean.reshape(-1)
    step_flat = timesteps.reshape(-1)
    vocab_local = table_w.shape[2]
    vocab_ids = lax.axis_index("narrow") * vocab_local + jnp.arange(vocab_local, dtype=jnp.int32)
    picks = (noised_flat[:, None] == vocab_ids[None, :]).astype(jnp.bfloat16)
    looked = add_heads(
        jnp.einsum("sv,dv->sd", picks, table_w[0], preferred_element_type=jnp.float32)
    )
    residual = math.sqrt(D) * looked + time_features(step_flat)
    kept_layers = []
    for layer_index in range(layers):
        residual, kept = layer_forward(
            residual,
            segments,
            query_w[layer_index],
            output_w[layer_index],
            expand_w[layer_index],
            reduce_w[layer_index],
            gain_w[2 * layer_index],
            gain_w[2 * layer_index + 1],
        )
        kept_layers.append(kept)
    final, scale_final = rms_forward(residual, gain_w[2 * layers])
    final_low = final.astype(jnp.bfloat16)
    logits = jnp.dot(final_low, table_w[1], preferred_element_type=jnp.float32)
    local_top = jnp.max(logits, axis=1)
    row_top = lax.pmax(local_top, "narrow")
    row_total = lax.psum(jnp.sum(jnp.exp(logits - row_top[:, None]), axis=1), "narrow")
    log_probs = logits - (row_top + jnp.log(row_total))[:, None]
    probs = jnp.exp(log_probs)
    clamped = jnp.maximum(step_flat, 2).astype(jnp.float32)[:, None]
    beta = 1.0 / (STEPS - clamped + 1.0)
    retain = (STEPS - clamped + 1.0) / STEPS
    spread = (clamped - 1.0) / (STEPS * V)
    at_noised = (vocab_ids[None, :] == noised_flat[:, None]).astype(jnp.float32)
    at_clean = (vocab_ids[None, :] == clean_flat[:, None]).astype(jnp.float32)
    forward_fac = beta / V + (1.0 - beta) * at_noised
    backward_fac = retain * at_clean + spread
    joint = forward_fac * backward_fac
    marginal = retain * probs + spread
    joint_total, cross, model_total, weighted, aligned, clean_logp = lax.psum(
        (
            jnp.sum(joint, axis=1),
            jnp.sum(joint * (jnp.log(backward_fac) - jnp.log(marginal)), axis=1),
            jnp.sum(forward_fac * marginal, axis=1),
            jnp.sum(probs * joint / marginal, axis=1),
            jnp.sum(forward_fac * probs, axis=1),
            jnp.sum(at_clean * log_probs, axis=1),
        ),
        "narrow",
    )
    divergence = cross / joint_total - jnp.log(joint_total) + jnp.log(model_total)
    first_step = step_flat == 1
    losses = jnp.where(first_step, -clean_logp, divergence)
    pull = retain * (
        -(joint / joint_total[:, None]) / marginal + forward_fac / model_total[:, None]
    )
    centre = retain[:, 0] * (-weighted / joint_total + aligned / model_total)
    grad_kl = probs * (pull - centre[:, None])
    grad_recon = probs - at_clean
    grad_logits = (
        (mask / token_total)[:, None] * jnp.where(first_step[:, None], grad_recon, grad_kl)
    ).astype(jnp.bfloat16)
    grad_table_out = jnp.einsum(
        "sd,sv->dv", final_low, grad_logits, preferred_element_type=jnp.float32
    )
    grad_final = back_heads(
        jnp.einsum("sv,dv->sd", grad_logits, table_w[1], preferred_element_type=jnp.float32)
    )
    grad_x, grad_gain_final = rms_backward(grad_final, residual, scale_final, gain_w[2 * layers])
    layer_grads = [None] * layers
    for layer_index in reversed(range(layers)):
        grad_x, produced = layer_backward(
            grad_x,
            kept_layers[layer_index],
            segments,
            query_w[layer_index],
            output_w[layer_index],
            expand_w[layer_index],
            reduce_w[layer_index],
            gain_w[2 * layer_index],
            gain_w[2 * layer_index + 1],
        )
        layer_grads[layer_index] = produced
    grad_look = (math.sqrt(D) * grad_x).astype(jnp.bfloat16)
    grad_table_in = jnp.einsum("sd,sv->dv", grad_look, picks, preferred_element_type=jnp.float32)
    stacked = [jnp.stack([entry[which] for entry in layer_grads]) for which in range(5)]
    gain_layers = stacked[4].reshape(2 * layers, -1)
    grad_tables_all = jnp.stack([grad_table_in, grad_table_out])
    grad_attn_in, grad_attn_out, grad_ffn_in, grad_ffn_out, grad_tables, grad_gains = (
        lax.psum_scatter(stacked[0], "wide", scatter_dimension=2, tiled=True),
        lax.psum_scatter(stacked[1], "wide", scatter_dimension=1, tiled=True),
        lax.psum_scatter(stacked[2], "wide", scatter_dimension=1, tiled=True),
        lax.psum_scatter(stacked[3], "wide", scatter_dimension=1, tiled=True),
        lax.psum_scatter(grad_tables_all, "wide", scatter_dimension=1, tiled=True),
        lax.psum_scatter(
            jnp.concatenate([gain_layers, grad_gain_final[None, :]], axis=0),
            "wide",
            scatter_dimension=1,
            tiled=True,
        ),
    )
    narrow_first = (lax.axis_index("narrow") == 0).astype(jnp.float32)
    squares = (
        jnp.sum(grad_attn_in * grad_attn_in)
        + jnp.sum(grad_attn_out * grad_attn_out)
        + jnp.sum(grad_ffn_in * grad_ffn_in)
        + jnp.sum(grad_ffn_out * grad_ffn_out)
        + jnp.sum(grad_tables * grad_tables)
        + narrow_first * jnp.sum(grad_gains * grad_gains)
    )
    squares, loss_sum = lax.psum(
        (squares, narrow_first * jnp.sum(mask * losses)), ("wide", "narrow")
    )
    grad_norm = jnp.sqrt(squares)
    factor = jnp.minimum(1.0, CLIP_NORM / (grad_norm + 1e-06))
    attn_in_next, attn_in_mean_next, attn_in_square_next, attn_in_copy = adam(
        attn_in, factor * grad_attn_in, attn_in_mean, attn_in_square, WEIGHT_DECAY, LEARN_RATE
    )
    attn_out_next, attn_out_mean_next, attn_out_square_next, attn_out_copy = adam(
        attn_out, factor * grad_attn_out, attn_out_mean, attn_out_square, WEIGHT_DECAY, LEARN_RATE
    )
    ffn_in_next, ffn_in_mean_next, ffn_in_square_next, ffn_in_copy = adam(
        ffn_in, factor * grad_ffn_in, ffn_in_mean, ffn_in_square, WEIGHT_DECAY, LEARN_RATE
    )
    ffn_out_next, ffn_out_mean_next, ffn_out_square_next, ffn_out_copy = adam(
        ffn_out, factor * grad_ffn_out, ffn_out_mean, ffn_out_square, WEIGHT_DECAY, LEARN_RATE
    )
    tables_next, tables_mean_next, tables_square_next, tables_copy = adam(
        tables, factor * grad_tables, tables_mean, tables_square, WEIGHT_DECAY, LEARN_RATE
    )
    gains_next, gains_mean_next, gains_square_next, gains_copy = adam(
        gains, factor * grad_gains, gains_mean, gains_square, 0.0, GAIN_RATE
    )
    return (
        loss_sum,
        token_total,
        grad_norm,
        attn_in_next,
        attn_in_mean_next,
        attn_in_square_next,
        attn_in_copy,
        attn_out_next,
        attn_out_mean_next,
        attn_out_square_next,
        attn_out_copy,
        ffn_in_next,
        ffn_in_mean_next,
        ffn_in_square_next,
        ffn_in_copy,
        ffn_out_next,
        ffn_out_mean_next,
        ffn_out_square_next,
        ffn_out_copy,
        tables_next,
        tables_mean_next,
        tables_square_next,
        tables_copy,
        gains_next,
        gains_mean_next,
        gains_square_next,
        gains_copy,
    )


MESH = pl.DeviceIdType.MESH
F32 = jnp.float32
BF16 = jnp.bfloat16
CHUNKS = 4
VMEM_LIMIT = 56 * 1024 * 1024
FORWARD_KIND = BF16
BACKWARD_KIND = BF16


def whole_vmem():
    return pl.BlockSpec(memory_space=pltpu.VMEM)


def dot_nn(a, b):
    return lax.dot_general(a, b, (((1,), (0,)), ((), ())), preferred_element_type=F32)


def dot_nt(a, b):
    return lax.dot_general(a, b, (((1,), (1,)), ((), ())), preferred_element_type=F32)


def remote(src, dst, send_sem, recv_sem, device):
    return pltpu.make_async_remote_copy(
        src_ref=src,
        dst_ref=dst,
        send_sem=send_sem,
        recv_sem=recv_sem,
        device_id=device,
        device_id_type=MESH,
    )


def greet(devices):
    barrier = pltpu.get_barrier_semaphore()
    for device in devices:
        pl.semaphore_signal(barrier, inc=1, device_id=device, device_id_type=MESH)
    pl.semaphore_wait(barrier, len(devices))


def group_places(seq_len):
    me = lax.axis_index("narrow")
    core = lax.rem(me, 2)
    half = seq_len // 2
    mine = pl.multiple_of(core * half, half)
    other = pl.multiple_of((1 - core) * half, half)
    return ({"narrow": me + 1 - 2 * core}, {"narrow": lax.rem(me + 2, 4)}, mine, other)


class Exchange:
    def __init__(self, refs, sems, base, sibling, partner):
        self.near_out, self.near_in, self.far_out, self.far_in = refs
        self.send, self.recv = sems
        self.base, self.sibling, self.partner = base, sibling, partner

    def near(self, j):
        return remote(
            self.near_out.at[j],
            self.near_in.at[j],
            self.send.at[self.base, j],
            self.recv.at[self.base, j],
            self.sibling,
        )

    def far(self, j):
        return remote(
            self.far_out.at[j],
            self.far_in.at[j],
            self.send.at[self.base + 1, j],
            self.recv.at[self.base + 1, j],
            self.partner,
        )

    def give(self, j, value):
        self.near_out[j] = value
        self.near(j).start()

    def pass_on(self, j, value):
        self.near(j).wait_recv()
        self.far_out[j] = (value + self.near_in[j]).astype(self.far_out.dtype)
        self.far(j).start()

    def take(self, j):
        self.far(j).wait_recv()
        return self.far_out[j].astype(F32) + self.far_in[j].astype(F32)

    def close(self):
        for j in range(CHUNKS):
            self.near(j).wait_send()
            self.far(j).wait_send()

    @staticmethod
    def scratch(chunk, width, kind):
        return [
            pltpu.VMEM((CHUNKS, chunk, width), F32),
            pltpu.VMEM((CHUNKS, chunk, width), F32),
            pltpu.VMEM((CHUNKS, chunk, width), kind),
            pltpu.VMEM((CHUNKS, chunk, width), kind),
        ]


class Share:
    def __init__(self, ref, sems, base, sibling, mine, chunk):
        self.ref, self.base, self.sibling, self.mine, self.chunk = ref, base, sibling, mine, chunk
        self.send, self.recv = sems

    def piece(self, j):
        rows = self.ref.at[pl.ds(pl.multiple_of(self.mine + j * self.chunk, self.chunk), self.chunk)]
        return remote(rows, rows, self.send.at[self.base, j], self.recv.at[self.base, j], self.sibling)

    def put(self, j, value):
        self.ref[pl.ds(pl.multiple_of(self.mine + j * self.chunk, self.chunk), self.chunk), :] = value
        self.piece(j).start()

    def arrived(self, j):
        self.piece(j).wait_recv()

    def close(self):
        for j in range(CHUNKS):
            self.piece(j).wait_send()


class Carry:
    def __init__(self, loads):
        self.loads = loads
        self.pieces = [(load, piece) for load in loads for piece in range(load.pieces)]
        self.relayed = 0

    def peers(self):
        ways = []
        for load in self.loads:
            ways += [way for way in load.ways if way not in ways]
        me, slow, fast, slows = wide_places(self.loads[0].count) if self.loads else (0, 0, 0, 0)
        found = []
        if "slow" in ways:
            found += [{"wide": 2 * lax.rem(slow + step, slows) + fast} for step in range(1, slows)]
        if "fast" in ways:
            found.append({"wide": me + 1 - 2 * fast})
        return found

    def start(self):
        for load in self.loads:
            load.start()

    def relay(self, part):
        until = int(part * len(self.pieces) + 0.5)
        for load, piece in self.pieces[self.relayed : until]:
            load.relay(piece)
        self.relayed = max(self.relayed, until)

    def finish(self):
        self.relay(1.0)
        for load in self.loads:
            load.finish()


class GatherLoad:
    ways = ("slow", "fast")

    def __init__(self, weights, index, lead, count, pieces=1):
        self.index, self.lead, self.count, self.pieces = index, lead, count, pieces
        shape, slows = weights.shape[1:], count // 2
        self.rows = shape[-2] // pieces
        self.operands, self.in_specs = [weights], [whole_vmem()]
        self.outs = [jax.ShapeDtypeStruct(shape[:lead] + (count,) + shape[lead:], BF16)]
        self.out_specs = [pl.BlockSpec(memory_space=pl.ANY)]
        self.scratch = [pltpu.VMEM(shape, BF16), pltpu.SemaphoreType.DMA] + [
            pltpu.SemaphoreType.DMA((pieces, slows))
        ] * 4

    def bind(self, given, out, scratch):
        self.shard, self.out = given[0], out[0]
        self.low, self.local, self.slow_send, self.slow_recv, self.fast_send, self.fast_recv = scratch
        self.me, self.slow, self.fast, self.slows = wide_places(self.count)

    def cut(self, ref, piece):
        if self.pieces == 1:
            return ref
        return ref.at[(slice(None),) * (len(ref.shape) - 2) + (pl.ds(piece * self.rows, self.rows),)]

    def at(self, owner):
        return self.out.at[(slice(None),) * self.lead + (owner,)]

    def slow_copy(self, piece, step):
        return remote(
            self.cut(self.low, piece), self.cut(self.at(self.me), piece),
            self.slow_send.at[piece, step], self.slow_recv.at[piece, step],
            {"wide": 2 * lax.rem(self.slow + step, self.slows) + self.fast},
        )

    def fast_copy(self, piece, step):
        block = self.cut(self.at(2 * lax.rem(self.slow + self.slows - step, self.slows) + self.fast), piece)
        return remote(
            self.cut(self.low, piece) if step == 0 else block, block,
            self.fast_send.at[piece, step], self.fast_recv.at[piece, step],
            {"wide": self.me + 1 - 2 * self.fast},
        )

    def own_copy(self):
        return pltpu.make_async_copy(self.low, self.at(self.me), self.local)

    def start(self):
        self.low[...] = self.shard[self.index].astype(BF16)
        for piece in range(self.pieces):
            for step in range(1, self.slows):
                self.slow_copy(piece, step).start()
            self.fast_copy(piece, 0).start()
        self.own_copy().start()

    def relay(self, piece):
        for step in range(1, self.slows):
            self.slow_copy(piece, step).wait_recv()
            self.fast_copy(piece, step).start()

    def finish(self):
        for piece in range(self.pieces):
            for step in range(self.slows):
                self.fast_copy(piece, step).wait()
                if step:
                    self.slow_copy(piece, step).wait_send()
        self.own_copy().wait()


class PairLoad:
    ways = ("fast",)
    pieces = 0

    def __init__(self, full, lead, count):
        self.lead, self.count = lead, count
        shape, slows = full.shape[:lead] + full.shape[lead + 1 :], count // 2
        self.operands, self.in_specs = [full], [whole_vmem()]
        self.outs, self.out_specs = [jax.ShapeDtypeStruct((slows,) + shape, BF16)], [whole_vmem()]
        self.scratch = [pltpu.VMEM((slows,) + shape, BF16)] + [pltpu.SemaphoreType.DMA((slows,))] * 2

    def bind(self, given, out, scratch):
        self.full, self.out = given[0], out[0]
        self.came, self.send, self.recv = scratch
        self.me, self.slow, self.fast, self.slows = wide_places(self.count)

    def block(self, step, fast):
        owner = 2 * lax.rem(self.slow + step, self.slows) + fast
        return self.full.at[(slice(None),) * self.lead + (owner,)]

    def copy(self, step):
        return remote(
            self.block(step, 1 - self.fast), self.came.at[step], self.send.at[step], self.recv.at[step],
            {"wide": self.me + 1 - 2 * self.fast},
        )

    def start(self):
        for step in range(self.slows):
            self.copy(step).start()

    def finish(self):
        for step in range(self.slows):
            self.copy(step).wait()
            total = self.block(step, self.fast)[...].astype(F32) + self.came[step].astype(F32)
            self.out[step] = total.astype(BF16)


class LineLoad:
    ways = ("slow",)
    pieces = 0

    def __init__(self, sums, count):
        self.count = count
        slows = count // 2
        self.operands, self.in_specs = [sums], [whole_vmem()]
        self.outs, self.out_specs = [jax.ShapeDtypeStruct(sums.shape[1:], F32)], [whole_vmem()]
        self.scratch = [pltpu.VMEM(sums.shape, BF16)] + [pltpu.SemaphoreType.DMA((slows,))] * 2

    def bind(self, given, out, scratch):
        self.sums, self.out = given[0], out[0]
        self.came, self.send, self.recv = scratch
        self.me, self.slow, self.fast, self.slows = wide_places(self.count)

    def copy(self, step):
        return remote(
            self.sums.at[step], self.came.at[step], self.send.at[step], self.recv.at[step],
            {"wide": 2 * lax.rem(self.slow + step, self.slows) + self.fast},
        )

    def start(self):
        for step in range(1, self.slows):
            self.copy(step).start()

    def finish(self):
        total = self.sums[0].astype(F32)
        for step in range(1, self.slows):
            self.copy(step).wait()
            total = total + self.came[step].astype(F32)
        self.out[...] = total


def run(body, name, operands, outs, scratch, collective_id=None, loads=()):
    counts = [len(operands)] + [len(load.operands) for load in loads]
    counts += [len(outs)] + [len(load.outs) for load in loads]
    counts += [len(scratch)] + [len(load.scratch) for load in loads]
    parts = 1 + len(loads)

    def kernel(*refs):
        groups, place = [], 0
        for count in counts:
            groups.append(refs[place : place + count])
            place += count
        for k, load in enumerate(loads, 1):
            load.bind(groups[k], groups[parts + k], groups[2 * parts + k])
        main = groups[0] + groups[parts] + groups[2 * parts]
        body(*main, carry=Carry(list(loads)))

    results = pl.pallas_call(
        kernel,
        out_shape=tuple(outs) + tuple(out for load in loads for out in load.outs),
        in_specs=[whole_vmem()] * len(operands) + [spec for load in loads for spec in load.in_specs],
        out_specs=(whole_vmem(),) * len(outs) + tuple(spec for load in loads for spec in load.out_specs),
        scratch_shapes=list(scratch) + [s for load in loads for s in load.scratch],
        compiler_params=pltpu.CompilerParams(
            collective_id=collective_id,
            has_side_effects=collective_id is not None,
            vmem_limit_bytes=VMEM_LIMIT,
        ),
        name=name,
    )(*operands, *[operand for load in loads for operand in load.operands])
    return results[: len(outs)], results[len(outs) :]


def sems(kinds):
    return [pltpu.SemaphoreType.DMA((kinds, CHUNKS)), pltpu.SemaphoreType.DMA((kinds, CHUNKS))]


def norm_of(value, gain):
    scale = lax.rsqrt(jnp.mean(value * value, axis=-1, keepdims=True) + NORM_EPS)
    return value * scale * gain


def norm_back(grad, value, gain):
    scale = lax.rsqrt(jnp.mean(value * value, axis=-1, keepdims=True) + NORM_EPS)
    unit = value * scale
    scaled = grad * gain
    back = scale * (scaled - unit * jnp.mean(scaled * unit, axis=-1, keepdims=True))
    return (back, jnp.sum(grad * unit, axis=0, keepdims=True))


GELU_A = math.sqrt(2.0 / math.pi)
GELU_B = 0.044715


def gelu_of(x):
    return 0.5 * x * (1.0 + jnp.tanh(GELU_A * (x + GELU_B * (x * x * x))))


def gelu_slope(x):
    square = x * x
    t = jnp.tanh(GELU_A * (x + GELU_B * (x * square)))
    return 0.5 * (1.0 + t) + 0.5 * x * (1.0 - t * t) * (GELU_A * (1.0 + 3.0 * GELU_B * square))


def rows_at(start, j, chunk):
    return pl.ds(pl.multiple_of(start + j * chunk, chunk), chunk)


def embed_kernel(ids, extra, table, gain, resid, normed, near_out, near_in, far_out, far_in, send, recv):
    seq_len, width = normed.shape
    chunk = seq_len // 2 // CHUNKS
    sibling, partner, mine, other = group_places(seq_len)
    vocab = table.shape[1]
    first = lax.axis_index("narrow") * vocab
    greet([sibling, partner])
    trade = Exchange((near_out, near_in, far_out, far_in), (send, recv), 0, sibling, partner)
    share = Share(normed, (send, recv), 2, sibling, mine, chunk)

    def partial(start, j):
        here = ids[rows_at(start, j, chunk), :] - first
        columns = lax.broadcasted_iota(jnp.int32, (chunk, vocab), 1)
        picks = (here == columns).astype(F32).astype(BF16)
        return dot_nt(picks, table[...])

    trade.give(0, partial(other, 0))
    for j in range(CHUNKS):
        if j + 1 < CHUNKS:
            trade.give(j + 1, partial(other, j + 1))
        trade.pass_on(j, partial(mine, j))
    for j in range(CHUNKS):
        x = math.sqrt(width) * trade.take(j) + extra[rows_at(0, j, chunk), :]
        resid[rows_at(0, j, chunk), :] = x
        share.put(j, norm_of(x, gain[...]).astype(BF16))
    for j in range(CHUNKS):
        share.arrived(j)
    trade.close()
    share.close()


def embed(ids, extra, table, gain, collective_id):
    seq_len, width = ids.shape[0], table.shape[0]
    chunk = seq_len // 2 // CHUNKS
    return pl.pallas_call(
        embed_kernel,
        out_shape=(
            jax.ShapeDtypeStruct((seq_len // 2, width), F32),
            jax.ShapeDtypeStruct((seq_len, width), BF16),
        ),
        in_specs=[whole_vmem()] * 4,
        out_specs=(whole_vmem(),) * 2,
        scratch_shapes=Exchange.scratch(chunk, width, FORWARD_KIND)
        + [pltpu.SemaphoreType.DMA((3, CHUNKS)), pltpu.SemaphoreType.DMA((3, CHUNKS))],
        compiler_params=pltpu.CompilerParams(
            collective_id=collective_id, has_side_effects=True, vmem_limit_bytes=VMEM_LIMIT
        ),
        name="embed",
    )(ids, extra, table, gain)


def ffn_kernel(
    mixed, resid, w_out, w_in, w_red, gain, gain_next,
    middle, normed, before, after, result, normed_next,
    near_out, near_in, far_out, far_in, near_out2, near_in2, far_out2, far_in2, own2, send, recv, carry,
):
    seq_len = normed.shape[0]
    chunk = seq_len // 2 // CHUNKS
    sibling, partner, mine, other = group_places(seq_len)
    greet([sibling, partner] + carry.peers())
    carry.start()
    sems = (send, recv)
    first = Exchange((near_out, near_in, far_out, far_in), sems, 0, sibling, partner)
    second = Exchange((near_out2, near_in2, far_out2, far_in2), sems, 2, sibling, partner)
    share = Share(normed, sems, 4, sibling, mine, chunk)
    share_next = Share(normed_next, sems, 5, sibling, mine, chunk)

    def project(start, j):
        return dot_nt(mixed[rows_at(start, j, chunk), :], w_out[...])

    def feed(rows):
        pre = dot_nn(normed[rows, :], w_in[...])
        before[rows, :] = pre
        act = gelu_of(pre).astype(BF16)
        after[rows, :] = act
        return dot_nt(act, w_red[...])

    first.give(0, project(other, 0))
    for j in range(CHUNKS):
        if j + 1 < CHUNKS:
            first.give(j + 1, project(other, j + 1))
        first.pass_on(j, project(mine, j))
    for j in range(CHUNKS):
        rows = rows_at(0, j, chunk)
        mid = resid[rows, :] + first.take(j)
        middle[rows, :] = mid
        share.put(j, norm_of(mid, gain[...]).astype(BF16))
        own2[j] = feed(rows_at(mine, j, chunk))
        share.arrived(j)
        second.give(j, feed(rows_at(other, j, chunk)))
        if j >= 1:
            second.pass_on(j - 1, own2[j - 1])
    second.pass_on(CHUNKS - 1, own2[CHUNKS - 1])
    carry.relay(0.5)
    for j in range(CHUNKS):
        rows = rows_at(0, j, chunk)
        x = middle[rows, :] + second.take(j)
        result[rows, :] = x
        share_next.put(j, norm_of(x, gain_next[...]).astype(BF16))
        if j == CHUNKS - 2:
            carry.relay(0.75)
    for j in range(CHUNKS):
        share_next.arrived(j)
    for part in (first, second, share, share_next):
        part.close()
    carry.finish()


def ffn_forward(mixed, resid, w_out, w_in, w_red, gain, gain_next, collective_id, loads):
    seq_len, width, hidden = mixed.shape[0], w_in.shape[0], w_in.shape[1]
    half, chunk = seq_len // 2, seq_len // 2 // CHUNKS
    return run(
        ffn_kernel,
        "ffn_forward",
        [mixed, resid, w_out, w_in, w_red, gain, gain_next],
        [
            jax.ShapeDtypeStruct((half, width), F32),
            jax.ShapeDtypeStruct((seq_len, width), BF16),
            jax.ShapeDtypeStruct((seq_len, hidden), F32),
            jax.ShapeDtypeStruct((seq_len, hidden), BF16),
            jax.ShapeDtypeStruct((half, width), F32),
            jax.ShapeDtypeStruct((seq_len, width), BF16),
        ],
        Exchange.scratch(chunk, width, FORWARD_KIND)
        + Exchange.scratch(chunk, width, FORWARD_KIND)
        + [pltpu.VMEM((CHUNKS, chunk, width), F32)]
        + sems(6),
        collective_id,
        loads,
    )


TILE = 256


def weight_grad(left_t, right, out):
    columns = right.shape[1]
    tile = TILE if columns % TILE == 0 else columns

    def step(i, _):
        where = pl.ds(pl.multiple_of(i * tile, tile), tile)
        out[:, where] = dot_nn(left_t[...], right[:, where]).astype(out.dtype)
        return 0

    if tile == columns:
        out[...] = dot_nn(left_t[...], right[...]).astype(out.dtype)
    else:
        lax.fori_loop(0, columns // tile, step, 0)


def ffn_back_kernel(
    grad, branch, w_red, w_in, w_out, before, after, normed, middle, gain, mixed,
    grad_middle, grad_attn, grad_mixed, d_red, d_in, d_out, d_gain,
    grad_before, turned, near_out, near_in, far_out, far_in, send, recv, carry,
):
    seq_len = normed.shape[0]
    chunk = seq_len // 2 // CHUNKS
    sibling, partner, mine, other = group_places(seq_len)
    greet([sibling, partner] + carry.peers())
    carry.start()
    sems = (send, recv)
    trade = Exchange((near_out, near_in, far_out, far_in), sems, 0, sibling, partner)
    share = Share(grad_attn, sems, 2, sibling, mine, chunk)

    def partial(start, j):
        rows = rows_at(start, j, chunk)
        back = dot_nn(branch[rows, :], w_red[...])
        low = (back * gelu_slope(before[rows, :])).astype(BF16)
        grad_before[rows, :] = low
        return dot_nt(low, w_in[...])

    trade.give(0, partial(other, 0))
    for j in range(CHUNKS):
        if j + 1 < CHUNKS:
            trade.give(j + 1, partial(other, j + 1))
        trade.pass_on(j, partial(mine, j))
    turned[...] = jnp.transpose(branch[...])
    weight_grad(turned, after, d_red)
    turned[...] = jnp.transpose(normed[...])
    weight_grad(turned, grad_before, d_in)
    gain_total = jnp.zeros(gain.shape, F32)
    for j in range(CHUNKS):
        rows = rows_at(0, j, chunk)
        back, gain_part = norm_back(trade.take(j), middle[rows, :], gain[...])
        gain_total = gain_total + gain_part
        total = back + grad[rows, :]
        grad_middle[rows, :] = total
        share.put(j, total.astype(BF16))
        here = rows_at(mine, j, chunk)
        grad_mixed[here, :] = dot_nn(grad_attn[here, :], w_out[...]).astype(BF16)
    for j in range(CHUNKS):
        share.arrived(j)
        here = rows_at(other, j, chunk)
        grad_mixed[here, :] = dot_nn(grad_attn[here, :], w_out[...]).astype(BF16)
    d_gain[...] = gain_total
    turned[...] = jnp.transpose(grad_attn[...])
    weight_grad(turned, mixed, d_out)
    trade.close()
    share.close()
    carry.finish()


def ffn_backward(grad, branch, w_red, w_in, w_out, before, after, normed, middle, gain, mixed, collective_id, loads):
    seq_len, width = normed.shape
    half, chunk = seq_len // 2, seq_len // 2 // CHUNKS
    return run(
        ffn_back_kernel,
        "ffn_backward",
        [grad, branch, w_red, w_in, w_out, before, after, normed, middle, gain, mixed],
        [
            jax.ShapeDtypeStruct((half, width), F32),
            jax.ShapeDtypeStruct((seq_len, width), BF16),
            jax.ShapeDtypeStruct(mixed.shape, BF16),
            jax.ShapeDtypeStruct(w_red.shape, BF16),
            jax.ShapeDtypeStruct(w_in.shape, BF16),
            jax.ShapeDtypeStruct(w_out.shape, BF16),
            jax.ShapeDtypeStruct(gain.shape, F32),
        ],
        [pltpu.VMEM(before.shape, BF16), pltpu.VMEM((width, seq_len), BF16)]
        + Exchange.scratch(chunk, width, BACKWARD_KIND)
        + sems(3),
        collective_id,
        loads,
    )


def norm_back_kernel(
    scale, grads, weights, normed, value, gain, upstream,
    grad_out, branch, d_weights, d_gain,
    turned, near_out, near_in, far_out, far_in, send, recv, carry,
):
    seq_len, width = normed.shape
    chunk = seq_len // 2 // CHUNKS
    sibling, partner, mine, other = group_places(seq_len)
    greet([sibling, partner] + carry.peers())
    carry.start()
    sems = (send, recv)
    trade = Exchange((near_out, near_in, far_out, far_in), sems, 0, sibling, partner)
    share = Share(branch, sems, 2, sibling, mine, chunk)

    def partial(start, j):
        rows = rows_at(start, j, chunk)
        total = None
        for which in range(grads.shape[0]):
            part = dot_nt(grads[which, rows, :], weights[which])
            total = part if total is None else total + part
        return total

    trade.give(0, partial(other, 0))
    for j in range(CHUNKS):
        if j + 1 < CHUNKS:
            trade.give(j + 1, partial(other, j + 1))
        trade.pass_on(j, partial(mine, j))
    turned[...] = jnp.transpose(normed[...])
    for which in range(grads.shape[0]):
        weight_grad(turned, grads.at[which], d_weights.at[which])
    gain_total = jnp.zeros(gain.shape, F32)
    for j in range(CHUNKS):
        rows = rows_at(0, j, chunk)
        back, gain_part = norm_back(trade.take(j), value[rows, :], gain[...])
        gain_total = gain_total + gain_part
        back = back + upstream[rows, :]
        grad_out[rows, :] = back
        share.put(j, (back if scale is None else scale * back).astype(BF16))
    d_gain[...] = gain_total
    for j in range(CHUNKS):
        share.arrived(j)
    trade.close()
    share.close()
    carry.finish()


def norm_backward(grads, weights, normed, value, gain, upstream, scale, collective_id, loads):
    seq_len, width = normed.shape
    half, chunk = seq_len // 2, seq_len // 2 // CHUNKS
    return run(
        functools.partial(norm_back_kernel, scale),
        "norm_backward",
        [grads, weights, normed, value, gain, upstream],
        [
            jax.ShapeDtypeStruct((half, width), F32),
            jax.ShapeDtypeStruct((seq_len, width), BF16),
            jax.ShapeDtypeStruct(weights.shape, BF16),
            jax.ShapeDtypeStruct(gain.shape, F32),
        ],
        [pltpu.VMEM((width, seq_len), BF16)] + Exchange.scratch(chunk, width, BACKWARD_KIND) + sems(3),
        collective_id,
        loads,
    )


def wide_places(count):
    me = lax.axis_index("wide")
    fast = lax.rem(me, 2)
    slow = me // 2
    return (me, slow, fast, count // 2)


def gather_kernel(arrays, lead, *refs):
    shards, outs = refs[:arrays], refs[arrays : 2 * arrays]
    lows = refs[2 * arrays : 3 * arrays]
    local, slow_send, slow_recv, fast_send, fast_recv = refs[3 * arrays :]
    count = outs[0].shape[lead[0]]
    me, slow, fast, slows = wide_places(count)
    beside = me + 1 - 2 * fast

    def at(which, owner):
        out = outs[which]
        return out.at[(slice(None),) * lead[which] + (owner,)]

    def along(step):
        return 2 * lax.rem(slow + step, slows) + fast

    def back(step):
        return 2 * lax.rem(slow + slows - step, slows) + fast

    def slow_copy(which, step):
        return remote(
            lows[which], at(which, me), slow_send.at[which, step - 1], slow_recv.at[which, step - 1],
            {"wide": along(step)},
        )

    def fast_copy(which, step):
        block = at(which, back(step))
        return remote(
            lows[which] if step == 0 else block, block, fast_send.at[which, step], fast_recv.at[which, step],
            {"wide": beside},
        )

    greet([{"wide": along(step)} for step in range(1, slows)] + [{"wide": beside}])
    for which in range(arrays):
        lows[which][...] = shards[which][...].astype(lows[which].dtype)
        for step in range(1, slows):
            slow_copy(which, step).start()
        fast_copy(which, 0).start()
        pltpu.make_async_copy(lows[which], at(which, me), local.at[which]).start()
    for which in range(arrays):
        for step in range(1, slows):
            slow_copy(which, step).wait_recv()
            fast_copy(which, step).start()
    for which in range(arrays):
        for step in range(slows):
            fast_copy(which, step).wait()
            if step:
                slow_copy(which, step).wait_send()
        pltpu.make_async_copy(lows[which], at(which, me), local.at[which]).wait()


def gather_wide(shards, leads, kinds, count, collective_id):
    arrays = len(shards)
    slows = count // 2
    return pl.pallas_call(
        functools.partial(gather_kernel, arrays, leads),
        out_shape=tuple(
            jax.ShapeDtypeStruct(s.shape[:lead] + (count,) + s.shape[lead:], kind)
            for s, lead, kind in zip(shards, leads, kinds)
        ),
        in_specs=[whole_vmem()] * arrays,
        out_specs=(pl.BlockSpec(memory_space=pl.ANY),) * arrays,
        scratch_shapes=[pltpu.VMEM(s.shape, kind) for s, kind in zip(shards, kinds)]
        + [
            pltpu.SemaphoreType.DMA((arrays,)),
            pltpu.SemaphoreType.DMA((arrays, slows - 1)),
            pltpu.SemaphoreType.DMA((arrays, slows - 1)),
            pltpu.SemaphoreType.DMA((arrays, slows)),
            pltpu.SemaphoreType.DMA((arrays, slows)),
        ],
        compiler_params=pltpu.CompilerParams(
            collective_id=collective_id, has_side_effects=True, vmem_limit_bytes=VMEM_LIMIT
        ),
        name="gather_weights",
    )(*shards)


def scatter_kernel(arrays, lead, *refs, carry):
    fulls, outs = refs[:arrays], refs[arrays : 2 * arrays]
    fast_in = refs[2 * arrays : 3 * arrays]
    sums = refs[3 * arrays : 4 * arrays]
    slow_in = refs[4 * arrays : 5 * arrays]
    paired, paired_in, fast_send, fast_recv, slow_send, slow_recv, near_send, near_recv = refs[5 * arrays :]
    count = fulls[0].shape[lead[0]]
    me, slow, fast, slows = wide_places(count)
    beside = me + 1 - 2 * fast
    place = lax.axis_index("narrow")
    sibling = {"narrow": place + 1 - 2 * lax.rem(place, 2)}
    sources = list(fulls[:-1]) + [paired]

    def block(which, owner):
        return sources[which].at[(slice(None),) * lead[which] + (owner,)]

    def along(step):
        return lax.rem(slow + step, slows)

    def fast_copy(which, step):
        owner = 2 * along(step) + 1 - fast
        return remote(
            block(which, owner), fast_in[which].at[step], fast_send.at[which, step], fast_recv.at[which, step],
            {"wide": beside},
        )

    def slow_copy(which, step):
        return remote(
            sums[which].at[step - 1], slow_in[which].at[step - 1],
            slow_send.at[which, step - 1], slow_recv.at[which, step - 1],
            {"wide": 2 * along(step) + fast},
        )

    greet([{"wide": 2 * along(step) + fast} for step in range(1, slows)] + [{"wide": beside}, sibling])
    carry.start()
    near = remote(fulls[-1], paired_in, near_send, near_recv, sibling)
    near.start()
    for which in range(arrays):
        if which == arrays - 1:
            near.wait()
            paired[...] = fulls[-1][...] + paired_in[...]
        for step in list(range(1, slows)) + [0]:
            fast_copy(which, step).start()
    for which in range(arrays):
        for step in range(1, slows):
            fast_copy(which, step).wait_recv()
            owner = 2 * along(step) + fast
            total = block(which, owner)[...].astype(F32) + fast_in[which][step].astype(F32)
            sums[which][step - 1] = total.astype(sums[which].dtype)
            slow_copy(which, step).start()
    for which in range(arrays):
        fast_copy(which, 0).wait_recv()
        total = block(which, me)[...].astype(F32) + fast_in[which][0].astype(F32)
        for step in range(1, slows):
            slow_copy(which, step).wait_recv()
            total = total + slow_in[which][step - 1].astype(F32)
        outs[which][...] = total
    for which in range(arrays):
        for step in range(slows):
            fast_copy(which, step).wait_send()
            if step:
                slow_copy(which, step).wait_send()
    carry.finish()


def scatter_wide(fulls, leads, collective_id, loads):
    arrays = len(fulls)
    slows = fulls[0].shape[leads[0]] // 2
    shapes = [f.shape[:lead] + f.shape[lead + 1 :] for f, lead in zip(fulls, leads)]
    kinds = [f.dtype for f in fulls]
    return run(
        functools.partial(scatter_kernel, arrays, leads),
        "scatter_grads",
        fulls,
        [jax.ShapeDtypeStruct(shape, F32) for shape in shapes],
        [pltpu.VMEM((slows,) + shape, kind) for shape, kind in zip(shapes, kinds)]
        + [pltpu.VMEM((slows - 1,) + shape, kind) for shape, kind in zip(shapes, kinds)]
        + [pltpu.VMEM((slows - 1,) + shape, kind) for shape, kind in zip(shapes, kinds)]
        + [pltpu.VMEM(fulls[-1].shape, F32)] * 2
        + [
            pltpu.SemaphoreType.DMA((arrays, slows)),
            pltpu.SemaphoreType.DMA((arrays, slows)),
            pltpu.SemaphoreType.DMA((arrays, slows - 1)),
            pltpu.SemaphoreType.DMA((arrays, slows - 1)),
            pltpu.SemaphoreType.DMA,
            pltpu.SemaphoreType.DMA,
        ],
        collective_id,
        loads,
    )


def head_lanes(value, head, size):
    lanes = lax.broadcasted_iota(jnp.int32, value.shape, 1)
    inside = (lanes >= head * size) & (lanes < (head + 1) * size)
    return jnp.where(inside, value, jnp.zeros_like(value))


def attention_kernel(normed, weights, key_seg, query_seg, projected, mixed, bias, values_t):
    seq_len = normed.shape[0]
    width = mixed.shape[1]
    block = bias.shape[1]
    heads = width // HD

    def project(i, _):
        rows = rows_at(0, i, block)
        for which in range(3):
            projected[which, rows, :] = dot_nn(normed[rows, :], weights[which]).astype(BF16)
        return 0

    lax.fori_loop(0, seq_len // block, project, 0)
    values_t[...] = jnp.transpose(projected[2])

    def queries(i, _):
        rows = rows_at(0, i, block)
        bias[...] = jnp.where(key_seg[...] == query_seg[:, rows], 0.0, -1e30)
        asked = projected[0, rows, :] * HD ** (-0.5)
        parts = []
        for head in range(heads):
            scores = dot_nt(projected[1], head_lanes(asked, head, HD)) + bias[...]
            powers = jnp.exp(scores - jnp.max(scores, axis=0, keepdims=True))
            probs = (powers * (1.0 / jnp.sum(powers, axis=0, keepdims=True))).astype(BF16)
            parts.append(dot_nn(values_t[head * HD : (head + 1) * HD, :], probs))
        mixed[rows, :] = jnp.transpose(jnp.concatenate(parts, axis=0)).astype(BF16)
        return 0

    lax.fori_loop(0, seq_len // block, queries, 0)


QUERY_BLOCK = 256


def attention(normed, weights, key_seg, query_seg):
    seq_len, width = normed.shape[0], weights.shape[2]
    block = min(QUERY_BLOCK, seq_len)
    return pl.pallas_call(
        attention_kernel,
        out_shape=(
            jax.ShapeDtypeStruct((3, seq_len, width), BF16),
            jax.ShapeDtypeStruct((seq_len, width), BF16),
        ),
        in_specs=[whole_vmem()] * 4,
        out_specs=(whole_vmem(),) * 2,
        scratch_shapes=[pltpu.VMEM((seq_len, block), F32), pltpu.VMEM((width, seq_len), BF16)],
        compiler_params=pltpu.CompilerParams(vmem_limit_bytes=VMEM_LIMIT),
        name="attention",
    )(normed, weights, key_seg, query_seg)


def attention_back_kernel(projected, grad_mixed, key_seg, query_seg, out, bias, keys_t, grad_keys, grad_values, carry):
    seq_len, width = grad_mixed.shape
    block = bias.shape[1]
    heads = width // HD
    scale = HD ** (-0.5)
    if carry.loads:
        greet(carry.peers())
    carry.start()
    keys_t[...] = jnp.transpose(projected[1])
    grad_keys[...] = jnp.zeros(grad_keys.shape, F32)
    grad_values[...] = jnp.zeros(grad_values.shape, F32)

    def queries(i, _):
        rows = rows_at(0, i, block)
        bias[...] = jnp.where(key_seg[...] == query_seg[:, rows], 0.0, -1e30)
        asked = projected[0, rows, :] * scale
        given = grad_mixed[rows, :]
        parts = []
        for head in range(heads):
            query = head_lanes(asked, head, HD)
            grad = head_lanes(given, head, HD)
            scores = dot_nt(projected[1], query) + bias[...]
            powers = jnp.exp(scores - jnp.max(scores, axis=0, keepdims=True))
            probs = powers * (1.0 / jnp.sum(powers, axis=0, keepdims=True))
            grad_probs = dot_nt(projected[2], grad)
            centre = jnp.sum(probs * grad_probs, axis=0, keepdims=True)
            grad_scores = (probs * (grad_probs - centre)).astype(BF16)
            parts.append(dot_nn(keys_t[head * HD : (head + 1) * HD, :], grad_scores))
            grad_keys[...] += dot_nn(grad_scores, query)
            grad_values[...] += dot_nn(probs.astype(BF16), grad)
        out[0, rows, :] = (jnp.transpose(jnp.concatenate(parts, axis=0)) * scale).astype(BF16)
        return 0

    lax.fori_loop(0, seq_len // block, queries, 0)
    out[1] = grad_keys[...].astype(BF16)
    out[2] = grad_values[...].astype(BF16)
    carry.finish()


def attention_back(projected, grad_mixed, key_seg, query_seg, collective_id, loads):
    seq_len, width = grad_mixed.shape
    block = min(QUERY_BLOCK, seq_len)
    return run(
        attention_back_kernel,
        "attention_back",
        [projected, grad_mixed, key_seg, query_seg],
        [jax.ShapeDtypeStruct(projected.shape, BF16)],
        [
            pltpu.VMEM((seq_len, block), F32),
            pltpu.VMEM((width, seq_len), BF16),
            pltpu.VMEM((seq_len, width), F32),
            pltpu.VMEM((seq_len, width), F32),
        ],
        collective_id if loads else None,
        loads,
    )


LANES = 128


def spread(row):
    return jnp.transpose(jnp.broadcast_to(row, (LANES, LANES)))


def to_rows(columns):
    lanes = lax.broadcasted_iota(jnp.int32, (LANES, LANES), 1)
    total = jnp.zeros((LANES, LANES), F32)
    for k, column in enumerate(columns):
        total = jnp.where(lanes == k, column, total)
    return jnp.transpose(total)[:8, :]


def loss_kernel(
    normed, table, info, value, gain,
    grad_out, branch, d_table, d_gain, losses,
    logits, grads, places, turned, stat_out, stat_in, sum_out, sum_in,
    near_out, near_in, far_out, far_in, send, recv, stat_send, stat_recv, sum_send, sum_recv,
):
    seq_len, width = normed.shape
    chunk = seq_len // 2 // CHUNKS
    vocab = table.shape[1]
    tiles = vocab // LANES
    blocks = seq_len // LANES
    me = lax.axis_index("narrow")
    sibling, partner, mine, other = group_places(seq_len)
    peers = [{"narrow": lax.rem(me + k, 4)} for k in range(1, 4)]
    greet(peers)
    sems = (send, recv)
    trade = Exchange((near_out, near_in, far_out, far_in), sems, 0, sibling, partner)
    share = Share(branch, sems, 2, sibling, mine, chunk)
    first = (me * vocab).astype(F32)
    whole = 4.0 * vocab
    lanes = lax.broadcasted_iota(jnp.int32, (LANES, LANES), 1).astype(F32)

    def stat_copy(b, k):
        return remote(stat_out.at[b], stat_in.at[k, b], stat_send.at[k, b], stat_recv.at[k, b], peers[k])

    def sum_copy(b, k):
        return remote(sum_out.at[b], sum_in.at[k, b], sum_send.at[k, b], sum_recv.at[k, b], peers[k])

    def tile_at(t):
        return pl.ds(pl.multiple_of(t * LANES, LANES), LANES)

    def ask(b, _):
        rows = rows_at(0, b, LANES)
        logits[rows, :] = dot_nn(normed[rows, :], table[...])
        here = info[:, rows]
        at_noised = spread(here[0:1] - first)
        at_clean = spread(here[1:2] - first)
        places[b, 0] = at_noised
        places[b, 1] = at_clean

        def top_step(t, top):
            return jnp.maximum(top, logits[rows, tile_at(t)])

        top = lax.fori_loop(1, tiles, top_step, logits[rows, tile_at(0)], unroll=4)
        top = jnp.max(top, axis=1, keepdims=True)
        top_wide = jnp.broadcast_to(top, (LANES, LANES))

        def sum_step(t, totals):
            powers, noised, clean = totals
            piece = logits[rows, tile_at(t)]
            column = lanes + (t * LANES).astype(F32)
            return (
                powers + jnp.exp(piece - top_wide),
                noised + jnp.where(column == at_noised, piece, 0.0),
                clean + jnp.where(column == at_clean, piece, 0.0),
            )

        zero = jnp.zeros((LANES, LANES), F32)
        totals = lax.fori_loop(0, tiles, sum_step, (zero, zero, zero))
        stat_out[b] = to_rows([top] + [jnp.sum(total, axis=1, keepdims=True) for total in totals])
        for k in range(3):
            stat_copy(b, k).start()
        return 0

    lax.fori_loop(0, blocks, ask, 0)

    def scalars(b):
        here = info[:, rows_at(0, b, LANES)]
        step = jnp.maximum(here[2:3], 2.0)
        left = STEPS - step + 1.0
        beta = 1.0 / left
        keep = left / STEPS
        rest = (step - 1.0) / (STEPS * whole)
        own = stat_out[b]
        others = [stat_in[k, b] for k in range(3)]
        top = own[0:1]
        for stat in others:
            top = jnp.maximum(top, stat[0:1])
        total = own[1:2] * jnp.exp(own[0:1] - top)
        noised, clean = own[2:3], own[3:4]
        for stat in others:
            total = total + stat[1:2] * jnp.exp(stat[0:1] - top)
            noised, clean = noised + stat[2:3], clean + stat[3:4]
        return here, beta, keep, rest, top + jnp.log(total), noised, clean

    def measure(b, _):
        rows = rows_at(0, b, LANES)
        for k in range(3):
            stat_copy(b, k).wait_recv()
        _, _, keep, rest, log_total, _, _ = scalars(b)
        log_wide = spread(log_total)
        ratio = spread(keep / rest)

        def step(t, totals):
            logs, shares = totals
            probs = jnp.exp(logits[rows, tile_at(t)] - log_wide)
            logits[rows, tile_at(t)] = probs
            grown = 1.0 + probs * ratio
            return (logs + jnp.log(grown), shares + probs / grown)

        zero = jnp.zeros((LANES, LANES), F32)
        totals = lax.fori_loop(0, tiles, step, (zero, zero))
        sum_out[b] = to_rows([jnp.sum(total, axis=1, keepdims=True) for total in totals])
        for k in range(3):
            sum_copy(b, k).start()
        return 0

    lax.fori_loop(0, blocks, measure, 0)

    def pull(b):
        rows = rows_at(0, b, LANES)
        for k in range(3):
            sum_copy(b, k).wait_recv()
        here, beta, keep, rest, log_total, noised, clean = scalars(b)
        sums = sum_out[b] + sum_in[0, b] + sum_in[1, b] + sum_in[2, b]
        log_sum, share_sum = sums[0:1], sums[1:2] / rest
        same = here[0:1] == here[1:2]
        first_step = here[2:3] == 1.0
        base_a, more_a = beta / whole, 1.0 - beta
        base_w = base_a * rest
        joint = whole * base_w + more_a * rest + base_a * keep + jnp.where(same, more_a * keep, 0.0)
        ratio = keep / rest
        prob_n, prob_c = jnp.exp(noised - log_total), jnp.exp(clean - log_total)
        grown_n, grown_c = 1.0 + prob_n * ratio, 1.0 + prob_c * ratio
        marginal_n, marginal_c = rest * grown_n, rest * grown_c
        log_n, log_c = jnp.log(grown_n), jnp.log(grown_c)
        weight_n = jnp.where(same, 0.0, more_a * rest)
        weight_c = jnp.where(same, more_a * rest + base_a * keep + more_a * keep, base_a * keep)
        lift = jnp.log((keep + rest) / rest)
        cross = -base_w * log_sum - weight_n * log_n - weight_c * log_c + (base_w + weight_c) * lift
        model = base_a * (keep + whole * rest) + more_a * marginal_n
        divergence = cross / joint - jnp.log(joint) + jnp.log(model)
        loss = jnp.where(first_step, log_total - clean, divergence)
        losses[:, rows] = here[4:5] * loss
        weighted = base_w * share_sum + weight_n * prob_n / marginal_n + weight_c * prob_c / marginal_c
        aligned = base_a + more_a * prob_n
        centre = keep * (aligned / model - weighted / joint)
        scale = here[3:4]
        zero = jnp.zeros_like(scale)
        even = scale * jnp.where(first_step, 1.0, keep * base_a / model - centre)
        bent = scale * jnp.where(first_step, zero, -keep * base_w / joint / rest)
        at_n = prob_n * keep * (more_a / model - weight_n / joint / marginal_n)
        at_c = -prob_c * keep * (weight_c / joint / marginal_c)
        extra_n = spread(scale * jnp.where(first_step, zero, at_n))
        extra_c = spread(scale * jnp.where(first_step, -1.0, at_c))
        even, bent, ratio = spread(even), spread(bent), spread(ratio)
        at_noised, at_clean = places[b, 0], places[b, 1]

        def step(t, _):
            probs = logits[rows, tile_at(t)]
            column = lanes + (t * LANES).astype(F32)
            grad = probs * (even + bent / (1.0 + probs * ratio))
            grad = grad + jnp.where(column == at_noised, extra_n, 0.0)
            grad = grad + jnp.where(column == at_clean, extra_c, 0.0)
            grads[rows, tile_at(t)] = grad.astype(BF16)
            return 0

        lax.fori_loop(0, tiles, step, 0)

    def partial(start, j):
        base = start // LANES + j * (chunk // LANES)
        for b in range(chunk // LANES):
            pull(base + b)
        return dot_nt(grads[rows_at(start, j, chunk), :], table[...])

    trade.give(0, partial(other, 0))
    for j in range(CHUNKS):
        if j + 1 < CHUNKS:
            trade.give(j + 1, partial(other, j + 1))
        trade.pass_on(j, partial(mine, j))
    turned[...] = jnp.transpose(normed[...])
    weight_grad(turned, grads, d_table)
    gain_total = jnp.zeros(gain.shape, F32)
    for j in range(CHUNKS):
        rows = rows_at(0, j, chunk)
        back, gain_part = norm_back(trade.take(j), value[rows, :], gain[...])
        gain_total = gain_total + gain_part
        grad_out[rows, :] = back
        share.put(j, back.astype(BF16))
    d_gain[...] = gain_total
    for j in range(CHUNKS):
        share.arrived(j)
    trade.close()
    share.close()

    def finish(b, _):
        for k in range(3):
            stat_copy(b, k).wait_send()
            sum_copy(b, k).wait_send()
        return 0

    lax.fori_loop(0, blocks, finish, 0)


def loss_and_back(normed, table, info, value, gain, collective_id):
    seq_len, width = normed.shape
    vocab = table.shape[1]
    half, chunk, blocks = seq_len // 2, seq_len // 2 // CHUNKS, seq_len // LANES
    return pl.pallas_call(
        loss_kernel,
        out_shape=(
            jax.ShapeDtypeStruct((half, width), F32),
            jax.ShapeDtypeStruct((seq_len, width), BF16),
            jax.ShapeDtypeStruct(table.shape, BF16),
            jax.ShapeDtypeStruct(gain.shape, F32),
            jax.ShapeDtypeStruct((1, seq_len), F32),
        ),
        in_specs=[whole_vmem()] * 5,
        out_specs=(whole_vmem(),) * 5,
        scratch_shapes=[
            pltpu.VMEM((seq_len, vocab), F32),
            pltpu.VMEM((seq_len, vocab), BF16),
            pltpu.VMEM((blocks, 2, LANES, LANES), F32),
            pltpu.VMEM((width, seq_len), BF16),
            pltpu.VMEM((blocks, 8, LANES), F32),
            pltpu.VMEM((3, blocks, 8, LANES), F32),
            pltpu.VMEM((blocks, 8, LANES), F32),
            pltpu.VMEM((3, blocks, 8, LANES), F32),
        ]
        + Exchange.scratch(chunk, width, BACKWARD_KIND)
        + [pltpu.SemaphoreType.DMA((3, CHUNKS)), pltpu.SemaphoreType.DMA((3, CHUNKS))]
        + [pltpu.SemaphoreType.DMA((3, blocks))] * 4,
        compiler_params=pltpu.CompilerParams(
            collective_id=collective_id, has_side_effects=True, vmem_limit_bytes=VMEM_LIMIT
        ),
        name="loss_and_back",
    )(normed, table, info, value, gain)


def scalars_kernel(given, out, near, along, across, send, recv):
    count = 2 * along.shape[0]
    me, slow, fast, slows = wide_places(count)
    place = lax.axis_index("narrow")
    beside = me + 1 - 2 * fast
    group = near.shape[0]

    def near_copy(step):
        return remote(
            near.at[place], near.at[place], send.at[0, step - 1], recv.at[0, step - 1],
            {"narrow": lax.rem(place + step, group)},
        )

    def along_copy(step):
        return remote(
            along.at[slow], along.at[slow], send.at[1, step - 1], recv.at[1, step - 1],
            {"wide": 2 * lax.rem(slow + step, slows) + fast},
        )

    greet(
        [{"narrow": lax.rem(place + step, group)} for step in range(1, group)]
        + [{"wide": 2 * lax.rem(slow + step, slows) + fast} for step in range(1, slows)]
        + [{"wide": beside}]
    )
    near[place] = given[...]
    for step in range(1, group):
        near_copy(step).start()
    for step in range(1, group):
        near_copy(step).wait()
    along[slow] = jnp.sum(near[...], axis=0)
    for step in range(1, slows):
        along_copy(step).start()
    for step in range(1, slows):
        along_copy(step).wait()
    across[0] = jnp.sum(along[...], axis=0)
    last = remote(across.at[0], across.at[1], send.at[2, 0], recv.at[2, 0], {"wide": beside})
    last.start()
    last.wait()
    out[...] = across[0] + across[1]


def sum_scalars(given, wide, narrow, collective_id):
    steps = max(wide // 2, narrow) - 1
    return pl.pallas_call(
        scalars_kernel,
        out_shape=jax.ShapeDtypeStruct(given.shape, F32),
        in_specs=[whole_vmem()],
        out_specs=whole_vmem(),
        scratch_shapes=[
            pltpu.VMEM((narrow,) + given.shape, F32),
            pltpu.VMEM((wide // 2,) + given.shape, F32),
            pltpu.VMEM((2,) + given.shape, F32),
            pltpu.SemaphoreType.DMA((3, steps)),
            pltpu.SemaphoreType.DMA((3, steps)),
        ],
        compiler_params=pltpu.CompilerParams(collective_id=collective_id, has_side_effects=True),
        name="sum_scalars",
    )(given)


def shares_tile(wide, narrow, noised, attn_in, attn_out, ffn_in):
    rows, seq_len = noised.shape
    return (
        narrow == 4
        and wide % 2 == 0
        and rows == 1
        and seq_len % (2 * CHUNKS * 128) == 0
        and attn_out.shape[1] % 16 == 0
        and ffn_in.shape[2] % 128 == 0
    )


def per_device(wide, narrow, *arrays):
    noised, attn_in, attn_out, ffn_in = arrays[0], arrays[5], arrays[6], arrays[7]
    if shares_tile(wide, narrow, noised, attn_in, attn_out, ffn_in):
        return tiled_device(wide, *arrays)
    return general_device(*arrays)


def tiled_device(
    wide,
    noised,
    clean,
    timesteps,
    segments,
    counted,
    attn_in,
    attn_out,
    ffn_in,
    ffn_out,
    tables,
    gains,
    attn_in_mean,
    attn_out_mean,
    ffn_in_mean,
    ffn_out_mean,
    tables_mean,
    gains_mean,
    attn_in_square,
    attn_out_square,
    ffn_in_square,
    ffn_out_square,
    tables_square,
    gains_square,
):
    layers = attn_in.shape[0]
    gain_rows, gain_cols = gains.shape
    mask = counted.reshape(-1).astype(jnp.float32)
    seq_len = mask.shape[0]
    half = seq_len // 2
    core = lax.rem(lax.axis_index("narrow"), 2)
    small = jnp.pad(
        jnp.concatenate(
            [
                lax.reduce_precision(gains, 8, 7),
                jnp.full((1, gain_cols), jnp.sum(mask), jnp.float32),
            ]
        ),
        ((0, -(gain_rows + 1) % 8), (0, -gain_cols % 128)),
    )
    first_layer = [attn_in[0], attn_out[0], ffn_in[0], ffn_out[0]]
    leads = (1, 0, 0, 0)
    small_all, table_first, *weights = gather_wide(
        [small, tables[0]] + first_layer, (0, 0) + leads, [F32] + [BF16] * 5, wide, 0
    )
    token_total = jnp.sum(small_all[:, gain_rows, 0])
    gain_w = small_all[:, :gain_rows, :gain_cols].transpose(1, 0, 2).reshape(gain_rows, 1, -1)
    table_first = table_first.reshape(-1, tables.shape[2])

    def joined(value, lead):
        return value.reshape(value.shape[:lead] + (-1,) + value.shape[lead + 2 :])

    noised_flat = noised.reshape(-1)
    clean_flat = clean.reshape(-1)
    step_flat = timesteps.reshape(-1)
    vocab_local = tables.shape[2]
    vocab_ids = lax.axis_index("narrow") * vocab_local + jnp.arange(vocab_local, dtype=jnp.int32)
    extra = time_features(lax.dynamic_slice(step_flat, (core * half,), (half,)))
    residual, normed = embed(noised_flat[:, None], extra, table_first, gain_w[0], 1)
    key_seg, query_seg = segments.reshape(-1, 1), segments.reshape(1, -1)
    kept = []
    for layer in range(layers):
        query_w, output_w, expand_w, reduce_w = four = [joined(value, lead) for value, lead in zip(weights, leads)]
        if layer + 1 < layers:
            loads = [
                GatherLoad(value, layer + 1, lead, wide)
                for value, lead in zip((attn_in, attn_out, ffn_in, ffn_out), leads)
            ]
        else:
            loads = [GatherLoad(tables, 1, 0, wide, 3)]
        projected, mixed = attention(normed, query_w, key_seg, query_seg)
        (middle, normed_two, before, after, result, normed_next), weights = ffn_forward(
            mixed, residual, output_w, expand_w, reduce_w,
            gain_w[2 * layer + 1], gain_w[2 * layer + 2], 2 + layer, loads,
        )
        kept.append((residual, normed, projected, mixed, middle, normed_two, before, after, four))
        residual, normed = result, normed_next
    table_last = joined(weights[0], 0)

    info = jnp.stack(
        [noised_flat.astype(F32), clean_flat.astype(F32), step_flat.astype(F32), mask / token_total, mask]
        + [jnp.zeros_like(mask)] * 3
    )
    grad, branch, d_last, gain_final, losses = loss_and_back(
        normed, table_last, info, residual, gain_w[2 * layers], 2 + layers
    )
    next_id = 3 + layers
    gain_grads = [None] * (2 * layers) + [gain_final]
    own = {}

    def by_owner(value, lead):
        shape = value.shape
        return value.reshape(shape[:lead] + (wide, shape[lead] // wide) + shape[lead + 1 :])

    class Route:
        waiting, halfway = [], []

        def take(self, pairs, lines):
            self.now = self.waiting[:pairs], self.halfway[:lines]
            self.waiting, self.halfway = self.waiting[pairs:], self.halfway[lines:]
            return [PairLoad(by_owner(value, lead), lead, wide) for _, value, lead in self.now[0]] + [
                LineLoad(sums, wide) for _, sums in self.now[1]
            ]

        def back(self, results):
            pairs, lines = self.now
            self.halfway = self.halfway + [(key, sums) for (key, _, _), sums in zip(pairs, results)]
            for (key, _), total in zip(lines, results[len(pairs) :]):
                own[key] = total

    route = Route()
    route.waiting = [(("tables", 1), d_last, 0)]
    for layer in reversed(range(layers)):
        residual, normed, projected, mixed, middle, normed_two, before, after, four = kept[layer]
        query_w, output_w, expand_w, reduce_w = four
        top = layer == layers - 1
        loads = route.take(1, 3)
        (grad_middle, grad_attn, grad_mixed, d_red, d_in, d_out, gain_two), carried = ffn_backward(
            grad, branch, reduce_w, expand_w, output_w, before, after,
            normed_two, middle, gain_w[2 * layer + 1], mixed, next_id, loads,
        )
        route.back(carried)
        route.waiting += [(("ffn_out", layer), d_red, 0), (("ffn_in", layer), d_in, 0)]
        loads = route.take(1, 0 if top else 1)
        (grad_projected,), carried = attention_back(projected, grad_mixed, key_seg, query_seg, next_id + 1, loads)
        route.back(carried)
        route.waiting += [(("attn_out", layer), d_out, 0)]
        loads = route.take(3, 1)
        (grad, branch, d_query, gain_one), carried = norm_backward(
            grad_projected, query_w, normed, residual, gain_w[2 * layer], grad_middle,
            math.sqrt(D) if layer == 0 else None, next_id + 2, loads,
        )
        route.back(carried)
        route.waiting += [(("attn_in", layer), d_query, 1)]
        next_id += 3
        gain_grads[2 * layer], gain_grads[2 * layer + 1] = gain_one, gain_two
    picks = (noised_flat[:, None] == vocab_ids[None, :]).astype(jnp.bfloat16)
    d_first = jnp.einsum("sd,sv->dv", branch, picks, preferred_element_type=jnp.float32)

    small_grad = jnp.pad(
        jnp.concatenate(gain_grads).reshape(gain_rows, wide, gain_cols).transpose(1, 0, 2),
        ((0, 0), (0, -gain_rows % 8), (0, -gain_cols % 128)),
    )
    rest = route.waiting + [(("tables", 0), d_first.astype(BF16), 0)]
    lines = route.halfway
    (*sums, total_small), carried = scatter_wide(
        [by_owner(value, lead) for _, value, lead in rest] + [small_grad],
        [lead for _, _, lead in rest] + [0],
        next_id,
        [LineLoad(value, wide) for _, value in lines],
    )
    for (key, _, _), total in zip(rest, sums):
        own[key] = total
    for (key, _), total in zip(lines, carried):
        own[key] = total
    grad_attn_in, grad_attn_out, grad_ffn_in, grad_ffn_out, grad_tables = [
        jnp.stack([own[name, index] for index in range(2)])
        for name in ("attn_in", "attn_out", "ffn_in", "ffn_out", "tables")
    ]
    grad_gains = total_small[:gain_rows, :gain_cols]
    narrow_first = (lax.axis_index("narrow") == 0).astype(jnp.float32)
    squares = (
        jnp.sum(grad_attn_in * grad_attn_in)
        + jnp.sum(grad_attn_out * grad_attn_out)
        + jnp.sum(grad_ffn_in * grad_ffn_in)
        + jnp.sum(grad_ffn_out * grad_ffn_out)
        + jnp.sum(grad_tables * grad_tables)
        + narrow_first * jnp.sum(grad_gains * grad_gains)
    )
    lanes = lax.broadcasted_iota(jnp.int32, (8, 128), 1)
    both = jnp.where(lanes == 0, squares, jnp.where(lanes == 1, narrow_first * jnp.sum(losses), 0.0))
    both = sum_scalars(both, wide, 4, next_id + 1)
    squares, loss_sum = both[0, 0], both[0, 1]
    grad_norm = jnp.sqrt(squares)
    factor = jnp.minimum(1.0, CLIP_NORM / (grad_norm + 1e-06))
    results = [loss_sum, token_total, grad_norm]
    for weight, gradient, first, second, decay, rate in (
        (attn_in, grad_attn_in, attn_in_mean, attn_in_square, WEIGHT_DECAY, LEARN_RATE),
        (attn_out, grad_attn_out, attn_out_mean, attn_out_square, WEIGHT_DECAY, LEARN_RATE),
        (ffn_in, grad_ffn_in, ffn_in_mean, ffn_in_square, WEIGHT_DECAY, LEARN_RATE),
        (ffn_out, grad_ffn_out, ffn_out_mean, ffn_out_square, WEIGHT_DECAY, LEARN_RATE),
        (tables, grad_tables, tables_mean, tables_square, WEIGHT_DECAY, LEARN_RATE),
        (gains, grad_gains, gains_mean, gains_square, 0.0, GAIN_RATE),
    ):
        results += adam(weight, factor * gradient, first, second, decay, rate)
    return tuple(results)


def solution(mesh):
    wide, narrow = mesh.shape["wide"], mesh.shape["narrow"]
    placed = (
        P("wide", None),
        P("wide", None),
        P("wide", None),
        P("wide", None),
        P("wide", None),
        P(None, None, "wide", "narrow"),
        P(None, "wide", "narrow"),
        P(None, "wide", "narrow"),
        P(None, "wide", "narrow"),
        P(None, "wide", "narrow"),
        P(None, "wide"),
        P(None, None, "wide", "narrow"),
        P(None, "wide", "narrow"),
        P(None, "wide", "narrow"),
        P(None, "wide", "narrow"),
        P(None, "wide", "narrow"),
        P(None, "wide"),
        P(None, None, "wide", "narrow"),
        P(None, "wide", "narrow"),
        P(None, "wide", "narrow"),
        P(None, "wide", "narrow"),
        P(None, "wide", "narrow"),
        P(None, "wide"),
    )
    return jax.shard_map(
        functools.partial(per_device, wide, narrow),
        mesh=mesh,
        in_specs=placed,
        out_specs=(
            P(),
            P(),
            P(),
            P(None, None, "wide", "narrow"),
            P(None, None, "wide", "narrow"),
            P(None, None, "wide", "narrow"),
            P(None, None, "wide", "narrow"),
            P(None, "wide", "narrow"),
            P(None, "wide", "narrow"),
            P(None, "wide", "narrow"),
            P(None, "wide", "narrow"),
            P(None, "wide", "narrow"),
            P(None, "wide", "narrow"),
            P(None, "wide", "narrow"),
            P(None, "wide", "narrow"),
            P(None, "wide", "narrow"),
            P(None, "wide", "narrow"),
            P(None, "wide", "narrow"),
            P(None, "wide", "narrow"),
            P(None, "wide", "narrow"),
            P(None, "wide", "narrow"),
            P(None, "wide", "narrow"),
            P(None, "wide", "narrow"),
            P(None, "wide"),
            P(None, "wide"),
            P(None, "wide"),
            P(None, "wide"),
        ),
        check_vma=False,
    )
```

```python
import functools
import math

import jax
import jax.numpy as jnp
from jax import lax
from jax.experimental import pallas as pl
from jax.experimental.pallas import tpu as pltpu
from jax.sharding import PartitionSpec as P

D = 768
HD = 64
V = 8192
STEPS = 1000
ADAM_STEP = 10


NORM_EPS = 1e-05
LEARN_RATE = 0.05
GAIN_RATE = 0.75
FIRST_DECAY = 0.9
SECOND_DECAY = 0.999
ADAM_EPS = 1e-08
WEIGHT_DECAY = 0.01
CLIP_NORM = 0.005
WIDE, NARROW = "wide", "narrow"


def add_heads(partial_value):
    return lax.psum(partial_value, NARROW)


def back_heads(partial_value):
    return lax.psum(partial_value, NARROW)


def rms_forward(value, gain):
    scale_row = lax.rsqrt(jnp.mean(value * value, axis=-1, keepdims=True) + NORM_EPS)
    return (value * scale_row * gain, scale_row)


def rms_backward(grad, value, scale_row, gain):
    unit = value * scale_row
    scaled = grad * gain
    back = scale_row * (scaled - unit * jnp.mean(scaled * unit, axis=-1, keepdims=True))
    return (back, jnp.sum(grad * unit, axis=0))


def time_features(timestep_row):
    half_width = D // 2
    rates = jnp.exp(-math.log(10000.0) * jnp.arange(half_width, dtype=jnp.float32) / half_width)
    angles = timestep_row.astype(jnp.float32)[:, None] * rates[None, :]
    return jnp.concatenate([jnp.sin(angles), jnp.cos(angles)], axis=1)


def masked_scores(queries, key_rows, segment):
    scores = jnp.einsum(
        "qhd,khd->hqk", queries, key_rows, preferred_element_type=jnp.float32
    ) * HD ** (-0.5)
    return jnp.where((segment[:, None] == segment[None, :])[None], scores, -1e30)


def attend(entry):
    queries, key_rows, values, segment = entry
    scores = masked_scores(queries, key_rows, segment)
    row_top = jnp.max(scores, axis=-1, keepdims=True)
    log_total = row_top + jnp.log(jnp.sum(jnp.exp(scores - row_top), axis=-1, keepdims=True))
    probs = jnp.exp(scores - log_total).astype(jnp.bfloat16)
    mixed = jnp.einsum("hqk,khd->qhd", probs, values, preferred_element_type=jnp.float32)
    return (mixed.astype(jnp.bfloat16), log_total)


def attend_back(entry):
    queries, key_rows, values, segment, log_total, grad_mixed = entry
    probs = jnp.exp(masked_scores(queries, key_rows, segment) - log_total)
    grad_probs = jnp.einsum("qhd,khd->hqk", grad_mixed, values, preferred_element_type=jnp.float32)
    grad_scores = (
        probs * (grad_probs - jnp.sum(probs * grad_probs, axis=-1, keepdims=True))
    ).astype(jnp.bfloat16)
    grad_query = jnp.einsum(
        "hqk,khd->qhd", grad_scores, key_rows, preferred_element_type=jnp.float32
    ) * HD ** (-0.5)
    grad_key = jnp.einsum(
        "hqk,qhd->khd", grad_scores, queries, preferred_element_type=jnp.float32
    ) * HD ** (-0.5)
    grad_value = jnp.einsum(
        "hqk,qhd->khd", probs.astype(jnp.bfloat16), grad_mixed, preferred_element_type=jnp.float32
    )
    return (grad_query, grad_key, grad_value)


def layer_forward(residual, segments, query_w, output_w, expand_w, reduce_w, gain_attn, gain_ffn):
    seq_count, seq_len = segments.shape
    normed, scale_one = rms_forward(residual, gain_attn)
    normed = normed.astype(jnp.bfloat16)
    projected = jnp.einsum(
        "sd,cde->cse", normed, query_w, preferred_element_type=jnp.float32
    ).astype(jnp.bfloat16)
    heads = projected.reshape(3, seq_count, seq_len, -1, HD)
    mixed, log_total = lax.map(attend, (heads[0], heads[1], heads[2], segments))
    mixed = mixed.reshape(seq_count * seq_len, -1)
    middle = residual + add_heads(
        jnp.einsum("se,de->sd", mixed, output_w, preferred_element_type=jnp.float32)
    )
    normed_two, scale_two = rms_forward(middle, gain_ffn)
    normed_two = normed_two.astype(jnp.bfloat16)
    before = jnp.dot(normed_two, expand_w, preferred_element_type=jnp.float32)
    after = jax.nn.gelu(before).astype(jnp.bfloat16)
    result = middle + add_heads(
        jnp.einsum("sf,df->sd", after, reduce_w, preferred_element_type=jnp.float32)
    )
    return (
        result,
        (
            residual,
            scale_one,
            normed,
            projected,
            log_total,
            mixed,
            middle,
            scale_two,
            normed_two,
            before,
            after,
        ),
    )


def layer_backward(
    grad, kept, segments, query_w, output_w, expand_w, reduce_w, gain_attn, gain_ffn
):
    (
        residual,
        scale_one,
        normed,
        projected,
        log_total,
        mixed,
        middle,
        scale_two,
        normed_two,
        before,
        after,
    ) = kept
    seq_count, seq_len = segments.shape
    grad_branch = grad.astype(jnp.bfloat16)
    grad_after = jnp.dot(grad_branch, reduce_w, preferred_element_type=jnp.float32)
    grad_reduce = jnp.einsum("sd,sf->df", grad_branch, after, preferred_element_type=jnp.float32)
    _, gelu_pull = jax.vjp(jax.nn.gelu, before)
    grad_before = gelu_pull(grad_after)[0].astype(jnp.bfloat16)
    grad_expand = jnp.einsum(
        "sd,sf->df", normed_two, grad_before, preferred_element_type=jnp.float32
    )
    grad_normed_two = back_heads(
        jnp.einsum("sf,df->sd", grad_before, expand_w, preferred_element_type=jnp.float32)
    )
    grad_middle, grad_gain_ffn = rms_backward(grad_normed_two, middle, scale_two, gain_ffn)
    grad_middle = grad_middle + grad
    grad_attn = grad_middle.astype(jnp.bfloat16)
    grad_mixed = jnp.dot(grad_attn, output_w, preferred_element_type=jnp.float32).astype(
        jnp.bfloat16
    )
    grad_output = jnp.einsum("sd,se->de", grad_attn, mixed, preferred_element_type=jnp.float32)
    heads = projected.reshape(3, seq_count, seq_len, -1, HD)
    grad_query, grad_key, grad_value = lax.map(
        attend_back,
        (
            heads[0],
            heads[1],
            heads[2],
            segments,
            log_total,
            grad_mixed.reshape(seq_count, seq_len, -1, HD),
        ),
    )
    grad_projected = (
        jnp.stack([grad_query, grad_key, grad_value])
        .reshape(3, seq_count * seq_len, -1)
        .astype(jnp.bfloat16)
    )
    grad_query_w = jnp.einsum(
        "sd,cse->cde", normed, grad_projected, preferred_element_type=jnp.float32
    )
    grad_normed = back_heads(
        jnp.einsum("cse,cde->sd", grad_projected, query_w, preferred_element_type=jnp.float32)
    )
    grad_input, grad_gain_attn = rms_backward(grad_normed, residual, scale_one, gain_attn)
    return (
        grad_input + grad_middle,
        (
            grad_query_w,
            grad_output,
            grad_expand,
            grad_reduce,
            jnp.stack([grad_gain_attn, grad_gain_ffn]),
        ),
    )


def adam(weight, grad, first, second, decay, rate):
    first_new = FIRST_DECAY * first + (1.0 - FIRST_DECAY) * grad
    second_new = SECOND_DECAY * second + (1.0 - SECOND_DECAY) * grad * grad
    first_hat = first_new / (1.0 - FIRST_DECAY**ADAM_STEP)
    second_hat = second_new / (1.0 - SECOND_DECAY**ADAM_STEP)
    weight_new = weight - rate * (first_hat / (jnp.sqrt(second_hat) + ADAM_EPS) + decay * weight)
    return (weight_new, first_new, second_new, weight_new.astype(jnp.bfloat16))


def general_device(
    noised,
    clean,
    timesteps,
    segments,
    counted,
    attn_in,
    attn_out,
    ffn_in,
    ffn_out,
    tables,
    gains,
    attn_in_mean,
    attn_out_mean,
    ffn_in_mean,
    ffn_out_mean,
    tables_mean,
    gains_mean,
    attn_in_square,
    attn_out_square,
    ffn_in_square,
    ffn_out_square,
    tables_square,
    gains_square,
):
    layers = attn_in.shape[0]
    mask = counted.reshape(-1).astype(jnp.float32)
    token_total = lax.psum(jnp.sum(mask), WIDE)
    query_w, output_w, expand_w, reduce_w, table_w, gain_low = (
        lax.all_gather(attn_in.astype(jnp.bfloat16), WIDE, axis=2, tiled=True),
        lax.all_gather(attn_out.astype(jnp.bfloat16), WIDE, axis=1, tiled=True),
        lax.all_gather(ffn_in.astype(jnp.bfloat16), WIDE, axis=1, tiled=True),
        lax.all_gather(ffn_out.astype(jnp.bfloat16), WIDE, axis=1, tiled=True),
        lax.all_gather(tables.astype(jnp.bfloat16), WIDE, axis=1, tiled=True),
        lax.all_gather(gains.astype(jnp.bfloat16), WIDE, axis=1, tiled=True),
    )
    gain_w = gain_low.astype(jnp.float32)
    noised_flat = noised.reshape(-1)
    clean_flat = clean.reshape(-1)
    step_flat = timesteps.reshape(-1)
    vocab_local = table_w.shape[2]
    vocab_ids = lax.axis_index(NARROW) * vocab_local + jnp.arange(vocab_local, dtype=jnp.int32)
    picks = (noised_flat[:, None] == vocab_ids[None, :]).astype(jnp.bfloat16)
    looked = add_heads(
        jnp.einsum("sv,dv->sd", picks, table_w[0], preferred_element_type=jnp.float32)
    )
    residual = math.sqrt(D) * looked + time_features(step_flat)
    kept_layers = []
    for layer_index in range(layers):
        residual, kept = layer_forward(
            residual,
            segments,
            query_w[layer_index],
            output_w[layer_index],
            expand_w[layer_index],
            reduce_w[layer_index],
            gain_w[2 * layer_index],
            gain_w[2 * layer_index + 1],
        )
        kept_layers.append(kept)
    final, scale_final = rms_forward(residual, gain_w[2 * layers])
    final_low = final.astype(jnp.bfloat16)
    logits = jnp.dot(final_low, table_w[1], preferred_element_type=jnp.float32)
    local_top = jnp.max(logits, axis=1)
    row_top = lax.pmax(local_top, NARROW)
    row_total = lax.psum(jnp.sum(jnp.exp(logits - row_top[:, None]), axis=1), NARROW)
    log_probs = logits - (row_top + jnp.log(row_total))[:, None]
    probs = jnp.exp(log_probs)
    clamped = jnp.maximum(step_flat, 2).astype(jnp.float32)[:, None]
    beta = 1.0 / (STEPS - clamped + 1.0)
    retain = (STEPS - clamped + 1.0) / STEPS
    spread = (clamped - 1.0) / (STEPS * V)
    at_noised = (vocab_ids[None, :] == noised_flat[:, None]).astype(jnp.float32)
    at_clean = (vocab_ids[None, :] == clean_flat[:, None]).astype(jnp.float32)
    forward_fac = beta / V + (1.0 - beta) * at_noised
    backward_fac = retain * at_clean + spread
    joint = forward_fac * backward_fac
    marginal = retain * probs + spread
    joint_total, cross, model_total, weighted, aligned, clean_logp = lax.psum(
        (
            jnp.sum(joint, axis=1),
            jnp.sum(joint * (jnp.log(backward_fac) - jnp.log(marginal)), axis=1),
            jnp.sum(forward_fac * marginal, axis=1),
            jnp.sum(probs * joint / marginal, axis=1),
            jnp.sum(forward_fac * probs, axis=1),
            jnp.sum(at_clean * log_probs, axis=1),
        ),
        NARROW,
    )
    divergence = cross / joint_total - jnp.log(joint_total) + jnp.log(model_total)
    first_step = step_flat == 1
    losses = jnp.where(first_step, -clean_logp, divergence)
    pull = retain * (
        -(joint / joint_total[:, None]) / marginal + forward_fac / model_total[:, None]
    )
    centre = retain[:, 0] * (-weighted / joint_total + aligned / model_total)
    grad_kl = probs * (pull - centre[:, None])
    grad_recon = probs - at_clean
    grad_logits = (
        (mask / token_total)[:, None] * jnp.where(first_step[:, None], grad_recon, grad_kl)
    ).astype(jnp.bfloat16)
    grad_table_out = jnp.einsum(
        "sd,sv->dv", final_low, grad_logits, preferred_element_type=jnp.float32
    )
    grad_final = back_heads(
        jnp.einsum("sv,dv->sd", grad_logits, table_w[1], preferred_element_type=jnp.float32)
    )
    grad_x, grad_gain_final = rms_backward(grad_final, residual, scale_final, gain_w[2 * layers])
    layer_grads = [None] * layers
    for layer_index in reversed(range(layers)):
        grad_x, produced = layer_backward(
            grad_x,
            kept_layers[layer_index],
            segments,
            query_w[layer_index],
            output_w[layer_index],
            expand_w[layer_index],
            reduce_w[layer_index],
            gain_w[2 * layer_index],
            gain_w[2 * layer_index + 1],
        )
        layer_grads[layer_index] = produced
    grad_look = (math.sqrt(D) * grad_x).astype(jnp.bfloat16)
    grad_table_in = jnp.einsum("sd,sv->dv", grad_look, picks, preferred_element_type=jnp.float32)
    stacked = [jnp.stack([entry[which] for entry in layer_grads]) for which in range(5)]
    gain_layers = stacked[4].reshape(2 * layers, -1)
    grad_tables_all = jnp.stack([grad_table_in, grad_table_out])
    grad_attn_in, grad_attn_out, grad_ffn_in, grad_ffn_out, grad_tables, grad_gains = (
        lax.psum_scatter(stacked[0], WIDE, scatter_dimension=2, tiled=True),
        lax.psum_scatter(stacked[1], WIDE, scatter_dimension=1, tiled=True),
        lax.psum_scatter(stacked[2], WIDE, scatter_dimension=1, tiled=True),
        lax.psum_scatter(stacked[3], WIDE, scatter_dimension=1, tiled=True),
        lax.psum_scatter(grad_tables_all, WIDE, scatter_dimension=1, tiled=True),
        lax.psum_scatter(
            jnp.concatenate([gain_layers, grad_gain_final[None, :]], axis=0),
            WIDE,
            scatter_dimension=1,
            tiled=True,
        ),
    )
    narrow_first = (lax.axis_index(NARROW) == 0).astype(jnp.float32)
    squares = (
        jnp.sum(grad_attn_in * grad_attn_in)
        + jnp.sum(grad_attn_out * grad_attn_out)
        + jnp.sum(grad_ffn_in * grad_ffn_in)
        + jnp.sum(grad_ffn_out * grad_ffn_out)
        + jnp.sum(grad_tables * grad_tables)
        + narrow_first * jnp.sum(grad_gains * grad_gains)
    )
    squares, loss_sum = lax.psum(
        (squares, narrow_first * jnp.sum(mask * losses)), (WIDE, NARROW)
    )
    grad_norm = jnp.sqrt(squares)
    factor = jnp.minimum(1.0, CLIP_NORM / (grad_norm + 1e-06))
    attn_in_next, attn_in_mean_next, attn_in_square_next, attn_in_copy = adam(
        attn_in, factor * grad_attn_in, attn_in_mean, attn_in_square, WEIGHT_DECAY, LEARN_RATE
    )
    attn_out_next, attn_out_mean_next, attn_out_square_next, attn_out_copy = adam(
        attn_out, factor * grad_attn_out, attn_out_mean, attn_out_square, WEIGHT_DECAY, LEARN_RATE
    )
    ffn_in_next, ffn_in_mean_next, ffn_in_square_next, ffn_in_copy = adam(
        ffn_in, factor * grad_ffn_in, ffn_in_mean, ffn_in_square, WEIGHT_DECAY, LEARN_RATE
    )
    ffn_out_next, ffn_out_mean_next, ffn_out_square_next, ffn_out_copy = adam(
        ffn_out, factor * grad_ffn_out, ffn_out_mean, ffn_out_square, WEIGHT_DECAY, LEARN_RATE
    )
    tables_next, tables_mean_next, tables_square_next, tables_copy = adam(
        tables, factor * grad_tables, tables_mean, tables_square, WEIGHT_DECAY, LEARN_RATE
    )
    gains_next, gains_mean_next, gains_square_next, gains_copy = adam(
        gains, factor * grad_gains, gains_mean, gains_square, 0.0, GAIN_RATE
    )
    return (
        loss_sum,
        token_total,
        grad_norm,
        attn_in_next,
        attn_in_mean_next,
        attn_in_square_next,
        attn_in_copy,
        attn_out_next,
        attn_out_mean_next,
        attn_out_square_next,
        attn_out_copy,
        ffn_in_next,
        ffn_in_mean_next,
        ffn_in_square_next,
        ffn_in_copy,
        ffn_out_next,
        ffn_out_mean_next,
        ffn_out_square_next,
        ffn_out_copy,
        tables_next,
        tables_mean_next,
        tables_square_next,
        tables_copy,
        gains_next,
        gains_mean_next,
        gains_square_next,
        gains_copy,
    )


MESH = pl.DeviceIdType.MESH
SLOW, FAST = 1, 2
EARLY, MIDDLE, LAST = 1, 2, 3
F32 = jnp.float32
BF16 = jnp.bfloat16
CHUNKS = 4
VMEM_LIMIT = 56 * 1024 * 1024
FORWARD_KIND = BF16
BACKWARD_KIND = BF16


def whole_vmem():
    return pl.BlockSpec(memory_space=pltpu.VMEM)


def dot_nn(a, b):
    return lax.dot_general(a, b, (((1,), (0,)), ((), ())), preferred_element_type=F32)


def dot_nt(a, b):
    return lax.dot_general(a, b, (((1,), (1,)), ((), ())), preferred_element_type=F32)


def remote(src, dst, send_sem, recv_sem, device):
    return pltpu.make_async_remote_copy(
        src_ref=src,
        dst_ref=dst,
        send_sem=send_sem,
        recv_sem=recv_sem,
        device_id=device,
        device_id_type=MESH,
    )


def greet(devices):
    barrier = pltpu.get_barrier_semaphore()
    for device in devices:
        pl.semaphore_signal(barrier, inc=1, device_id=device, device_id_type=MESH)
    pl.semaphore_wait(barrier, len(devices))


def group_places(seq_len):
    me = lax.axis_index(NARROW)
    core = lax.rem(me, 2)
    half = seq_len // 2
    mine = pl.multiple_of(core * half, half)
    other = pl.multiple_of((1 - core) * half, half)
    return ({NARROW: me + 1 - 2 * core}, {NARROW: lax.rem(me + 2, 4)}, mine, other)


class Exchange:
    def __init__(self, refs, sems, base, sibling, partner):
        self.near_out, self.near_in, self.far_out, self.far_in = refs
        self.send, self.recv = sems
        self.base, self.sibling, self.partner = base, sibling, partner

    def near(self, j):
        return remote(
            self.near_out.at[j],
            self.near_in.at[j],
            self.send.at[self.base, j],
            self.recv.at[self.base, j],
            self.sibling,
        )

    def far(self, j):
        return remote(
            self.far_out.at[j],
            self.far_in.at[j],
            self.send.at[self.base + 1, j],
            self.recv.at[self.base + 1, j],
            self.partner,
        )

    def give(self, j, value):
        self.near_out[j] = value
        self.near(j).start()

    def pass_on(self, j, value):
        self.near(j).wait_recv()
        self.far_out[j] = (value + self.near_in[j]).astype(self.far_out.dtype)
        self.far(j).start()

    def take(self, j):
        self.far(j).wait_recv()
        return self.far_out[j].astype(F32) + self.far_in[j].astype(F32)

    def close(self):
        for j in range(CHUNKS):
            self.near(j).wait_send()
            self.far(j).wait_send()

    @staticmethod
    def scratch(chunk, width, kind):
        return [
            pltpu.VMEM((CHUNKS, chunk, width), F32),
            pltpu.VMEM((CHUNKS, chunk, width), F32),
            pltpu.VMEM((CHUNKS, chunk, width), kind),
            pltpu.VMEM((CHUNKS, chunk, width), kind),
        ]


class Share:
    def __init__(self, ref, sems, base, sibling, mine, chunk):
        self.ref, self.base, self.sibling, self.mine, self.chunk = ref, base, sibling, mine, chunk
        self.send, self.recv = sems

    def piece(self, j):
        rows = self.ref.at[pl.ds(pl.multiple_of(self.mine + j * self.chunk, self.chunk), self.chunk)]
        return remote(rows, rows, self.send.at[self.base, j], self.recv.at[self.base, j], self.sibling)

    def put(self, j, value):
        self.ref[pl.ds(pl.multiple_of(self.mine + j * self.chunk, self.chunk), self.chunk), :] = value
        self.piece(j).start()

    def arrived(self, j):
        self.piece(j).wait_recv()

    def close(self):
        for j in range(CHUNKS):
            self.piece(j).wait_send()


def wide_places(count):
    me = lax.axis_index(WIDE)
    fast = lax.rem(me, 2)
    slow = me // 2
    return (me, slow, fast, count // 2)


class Carry:
    def __init__(self, loads):
        self.loads = loads

    def peers(self):
        ways = []
        for load in self.loads:
            ways += [way for way in load.ways if way not in ways]
        me, slow, fast, slows = wide_places(self.loads[0].count) if self.loads else (0, 0, 0, 0)
        found = []
        if SLOW in ways:
            found += [{WIDE: 2 * lax.rem(slow + step, slows) + fast} for step in range(1, slows)]
        if FAST in ways:
            found.append({WIDE: me + 1 - 2 * fast})
        return found

    def start(self, late=False):
        for load in self.loads:
            if load.late == late:
                load.start()

    def relay(self, stage):
        for load in self.loads:
            if load.stage == stage:
                load.relay()

    def finish(self):
        self.relay(LAST)
        for load in self.loads:
            load.finish()


def part_of(weights, index, window):
    shape = weights.shape[1:]
    return shape if window is None else shape[:-1] + (window[1],)


class SlowLoad:
    ways, late, stage = (SLOW,), False, None

    def __init__(self, weights, index, lead, count, window=None):
        self.index, self.lead, self.count, self.window = index, lead, count, window
        shape, slows = part_of(weights, index, window), count // 2
        self.operands, self.in_specs = [weights], [whole_vmem()]
        self.outs = [jax.ShapeDtypeStruct((slows,) + shape, BF16)]
        self.out_specs = [pl.BlockSpec(memory_space=pl.ANY)]
        self.scratch = [pltpu.VMEM(shape, BF16), pltpu.SemaphoreType.DMA] + [pltpu.SemaphoreType.DMA((slows,))] * 2

    def bind(self, given, out, scratch):
        self.shard, self.out = given[0], out[0]
        self.low, self.local, self.send, self.recv = scratch
        self.me, self.slow, self.fast, self.slows = wide_places(self.count)

    def cast(self):
        if self.window is None:
            self.low[...] = self.shard[self.index].astype(BF16)
        else:
            self.low[...] = self.shard[self.index, :, self.window[0] : self.window[0] + self.window[1]].astype(BF16)

    def target(self):
        return self.out.at[self.slow]

    def slow_copy(self, step):
        return remote(
            self.low, self.target(), self.send.at[step], self.recv.at[step],
            {WIDE: 2 * lax.rem(self.slow + step, self.slows) + self.fast},
        )

    def own_copy(self):
        return pltpu.make_async_copy(self.low, self.target(), self.local)

    def start(self):
        self.cast()
        for step in range(1, self.slows):
            self.slow_copy(step).start()
        self.own_copy().start()

    def finish(self):
        for step in range(1, self.slows):
            self.slow_copy(step).wait()
        self.own_copy().wait()


class FastLoad:
    ways, late, stage = (FAST,), False, None

    def __init__(self, blocks, lead, count):
        self.lead, self.count = lead, count
        shape, slows = blocks.shape[1:], count // 2
        self.operands, self.in_specs = [blocks], [pl.BlockSpec(memory_space=pl.ANY)]
        self.outs = [jax.ShapeDtypeStruct(shape[:lead] + (count,) + shape[lead:], BF16)]
        self.out_specs = [pl.BlockSpec(memory_space=pl.ANY)]
        self.scratch = [pltpu.SemaphoreType.DMA((slows,))] * 3

    def bind(self, given, out, scratch):
        self.blocks, self.out = given[0], out[0]
        self.local, self.send, self.recv = scratch
        self.me, self.slow, self.fast, self.slows = wide_places(self.count)

    def copies(self, step):
        target = self.out.at[(slice(None),) * self.lead + (2 * step + self.fast,)]
        return (
            remote(
                self.blocks.at[step], target, self.send.at[step], self.recv.at[step],
                {WIDE: self.me + 1 - 2 * self.fast},
            ),
            pltpu.make_async_copy(self.blocks.at[step], target, self.local.at[step]),
        )

    def start(self):
        for step in range(self.slows):
            for copy in self.copies(step):
                copy.start()

    def finish(self):
        for step in range(self.slows):
            for copy in self.copies(step):
                copy.wait()


class GatherLoad(SlowLoad):
    ways = (SLOW, FAST)

    def __init__(self, weights, index, lead, count, stage, window=None, late=False):
        super().__init__(weights, index, lead, count, window)
        self.stage, self.late = stage, late
        shape, slows = part_of(weights, index, window), count // 2
        self.outs = [jax.ShapeDtypeStruct(shape[:lead] + (count,) + shape[lead:], BF16)]
        self.scratch = self.scratch + [pltpu.SemaphoreType.DMA((slows,))] * 2

    def bind(self, given, out, scratch):
        super().bind(given, out, scratch[:-2])
        self.fast_send, self.fast_recv = scratch[-2:]

    def at(self, owner):
        return self.out.at[(slice(None),) * self.lead + (owner,)]

    def target(self):
        return self.at(self.me)

    def fast_copy(self, step):
        block = self.at(2 * lax.rem(self.slow + self.slows - step, self.slows) + self.fast)
        return remote(
            self.low if step == 0 else block, block, self.fast_send.at[step], self.fast_recv.at[step],
            {WIDE: self.me + 1 - 2 * self.fast},
        )

    def start(self):
        super().start()
        self.fast_copy(0).start()

    def relay(self):
        for step in range(1, self.slows):
            self.slow_copy(step).wait_recv()
            self.fast_copy(step).start()

    def finish(self):
        for step in range(self.slows):
            self.fast_copy(step).wait()
            if step:
                self.slow_copy(step).wait_send()
        self.own_copy().wait()


class PairLoad:
    ways, late, stage = (FAST,), False, None

    def __init__(self, full, lead, count):
        self.lead, self.count = lead, count
        shape, slows = full.shape[:lead] + full.shape[lead + 1 :], count // 2
        self.operands, self.in_specs = [full], [whole_vmem()]
        self.outs, self.out_specs = [jax.ShapeDtypeStruct((slows,) + shape, BF16)], [whole_vmem()]
        self.scratch = [pltpu.VMEM((slows,) + shape, BF16)] + [pltpu.SemaphoreType.DMA((slows,))] * 2

    def bind(self, given, out, scratch):
        self.full, self.out = given[0], out[0]
        self.came, self.send, self.recv = scratch
        self.me, self.slow, self.fast, self.slows = wide_places(self.count)

    def block(self, step, fast):
        owner = 2 * lax.rem(self.slow + step, self.slows) + fast
        return self.full.at[(slice(None),) * self.lead + (owner,)]

    def copy(self, step):
        return remote(
            self.block(step, 1 - self.fast), self.came.at[step], self.send.at[step], self.recv.at[step],
            {WIDE: self.me + 1 - 2 * self.fast},
        )

    def start(self):
        for step in range(self.slows):
            self.copy(step).start()

    def finish(self):
        for step in range(self.slows):
            self.copy(step).wait()
            total = self.block(step, self.fast)[...].astype(F32) + self.came[step].astype(F32)
            self.out[step] = total.astype(BF16)


class LineLoad:
    ways, late, stage = (SLOW,), False, None

    def __init__(self, sums, count):
        self.count = count
        slows = count // 2
        self.operands, self.in_specs = [sums], [whole_vmem()]
        self.outs = [jax.ShapeDtypeStruct(sums.shape[1:], F32), jax.ShapeDtypeStruct((8, 128), F32)]
        self.out_specs = [whole_vmem()] * 2
        self.scratch = [pltpu.VMEM(sums.shape, BF16)] + [pltpu.SemaphoreType.DMA((slows,))] * 2

    def bind(self, given, out, scratch):
        self.sums, (self.out, self.squares) = given[0], out
        self.came, self.send, self.recv = scratch
        self.me, self.slow, self.fast, self.slows = wide_places(self.count)

    def copy(self, step):
        return remote(
            self.sums.at[step], self.came.at[step], self.send.at[step], self.recv.at[step],
            {WIDE: 2 * lax.rem(self.slow + step, self.slows) + self.fast},
        )

    def start(self):
        for step in range(1, self.slows):
            self.copy(step).start()

    def finish(self):
        total = self.sums[0].astype(F32)
        for step in range(1, self.slows):
            self.copy(step).wait()
            total = total + self.came[step].astype(F32)
        self.out[...] = total
        self.squares[...] = jnp.full(self.squares.shape, jnp.sum(total * total), F32)


def run(body, name, operands, outs, scratch, collective_id=None, loads=()):
    counts = [len(operands)] + [len(load.operands) for load in loads]
    counts += [len(outs)] + [len(load.outs) for load in loads]
    counts += [len(scratch)] + [len(load.scratch) for load in loads]
    parts = 1 + len(loads)

    def kernel(*refs):
        groups, place = [], 0
        for count in counts:
            groups.append(refs[place : place + count])
            place += count
        for k, load in enumerate(loads, 1):
            load.bind(groups[k], groups[parts + k], groups[2 * parts + k])
        main = groups[0] + groups[parts] + groups[2 * parts]
        body(*main, carry=Carry(list(loads)))

    results = pl.pallas_call(
        kernel,
        out_shape=tuple(outs) + tuple(out for load in loads for out in load.outs),
        in_specs=[whole_vmem()] * len(operands) + [spec for load in loads for spec in load.in_specs],
        out_specs=(whole_vmem(),) * len(outs) + tuple(spec for load in loads for spec in load.out_specs),
        scratch_shapes=list(scratch) + [s for load in loads for s in load.scratch],
        compiler_params=pltpu.CompilerParams(
            collective_id=collective_id,
            has_side_effects=collective_id is not None,
            vmem_limit_bytes=VMEM_LIMIT,
        ),
        name=name,
    )(*operands, *[operand for load in loads for operand in load.operands])
    return results[: len(outs)], results[len(outs) :]


def sems(kinds):
    return [pltpu.SemaphoreType.DMA((kinds, CHUNKS)), pltpu.SemaphoreType.DMA((kinds, CHUNKS))]


def norm_of(value, gain):
    scale = lax.rsqrt(jnp.mean(value * value, axis=-1, keepdims=True) + NORM_EPS)
    return value * scale * gain


def norm_back(grad, value, gain):
    scale = lax.rsqrt(jnp.mean(value * value, axis=-1, keepdims=True) + NORM_EPS)
    unit = value * scale
    scaled = grad * gain
    back = scale * (scaled - unit * jnp.mean(scaled * unit, axis=-1, keepdims=True))
    return (back, jnp.sum(grad * unit, axis=0, keepdims=True))


GELU_A = math.sqrt(2.0 / math.pi)
GELU_B = 0.044715


def gelu_of(x):
    return 0.5 * x * (1.0 + jnp.tanh(GELU_A * (x + GELU_B * (x * x * x))))


def gelu_slope(x):
    square = x * x
    t = jnp.tanh(GELU_A * (x + GELU_B * (x * square)))
    return 0.5 * (1.0 + t) + 0.5 * x * (1.0 - t * t) * (GELU_A * (1.0 + 3.0 * GELU_B * square))


def rows_at(start, j, chunk):
    return pl.ds(pl.multiple_of(start + j * chunk, chunk), chunk)


LANES = 128


def spread(row):
    return jnp.transpose(jnp.broadcast_to(row, (LANES, LANES)))


def feature_places(owner, width, share):
    lane = lax.broadcasted_iota(jnp.int32, (LANES, width), 0)
    feature = lax.broadcasted_iota(jnp.int32, (LANES, width), 1)
    return ((feature == lane + owner * share) & (lane < share)).astype(F32).astype(BF16)


def token_picks(ids, vocab, first):
    here = spread(ids.astype(F32) - first.astype(F32))
    lane = lax.broadcasted_iota(jnp.int32, (LANES, LANES), 1).astype(F32)
    return [jnp.where(here == lane + float(t * LANES), 1.0, 0.0).astype(BF16) for t in range(vocab // LANES)]


def embed_kernel(
    ids, counted, gains, extra, table,
    resid, normed, gain_all, count_all, ids_all,
    low, picks, small, near_out, near_in, own, far_out, far_in, wide_out, wide_in, part_out, part_in,
    id_send, id_recv, small_send, small_recv, near_send, near_recv, far_send, far_recv, wide_send, wide_recv,
    part_send, part_recv, send, recv, carry,
):
    seq_len, width = normed.shape
    chunk = seq_len // 2 // CHUNKS
    quarter = seq_len // 4
    share, vocab = table.shape[1:]
    owners = ids_all.shape[0]
    id_rows = ids.shape[0]
    sibling, partner, mine, other = group_places(seq_len)
    place = lax.axis_index(NARROW)
    side = lax.div(place, 2)
    me = lax.axis_index(WIDE)
    first = place * vocab
    around = [lax.rem(me + step, owners) for step in range(owners)]

    def id_copy(step):
        return remote(ids_all.at[me], ids_all.at[me], id_send.at[step], id_recv.at[step], {WIDE: around[step]})

    def small_copy(step):
        return remote(small.at[me], small.at[me], small_send.at[step], small_recv.at[step], {WIDE: around[step]})

    def near_copy(step):
        return remote(near_out.at[step], near_in.at[step], near_send.at[step], near_recv.at[step], sibling)

    def far_copy(step):
        return remote(far_out.at[step], far_in.at[step], far_send.at[step], far_recv.at[step], partner)

    def wide_copy(step):
        return remote(wide_out.at[step], wide_in.at[me], wide_send.at[step], wide_recv.at[step], {WIDE: around[step]})

    def part_copy(piece):
        rows = pl.ds(piece * LANES, LANES)
        return remote(part_out.at[rows], part_in.at[rows], part_send.at[piece], part_recv.at[piece], partner)

    ids_all[me] = ids[...]
    small[me] = jnp.zeros(small.shape[1:], F32)
    small[me, : gains.shape[0], : gains.shape[1]] = gains[...].astype(BF16).astype(F32)
    count = jnp.sum(counted[...].astype(F32), keepdims=True)
    small[me, gains.shape[0] : gains.shape[0] + 1, :] = jnp.broadcast_to(count, (1, small.shape[2]))
    greet([{WIDE: device} for device in around[1:]] + [sibling, partner])
    for step in range(1, owners):
        id_copy(step).start()
    for step in range(1, owners):
        small_copy(step).start()
    carry.start()
    low[...] = jnp.zeros(low.shape, BF16)
    low[:share, :] = table[0].astype(BF16)

    def look_up(step):
        row = lax.rem(me + step, owners)

        def block(start, b):
            place_of = start // LANES + b
            for t, pick in enumerate(token_picks(ids_all[row, pl.ds(place_of, 1), :], vocab, first)):
                picks[:, t * LANES : (t + 1) * LANES] = pick
            return dot_nt(picks[...], low[...]).astype(BF16)

        def theirs(b, _):
            near_out[step, rows_at(0, b, LANES), :] = block(other, b)
            return 0

        def ours(b, _):
            own[step, rows_at(0, b, LANES), :] = block(mine, b)
            return 0

        lax.fori_loop(0, seq_len // 2 // LANES, theirs, 0)
        near_copy(step).start()
        lax.fori_loop(0, seq_len // 2 // LANES, ours, 0)

    def halve(step):
        near_copy(step).wait_recv()
        total = own[step] + near_in[step]
        own[step] = total
        far_out[step] = own[step, pl.ds(pl.multiple_of((1 - side) * quarter, quarter), quarter), :]
        far_copy(step).start()

    def deliver(step):
        far_copy(step).wait_recv()
        total = own[step, pl.ds(pl.multiple_of(side * quarter, quarter), quarter), :] + far_in[step]
        if step % owners == 0:
            wide_in[me] = total
        else:
            wide_out[step] = total
            wide_copy(step).start()

    order = list(range(1, owners)) + [0]
    for turn in range(owners + 2):
        if turn < owners:
            if order[turn]:
                id_copy(owners - order[turn]).wait_recv()
            look_up(order[turn])
        if 1 <= turn < owners + 1:
            halve(order[turn - 1])
        if turn >= 2:
            deliver(order[turn - 2])
    carry.start(True)
    for step in range(1, owners):
        small_copy(step).wait_recv()
    total = None
    for owner in range(owners):
        part = dot_nn(small[owner].astype(BF16), feature_places(owner, width, share))
        total = part if total is None else total + part
    gain_all[...] = total
    count_all[...] = jnp.sum(small[...], axis=0)
    for step in range(1, owners):
        wide_copy(step).wait_recv()
    pieces = quarter // LANES
    at_side = pl.multiple_of(side * quarter, quarter)
    at_other = pl.multiple_of((1 - side) * quarter, quarter)
    for piece in range(pieces):
        rows = pl.ds(piece * LANES, LANES)
        found = None
        for owner in range(owners):
            part = dot_nn(wide_in[owner, rows, :], feature_places(owner, width, share))
            found = part if found is None else found + part
        part_out[rows, :] = found.astype(BF16)
        part_copy(piece).start()
    carry.relay(EARLY)
    give = Share(normed, (send, recv), 0, sibling, mine, chunk)

    def finish(start, source, piece):
        rows = rows_at(start, piece, LANES)
        x = math.sqrt(width) * source[pl.ds(piece * LANES, LANES), :].astype(F32) + extra[rows, :]
        resid[rows, :] = x
        here = rows_at(mine + start, piece, LANES)
        normed[here, :] = norm_of(x, gain_all[0:1, :]).astype(BF16)
        give_rows(here, piece if source is part_out else pieces + piece).start()

    def give_rows(here, k):
        return remote(normed.at[here], normed.at[here], send.at[0, k], recv.at[0, k], sibling)

    for piece in range(pieces):
        finish(at_side, part_out, piece)
    for piece in range(pieces):
        part_copy(piece).wait_recv()
        finish(at_other, part_in, piece)
    carry.relay(MIDDLE)
    for k in range(2 * pieces):
        give_rows(rows_at(mine, k % pieces, LANES), k).wait()
    for step in range(owners):
        near_copy(step).wait_send()
        far_copy(step).wait_send()
        if step:
            id_copy(step).wait_send()
            small_copy(step).wait_send()
            wide_copy(step).wait_send()
    for piece in range(pieces):
        part_copy(piece).wait_send()
    carry.finish()


def embed(ids, counted, gains, extra, tables, owners, collective_id, loads):
    seq_len = ids.size
    half, width = extra.shape
    share, vocab = tables.shape[1:]
    dma = pltpu.SemaphoreType.DMA
    return run(
        embed_kernel,
        "embed",
        [ids, counted, gains, extra, tables],
        [
            jax.ShapeDtypeStruct((half, width), F32),
            jax.ShapeDtypeStruct((seq_len, width), BF16),
            jax.ShapeDtypeStruct((8, width), F32),
            jax.ShapeDtypeStruct((8, LANES), F32),
            jax.ShapeDtypeStruct((owners,) + ids.shape, jnp.int32),
        ],
        [
            pltpu.VMEM((LANES, vocab), BF16),
            pltpu.VMEM((LANES, vocab), BF16),
            pltpu.VMEM((owners, 8, LANES), F32),
            pltpu.VMEM((owners, half, LANES), BF16),
            pltpu.VMEM((owners, half, LANES), BF16),
            pltpu.VMEM((owners, half, LANES), BF16),
            pltpu.VMEM((owners, half // 2, LANES), BF16),
            pltpu.VMEM((owners, half // 2, LANES), BF16),
            pltpu.VMEM((owners, half // 2, LANES), BF16),
            pltpu.VMEM((owners, half // 2, LANES), BF16),
            pltpu.VMEM((half // 2, width), BF16),
            pltpu.VMEM((half // 2, width), BF16),
        ]
        + [dma((owners,))] * 10
        + [dma((half // 2 // LANES,))] * 2
        + [dma((1, half // LANES))] * 2,
        collective_id,
        loads,
    )


def ffn_kernel(
    layer, mixed, resid, w_out, w_in, w_red, gains,
    middle, normed, before, after, result, normed_next,
    near_out, near_in, far_out, far_in, near_out2, near_in2, far_out2, far_in2, own2, send, recv, carry,
):
    seq_len = normed.shape[0]
    chunk = seq_len // 2 // CHUNKS
    sibling, partner, mine, other = group_places(seq_len)
    greet([sibling, partner] + carry.peers())
    carry.start()
    sems = (send, recv)
    first = Exchange((near_out, near_in, far_out, far_in), sems, 0, sibling, partner)
    second = Exchange((near_out2, near_in2, far_out2, far_in2), sems, 2, sibling, partner)
    share = Share(normed, sems, 4, sibling, mine, chunk)
    share_next = Share(normed_next, sems, 5, sibling, mine, chunk)

    def project(start, j):
        return dot_nt(mixed[rows_at(start, j, chunk), :], w_out[...])

    def feed(rows):
        pre = dot_nn(normed[rows, :], w_in[...])
        before[rows, :] = pre
        act = gelu_of(pre).astype(BF16)
        after[rows, :] = act
        return dot_nt(act, w_red[...])

    first.give(0, project(other, 0))
    for j in range(CHUNKS):
        if j + 1 < CHUNKS:
            first.give(j + 1, project(other, j + 1))
        first.pass_on(j, project(mine, j))
    for j in range(CHUNKS):
        rows = rows_at(0, j, chunk)
        mid = resid[rows, :] + first.take(j)
        middle[rows, :] = mid
        share.put(j, norm_of(mid, gains[2 * layer + 1 : 2 * layer + 2, :]).astype(BF16))
        own2[j] = feed(rows_at(mine, j, chunk))
        share.arrived(j)
        second.give(j, feed(rows_at(other, j, chunk)))
        if j >= 1:
            second.pass_on(j - 1, own2[j - 1])
    second.pass_on(CHUNKS - 1, own2[CHUNKS - 1])
    carry.relay(EARLY)
    for j in range(CHUNKS):
        rows = rows_at(0, j, chunk)
        x = middle[rows, :] + second.take(j)
        result[rows, :] = x
        share_next.put(j, norm_of(x, gains[2 * layer + 2 : 2 * layer + 3, :]).astype(BF16))
        if j == CHUNKS - 2:
            carry.relay(MIDDLE)
    for j in range(CHUNKS):
        share_next.arrived(j)
    for part in (first, second, share, share_next):
        part.close()
    carry.finish()


def ffn_forward(layer, mixed, resid, w_out, w_in, w_red, gains, collective_id, loads):
    seq_len, width, hidden = mixed.shape[0], w_in.shape[0], w_in.shape[1]
    half, chunk = seq_len // 2, seq_len // 2 // CHUNKS
    return run(
        functools.partial(ffn_kernel, layer),
        "ffn_forward",
        [mixed, resid, w_out, w_in, w_red, gains],
        [
            jax.ShapeDtypeStruct((half, width), F32),
            jax.ShapeDtypeStruct((seq_len, width), BF16),
            jax.ShapeDtypeStruct((seq_len, hidden), F32),
            jax.ShapeDtypeStruct((seq_len, hidden), BF16),
            jax.ShapeDtypeStruct((half, width), F32),
            jax.ShapeDtypeStruct((seq_len, width), BF16),
        ],
        Exchange.scratch(chunk, width, FORWARD_KIND)
        + Exchange.scratch(chunk, width, FORWARD_KIND)
        + [pltpu.VMEM((CHUNKS, chunk, width), F32)]
        + sems(6),
        collective_id,
        loads,
    )


TILE = 256


def weight_grad(left_t, right, out):
    columns = right.shape[1]
    tile = TILE if columns % TILE == 0 else columns

    def step(i, _):
        where = pl.ds(pl.multiple_of(i * tile, tile), tile)
        out[:, where] = dot_nn(left_t[...], right[:, where]).astype(out.dtype)
        return 0

    if tile == columns:
        out[...] = dot_nn(left_t[...], right[...]).astype(out.dtype)
    else:
        lax.fori_loop(0, columns // tile, step, 0)


def ffn_back_kernel(
    row, grad, branch, w_red, w_in, w_out, before, after, normed, middle, gain, mixed,
    grad_middle, grad_attn, grad_mixed, d_red, d_in, d_out, d_gain,
    grad_before, turned, near_out, near_in, far_out, far_in, send, recv, carry,
):
    seq_len = normed.shape[0]
    chunk = seq_len // 2 // CHUNKS
    sibling, partner, mine, other = group_places(seq_len)
    greet([sibling, partner] + carry.peers())
    carry.start()
    sems = (send, recv)
    trade = Exchange((near_out, near_in, far_out, far_in), sems, 0, sibling, partner)
    share = Share(grad_attn, sems, 2, sibling, mine, chunk)

    def partial(start, j):
        rows = rows_at(start, j, chunk)
        back = dot_nn(branch[rows, :], w_red[...])
        low = (back * gelu_slope(before[rows, :])).astype(BF16)
        grad_before[rows, :] = low
        return dot_nt(low, w_in[...])

    trade.give(0, partial(other, 0))
    for j in range(CHUNKS):
        if j + 1 < CHUNKS:
            trade.give(j + 1, partial(other, j + 1))
        trade.pass_on(j, partial(mine, j))
    turned[...] = jnp.transpose(branch[...])
    weight_grad(turned, after, d_red)
    turned[...] = jnp.transpose(normed[...])
    weight_grad(turned, grad_before, d_in)
    gain_total = jnp.zeros((1, gain.shape[1]), F32)
    for j in range(CHUNKS):
        rows = rows_at(0, j, chunk)
        back, gain_part = norm_back(trade.take(j), middle[rows, :], gain[row : row + 1, :])
        gain_total = gain_total + gain_part
        total = back + grad[rows, :]
        grad_middle[rows, :] = total
        share.put(j, total.astype(BF16))
        here = rows_at(mine, j, chunk)
        grad_mixed[here, :] = dot_nn(grad_attn[here, :], w_out[...]).astype(BF16)
    for j in range(CHUNKS):
        share.arrived(j)
        here = rows_at(other, j, chunk)
        grad_mixed[here, :] = dot_nn(grad_attn[here, :], w_out[...]).astype(BF16)
    d_gain[...] = gain_total
    turned[...] = jnp.transpose(grad_attn[...])
    weight_grad(turned, mixed, d_out)
    trade.close()
    share.close()
    carry.finish()


def ffn_backward(row, grad, branch, w_red, w_in, w_out, before, after, normed, middle, gain, mixed, collective_id, loads):
    seq_len, width = normed.shape
    half, chunk = seq_len // 2, seq_len // 2 // CHUNKS
    return run(
        functools.partial(ffn_back_kernel, row),
        "ffn_backward",
        [grad, branch, w_red, w_in, w_out, before, after, normed, middle, gain, mixed],
        [
            jax.ShapeDtypeStruct((half, width), F32),
            jax.ShapeDtypeStruct((seq_len, width), BF16),
            jax.ShapeDtypeStruct(mixed.shape, BF16),
            jax.ShapeDtypeStruct(w_red.shape, BF16),
            jax.ShapeDtypeStruct(w_in.shape, BF16),
            jax.ShapeDtypeStruct(w_out.shape, BF16),
            jax.ShapeDtypeStruct((1, gain.shape[1]), F32),
        ],
        [pltpu.VMEM(before.shape, BF16), pltpu.VMEM((width, seq_len), BF16)]
        + Exchange.scratch(chunk, width, BACKWARD_KIND)
        + sems(3),
        collective_id,
        loads,
    )


def norm_back_kernel(
    scale, row, grads, weights, normed, value, gain, upstream,
    grad_out, branch, d_weights, d_gain,
    turned, near_out, near_in, far_out, far_in, send, recv, carry,
):
    seq_len, width = normed.shape
    chunk = seq_len // 2 // CHUNKS
    sibling, partner, mine, other = group_places(seq_len)
    greet([sibling, partner] + carry.peers())
    carry.start()
    sems = (send, recv)
    trade = Exchange((near_out, near_in, far_out, far_in), sems, 0, sibling, partner)
    share = Share(branch, sems, 2, sibling, mine, chunk)

    def partial(start, j):
        rows = rows_at(start, j, chunk)
        total = None
        for which in range(grads.shape[0]):
            part = dot_nt(grads[which, rows, :], weights[which])
            total = part if total is None else total + part
        return total

    trade.give(0, partial(other, 0))
    for j in range(CHUNKS):
        if j + 1 < CHUNKS:
            trade.give(j + 1, partial(other, j + 1))
        trade.pass_on(j, partial(mine, j))
    turned[...] = jnp.transpose(normed[...])
    for which in range(grads.shape[0]):
        weight_grad(turned, grads.at[which], d_weights.at[which])
    gain_total = jnp.zeros((1, gain.shape[1]), F32)
    for j in range(CHUNKS):
        rows = rows_at(0, j, chunk)
        back, gain_part = norm_back(trade.take(j), value[rows, :], gain[row : row + 1, :])
        gain_total = gain_total + gain_part
        back = back + upstream[rows, :]
        grad_out[rows, :] = back
        share.put(j, (back if scale is None else scale * back).astype(BF16))
    d_gain[...] = gain_total
    for j in range(CHUNKS):
        share.arrived(j)
    trade.close()
    share.close()
    carry.finish()


def norm_backward(row, grads, weights, normed, value, gain, upstream, scale, collective_id, loads):
    seq_len, width = normed.shape
    half, chunk = seq_len // 2, seq_len // 2 // CHUNKS
    return run(
        functools.partial(norm_back_kernel, scale, row),
        "norm_backward",
        [grads, weights, normed, value, gain, upstream],
        [
            jax.ShapeDtypeStruct((half, width), F32),
            jax.ShapeDtypeStruct((seq_len, width), BF16),
            jax.ShapeDtypeStruct(weights.shape, BF16),
            jax.ShapeDtypeStruct((1, gain.shape[1]), F32),
        ],
        [pltpu.VMEM((width, seq_len), BF16)] + Exchange.scratch(chunk, width, BACKWARD_KIND) + sems(3),
        collective_id,
        loads,
    )


def head_lanes(value, head, size):
    lanes = lax.broadcasted_iota(jnp.int32, value.shape, 1)
    inside = (lanes >= head * size) & (lanes < (head + 1) * size)
    return jnp.where(inside, value, jnp.zeros_like(value))


def attention_kernel(normed, weights, key_seg, query_seg, projected, mixed, bias, values_t, carry):
    seq_len = normed.shape[0]
    width = mixed.shape[1]
    block = bias.shape[1]
    heads = width // HD
    if carry.loads:
        greet(carry.peers())
    carry.start()

    def project(i, _):
        rows = rows_at(0, i, block)
        for which in range(3):
            projected[which, rows, :] = dot_nn(normed[rows, :], weights[which]).astype(BF16)
        return 0

    lax.fori_loop(0, seq_len // block, project, 0)
    values_t[...] = jnp.transpose(projected[2])

    def queries(i, _):
        rows = rows_at(0, i, block)
        bias[...] = jnp.where(key_seg[...] == query_seg[:, rows], 0.0, -1e30)
        asked = projected[0, rows, :] * HD ** (-0.5)
        parts = []
        for head in range(heads):
            scores = dot_nt(projected[1], head_lanes(asked, head, HD)) + bias[...]
            powers = jnp.exp(scores - jnp.max(scores, axis=0, keepdims=True))
            probs = (powers * (1.0 / jnp.sum(powers, axis=0, keepdims=True))).astype(BF16)
            parts.append(dot_nn(values_t[head * HD : (head + 1) * HD, :], probs))
        mixed[rows, :] = jnp.transpose(jnp.concatenate(parts, axis=0)).astype(BF16)
        return 0

    lax.fori_loop(0, seq_len // block, queries, 0)
    carry.finish()


QUERY_BLOCK = 256


def attention(normed, weights, key_seg, query_seg, collective_id, loads):
    seq_len, width = normed.shape[0], weights.shape[2]
    block = min(QUERY_BLOCK, seq_len)
    return run(
        attention_kernel,
        "attention",
        [normed, weights, key_seg, query_seg],
        [
            jax.ShapeDtypeStruct((3, seq_len, width), BF16),
            jax.ShapeDtypeStruct((seq_len, width), BF16),
        ],
        [pltpu.VMEM((seq_len, block), F32), pltpu.VMEM((width, seq_len), BF16)],
        collective_id if loads else None,
        loads,
    )


def attention_back_kernel(projected, grad_mixed, key_seg, query_seg, out, bias, keys_t, grad_keys, grad_values, carry):
    seq_len, width = grad_mixed.shape
    block = bias.shape[1]
    heads = width // HD
    scale = HD ** (-0.5)
    if carry.loads:
        greet(carry.peers())
    carry.start()
    keys_t[...] = jnp.transpose(projected[1])
    grad_keys[...] = jnp.zeros(grad_keys.shape, F32)
    grad_values[...] = jnp.zeros(grad_values.shape, F32)

    def queries(i, _):
        rows = rows_at(0, i, block)
        bias[...] = jnp.where(key_seg[...] == query_seg[:, rows], 0.0, -1e30)
        asked = projected[0, rows, :] * scale
        given = grad_mixed[rows, :]
        parts = []
        for head in range(heads):
            query = head_lanes(asked, head, HD)
            grad = head_lanes(given, head, HD)
            scores = dot_nt(projected[1], query) + bias[...]
            powers = jnp.exp(scores - jnp.max(scores, axis=0, keepdims=True))
            probs = powers * (1.0 / jnp.sum(powers, axis=0, keepdims=True))
            grad_probs = dot_nt(projected[2], grad)
            centre = jnp.sum(probs * grad_probs, axis=0, keepdims=True)
            grad_scores = (probs * (grad_probs - centre)).astype(BF16)
            parts.append(dot_nn(keys_t[head * HD : (head + 1) * HD, :], grad_scores))
            grad_keys[...] += dot_nn(grad_scores, query)
            grad_values[...] += dot_nn(probs.astype(BF16), grad)
        out[0, rows, :] = (jnp.transpose(jnp.concatenate(parts, axis=0)) * scale).astype(BF16)
        return 0

    lax.fori_loop(0, seq_len // block, queries, 0)
    out[1] = grad_keys[...].astype(BF16)
    out[2] = grad_values[...].astype(BF16)
    carry.finish()


def attention_back(projected, grad_mixed, key_seg, query_seg, collective_id, loads):
    seq_len, width = grad_mixed.shape
    block = min(QUERY_BLOCK, seq_len)
    return run(
        attention_back_kernel,
        "attention_back",
        [projected, grad_mixed, key_seg, query_seg],
        [jax.ShapeDtypeStruct(projected.shape, BF16)],
        [
            pltpu.VMEM((seq_len, block), F32),
            pltpu.VMEM((width, seq_len), BF16),
            pltpu.VMEM((seq_len, width), F32),
            pltpu.VMEM((seq_len, width), F32),
        ],
        collective_id if loads else None,
        loads,
    )


def to_rows(columns):
    lanes = lax.broadcasted_iota(jnp.int32, (LANES, LANES), 1)
    total = jnp.zeros((LANES, LANES), F32)
    for k, column in enumerate(columns):
        total = jnp.where(lanes == k, column, total)
    return jnp.transpose(total)[:8, :]


def loss_kernel(
    pieces, row, normed, info, value, gain, *refs, carry,
):
    tables, refs = refs[:pieces], refs[pieces:]
    (grad_out, branch, d_gain, losses), refs = refs[:4], refs[4:]
    d_tables, refs = refs[:pieces], refs[pieces:]
    loss_body(row, normed, info, value, gain, tables, grad_out, branch, d_gain, losses, d_tables, *refs, carry)


def loss_body(
    row, normed, info, value, gain, tables, grad_out, branch, d_gain, losses, d_tables,
    logits, grads, places, turned, stat_out, stat_in, sum_out, sum_in,
    near_out, near_in, far_out, far_in, send, recv, stat_send, stat_recv, sum_send, sum_recv, carry,
):
    seq_len, width = normed.shape
    chunk = seq_len // 2 // CHUNKS
    piece_width = tables[0].shape[1]
    vocab = piece_width * len(tables)
    tiles = vocab // LANES
    blocks = seq_len // LANES
    me = lax.axis_index(NARROW)
    sibling, partner, mine, other = group_places(seq_len)
    peers = [{NARROW: lax.rem(me + k, 4)} for k in range(1, 4)]
    greet(peers + carry.peers())
    carry.start()
    sems = (send, recv)
    trade = Exchange((near_out, near_in, far_out, far_in), sems, 0, sibling, partner)
    share = Share(branch, sems, 2, sibling, mine, chunk)
    first = (me * vocab).astype(F32)
    whole = 4.0 * vocab
    lanes = lax.broadcasted_iota(jnp.int32, (LANES, LANES), 1).astype(F32)

    def stat_copy(b, k):
        return remote(stat_out.at[b], stat_in.at[k, b], stat_send.at[k, b], stat_recv.at[k, b], peers[k])

    def sum_copy(b, k):
        return remote(sum_out.at[b], sum_in.at[k, b], sum_send.at[k, b], sum_recv.at[k, b], peers[k])

    def tile_at(t):
        return pl.ds(pl.multiple_of(t * LANES, LANES), LANES)

    def ask(b, _):
        rows = rows_at(0, b, LANES)
        for k, table in enumerate(tables):
            logits[rows, k * piece_width : (k + 1) * piece_width] = dot_nn(normed[rows, :], table[...])
        here = info[:, rows]
        at_noised = spread(here[0:1] - first)
        at_clean = spread(here[1:2] - first)
        places[b, 0] = at_noised
        places[b, 1] = at_clean

        def top_step(t, top):
            return jnp.maximum(top, logits[rows, tile_at(t)])

        top = lax.fori_loop(1, tiles, top_step, logits[rows, tile_at(0)], unroll=4)
        top = jnp.max(top, axis=1, keepdims=True)
        top_wide = jnp.broadcast_to(top, (LANES, LANES))

        def sum_step(t, totals):
            powers, noised, clean = totals
            piece = logits[rows, tile_at(t)]
            column = lanes + (t * LANES).astype(F32)
            return (
                powers + jnp.exp(piece - top_wide),
                noised + jnp.where(column == at_noised, piece, 0.0),
                clean + jnp.where(column == at_clean, piece, 0.0),
            )

        zero = jnp.zeros((LANES, LANES), F32)
        totals = lax.fori_loop(0, tiles, sum_step, (zero, zero, zero))
        stat_out[b] = to_rows([top] + [jnp.sum(total, axis=1, keepdims=True) for total in totals])
        for k in range(3):
            stat_copy(b, k).start()
        return 0

    lax.fori_loop(0, blocks, ask, 0)

    def scalars(b):
        here = info[:, rows_at(0, b, LANES)]
        step = jnp.maximum(here[2:3], 2.0)
        left = STEPS - step + 1.0
        beta = 1.0 / left
        keep = left / STEPS
        rest = (step - 1.0) / (STEPS * whole)
        own = stat_out[b]
        others = [stat_in[k, b] for k in range(3)]
        top = own[0:1]
        for stat in others:
            top = jnp.maximum(top, stat[0:1])
        total = own[1:2] * jnp.exp(own[0:1] - top)
        noised, clean = own[2:3], own[3:4]
        for stat in others:
            total = total + stat[1:2] * jnp.exp(stat[0:1] - top)
            noised, clean = noised + stat[2:3], clean + stat[3:4]
        return here, beta, keep, rest, top + jnp.log(total), noised, clean

    def measure(b, _):
        rows = rows_at(0, b, LANES)
        for k in range(3):
            stat_copy(b, k).wait_recv()
        _, _, keep, rest, log_total, _, _ = scalars(b)
        log_wide = spread(log_total)
        ratio = spread(keep / rest)

        def step(t, totals):
            logs, shares = totals
            probs = jnp.exp(logits[rows, tile_at(t)] - log_wide)
            logits[rows, tile_at(t)] = probs
            grown = 1.0 + probs * ratio
            return (logs + jnp.log(grown), shares + probs / grown)

        zero = jnp.zeros((LANES, LANES), F32)
        totals = lax.fori_loop(0, tiles, step, (zero, zero))
        sum_out[b] = to_rows([jnp.sum(total, axis=1, keepdims=True) for total in totals])
        for k in range(3):
            sum_copy(b, k).start()
        return 0

    lax.fori_loop(0, blocks, measure, 0)

    def pull(b):
        rows = rows_at(0, b, LANES)
        for k in range(3):
            sum_copy(b, k).wait_recv()
        here, beta, keep, rest, log_total, noised, clean = scalars(b)
        sums = sum_out[b] + sum_in[0, b] + sum_in[1, b] + sum_in[2, b]
        log_sum, share_sum = sums[0:1], sums[1:2] / rest
        same = here[0:1] == here[1:2]
        first_step = here[2:3] == 1.0
        base_a, more_a = beta / whole, 1.0 - beta
        base_w = base_a * rest
        joint = whole * base_w + more_a * rest + base_a * keep + jnp.where(same, more_a * keep, 0.0)
        ratio = keep / rest
        prob_n, prob_c = jnp.exp(noised - log_total), jnp.exp(clean - log_total)
        grown_n, grown_c = 1.0 + prob_n * ratio, 1.0 + prob_c * ratio
        marginal_n, marginal_c = rest * grown_n, rest * grown_c
        log_n, log_c = jnp.log(grown_n), jnp.log(grown_c)
        weight_n = jnp.where(same, 0.0, more_a * rest)
        weight_c = jnp.where(same, more_a * rest + base_a * keep + more_a * keep, base_a * keep)
        lift = jnp.log((keep + rest) / rest)
        cross = -base_w * log_sum - weight_n * log_n - weight_c * log_c + (base_w + weight_c) * lift
        model = base_a * (keep + whole * rest) + more_a * marginal_n
        divergence = cross / joint - jnp.log(joint) + jnp.log(model)
        loss = jnp.where(first_step, log_total - clean, divergence)
        losses[:, rows] = here[4:5] * loss
        weighted = base_w * share_sum + weight_n * prob_n / marginal_n + weight_c * prob_c / marginal_c
        aligned = base_a + more_a * prob_n
        centre = keep * (aligned / model - weighted / joint)
        scale = here[3:4]
        zero = jnp.zeros_like(scale)
        even = scale * jnp.where(first_step, 1.0, keep * base_a / model - centre)
        bent = scale * jnp.where(first_step, zero, -keep * base_w / joint / rest)
        at_n = prob_n * keep * (more_a / model - weight_n / joint / marginal_n)
        at_c = -prob_c * keep * (weight_c / joint / marginal_c)
        extra_n = spread(scale * jnp.where(first_step, zero, at_n))
        extra_c = spread(scale * jnp.where(first_step, -1.0, at_c))
        even, bent, ratio = spread(even), spread(bent), spread(ratio)
        at_noised, at_clean = places[b, 0], places[b, 1]

        def step(t, _):
            probs = logits[rows, tile_at(t)]
            column = lanes + (t * LANES).astype(F32)
            grad = probs * (even + bent / (1.0 + probs * ratio))
            grad = grad + jnp.where(column == at_noised, extra_n, 0.0)
            grad = grad + jnp.where(column == at_clean, extra_c, 0.0)
            grads[rows, tile_at(t)] = grad.astype(BF16)
            return 0

        lax.fori_loop(0, tiles, step, 0)

    def partial(start, j):
        base = start // LANES + j * (chunk // LANES)
        for b in range(chunk // LANES):
            pull(base + b)
        total = None
        for k, table in enumerate(tables):
            part = dot_nt(grads[rows_at(start, j, chunk), k * piece_width : (k + 1) * piece_width], table[...])
            total = part if total is None else total + part
        return total

    trade.give(0, partial(other, 0))
    for j in range(CHUNKS):
        if j + 1 < CHUNKS:
            trade.give(j + 1, partial(other, j + 1))
        trade.pass_on(j, partial(mine, j))
    turned[...] = jnp.transpose(normed[...])
    for k, d_table in enumerate(d_tables):
        weight_grad(turned, grads.at[:, k * piece_width : (k + 1) * piece_width], d_table)
    gain_total = jnp.zeros((1, gain.shape[1]), F32)
    for j in range(CHUNKS):
        rows = rows_at(0, j, chunk)
        back, gain_part = norm_back(trade.take(j), value[rows, :], gain[row : row + 1, :])
        gain_total = gain_total + gain_part
        grad_out[rows, :] = back
        share.put(j, back.astype(BF16))
    d_gain[...] = gain_total
    for j in range(CHUNKS):
        share.arrived(j)
    trade.close()
    share.close()

    def finish(b, _):
        for k in range(3):
            stat_copy(b, k).wait_send()
            sum_copy(b, k).wait_send()
        return 0

    lax.fori_loop(0, blocks, finish, 0)
    carry.finish()


def loss_and_back(row, normed, tables, info, value, gain, collective_id, loads):
    seq_len, width = normed.shape
    vocab = sum(table.shape[1] for table in tables)
    half, chunk, blocks = seq_len // 2, seq_len // 2 // CHUNKS, seq_len // LANES
    return run(
        functools.partial(loss_kernel, len(tables), row),
        "loss_and_back",
        [normed, info, value, gain, *tables],
        [
            jax.ShapeDtypeStruct((half, width), F32),
            jax.ShapeDtypeStruct((seq_len, width), BF16),
            jax.ShapeDtypeStruct((1, width), F32),
            jax.ShapeDtypeStruct((1, seq_len), F32),
        ]
        + [jax.ShapeDtypeStruct(table.shape, BF16) for table in tables],
        [
            pltpu.VMEM((seq_len, vocab), F32),
            pltpu.VMEM((seq_len, vocab), BF16),
            pltpu.VMEM((blocks, 2, LANES, LANES), F32),
            pltpu.VMEM((width, seq_len), BF16),
            pltpu.VMEM((blocks, 8, LANES), F32),
            pltpu.VMEM((3, blocks, 8, LANES), F32),
            pltpu.VMEM((blocks, 8, LANES), F32),
            pltpu.VMEM((3, blocks, 8, LANES), F32),
        ]
        + Exchange.scratch(chunk, width, BACKWARD_KIND)
        + sems(3)
        + [pltpu.SemaphoreType.DMA((3, blocks))] * 4,
        collective_id,
        loads,
    )


def sum_ways(place, me, slow, fast, slows, group):
    near = [{NARROW: lax.rem(place + step, group)} for step in range(1, group)]
    return near, {WIDE: me + 1 - 2 * fast}


def tail_kernel(
    layers, branch, ids_all, losses, full, *refs, carry,
):
    gain_parts, refs = refs[: 2 * layers + 1], refs[2 * layers + 1 :]
    squares, refs = refs[: len(refs) - 31], refs[len(refs) - 31 :]
    tail_body(branch, ids_all, losses, full, gain_parts, squares, *refs, carry)


def tail_body(
    branch, ids_all, losses, full, gain_parts, squares,
    d_table, d_full, d_small, scalars,
    out_blocks, all_in, picks, total, gains_out, gains_in, blocks, block_in, line_out, line_in,
    fast_in, sums, slow_in, near, along, across,
    wide_send, wide_recv, far_send, far_recv, near_send, near_recv,
    pair_send, pair_recv, line_send, line_recv, sum_sems,
    carry,
):
    seq_len, width = branch.shape
    quarter, half = seq_len // 4, seq_len // 2
    owners = ids_all.shape[0]
    share, vocab = d_table.shape
    sibling, partner, mine, other = group_places(seq_len)
    place = lax.axis_index(NARROW)
    side = lax.div(place, 2)
    me, slow, fast, slows = wide_places(owners)
    beside = {WIDE: me + 1 - 2 * fast}
    group = near.shape[0]
    first = place * vocab
    around = [lax.rem(me + step, owners) for step in range(owners)]
    at_quarter = pl.multiple_of(mine + side * quarter, quarter)
    across_quarter = pl.multiple_of(mine + (1 - side) * quarter, quarter)

    def along_way(step):
        return {WIDE: 2 * lax.rem(slow + step, slows) + fast}

    def wide_copy(step):
        return remote(
            out_blocks.at[around[step]], all_in.at[me, pl.ds(at_quarter, quarter)],
            wide_send.at[step], wide_recv.at[step], {WIDE: around[step]},
        )

    def far_copy(step):
        rows = all_in.at[around[step], pl.ds(at_quarter, quarter)]
        return remote(rows, rows, far_send.at[step], far_recv.at[step], partner)

    def near_copy(step):
        rows = all_in.at[around[step], pl.ds(mine, half)]
        return remote(rows, rows, near_send.at[step], near_recv.at[step], sibling)

    def block(owner):
        return full.at[:, owner]

    def pair_copy(step):
        return remote(
            block(2 * lax.rem(slow + step, slows) + 1 - fast), fast_in.at[step],
            pair_send.at[step], pair_recv.at[step], beside,
        )

    def line_copy(step):
        return remote(sums.at[step], slow_in.at[step], line_send.at[step], line_recv.at[step], along_way(step))

    def gain_near():
        return remote(gains_out, gains_in, sum_sems.at[0, 0], sum_sems.at[1, 0], sibling)

    def gain_pair(step):
        return remote(
            blocks.at[2 * lax.rem(slow + step, slows) + 1 - fast], block_in.at[step],
            sum_sems.at[2, step], sum_sems.at[3, step], beside,
        )

    def gain_line(step):
        return remote(line_out.at[step], line_in.at[step], sum_sems.at[4, step], sum_sems.at[5, step], along_way(step))

    near_ways = [{NARROW: lax.rem(place + step, group)} for step in range(1, group)]
    greet([{WIDE: device} for device in around[1:]] + near_ways)
    for step in range(slows):
        pair_copy(step).start()
    gains_out[...] = jnp.zeros(gains_out.shape, F32)
    for row, part in enumerate(gain_parts):
        gains_out[row : row + 1, :] = part[...]
    gain_near().start()
    for owner in range(owners):
        out_blocks[owner] = dot_nt(
            branch[pl.ds(at_quarter, quarter), :], feature_places(owner, width, share)
        ).astype(BF16)
    for step in range(1, owners):
        wide_copy(step).start()
    all_in[me, pl.ds(at_quarter, quarter), :] = out_blocks[me]
    carry.start()
    gain_near().wait_recv()
    both = gains_out[...] + gains_in[...]
    for owner in range(owners):
        blocks[owner] = lax.dot_general(
            both, feature_places(owner, width, share).astype(F32), (((1,), (1,)), ((), ())),
            precision=lax.Precision.HIGHEST, preferred_element_type=F32,
        )
    for step in range(slows):
        gain_pair(step).start()

    def hand_on(step):
        if step:
            wide_copy(owners - step).wait_recv()
        far_copy(step).start()

    def hand_over(step):
        far_copy(step).wait_recv()
        near_copy(step).start()

    def gather_grad(step, first_turn):
        near_copy(step).wait_recv()
        row = around[step]

        def make(b, _):
            rows = rows_at(0, b, LANES)
            for t, pick in enumerate(token_picks(ids_all[row, pl.ds(b, 1), :], vocab, first)):
                picks[rows, t * LANES : (t + 1) * LANES] = pick
            return 0

        lax.fori_loop(0, seq_len // LANES, make, 0)
        turned = jnp.transpose(all_in[row])

        def columns(i, _):
            where = pl.ds(pl.multiple_of(i * TILE, TILE), TILE)
            part = dot_nn(turned, picks[:, where])
            total[:, where] = part if first_turn else total[:, where] + part
            return 0

        lax.fori_loop(0, vocab // TILE, columns, 0)

    order = [0] + list(range(1, owners))
    for turn in range(owners + 2):
        if turn < owners:
            hand_on(order[turn])
        if 1 <= turn < owners + 1:
            hand_over(order[turn - 1])
        if turn == 1:
            for step in list(range(1, slows)) + [0]:
                pair_copy(step).wait_recv()
                owner = 2 * lax.rem(slow + step, slows) + fast
                sums[step] = (block(owner)[...].astype(F32) + fast_in[step].astype(F32)).astype(BF16)
                if step:
                    line_copy(step).start()
            for step in list(range(1, slows)) + [0]:
                gain_pair(step).wait_recv()
                line_out[step] = blocks[2 * lax.rem(slow + step, slows) + fast] + block_in[step]
                if step:
                    gain_line(step).start()
        if turn >= 2:
            gather_grad(order[turn - 2], turn == 2)
    d_table[...] = total[:share, :]
    result = sums[0].astype(F32)
    small = line_out[0]
    for step in range(1, slows):
        line_copy(step).wait_recv()
        result = result + slow_in[step].astype(F32)
        gain_line(step).wait_recv()
        small = small + line_in[step]
    d_full[...] = result
    d_small[...] = small
    carry.finish()
    square = jnp.sum(result * result) + jnp.sum(d_table[...] * d_table[...])
    for part in squares:
        square = square + part[0, 0]
    for load in carry.loads:
        square = square + load.squares[0, 0]
    lead = (place == 0).astype(F32)
    square = square + lead * jnp.sum(small * small)
    lanes = lax.broadcasted_iota(jnp.int32, (8, LANES), 1)
    given = jnp.where(lanes == 0, square, jnp.where(lanes == 1, lead * jnp.sum(losses[...]), 0.0))

    def scalar_near(step):
        return remote(near.at[place], near.at[place], sum_sems.at[6, step], sum_sems.at[7, step], near_ways[step - 1])

    def scalar_line(step):
        return remote(along.at[slow], along.at[slow], sum_sems.at[8, step], sum_sems.at[9, step], along_way(step))

    near[place] = given
    for step in range(1, group):
        scalar_near(step).start()
    for step in range(1, group):
        scalar_near(step).wait()
    along[slow] = jnp.sum(near[...], axis=0)
    for step in range(1, slows):
        scalar_line(step).start()
    for step in range(1, slows):
        scalar_line(step).wait()
    across[0] = jnp.sum(along[...], axis=0)
    last = remote(across.at[0], across.at[1], sum_sems.at[10, 0], sum_sems.at[11, 0], beside)
    last.start()
    last.wait()
    scalars[...] = across[0] + across[1]
    gain_near().wait_send()
    for step in range(owners):
        far_copy(step).wait_send()
        near_copy(step).wait_send()
        if step:
            wide_copy(step).wait_send()
    for step in range(slows):
        pair_copy(step).wait_send()
        gain_pair(step).wait_send()
        if step:
            line_copy(step).wait_send()
            gain_line(step).wait_send()


def tail(branch, ids_all, losses, full, gain_parts, squares, share, vocab, group, collective_id, loads):
    seq_len, width = branch.shape
    owners = ids_all.shape[0]
    slows = owners // 2
    shape = full.shape[:1] + full.shape[2:]
    dma = pltpu.SemaphoreType.DMA
    small = (8, LANES)
    return run(
        functools.partial(tail_kernel, (len(gain_parts) - 1) // 2),
        "tail",
        [branch, ids_all, losses, full, *gain_parts, *squares],
        [
            jax.ShapeDtypeStruct((share, vocab), F32),
            jax.ShapeDtypeStruct(shape, F32),
            jax.ShapeDtypeStruct(small, F32),
            jax.ShapeDtypeStruct(small, F32),
        ],
        [
            pltpu.VMEM((owners, seq_len // 4, LANES), BF16),
            pltpu.VMEM((owners, seq_len, LANES), BF16),
            pltpu.VMEM((seq_len, vocab), BF16),
            pltpu.VMEM((LANES, vocab), F32),
            pltpu.VMEM((8, width), F32),
            pltpu.VMEM((8, width), F32),
            pltpu.VMEM((owners,) + small, F32),
            pltpu.VMEM((slows,) + small, F32),
            pltpu.VMEM((slows,) + small, F32),
            pltpu.VMEM((slows,) + small, F32),
            pltpu.VMEM((slows,) + shape, BF16),
            pltpu.VMEM((slows,) + shape, BF16),
            pltpu.VMEM((slows,) + shape, BF16),
            pltpu.VMEM((group,) + small, F32),
            pltpu.VMEM((slows,) + small, F32),
            pltpu.VMEM((2,) + small, F32),
        ]
        + [dma((owners,))] * 6
        + [dma((slows,))] * 4
        + [dma((12, max(slows, group)))],
        collective_id,
        loads,
    )


PIECES = 4
TABLE, ATTN_IN, ATTN_OUT, FFN_IN, FFN_OUT = range(5)


def shares_tile(wide, narrow, noised, attn_out, ffn_in, tables):
    rows, seq_len = noised.shape
    return (
        narrow == 4
        and wide % 2 == 0
        and rows == 1
        and seq_len % (2 * CHUNKS * 128) == 0
        and attn_out.shape[1] % 16 == 0
        and attn_out.shape[1] <= LANES
        and ffn_in.shape[2] % 128 == 0
        and tables.shape[1] == attn_out.shape[1]
        and tables.shape[2] % (PIECES * TILE) == 0
    )


def per_device(wide, narrow, *arrays):
    noised, attn_out, ffn_in, tables = arrays[0], arrays[6], arrays[7], arrays[9]
    if shares_tile(wide, narrow, noised, attn_out, ffn_in, tables):
        return tiled_device(wide, *arrays)
    return general_device(*arrays)


def tiled_device(
    wide,
    noised,
    clean,
    timesteps,
    segments,
    counted,
    attn_in,
    attn_out,
    ffn_in,
    ffn_out,
    tables,
    gains,
    attn_in_mean,
    attn_out_mean,
    ffn_in_mean,
    ffn_out_mean,
    tables_mean,
    gains_mean,
    attn_in_square,
    attn_out_square,
    ffn_in_square,
    ffn_out_square,
    tables_square,
    gains_square,
):
    layers = attn_in.shape[0]
    gain_rows, gain_cols = gains.shape
    mask = counted.reshape(-1).astype(jnp.float32)
    seq_len = mask.shape[0]
    half = seq_len // 2
    core = lax.rem(lax.axis_index(NARROW), 2)
    share, vocab = tables.shape[1:]
    leads = (1, 0, 0, 0)
    four = (attn_in, attn_out, ffn_in, ffn_out)

    def joined(value, lead):
        return value.reshape(value.shape[:lead] + (-1,) + value.shape[lead + 2 :])

    step_flat = timesteps.reshape(-1)
    extra = time_features(lax.dynamic_slice(step_flat, (core * half,), (half,)))
    ids = noised.reshape(-1, LANES)
    quarter = vocab // PIECES
    windows = [(k * quarter, quarter) for k in range(PIECES)]
    (residual, normed, gain_w, counts, ids_all), carried = embed(
        ids, counted, gains, extra, tables, wide, 0,
        [
            GatherLoad(attn_in, 0, 1, wide, EARLY),
            GatherLoad(attn_out, 0, 0, wide, MIDDLE),
            GatherLoad(ffn_in, 0, 0, wide, LAST, late=True),
            SlowLoad(ffn_out, 0, 0, wide),
        ],
    )
    token_total = counts[gain_rows, 0]
    query_w, output_w, expand_w, reduce_line = carried
    next_id = 1
    tables_w = []
    table_lines = []
    key_seg, query_seg = segments.reshape(-1, 1), segments.reshape(1, -1)
    kept = []
    for layer in range(layers):
        more = layer + 1 < layers
        loads = [FastLoad(reduce_line, 0, wide)]
        if more:
            loads.append(SlowLoad(ffn_in, layer + 1, 0, wide))
        else:
            loads.append(SlowLoad(tables, 1, 0, wide, windows[1]))
        query_w, output_w, expand_w = joined(query_w, 1), joined(output_w, 0), joined(expand_w, 0)
        (projected, mixed), carried = attention(normed, query_w, key_seg, query_seg, next_id, loads)
        reduce_w = joined(carried[0], 0)
        if more:
            loads = [
                FastLoad(carried[1], 0, wide),
                GatherLoad(attn_in, layer + 1, 1, wide, EARLY),
                GatherLoad(attn_out, layer + 1, 0, wide, EARLY),
                SlowLoad(ffn_out, layer + 1, 0, wide),
            ]
            if layer + 2 == layers:
                loads.append(SlowLoad(tables, 1, 0, wide, windows[0]))
        else:
            loads = [
                FastLoad(table_line, 0, wide),
                FastLoad(carried[1], 0, wide),
                GatherLoad(tables, 1, 0, wide, EARLY, windows[2]),
                GatherLoad(tables, 1, 0, wide, MIDDLE, windows[3]),
            ]
        (middle, normed_two, before, after, result, normed_next), carried = ffn_forward(
            layer, mixed, residual, output_w, expand_w, reduce_w, gain_w, next_id + 1, loads
        )
        next_id += 2
        kept.append(
            (residual, normed, projected, mixed, middle, normed_two, before, after)
            + (query_w, output_w, expand_w, reduce_w)
        )
        residual, normed = result, normed_next
        if more:
            expand_w, query_w, output_w, reduce_line, *rest = carried
            if rest:
                table_line = rest[0]
        else:
            tables_w = [joined(value, 0) for value in carried]

    noised_flat, clean_flat = noised.reshape(-1), clean.reshape(-1)
    info = jnp.stack(
        [noised_flat.astype(F32), clean_flat.astype(F32), step_flat.astype(F32), mask / token_total, mask]
        + [jnp.zeros_like(mask)] * 3
    )
    (grad, branch, gain_final, losses, *d_last), _ = loss_and_back(
        2 * layers, normed, tables_w, info, residual, gain_w, next_id, []
    )
    next_id += 1
    gain_grads = [None] * (2 * layers) + [gain_final]
    own, squares = {}, []

    def by_owner(value, lead):
        shape = value.shape
        return value.reshape(shape[:lead] + (wide, shape[lead] // wide) + shape[lead + 1 :])

    class Route:
        waiting, halfway = [], []

        def take(self, pairs, lines):
            self.now = self.waiting[:pairs], self.halfway[:lines]
            self.waiting, self.halfway = self.waiting[pairs:], self.halfway[lines:]
            return [PairLoad(by_owner(value, lead), lead, wide) for _, value, lead in self.now[0]] + [
                LineLoad(sums, wide) for _, sums in self.now[1]
            ]

        def back(self, results):
            pairs, lines = self.now
            self.halfway = self.halfway + [(key, sums) for (key, _, _), sums in zip(pairs, results)]
            for k, (key, _) in enumerate(lines):
                own[key] = results[len(pairs) + 2 * k]
                squares.append(results[len(pairs) + 2 * k + 1])

    route = Route()
    route.waiting = [((TABLE, k), piece, 0) for k, piece in enumerate(d_last)]
    for layer in reversed(range(layers)):
        residual, normed, projected, mixed, middle, normed_two, before, after, *four_w = kept[layer]
        query_w, output_w, expand_w, reduce_w = four_w
        top = layer == layers - 1
        loads = route.take(3 if top else 2, 3)
        (grad_middle, grad_attn, grad_mixed, d_red, d_in, d_out, gain_two), carried = ffn_backward(
            2 * layer + 1, grad, branch, reduce_w, expand_w, output_w, before, after,
            normed_two, middle, gain_w, mixed, next_id, loads,
        )
        route.back(carried)
        route.waiting += [((FFN_OUT, layer), d_red, 0), ((FFN_IN, layer), d_in, 0)]
        loads = route.take(1, 2)
        (grad_projected,), carried = attention_back(projected, grad_mixed, key_seg, query_seg, next_id + 1, loads)
        route.back(carried)
        route.waiting += [((ATTN_OUT, layer), d_out, 0)]
        loads = route.take(2, 2)
        (grad, branch, d_query, gain_one), carried = norm_backward(
            2 * layer, grad_projected, query_w, normed, residual, gain_w, grad_middle,
            math.sqrt(D) if layer == 0 else None, next_id + 2, loads,
        )
        route.back(carried)
        route.waiting += [((ATTN_IN, layer), d_query, 1)]
        next_id += 3
        gain_grads[2 * layer], gain_grads[2 * layer + 1] = gain_one, gain_two
    (key, last_full, _), = route.waiting
    lines = route.halfway
    (own_first, own[key], total_small, scalars), carried = tail(
        branch, ids_all, losses, by_owner(last_full, 1), gain_grads, squares, share, vocab, 4, next_id,
        [LineLoad(value, wide) for _, value in lines],
    )
    for k, (key, _) in enumerate(lines):
        own[key] = carried[2 * k]
    grad_attn_in, grad_attn_out, grad_ffn_in, grad_ffn_out = [
        jnp.stack([own[name, index] for index in range(layers)]) for name in (ATTN_IN, ATTN_OUT, FFN_IN, FFN_OUT)
    ]
    grad_tables = jnp.stack([own_first, jnp.concatenate([own[TABLE, k] for k in range(PIECES)], axis=1)])
    grad_gains = total_small[:gain_rows, :gain_cols]
    total_square, loss_sum = scalars[0, 0], scalars[0, 1]
    grad_norm = jnp.sqrt(total_square)
    factor = jnp.minimum(1.0, CLIP_NORM / (grad_norm + 1e-06))
    results = [loss_sum, token_total, grad_norm]
    for weight, gradient, first, second, decay, rate in (
        (attn_in, grad_attn_in, attn_in_mean, attn_in_square, WEIGHT_DECAY, LEARN_RATE),
        (attn_out, grad_attn_out, attn_out_mean, attn_out_square, WEIGHT_DECAY, LEARN_RATE),
        (ffn_in, grad_ffn_in, ffn_in_mean, ffn_in_square, WEIGHT_DECAY, LEARN_RATE),
        (ffn_out, grad_ffn_out, ffn_out_mean, ffn_out_square, WEIGHT_DECAY, LEARN_RATE),
        (tables, grad_tables, tables_mean, tables_square, WEIGHT_DECAY, LEARN_RATE),
        (gains, grad_gains, gains_mean, gains_square, 0.0, GAIN_RATE),
    ):
        results += adam(weight, factor * gradient, first, second, decay, rate)
    return tuple(results)


def solution(mesh):
    wide, narrow = mesh.shape[WIDE], mesh.shape[NARROW]
    placed = (
        P(WIDE, None),
        P(WIDE, None),
        P(WIDE, None),
        P(WIDE, None),
        P(WIDE, None),
        P(None, None, WIDE, NARROW),
        P(None, WIDE, NARROW),
        P(None, WIDE, NARROW),
        P(None, WIDE, NARROW),
        P(None, WIDE, NARROW),
        P(None, WIDE),
        P(None, None, WIDE, NARROW),
        P(None, WIDE, NARROW),
        P(None, WIDE, NARROW),
        P(None, WIDE, NARROW),
        P(None, WIDE, NARROW),
        P(None, WIDE),
        P(None, None, WIDE, NARROW),
        P(None, WIDE, NARROW),
        P(None, WIDE, NARROW),
        P(None, WIDE, NARROW),
        P(None, WIDE, NARROW),
        P(None, WIDE),
    )
    return jax.shard_map(
        functools.partial(per_device, wide, narrow),
        mesh=mesh,
        in_specs=placed,
        out_specs=(
            P(),
            P(),
            P(),
            P(None, None, WIDE, NARROW),
            P(None, None, WIDE, NARROW),
            P(None, None, WIDE, NARROW),
            P(None, None, WIDE, NARROW),
            P(None, WIDE, NARROW),
            P(None, WIDE, NARROW),
            P(None, WIDE, NARROW),
            P(None, WIDE, NARROW),
            P(None, WIDE, NARROW),
            P(None, WIDE, NARROW),
            P(None, WIDE, NARROW),
            P(None, WIDE, NARROW),
            P(None, WIDE, NARROW),
            P(None, WIDE, NARROW),
            P(None, WIDE, NARROW),
            P(None, WIDE, NARROW),
            P(None, WIDE, NARROW),
            P(None, WIDE, NARROW),
            P(None, WIDE, NARROW),
            P(None, WIDE, NARROW),
            P(None, WIDE),
            P(None, WIDE),
            P(None, WIDE),
            P(None, WIDE),
        ),
        check_vma=False,
    )
```

```python
import functools
import math

import jax
import jax.numpy as jnp
from jax import lax
from jax.experimental import pallas as pl
from jax.experimental.pallas import tpu as pltpu
from jax.sharding import PartitionSpec as P

D = 768
HD = 64
V = 8192
STEPS = 1000
ADAM_STEP = 10


NORM_EPS = 1e-05
LEARN_RATE = 0.05
GAIN_RATE = 0.75
FIRST_DECAY = 0.9
SECOND_DECAY = 0.999
ADAM_EPS = 1e-08
WEIGHT_DECAY = 0.01
CLIP_NORM = 0.005
WIDE, NARROW = "wide", "narrow"


def add_heads(partial_value):
    return lax.psum(partial_value, NARROW)


def back_heads(partial_value):
    return lax.psum(partial_value, NARROW)


def rms_forward(value, gain):
    scale_row = lax.rsqrt(jnp.mean(value * value, axis=-1, keepdims=True) + NORM_EPS)
    return (value * scale_row * gain, scale_row)


def rms_backward(grad, value, scale_row, gain):
    unit = value * scale_row
    scaled = grad * gain
    back = scale_row * (scaled - unit * jnp.mean(scaled * unit, axis=-1, keepdims=True))
    return (back, jnp.sum(grad * unit, axis=0))


def time_features(timestep_row):
    half_width = D // 2
    rates = jnp.exp(-math.log(10000.0) * jnp.arange(half_width, dtype=jnp.float32) / half_width)
    angles = timestep_row.astype(jnp.float32)[:, None] * rates[None, :]
    return jnp.concatenate([jnp.sin(angles), jnp.cos(angles)], axis=1)


def masked_scores(queries, key_rows, segment):
    scores = jnp.einsum(
        "qhd,khd->hqk", queries, key_rows, preferred_element_type=jnp.float32
    ) * HD ** (-0.5)
    return jnp.where((segment[:, None] == segment[None, :])[None], scores, -1e30)


def attend(entry):
    queries, key_rows, values, segment = entry
    scores = masked_scores(queries, key_rows, segment)
    row_top = jnp.max(scores, axis=-1, keepdims=True)
    log_total = row_top + jnp.log(jnp.sum(jnp.exp(scores - row_top), axis=-1, keepdims=True))
    probs = jnp.exp(scores - log_total).astype(jnp.bfloat16)
    mixed = jnp.einsum("hqk,khd->qhd", probs, values, preferred_element_type=jnp.float32)
    return (mixed.astype(jnp.bfloat16), log_total)


def attend_back(entry):
    queries, key_rows, values, segment, log_total, grad_mixed = entry
    probs = jnp.exp(masked_scores(queries, key_rows, segment) - log_total)
    grad_probs = jnp.einsum("qhd,khd->hqk", grad_mixed, values, preferred_element_type=jnp.float32)
    grad_scores = (
        probs * (grad_probs - jnp.sum(probs * grad_probs, axis=-1, keepdims=True))
    ).astype(jnp.bfloat16)
    grad_query = jnp.einsum(
        "hqk,khd->qhd", grad_scores, key_rows, preferred_element_type=jnp.float32
    ) * HD ** (-0.5)
    grad_key = jnp.einsum(
        "hqk,qhd->khd", grad_scores, queries, preferred_element_type=jnp.float32
    ) * HD ** (-0.5)
    grad_value = jnp.einsum(
        "hqk,qhd->khd", probs.astype(jnp.bfloat16), grad_mixed, preferred_element_type=jnp.float32
    )
    return (grad_query, grad_key, grad_value)


def layer_forward(residual, segments, query_w, output_w, expand_w, reduce_w, gain_attn, gain_ffn):
    seq_count, seq_len = segments.shape
    normed, scale_one = rms_forward(residual, gain_attn)
    normed = normed.astype(jnp.bfloat16)
    projected = jnp.einsum(
        "sd,cde->cse", normed, query_w, preferred_element_type=jnp.float32
    ).astype(jnp.bfloat16)
    heads = projected.reshape(3, seq_count, seq_len, -1, HD)
    mixed, log_total = lax.map(attend, (heads[0], heads[1], heads[2], segments))
    mixed = mixed.reshape(seq_count * seq_len, -1)
    middle = residual + add_heads(
        jnp.einsum("se,de->sd", mixed, output_w, preferred_element_type=jnp.float32)
    )
    normed_two, scale_two = rms_forward(middle, gain_ffn)
    normed_two = normed_two.astype(jnp.bfloat16)
    before = jnp.dot(normed_two, expand_w, preferred_element_type=jnp.float32)
    after = jax.nn.gelu(before).astype(jnp.bfloat16)
    result = middle + add_heads(
        jnp.einsum("sf,df->sd", after, reduce_w, preferred_element_type=jnp.float32)
    )
    return (
        result,
        (
            residual,
            scale_one,
            normed,
            projected,
            log_total,
            mixed,
            middle,
            scale_two,
            normed_two,
            before,
            after,
        ),
    )


def layer_backward(
    grad, kept, segments, query_w, output_w, expand_w, reduce_w, gain_attn, gain_ffn
):
    (
        residual,
        scale_one,
        normed,
        projected,
        log_total,
        mixed,
        middle,
        scale_two,
        normed_two,
        before,
        after,
    ) = kept
    seq_count, seq_len = segments.shape
    grad_branch = grad.astype(jnp.bfloat16)
    grad_after = jnp.dot(grad_branch, reduce_w, preferred_element_type=jnp.float32)
    grad_reduce = jnp.einsum("sd,sf->df", grad_branch, after, preferred_element_type=jnp.float32)
    _, gelu_pull = jax.vjp(jax.nn.gelu, before)
    grad_before = gelu_pull(grad_after)[0].astype(jnp.bfloat16)
    grad_expand = jnp.einsum(
        "sd,sf->df", normed_two, grad_before, preferred_element_type=jnp.float32
    )
    grad_normed_two = back_heads(
        jnp.einsum("sf,df->sd", grad_before, expand_w, preferred_element_type=jnp.float32)
    )
    grad_middle, grad_gain_ffn = rms_backward(grad_normed_two, middle, scale_two, gain_ffn)
    grad_middle = grad_middle + grad
    grad_attn = grad_middle.astype(jnp.bfloat16)
    grad_mixed = jnp.dot(grad_attn, output_w, preferred_element_type=jnp.float32).astype(
        jnp.bfloat16
    )
    grad_output = jnp.einsum("sd,se->de", grad_attn, mixed, preferred_element_type=jnp.float32)
    heads = projected.reshape(3, seq_count, seq_len, -1, HD)
    grad_query, grad_key, grad_value = lax.map(
        attend_back,
        (
            heads[0],
            heads[1],
            heads[2],
            segments,
            log_total,
            grad_mixed.reshape(seq_count, seq_len, -1, HD),
        ),
    )
    grad_projected = (
        jnp.stack([grad_query, grad_key, grad_value])
        .reshape(3, seq_count * seq_len, -1)
        .astype(jnp.bfloat16)
    )
    grad_query_w = jnp.einsum(
        "sd,cse->cde", normed, grad_projected, preferred_element_type=jnp.float32
    )
    grad_normed = back_heads(
        jnp.einsum("cse,cde->sd", grad_projected, query_w, preferred_element_type=jnp.float32)
    )
    grad_input, grad_gain_attn = rms_backward(grad_normed, residual, scale_one, gain_attn)
    return (
        grad_input + grad_middle,
        (
            grad_query_w,
            grad_output,
            grad_expand,
            grad_reduce,
            jnp.stack([grad_gain_attn, grad_gain_ffn]),
        ),
    )


def adam(weight, grad, first, second, decay, rate):
    first_new = FIRST_DECAY * first + (1.0 - FIRST_DECAY) * grad
    second_new = SECOND_DECAY * second + (1.0 - SECOND_DECAY) * grad * grad
    first_hat = first_new / (1.0 - FIRST_DECAY**ADAM_STEP)
    second_hat = second_new / (1.0 - SECOND_DECAY**ADAM_STEP)
    weight_new = weight - rate * (first_hat / (jnp.sqrt(second_hat) + ADAM_EPS) + decay * weight)
    return (weight_new, first_new, second_new, weight_new.astype(jnp.bfloat16))


def general_device(
    noised,
    clean,
    timesteps,
    segments,
    counted,
    attn_in,
    attn_out,
    ffn_in,
    ffn_out,
    tables,
    gains,
    attn_in_mean,
    attn_out_mean,
    ffn_in_mean,
    ffn_out_mean,
    tables_mean,
    gains_mean,
    attn_in_square,
    attn_out_square,
    ffn_in_square,
    ffn_out_square,
    tables_square,
    gains_square,
):
    layers = attn_in.shape[0]
    mask = counted.reshape(-1).astype(jnp.float32)
    token_total = lax.psum(jnp.sum(mask), WIDE)
    query_w, output_w, expand_w, reduce_w, table_w, gain_low = (
        lax.all_gather(attn_in.astype(jnp.bfloat16), WIDE, axis=2, tiled=True),
        lax.all_gather(attn_out.astype(jnp.bfloat16), WIDE, axis=1, tiled=True),
        lax.all_gather(ffn_in.astype(jnp.bfloat16), WIDE, axis=1, tiled=True),
        lax.all_gather(ffn_out.astype(jnp.bfloat16), WIDE, axis=1, tiled=True),
        lax.all_gather(tables.astype(jnp.bfloat16), WIDE, axis=1, tiled=True),
        lax.all_gather(gains.astype(jnp.bfloat16), WIDE, axis=1, tiled=True),
    )
    gain_w = gain_low.astype(jnp.float32)
    noised_flat = noised.reshape(-1)
    clean_flat = clean.reshape(-1)
    step_flat = timesteps.reshape(-1)
    vocab_local = table_w.shape[2]
    vocab_ids = lax.axis_index(NARROW) * vocab_local + jnp.arange(vocab_local, dtype=jnp.int32)
    picks = (noised_flat[:, None] == vocab_ids[None, :]).astype(jnp.bfloat16)
    looked = add_heads(
        jnp.einsum("sv,dv->sd", picks, table_w[0], preferred_element_type=jnp.float32)
    )
    residual = math.sqrt(D) * looked + time_features(step_flat)
    kept_layers = []
    for layer_index in range(layers):
        residual, kept = layer_forward(
            residual,
            segments,
            query_w[layer_index],
            output_w[layer_index],
            expand_w[layer_index],
            reduce_w[layer_index],
            gain_w[2 * layer_index],
            gain_w[2 * layer_index + 1],
        )
        kept_layers.append(kept)
    final, scale_final = rms_forward(residual, gain_w[2 * layers])
    final_low = final.astype(jnp.bfloat16)
    logits = jnp.dot(final_low, table_w[1], preferred_element_type=jnp.float32)
    local_top = jnp.max(logits, axis=1)
    row_top = lax.pmax(local_top, NARROW)
    row_total = lax.psum(jnp.sum(jnp.exp(logits - row_top[:, None]), axis=1), NARROW)
    log_probs = logits - (row_top + jnp.log(row_total))[:, None]
    probs = jnp.exp(log_probs)
    clamped = jnp.maximum(step_flat, 2).astype(jnp.float32)[:, None]
    beta = 1.0 / (STEPS - clamped + 1.0)
    retain = (STEPS - clamped + 1.0) / STEPS
    spread = (clamped - 1.0) / (STEPS * V)
    at_noised = (vocab_ids[None, :] == noised_flat[:, None]).astype(jnp.float32)
    at_clean = (vocab_ids[None, :] == clean_flat[:, None]).astype(jnp.float32)
    forward_fac = beta / V + (1.0 - beta) * at_noised
    backward_fac = retain * at_clean + spread
    joint = forward_fac * backward_fac
    marginal = retain * probs + spread
    joint_total, cross, model_total, weighted, aligned, clean_logp = lax.psum(
        (
            jnp.sum(joint, axis=1),
            jnp.sum(joint * (jnp.log(backward_fac) - jnp.log(marginal)), axis=1),
            jnp.sum(forward_fac * marginal, axis=1),
            jnp.sum(probs * joint / marginal, axis=1),
            jnp.sum(forward_fac * probs, axis=1),
            jnp.sum(at_clean * log_probs, axis=1),
        ),
        NARROW,
    )
    divergence = cross / joint_total - jnp.log(joint_total) + jnp.log(model_total)
    first_step = step_flat == 1
    losses = jnp.where(first_step, -clean_logp, divergence)
    pull = retain * (
        -(joint / joint_total[:, None]) / marginal + forward_fac / model_total[:, None]
    )
    centre = retain[:, 0] * (-weighted / joint_total + aligned / model_total)
    grad_kl = probs * (pull - centre[:, None])
    grad_recon = probs - at_clean
    grad_logits = (
        (mask / token_total)[:, None] * jnp.where(first_step[:, None], grad_recon, grad_kl)
    ).astype(jnp.bfloat16)
    grad_table_out = jnp.einsum(
        "sd,sv->dv", final_low, grad_logits, preferred_element_type=jnp.float32
    )
    grad_final = back_heads(
        jnp.einsum("sv,dv->sd", grad_logits, table_w[1], preferred_element_type=jnp.float32)
    )
    grad_x, grad_gain_final = rms_backward(grad_final, residual, scale_final, gain_w[2 * layers])
    layer_grads = [None] * layers
    for layer_index in reversed(range(layers)):
        grad_x, produced = layer_backward(
            grad_x,
            kept_layers[layer_index],
            segments,
            query_w[layer_index],
            output_w[layer_index],
            expand_w[layer_index],
            reduce_w[layer_index],
            gain_w[2 * layer_index],
            gain_w[2 * layer_index + 1],
        )
        layer_grads[layer_index] = produced
    grad_look = (math.sqrt(D) * grad_x).astype(jnp.bfloat16)
    grad_table_in = jnp.einsum("sd,sv->dv", grad_look, picks, preferred_element_type=jnp.float32)
    stacked = [jnp.stack([entry[which] for entry in layer_grads]) for which in range(5)]
    gain_layers = stacked[4].reshape(2 * layers, -1)
    grad_tables_all = jnp.stack([grad_table_in, grad_table_out])
    grad_attn_in, grad_attn_out, grad_ffn_in, grad_ffn_out, grad_tables, grad_gains = (
        lax.psum_scatter(stacked[0], WIDE, scatter_dimension=2, tiled=True),
        lax.psum_scatter(stacked[1], WIDE, scatter_dimension=1, tiled=True),
        lax.psum_scatter(stacked[2], WIDE, scatter_dimension=1, tiled=True),
        lax.psum_scatter(stacked[3], WIDE, scatter_dimension=1, tiled=True),
        lax.psum_scatter(grad_tables_all, WIDE, scatter_dimension=1, tiled=True),
        lax.psum_scatter(
            jnp.concatenate([gain_layers, grad_gain_final[None, :]], axis=0),
            WIDE,
            scatter_dimension=1,
            tiled=True,
        ),
    )
    narrow_first = (lax.axis_index(NARROW) == 0).astype(jnp.float32)
    squares = (
        jnp.sum(grad_attn_in * grad_attn_in)
        + jnp.sum(grad_attn_out * grad_attn_out)
        + jnp.sum(grad_ffn_in * grad_ffn_in)
        + jnp.sum(grad_ffn_out * grad_ffn_out)
        + jnp.sum(grad_tables * grad_tables)
        + narrow_first * jnp.sum(grad_gains * grad_gains)
    )
    squares, loss_sum = lax.psum(
        (squares, narrow_first * jnp.sum(mask * losses)), (WIDE, NARROW)
    )
    grad_norm = jnp.sqrt(squares)
    factor = jnp.minimum(1.0, CLIP_NORM / (grad_norm + 1e-06))
    attn_in_next, attn_in_mean_next, attn_in_square_next, attn_in_copy = adam(
        attn_in, factor * grad_attn_in, attn_in_mean, attn_in_square, WEIGHT_DECAY, LEARN_RATE
    )
    attn_out_next, attn_out_mean_next, attn_out_square_next, attn_out_copy = adam(
        attn_out, factor * grad_attn_out, attn_out_mean, attn_out_square, WEIGHT_DECAY, LEARN_RATE
    )
    ffn_in_next, ffn_in_mean_next, ffn_in_square_next, ffn_in_copy = adam(
        ffn_in, factor * grad_ffn_in, ffn_in_mean, ffn_in_square, WEIGHT_DECAY, LEARN_RATE
    )
    ffn_out_next, ffn_out_mean_next, ffn_out_square_next, ffn_out_copy = adam(
        ffn_out, factor * grad_ffn_out, ffn_out_mean, ffn_out_square, WEIGHT_DECAY, LEARN_RATE
    )
    tables_next, tables_mean_next, tables_square_next, tables_copy = adam(
        tables, factor * grad_tables, tables_mean, tables_square, WEIGHT_DECAY, LEARN_RATE
    )
    gains_next, gains_mean_next, gains_square_next, gains_copy = adam(
        gains, factor * grad_gains, gains_mean, gains_square, 0.0, GAIN_RATE
    )
    return (
        loss_sum,
        token_total,
        grad_norm,
        attn_in_next,
        attn_in_mean_next,
        attn_in_square_next,
        attn_in_copy,
        attn_out_next,
        attn_out_mean_next,
        attn_out_square_next,
        attn_out_copy,
        ffn_in_next,
        ffn_in_mean_next,
        ffn_in_square_next,
        ffn_in_copy,
        ffn_out_next,
        ffn_out_mean_next,
        ffn_out_square_next,
        ffn_out_copy,
        tables_next,
        tables_mean_next,
        tables_square_next,
        tables_copy,
        gains_next,
        gains_mean_next,
        gains_square_next,
        gains_copy,
    )


MESH = pl.DeviceIdType.MESH
SLOW, FAST = 1, 2
FIRST, SECOND, THIRD, LAST = 1, 2, 3, 4
F32 = jnp.float32
BF16 = jnp.bfloat16
CHUNKS = 4
VMEM_LIMIT = 56 * 1024 * 1024
FORWARD_KIND = BF16
BACKWARD_KIND = BF16


def whole_vmem():
    return pl.BlockSpec(memory_space=pltpu.VMEM)


def dot_nn(a, b):
    return lax.dot_general(a, b, (((1,), (0,)), ((), ())), preferred_element_type=F32)


def dot_nt(a, b):
    return lax.dot_general(a, b, (((1,), (1,)), ((), ())), preferred_element_type=F32)


def remote(src, dst, send_sem, recv_sem, device):
    return pltpu.make_async_remote_copy(
        src_ref=src,
        dst_ref=dst,
        send_sem=send_sem,
        recv_sem=recv_sem,
        device_id=device,
        device_id_type=MESH,
    )


def greet(devices):
    barrier = pltpu.get_barrier_semaphore()
    for device in devices:
        pl.semaphore_signal(barrier, inc=1, device_id=device, device_id_type=MESH)
    pl.semaphore_wait(barrier, len(devices))


def group_places(seq_len):
    me = lax.axis_index(NARROW)
    core = lax.rem(me, 2)
    half = seq_len // 2
    mine = pl.multiple_of(core * half, half)
    other = pl.multiple_of((1 - core) * half, half)
    return ({NARROW: me + 1 - 2 * core}, {NARROW: lax.rem(me + 2, 4)}, mine, other)


class Exchange:
    def __init__(self, refs, sems, base, sibling, partner):
        self.near_out, self.near_in, self.far_out, self.far_in = refs
        self.send, self.recv = sems
        self.base, self.sibling, self.partner = base, sibling, partner

    def near(self, j):
        return remote(
            self.near_out.at[j],
            self.near_in.at[j],
            self.send.at[self.base, j],
            self.recv.at[self.base, j],
            self.sibling,
        )

    def far(self, j):
        return remote(
            self.far_out.at[j],
            self.far_in.at[j],
            self.send.at[self.base + 1, j],
            self.recv.at[self.base + 1, j],
            self.partner,
        )

    def give(self, j, value):
        self.near_out[j] = value
        self.near(j).start()

    def pass_on(self, j, value):
        self.near(j).wait_recv()
        self.far_out[j] = (value + self.near_in[j]).astype(self.far_out.dtype)
        self.far(j).start()

    def take(self, j):
        self.far(j).wait_recv()
        return self.far_out[j].astype(F32) + self.far_in[j].astype(F32)

    def close(self):
        for j in range(CHUNKS):
            self.near(j).wait_send()
            self.far(j).wait_send()

    @staticmethod
    def scratch(chunk, width, kind):
        return [
            pltpu.VMEM((CHUNKS, chunk, width), F32),
            pltpu.VMEM((CHUNKS, chunk, width), F32),
            pltpu.VMEM((CHUNKS, chunk, width), kind),
            pltpu.VMEM((CHUNKS, chunk, width), kind),
        ]


class Share:
    def __init__(self, ref, sems, base, sibling, mine, chunk):
        self.ref, self.base, self.sibling, self.mine, self.chunk = ref, base, sibling, mine, chunk
        self.send, self.recv = sems

    def piece(self, j):
        rows = self.ref.at[pl.ds(pl.multiple_of(self.mine + j * self.chunk, self.chunk), self.chunk)]
        return remote(rows, rows, self.send.at[self.base, j], self.recv.at[self.base, j], self.sibling)

    def put(self, j, value):
        self.ref[pl.ds(pl.multiple_of(self.mine + j * self.chunk, self.chunk), self.chunk), :] = value
        self.piece(j).start()

    def arrived(self, j):
        self.piece(j).wait_recv()

    def close(self):
        for j in range(CHUNKS):
            self.piece(j).wait_send()


def wide_places(count):
    me = lax.axis_index(WIDE)
    fast = lax.rem(me, 2)
    slow = me // 2
    return (me, slow, fast, count // 2)


class Carry:
    def __init__(self, loads):
        self.loads = loads

    def peers(self):
        ways = []
        for load in self.loads:
            ways += [way for way in load.ways if way not in ways]
        me, slow, fast, slows = wide_places(self.loads[0].count) if self.loads else (0, 0, 0, 0)
        found = []
        if SLOW in ways:
            found += [{WIDE: 2 * lax.rem(slow + step, slows) + fast} for step in range(1, slows)]
        if FAST in ways:
            found.append({WIDE: me + 1 - 2 * fast})
        return found

    def start(self, late=0):
        for load in self.loads:
            if load.late == late:
                load.start()

    def need(self):
        for load in self.loads:
            if load.needed:
                load.finish()

    def relay(self, stage):
        for load in self.loads:
            if load.stage == stage:
                load.relay()

    def finish(self):
        self.relay(LAST)
        for load in self.loads:
            if not load.needed:
                load.finish()


def part_of(weights, index, window):
    shape = weights.shape[1:]
    return shape if window is None else shape[:-1] + (window[1],)


class SlowLoad:
    ways, late, stage, needed = (SLOW,), 0, None, False

    def __init__(self, weights, index, lead, count, window=None):
        self.index, self.lead, self.count, self.window = index, lead, count, window
        shape, slows = part_of(weights, index, window), count // 2
        self.operands, self.in_specs = [weights], [whole_vmem()]
        self.outs = [jax.ShapeDtypeStruct((slows,) + shape, BF16)]
        self.out_specs = [pl.BlockSpec(memory_space=pl.ANY)]
        self.scratch = [pltpu.VMEM(shape, BF16), pltpu.SemaphoreType.DMA] + [pltpu.SemaphoreType.DMA((slows,))] * 2

    def bind(self, given, out, scratch):
        self.shard, self.out = given[0], out[0]
        self.low, self.local, self.send, self.recv = scratch
        self.me, self.slow, self.fast, self.slows = wide_places(self.count)

    def cast(self):
        if self.window is None:
            self.low[...] = self.shard[self.index].astype(BF16)
        else:
            self.low[...] = self.shard[self.index, :, self.window[0] : self.window[0] + self.window[1]].astype(BF16)

    def target(self):
        return self.out.at[self.slow]

    def slow_copy(self, step):
        return remote(
            self.low, self.target(), self.send.at[step], self.recv.at[step],
            {WIDE: 2 * lax.rem(self.slow + step, self.slows) + self.fast},
        )

    def own_copy(self):
        return pltpu.make_async_copy(self.low, self.target(), self.local)

    def start(self):
        self.cast()
        for step in range(1, self.slows):
            self.slow_copy(step).start()
        self.own_copy().start()

    def finish(self):
        for step in range(1, self.slows):
            self.slow_copy(step).wait()
        self.own_copy().wait()


class FastLoad:
    ways, late, stage, needed = (FAST,), 0, None, False

    def __init__(self, blocks, lead, count):
        self.lead, self.count = lead, count
        shape, slows = blocks.shape[1:], count // 2
        self.operands, self.in_specs = [blocks], [pl.BlockSpec(memory_space=pl.ANY)]
        self.outs = [jax.ShapeDtypeStruct(shape[:lead] + (count,) + shape[lead:], BF16)]
        self.out_specs = [pl.BlockSpec(memory_space=pl.ANY)]
        self.scratch = [pltpu.SemaphoreType.DMA((slows,))] * 3

    def bind(self, given, out, scratch):
        self.blocks, self.out = given[0], out[0]
        self.local, self.send, self.recv = scratch
        self.me, self.slow, self.fast, self.slows = wide_places(self.count)

    def copies(self, step):
        target = self.out.at[(slice(None),) * self.lead + (2 * step + self.fast,)]
        return (
            remote(
                self.blocks.at[step], target, self.send.at[step], self.recv.at[step],
                {WIDE: self.me + 1 - 2 * self.fast},
            ),
            pltpu.make_async_copy(self.blocks.at[step], target, self.local.at[step]),
        )

    def start(self):
        for step in range(self.slows):
            for copy in self.copies(step):
                copy.start()

    def finish(self):
        for step in range(self.slows):
            for copy in self.copies(step):
                copy.wait()


class GatherLoad(SlowLoad):
    ways = (SLOW, FAST)

    def __init__(self, weights, index, lead, count, stage, window=None, late=0, needed=False):
        super().__init__(weights, index, lead, count, window)
        self.stage, self.late, self.needed = stage, late, needed
        shape, slows = part_of(weights, index, window), count // 2
        self.outs = [jax.ShapeDtypeStruct(shape[:lead] + (count,) + shape[lead:], BF16)]
        if needed:
            self.out_specs = [whole_vmem()]
        self.scratch = self.scratch + [pltpu.SemaphoreType.DMA((slows,))] * 2

    def bind(self, given, out, scratch):
        super().bind(given, out, scratch[:-2])
        self.fast_send, self.fast_recv = scratch[-2:]

    def at(self, owner):
        return self.out.at[(slice(None),) * self.lead + (owner,)]

    def target(self):
        return self.at(self.me)

    def fast_copy(self, step):
        block = self.at(2 * lax.rem(self.slow + self.slows - step, self.slows) + self.fast)
        return remote(
            self.low if step == 0 else block, block, self.fast_send.at[step], self.fast_recv.at[step],
            {WIDE: self.me + 1 - 2 * self.fast},
        )

    def start(self):
        super().start()
        self.fast_copy(0).start()

    def relay(self):
        for step in range(1, self.slows):
            self.slow_copy(step).wait_recv()
            self.fast_copy(step).start()

    def finish(self):
        for step in range(self.slows):
            self.fast_copy(step).wait()
            if step:
                self.slow_copy(step).wait_send()
        self.own_copy().wait()


class PairLoad:
    ways, late, stage, needed = (FAST,), 0, None, False

    def __init__(self, full, lead, count):
        self.lead, self.count = lead, count
        shape, slows = full.shape[:lead] + full.shape[lead + 1 :], count // 2
        self.operands, self.in_specs = [full], [whole_vmem()]
        self.outs, self.out_specs = [jax.ShapeDtypeStruct((slows,) + shape, BF16)], [whole_vmem()]
        self.scratch = [pltpu.VMEM((slows,) + shape, BF16)] + [pltpu.SemaphoreType.DMA((slows,))] * 2

    def bind(self, given, out, scratch):
        self.full, self.out = given[0], out[0]
        self.came, self.send, self.recv = scratch
        self.me, self.slow, self.fast, self.slows = wide_places(self.count)

    def block(self, step, fast):
        owner = 2 * lax.rem(self.slow + step, self.slows) + fast
        return self.full.at[(slice(None),) * self.lead + (owner,)]

    def copy(self, step):
        return remote(
            self.block(step, 1 - self.fast), self.came.at[step], self.send.at[step], self.recv.at[step],
            {WIDE: self.me + 1 - 2 * self.fast},
        )

    def start(self):
        for step in range(self.slows):
            self.copy(step).start()

    def finish(self):
        for step in range(self.slows):
            self.copy(step).wait()
            total = self.block(step, self.fast)[...].astype(F32) + self.came[step].astype(F32)
            self.out[step] = total.astype(BF16)


class LineLoad:
    ways, late, stage, needed = (SLOW,), 0, None, False

    def __init__(self, sums, count):
        self.count = count
        slows = count // 2
        self.operands, self.in_specs = [sums], [whole_vmem()]
        self.outs = [jax.ShapeDtypeStruct(sums.shape[1:], F32), jax.ShapeDtypeStruct((8, 128), F32)]
        self.out_specs = [whole_vmem()] * 2
        self.scratch = [pltpu.VMEM(sums.shape, BF16)] + [pltpu.SemaphoreType.DMA((slows,))] * 2

    def bind(self, given, out, scratch):
        self.sums, (self.out, self.squares) = given[0], out
        self.came, self.send, self.recv = scratch
        self.me, self.slow, self.fast, self.slows = wide_places(self.count)

    def copy(self, step):
        return remote(
            self.sums.at[step], self.came.at[step], self.send.at[step], self.recv.at[step],
            {WIDE: 2 * lax.rem(self.slow + step, self.slows) + self.fast},
        )

    def start(self):
        for step in range(1, self.slows):
            self.copy(step).start()

    def finish(self):
        total = self.sums[0].astype(F32)
        for step in range(1, self.slows):
            self.copy(step).wait()
            total = total + self.came[step].astype(F32)
        self.out[...] = total
        self.squares[...] = jnp.full(self.squares.shape, jnp.sum(total * total), F32)


def run(body, name, operands, outs, scratch, collective_id=None, loads=()):
    counts = [len(operands)] + [len(load.operands) for load in loads]
    counts += [len(outs)] + [len(load.outs) for load in loads]
    counts += [len(scratch)] + [len(load.scratch) for load in loads]
    parts = 1 + len(loads)

    def kernel(*refs):
        groups, place = [], 0
        for count in counts:
            groups.append(refs[place : place + count])
            place += count
        for k, load in enumerate(loads, 1):
            load.bind(groups[k], groups[parts + k], groups[2 * parts + k])
        main = groups[0] + groups[parts] + groups[2 * parts]
        body(*main, carry=Carry(list(loads)))

    results = pl.pallas_call(
        kernel,
        out_shape=tuple(outs) + tuple(out for load in loads for out in load.outs),
        in_specs=[whole_vmem()] * len(operands) + [spec for load in loads for spec in load.in_specs],
        out_specs=(whole_vmem(),) * len(outs) + tuple(spec for load in loads for spec in load.out_specs),
        scratch_shapes=list(scratch) + [s for load in loads for s in load.scratch],
        compiler_params=pltpu.CompilerParams(
            collective_id=collective_id,
            has_side_effects=collective_id is not None,
            vmem_limit_bytes=VMEM_LIMIT,
        ),
        name=name,
    )(*operands, *[operand for load in loads for operand in load.operands])
    return results[: len(outs)], results[len(outs) :]


def sems(kinds):
    return [pltpu.SemaphoreType.DMA((kinds, CHUNKS)), pltpu.SemaphoreType.DMA((kinds, CHUNKS))]


def norm_of(value, gain):
    scale = lax.rsqrt(jnp.mean(value * value, axis=-1, keepdims=True) + NORM_EPS)
    return value * scale * gain


def norm_back(grad, value, gain):
    scale = lax.rsqrt(jnp.mean(value * value, axis=-1, keepdims=True) + NORM_EPS)
    unit = value * scale
    scaled = grad * gain
    back = scale * (scaled - unit * jnp.mean(scaled * unit, axis=-1, keepdims=True))
    return (back, jnp.sum(grad * unit, axis=0, keepdims=True))


GELU_A = math.sqrt(2.0 / math.pi)
GELU_B = 0.044715


def gelu_of(x):
    return 0.5 * x * (1.0 + jnp.tanh(GELU_A * (x + GELU_B * (x * x * x))))


def gelu_slope(x):
    square = x * x
    t = jnp.tanh(GELU_A * (x + GELU_B * (x * square)))
    return 0.5 * (1.0 + t) + 0.5 * x * (1.0 - t * t) * (GELU_A * (1.0 + 3.0 * GELU_B * square))


def rows_at(start, j, chunk):
    return pl.ds(pl.multiple_of(start + j * chunk, chunk), chunk)


LANES = 128


def spread(row):
    return jnp.transpose(jnp.broadcast_to(row, (LANES, LANES)))


def feature_places(owner, width, share):
    lane = lax.broadcasted_iota(jnp.int32, (LANES, width), 0)
    feature = lax.broadcasted_iota(jnp.int32, (LANES, width), 1)
    return ((feature == lane + owner * share) & (lane < share)).astype(F32).astype(BF16)


def token_picks(ids, vocab, first):
    here = spread(ids.astype(F32) - first.astype(F32))
    lane = lax.broadcasted_iota(jnp.int32, (LANES, LANES), 1).astype(F32)
    return [jnp.where(here == lane + float(t * LANES), 1.0, 0.0).astype(BF16) for t in range(vocab // LANES)]


def embed_kernel(
    ids, counted, gains, extra, table,
    resid, normed, gain_all, count_all, ids_all,
    low, picks, small, near_out, near_in, own, far_out, far_in, wide_out, wide_in, part_out, part_in,
    id_send, id_recv, small_send, small_recv, near_send, near_recv, far_send, far_recv, wide_send, wide_recv,
    part_send, part_recv, send, recv, carry,
):
    seq_len, width = normed.shape
    chunk = seq_len // 2 // CHUNKS
    quarter = seq_len // 4
    share, vocab = table.shape[1:]
    owners = ids_all.shape[0]
    id_rows = ids.shape[0]
    sibling, partner, mine, other = group_places(seq_len)
    place = lax.axis_index(NARROW)
    side = lax.div(place, 2)
    me = lax.axis_index(WIDE)
    first = place * vocab
    around = [lax.rem(me + step, owners) for step in range(owners)]

    def id_copy(step):
        return remote(ids_all.at[me], ids_all.at[me], id_send.at[step], id_recv.at[step], {WIDE: around[step]})

    def small_copy(step):
        return remote(small.at[me], small.at[me], small_send.at[step], small_recv.at[step], {WIDE: around[step]})

    def near_copy(step):
        return remote(near_out.at[step], near_in.at[step], near_send.at[step], near_recv.at[step], sibling)

    def far_copy(step):
        return remote(far_out.at[step], far_in.at[step], far_send.at[step], far_recv.at[step], partner)

    def wide_copy(step):
        return remote(wide_out.at[step], wide_in.at[me], wide_send.at[step], wide_recv.at[step], {WIDE: around[step]})

    def part_copy(piece):
        rows = pl.ds(piece * LANES, LANES)
        return remote(part_out.at[rows], part_in.at[rows], part_send.at[piece], part_recv.at[piece], partner)

    ids_all[me] = ids[...]
    small[me] = jnp.zeros(small.shape[1:], F32)
    small[me, : gains.shape[0], : gains.shape[1]] = gains[...].astype(BF16).astype(F32)
    count = jnp.sum(counted[...].astype(F32), keepdims=True)
    small[me, gains.shape[0] : gains.shape[0] + 1, :] = jnp.broadcast_to(count, (1, small.shape[2]))
    greet([{WIDE: device} for device in around[1:]] + [sibling, partner])
    for step in range(1, owners):
        id_copy(step).start()
    for step in range(1, owners):
        small_copy(step).start()
    carry.start()
    padded = jnp.concatenate([table[0], jnp.zeros((LANES - share, vocab), F32)], axis=0)
    low[...] = jnp.transpose(padded).astype(BF16)

    def look_up(step):
        row = lax.rem(me + step, owners)

        def find(start):
            def block(b, _):
                place_of = start // LANES + b
                for t, pick in enumerate(token_picks(ids_all[row, pl.ds(place_of, 1), :], vocab, first)):
                    picks[rows_at(0, b, LANES), t * LANES : (t + 1) * LANES] = pick
                return 0

            lax.fori_loop(0, seq_len // 2 // LANES, block, 0)
            return dot_nn(picks[...], low[...]).astype(BF16)

        near_out[step] = find(other)
        near_copy(step).start()
        own[step] = find(mine)

    def halve(step):
        near_copy(step).wait_recv()
        total = own[step] + near_in[step]
        own[step] = total
        far_out[step] = own[step, pl.ds(pl.multiple_of((1 - side) * quarter, quarter), quarter), :]
        far_copy(step).start()

    def deliver(step):
        far_copy(step).wait_recv()
        total = own[step, pl.ds(pl.multiple_of(side * quarter, quarter), quarter), :] + far_in[step]
        if step % owners == 0:
            wide_in[me] = total
        else:
            wide_out[step] = total
            wide_copy(step).start()

    order = list(range(1, owners)) + [0]
    for turn in range(owners + 2):
        if turn < owners:
            if order[turn]:
                id_copy(owners - order[turn]).wait_recv()
            look_up(order[turn])
        if 1 <= turn < owners + 1:
            halve(order[turn - 1])
        if turn >= 2:
            deliver(order[turn - 2])
    carry.start(1)
    for step in range(1, owners):
        small_copy(step).wait_recv()
    total = None
    for owner in range(owners):
        part = dot_nn(small[owner].astype(BF16), feature_places(owner, width, share))
        total = part if total is None else total + part
    gain_all[...] = total
    count_all[...] = jnp.sum(small[...], axis=0)
    for step in range(1, owners):
        wide_copy(step).wait_recv()
    pieces = quarter // LANES
    at_side = pl.multiple_of(side * quarter, quarter)
    at_other = pl.multiple_of((1 - side) * quarter, quarter)
    for piece in range(pieces):
        rows = pl.ds(piece * LANES, LANES)
        found = None
        for owner in range(owners):
            part = dot_nn(wide_in[owner, rows, :], feature_places(owner, width, share))
            found = part if found is None else found + part
        part_out[rows, :] = found.astype(BF16)
        part_copy(piece).start()
    carry.relay(FIRST)

    def finish(start, source, piece):
        rows = rows_at(start, piece, LANES)
        x = math.sqrt(width) * source[pl.ds(piece * LANES, LANES), :].astype(F32) + extra[rows, :]
        resid[rows, :] = x
        here = rows_at(mine + start, piece, LANES)
        normed[here, :] = norm_of(x, gain_all[0:1, :]).astype(BF16)
        give_rows(here, piece if source is part_out else pieces + piece).start()

    def give_rows(here, k):
        return remote(normed.at[here], normed.at[here], send.at[0, k], recv.at[0, k], sibling)

    for piece in range(pieces):
        finish(at_side, part_out, piece)
    for piece in range(pieces):
        part_copy(piece).wait_recv()
        finish(at_other, part_in, piece)
    carry.relay(SECOND)
    for k in range(2 * pieces):
        give_rows(rows_at(mine, k % pieces, LANES), k).wait()
    for step in range(owners):
        near_copy(step).wait_send()
        far_copy(step).wait_send()
        if step:
            id_copy(step).wait_send()
            small_copy(step).wait_send()
            wide_copy(step).wait_send()
    for piece in range(pieces):
        part_copy(piece).wait_send()
    carry.finish()


def embed(ids, counted, gains, extra, tables, owners, collective_id, loads):
    seq_len = ids.size
    half, width = extra.shape
    share, vocab = tables.shape[1:]
    dma = pltpu.SemaphoreType.DMA
    return run(
        embed_kernel,
        "embed",
        [ids, counted, gains, extra, tables],
        [
            jax.ShapeDtypeStruct((half, width), F32),
            jax.ShapeDtypeStruct((seq_len, width), BF16),
            jax.ShapeDtypeStruct((8, width), F32),
            jax.ShapeDtypeStruct((8, LANES), F32),
            jax.ShapeDtypeStruct((owners,) + ids.shape, jnp.int32),
        ],
        [
            pltpu.VMEM((vocab, LANES), BF16),
            pltpu.VMEM((half, vocab), BF16),
            pltpu.VMEM((owners, 8, LANES), F32),
            pltpu.VMEM((owners, half, LANES), BF16),
            pltpu.VMEM((owners, half, LANES), BF16),
            pltpu.VMEM((owners, half, LANES), BF16),
            pltpu.VMEM((owners, half // 2, LANES), BF16),
            pltpu.VMEM((owners, half // 2, LANES), BF16),
            pltpu.VMEM((owners, half // 2, LANES), BF16),
            pltpu.VMEM((owners, half // 2, LANES), BF16),
            pltpu.VMEM((half // 2, width), BF16),
            pltpu.VMEM((half // 2, width), BF16),
        ]
        + [dma((owners,))] * 10
        + [dma((half // 2 // LANES,))] * 2
        + [dma((1, half // LANES))] * 2,
        collective_id,
        loads,
    )


TILE = 256


def weight_grad(left_t, right, out):
    columns = right.shape[1]
    tile = TILE if columns % TILE == 0 else columns

    def step(i, _):
        where = pl.ds(pl.multiple_of(i * tile, tile), tile)
        out[:, where] = dot_nn(left_t[...], right[:, where]).astype(out.dtype)
        return 0

    if tile == columns:
        out[...] = dot_nn(left_t[...], right[...]).astype(out.dtype)
    else:
        lax.fori_loop(0, columns // tile, step, 0)


def ffn_back_kernel(
    row, grad, branch, w_red, w_in, w_out, before, after, normed, middle, gain, mixed,
    grad_middle, grad_attn, grad_mixed, d_red, d_in, d_out, d_gain,
    grad_before, turned, near_out, near_in, far_out, far_in, send, recv, carry,
):
    seq_len = normed.shape[0]
    chunk = seq_len // 2 // CHUNKS
    sibling, partner, mine, other = group_places(seq_len)
    greet([sibling, partner] + carry.peers())
    carry.start()
    sems = (send, recv)
    trade = Exchange((near_out, near_in, far_out, far_in), sems, 0, sibling, partner)
    share = Share(grad_attn, sems, 2, sibling, mine, chunk)

    def partial(start, j):
        rows = rows_at(start, j, chunk)
        back = dot_nn(branch[rows, :], w_red[...])
        low = (back * gelu_slope(before[rows, :])).astype(BF16)
        grad_before[rows, :] = low
        return dot_nt(low, w_in[...])

    trade.give(0, partial(other, 0))
    for j in range(CHUNKS):
        if j + 1 < CHUNKS:
            trade.give(j + 1, partial(other, j + 1))
        trade.pass_on(j, partial(mine, j))
    turned[...] = jnp.transpose(branch[...])
    weight_grad(turned, after, d_red)
    turned[...] = jnp.transpose(normed[...])
    weight_grad(turned, grad_before, d_in)
    gain_total = jnp.zeros((1, gain.shape[1]), F32)
    for j in range(CHUNKS):
        rows = rows_at(0, j, chunk)
        back, gain_part = norm_back(trade.take(j), middle[rows, :], gain[row : row + 1, :])
        gain_total = gain_total + gain_part
        total = back + grad[rows, :]
        grad_middle[rows, :] = total
        share.put(j, total.astype(BF16))
        here = rows_at(mine, j, chunk)
        grad_mixed[here, :] = dot_nn(grad_attn[here, :], w_out[...]).astype(BF16)
    for j in range(CHUNKS):
        share.arrived(j)
        here = rows_at(other, j, chunk)
        grad_mixed[here, :] = dot_nn(grad_attn[here, :], w_out[...]).astype(BF16)
    d_gain[...] = gain_total
    turned[...] = jnp.transpose(grad_attn[...])
    weight_grad(turned, mixed, d_out)
    trade.close()
    share.close()
    carry.finish()


def ffn_backward(row, grad, branch, w_red, w_in, w_out, before, after, normed, middle, gain, mixed, collective_id, loads):
    seq_len, width = normed.shape
    half, chunk = seq_len // 2, seq_len // 2 // CHUNKS
    return run(
        functools.partial(ffn_back_kernel, row),
        "ffn_backward",
        [grad, branch, w_red, w_in, w_out, before, after, normed, middle, gain, mixed],
        [
            jax.ShapeDtypeStruct((half, width), F32),
            jax.ShapeDtypeStruct((seq_len, width), BF16),
            jax.ShapeDtypeStruct(mixed.shape, BF16),
            jax.ShapeDtypeStruct(w_red.shape, BF16),
            jax.ShapeDtypeStruct(w_in.shape, BF16),
            jax.ShapeDtypeStruct(w_out.shape, BF16),
            jax.ShapeDtypeStruct((1, gain.shape[1]), F32),
        ],
        [pltpu.VMEM(before.shape, BF16), pltpu.VMEM((width, seq_len), BF16)]
        + Exchange.scratch(chunk, width, BACKWARD_KIND)
        + sems(3),
        collective_id,
        loads,
    )


def norm_back_kernel(
    scale, row, grads, weights, normed, value, gain, upstream,
    grad_out, branch, d_weights, d_gain,
    turned, near_out, near_in, far_out, far_in, send, recv, carry,
):
    seq_len, width = normed.shape
    chunk = seq_len // 2 // CHUNKS
    sibling, partner, mine, other = group_places(seq_len)
    greet([sibling, partner] + carry.peers())
    carry.start()
    sems = (send, recv)
    trade = Exchange((near_out, near_in, far_out, far_in), sems, 0, sibling, partner)
    share = Share(branch, sems, 2, sibling, mine, chunk)

    def partial(start, j):
        rows = rows_at(start, j, chunk)
        total = None
        for which in range(grads.shape[0]):
            part = dot_nt(grads[which, rows, :], weights[which])
            total = part if total is None else total + part
        return total

    trade.give(0, partial(other, 0))
    for j in range(CHUNKS):
        if j + 1 < CHUNKS:
            trade.give(j + 1, partial(other, j + 1))
        trade.pass_on(j, partial(mine, j))
    turned[...] = jnp.transpose(normed[...])
    for which in range(grads.shape[0]):
        weight_grad(turned, grads.at[which], d_weights.at[which])
    gain_total = jnp.zeros((1, gain.shape[1]), F32)
    for j in range(CHUNKS):
        rows = rows_at(0, j, chunk)
        back, gain_part = norm_back(trade.take(j), value[rows, :], gain[row : row + 1, :])
        gain_total = gain_total + gain_part
        back = back + upstream[rows, :]
        grad_out[rows, :] = back
        share.put(j, (back if scale is None else scale * back).astype(BF16))
    d_gain[...] = gain_total
    for j in range(CHUNKS):
        share.arrived(j)
    trade.close()
    share.close()
    carry.finish()


def norm_backward(row, grads, weights, normed, value, gain, upstream, scale, collective_id, loads):
    seq_len, width = normed.shape
    half, chunk = seq_len // 2, seq_len // 2 // CHUNKS
    return run(
        functools.partial(norm_back_kernel, scale, row),
        "norm_backward",
        [grads, weights, normed, value, gain, upstream],
        [
            jax.ShapeDtypeStruct((half, width), F32),
            jax.ShapeDtypeStruct((seq_len, width), BF16),
            jax.ShapeDtypeStruct(weights.shape, BF16),
            jax.ShapeDtypeStruct((1, gain.shape[1]), F32),
        ],
        [pltpu.VMEM((width, seq_len), BF16)] + Exchange.scratch(chunk, width, BACKWARD_KIND) + sems(3),
        collective_id,
        loads,
    )


def head_lanes(value, head, size):
    lanes = lax.broadcasted_iota(jnp.int32, value.shape, 1)
    inside = (lanes >= head * size) & (lanes < (head + 1) * size)
    return jnp.where(inside, value, jnp.zeros_like(value))


QUERY_BLOCK = 256


def forward_kernel(
    layer, normed, w_query, key_seg, query_seg, resid, w_out, w_in, gains,
    projected, mixed, middle, normed_two, before, after, result, normed_next,
    bias, values_t, near_out, near_in, far_out, far_in, near_out2, near_in2, far_out2, far_in2, own2, send, recv,
    carry,
):
    seq_len, width = normed.shape
    chunk = seq_len // 2 // CHUNKS
    block = bias.shape[1]
    heads = mixed.shape[1] // HD
    sibling, partner, mine, other = group_places(seq_len)
    greet([sibling, partner] + carry.peers())
    carry.start()
    pair = (send, recv)
    first = Exchange((near_out, near_in, far_out, far_in), pair, 0, sibling, partner)
    second = Exchange((near_out2, near_in2, far_out2, far_in2), pair, 2, sibling, partner)
    share = Share(normed_two, pair, 4, sibling, mine, chunk)
    share_next = Share(normed_next, pair, 5, sibling, mine, chunk)

    def ask(i, _):
        rows = rows_at(0, i, block)
        for which in range(3):
            projected[which, rows, :] = dot_nn(normed[rows, :], w_query[which]).astype(BF16)
        return 0

    lax.fori_loop(0, seq_len // block, ask, 0)
    values_t[...] = jnp.transpose(projected[2])

    def attend_rows(start):
        rows = pl.ds(pl.multiple_of(start, block), block)
        bias[...] = jnp.where(key_seg[...] == query_seg[:, rows], 0.0, -1e30)
        asked = projected[0, rows, :] * HD ** (-0.5)
        parts = []
        for head in range(heads):
            scores = dot_nt(projected[1], head_lanes(asked, head, HD)) + bias[...]
            powers = jnp.exp(scores - jnp.max(scores, axis=0, keepdims=True))
            probs = (powers * (1.0 / jnp.sum(powers, axis=0, keepdims=True))).astype(BF16)
            parts.append(dot_nn(values_t[head * HD : (head + 1) * HD, :], probs))
        mixed[rows, :] = jnp.transpose(jnp.concatenate(parts, axis=0)).astype(BF16)

    def project(start, j):
        return dot_nt(mixed[rows_at(start, j, chunk), :], w_out[...])

    def feed(rows):
        pre = dot_nn(normed_two[rows, :], w_in[...])
        before[rows, :] = pre
        act = gelu_of(pre).astype(BF16)
        after[rows, :] = act
        return dot_nt(act, w_red())

    per_block = block // chunk
    for part in range(CHUNKS // per_block):

        def both(i, _):
            attend_rows(jnp.where(i == 0, other, mine) + part * block)
            return 0

        lax.fori_loop(0, 2, both, 0)
        for j in range(part * per_block, (part + 1) * per_block):
            first.give(j, project(other, j))
        if part == 0:
            carry.relay(FIRST)
            carry.start(1)
        for j in range(part * per_block, (part + 1) * per_block):
            first.pass_on(j, project(mine, j))
    carry.need()
    reduced = [load.out for load in carry.loads if load.needed][0]

    def w_red():
        return reduced[...].reshape(w_in.shape)

    for j in range(CHUNKS):
        rows = rows_at(0, j, chunk)
        mid = resid[rows, :] + first.take(j)
        middle[rows, :] = mid
        share.put(j, norm_of(mid, gains[2 * layer + 1 : 2 * layer + 2, :]).astype(BF16))
        own2[j] = feed(rows_at(mine, j, chunk))
        share.arrived(j)
        second.give(j, feed(rows_at(other, j, chunk)))
        if j >= 1:
            second.pass_on(j - 1, own2[j - 1])
    second.pass_on(CHUNKS - 1, own2[CHUNKS - 1])
    carry.relay(SECOND)
    for j in range(CHUNKS):
        rows = rows_at(0, j, chunk)
        x = middle[rows, :] + second.take(j)
        result[rows, :] = x
        share_next.put(j, norm_of(x, gains[2 * layer + 2 : 2 * layer + 3, :]).astype(BF16))
        if j == CHUNKS - 2:
            carry.relay(THIRD)
    for j in range(CHUNKS):
        share_next.arrived(j)
    for part in (first, second, share, share_next):
        part.close()
    carry.finish()


def forward_block(layer, normed, w_query, key_seg, query_seg, resid, w_out, w_in, gains, collective_id, loads):
    seq_len, width = normed.shape
    hidden, heads_width = w_in.shape[1], w_query.shape[2]
    half, chunk = seq_len // 2, seq_len // 2 // CHUNKS
    block = max(chunk, min(QUERY_BLOCK, half))
    return run(
        functools.partial(forward_kernel, layer),
        "forward_block",
        [normed, w_query, key_seg, query_seg, resid, w_out, w_in, gains],
        [
            jax.ShapeDtypeStruct((3, seq_len, heads_width), BF16),
            jax.ShapeDtypeStruct((seq_len, heads_width), BF16),
            jax.ShapeDtypeStruct((half, width), F32),
            jax.ShapeDtypeStruct((seq_len, width), BF16),
            jax.ShapeDtypeStruct((seq_len, hidden), F32),
            jax.ShapeDtypeStruct((seq_len, hidden), BF16),
            jax.ShapeDtypeStruct((half, width), F32),
            jax.ShapeDtypeStruct((seq_len, width), BF16),
        ],
        [pltpu.VMEM((seq_len, block), F32), pltpu.VMEM((heads_width, seq_len), BF16)]
        + Exchange.scratch(chunk, width, FORWARD_KIND)
        + Exchange.scratch(chunk, width, FORWARD_KIND)
        + [pltpu.VMEM((CHUNKS, chunk, width), F32)]
        + sems(6),
        collective_id,
        loads,
    )


def attention_back_kernel(projected, grad_mixed, key_seg, query_seg, out, bias, keys_t, grad_keys, grad_values, carry):
    seq_len, width = grad_mixed.shape
    block = bias.shape[1]
    heads = width // HD
    scale = HD ** (-0.5)
    if carry.loads:
        greet(carry.peers())
    carry.start()
    keys_t[...] = jnp.transpose(projected[1])
    grad_keys[...] = jnp.zeros(grad_keys.shape, F32)
    grad_values[...] = jnp.zeros(grad_values.shape, F32)

    def queries(i, _):
        rows = rows_at(0, i, block)
        bias[...] = jnp.where(key_seg[...] == query_seg[:, rows], 0.0, -1e30)
        asked = projected[0, rows, :] * scale
        given = grad_mixed[rows, :]
        parts = []
        for head in range(heads):
            query = head_lanes(asked, head, HD)
            grad = head_lanes(given, head, HD)
            scores = dot_nt(projected[1], query) + bias[...]
            powers = jnp.exp(scores - jnp.max(scores, axis=0, keepdims=True))
            probs = powers * (1.0 / jnp.sum(powers, axis=0, keepdims=True))
            grad_probs = dot_nt(projected[2], grad)
            centre = jnp.sum(probs * grad_probs, axis=0, keepdims=True)
            grad_scores = (probs * (grad_probs - centre)).astype(BF16)
            parts.append(dot_nn(keys_t[head * HD : (head + 1) * HD, :], grad_scores))
            grad_keys[...] += dot_nn(grad_scores, query)
            grad_values[...] += dot_nn(probs.astype(BF16), grad)
        out[0, rows, :] = (jnp.transpose(jnp.concatenate(parts, axis=0)) * scale).astype(BF16)
        return 0

    lax.fori_loop(0, seq_len // block, queries, 0)
    out[1] = grad_keys[...].astype(BF16)
    out[2] = grad_values[...].astype(BF16)
    carry.finish()


def attention_back(projected, grad_mixed, key_seg, query_seg, collective_id, loads):
    seq_len, width = grad_mixed.shape
    block = min(QUERY_BLOCK, seq_len)
    return run(
        attention_back_kernel,
        "attention_back",
        [projected, grad_mixed, key_seg, query_seg],
        [jax.ShapeDtypeStruct(projected.shape, BF16)],
        [
            pltpu.VMEM((seq_len, block), F32),
            pltpu.VMEM((width, seq_len), BF16),
            pltpu.VMEM((seq_len, width), F32),
            pltpu.VMEM((seq_len, width), F32),
        ],
        collective_id if loads else None,
        loads,
    )


def to_rows(columns):
    lanes = lax.broadcasted_iota(jnp.int32, (LANES, LANES), 1)
    total = jnp.zeros((LANES, LANES), F32)
    for k, column in enumerate(columns):
        total = jnp.where(lanes == k, column, total)
    return jnp.transpose(total)[:8, :]


def loss_kernel(
    pieces, row, normed, info, value, gain, *refs, carry,
):
    tables, refs = refs[:pieces], refs[pieces:]
    (grad_out, branch, d_gain, losses), refs = refs[:4], refs[4:]
    d_tables, refs = refs[:pieces], refs[pieces:]
    loss_body(row, normed, info, value, gain, tables, grad_out, branch, d_gain, losses, d_tables, *refs, carry)


def loss_body(
    row, normed, info, value, gain, tables, grad_out, branch, d_gain, losses, d_tables,
    logits, grads, places, turned, stat_out, stat_in, sum_out, sum_in,
    near_out, near_in, far_out, far_in, send, recv, stat_send, stat_recv, sum_send, sum_recv, carry,
):
    seq_len, width = normed.shape
    chunk = seq_len // 2 // CHUNKS
    piece_width = tables[0].shape[1]
    vocab = piece_width * len(tables)
    tiles = vocab // LANES
    blocks = seq_len // LANES
    me = lax.axis_index(NARROW)
    sibling, partner, mine, other = group_places(seq_len)
    peers = [{NARROW: lax.rem(me + k, 4)} for k in range(1, 4)]
    greet(peers + carry.peers())
    carry.start()
    sems = (send, recv)
    trade = Exchange((near_out, near_in, far_out, far_in), sems, 0, sibling, partner)
    share = Share(branch, sems, 2, sibling, mine, chunk)
    first = (me * vocab).astype(F32)
    whole = 4.0 * vocab
    lanes = lax.broadcasted_iota(jnp.int32, (LANES, LANES), 1).astype(F32)

    def stat_copy(b, k):
        return remote(stat_out.at[b], stat_in.at[k, b], stat_send.at[k, b], stat_recv.at[k, b], peers[k])

    def sum_copy(b, k):
        return remote(sum_out.at[b], sum_in.at[k, b], sum_send.at[k, b], sum_recv.at[k, b], peers[k])

    def tile_at(t):
        return pl.ds(pl.multiple_of(t * LANES, LANES), LANES)

    def ask(b):
        rows = rows_at(0, b, LANES)
        here = info[:, rows]
        at_noised = spread(here[0:1] - first)
        at_clean = spread(here[1:2] - first)
        places[b, 0] = at_noised
        places[b, 1] = at_clean

        def top_step(t, top):
            return jnp.maximum(top, logits[rows, tile_at(t)])

        top = lax.fori_loop(1, tiles, top_step, logits[rows, tile_at(0)], unroll=4)
        top = jnp.max(top, axis=1, keepdims=True)
        top_wide = jnp.broadcast_to(top, (LANES, LANES))

        def sum_step(t, totals):
            powers, noised, clean = totals
            piece = logits[rows, tile_at(t)]
            column = lanes + (t * LANES).astype(F32)
            return (
                powers + jnp.exp(piece - top_wide),
                noised + jnp.where(column == at_noised, piece, 0.0),
                clean + jnp.where(column == at_clean, piece, 0.0),
            )

        zero = jnp.zeros((LANES, LANES), F32)
        totals = lax.fori_loop(0, tiles, sum_step, (zero, zero, zero), unroll=2)
        stat_out[b] = to_rows([top] + [jnp.sum(total, axis=1, keepdims=True) for total in totals])
        for k in range(3):
            stat_copy(b, k).start()

    def product(i, _):
        rows = rows_at(0, i, TILE)
        for k, table in enumerate(tables):
            logits[rows, k * piece_width : (k + 1) * piece_width] = dot_nn(normed[rows, :], table[...])
        for b in range(TILE // LANES):
            ask(i * (TILE // LANES) + b)
        return 0

    lax.fori_loop(0, seq_len // TILE, product, 0)

    def scalars(b):
        here = info[:, rows_at(0, b, LANES)]
        step = jnp.maximum(here[2:3], 2.0)
        left = STEPS - step + 1.0
        beta = 1.0 / left
        keep = left / STEPS
        rest = (step - 1.0) / (STEPS * whole)
        own = stat_out[b]
        others = [stat_in[k, b] for k in range(3)]
        top = own[0:1]
        for stat in others:
            top = jnp.maximum(top, stat[0:1])
        total = own[1:2] * jnp.exp(own[0:1] - top)
        noised, clean = own[2:3], own[3:4]
        for stat in others:
            total = total + stat[1:2] * jnp.exp(stat[0:1] - top)
            noised, clean = noised + stat[2:3], clean + stat[3:4]
        return here, beta, keep, rest, top + jnp.log(total), noised, clean

    def measure(b, _):
        rows = rows_at(0, b, LANES)
        for k in range(3):
            stat_copy(b, k).wait_recv()
        _, _, keep, rest, log_total, _, _ = scalars(b)
        log_wide = spread(log_total)
        ratio = spread(keep / rest)

        def step(t, totals):
            logs, shares = totals
            probs = jnp.exp(logits[rows, tile_at(t)] - log_wide)
            logits[rows, tile_at(t)] = probs
            grown = 1.0 + probs * ratio
            return (logs + jnp.log(grown), shares + probs / grown)

        zero = jnp.zeros((LANES, LANES), F32)
        totals = lax.fori_loop(0, tiles, step, (zero, zero), unroll=2)
        sum_out[b] = to_rows([jnp.sum(total, axis=1, keepdims=True) for total in totals])
        for k in range(3):
            sum_copy(b, k).start()
        return 0

    lax.fori_loop(0, blocks, measure, 0)

    def pull(b):
        rows = rows_at(0, b, LANES)
        for k in range(3):
            sum_copy(b, k).wait_recv()
        here, beta, keep, rest, log_total, noised, clean = scalars(b)
        sums = sum_out[b] + sum_in[0, b] + sum_in[1, b] + sum_in[2, b]
        log_sum, share_sum = sums[0:1], sums[1:2] / rest
        same = here[0:1] == here[1:2]
        first_step = here[2:3] == 1.0
        base_a, more_a = beta / whole, 1.0 - beta
        base_w = base_a * rest
        joint = whole * base_w + more_a * rest + base_a * keep + jnp.where(same, more_a * keep, 0.0)
        ratio = keep / rest
        prob_n, prob_c = jnp.exp(noised - log_total), jnp.exp(clean - log_total)
        grown_n, grown_c = 1.0 + prob_n * ratio, 1.0 + prob_c * ratio
        marginal_n, marginal_c = rest * grown_n, rest * grown_c
        log_n, log_c = jnp.log(grown_n), jnp.log(grown_c)
        weight_n = jnp.where(same, 0.0, more_a * rest)
        weight_c = jnp.where(same, more_a * rest + base_a * keep + more_a * keep, base_a * keep)
        lift = jnp.log((keep + rest) / rest)
        cross = -base_w * log_sum - weight_n * log_n - weight_c * log_c + (base_w + weight_c) * lift
        model = base_a * (keep + whole * rest) + more_a * marginal_n
        divergence = cross / joint - jnp.log(joint) + jnp.log(model)
        loss = jnp.where(first_step, log_total - clean, divergence)
        losses[:, rows] = here[4:5] * loss
        weighted = base_w * share_sum + weight_n * prob_n / marginal_n + weight_c * prob_c / marginal_c
        aligned = base_a + more_a * prob_n
        centre = keep * (aligned / model - weighted / joint)
        scale = here[3:4]
        zero = jnp.zeros_like(scale)
        even = scale * jnp.where(first_step, 1.0, keep * base_a / model - centre)
        bent = scale * jnp.where(first_step, zero, -keep * base_w / joint / rest)
        at_n = prob_n * keep * (more_a / model - weight_n / joint / marginal_n)
        at_c = -prob_c * keep * (weight_c / joint / marginal_c)
        extra_n = spread(scale * jnp.where(first_step, zero, at_n))
        extra_c = spread(scale * jnp.where(first_step, -1.0, at_c))
        even, bent, ratio = spread(even), spread(bent), spread(ratio)
        at_noised, at_clean = places[b, 0], places[b, 1]

        def step(t, _):
            probs = logits[rows, tile_at(t)]
            column = lanes + (t * LANES).astype(F32)
            grad = probs * (even + bent / (1.0 + probs * ratio))
            grad = grad + jnp.where(column == at_noised, extra_n, 0.0)
            grad = grad + jnp.where(column == at_clean, extra_c, 0.0)
            grads[rows, tile_at(t)] = grad.astype(BF16)
            return 0

        lax.fori_loop(0, tiles, step, 0, unroll=2)

    def partial(start, j):
        base = start // LANES + j * (chunk // LANES)
        for b in range(chunk // LANES):
            pull(base + b)
        total = None
        for k, table in enumerate(tables):
            part = dot_nt(grads[rows_at(start, j, chunk), k * piece_width : (k + 1) * piece_width], table[...])
            total = part if total is None else total + part
        return total

    trade.give(0, partial(other, 0))
    for j in range(CHUNKS):
        if j + 1 < CHUNKS:
            trade.give(j + 1, partial(other, j + 1))
        trade.pass_on(j, partial(mine, j))
    turned[...] = jnp.transpose(normed[...])
    for k, d_table in enumerate(d_tables):
        weight_grad(turned, grads.at[:, k * piece_width : (k + 1) * piece_width], d_table)
    gain_total = jnp.zeros((1, gain.shape[1]), F32)
    for j in range(CHUNKS):
        rows = rows_at(0, j, chunk)
        back, gain_part = norm_back(trade.take(j), value[rows, :], gain[row : row + 1, :])
        gain_total = gain_total + gain_part
        grad_out[rows, :] = back
        share.put(j, back.astype(BF16))
    d_gain[...] = gain_total
    for j in range(CHUNKS):
        share.arrived(j)
    trade.close()
    share.close()

    def finish(b, _):
        for k in range(3):
            stat_copy(b, k).wait_send()
            sum_copy(b, k).wait_send()
        return 0

    lax.fori_loop(0, blocks, finish, 0)
    carry.finish()


def loss_and_back(row, normed, tables, info, value, gain, collective_id, loads):
    seq_len, width = normed.shape
    vocab = sum(table.shape[1] for table in tables)
    half, chunk, blocks = seq_len // 2, seq_len // 2 // CHUNKS, seq_len // LANES
    return run(
        functools.partial(loss_kernel, len(tables), row),
        "loss_and_back",
        [normed, info, value, gain, *tables],
        [
            jax.ShapeDtypeStruct((half, width), F32),
            jax.ShapeDtypeStruct((seq_len, width), BF16),
            jax.ShapeDtypeStruct((1, width), F32),
            jax.ShapeDtypeStruct((1, seq_len), F32),
        ]
        + [jax.ShapeDtypeStruct(table.shape, BF16) for table in tables],
        [
            pltpu.VMEM((seq_len, vocab), F32),
            pltpu.VMEM((seq_len, vocab), BF16),
            pltpu.VMEM((blocks, 2, LANES, LANES), F32),
            pltpu.VMEM((width, seq_len), BF16),
            pltpu.VMEM((blocks, 8, LANES), F32),
            pltpu.VMEM((3, blocks, 8, LANES), F32),
            pltpu.VMEM((blocks, 8, LANES), F32),
            pltpu.VMEM((3, blocks, 8, LANES), F32),
        ]
        + Exchange.scratch(chunk, width, BACKWARD_KIND)
        + sems(3)
        + [pltpu.SemaphoreType.DMA((3, blocks))] * 4,
        collective_id,
        loads,
    )


def sum_ways(place, me, slow, fast, slows, group):
    near = [{NARROW: lax.rem(place + step, group)} for step in range(1, group)]
    return near, {WIDE: me + 1 - 2 * fast}


def tail_kernel(
    layers, branch, ids_all, losses, full, *refs, carry,
):
    gain_parts, refs = refs[: 2 * layers + 1], refs[2 * layers + 1 :]
    squares, refs = refs[: len(refs) - 32], refs[len(refs) - 32 :]
    tail_body(branch, ids_all, losses, full, gain_parts, squares, *refs, carry)


def tail_body(
    branch, ids_all, losses, full, gain_parts, squares,
    d_table, d_full, d_small, scalars,
    out_blocks, all_in, masked, picks, total, gains_out, gains_in, blocks, block_in, line_out, line_in,
    fast_in, sums, slow_in, near, along, across,
    wide_send, wide_recv, far_send, far_recv, near_send, near_recv,
    pair_send, pair_recv, line_send, line_recv, sum_sems,
    carry,
):
    seq_len, width = branch.shape
    quarter, half = seq_len // 4, seq_len // 2
    owners = ids_all.shape[0]
    share, vocab = d_table.shape
    sibling, partner, mine, other = group_places(seq_len)
    place = lax.axis_index(NARROW)
    side = lax.div(place, 2)
    me, slow, fast, slows = wide_places(owners)
    beside = {WIDE: me + 1 - 2 * fast}
    group = near.shape[0]
    first = place * vocab
    around = [lax.rem(me + step, owners) for step in range(owners)]
    at_quarter = pl.multiple_of(mine + side * quarter, quarter)
    across_quarter = pl.multiple_of(mine + (1 - side) * quarter, quarter)

    def along_way(step):
        return {WIDE: 2 * lax.rem(slow + step, slows) + fast}

    def wide_copy(step):
        return remote(
            out_blocks.at[around[step]], all_in.at[me, pl.ds(at_quarter, quarter)],
            wide_send.at[step], wide_recv.at[step], {WIDE: around[step]},
        )

    def far_copy(step):
        rows = all_in.at[around[step], pl.ds(at_quarter, quarter)]
        return remote(rows, rows, far_send.at[step], far_recv.at[step], partner)

    def near_copy(step):
        rows = all_in.at[around[step], pl.ds(mine, half)]
        return remote(rows, rows, near_send.at[step], near_recv.at[step], sibling)

    def block(owner):
        return full.at[:, owner]

    def pair_copy(step):
        return remote(
            block(2 * lax.rem(slow + step, slows) + 1 - fast), fast_in.at[step],
            pair_send.at[step], pair_recv.at[step], beside,
        )

    def line_copy(step):
        return remote(sums.at[step], slow_in.at[step], line_send.at[step], line_recv.at[step], along_way(step))

    def gain_near():
        return remote(gains_out, gains_in, sum_sems.at[0, 0], sum_sems.at[1, 0], sibling)

    def gain_pair(step):
        return remote(
            blocks.at[2 * lax.rem(slow + step, slows) + 1 - fast], block_in.at[step],
            sum_sems.at[2, step], sum_sems.at[3, step], beside,
        )

    def gain_line(step):
        return remote(line_out.at[step], line_in.at[step], sum_sems.at[4, step], sum_sems.at[5, step], along_way(step))

    near_ways = [{NARROW: lax.rem(place + step, group)} for step in range(1, group)]
    greet([{WIDE: device} for device in around[1:]] + near_ways)
    for step in range(slows):
        pair_copy(step).start()
    gains_out[...] = jnp.zeros(gains_out.shape, F32)
    for row, part in enumerate(gain_parts):
        gains_out[row : row + 1, :] = part[...]
    gain_near().start()
    for owner in range(owners):
        out_blocks[owner] = dot_nt(
            branch[pl.ds(at_quarter, quarter), :], feature_places(owner, width, share)
        ).astype(BF16)
    for step in range(1, owners):
        wide_copy(step).start()
    all_in[me, pl.ds(at_quarter, quarter), :] = out_blocks[me]
    carry.start()
    gain_near().wait_recv()
    both = gains_out[...] + gains_in[...]
    for owner in range(owners):
        blocks[owner] = lax.dot_general(
            both, feature_places(owner, width, share).astype(F32), (((1,), (1,)), ((), ())),
            precision=lax.Precision.HIGHEST, preferred_element_type=F32,
        )
    for step in range(slows):
        gain_pair(step).start()

    def hand_on(step):
        if step:
            wide_copy(owners - step).wait_recv()
        far_copy(step).start()

    def hand_over(step):
        far_copy(step).wait_recv()
        near_copy(step).start()

    def gather_grad(step, first_turn):
        near_copy(step).wait_recv()
        row = around[step]

        def make(b, _):
            rows = rows_at(0, b, LANES)
            here = ids_all[row, pl.ds(b, 1), :] - first
            high = lax.shift_right_arithmetic(here, 7)
            rest = spread((here - high * LANES).astype(F32))
            lane = lax.broadcasted_iota(jnp.int32, (LANES, LANES), 1).astype(F32)
            picks[rows, :] = jnp.where(rest == lane, 1.0, 0.0).astype(BF16)
            turned = jnp.transpose(all_in[row, rows, :])
            for t in range(vocab // LANES):
                inside = jnp.where(high == t, 1.0, 0.0).astype(BF16)
                masked[t * LANES : (t + 1) * LANES, rows] = turned * inside
            return 0

        lax.fori_loop(0, seq_len // LANES, make, 0)
        span = 2 * TILE

        def some(i, _):
            rows = rows_at(0, i, span)
            part = dot_nn(masked[rows, :], picks[...])
            total[rows, :] = part if first_turn else total[rows, :] + part
            return 0

        lax.fori_loop(0, vocab // span, some, 0)

    order = [0] + list(range(1, owners))
    for turn in range(owners + 2):
        if turn < owners:
            hand_on(order[turn])
        if 1 <= turn < owners + 1:
            hand_over(order[turn - 1])
        if turn == 1:
            for step in list(range(1, slows)) + [0]:
                pair_copy(step).wait_recv()
                owner = 2 * lax.rem(slow + step, slows) + fast
                sums[step] = (block(owner)[...].astype(F32) + fast_in[step].astype(F32)).astype(BF16)
                if step:
                    line_copy(step).start()
            for step in list(range(1, slows)) + [0]:
                gain_pair(step).wait_recv()
                line_out[step] = blocks[2 * lax.rem(slow + step, slows) + fast] + block_in[step]
                if step:
                    gain_line(step).start()
        if turn >= 2:
            gather_grad(order[turn - 2], turn == 2)
    for t in range(vocab // LANES):
        d_table[:, t * LANES : (t + 1) * LANES] = total[t * LANES : t * LANES + share, :]
    result = sums[0].astype(F32)
    small = line_out[0]
    for step in range(1, slows):
        line_copy(step).wait_recv()
        result = result + slow_in[step].astype(F32)
        gain_line(step).wait_recv()
        small = small + line_in[step]
    d_full[...] = result
    d_small[...] = small
    carry.finish()
    square = jnp.sum(result * result) + jnp.sum(d_table[...] * d_table[...])
    for part in squares:
        square = square + part[0, 0]
    for load in carry.loads:
        square = square + load.squares[0, 0]
    lead = (place == 0).astype(F32)
    square = square + lead * jnp.sum(small * small)
    lanes = lax.broadcasted_iota(jnp.int32, (8, LANES), 1)
    given = jnp.where(lanes == 0, square, jnp.where(lanes == 1, lead * jnp.sum(losses[...]), 0.0))

    def scalar_near(step):
        return remote(near.at[place], near.at[place], sum_sems.at[6, step], sum_sems.at[7, step], near_ways[step - 1])

    def scalar_line(step):
        return remote(along.at[slow], along.at[slow], sum_sems.at[8, step], sum_sems.at[9, step], along_way(step))

    near[place] = given
    for step in range(1, group):
        scalar_near(step).start()
    for step in range(1, group):
        scalar_near(step).wait()
    along[slow] = jnp.sum(near[...], axis=0)
    for step in range(1, slows):
        scalar_line(step).start()
    for step in range(1, slows):
        scalar_line(step).wait()
    across[0] = jnp.sum(along[...], axis=0)
    last = remote(across.at[0], across.at[1], sum_sems.at[10, 0], sum_sems.at[11, 0], beside)
    last.start()
    last.wait()
    scalars[...] = across[0] + across[1]
    gain_near().wait_send()
    for step in range(owners):
        far_copy(step).wait_send()
        near_copy(step).wait_send()
        if step:
            wide_copy(step).wait_send()
    for step in range(slows):
        pair_copy(step).wait_send()
        gain_pair(step).wait_send()
        if step:
            line_copy(step).wait_send()
            gain_line(step).wait_send()


def tail(branch, ids_all, losses, full, gain_parts, squares, share, vocab, group, collective_id, loads):
    seq_len, width = branch.shape
    owners = ids_all.shape[0]
    slows = owners // 2
    shape = full.shape[:1] + full.shape[2:]
    dma = pltpu.SemaphoreType.DMA
    small = (8, LANES)
    return run(
        functools.partial(tail_kernel, (len(gain_parts) - 1) // 2),
        "tail",
        [branch, ids_all, losses, full, *gain_parts, *squares],
        [
            jax.ShapeDtypeStruct((share, vocab), F32),
            jax.ShapeDtypeStruct(shape, F32),
            jax.ShapeDtypeStruct(small, F32),
            jax.ShapeDtypeStruct(small, F32),
        ],
        [
            pltpu.VMEM((owners, seq_len // 4, LANES), BF16),
            pltpu.VMEM((owners, seq_len, LANES), BF16),
            pltpu.VMEM((vocab, seq_len), BF16),
            pltpu.VMEM((seq_len, LANES), BF16),
            pltpu.VMEM((vocab, LANES), F32),
            pltpu.VMEM((8, width), F32),
            pltpu.VMEM((8, width), F32),
            pltpu.VMEM((owners,) + small, F32),
            pltpu.VMEM((slows,) + small, F32),
            pltpu.VMEM((slows,) + small, F32),
            pltpu.VMEM((slows,) + small, F32),
            pltpu.VMEM((slows,) + shape, BF16),
            pltpu.VMEM((slows,) + shape, BF16),
            pltpu.VMEM((slows,) + shape, BF16),
            pltpu.VMEM((group,) + small, F32),
            pltpu.VMEM((slows,) + small, F32),
            pltpu.VMEM((2,) + small, F32),
        ]
        + [dma((owners,))] * 6
        + [dma((slows,))] * 4
        + [dma((12, max(slows, group)))],
        collective_id,
        loads,
    )


PIECES = 4
TABLE, ATTN_IN, ATTN_OUT, FFN_IN, FFN_OUT = range(5)


def shares_tile(wide, narrow, noised, attn_out, ffn_in, tables):
    rows, seq_len = noised.shape
    return (
        narrow == 4
        and wide % 2 == 0
        and rows == 1
        and seq_len % (2 * CHUNKS * 128) == 0
        and attn_out.shape[1] % 16 == 0
        and attn_out.shape[1] <= LANES
        and ffn_in.shape[2] % 128 == 0
        and tables.shape[1] == attn_out.shape[1]
        and tables.shape[2] % (PIECES * TILE) == 0
    )


def per_device(wide, narrow, *arrays):
    noised, attn_out, ffn_in, tables = arrays[0], arrays[6], arrays[7], arrays[9]
    if shares_tile(wide, narrow, noised, attn_out, ffn_in, tables):
        return tiled_device(wide, *arrays)
    return general_device(*arrays)


def tiled_device(
    wide,
    noised,
    clean,
    timesteps,
    segments,
    counted,
    attn_in,
    attn_out,
    ffn_in,
    ffn_out,
    tables,
    gains,
    attn_in_mean,
    attn_out_mean,
    ffn_in_mean,
    ffn_out_mean,
    tables_mean,
    gains_mean,
    attn_in_square,
    attn_out_square,
    ffn_in_square,
    ffn_out_square,
    tables_square,
    gains_square,
):
    layers = attn_in.shape[0]
    gain_rows, gain_cols = gains.shape
    mask = counted.reshape(-1).astype(jnp.float32)
    seq_len = mask.shape[0]
    half = seq_len // 2
    core = lax.rem(lax.axis_index(NARROW), 2)
    share, vocab = tables.shape[1:]
    leads = (1, 0, 0, 0)
    four = (attn_in, attn_out, ffn_in, ffn_out)

    def joined(value, lead):
        return value.reshape(value.shape[:lead] + (-1,) + value.shape[lead + 2 :])

    step_flat = timesteps.reshape(-1)
    extra = time_features(lax.dynamic_slice(step_flat, (core * half,), (half,)))
    ids = noised.reshape(-1, LANES)
    quarter = vocab // PIECES
    windows = [(k * quarter, quarter) for k in range(PIECES)]
    (residual, normed, gain_w, counts, ids_all), carried = embed(
        ids, counted, gains, extra, tables, wide, 0,
        [
            GatherLoad(attn_in, 0, 1, wide, FIRST),
            GatherLoad(attn_out, 0, 0, wide, FIRST),
            GatherLoad(ffn_in, 0, 0, wide, LAST, late=1),
        ],
    )
    token_total = counts[gain_rows, 0]
    next_id = 1
    key_seg, query_seg = segments.reshape(-1, 1), segments.reshape(1, -1)
    kept = []
    for layer in range(layers):
        query_w, output_w, expand_w = [joined(value, lead) for value, lead in zip(carried, leads)]
        loads = [GatherLoad(ffn_out, layer, 0, wide, FIRST, needed=True)]
        if layer + 1 < layers:
            loads += [
                GatherLoad(attn_in, layer + 1, 1, wide, SECOND, late=1),
                GatherLoad(attn_out, layer + 1, 0, wide, SECOND, late=1),
                GatherLoad(ffn_in, layer + 1, 0, wide, THIRD, late=1),
            ]
        else:
            loads += [
                GatherLoad(tables, 1, 0, wide, stage, window, late)
                for window, stage, late in zip(windows, (SECOND, SECOND, THIRD, LAST), (0, 1, 1, 1))
            ]
        (projected, mixed, middle, normed_two, before, after, result, normed_next), carried = forward_block(
            layer, normed, query_w, key_seg, query_seg, residual, output_w, expand_w, gain_w, next_id, loads
        )
        next_id += 1
        reduce_w, *carried = carried
        kept.append(
            (residual, normed, projected, mixed, middle, normed_two, before, after)
            + (query_w, output_w, expand_w, joined(reduce_w, 0))
        )
        residual, normed = result, normed_next
    tables_w = [joined(value, 0) for value in carried]

    noised_flat, clean_flat = noised.reshape(-1), clean.reshape(-1)
    info = jnp.stack(
        [noised_flat.astype(F32), clean_flat.astype(F32), step_flat.astype(F32), mask / token_total, mask]
        + [jnp.zeros_like(mask)] * 3
    )
    (grad, branch, gain_final, losses, *d_last), _ = loss_and_back(
        2 * layers, normed, tables_w, info, residual, gain_w, next_id, []
    )
    next_id += 1
    gain_grads = [None] * (2 * layers) + [gain_final]
    own, squares = {}, []

    def by_owner(value, lead):
        shape = value.shape
        return value.reshape(shape[:lead] + (wide, shape[lead] // wide) + shape[lead + 1 :])

    class Route:
        waiting, halfway = [], []

        def take(self, pairs, lines):
            self.now = self.waiting[:pairs], self.halfway[:lines]
            self.waiting, self.halfway = self.waiting[pairs:], self.halfway[lines:]
            return [PairLoad(by_owner(value, lead), lead, wide) for _, value, lead in self.now[0]] + [
                LineLoad(sums, wide) for _, sums in self.now[1]
            ]

        def back(self, results):
            pairs, lines = self.now
            self.halfway = self.halfway + [(key, sums) for (key, _, _), sums in zip(pairs, results)]
            for k, (key, _) in enumerate(lines):
                own[key] = results[len(pairs) + 2 * k]
                squares.append(results[len(pairs) + 2 * k + 1])

    route = Route()
    route.waiting = [((TABLE, k), piece, 0) for k, piece in enumerate(d_last)]
    for layer in reversed(range(layers)):
        residual, normed, projected, mixed, middle, normed_two, before, after, *four_w = kept[layer]
        query_w, output_w, expand_w, reduce_w = four_w
        top = layer == layers - 1
        loads = route.take(3 if top else 2, 3)
        (grad_middle, grad_attn, grad_mixed, d_red, d_in, d_out, gain_two), carried = ffn_backward(
            2 * layer + 1, grad, branch, reduce_w, expand_w, output_w, before, after,
            normed_two, middle, gain_w, mixed, next_id, loads,
        )
        route.back(carried)
        route.waiting += [((FFN_OUT, layer), d_red, 0), ((FFN_IN, layer), d_in, 0)]
        loads = route.take(1, 2)
        (grad_projected,), carried = attention_back(projected, grad_mixed, key_seg, query_seg, next_id + 1, loads)
        route.back(carried)
        route.waiting += [((ATTN_OUT, layer), d_out, 0)]
        loads = route.take(2, 2)
        (grad, branch, d_query, gain_one), carried = norm_backward(
            2 * layer, grad_projected, query_w, normed, residual, gain_w, grad_middle,
            math.sqrt(D) if layer == 0 else None, next_id + 2, loads,
        )
        route.back(carried)
        route.waiting += [((ATTN_IN, layer), d_query, 1)]
        next_id += 3
        gain_grads[2 * layer], gain_grads[2 * layer + 1] = gain_one, gain_two
    (key, last_full, _), = route.waiting
    lines = route.halfway
    (own_first, own[key], total_small, scalars), carried = tail(
        branch, ids_all, losses, by_owner(last_full, 1), gain_grads, squares, share, vocab, 4, next_id,
        [LineLoad(value, wide) for _, value in lines],
    )
    for k, (key, _) in enumerate(lines):
        own[key] = carried[2 * k]
    grad_attn_in, grad_attn_out, grad_ffn_in, grad_ffn_out = [
        jnp.stack([own[name, index] for index in range(layers)]) for name in (ATTN_IN, ATTN_OUT, FFN_IN, FFN_OUT)
    ]
    grad_tables = jnp.stack([own_first, jnp.concatenate([own[TABLE, k] for k in range(PIECES)], axis=1)])
    grad_gains = total_small[:gain_rows, :gain_cols]
    total_square, loss_sum = scalars[0, 0], scalars[0, 1]
    grad_norm = jnp.sqrt(total_square)
    factor = jnp.minimum(1.0, CLIP_NORM / (grad_norm + 1e-06))
    results = [loss_sum, token_total, grad_norm]
    for weight, gradient, first, second, decay, rate in (
        (attn_in, grad_attn_in, attn_in_mean, attn_in_square, WEIGHT_DECAY, LEARN_RATE),
        (attn_out, grad_attn_out, attn_out_mean, attn_out_square, WEIGHT_DECAY, LEARN_RATE),
        (ffn_in, grad_ffn_in, ffn_in_mean, ffn_in_square, WEIGHT_DECAY, LEARN_RATE),
        (ffn_out, grad_ffn_out, ffn_out_mean, ffn_out_square, WEIGHT_DECAY, LEARN_RATE),
        (tables, grad_tables, tables_mean, tables_square, WEIGHT_DECAY, LEARN_RATE),
        (gains, grad_gains, gains_mean, gains_square, 0.0, GAIN_RATE),
    ):
        results += adam(weight, factor * gradient, first, second, decay, rate)
    return tuple(results)


def solution(mesh):
    wide, narrow = mesh.shape[WIDE], mesh.shape[NARROW]
    placed = (
        P(WIDE, None),
        P(WIDE, None),
        P(WIDE, None),
        P(WIDE, None),
        P(WIDE, None),
        P(None, None, WIDE, NARROW),
        P(None, WIDE, NARROW),
        P(None, WIDE, NARROW),
        P(None, WIDE, NARROW),
        P(None, WIDE, NARROW),
        P(None, WIDE),
        P(None, None, WIDE, NARROW),
        P(None, WIDE, NARROW),
        P(None, WIDE, NARROW),
        P(None, WIDE, NARROW),
        P(None, WIDE, NARROW),
        P(None, WIDE),
        P(None, None, WIDE, NARROW),
        P(None, WIDE, NARROW),
        P(None, WIDE, NARROW),
        P(None, WIDE, NARROW),
        P(None, WIDE, NARROW),
        P(None, WIDE),
    )
    return jax.shard_map(
        functools.partial(per_device, wide, narrow),
        mesh=mesh,
        in_specs=placed,
        out_specs=(
            P(),
            P(),
            P(),
            P(None, None, WIDE, NARROW),
            P(None, None, WIDE, NARROW),
            P(None, None, WIDE, NARROW),
            P(None, None, WIDE, NARROW),
            P(None, WIDE, NARROW),
            P(None, WIDE, NARROW),
            P(None, WIDE, NARROW),
            P(None, WIDE, NARROW),
            P(None, WIDE, NARROW),
            P(None, WIDE, NARROW),
            P(None, WIDE, NARROW),
            P(None, WIDE, NARROW),
            P(None, WIDE, NARROW),
            P(None, WIDE, NARROW),
            P(None, WIDE, NARROW),
            P(None, WIDE, NARROW),
            P(None, WIDE, NARROW),
            P(None, WIDE, NARROW),
            P(None, WIDE, NARROW),
            P(None, WIDE, NARROW),
            P(None, WIDE),
            P(None, WIDE),
            P(None, WIDE),
            P(None, WIDE),
        ),
        check_vma=False,
    )
```

```python
import functools
import math

import jax
import jax.numpy as jnp
from jax import lax
from jax.experimental import pallas as pl
from jax.experimental.pallas import tpu as pltpu
from jax.sharding import PartitionSpec as P

D = 768
HD = 64
V = 8192
STEPS = 1000
ADAM_STEP = 10


NORM_EPS = 1e-05
LEARN_RATE = 0.05
GAIN_RATE = 0.75
FIRST_DECAY = 0.9
SECOND_DECAY = 0.999
ADAM_EPS = 1e-08
WEIGHT_DECAY = 0.01
CLIP_NORM = 0.005
WIDE, NARROW = "wide", "narrow"


def add_heads(partial_value):
    return lax.psum(partial_value, NARROW)


def back_heads(partial_value):
    return lax.psum(partial_value, NARROW)


def rms_forward(value, gain):
    scale_row = lax.rsqrt(jnp.mean(value * value, axis=-1, keepdims=True) + NORM_EPS)
    return (value * scale_row * gain, scale_row)


def rms_backward(grad, value, scale_row, gain):
    unit = value * scale_row
    scaled = grad * gain
    back = scale_row * (scaled - unit * jnp.mean(scaled * unit, axis=-1, keepdims=True))
    return (back, jnp.sum(grad * unit, axis=0))


def time_features(timestep_row):
    half_width = D // 2
    rates = jnp.exp(-math.log(10000.0) * jnp.arange(half_width, dtype=jnp.float32) / half_width)
    angles = timestep_row.astype(jnp.float32)[:, None] * rates[None, :]
    return jnp.concatenate([jnp.sin(angles), jnp.cos(angles)], axis=1)


def masked_scores(queries, key_rows, segment):
    scores = jnp.einsum(
        "qhd,khd->hqk", queries, key_rows, preferred_element_type=jnp.float32
    ) * HD ** (-0.5)
    return jnp.where((segment[:, None] == segment[None, :])[None], scores, -1e30)


def attend(entry):
    queries, key_rows, values, segment = entry
    scores = masked_scores(queries, key_rows, segment)
    row_top = jnp.max(scores, axis=-1, keepdims=True)
    log_total = row_top + jnp.log(jnp.sum(jnp.exp(scores - row_top), axis=-1, keepdims=True))
    probs = jnp.exp(scores - log_total).astype(jnp.bfloat16)
    mixed = jnp.einsum("hqk,khd->qhd", probs, values, preferred_element_type=jnp.float32)
    return (mixed.astype(jnp.bfloat16), log_total)


def attend_back(entry):
    queries, key_rows, values, segment, log_total, grad_mixed = entry
    probs = jnp.exp(masked_scores(queries, key_rows, segment) - log_total)
    grad_probs = jnp.einsum("qhd,khd->hqk", grad_mixed, values, preferred_element_type=jnp.float32)
    grad_scores = (
        probs * (grad_probs - jnp.sum(probs * grad_probs, axis=-1, keepdims=True))
    ).astype(jnp.bfloat16)
    grad_query = jnp.einsum(
        "hqk,khd->qhd", grad_scores, key_rows, preferred_element_type=jnp.float32
    ) * HD ** (-0.5)
    grad_key = jnp.einsum(
        "hqk,qhd->khd", grad_scores, queries, preferred_element_type=jnp.float32
    ) * HD ** (-0.5)
    grad_value = jnp.einsum(
        "hqk,qhd->khd", probs.astype(jnp.bfloat16), grad_mixed, preferred_element_type=jnp.float32
    )
    return (grad_query, grad_key, grad_value)


def layer_forward(residual, segments, query_w, output_w, expand_w, reduce_w, gain_attn, gain_ffn):
    seq_count, seq_len = segments.shape
    normed, scale_one = rms_forward(residual, gain_attn)
    normed = normed.astype(jnp.bfloat16)
    projected = jnp.einsum(
        "sd,cde->cse", normed, query_w, preferred_element_type=jnp.float32
    ).astype(jnp.bfloat16)
    heads = projected.reshape(3, seq_count, seq_len, -1, HD)
    mixed, log_total = lax.map(attend, (heads[0], heads[1], heads[2], segments))
    mixed = mixed.reshape(seq_count * seq_len, -1)
    middle = residual + add_heads(
        jnp.einsum("se,de->sd", mixed, output_w, preferred_element_type=jnp.float32)
    )
    normed_two, scale_two = rms_forward(middle, gain_ffn)
    normed_two = normed_two.astype(jnp.bfloat16)
    before = jnp.dot(normed_two, expand_w, preferred_element_type=jnp.float32)
    after = jax.nn.gelu(before).astype(jnp.bfloat16)
    result = middle + add_heads(
        jnp.einsum("sf,df->sd", after, reduce_w, preferred_element_type=jnp.float32)
    )
    return (
        result,
        (
            residual,
            scale_one,
            normed,
            projected,
            log_total,
            mixed,
            middle,
            scale_two,
            normed_two,
            before,
            after,
        ),
    )


def layer_backward(
    grad, kept, segments, query_w, output_w, expand_w, reduce_w, gain_attn, gain_ffn
):
    (
        residual,
        scale_one,
        normed,
        projected,
        log_total,
        mixed,
        middle,
        scale_two,
        normed_two,
        before,
        after,
    ) = kept
    seq_count, seq_len = segments.shape
    grad_branch = grad.astype(jnp.bfloat16)
    grad_after = jnp.dot(grad_branch, reduce_w, preferred_element_type=jnp.float32)
    grad_reduce = jnp.einsum("sd,sf->df", grad_branch, after, preferred_element_type=jnp.float32)
    _, gelu_pull = jax.vjp(jax.nn.gelu, before)
    grad_before = gelu_pull(grad_after)[0].astype(jnp.bfloat16)
    grad_expand = jnp.einsum(
        "sd,sf->df", normed_two, grad_before, preferred_element_type=jnp.float32
    )
    grad_normed_two = back_heads(
        jnp.einsum("sf,df->sd", grad_before, expand_w, preferred_element_type=jnp.float32)
    )
    grad_middle, grad_gain_ffn = rms_backward(grad_normed_two, middle, scale_two, gain_ffn)
    grad_middle = grad_middle + grad
    grad_attn = grad_middle.astype(jnp.bfloat16)
    grad_mixed = jnp.dot(grad_attn, output_w, preferred_element_type=jnp.float32).astype(
        jnp.bfloat16
    )
    grad_output = jnp.einsum("sd,se->de", grad_attn, mixed, preferred_element_type=jnp.float32)
    heads = projected.reshape(3, seq_count, seq_len, -1, HD)
    grad_query, grad_key, grad_value = lax.map(
        attend_back,
        (
            heads[0],
            heads[1],
            heads[2],
            segments,
            log_total,
            grad_mixed.reshape(seq_count, seq_len, -1, HD),
        ),
    )
    grad_projected = (
        jnp.stack([grad_query, grad_key, grad_value])
        .reshape(3, seq_count * seq_len, -1)
        .astype(jnp.bfloat16)
    )
    grad_query_w = jnp.einsum(
        "sd,cse->cde", normed, grad_projected, preferred_element_type=jnp.float32
    )
    grad_normed = back_heads(
        jnp.einsum("cse,cde->sd", grad_projected, query_w, preferred_element_type=jnp.float32)
    )
    grad_input, grad_gain_attn = rms_backward(grad_normed, residual, scale_one, gain_attn)
    return (
        grad_input + grad_middle,
        (
            grad_query_w,
            grad_output,
            grad_expand,
            grad_reduce,
            jnp.stack([grad_gain_attn, grad_gain_ffn]),
        ),
    )


def adam(weight, grad, first, second, decay, rate):
    first_new = FIRST_DECAY * first + (1.0 - FIRST_DECAY) * grad
    second_new = SECOND_DECAY * second + (1.0 - SECOND_DECAY) * grad * grad
    first_hat = first_new / (1.0 - FIRST_DECAY**ADAM_STEP)
    second_hat = second_new / (1.0 - SECOND_DECAY**ADAM_STEP)
    weight_new = weight - rate * (first_hat / (jnp.sqrt(second_hat) + ADAM_EPS) + decay * weight)
    return (weight_new, first_new, second_new, weight_new.astype(jnp.bfloat16))


def general_device(
    noised,
    clean,
    timesteps,
    segments,
    counted,
    attn_in,
    attn_out,
    ffn_in,
    ffn_out,
    tables,
    gains,
    attn_in_mean,
    attn_out_mean,
    ffn_in_mean,
    ffn_out_mean,
    tables_mean,
    gains_mean,
    attn_in_square,
    attn_out_square,
    ffn_in_square,
    ffn_out_square,
    tables_square,
    gains_square,
):
    layers = attn_in.shape[0]
    mask = counted.reshape(-1).astype(jnp.float32)
    token_total = lax.psum(jnp.sum(mask), WIDE)
    query_w, output_w, expand_w, reduce_w, table_w, gain_low = (
        lax.all_gather(attn_in.astype(jnp.bfloat16), WIDE, axis=2, tiled=True),
        lax.all_gather(attn_out.astype(jnp.bfloat16), WIDE, axis=1, tiled=True),
        lax.all_gather(ffn_in.astype(jnp.bfloat16), WIDE, axis=1, tiled=True),
        lax.all_gather(ffn_out.astype(jnp.bfloat16), WIDE, axis=1, tiled=True),
        lax.all_gather(tables.astype(jnp.bfloat16), WIDE, axis=1, tiled=True),
        lax.all_gather(gains.astype(jnp.bfloat16), WIDE, axis=1, tiled=True),
    )
    gain_w = gain_low.astype(jnp.float32)
    noised_flat = noised.reshape(-1)
    clean_flat = clean.reshape(-1)
    step_flat = timesteps.reshape(-1)
    vocab_local = table_w.shape[2]
    vocab_ids = lax.axis_index(NARROW) * vocab_local + jnp.arange(vocab_local, dtype=jnp.int32)
    picks = (noised_flat[:, None] == vocab_ids[None, :]).astype(jnp.bfloat16)
    looked = add_heads(
        jnp.einsum("sv,dv->sd", picks, table_w[0], preferred_element_type=jnp.float32)
    )
    residual = math.sqrt(D) * looked + time_features(step_flat)
    kept_layers = []
    for layer_index in range(layers):
        residual, kept = layer_forward(
            residual,
            segments,
            query_w[layer_index],
            output_w[layer_index],
            expand_w[layer_index],
            reduce_w[layer_index],
            gain_w[2 * layer_index],
            gain_w[2 * layer_index + 1],
        )
        kept_layers.append(kept)
    final, scale_final = rms_forward(residual, gain_w[2 * layers])
    final_low = final.astype(jnp.bfloat16)
    logits = jnp.dot(final_low, table_w[1], preferred_element_type=jnp.float32)
    local_top = jnp.max(logits, axis=1)
    row_top = lax.pmax(local_top, NARROW)
    row_total = lax.psum(jnp.sum(jnp.exp(logits - row_top[:, None]), axis=1), NARROW)
    log_probs = logits - (row_top + jnp.log(row_total))[:, None]
    probs = jnp.exp(log_probs)
    clamped = jnp.maximum(step_flat, 2).astype(jnp.float32)[:, None]
    beta = 1.0 / (STEPS - clamped + 1.0)
    retain = (STEPS - clamped + 1.0) / STEPS
    spread = (clamped - 1.0) / (STEPS * V)
    at_noised = (vocab_ids[None, :] == noised_flat[:, None]).astype(jnp.float32)
    at_clean = (vocab_ids[None, :] == clean_flat[:, None]).astype(jnp.float32)
    forward_fac = beta / V + (1.0 - beta) * at_noised
    backward_fac = retain * at_clean + spread
    joint = forward_fac * backward_fac
    marginal = retain * probs + spread
    joint_total, cross, model_total, weighted, aligned, clean_logp = lax.psum(
        (
            jnp.sum(joint, axis=1),
            jnp.sum(joint * (jnp.log(backward_fac) - jnp.log(marginal)), axis=1),
            jnp.sum(forward_fac * marginal, axis=1),
            jnp.sum(probs * joint / marginal, axis=1),
            jnp.sum(forward_fac * probs, axis=1),
            jnp.sum(at_clean * log_probs, axis=1),
        ),
        NARROW,
    )
    divergence = cross / joint_total - jnp.log(joint_total) + jnp.log(model_total)
    first_step = step_flat == 1
    losses = jnp.where(first_step, -clean_logp, divergence)
    pull = retain * (
        -(joint / joint_total[:, None]) / marginal + forward_fac / model_total[:, None]
    )
    centre = retain[:, 0] * (-weighted / joint_total + aligned / model_total)
    grad_kl = probs * (pull - centre[:, None])
    grad_recon = probs - at_clean
    grad_logits = (
        (mask / token_total)[:, None] * jnp.where(first_step[:, None], grad_recon, grad_kl)
    ).astype(jnp.bfloat16)
    grad_table_out = jnp.einsum(
        "sd,sv->dv", final_low, grad_logits, preferred_element_type=jnp.float32
    )
    grad_final = back_heads(
        jnp.einsum("sv,dv->sd", grad_logits, table_w[1], preferred_element_type=jnp.float32)
    )
    grad_x, grad_gain_final = rms_backward(grad_final, residual, scale_final, gain_w[2 * layers])
    layer_grads = [None] * layers
    for layer_index in reversed(range(layers)):
        grad_x, produced = layer_backward(
            grad_x,
            kept_layers[layer_index],
            segments,
            query_w[layer_index],
            output_w[layer_index],
            expand_w[layer_index],
            reduce_w[layer_index],
            gain_w[2 * layer_index],
            gain_w[2 * layer_index + 1],
        )
        layer_grads[layer_index] = produced
    grad_look = (math.sqrt(D) * grad_x).astype(jnp.bfloat16)
    grad_table_in = jnp.einsum("sd,sv->dv", grad_look, picks, preferred_element_type=jnp.float32)
    stacked = [jnp.stack([entry[which] for entry in layer_grads]) for which in range(5)]
    gain_layers = stacked[4].reshape(2 * layers, -1)
    grad_tables_all = jnp.stack([grad_table_in, grad_table_out])
    grad_attn_in, grad_attn_out, grad_ffn_in, grad_ffn_out, grad_tables, grad_gains = (
        lax.psum_scatter(stacked[0], WIDE, scatter_dimension=2, tiled=True),
        lax.psum_scatter(stacked[1], WIDE, scatter_dimension=1, tiled=True),
        lax.psum_scatter(stacked[2], WIDE, scatter_dimension=1, tiled=True),
        lax.psum_scatter(stacked[3], WIDE, scatter_dimension=1, tiled=True),
        lax.psum_scatter(grad_tables_all, WIDE, scatter_dimension=1, tiled=True),
        lax.psum_scatter(
            jnp.concatenate([gain_layers, grad_gain_final[None, :]], axis=0),
            WIDE,
            scatter_dimension=1,
            tiled=True,
        ),
    )
    narrow_first = (lax.axis_index(NARROW) == 0).astype(jnp.float32)
    squares = (
        jnp.sum(grad_attn_in * grad_attn_in)
        + jnp.sum(grad_attn_out * grad_attn_out)
        + jnp.sum(grad_ffn_in * grad_ffn_in)
        + jnp.sum(grad_ffn_out * grad_ffn_out)
        + jnp.sum(grad_tables * grad_tables)
        + narrow_first * jnp.sum(grad_gains * grad_gains)
    )
    squares, loss_sum = lax.psum(
        (squares, narrow_first * jnp.sum(mask * losses)), (WIDE, NARROW)
    )
    grad_norm = jnp.sqrt(squares)
    factor = jnp.minimum(1.0, CLIP_NORM / (grad_norm + 1e-06))
    attn_in_next, attn_in_mean_next, attn_in_square_next, attn_in_copy = adam(
        attn_in, factor * grad_attn_in, attn_in_mean, attn_in_square, WEIGHT_DECAY, LEARN_RATE
    )
    attn_out_next, attn_out_mean_next, attn_out_square_next, attn_out_copy = adam(
        attn_out, factor * grad_attn_out, attn_out_mean, attn_out_square, WEIGHT_DECAY, LEARN_RATE
    )
    ffn_in_next, ffn_in_mean_next, ffn_in_square_next, ffn_in_copy = adam(
        ffn_in, factor * grad_ffn_in, ffn_in_mean, ffn_in_square, WEIGHT_DECAY, LEARN_RATE
    )
    ffn_out_next, ffn_out_mean_next, ffn_out_square_next, ffn_out_copy = adam(
        ffn_out, factor * grad_ffn_out, ffn_out_mean, ffn_out_square, WEIGHT_DECAY, LEARN_RATE
    )
    tables_next, tables_mean_next, tables_square_next, tables_copy = adam(
        tables, factor * grad_tables, tables_mean, tables_square, WEIGHT_DECAY, LEARN_RATE
    )
    gains_next, gains_mean_next, gains_square_next, gains_copy = adam(
        gains, factor * grad_gains, gains_mean, gains_square, 0.0, GAIN_RATE
    )
    return (
        loss_sum,
        token_total,
        grad_norm,
        attn_in_next,
        attn_in_mean_next,
        attn_in_square_next,
        attn_in_copy,
        attn_out_next,
        attn_out_mean_next,
        attn_out_square_next,
        attn_out_copy,
        ffn_in_next,
        ffn_in_mean_next,
        ffn_in_square_next,
        ffn_in_copy,
        ffn_out_next,
        ffn_out_mean_next,
        ffn_out_square_next,
        ffn_out_copy,
        tables_next,
        tables_mean_next,
        tables_square_next,
        tables_copy,
        gains_next,
        gains_mean_next,
        gains_square_next,
        gains_copy,
    )


MESH = pl.DeviceIdType.MESH
SLOW, FAST = 1, 2
HBM, KEPT, LOCAL = 1, 2, 3
F32 = jnp.float32
BF16 = jnp.bfloat16
CHUNKS = 4
VMEM_LIMIT = 61 * 1024 * 1024
FORWARD_KIND = BF16
BACKWARD_KIND = BF16


def whole_vmem():
    return pl.BlockSpec(memory_space=pltpu.VMEM)


def dot_nn(a, b):
    return lax.dot_general(a, b, (((1,), (0,)), ((), ())), preferred_element_type=F32)


def dot_nt(a, b):
    return lax.dot_general(a, b, (((1,), (1,)), ((), ())), preferred_element_type=F32)


def remote(src, dst, send_sem, recv_sem, device):
    return pltpu.make_async_remote_copy(
        src_ref=src,
        dst_ref=dst,
        send_sem=send_sem,
        recv_sem=recv_sem,
        device_id=device,
        device_id_type=MESH,
    )


def greet(devices):
    barrier = pltpu.get_barrier_semaphore()
    for device in devices:
        pl.semaphore_signal(barrier, inc=1, device_id=device, device_id_type=MESH)
    pl.semaphore_wait(barrier, len(devices))


def group_places(seq_len):
    me = lax.axis_index(NARROW)
    core = lax.rem(me, 2)
    half = seq_len // 2
    mine = pl.multiple_of(core * half, half)
    other = pl.multiple_of((1 - core) * half, half)
    return ({NARROW: me + 1 - 2 * core}, {NARROW: lax.rem(me + 2, 4)}, mine, other)


class Exchange:
    def __init__(self, refs, sems, base, sibling, partner):
        self.near_out, self.near_in, self.far_out, self.far_in = refs
        self.send, self.recv = sems
        self.base, self.sibling, self.partner = base, sibling, partner

    def near(self, j):
        return remote(
            self.near_out.at[j],
            self.near_in.at[j],
            self.send.at[self.base, j],
            self.recv.at[self.base, j],
            self.sibling,
        )

    def far(self, j):
        return remote(
            self.far_out.at[j],
            self.far_in.at[j],
            self.send.at[self.base + 1, j],
            self.recv.at[self.base + 1, j],
            self.partner,
        )

    def give(self, j, value):
        self.near_out[j] = value
        self.near(j).start()

    def pass_on(self, j, value):
        self.near(j).wait_recv()
        self.far_out[j] = (value + self.near_in[j]).astype(self.far_out.dtype)
        self.far(j).start()

    def take(self, j):
        self.far(j).wait_recv()
        return self.far_out[j].astype(F32) + self.far_in[j].astype(F32)

    def close(self):
        for j in range(CHUNKS):
            self.near(j).wait_send()
            self.far(j).wait_send()

    @staticmethod
    def scratch(chunk, width, kind):
        return [
            pltpu.VMEM((CHUNKS, chunk, width), F32),
            pltpu.VMEM((CHUNKS, chunk, width), F32),
            pltpu.VMEM((CHUNKS, chunk, width), kind),
            pltpu.VMEM((CHUNKS, chunk, width), kind),
        ]


class Share:
    def __init__(self, ref, sems, base, sibling, mine, chunk):
        self.ref, self.base, self.sibling, self.mine, self.chunk = ref, base, sibling, mine, chunk
        self.send, self.recv = sems

    def piece(self, j):
        rows = self.ref.at[pl.ds(pl.multiple_of(self.mine + j * self.chunk, self.chunk), self.chunk)]
        return remote(rows, rows, self.send.at[self.base, j], self.recv.at[self.base, j], self.sibling)

    def put(self, j, value):
        self.ref[pl.ds(pl.multiple_of(self.mine + j * self.chunk, self.chunk), self.chunk), :] = value
        self.piece(j).start()

    def arrived(self, j):
        self.piece(j).wait_recv()

    def close(self):
        for j in range(CHUNKS):
            self.piece(j).wait_send()


def wide_places(count):
    me = lax.axis_index(WIDE)
    fast = lax.rem(me, 2)
    slow = me // 2
    return (me, slow, fast, count // 2)


class Carry:
    def __init__(self, loads):
        self.loads = loads

    def peers(self):
        ways = []
        for load in self.loads:
            ways += [way for way in load.ways if way not in ways]
        me, slow, fast, slows = wide_places(self.loads[0].count) if self.loads else (0, 0, 0, 0)
        found = []
        if SLOW in ways:
            found += [{WIDE: 2 * lax.rem(slow + step, slows) + fast} for step in range(1, slows)]
        if FAST in ways:
            found.append({WIDE: me + 1 - 2 * fast})
        return found

    def begin(self, *which):
        for k in which:
            self.loads[k].start()

    def hand_on(self, *which):
        for k in which:
            self.loads[k].relay()

    def end(self, *which):
        for k in which:
            self.loads[k].finish()

    def all(self):
        return range(len(self.loads))


def part_of(weights, index, window):
    shape = weights.shape[1:]
    return shape if window is None else shape[:-1] + (window[1],)


class SlowLoad:
    ways = (SLOW,)

    def __init__(self, weights, index, lead, count, window=None):
        self.index, self.lead, self.count, self.window = index, lead, count, window
        shape, slows = part_of(weights, index, window), count // 2
        self.operands, self.in_specs = [weights], [whole_vmem()]
        self.outs = [jax.ShapeDtypeStruct((slows,) + shape, BF16)]
        self.out_specs = [pl.BlockSpec(memory_space=pl.ANY)]
        self.scratch = [pltpu.VMEM(shape, BF16), pltpu.SemaphoreType.DMA] + [pltpu.SemaphoreType.DMA((slows,))] * 2

    def bind(self, given, out, scratch):
        self.shard, self.out = given[0], out[0]
        self.low, self.local, self.send, self.recv = scratch
        self.me, self.slow, self.fast, self.slows = wide_places(self.count)

    def cast(self):
        if self.window is None:
            self.low[...] = self.shard[self.index].astype(BF16)
        else:
            self.low[...] = self.shard[self.index, :, self.window[0] : self.window[0] + self.window[1]].astype(BF16)

    def target(self):
        return self.out.at[self.slow]

    def slow_copy(self, step):
        return remote(
            self.low, self.target(), self.send.at[step], self.recv.at[step],
            {WIDE: 2 * lax.rem(self.slow + step, self.slows) + self.fast},
        )

    def own_copy(self):
        return pltpu.make_async_copy(self.low, self.target(), self.local)

    def start(self):
        self.cast()
        for step in range(1, self.slows):
            self.slow_copy(step).start()
        self.own_copy().start()

    def finish(self):
        for step in range(1, self.slows):
            self.slow_copy(step).wait()
        self.own_copy().wait()


class FastLoad:
    ways = (FAST,)

    def __init__(self, blocks, lead, count):
        self.lead, self.count = lead, count
        shape, slows = blocks.shape[1:], count // 2
        self.operands, self.in_specs = [blocks], [pl.BlockSpec(memory_space=pl.ANY)]
        self.outs = [jax.ShapeDtypeStruct(shape[:lead] + (count,) + shape[lead:], BF16)]
        self.out_specs = [whole_vmem()]
        self.scratch = [pltpu.SemaphoreType.DMA((slows,))] * 3

    def value(self):
        return self.out[...].reshape((-1, self.out.shape[-1]))

    def bind(self, given, out, scratch):
        self.blocks, self.out = given[0], out[0]
        self.local, self.send, self.recv = scratch
        self.me, self.slow, self.fast, self.slows = wide_places(self.count)

    def copies(self, step):
        target = self.out.at[(slice(None),) * self.lead + (2 * step + self.fast,)]
        return (
            remote(
                self.blocks.at[step], target, self.send.at[step], self.recv.at[step],
                {WIDE: self.me + 1 - 2 * self.fast},
            ),
            pltpu.make_async_copy(self.blocks.at[step], target, self.local.at[step]),
        )

    def start(self):
        for step in range(self.slows):
            for copy in self.copies(step):
                copy.start()

    def finish(self):
        for step in range(self.slows):
            for copy in self.copies(step):
                copy.wait()


class GatherLoad(SlowLoad):
    ways = (SLOW, FAST)

    def __init__(self, weights, index, lead, count, window=None, place=HBM):
        super().__init__(weights, index, lead, count, window)
        shape, slows = part_of(weights, index, window), count // 2
        whole = shape[:lead] + (count,) + shape[lead:]
        self.outs = [jax.ShapeDtypeStruct(whole, BF16)]
        self.scratch = self.scratch + [pltpu.SemaphoreType.DMA((slows,))] * 2
        if place == KEPT:
            self.out_specs = [whole_vmem()]
        self.local_out = place == LOCAL
        if self.local_out:
            self.outs, self.out_specs = [], []
            self.scratch = self.scratch + [pltpu.VMEM(whole, BF16)]

    def bind(self, given, out, scratch):
        if self.local_out:
            out, scratch = scratch[-1:], scratch[:-1]
        super().bind(given, out, scratch[:-2])
        self.fast_send, self.fast_recv = scratch[-2:]

    def value(self, *index):
        found = self.out[index] if index else self.out[...]
        return found.reshape((-1, found.shape[-1]))

    def at(self, owner):
        return self.out.at[(slice(None),) * self.lead + (owner,)]

    def target(self):
        return self.at(self.me)

    def fast_copy(self, step):
        block = self.at(2 * lax.rem(self.slow + self.slows - step, self.slows) + self.fast)
        return remote(
            self.low if step == 0 else block, block, self.fast_send.at[step], self.fast_recv.at[step],
            {WIDE: self.me + 1 - 2 * self.fast},
        )

    def start(self):
        super().start()
        self.fast_copy(0).start()

    def relay(self):
        for step in range(1, self.slows):
            self.slow_copy(step).wait_recv()
            self.fast_copy(step).start()

    def finish(self):
        for step in range(self.slows):
            self.fast_copy(step).wait()
            if step:
                self.slow_copy(step).wait_send()
        self.own_copy().wait()


class PairLoad:
    ways = (FAST,)

    def __init__(self, full, lead, count):
        self.lead, self.count = lead, count
        shape, slows = full.shape[:lead] + full.shape[lead + 1 :], count // 2
        self.operands, self.in_specs = [full], [whole_vmem()]
        self.outs, self.out_specs = [jax.ShapeDtypeStruct((slows,) + shape, BF16)], [whole_vmem()]
        self.scratch = [pltpu.VMEM((slows,) + shape, BF16)] + [pltpu.SemaphoreType.DMA((slows,))] * 2

    def bind(self, given, out, scratch):
        self.full, self.out = given[0], out[0]
        self.came, self.send, self.recv = scratch
        self.me, self.slow, self.fast, self.slows = wide_places(self.count)

    def block(self, step, fast):
        owner = 2 * lax.rem(self.slow + step, self.slows) + fast
        return self.full.at[(slice(None),) * self.lead + (owner,)]

    def copy(self, step):
        return remote(
            self.block(step, 1 - self.fast), self.came.at[step], self.send.at[step], self.recv.at[step],
            {WIDE: self.me + 1 - 2 * self.fast},
        )

    def start(self):
        for step in range(self.slows):
            self.copy(step).start()

    def finish(self):
        for step in range(self.slows):
            self.copy(step).wait()
            total = self.block(step, self.fast)[...].astype(F32) + self.came[step].astype(F32)
            self.out[step] = total.astype(BF16)


class LineLoad:
    ways = (SLOW,)

    def __init__(self, sums, count):
        self.count = count
        slows = count // 2
        self.operands, self.in_specs = [sums], [whole_vmem()]
        self.outs = [jax.ShapeDtypeStruct(sums.shape[1:], F32), jax.ShapeDtypeStruct((8, 128), F32)]
        self.out_specs = [whole_vmem()] * 2
        self.scratch = [pltpu.VMEM(sums.shape, BF16)] + [pltpu.SemaphoreType.DMA((slows,))] * 2

    def bind(self, given, out, scratch):
        self.sums, (self.out, self.squares) = given[0], out
        self.came, self.send, self.recv = scratch
        self.me, self.slow, self.fast, self.slows = wide_places(self.count)

    def copy(self, step):
        return remote(
            self.sums.at[step], self.came.at[step], self.send.at[step], self.recv.at[step],
            {WIDE: 2 * lax.rem(self.slow + step, self.slows) + self.fast},
        )

    def start(self):
        for step in range(1, self.slows):
            self.copy(step).start()

    def finish(self):
        total = self.sums[0].astype(F32)
        for step in range(1, self.slows):
            self.copy(step).wait()
            total = total + self.came[step].astype(F32)
        self.out[...] = total
        self.squares[...] = jnp.full(self.squares.shape, jnp.sum(total * total), F32)


def run(body, name, operands, outs, scratch, collective_id=None, loads=()):
    given, in_specs, taken = list(operands), [whole_vmem()] * len(operands), []
    for load in loads:
        places = []
        for operand, spec in zip(load.operands, load.in_specs):
            known = [k for k, other in enumerate(given) if other is operand]
            if not known:
                known = [len(given)]
                given.append(operand)
                in_specs.append(spec)
            places.append(known[0])
        taken.append(places)
    counts = [len(given), len(outs)] + [len(load.outs) for load in loads]
    counts += [len(scratch)] + [len(load.scratch) for load in loads]
    parts = 1 + len(loads)

    def kernel(*refs):
        groups, place = [], 0
        for count in counts:
            groups.append(refs[place : place + count])
            place += count
        for k, load in enumerate(loads):
            load.bind([groups[0][p] for p in taken[k]], groups[2 + k], groups[2 + parts + k])
        body(*groups[0][: len(operands)], *groups[1], *groups[1 + parts], carry=Carry(list(loads)))

    results = pl.pallas_call(
        kernel,
        out_shape=tuple(outs) + tuple(out for load in loads for out in load.outs),
        in_specs=in_specs,
        out_specs=(whole_vmem(),) * len(outs) + tuple(spec for load in loads for spec in load.out_specs),
        scratch_shapes=list(scratch) + [s for load in loads for s in load.scratch],
        compiler_params=pltpu.CompilerParams(
            collective_id=collective_id,
            has_side_effects=collective_id is not None,
            vmem_limit_bytes=VMEM_LIMIT,
        ),
        name=name,
    )(*given)
    return results[: len(outs)], results[len(outs) :]


def sems(kinds):
    return [pltpu.SemaphoreType.DMA((kinds, CHUNKS)), pltpu.SemaphoreType.DMA((kinds, CHUNKS))]


def norm_of(value, gain):
    scale = lax.rsqrt(jnp.mean(value * value, axis=-1, keepdims=True) + NORM_EPS)
    return value * scale * gain


def norm_back(grad, value, gain):
    scale = lax.rsqrt(jnp.mean(value * value, axis=-1, keepdims=True) + NORM_EPS)
    unit = value * scale
    scaled = grad * gain
    back = scale * (scaled - unit * jnp.mean(scaled * unit, axis=-1, keepdims=True))
    return (back, jnp.sum(grad * unit, axis=0, keepdims=True))


GELU_A = math.sqrt(2.0 / math.pi)
GELU_B = 0.044715


def gelu_of(x):
    return 0.5 * x * (1.0 + jnp.tanh(GELU_A * (x + GELU_B * (x * x * x))))


def gelu_slope(x):
    square = x * x
    t = jnp.tanh(GELU_A * (x + GELU_B * (x * square)))
    return 0.5 * (1.0 + t) + 0.5 * x * (1.0 - t * t) * (GELU_A * (1.0 + 3.0 * GELU_B * square))


def rows_at(start, j, chunk):
    return pl.ds(pl.multiple_of(start + j * chunk, chunk), chunk)


LANES = 128


def spread(row):
    return jnp.transpose(jnp.broadcast_to(row, (LANES, LANES)))


def feature_places(owner, width, share):
    lane = lax.broadcasted_iota(jnp.int32, (LANES, width), 0)
    feature = lax.broadcasted_iota(jnp.int32, (LANES, width), 1)
    return ((feature == lane + owner * share) & (lane < share)).astype(F32).astype(BF16)


def token_picks(ids, vocab, first):
    here = spread(ids.astype(F32) - first.astype(F32))
    lane = lax.broadcasted_iota(jnp.int32, (LANES, LANES), 1).astype(F32)
    return [jnp.where(here == lane + float(t * LANES), 1.0, 0.0).astype(BF16) for t in range(vocab // LANES)]


def embed_part(
    ids, counted, gains, extra, table,
    resid, normed, gain_all, count_all, ids_all,
    low, picks, small, near_out, near_in, own, far_out, far_in, wide_out, wide_in, part_out, part_in,
    id_send, id_recv, small_send, small_recv, near_send, near_recv, far_send, far_recv, wide_send, wide_recv,
    part_send, part_recv, send, recv, carry,
):
    seq_len, width = normed.shape
    chunk = seq_len // 2 // CHUNKS
    quarter = seq_len // 4
    share, vocab = table.shape[1:]
    owners = ids_all.shape[0]
    id_rows = ids.shape[0]
    sibling, partner, mine, other = group_places(seq_len)
    place = lax.axis_index(NARROW)
    side = lax.div(place, 2)
    me = lax.axis_index(WIDE)
    first = place * vocab
    around = [lax.rem(me + step, owners) for step in range(owners)]

    def id_copy(step):
        return remote(ids_all.at[me], ids_all.at[me], id_send.at[step], id_recv.at[step], {WIDE: around[step]})

    def small_copy(step):
        return remote(small.at[me], small.at[me], small_send.at[step], small_recv.at[step], {WIDE: around[step]})

    def near_copy(step):
        return remote(near_out.at[step], near_in.at[step], near_send.at[step], near_recv.at[step], sibling)

    def far_copy(step):
        return remote(far_out.at[step], far_in.at[step], far_send.at[step], far_recv.at[step], partner)

    def wide_copy(step):
        return remote(wide_out.at[step], wide_in.at[me], wide_send.at[step], wide_recv.at[step], {WIDE: around[step]})

    def part_copy(piece):
        rows = pl.ds(piece * LANES, LANES)
        return remote(part_out.at[rows], part_in.at[rows], part_send.at[piece], part_recv.at[piece], partner)

    ids_all[me] = ids[...]
    small[me] = jnp.zeros(small.shape[1:], F32)
    small[me, : gains.shape[0], : gains.shape[1]] = gains[...].astype(BF16).astype(F32)
    count = jnp.sum(counted[...].astype(F32), keepdims=True)
    small[me, gains.shape[0] : gains.shape[0] + 1, :] = jnp.broadcast_to(count, (1, small.shape[2]))
    greet([{WIDE: device} for device in around[1:]] + [sibling, partner])
    for step in range(1, owners):
        id_copy(step).start()
    for step in range(1, owners):
        small_copy(step).start()
    carry.begin(0, 1)
    padded = jnp.concatenate([table[0], jnp.zeros((LANES - share, vocab), F32)], axis=0)
    low[...] = jnp.transpose(padded).astype(BF16)

    def look_up(step):
        row = lax.rem(me + step, owners)

        def find(start):
            def block(b, _):
                place_of = start // LANES + b
                for t, pick in enumerate(token_picks(ids_all[row, pl.ds(place_of, 1), :], vocab, first)):
                    picks[rows_at(0, b, LANES), t * LANES : (t + 1) * LANES] = pick
                return 0

            lax.fori_loop(0, seq_len // 2 // LANES, block, 0)
            return dot_nn(picks[...], low[...]).astype(BF16)

        near_out[step] = find(other)
        near_copy(step).start()
        own[step] = find(mine)

    def halve(step):
        near_copy(step).wait_recv()
        total = own[step] + near_in[step]
        own[step] = total
        far_out[step] = own[step, pl.ds(pl.multiple_of((1 - side) * quarter, quarter), quarter), :]
        far_copy(step).start()

    def deliver(step):
        far_copy(step).wait_recv()
        total = own[step, pl.ds(pl.multiple_of(side * quarter, quarter), quarter), :] + far_in[step]
        if step % owners == 0:
            wide_in[me] = total
        else:
            wide_out[step] = total
            wide_copy(step).start()

    order = list(range(1, owners)) + [0]
    for turn in range(owners + 2):
        if turn < owners:
            if order[turn]:
                id_copy(owners - order[turn]).wait_recv()
            look_up(order[turn])
        if 1 <= turn < owners + 1:
            halve(order[turn - 1])
        if turn >= 2:
            deliver(order[turn - 2])
        if turn == 1:
            carry.begin(2)
    carry.begin(3)
    carry.hand_on(0, 1)
    for step in range(1, owners):
        small_copy(step).wait_recv()
    total = None
    for owner in range(owners):
        part = dot_nn(small[owner].astype(BF16), feature_places(owner, width, share))
        total = part if total is None else total + part
    gain_all[...] = total
    count_all[...] = jnp.sum(small[...], axis=0)
    for step in range(1, owners):
        wide_copy(step).wait_recv()
    pieces = quarter // LANES
    at_side = pl.multiple_of(side * quarter, quarter)
    at_other = pl.multiple_of((1 - side) * quarter, quarter)
    for piece in range(pieces):
        rows = pl.ds(piece * LANES, LANES)
        found = None
        for owner in range(owners):
            part = dot_nn(wide_in[owner, rows, :], feature_places(owner, width, share))
            found = part if found is None else found + part
        part_out[rows, :] = found.astype(BF16)
        part_copy(piece).start()

    def finish(start, source, piece):
        rows = rows_at(start, piece, LANES)
        x = math.sqrt(width) * source[pl.ds(piece * LANES, LANES), :].astype(F32) + extra[rows, :]
        resid[rows, :] = x
        here = rows_at(mine + start, piece, LANES)
        normed[here, :] = norm_of(x, gain_all[0:1, :]).astype(BF16)
        give_rows(here, piece if source is part_out else pieces + piece).start()

    def give_rows(here, k):
        return remote(normed.at[here], normed.at[here], send.at[0, k], recv.at[0, k], sibling)

    for piece in range(pieces):
        finish(at_side, part_out, piece)
    for piece in range(pieces):
        part_copy(piece).wait_recv()
        finish(at_other, part_in, piece)
    carry.hand_on(2)
    for k in range(2 * pieces):
        give_rows(rows_at(mine, k % pieces, LANES), k).wait()
    for step in range(owners):
        near_copy(step).wait_send()
        far_copy(step).wait_send()
        if step:
            id_copy(step).wait_send()
            small_copy(step).wait_send()
            wide_copy(step).wait_send()
    for piece in range(pieces):
        part_copy(piece).wait_send()


QUERY_BLOCK = 256


def forward_part(
    layer, weights, points, normed, key_seg, query_seg, resid, gains,
    projected, mixed, middle, normed_two, result, normed_next,
    bias, values_t, near_out, near_in, far_out, far_in, near_out2, near_in2, far_out2, far_in2, own2, send, recv,
):
    w_query, w_out, w_in, w_red = weights
    at_half, at_feed, at_sent, at_last = points
    seq_len, width = normed.shape
    chunk = seq_len // 2 // CHUNKS
    block = bias.shape[1]
    heads = mixed.shape[1] // HD
    sibling, partner, mine, other = group_places(seq_len)
    pair = (send, recv)
    first = Exchange((near_out, near_in, far_out, far_in), pair, 0, sibling, partner)
    second = Exchange((near_out2, near_in2, far_out2, far_in2), pair, 2, sibling, partner)
    share = Share(normed_two, pair, 4, sibling, mine, chunk)
    share_next = Share(normed_next, pair, 5, sibling, mine, chunk)

    def ask(i, _):
        rows = rows_at(0, i, block)
        for which in range(3):
            projected[which, rows, :] = dot_nn(normed[rows, :], w_query(which)).astype(BF16)
        return 0

    lax.fori_loop(0, seq_len // block, ask, 0)
    values_t[...] = jnp.transpose(projected[2])

    def attend_rows(start):
        rows = pl.ds(pl.multiple_of(start, block), block)
        bias[...] = jnp.where(key_seg[...] == query_seg[:, rows], 0.0, -1e30)
        asked = projected[0, rows, :] * HD ** (-0.5)
        parts = []
        for head in range(heads):
            scores = dot_nt(projected[1], head_lanes(asked, head, HD)) + bias[...]
            powers = jnp.exp(scores - jnp.max(scores, axis=0, keepdims=True))
            probs = (powers * (1.0 / jnp.sum(powers, axis=0, keepdims=True))).astype(BF16)
            parts.append(dot_nn(values_t[head * HD : (head + 1) * HD, :], probs))
        mixed[rows, :] = jnp.transpose(jnp.concatenate(parts, axis=0)).astype(BF16)

    def project(start, j):
        return dot_nt(mixed[rows_at(start, j, chunk), :], w_out())

    def feed(rows):
        pre = dot_nn(normed_two[rows, :], w_in())
        return dot_nt(gelu_of(pre).astype(BF16), w_red())

    per_block = block // chunk
    for part in range(CHUNKS // per_block):

        def both(i, _):
            attend_rows(jnp.where(i == 0, other, mine) + part * block)
            return 0

        lax.fori_loop(0, 2, both, 0)
        for j in range(part * per_block, (part + 1) * per_block):
            first.give(j, project(other, j))
        if part == 0:
            at_half()
        for j in range(part * per_block, (part + 1) * per_block):
            first.pass_on(j, project(mine, j))
    at_feed()
    for j in range(CHUNKS):
        rows = rows_at(0, j, chunk)
        mid = resid[rows, :] + first.take(j)
        middle[rows, :] = mid
        share.put(j, norm_of(mid, gains[2 * layer + 1 : 2 * layer + 2, :]).astype(BF16))
        own2[j] = feed(rows_at(mine, j, chunk))
        share.arrived(j)
        second.give(j, feed(rows_at(other, j, chunk)))
        if j >= 1:
            second.pass_on(j - 1, own2[j - 1])
    second.pass_on(CHUNKS - 1, own2[CHUNKS - 1])
    at_sent()
    for j in range(CHUNKS):
        rows = rows_at(0, j, chunk)
        x = middle[rows, :] + second.take(j)
        result[rows, :] = x
        share_next.put(j, norm_of(x, gains[2 * layer + 2 : 2 * layer + 3, :]).astype(BF16))
        if j == CHUNKS - 2:
            at_last()
    for j in range(CHUNKS):
        share_next.arrived(j)
    for part in (first, second, share, share_next):
        part.close()


def layer_outs(seq_len, width, heads_width):
    return [
        jax.ShapeDtypeStruct((3, seq_len, heads_width), BF16),
        jax.ShapeDtypeStruct((seq_len, heads_width), BF16),
        jax.ShapeDtypeStruct((seq_len // 2, width), F32),
        jax.ShapeDtypeStruct((seq_len, width), BF16),
    ]


def layer_scratch(seq_len, width, heads_width):
    half, chunk = seq_len // 2, seq_len // 2 // CHUNKS
    block = max(chunk, min(QUERY_BLOCK, half))
    return (
        [pltpu.VMEM((seq_len, block), F32), pltpu.VMEM((heads_width, seq_len), BF16)]
        + Exchange.scratch(chunk, width, FORWARD_KIND)
        + Exchange.scratch(chunk, width, FORWARD_KIND)
        + [pltpu.VMEM((CHUNKS, chunk, width), F32)]
        + sems(6)
    )


LAYER_SCRATCH = 13


def front_kernel(
    ids, counted, gains, extra, table, key_seg, query_seg,
    resid, normed, gain_all, count_all, ids_all, projected, mixed, middle, normed_two, result, normed_next,
    *scratch, carry,
):
    embed_part(
        ids, counted, gains, extra, table, resid, normed, gain_all, count_all, ids_all,
        *scratch[:-LAYER_SCRATCH], carry,
    )
    carry.end(0, 1)
    later = list(carry.all())[4:]

    def at_half():
        carry.hand_on(3)
        carry.begin(*later[:2])

    def at_feed():
        carry.end(2, 3)
        carry.begin(*later[2:])

    forward_part(
        0,
        [carry.loads[0].value] + [load.value for load in carry.loads[1:4]],
        (at_half, at_feed, lambda: carry.hand_on(*later[:2]), lambda: carry.hand_on(*later[2:3])),
        normed, key_seg, query_seg, resid, gain_all,
        projected, mixed, middle, normed_two, result, normed_next, *scratch[-LAYER_SCRATCH:],
    )
    carry.end(*later)


def front(ids, counted, gains, extra, tables, key_seg, query_seg, owners, heads_width, collective_id, loads):
    seq_len = ids.size
    half, width = extra.shape
    share, vocab = tables.shape[1:]
    dma = pltpu.SemaphoreType.DMA
    return run(
        front_kernel,
        "front",
        [ids, counted, gains, extra, tables, key_seg, query_seg],
        [
            jax.ShapeDtypeStruct((half, width), F32),
            jax.ShapeDtypeStruct((seq_len, width), BF16),
            jax.ShapeDtypeStruct((8, width), F32),
            jax.ShapeDtypeStruct((8, LANES), F32),
            jax.ShapeDtypeStruct((owners,) + ids.shape, jnp.int32),
        ]
        + layer_outs(seq_len, width, heads_width)
        + [jax.ShapeDtypeStruct((half, width), F32), jax.ShapeDtypeStruct((seq_len, width), BF16)],
        [
            pltpu.VMEM((vocab, LANES), BF16),
            pltpu.VMEM((half, vocab), BF16),
            pltpu.VMEM((owners, 8, LANES), F32),
            pltpu.VMEM((owners, half, LANES), BF16),
            pltpu.VMEM((owners, half, LANES), BF16),
            pltpu.VMEM((owners, half, LANES), BF16),
            pltpu.VMEM((owners, half // 2, LANES), BF16),
            pltpu.VMEM((owners, half // 2, LANES), BF16),
            pltpu.VMEM((owners, half // 2, LANES), BF16),
            pltpu.VMEM((owners, half // 2, LANES), BF16),
            pltpu.VMEM((half // 2, width), BF16),
            pltpu.VMEM((half // 2, width), BF16),
        ]
        + [dma((owners,))] * 10
        + [dma((half // 2 // LANES,))] * 2
        + [dma((1, half // LANES))] * 2
        + layer_scratch(seq_len, width, heads_width),
        collective_id,
        loads,
    )


TILE = 256


def weight_grad(left_t, right, out):
    columns = right.shape[1]
    tile = TILE if columns % TILE == 0 else columns

    def step(i, _):
        where = pl.ds(pl.multiple_of(i * tile, tile), tile)
        out[:, where] = dot_nn(left_t[...], right[:, where]).astype(out.dtype)
        return 0

    if tile == columns:
        out[...] = dot_nn(left_t[...], right[...]).astype(out.dtype)
    else:
        lax.fori_loop(0, columns // tile, step, 0)


def ffn_back_kernel(
    row, grad, branch, w_red, w_in, w_out, normed, middle, gain, mixed,
    grad_middle, grad_attn, grad_mixed, d_red, d_in, d_out, d_gain,
    grad_before, after, turned, near_out, near_in, far_out, far_in, send, recv, carry,
):
    seq_len = normed.shape[0]
    chunk = seq_len // 2 // CHUNKS
    sibling, partner, mine, other = group_places(seq_len)
    greet([sibling, partner] + carry.peers())
    carry.begin(*carry.all())
    sems = (send, recv)
    trade = Exchange((near_out, near_in, far_out, far_in), sems, 0, sibling, partner)
    share = Share(grad_attn, sems, 2, sibling, mine, chunk)

    def partial(start, j):
        rows = rows_at(start, j, chunk)
        pre = dot_nn(normed[rows, :], w_in[...])
        after[rows, :] = gelu_of(pre).astype(BF16)
        low = (dot_nn(branch[rows, :], w_red[...]) * gelu_slope(pre)).astype(BF16)
        grad_before[rows, :] = low
        return dot_nt(low, w_in[...])

    trade.give(0, partial(other, 0))
    for j in range(CHUNKS):
        if j + 1 < CHUNKS:
            trade.give(j + 1, partial(other, j + 1))
        trade.pass_on(j, partial(mine, j))
    turned[...] = jnp.transpose(branch[...])
    weight_grad(turned, after, d_red)
    turned[...] = jnp.transpose(normed[...])
    weight_grad(turned, grad_before, d_in)
    gain_total = jnp.zeros((1, gain.shape[1]), F32)
    for j in range(CHUNKS):
        rows = rows_at(0, j, chunk)
        back, gain_part = norm_back(trade.take(j), middle[rows, :], gain[row : row + 1, :])
        gain_total = gain_total + gain_part
        total = back + grad[rows, :]
        grad_middle[rows, :] = total
        share.put(j, total.astype(BF16))
        here = rows_at(mine, j, chunk)
        grad_mixed[here, :] = dot_nn(grad_attn[here, :], w_out[...]).astype(BF16)
    for j in range(CHUNKS):
        share.arrived(j)
        here = rows_at(other, j, chunk)
        grad_mixed[here, :] = dot_nn(grad_attn[here, :], w_out[...]).astype(BF16)
    d_gain[...] = gain_total
    turned[...] = jnp.transpose(grad_attn[...])
    weight_grad(turned, mixed, d_out)
    trade.close()
    share.close()
    carry.end(*carry.all())


def ffn_backward(row, grad, branch, w_red, w_in, w_out, normed, middle, gain, mixed, collective_id, loads):
    seq_len, width = normed.shape
    half, chunk = seq_len // 2, seq_len // 2 // CHUNKS
    return run(
        functools.partial(ffn_back_kernel, row),
        "ffn_backward",
        [grad, branch, w_red, w_in, w_out, normed, middle, gain, mixed],
        [
            jax.ShapeDtypeStruct((half, width), F32),
            jax.ShapeDtypeStruct((seq_len, width), BF16),
            jax.ShapeDtypeStruct(mixed.shape, BF16),
            jax.ShapeDtypeStruct(w_red.shape, BF16),
            jax.ShapeDtypeStruct(w_in.shape, BF16),
            jax.ShapeDtypeStruct(w_out.shape, BF16),
            jax.ShapeDtypeStruct((1, gain.shape[1]), F32),
        ],
        [pltpu.VMEM((seq_len, w_in.shape[1]), BF16)] * 2 + [pltpu.VMEM((width, seq_len), BF16)]
        + Exchange.scratch(chunk, width, BACKWARD_KIND)
        + sems(3),
        collective_id,
        loads,
    )


def norm_back_kernel(
    scale, row, grads, weights, normed, value, gain, upstream,
    grad_out, branch, d_weights, d_gain,
    turned, near_out, near_in, far_out, far_in, send, recv, carry,
):
    seq_len, width = normed.shape
    chunk = seq_len // 2 // CHUNKS
    sibling, partner, mine, other = group_places(seq_len)
    greet([sibling, partner] + carry.peers())
    carry.begin(*carry.all())
    sems = (send, recv)
    trade = Exchange((near_out, near_in, far_out, far_in), sems, 0, sibling, partner)
    share = Share(branch, sems, 2, sibling, mine, chunk)

    def partial(start, j):
        rows = rows_at(start, j, chunk)
        total = None
        for which in range(grads.shape[0]):
            part = dot_nt(grads[which, rows, :], weights[which])
            total = part if total is None else total + part
        return total

    trade.give(0, partial(other, 0))
    for j in range(CHUNKS):
        if j + 1 < CHUNKS:
            trade.give(j + 1, partial(other, j + 1))
        trade.pass_on(j, partial(mine, j))
    turned[...] = jnp.transpose(normed[...])
    for which in range(grads.shape[0]):
        weight_grad(turned, grads.at[which], d_weights.at[which])
    gain_total = jnp.zeros((1, gain.shape[1]), F32)
    for j in range(CHUNKS):
        rows = rows_at(0, j, chunk)
        back, gain_part = norm_back(trade.take(j), value[rows, :], gain[row : row + 1, :])
        gain_total = gain_total + gain_part
        back = back + upstream[rows, :]
        grad_out[rows, :] = back
        share.put(j, (back if scale is None else scale * back).astype(BF16))
    d_gain[...] = gain_total
    for j in range(CHUNKS):
        share.arrived(j)
    trade.close()
    share.close()
    carry.end(*carry.all())


def norm_backward(row, grads, weights, normed, value, gain, upstream, scale, collective_id, loads):
    seq_len, width = normed.shape
    half, chunk = seq_len // 2, seq_len // 2 // CHUNKS
    return run(
        functools.partial(norm_back_kernel, scale, row),
        "norm_backward",
        [grads, weights, normed, value, gain, upstream],
        [
            jax.ShapeDtypeStruct((half, width), F32),
            jax.ShapeDtypeStruct((seq_len, width), BF16),
            jax.ShapeDtypeStruct(weights.shape, BF16),
            jax.ShapeDtypeStruct((1, gain.shape[1]), F32),
        ],
        [pltpu.VMEM((width, seq_len), BF16)] + Exchange.scratch(chunk, width, BACKWARD_KIND) + sems(3),
        collective_id,
        loads,
    )


def head_lanes(value, head, size):
    lanes = lax.broadcasted_iota(jnp.int32, value.shape, 1)
    inside = (lanes >= head * size) & (lanes < (head + 1) * size)
    return jnp.where(inside, value, jnp.zeros_like(value))


def attention_back_kernel(projected, grad_mixed, key_seg, query_seg, out, bias, keys_t, grad_keys, grad_values, carry):
    seq_len, width = grad_mixed.shape
    block = bias.shape[1]
    heads = width // HD
    scale = HD ** (-0.5)
    if carry.loads:
        greet(carry.peers())
    carry.begin(*carry.all())
    keys_t[...] = jnp.transpose(projected[1])
    grad_keys[...] = jnp.zeros(grad_keys.shape, F32)
    grad_values[...] = jnp.zeros(grad_values.shape, F32)

    def queries(i, _):
        rows = rows_at(0, i, block)
        bias[...] = jnp.where(key_seg[...] == query_seg[:, rows], 0.0, -1e30)
        asked = projected[0, rows, :] * scale
        given = grad_mixed[rows, :]
        parts = []
        for head in range(heads):
            query = head_lanes(asked, head, HD)
            grad = head_lanes(given, head, HD)
            scores = dot_nt(projected[1], query) + bias[...]
            powers = jnp.exp(scores - jnp.max(scores, axis=0, keepdims=True))
            probs = powers * (1.0 / jnp.sum(powers, axis=0, keepdims=True))
            grad_probs = dot_nt(projected[2], grad)
            centre = jnp.sum(probs * grad_probs, axis=0, keepdims=True)
            grad_scores = (probs * (grad_probs - centre)).astype(BF16)
            parts.append(dot_nn(keys_t[head * HD : (head + 1) * HD, :], grad_scores))
            grad_keys[...] += dot_nn(grad_scores, query)
            grad_values[...] += dot_nn(probs.astype(BF16), grad)
        out[0, rows, :] = (jnp.transpose(jnp.concatenate(parts, axis=0)) * scale).astype(BF16)
        return 0

    lax.fori_loop(0, seq_len // block, queries, 0)
    out[1] = grad_keys[...].astype(BF16)
    out[2] = grad_values[...].astype(BF16)
    carry.end(*carry.all())


def attention_back(projected, grad_mixed, key_seg, query_seg, collective_id, loads):
    seq_len, width = grad_mixed.shape
    block = min(QUERY_BLOCK, seq_len)
    return run(
        attention_back_kernel,
        "attention_back",
        [projected, grad_mixed, key_seg, query_seg],
        [jax.ShapeDtypeStruct(projected.shape, BF16)],
        [
            pltpu.VMEM((seq_len, block), F32),
            pltpu.VMEM((width, seq_len), BF16),
            pltpu.VMEM((seq_len, width), F32),
            pltpu.VMEM((seq_len, width), F32),
        ],
        collective_id if loads else None,
        loads,
    )


def to_rows(columns):
    lanes = lax.broadcasted_iota(jnp.int32, (LANES, LANES), 1)
    total = jnp.zeros((LANES, LANES), F32)
    for k, column in enumerate(columns):
        total = jnp.where(lanes == k, column, total)
    return jnp.transpose(total)[:8, :]


def loss_part(
    row, normed, info, value, gain, table_loads, grad_out, branch, d_gain, losses, d_tables,
    logits, grads, places, turned, stat_out, stat_in, sum_out, sum_in,
    stat_send, stat_recv, sum_send, sum_recv, near_out, near_in, far_out, far_in, send, recv,
):
    seq_len, width = normed.shape
    chunk = seq_len // 2 // CHUNKS
    piece_width = table_loads[0].out.shape[-1]
    vocab = piece_width * len(table_loads)
    tiles = vocab // LANES
    blocks = seq_len // LANES
    me = lax.axis_index(NARROW)
    sibling, partner, mine, other = group_places(seq_len)
    peers = [{NARROW: lax.rem(me + k, 4)} for k in range(1, 4)]
    sems = (send, recv)
    trade = Exchange((near_out, near_in, far_out, far_in), sems, 0, sibling, partner)
    share = Share(branch, sems, 2, sibling, mine, chunk)
    first = (me * vocab).astype(F32)
    whole = 4.0 * vocab
    lanes = lax.broadcasted_iota(jnp.int32, (LANES, LANES), 1).astype(F32)

    def stat_copy(b, k):
        return remote(stat_out.at[b], stat_in.at[k, b], stat_send.at[k, b], stat_recv.at[k, b], peers[k])

    def sum_copy(b, k):
        return remote(sum_out.at[b], sum_in.at[k, b], sum_send.at[k, b], sum_recv.at[k, b], peers[k])

    def tile_at(t):
        return pl.ds(pl.multiple_of(t * LANES, LANES), LANES)

    def ask(b, _):
        rows = rows_at(0, b, LANES)
        here = info[:, rows]
        at_noised = spread(here[0:1] - first)
        at_clean = spread(here[1:2] - first)
        places[b, 0] = at_noised
        places[b, 1] = at_clean

        def top_step(t, top):
            return jnp.maximum(top, logits[rows, tile_at(t)])

        top = lax.fori_loop(1, tiles, top_step, logits[rows, tile_at(0)], unroll=4)
        top = jnp.max(top, axis=1, keepdims=True)
        top_wide = jnp.broadcast_to(top, (LANES, LANES))

        def sum_step(t, totals):
            powers, noised, clean = totals
            piece = logits[rows, tile_at(t)]
            column = lanes + (t * LANES).astype(F32)
            return (
                powers + jnp.exp(piece - top_wide),
                noised + jnp.where(column == at_noised, piece, 0.0),
                clean + jnp.where(column == at_clean, piece, 0.0),
            )

        zero = jnp.zeros((LANES, LANES), F32)
        totals = lax.fori_loop(0, tiles, sum_step, (zero, zero, zero), unroll=2)
        stat_out[b] = to_rows([top] + [jnp.sum(total, axis=1, keepdims=True) for total in totals])
        for k in range(3):
            stat_copy(b, k).start()
        return 0

    for k, table in enumerate(table_loads):
        if k == len(table_loads) - 1:
            table.finish()

        def product(i, _):
            rows = rows_at(0, i, TILE)
            logits[rows, k * piece_width : (k + 1) * piece_width] = dot_nn(normed[rows, :], table.value())
            return 0

        lax.fori_loop(0, seq_len // TILE, product, 0)
    lax.fori_loop(0, blocks, ask, 0)

    def scalars(b):
        here = info[:, rows_at(0, b, LANES)]
        step = jnp.maximum(here[2:3], 2.0)
        left = STEPS - step + 1.0
        beta = 1.0 / left
        keep = left / STEPS
        rest = (step - 1.0) / (STEPS * whole)
        own = stat_out[b]
        others = [stat_in[k, b] for k in range(3)]
        top = own[0:1]
        for stat in others:
            top = jnp.maximum(top, stat[0:1])
        total = own[1:2] * jnp.exp(own[0:1] - top)
        noised, clean = own[2:3], own[3:4]
        for stat in others:
            total = total + stat[1:2] * jnp.exp(stat[0:1] - top)
            noised, clean = noised + stat[2:3], clean + stat[3:4]
        return here, beta, keep, rest, top + jnp.log(total), noised, clean

    def measure(b, _):
        rows = rows_at(0, b, LANES)
        for k in range(3):
            stat_copy(b, k).wait_recv()
        _, _, keep, rest, log_total, _, _ = scalars(b)
        log_wide = spread(log_total)
        ratio = spread(keep / rest)

        def step(t, totals):
            logs, shares = totals
            probs = jnp.exp(logits[rows, tile_at(t)] - log_wide)
            logits[rows, tile_at(t)] = probs
            grown = 1.0 + probs * ratio
            return (logs + jnp.log(grown), shares + probs / grown)

        zero = jnp.zeros((LANES, LANES), F32)
        totals = lax.fori_loop(0, tiles, step, (zero, zero), unroll=2)
        sum_out[b] = to_rows([jnp.sum(total, axis=1, keepdims=True) for total in totals])
        for k in range(3):
            sum_copy(b, k).start()
        return 0

    lax.fori_loop(0, blocks, measure, 0)

    def pull(b):
        rows = rows_at(0, b, LANES)
        for k in range(3):
            sum_copy(b, k).wait_recv()
        here, beta, keep, rest, log_total, noised, clean = scalars(b)
        sums = sum_out[b] + sum_in[0, b] + sum_in[1, b] + sum_in[2, b]
        log_sum, share_sum = sums[0:1], sums[1:2] / rest
        same = here[0:1] == here[1:2]
        first_step = here[2:3] == 1.0
        base_a, more_a = beta / whole, 1.0 - beta
        base_w = base_a * rest
        joint = whole * base_w + more_a * rest + base_a * keep + jnp.where(same, more_a * keep, 0.0)
        ratio = keep / rest
        prob_n, prob_c = jnp.exp(noised - log_total), jnp.exp(clean - log_total)
        grown_n, grown_c = 1.0 + prob_n * ratio, 1.0 + prob_c * ratio
        marginal_n, marginal_c = rest * grown_n, rest * grown_c
        log_n, log_c = jnp.log(grown_n), jnp.log(grown_c)
        weight_n = jnp.where(same, 0.0, more_a * rest)
        weight_c = jnp.where(same, more_a * rest + base_a * keep + more_a * keep, base_a * keep)
        lift = jnp.log((keep + rest) / rest)
        cross = -base_w * log_sum - weight_n * log_n - weight_c * log_c + (base_w + weight_c) * lift
        model = base_a * (keep + whole * rest) + more_a * marginal_n
        divergence = cross / joint - jnp.log(joint) + jnp.log(model)
        loss = jnp.where(first_step, log_total - clean, divergence)
        losses[:, rows] = here[4:5] * loss
        weighted = base_w * share_sum + weight_n * prob_n / marginal_n + weight_c * prob_c / marginal_c
        aligned = base_a + more_a * prob_n
        centre = keep * (aligned / model - weighted / joint)
        scale = here[3:4]
        zero = jnp.zeros_like(scale)
        even = scale * jnp.where(first_step, 1.0, keep * base_a / model - centre)
        bent = scale * jnp.where(first_step, zero, -keep * base_w / joint / rest)
        at_n = prob_n * keep * (more_a / model - weight_n / joint / marginal_n)
        at_c = -prob_c * keep * (weight_c / joint / marginal_c)
        extra_n = spread(scale * jnp.where(first_step, zero, at_n))
        extra_c = spread(scale * jnp.where(first_step, -1.0, at_c))
        even, bent, ratio = spread(even), spread(bent), spread(ratio)
        at_noised, at_clean = places[b, 0], places[b, 1]

        def step(t, _):
            probs = logits[rows, tile_at(t)]
            column = lanes + (t * LANES).astype(F32)
            grad = probs * (even + bent / (1.0 + probs * ratio))
            grad = grad + jnp.where(column == at_noised, extra_n, 0.0)
            grad = grad + jnp.where(column == at_clean, extra_c, 0.0)
            grads[rows, tile_at(t)] = grad.astype(BF16)
            return 0

        lax.fori_loop(0, tiles, step, 0, unroll=2)

    def partial(start, j):
        base = start // LANES + j * (chunk // LANES)
        for b in range(chunk // LANES):
            pull(base + b)
        total = None
        for k, table in enumerate(table_loads):
            part = dot_nt(grads[rows_at(start, j, chunk), k * piece_width : (k + 1) * piece_width], table.value())
            total = part if total is None else total + part
        return total

    trade.give(0, partial(other, 0))
    for j in range(CHUNKS):
        if j + 1 < CHUNKS:
            trade.give(j + 1, partial(other, j + 1))
        trade.pass_on(j, partial(mine, j))
    turned[...] = jnp.transpose(normed[...])
    for k, d_table in enumerate(d_tables):
        weight_grad(turned, grads.at[:, k * piece_width : (k + 1) * piece_width], d_table)
    gain_total = jnp.zeros((1, gain.shape[1]), F32)
    for j in range(CHUNKS):
        rows = rows_at(0, j, chunk)
        back, gain_part = norm_back(trade.take(j), value[rows, :], gain[row : row + 1, :])
        gain_total = gain_total + gain_part
        grad_out[rows, :] = back
        share.put(j, back.astype(BF16))
    d_gain[...] = gain_total
    for j in range(CHUNKS):
        share.arrived(j)
    trade.close()
    share.close()

    def finish(b, _):
        for k in range(3):
            stat_copy(b, k).wait_send()
            sum_copy(b, k).wait_send()
        return 0

    lax.fori_loop(0, blocks, finish, 0)


def back_kernel(
    layer, normed, key_seg, query_seg, resid, w_query, w_out, w_in, gains, info,
    projected, mixed, middle, normed_two, grad_out, branch, d_gain, losses, *refs, carry,
):
    pieces = len(carry.loads) - 1
    d_tables, refs = refs[:pieces], refs[pieces:]
    (result, normed_next), refs = refs[:2], refs[2:]
    loss_scratch, layer_refs = refs[:-LAYER_SCRATCH], refs[-LAYER_SCRATCH:]
    me = lax.axis_index(NARROW)
    greet([{NARROW: lax.rem(me + k, 4)} for k in range(1, 4)] + carry.peers())
    carry.begin(0, 1)

    def at_half():
        carry.begin(2)

    def at_feed():
        carry.end(0)
        carry.hand_on(1)
        carry.begin(3)

    def at_sent():
        carry.hand_on(2)
        carry.begin(4)

    def at_last():
        carry.hand_on(3)

    forward_part(
        layer,
        [lambda which: w_query[which], lambda: w_out[...], lambda: w_in[...], carry.loads[0].value],
        (at_half, at_feed, at_sent, at_last),
        normed, key_seg, query_seg, resid, gains,
        projected, mixed, middle, normed_two, result, normed_next, *layer_refs,
    )
    carry.hand_on(4)
    carry.end(1, 2, 3)
    loss_part(
        2 * layer + 2, normed_next, info, result, gains, carry.loads[1:], grad_out, branch, d_gain, losses, d_tables,
        *loss_scratch, *layer_refs[2:6], *layer_refs[-2:],
    )


def last_and_loss(
    layer, normed, key_seg, query_seg, resid, w_query, w_out, w_in, gains, info, vocab, collective_id, loads
):
    seq_len, width = normed.shape
    heads_width = w_query.shape[2]
    half, blocks = seq_len // 2, seq_len // LANES
    pieces = len(loads) - 1
    return run(
        functools.partial(back_kernel, layer),
        "last_and_loss",
        [normed, key_seg, query_seg, resid, w_query, w_out, w_in, gains, info],
        layer_outs(seq_len, width, heads_width)
        + [
            jax.ShapeDtypeStruct((half, width), F32),
            jax.ShapeDtypeStruct((seq_len, width), BF16),
            jax.ShapeDtypeStruct((1, width), F32),
            jax.ShapeDtypeStruct((1, seq_len), F32),
        ]
        + [jax.ShapeDtypeStruct((width, vocab // pieces), BF16)] * pieces,
        [
            pltpu.VMEM((half, width), F32),
            pltpu.VMEM((seq_len, width), BF16),
            pltpu.VMEM((seq_len, vocab), F32),
            pltpu.VMEM((seq_len, vocab), BF16),
            pltpu.VMEM((blocks, 2, LANES, LANES), F32),
            pltpu.VMEM((width, seq_len), BF16),
            pltpu.VMEM((blocks, 8, LANES), F32),
            pltpu.VMEM((3, blocks, 8, LANES), F32),
            pltpu.VMEM((blocks, 8, LANES), F32),
            pltpu.VMEM((3, blocks, 8, LANES), F32),
        ]
        + [pltpu.SemaphoreType.DMA((3, blocks))] * 4
        + layer_scratch(seq_len, width, heads_width),
        collective_id,
        loads,
    )


def sum_ways(place, me, slow, fast, slows, group):
    near = [{NARROW: lax.rem(place + step, group)} for step in range(1, group)]
    return near, {WIDE: me + 1 - 2 * fast}


def tail_kernel(
    layers, branch, ids_all, losses, full, *refs, carry,
):
    gain_parts, refs = refs[: 2 * layers + 1], refs[2 * layers + 1 :]
    squares, refs = refs[: len(refs) - 32], refs[len(refs) - 32 :]
    tail_body(branch, ids_all, losses, full, gain_parts, squares, *refs, carry)


def tail_body(
    branch, ids_all, losses, full, gain_parts, squares,
    d_table, d_full, d_small, scalars,
    out_blocks, all_in, masked, picks, total, gains_out, gains_in, blocks, block_in, line_out, line_in,
    fast_in, sums, slow_in, near, along, across,
    wide_send, wide_recv, far_send, far_recv, near_send, near_recv,
    pair_send, pair_recv, line_send, line_recv, sum_sems,
    carry,
):
    seq_len, width = branch.shape
    quarter, half = seq_len // 4, seq_len // 2
    owners = ids_all.shape[0]
    share, vocab = d_table.shape
    sibling, partner, mine, other = group_places(seq_len)
    place = lax.axis_index(NARROW)
    side = lax.div(place, 2)
    me, slow, fast, slows = wide_places(owners)
    beside = {WIDE: me + 1 - 2 * fast}
    group = near.shape[0]
    first = place * vocab
    around = [lax.rem(me + step, owners) for step in range(owners)]
    at_quarter = pl.multiple_of(mine + side * quarter, quarter)
    across_quarter = pl.multiple_of(mine + (1 - side) * quarter, quarter)

    def along_way(step):
        return {WIDE: 2 * lax.rem(slow + step, slows) + fast}

    def wide_copy(step):
        return remote(
            out_blocks.at[around[step]], all_in.at[me, pl.ds(at_quarter, quarter)],
            wide_send.at[step], wide_recv.at[step], {WIDE: around[step]},
        )

    def far_copy(step):
        rows = all_in.at[around[step], pl.ds(at_quarter, quarter)]
        return remote(rows, rows, far_send.at[step], far_recv.at[step], partner)

    def near_copy(step):
        rows = all_in.at[around[step], pl.ds(mine, half)]
        return remote(rows, rows, near_send.at[step], near_recv.at[step], sibling)

    def block(owner):
        return full.at[:, owner]

    def pair_copy(step):
        return remote(
            block(2 * lax.rem(slow + step, slows) + 1 - fast), fast_in.at[step],
            pair_send.at[step], pair_recv.at[step], beside,
        )

    def line_copy(step):
        return remote(sums.at[step], slow_in.at[step], line_send.at[step], line_recv.at[step], along_way(step))

    def gain_near():
        return remote(gains_out, gains_in, sum_sems.at[0, 0], sum_sems.at[1, 0], sibling)

    def gain_pair(step):
        return remote(
            blocks.at[2 * lax.rem(slow + step, slows) + 1 - fast], block_in.at[step],
            sum_sems.at[2, step], sum_sems.at[3, step], beside,
        )

    def gain_line(step):
        return remote(line_out.at[step], line_in.at[step], sum_sems.at[4, step], sum_sems.at[5, step], along_way(step))

    near_ways = [{NARROW: lax.rem(place + step, group)} for step in range(1, group)]
    greet([{WIDE: device} for device in around[1:]] + near_ways)
    for step in range(slows):
        pair_copy(step).start()
    gains_out[...] = jnp.zeros(gains_out.shape, F32)
    for row, part in enumerate(gain_parts):
        gains_out[row : row + 1, :] = part[...]
    gain_near().start()
    for owner in range(owners):
        out_blocks[owner] = dot_nt(
            branch[pl.ds(at_quarter, quarter), :], feature_places(owner, width, share)
        ).astype(BF16)
    for step in range(1, owners):
        wide_copy(step).start()
    all_in[me, pl.ds(at_quarter, quarter), :] = out_blocks[me]
    carry.begin(*carry.all())
    gain_near().wait_recv()
    both = gains_out[...] + gains_in[...]
    for owner in range(owners):
        blocks[owner] = lax.dot_general(
            both, feature_places(owner, width, share).astype(F32), (((1,), (1,)), ((), ())),
            precision=lax.Precision.HIGHEST, preferred_element_type=F32,
        )
    for step in range(slows):
        gain_pair(step).start()

    def hand_on(step):
        if step:
            wide_copy(owners - step).wait_recv()
        far_copy(step).start()

    def hand_over(step):
        far_copy(step).wait_recv()
        near_copy(step).start()

    def gather_grad(step, first_turn):
        near_copy(step).wait_recv()
        row = around[step]

        def make(b, _):
            rows = rows_at(0, b, LANES)
            here = ids_all[row, pl.ds(b, 1), :] - first
            high = lax.shift_right_arithmetic(here, 7)
            rest = spread((here - high * LANES).astype(F32))
            lane = lax.broadcasted_iota(jnp.int32, (LANES, LANES), 1).astype(F32)
            picks[rows, :] = jnp.where(rest == lane, 1.0, 0.0).astype(BF16)
            turned = jnp.transpose(all_in[row, rows, :])
            for t in range(vocab // LANES):
                inside = jnp.where(high == t, 1.0, 0.0).astype(BF16)
                masked[t * LANES : (t + 1) * LANES, rows] = turned * inside
            return 0

        lax.fori_loop(0, seq_len // LANES, make, 0)
        span = 2 * TILE

        def some(i, _):
            rows = rows_at(0, i, span)
            part = dot_nn(masked[rows, :], picks[...])
            total[rows, :] = part if first_turn else total[rows, :] + part
            return 0

        lax.fori_loop(0, vocab // span, some, 0)

    order = [0] + list(range(1, owners))
    for turn in range(owners + 2):
        if turn < owners:
            hand_on(order[turn])
        if 1 <= turn < owners + 1:
            hand_over(order[turn - 1])
        if turn == 1:
            for step in list(range(1, slows)) + [0]:
                pair_copy(step).wait_recv()
                owner = 2 * lax.rem(slow + step, slows) + fast
                sums[step] = (block(owner)[...].astype(F32) + fast_in[step].astype(F32)).astype(BF16)
                if step:
                    line_copy(step).start()
            for step in list(range(1, slows)) + [0]:
                gain_pair(step).wait_recv()
                line_out[step] = blocks[2 * lax.rem(slow + step, slows) + fast] + block_in[step]
                if step:
                    gain_line(step).start()
        if turn >= 2:
            gather_grad(order[turn - 2], turn == 2)
    for t in range(vocab // LANES):
        d_table[:, t * LANES : (t + 1) * LANES] = total[t * LANES : t * LANES + share, :]
    result = sums[0].astype(F32)
    small = line_out[0]
    for step in range(1, slows):
        line_copy(step).wait_recv()
        result = result + slow_in[step].astype(F32)
        gain_line(step).wait_recv()
        small = small + line_in[step]
    d_full[...] = result
    d_small[...] = small
    carry.end(*carry.all())
    square = jnp.sum(result * result) + jnp.sum(d_table[...] * d_table[...])
    for part in squares:
        square = square + part[0, 0]
    for load in carry.loads:
        square = square + load.squares[0, 0]
    lead = (place == 0).astype(F32)
    square = square + lead * jnp.sum(small * small)
    lanes = lax.broadcasted_iota(jnp.int32, (8, LANES), 1)
    given = jnp.where(lanes == 0, square, jnp.where(lanes == 1, lead * jnp.sum(losses[...]), 0.0))

    def scalar_near(step):
        return remote(near.at[place], near.at[place], sum_sems.at[6, step], sum_sems.at[7, step], near_ways[step - 1])

    def scalar_line(step):
        return remote(along.at[slow], along.at[slow], sum_sems.at[8, step], sum_sems.at[9, step], along_way(step))

    near[place] = given
    for step in range(1, group):
        scalar_near(step).start()
    for step in range(1, group):
        scalar_near(step).wait()
    along[slow] = jnp.sum(near[...], axis=0)
    for step in range(1, slows):
        scalar_line(step).start()
    for step in range(1, slows):
        scalar_line(step).wait()
    across[0] = jnp.sum(along[...], axis=0)
    last = remote(across.at[0], across.at[1], sum_sems.at[10, 0], sum_sems.at[11, 0], beside)
    last.start()
    last.wait()
    scalars[...] = across[0] + across[1]
    gain_near().wait_send()
    for step in range(owners):
        far_copy(step).wait_send()
        near_copy(step).wait_send()
        if step:
            wide_copy(step).wait_send()
    for step in range(slows):
        pair_copy(step).wait_send()
        gain_pair(step).wait_send()
        if step:
            line_copy(step).wait_send()
            gain_line(step).wait_send()


def tail(branch, ids_all, losses, full, gain_parts, squares, share, vocab, group, collective_id, loads):
    seq_len, width = branch.shape
    owners = ids_all.shape[0]
    slows = owners // 2
    shape = full.shape[:1] + full.shape[2:]
    dma = pltpu.SemaphoreType.DMA
    small = (8, LANES)
    return run(
        functools.partial(tail_kernel, (len(gain_parts) - 1) // 2),
        "tail",
        [branch, ids_all, losses, full, *gain_parts, *squares],
        [
            jax.ShapeDtypeStruct((share, vocab), F32),
            jax.ShapeDtypeStruct(shape, F32),
            jax.ShapeDtypeStruct(small, F32),
            jax.ShapeDtypeStruct(small, F32),
        ],
        [
            pltpu.VMEM((owners, seq_len // 4, LANES), BF16),
            pltpu.VMEM((owners, seq_len, LANES), BF16),
            pltpu.VMEM((vocab, seq_len), BF16),
            pltpu.VMEM((seq_len, LANES), BF16),
            pltpu.VMEM((vocab, LANES), F32),
            pltpu.VMEM((8, width), F32),
            pltpu.VMEM((8, width), F32),
            pltpu.VMEM((owners,) + small, F32),
            pltpu.VMEM((slows,) + small, F32),
            pltpu.VMEM((slows,) + small, F32),
            pltpu.VMEM((slows,) + small, F32),
            pltpu.VMEM((slows,) + shape, BF16),
            pltpu.VMEM((slows,) + shape, BF16),
            pltpu.VMEM((slows,) + shape, BF16),
            pltpu.VMEM((group,) + small, F32),
            pltpu.VMEM((slows,) + small, F32),
            pltpu.VMEM((2,) + small, F32),
        ]
        + [dma((owners,))] * 6
        + [dma((slows,))] * 4
        + [dma((12, max(slows, group)))],
        collective_id,
        loads,
    )


PIECES = 4
TABLE, ATTN_IN, ATTN_OUT, FFN_IN, FFN_OUT = range(5)


def shares_tile(wide, narrow, noised, attn_out, ffn_in, tables):
    rows, seq_len = noised.shape
    return (
        attn_out.shape[0] == 2
        and narrow == 4
        and wide % 2 == 0
        and rows == 1
        and seq_len % (2 * CHUNKS * 128) == 0
        and attn_out.shape[1] % 16 == 0
        and attn_out.shape[1] <= LANES
        and ffn_in.shape[2] % 128 == 0
        and tables.shape[1] == attn_out.shape[1]
        and tables.shape[2] % (PIECES * TILE) == 0
    )


def per_device(wide, narrow, *arrays):
    noised, attn_out, ffn_in, tables = arrays[0], arrays[6], arrays[7], arrays[9]
    if shares_tile(wide, narrow, noised, attn_out, ffn_in, tables):
        return tiled_device(wide, *arrays)
    return general_device(*arrays)


def tiled_device(
    wide,
    noised,
    clean,
    timesteps,
    segments,
    counted,
    attn_in,
    attn_out,
    ffn_in,
    ffn_out,
    tables,
    gains,
    attn_in_mean,
    attn_out_mean,
    ffn_in_mean,
    ffn_out_mean,
    tables_mean,
    gains_mean,
    attn_in_square,
    attn_out_square,
    ffn_in_square,
    ffn_out_square,
    tables_square,
    gains_square,
):
    layers = attn_in.shape[0]
    gain_rows, gain_cols = gains.shape
    mask = counted.reshape(-1).astype(jnp.float32)
    seq_len = mask.shape[0]
    half = seq_len // 2
    core = lax.rem(lax.axis_index(NARROW), 2)
    share, vocab = tables.shape[1:]
    leads = (1, 0, 0, 0)
    four = (attn_in, attn_out, ffn_in, ffn_out)

    def joined(value, lead):
        return value.reshape(value.shape[:lead] + (-1,) + value.shape[lead + 2 :])

    step_flat = timesteps.reshape(-1)
    extra = time_features(lax.dynamic_slice(step_flat, (core * half,), (half,)))
    ids = noised.reshape(-1, LANES)
    quarter = vocab // PIECES
    windows = [(k * quarter, quarter) for k in range(PIECES)]
    key_seg, query_seg = segments.reshape(-1, 1), segments.reshape(1, -1)
    weights = (attn_in, attn_out, ffn_in, ffn_out)
    (residual, normed, gain_w, counts, ids_all, projected, mixed, middle, normed_two, result, normed_next), carried = front(
        ids, counted, gains, extra, tables, key_seg, query_seg, wide, attn_out.shape[2], 0,
        [GatherLoad(value, 0, lead, wide, place=KEPT) for value, lead in zip(weights, leads)]
        + [GatherLoad(value, 1, lead, wide) for value, lead in zip(weights[:3], leads)]
        + [SlowLoad(ffn_out, 1, 0, wide)],
    )
    token_total = counts[gain_rows, 0]
    first_w = [joined(value, lead) for value, lead in zip(carried[:4], leads)]
    query_w, output_w, expand_w = [joined(value, lead) for value, lead in zip(carried[4:7], leads)]
    kept = [(residual, normed, projected, mixed, middle, normed_two, *first_w)]
    noised_flat, clean_flat = noised.reshape(-1), clean.reshape(-1)
    info = jnp.stack(
        [noised_flat.astype(F32), clean_flat.astype(F32), step_flat.astype(F32), mask / token_total, mask]
        + [jnp.zeros_like(mask)] * 3
    )
    (projected, mixed, middle, normed_two, grad, branch, gain_final, losses, *d_last), (reduce_w,) = last_and_loss(
        1, normed_next, key_seg, query_seg, result, query_w, output_w, expand_w, gain_w, info, vocab, 1,
        [FastLoad(carried[7], 0, wide)]
        + [GatherLoad(tables, 1, 0, wide, window, place=LOCAL) for window in windows],
    )
    kept.append(
        (result, normed_next, projected, mixed, middle, normed_two, query_w, output_w, expand_w, joined(reduce_w, 0))
    )
    next_id = 2
    gain_grads = [None] * (2 * layers) + [gain_final]
    own, squares = {}, []

    def by_owner(value, lead):
        shape = value.shape
        return value.reshape(shape[:lead] + (wide, shape[lead] // wide) + shape[lead + 1 :])

    class Route:
        waiting, halfway = [], []

        def take(self, pairs, lines):
            self.now = self.waiting[:pairs], self.halfway[:lines]
            self.waiting, self.halfway = self.waiting[pairs:], self.halfway[lines:]
            return [PairLoad(by_owner(value, lead), lead, wide) for _, value, lead in self.now[0]] + [
                LineLoad(sums, wide) for _, sums in self.now[1]
            ]

        def back(self, results):
            pairs, lines = self.now
            self.halfway = self.halfway + [(key, sums) for (key, _, _), sums in zip(pairs, results)]
            for k, (key, _) in enumerate(lines):
                own[key] = results[len(pairs) + 2 * k]
                squares.append(results[len(pairs) + 2 * k + 1])

    route = Route()
    route.waiting = [((TABLE, k), piece, 0) for k, piece in enumerate(d_last)]
    for layer in reversed(range(layers)):
        residual, normed, projected, mixed, middle, normed_two, *four_w = kept[layer]
        query_w, output_w, expand_w, reduce_w = four_w
        top = layer == layers - 1
        loads = route.take(3 if top else 2, 3)
        (grad_middle, grad_attn, grad_mixed, d_red, d_in, d_out, gain_two), carried = ffn_backward(
            2 * layer + 1, grad, branch, reduce_w, expand_w, output_w,
            normed_two, middle, gain_w, mixed, next_id, loads,
        )
        route.back(carried)
        route.waiting += [((FFN_OUT, layer), d_red, 0), ((FFN_IN, layer), d_in, 0)]
        loads = route.take(1, 2)
        (grad_projected,), carried = attention_back(projected, grad_mixed, key_seg, query_seg, next_id + 1, loads)
        route.back(carried)
        route.waiting += [((ATTN_OUT, layer), d_out, 0)]
        loads = route.take(2, 2)
        (grad, branch, d_query, gain_one), carried = norm_backward(
            2 * layer, grad_projected, query_w, normed, residual, gain_w, grad_middle,
            math.sqrt(D) if layer == 0 else None, next_id + 2, loads,
        )
        route.back(carried)
        route.waiting += [((ATTN_IN, layer), d_query, 1)]
        next_id += 3
        gain_grads[2 * layer], gain_grads[2 * layer + 1] = gain_one, gain_two
    (key, last_full, _), = route.waiting
    lines = route.halfway
    (own_first, own[key], total_small, scalars), carried = tail(
        branch, ids_all, losses, by_owner(last_full, 1), gain_grads, squares, share, vocab, 4, next_id,
        [LineLoad(value, wide) for _, value in lines],
    )
    for k, (key, _) in enumerate(lines):
        own[key] = carried[2 * k]
    grad_attn_in, grad_attn_out, grad_ffn_in, grad_ffn_out = [
        jnp.stack([own[name, index] for index in range(layers)]) for name in (ATTN_IN, ATTN_OUT, FFN_IN, FFN_OUT)
    ]
    grad_tables = jnp.stack([own_first, jnp.concatenate([own[TABLE, k] for k in range(PIECES)], axis=1)])
    grad_gains = total_small[:gain_rows, :gain_cols]
    total_square, loss_sum = scalars[0, 0], scalars[0, 1]
    grad_norm = jnp.sqrt(total_square)
    factor = jnp.minimum(1.0, CLIP_NORM / (grad_norm + 1e-06))
    results = [loss_sum, token_total, grad_norm]
    for weight, gradient, first, second, decay, rate in (
        (attn_in, grad_attn_in, attn_in_mean, attn_in_square, WEIGHT_DECAY, LEARN_RATE),
        (attn_out, grad_attn_out, attn_out_mean, attn_out_square, WEIGHT_DECAY, LEARN_RATE),
        (ffn_in, grad_ffn_in, ffn_in_mean, ffn_in_square, WEIGHT_DECAY, LEARN_RATE),
        (ffn_out, grad_ffn_out, ffn_out_mean, ffn_out_square, WEIGHT_DECAY, LEARN_RATE),
        (tables, grad_tables, tables_mean, tables_square, WEIGHT_DECAY, LEARN_RATE),
        (gains, grad_gains, gains_mean, gains_square, 0.0, GAIN_RATE),
    ):
        results += adam(weight, factor * gradient, first, second, decay, rate)
    return tuple(results)


def solution(mesh):
    wide, narrow = mesh.shape[WIDE], mesh.shape[NARROW]
    placed = (
        P(WIDE, None),
        P(WIDE, None),
        P(WIDE, None),
        P(WIDE, None),
        P(WIDE, None),
        P(None, None, WIDE, NARROW),
        P(None, WIDE, NARROW),
        P(None, WIDE, NARROW),
        P(None, WIDE, NARROW),
        P(None, WIDE, NARROW),
        P(None, WIDE),
        P(None, None, WIDE, NARROW),
        P(None, WIDE, NARROW),
        P(None, WIDE, NARROW),
        P(None, WIDE, NARROW),
        P(None, WIDE, NARROW),
        P(None, WIDE),
        P(None, None, WIDE, NARROW),
        P(None, WIDE, NARROW),
        P(None, WIDE, NARROW),
        P(None, WIDE, NARROW),
        P(None, WIDE, NARROW),
        P(None, WIDE),
    )
    return jax.shard_map(
        functools.partial(per_device, wide, narrow),
        mesh=mesh,
        in_specs=placed,
        out_specs=(
            P(),
            P(),
            P(),
            P(None, None, WIDE, NARROW),
            P(None, None, WIDE, NARROW),
            P(None, None, WIDE, NARROW),
            P(None, None, WIDE, NARROW),
            P(None, WIDE, NARROW),
            P(None, WIDE, NARROW),
            P(None, WIDE, NARROW),
            P(None, WIDE, NARROW),
            P(None, WIDE, NARROW),
            P(None, WIDE, NARROW),
            P(None, WIDE, NARROW),
            P(None, WIDE, NARROW),
            P(None, WIDE, NARROW),
            P(None, WIDE, NARROW),
            P(None, WIDE, NARROW),
            P(None, WIDE, NARROW),
            P(None, WIDE, NARROW),
            P(None, WIDE, NARROW),
            P(None, WIDE, NARROW),
            P(None, WIDE, NARROW),
            P(None, WIDE),
            P(None, WIDE),
            P(None, WIDE),
            P(None, WIDE),
        ),
        check_vma=False,
    )
```

```python
import functools
import math

import jax
import jax.numpy as jnp
from jax import lax
from jax.experimental import pallas as pl
from jax.experimental.pallas import tpu as pltpu
from jax.sharding import PartitionSpec as P

D = 768
HD = 64
V = 8192
STEPS = 1000
ADAM_STEP = 10


NORM_EPS = 1e-05
LEARN_RATE = 0.05
GAIN_RATE = 0.75
FIRST_DECAY = 0.9
SECOND_DECAY = 0.999
ADAM_EPS = 1e-08
WEIGHT_DECAY = 0.01
CLIP_NORM = 0.005
WIDE, NARROW = "wide", "narrow"


def add_heads(partial_value):
    return lax.psum(partial_value, NARROW)


def back_heads(partial_value):
    return lax.psum(partial_value, NARROW)


def rms_forward(value, gain):
    scale_row = lax.rsqrt(jnp.mean(value * value, axis=-1, keepdims=True) + NORM_EPS)
    return (value * scale_row * gain, scale_row)


def rms_backward(grad, value, scale_row, gain):
    unit = value * scale_row
    scaled = grad * gain
    back = scale_row * (scaled - unit * jnp.mean(scaled * unit, axis=-1, keepdims=True))
    return (back, jnp.sum(grad * unit, axis=0))


def time_features(timestep_row):
    half_width = D // 2
    rates = jnp.exp(-math.log(10000.0) * jnp.arange(half_width, dtype=jnp.float32) / half_width)
    angles = timestep_row.astype(jnp.float32)[:, None] * rates[None, :]
    return jnp.concatenate([jnp.sin(angles), jnp.cos(angles)], axis=1)


def masked_scores(queries, key_rows, segment):
    scores = jnp.einsum(
        "qhd,khd->hqk", queries, key_rows, preferred_element_type=jnp.float32
    ) * HD ** (-0.5)
    return jnp.where((segment[:, None] == segment[None, :])[None], scores, -1e30)


def attend(entry):
    queries, key_rows, values, segment = entry
    scores = masked_scores(queries, key_rows, segment)
    row_top = jnp.max(scores, axis=-1, keepdims=True)
    log_total = row_top + jnp.log(jnp.sum(jnp.exp(scores - row_top), axis=-1, keepdims=True))
    probs = jnp.exp(scores - log_total).astype(jnp.bfloat16)
    mixed = jnp.einsum("hqk,khd->qhd", probs, values, preferred_element_type=jnp.float32)
    return (mixed.astype(jnp.bfloat16), log_total)


def attend_back(entry):
    queries, key_rows, values, segment, log_total, grad_mixed = entry
    probs = jnp.exp(masked_scores(queries, key_rows, segment) - log_total)
    grad_probs = jnp.einsum("qhd,khd->hqk", grad_mixed, values, preferred_element_type=jnp.float32)
    grad_scores = (
        probs * (grad_probs - jnp.sum(probs * grad_probs, axis=-1, keepdims=True))
    ).astype(jnp.bfloat16)
    grad_query = jnp.einsum(
        "hqk,khd->qhd", grad_scores, key_rows, preferred_element_type=jnp.float32
    ) * HD ** (-0.5)
    grad_key = jnp.einsum(
        "hqk,qhd->khd", grad_scores, queries, preferred_element_type=jnp.float32
    ) * HD ** (-0.5)
    grad_value = jnp.einsum(
        "hqk,qhd->khd", probs.astype(jnp.bfloat16), grad_mixed, preferred_element_type=jnp.float32
    )
    return (grad_query, grad_key, grad_value)


def layer_forward(residual, segments, query_w, output_w, expand_w, reduce_w, gain_attn, gain_ffn):
    seq_count, seq_len = segments.shape
    normed, scale_one = rms_forward(residual, gain_attn)
    normed = normed.astype(jnp.bfloat16)
    projected = jnp.einsum(
        "sd,cde->cse", normed, query_w, preferred_element_type=jnp.float32
    ).astype(jnp.bfloat16)
    heads = projected.reshape(3, seq_count, seq_len, -1, HD)
    mixed, log_total = lax.map(attend, (heads[0], heads[1], heads[2], segments))
    mixed = mixed.reshape(seq_count * seq_len, -1)
    middle = residual + add_heads(
        jnp.einsum("se,de->sd", mixed, output_w, preferred_element_type=jnp.float32)
    )
    normed_two, scale_two = rms_forward(middle, gain_ffn)
    normed_two = normed_two.astype(jnp.bfloat16)
    before = jnp.dot(normed_two, expand_w, preferred_element_type=jnp.float32)
    after = jax.nn.gelu(before).astype(jnp.bfloat16)
    result = middle + add_heads(
        jnp.einsum("sf,df->sd", after, reduce_w, preferred_element_type=jnp.float32)
    )
    return (
        result,
        (
            residual,
            scale_one,
            normed,
            projected,
            log_total,
            mixed,
            middle,
            scale_two,
            normed_two,
            before,
            after,
        ),
    )


def layer_backward(
    grad, kept, segments, query_w, output_w, expand_w, reduce_w, gain_attn, gain_ffn
):
    (
        residual,
        scale_one,
        normed,
        projected,
        log_total,
        mixed,
        middle,
        scale_two,
        normed_two,
        before,
        after,
    ) = kept
    seq_count, seq_len = segments.shape
    grad_branch = grad.astype(jnp.bfloat16)
    grad_after = jnp.dot(grad_branch, reduce_w, preferred_element_type=jnp.float32)
    grad_reduce = jnp.einsum("sd,sf->df", grad_branch, after, preferred_element_type=jnp.float32)
    _, gelu_pull = jax.vjp(jax.nn.gelu, before)
    grad_before = gelu_pull(grad_after)[0].astype(jnp.bfloat16)
    grad_expand = jnp.einsum(
        "sd,sf->df", normed_two, grad_before, preferred_element_type=jnp.float32
    )
    grad_normed_two = back_heads(
        jnp.einsum("sf,df->sd", grad_before, expand_w, preferred_element_type=jnp.float32)
    )
    grad_middle, grad_gain_ffn = rms_backward(grad_normed_two, middle, scale_two, gain_ffn)
    grad_middle = grad_middle + grad
    grad_attn = grad_middle.astype(jnp.bfloat16)
    grad_mixed = jnp.dot(grad_attn, output_w, preferred_element_type=jnp.float32).astype(
        jnp.bfloat16
    )
    grad_output = jnp.einsum("sd,se->de", grad_attn, mixed, preferred_element_type=jnp.float32)
    heads = projected.reshape(3, seq_count, seq_len, -1, HD)
    grad_query, grad_key, grad_value = lax.map(
        attend_back,
        (
            heads[0],
            heads[1],
            heads[2],
            segments,
            log_total,
            grad_mixed.reshape(seq_count, seq_len, -1, HD),
        ),
    )
    grad_projected = (
        jnp.stack([grad_query, grad_key, grad_value])
        .reshape(3, seq_count * seq_len, -1)
        .astype(jnp.bfloat16)
    )
    grad_query_w = jnp.einsum(
        "sd,cse->cde", normed, grad_projected, preferred_element_type=jnp.float32
    )
    grad_normed = back_heads(
        jnp.einsum("cse,cde->sd", grad_projected, query_w, preferred_element_type=jnp.float32)
    )
    grad_input, grad_gain_attn = rms_backward(grad_normed, residual, scale_one, gain_attn)
    return (
        grad_input + grad_middle,
        (
            grad_query_w,
            grad_output,
            grad_expand,
            grad_reduce,
            jnp.stack([grad_gain_attn, grad_gain_ffn]),
        ),
    )


def adam(weight, grad, first, second, decay, rate):
    first_new = FIRST_DECAY * first + (1.0 - FIRST_DECAY) * grad
    second_new = SECOND_DECAY * second + (1.0 - SECOND_DECAY) * grad * grad
    first_hat = first_new / (1.0 - FIRST_DECAY**ADAM_STEP)
    second_hat = second_new / (1.0 - SECOND_DECAY**ADAM_STEP)
    weight_new = weight - rate * (first_hat / (jnp.sqrt(second_hat) + ADAM_EPS) + decay * weight)
    return (weight_new, first_new, second_new, weight_new.astype(jnp.bfloat16))


def general_device(
    noised,
    clean,
    timesteps,
    segments,
    counted,
    attn_in,
    attn_out,
    ffn_in,
    ffn_out,
    tables,
    gains,
    attn_in_mean,
    attn_out_mean,
    ffn_in_mean,
    ffn_out_mean,
    tables_mean,
    gains_mean,
    attn_in_square,
    attn_out_square,
    ffn_in_square,
    ffn_out_square,
    tables_square,
    gains_square,
):
    layers = attn_in.shape[0]
    mask = counted.reshape(-1).astype(jnp.float32)
    token_total = lax.psum(jnp.sum(mask), WIDE)
    query_w, output_w, expand_w, reduce_w, table_w, gain_low = (
        lax.all_gather(attn_in.astype(jnp.bfloat16), WIDE, axis=2, tiled=True),
        lax.all_gather(attn_out.astype(jnp.bfloat16), WIDE, axis=1, tiled=True),
        lax.all_gather(ffn_in.astype(jnp.bfloat16), WIDE, axis=1, tiled=True),
        lax.all_gather(ffn_out.astype(jnp.bfloat16), WIDE, axis=1, tiled=True),
        lax.all_gather(tables.astype(jnp.bfloat16), WIDE, axis=1, tiled=True),
        lax.all_gather(gains.astype(jnp.bfloat16), WIDE, axis=1, tiled=True),
    )
    gain_w = gain_low.astype(jnp.float32)
    noised_flat = noised.reshape(-1)
    clean_flat = clean.reshape(-1)
    step_flat = timesteps.reshape(-1)
    vocab_local = table_w.shape[2]
    vocab_ids = lax.axis_index(NARROW) * vocab_local + jnp.arange(vocab_local, dtype=jnp.int32)
    picks = (noised_flat[:, None] == vocab_ids[None, :]).astype(jnp.bfloat16)
    looked = add_heads(
        jnp.einsum("sv,dv->sd", picks, table_w[0], preferred_element_type=jnp.float32)
    )
    residual = math.sqrt(D) * looked + time_features(step_flat)
    kept_layers = []
    for layer_index in range(layers):
        residual, kept = layer_forward(
            residual,
            segments,
            query_w[layer_index],
            output_w[layer_index],
            expand_w[layer_index],
            reduce_w[layer_index],
            gain_w[2 * layer_index],
            gain_w[2 * layer_index + 1],
        )
        kept_layers.append(kept)
    final, scale_final = rms_forward(residual, gain_w[2 * layers])
    final_low = final.astype(jnp.bfloat16)
    logits = jnp.dot(final_low, table_w[1], preferred_element_type=jnp.float32)
    local_top = jnp.max(logits, axis=1)
    row_top = lax.pmax(local_top, NARROW)
    row_total = lax.psum(jnp.sum(jnp.exp(logits - row_top[:, None]), axis=1), NARROW)
    log_probs = logits - (row_top + jnp.log(row_total))[:, None]
    probs = jnp.exp(log_probs)
    clamped = jnp.maximum(step_flat, 2).astype(jnp.float32)[:, None]
    beta = 1.0 / (STEPS - clamped + 1.0)
    retain = (STEPS - clamped + 1.0) / STEPS
    spread = (clamped - 1.0) / (STEPS * V)
    at_noised = (vocab_ids[None, :] == noised_flat[:, None]).astype(jnp.float32)
    at_clean = (vocab_ids[None, :] == clean_flat[:, None]).astype(jnp.float32)
    forward_fac = beta / V + (1.0 - beta) * at_noised
    backward_fac = retain * at_clean + spread
    joint = forward_fac * backward_fac
    marginal = retain * probs + spread
    joint_total, cross, model_total, weighted, aligned, clean_logp = lax.psum(
        (
            jnp.sum(joint, axis=1),
            jnp.sum(joint * (jnp.log(backward_fac) - jnp.log(marginal)), axis=1),
            jnp.sum(forward_fac * marginal, axis=1),
            jnp.sum(probs * joint / marginal, axis=1),
            jnp.sum(forward_fac * probs, axis=1),
            jnp.sum(at_clean * log_probs, axis=1),
        ),
        NARROW,
    )
    divergence = cross / joint_total - jnp.log(joint_total) + jnp.log(model_total)
    first_step = step_flat == 1
    losses = jnp.where(first_step, -clean_logp, divergence)
    pull = retain * (
        -(joint / joint_total[:, None]) / marginal + forward_fac / model_total[:, None]
    )
    centre = retain[:, 0] * (-weighted / joint_total + aligned / model_total)
    grad_kl = probs * (pull - centre[:, None])
    grad_recon = probs - at_clean
    grad_logits = (
        (mask / token_total)[:, None] * jnp.where(first_step[:, None], grad_recon, grad_kl)
    ).astype(jnp.bfloat16)
    grad_table_out = jnp.einsum(
        "sd,sv->dv", final_low, grad_logits, preferred_element_type=jnp.float32
    )
    grad_final = back_heads(
        jnp.einsum("sv,dv->sd", grad_logits, table_w[1], preferred_element_type=jnp.float32)
    )
    grad_x, grad_gain_final = rms_backward(grad_final, residual, scale_final, gain_w[2 * layers])
    layer_grads = [None] * layers
    for layer_index in reversed(range(layers)):
        grad_x, produced = layer_backward(
            grad_x,
            kept_layers[layer_index],
            segments,
            query_w[layer_index],
            output_w[layer_index],
            expand_w[layer_index],
            reduce_w[layer_index],
            gain_w[2 * layer_index],
            gain_w[2 * layer_index + 1],
        )
        layer_grads[layer_index] = produced
    grad_look = (math.sqrt(D) * grad_x).astype(jnp.bfloat16)
    grad_table_in = jnp.einsum("sd,sv->dv", grad_look, picks, preferred_element_type=jnp.float32)
    stacked = [jnp.stack([entry[which] for entry in layer_grads]) for which in range(5)]
    gain_layers = stacked[4].reshape(2 * layers, -1)
    grad_tables_all = jnp.stack([grad_table_in, grad_table_out])
    grad_attn_in, grad_attn_out, grad_ffn_in, grad_ffn_out, grad_tables, grad_gains = (
        lax.psum_scatter(stacked[0], WIDE, scatter_dimension=2, tiled=True),
        lax.psum_scatter(stacked[1], WIDE, scatter_dimension=1, tiled=True),
        lax.psum_scatter(stacked[2], WIDE, scatter_dimension=1, tiled=True),
        lax.psum_scatter(stacked[3], WIDE, scatter_dimension=1, tiled=True),
        lax.psum_scatter(grad_tables_all, WIDE, scatter_dimension=1, tiled=True),
        lax.psum_scatter(
            jnp.concatenate([gain_layers, grad_gain_final[None, :]], axis=0),
            WIDE,
            scatter_dimension=1,
            tiled=True,
        ),
    )
    narrow_first = (lax.axis_index(NARROW) == 0).astype(jnp.float32)
    squares = (
        jnp.sum(grad_attn_in * grad_attn_in)
        + jnp.sum(grad_attn_out * grad_attn_out)
        + jnp.sum(grad_ffn_in * grad_ffn_in)
        + jnp.sum(grad_ffn_out * grad_ffn_out)
        + jnp.sum(grad_tables * grad_tables)
        + narrow_first * jnp.sum(grad_gains * grad_gains)
    )
    squares, loss_sum = lax.psum(
        (squares, narrow_first * jnp.sum(mask * losses)), (WIDE, NARROW)
    )
    grad_norm = jnp.sqrt(squares)
    factor = jnp.minimum(1.0, CLIP_NORM / (grad_norm + 1e-06))
    attn_in_next, attn_in_mean_next, attn_in_square_next, attn_in_copy = adam(
        attn_in, factor * grad_attn_in, attn_in_mean, attn_in_square, WEIGHT_DECAY, LEARN_RATE
    )
    attn_out_next, attn_out_mean_next, attn_out_square_next, attn_out_copy = adam(
        attn_out, factor * grad_attn_out, attn_out_mean, attn_out_square, WEIGHT_DECAY, LEARN_RATE
    )
    ffn_in_next, ffn_in_mean_next, ffn_in_square_next, ffn_in_copy = adam(
        ffn_in, factor * grad_ffn_in, ffn_in_mean, ffn_in_square, WEIGHT_DECAY, LEARN_RATE
    )
    ffn_out_next, ffn_out_mean_next, ffn_out_square_next, ffn_out_copy = adam(
        ffn_out, factor * grad_ffn_out, ffn_out_mean, ffn_out_square, WEIGHT_DECAY, LEARN_RATE
    )
    tables_next, tables_mean_next, tables_square_next, tables_copy = adam(
        tables, factor * grad_tables, tables_mean, tables_square, WEIGHT_DECAY, LEARN_RATE
    )
    gains_next, gains_mean_next, gains_square_next, gains_copy = adam(
        gains, factor * grad_gains, gains_mean, gains_square, 0.0, GAIN_RATE
    )
    return (
        loss_sum,
        token_total,
        grad_norm,
        attn_in_next,
        attn_in_mean_next,
        attn_in_square_next,
        attn_in_copy,
        attn_out_next,
        attn_out_mean_next,
        attn_out_square_next,
        attn_out_copy,
        ffn_in_next,
        ffn_in_mean_next,
        ffn_in_square_next,
        ffn_in_copy,
        ffn_out_next,
        ffn_out_mean_next,
        ffn_out_square_next,
        ffn_out_copy,
        tables_next,
        tables_mean_next,
        tables_square_next,
        tables_copy,
        gains_next,
        gains_mean_next,
        gains_square_next,
        gains_copy,
    )


MESH = pl.DeviceIdType.MESH
SLOW, FAST = 1, 2
HBM, KEPT, LOCAL = 1, 2, 3
F32 = jnp.float32
BF16 = jnp.bfloat16
CHUNKS = 4
VMEM_LIMIT = 61 * 1024 * 1024
FORWARD_KIND = BF16
BACKWARD_KIND = BF16


def whole_vmem():
    return pl.BlockSpec(memory_space=pltpu.VMEM)


def dot_nn(a, b):
    return lax.dot_general(a, b, (((1,), (0,)), ((), ())), preferred_element_type=F32)


def dot_nt(a, b):
    return lax.dot_general(a, b, (((1,), (1,)), ((), ())), preferred_element_type=F32)


def remote(src, dst, send_sem, recv_sem, device):
    return pltpu.make_async_remote_copy(
        src_ref=src,
        dst_ref=dst,
        send_sem=send_sem,
        recv_sem=recv_sem,
        device_id=device,
        device_id_type=MESH,
    )


def greet(devices):
    barrier = pltpu.get_barrier_semaphore()
    for device in devices:
        pl.semaphore_signal(barrier, inc=1, device_id=device, device_id_type=MESH)
    pl.semaphore_wait(barrier, len(devices))


def group_places(seq_len):
    me = lax.axis_index(NARROW)
    core = lax.rem(me, 2)
    half = seq_len // 2
    mine = pl.multiple_of(core * half, half)
    other = pl.multiple_of((1 - core) * half, half)
    return ({NARROW: me + 1 - 2 * core}, {NARROW: lax.rem(me + 2, 4)}, mine, other)


class Exchange:
    def __init__(self, refs, sems, base, sibling, partner):
        self.near_out, self.near_in, self.far_out, self.far_in = refs
        self.send, self.recv = sems
        self.base, self.sibling, self.partner = base, sibling, partner

    def near(self, j):
        return remote(
            self.near_out.at[j],
            self.near_in.at[j],
            self.send.at[self.base, j],
            self.recv.at[self.base, j],
            self.sibling,
        )

    def far(self, j):
        return remote(
            self.far_out.at[j],
            self.far_in.at[j],
            self.send.at[self.base + 1, j],
            self.recv.at[self.base + 1, j],
            self.partner,
        )

    def give(self, j, value):
        self.near_out[j] = value
        self.near(j).start()

    def pass_on(self, j, value):
        self.near(j).wait_recv()
        self.far_out[j] = (value + self.near_in[j]).astype(self.far_out.dtype)
        self.far(j).start()

    def take(self, j):
        self.far(j).wait_recv()
        return self.far_out[j].astype(F32) + self.far_in[j].astype(F32)

    def close(self):
        for j in range(CHUNKS):
            self.near(j).wait_send()
            self.far(j).wait_send()

    @staticmethod
    def scratch(chunk, width, kind):
        return [
            pltpu.VMEM((CHUNKS, chunk, width), F32),
            pltpu.VMEM((CHUNKS, chunk, width), F32),
            pltpu.VMEM((CHUNKS, chunk, width), kind),
            pltpu.VMEM((CHUNKS, chunk, width), kind),
        ]


class Share:
    def __init__(self, ref, sems, base, sibling, mine, chunk):
        self.ref, self.base, self.sibling, self.mine, self.chunk = ref, base, sibling, mine, chunk
        self.send, self.recv = sems

    def piece(self, j):
        rows = self.ref.at[pl.ds(pl.multiple_of(self.mine + j * self.chunk, self.chunk), self.chunk)]
        return remote(rows, rows, self.send.at[self.base, j], self.recv.at[self.base, j], self.sibling)

    def put(self, j, value):
        self.ref[pl.ds(pl.multiple_of(self.mine + j * self.chunk, self.chunk), self.chunk), :] = value
        self.piece(j).start()

    def arrived(self, j):
        self.piece(j).wait_recv()

    def close(self):
        for j in range(CHUNKS):
            self.piece(j).wait_send()


def wide_places(count):
    me = lax.axis_index(WIDE)
    fast = lax.rem(me, 2)
    slow = me // 2
    return (me, slow, fast, count // 2)


class Carry:
    def __init__(self, loads):
        self.loads = loads

    def peers(self):
        ways = []
        for load in self.loads:
            ways += [way for way in load.ways if way not in ways]
        me, slow, fast, slows = wide_places(self.loads[0].count) if self.loads else (0, 0, 0, 0)
        found = []
        if SLOW in ways:
            found += [{WIDE: 2 * lax.rem(slow + step, slows) + fast} for step in range(1, slows)]
        if FAST in ways:
            found.append({WIDE: me + 1 - 2 * fast})
        return found

    def begin(self, *which):
        for k in which:
            self.loads[k].start()

    def hand_on(self, *which):
        for k in which:
            self.loads[k].relay()

    def end(self, *which):
        for k in which:
            self.loads[k].finish()

    def all(self):
        return range(len(self.loads))


def part_of(weights, index, window):
    shape = weights.shape[1:]
    return shape if window is None else shape[:-1] + (window[1],)


class SlowLoad:
    ways = (SLOW,)

    def __init__(self, weights, index, lead, count, window=None):
        self.index, self.lead, self.count, self.window = index, lead, count, window
        shape, slows = part_of(weights, index, window), count // 2
        self.operands, self.in_specs = [weights], [whole_vmem()]
        self.outs = [jax.ShapeDtypeStruct((slows,) + shape, BF16)]
        self.out_specs = [pl.BlockSpec(memory_space=pl.ANY)]
        self.scratch = [pltpu.VMEM(shape, BF16), pltpu.SemaphoreType.DMA] + [pltpu.SemaphoreType.DMA((slows,))] * 2

    def bind(self, given, out, scratch):
        self.shard, self.out = given[0], out[0]
        self.low, self.local, self.send, self.recv = scratch
        self.me, self.slow, self.fast, self.slows = wide_places(self.count)

    def cast(self):
        if self.window is None:
            self.low[...] = self.shard[self.index].astype(BF16)
        else:
            self.low[...] = self.shard[self.index, :, self.window[0] : self.window[0] + self.window[1]].astype(BF16)

    def target(self):
        return self.out.at[self.slow]

    def slow_copy(self, step):
        return remote(
            self.low, self.target(), self.send.at[step], self.recv.at[step],
            {WIDE: 2 * lax.rem(self.slow + step, self.slows) + self.fast},
        )

    def own_copy(self):
        return pltpu.make_async_copy(self.low, self.target(), self.local)

    def start(self):
        self.cast()
        for step in range(1, self.slows):
            self.slow_copy(step).start()
        self.own_copy().start()

    def finish(self):
        for step in range(1, self.slows):
            self.slow_copy(step).wait()
        self.own_copy().wait()


class FastLoad:
    ways = (FAST,)

    def __init__(self, blocks, lead, count):
        self.lead, self.count = lead, count
        shape, slows = blocks.shape[1:], count // 2
        self.operands, self.in_specs = [blocks], [pl.BlockSpec(memory_space=pl.ANY)]
        self.outs = [jax.ShapeDtypeStruct(shape[:lead] + (count,) + shape[lead:], BF16)]
        self.out_specs = [whole_vmem()]
        self.scratch = [pltpu.SemaphoreType.DMA((slows,))] * 3

    def value(self):
        return self.out[...].reshape((-1, self.out.shape[-1]))

    def bind(self, given, out, scratch):
        self.blocks, self.out = given[0], out[0]
        self.local, self.send, self.recv = scratch
        self.me, self.slow, self.fast, self.slows = wide_places(self.count)

    def copies(self, step):
        target = self.out.at[(slice(None),) * self.lead + (2 * step + self.fast,)]
        return (
            remote(
                self.blocks.at[step], target, self.send.at[step], self.recv.at[step],
                {WIDE: self.me + 1 - 2 * self.fast},
            ),
            pltpu.make_async_copy(self.blocks.at[step], target, self.local.at[step]),
        )

    def start(self):
        for step in range(self.slows):
            for copy in self.copies(step):
                copy.start()

    def finish(self):
        for step in range(self.slows):
            for copy in self.copies(step):
                copy.wait()


class GatherLoad(SlowLoad):
    ways = (SLOW, FAST)

    def __init__(self, weights, index, lead, count, window=None, place=HBM):
        super().__init__(weights, index, lead, count, window)
        shape, slows = part_of(weights, index, window), count // 2
        whole = shape[:lead] + (count,) + shape[lead:]
        self.outs = [jax.ShapeDtypeStruct(whole, BF16)]
        self.scratch = self.scratch + [pltpu.SemaphoreType.DMA((slows,))] * 2
        if place == KEPT:
            self.out_specs = [whole_vmem()]
        self.local_out = place == LOCAL
        if self.local_out:
            self.outs, self.out_specs = [], []
            self.scratch = self.scratch + [pltpu.VMEM(whole, BF16)]

    def bind(self, given, out, scratch):
        if self.local_out:
            out, scratch = scratch[-1:], scratch[:-1]
        super().bind(given, out, scratch[:-2])
        self.fast_send, self.fast_recv = scratch[-2:]

    def value(self, *index):
        found = self.out[index] if index else self.out[...]
        return found.reshape((-1, found.shape[-1]))

    def at(self, owner):
        return self.out.at[(slice(None),) * self.lead + (owner,)]

    def target(self):
        return self.at(self.me)

    def fast_copy(self, step):
        block = self.at(2 * lax.rem(self.slow + self.slows - step, self.slows) + self.fast)
        return remote(
            self.low if step == 0 else block, block, self.fast_send.at[step], self.fast_recv.at[step],
            {WIDE: self.me + 1 - 2 * self.fast},
        )

    def start(self):
        super().start()
        self.fast_copy(0).start()

    def relay(self):
        for step in range(1, self.slows):
            self.slow_copy(step).wait_recv()
            self.fast_copy(step).start()

    def finish(self):
        for step in range(self.slows):
            self.fast_copy(step).wait()
            if step:
                self.slow_copy(step).wait_send()
        self.own_copy().wait()


class PairLoad:
    ways = (FAST,)

    def __init__(self, full, lead, inside=False):
        self.lead, self.count, self.inside = lead, full.shape[lead], inside
        self.shape, self.slows = full.shape[:lead] + full.shape[lead + 1 :], self.count // 2
        self.operands, self.in_specs = ([], []) if inside else ([full], [whole_vmem()])
        self.outs, self.out_specs = [jax.ShapeDtypeStruct((self.slows,) + self.shape, BF16)], [whole_vmem()]
        self.scratch = [pltpu.VMEM((self.slows,) + self.shape, BF16)] + [pltpu.SemaphoreType.DMA((self.slows,))] * 2

    def bind(self, given, out, scratch):
        self.full = None if self.inside else given[0]
        self.out = out[0]
        self.came, self.send, self.recv = scratch
        self.me, self.slow, self.fast, self.slows = wide_places(self.count)

    def block(self, step, fast):
        owner = 2 * lax.rem(self.slow + step, self.slows) + fast
        return self.full.at[(slice(None),) * self.lead + (owner,)]

    def copy(self, step):
        return remote(
            self.block(step, 1 - self.fast), self.came.at[step], self.send.at[step], self.recv.at[step],
            {WIDE: self.me + 1 - 2 * self.fast},
        )

    def start(self):
        for step in list(range(1, self.slows)) + [0]:
            self.copy(step).start()

    def finish(self):
        for step in range(self.slows):
            self.copy(step).wait()
            total = self.block(step, self.fast)[...].astype(F32) + self.came[step].astype(F32)
            self.out[step] = total.astype(BF16)


class ReduceLoad(PairLoad):
    ways = (SLOW, FAST)

    def __init__(self, full, lead, inside=False):
        super().__init__(full, lead, inside)
        self.outs = [jax.ShapeDtypeStruct(self.shape, F32), jax.ShapeDtypeStruct((8, 128), F32)]
        self.out_specs = [whole_vmem()] * 2
        self.scratch = (
            self.scratch
            + [pltpu.VMEM((self.slows - 1,) + self.shape, BF16)]
            + [pltpu.SemaphoreType.DMA((self.slows,))] * 2
        )

    def bind(self, given, out, scratch):
        super().bind(given, out[:1], scratch[:3])
        self.squares = out[1]
        self.landed, self.line_send, self.line_recv = scratch[3:]

    def line_copy(self, step):
        return remote(
            self.came.at[step], self.landed.at[step - 1], self.line_send.at[step], self.line_recv.at[step],
            {WIDE: 2 * lax.rem(self.slow + step, self.slows) + self.fast},
        )

    def relay(self):
        for step in list(range(1, self.slows)) + [0]:
            self.copy(step).wait()
            total = self.block(step, self.fast)[...].astype(F32) + self.came[step].astype(F32)
            self.came[step] = total.astype(BF16)
            if step:
                self.line_copy(step).start()

    def finish(self):
        total = self.came[0].astype(F32)
        for step in range(1, self.slows):
            self.line_copy(step).wait()
            total = total + self.landed[step - 1].astype(F32)
        self.out[...] = total
        self.squares[...] = jnp.full(self.squares.shape, jnp.sum(total * total), F32)


class LineLoad:
    ways = (SLOW,)

    def __init__(self, sums, count):
        self.count = count
        slows = count // 2
        self.operands, self.in_specs = [sums], [whole_vmem()]
        self.outs = [jax.ShapeDtypeStruct(sums.shape[1:], F32), jax.ShapeDtypeStruct((8, 128), F32)]
        self.out_specs = [whole_vmem()] * 2
        self.scratch = [pltpu.VMEM(sums.shape, BF16)] + [pltpu.SemaphoreType.DMA((slows,))] * 2

    def bind(self, given, out, scratch):
        self.sums, (self.out, self.squares) = given[0], out
        self.came, self.send, self.recv = scratch
        self.me, self.slow, self.fast, self.slows = wide_places(self.count)

    def copy(self, step):
        return remote(
            self.sums.at[step], self.came.at[step], self.send.at[step], self.recv.at[step],
            {WIDE: 2 * lax.rem(self.slow + step, self.slows) + self.fast},
        )

    def start(self):
        for step in range(1, self.slows):
            self.copy(step).start()

    def finish(self):
        total = self.sums[0].astype(F32)
        for step in range(1, self.slows):
            self.copy(step).wait()
            total = total + self.came[step].astype(F32)
        self.out[...] = total
        self.squares[...] = jnp.full(self.squares.shape, jnp.sum(total * total), F32)


def run(body, name, operands, outs, scratch, collective_id=None, loads=(), far_operands=()):
    given, taken = list(operands), []
    in_specs = [
        pl.BlockSpec(memory_space=pl.ANY) if k in far_operands else whole_vmem() for k in range(len(operands))
    ]
    for load in loads:
        places = []
        for operand, spec in zip(load.operands, load.in_specs):
            known = [k for k, other in enumerate(given) if other is operand]
            if not known:
                known = [len(given)]
                given.append(operand)
                in_specs.append(spec)
            places.append(known[0])
        taken.append(places)
    counts = [len(given), len(outs)] + [len(load.outs) for load in loads]
    counts += [len(scratch)] + [len(load.scratch) for load in loads]
    parts = 1 + len(loads)

    def kernel(*refs):
        groups, place = [], 0
        for count in counts:
            groups.append(refs[place : place + count])
            place += count
        for k, load in enumerate(loads):
            load.bind([groups[0][p] for p in taken[k]], groups[2 + k], groups[2 + parts + k])
        body(*groups[0][: len(operands)], *groups[1], *groups[1 + parts], carry=Carry(list(loads)))

    results = pl.pallas_call(
        kernel,
        out_shape=tuple(outs) + tuple(out for load in loads for out in load.outs),
        in_specs=in_specs,
        out_specs=(whole_vmem(),) * len(outs) + tuple(spec for load in loads for spec in load.out_specs),
        scratch_shapes=list(scratch) + [s for load in loads for s in load.scratch],
        compiler_params=pltpu.CompilerParams(
            collective_id=collective_id,
            has_side_effects=collective_id is not None,
            vmem_limit_bytes=VMEM_LIMIT,
        ),
        name=name,
    )(*given)
    return results[: len(outs)], results[len(outs) :]


def sems(kinds):
    return [pltpu.SemaphoreType.DMA((kinds, CHUNKS)), pltpu.SemaphoreType.DMA((kinds, CHUNKS))]


def norm_of(value, gain):
    scale = lax.rsqrt(jnp.mean(value * value, axis=-1, keepdims=True) + NORM_EPS)
    return value * scale * gain


def norm_back(grad, value, gain):
    scale = lax.rsqrt(jnp.mean(value * value, axis=-1, keepdims=True) + NORM_EPS)
    unit = value * scale
    scaled = grad * gain
    back = scale * (scaled - unit * jnp.mean(scaled * unit, axis=-1, keepdims=True))
    return (back, jnp.sum(grad * unit, axis=0, keepdims=True))


GELU_A = math.sqrt(2.0 / math.pi)
GELU_B = 0.044715


def gelu_of(x):
    return 0.5 * x * (1.0 + jnp.tanh(GELU_A * (x + GELU_B * (x * x * x))))


def gelu_slope(x):
    square = x * x
    t = jnp.tanh(GELU_A * (x + GELU_B * (x * square)))
    return 0.5 * (1.0 + t) + 0.5 * x * (1.0 - t * t) * (GELU_A * (1.0 + 3.0 * GELU_B * square))


def rows_at(start, j, chunk):
    return pl.ds(pl.multiple_of(start + j * chunk, chunk), chunk)


LANES = 128


def spread(row):
    return jnp.transpose(jnp.broadcast_to(row, (LANES, LANES)))


def feature_places(owner, width, share):
    lane = lax.broadcasted_iota(jnp.int32, (LANES, width), 0)
    feature = lax.broadcasted_iota(jnp.int32, (LANES, width), 1)
    return ((feature == lane + owner * share) & (lane < share)).astype(F32).astype(BF16)


def token_picks(ids, vocab, first):
    here = spread(ids.astype(F32) - first.astype(F32))
    lane = lax.broadcasted_iota(jnp.int32, (LANES, LANES), 1).astype(F32)
    return [jnp.where(here == lane + float(t * LANES), 1.0, 0.0).astype(BF16) for t in range(vocab // LANES)]


def embed_part(
    ids, counted, gains, extra, table,
    resid, normed, gain_all, count_all, ids_all,
    low, picks, small, near_out, near_in, own, far_out, far_in, wide_out, wide_in, part_out, part_in,
    id_send, id_recv, small_send, small_recv, near_send, near_recv, far_send, far_recv, wide_send, wide_recv,
    part_send, part_recv, send, recv, carry,
):
    seq_len, width = normed.shape
    chunk = seq_len // 2 // CHUNKS
    quarter = seq_len // 4
    share, vocab = table.shape[1:]
    owners = ids_all.shape[0]
    id_rows = ids.shape[0]
    sibling, partner, mine, other = group_places(seq_len)
    place = lax.axis_index(NARROW)
    side = lax.div(place, 2)
    me = lax.axis_index(WIDE)
    first = place * vocab
    around = [lax.rem(me + step, owners) for step in range(owners)]

    def id_copy(step):
        return remote(ids_all.at[me], ids_all.at[me], id_send.at[step], id_recv.at[step], {WIDE: around[step]})

    def small_copy(step):
        return remote(small.at[me], small.at[me], small_send.at[step], small_recv.at[step], {WIDE: around[step]})

    def near_copy(step):
        return remote(near_out.at[step], near_in.at[step], near_send.at[step], near_recv.at[step], sibling)

    def far_copy(step):
        return remote(far_out.at[step], far_in.at[step], far_send.at[step], far_recv.at[step], partner)

    def wide_copy(step):
        return remote(wide_out.at[step], wide_in.at[me], wide_send.at[step], wide_recv.at[step], {WIDE: around[step]})

    def part_copy(piece):
        rows = pl.ds(piece * LANES, LANES)
        return remote(part_out.at[rows], part_in.at[rows], part_send.at[piece], part_recv.at[piece], partner)

    ids_all[me] = ids[...]
    small[me] = jnp.zeros(small.shape[1:], F32)
    small[me, : gains.shape[0], : gains.shape[1]] = gains[...].astype(BF16).astype(F32)
    count = jnp.sum(counted[...].astype(F32), keepdims=True)
    small[me, gains.shape[0] : gains.shape[0] + 1, :] = jnp.broadcast_to(count, (1, small.shape[2]))
    greet([{WIDE: device} for device in around[1:]] + [sibling, partner])
    for step in range(1, owners):
        id_copy(step).start()
    for step in range(1, owners):
        small_copy(step).start()
    carry.begin(0, 1)
    padded = jnp.concatenate([table[0], jnp.zeros((LANES - share, vocab), F32)], axis=0)
    low[...] = jnp.transpose(padded).astype(BF16)

    def look_up(step):
        row = lax.rem(me + step, owners)

        def find(start):
            def block(b, _):
                place_of = start // LANES + b
                for t, pick in enumerate(token_picks(ids_all[row, pl.ds(place_of, 1), :], vocab, first)):
                    picks[rows_at(0, b, LANES), t * LANES : (t + 1) * LANES] = pick
                return 0

            lax.fori_loop(0, seq_len // 2 // LANES, block, 0)
            return dot_nn(picks[...], low[...]).astype(BF16)

        near_out[step] = find(other)
        near_copy(step).start()
        own[step] = find(mine)

    def halve(step):
        near_copy(step).wait_recv()
        total = own[step] + near_in[step]
        own[step] = total
        far_out[step] = own[step, pl.ds(pl.multiple_of((1 - side) * quarter, quarter), quarter), :]
        far_copy(step).start()

    def deliver(step):
        far_copy(step).wait_recv()
        total = own[step, pl.ds(pl.multiple_of(side * quarter, quarter), quarter), :] + far_in[step]
        if step % owners == 0:
            wide_in[me] = total
        else:
            wide_out[step] = total
            wide_copy(step).start()

    order = list(range(1, owners)) + [0]
    for turn in range(owners + 2):
        if turn < owners:
            if order[turn]:
                id_copy(owners - order[turn]).wait_recv()
            look_up(order[turn])
        if 1 <= turn < owners + 1:
            halve(order[turn - 1])
        if turn >= 2:
            deliver(order[turn - 2])
        if turn == 1:
            carry.begin(2)
    carry.begin(3)
    carry.hand_on(0, 1)
    for step in range(1, owners):
        small_copy(step).wait_recv()
    total = None
    for owner in range(owners):
        part = dot_nn(small[owner].astype(BF16), feature_places(owner, width, share))
        total = part if total is None else total + part
    gain_all[...] = total
    count_all[...] = jnp.sum(small[...], axis=0)
    for step in range(1, owners):
        wide_copy(step).wait_recv()
    pieces = quarter // LANES
    at_side = pl.multiple_of(side * quarter, quarter)
    at_other = pl.multiple_of((1 - side) * quarter, quarter)
    for piece in range(pieces):
        rows = pl.ds(piece * LANES, LANES)
        found = None
        for owner in range(owners):
            part = dot_nn(wide_in[owner, rows, :], feature_places(owner, width, share))
            found = part if found is None else found + part
        part_out[rows, :] = found.astype(BF16)
        part_copy(piece).start()

    def finish(start, source, piece):
        rows = rows_at(start, piece, LANES)
        x = math.sqrt(width) * source[pl.ds(piece * LANES, LANES), :].astype(F32) + extra[rows, :]
        resid[rows, :] = x
        here = rows_at(mine + start, piece, LANES)
        normed[here, :] = norm_of(x, gain_all[0:1, :]).astype(BF16)
        give_rows(here, piece if source is part_out else pieces + piece).start()

    def give_rows(here, k):
        return remote(normed.at[here], normed.at[here], send.at[0, k], recv.at[0, k], sibling)

    for piece in range(pieces):
        finish(at_side, part_out, piece)
    for piece in range(pieces):
        part_copy(piece).wait_recv()
        finish(at_other, part_in, piece)
    carry.hand_on(2)
    for k in range(2 * pieces):
        give_rows(rows_at(mine, k % pieces, LANES), k).wait()
    for step in range(owners):
        near_copy(step).wait_send()
        far_copy(step).wait_send()
        if step:
            id_copy(step).wait_send()
            small_copy(step).wait_send()
            wide_copy(step).wait_send()
    for piece in range(pieces):
        part_copy(piece).wait_send()


QUERY_BLOCK = 256


def forward_part(
    layer, weights, points, normed, key_seg, query_seg, resid, gains,
    projected, mixed, middle, normed_two, result, normed_next,
    bias, values_t, near_out, near_in, far_out, far_in, near_out2, near_in2, far_out2, far_in2, own2, send, recv,
):
    w_query, w_out, w_in, w_red = weights
    at_half, at_feed, at_sent, at_last = points
    seq_len, width = normed.shape
    chunk = seq_len // 2 // CHUNKS
    block = bias.shape[1]
    heads = mixed.shape[1] // HD
    sibling, partner, mine, other = group_places(seq_len)
    pair = (send, recv)
    first = Exchange((near_out, near_in, far_out, far_in), pair, 0, sibling, partner)
    second = Exchange((near_out2, near_in2, far_out2, far_in2), pair, 2, sibling, partner)
    share = Share(normed_two, pair, 4, sibling, mine, chunk)
    share_next = Share(normed_next, pair, 5, sibling, mine, chunk)

    def ask(i, _):
        rows = rows_at(0, i, block)
        for which in range(3):
            projected[which, rows, :] = dot_nn(normed[rows, :], w_query(which)).astype(BF16)
        return 0

    lax.fori_loop(0, seq_len // block, ask, 0)
    values_t[...] = jnp.transpose(projected[2])

    def attend_rows(start):
        rows = pl.ds(pl.multiple_of(start, block), block)
        bias[...] = jnp.where(key_seg[...] == query_seg[:, rows], 0.0, -1e30)
        asked = projected[0, rows, :] * HD ** (-0.5)
        parts = []
        for head in range(heads):
            scores = dot_nt(projected[1], head_lanes(asked, head, HD)) + bias[...]
            powers = jnp.exp(scores - jnp.max(scores, axis=0, keepdims=True))
            probs = (powers * (1.0 / jnp.sum(powers, axis=0, keepdims=True))).astype(BF16)
            parts.append(dot_nn(values_t[head * HD : (head + 1) * HD, :], probs))
        mixed[rows, :] = jnp.transpose(jnp.concatenate(parts, axis=0)).astype(BF16)

    def project(start, j):
        return dot_nt(mixed[rows_at(start, j, chunk), :], w_out())

    def feed(rows):
        pre = dot_nn(normed_two[rows, :], w_in())
        return dot_nt(gelu_of(pre).astype(BF16), w_red())

    per_block = block // chunk
    for part in range(CHUNKS // per_block):

        def both(i, _):
            attend_rows(jnp.where(i == 0, other, mine) + part * block)
            return 0

        lax.fori_loop(0, 2, both, 0)
        for j in range(part * per_block, (part + 1) * per_block):
            first.give(j, project(other, j))
        if part == 0:
            at_half()
        for j in range(part * per_block, (part + 1) * per_block):
            first.pass_on(j, project(mine, j))
    at_feed()
    for j in range(CHUNKS):
        rows = rows_at(0, j, chunk)
        mid = resid[rows, :] + first.take(j)
        middle[rows, :] = mid
        share.put(j, norm_of(mid, gains[2 * layer + 1 : 2 * layer + 2, :]).astype(BF16))
        own2[j] = feed(rows_at(mine, j, chunk))
        share.arrived(j)
        second.give(j, feed(rows_at(other, j, chunk)))
        if j >= 1:
            second.pass_on(j - 1, own2[j - 1])
    second.pass_on(CHUNKS - 1, own2[CHUNKS - 1])
    at_sent()
    for j in range(CHUNKS):
        rows = rows_at(0, j, chunk)
        x = middle[rows, :] + second.take(j)
        result[rows, :] = x
        share_next.put(j, norm_of(x, gains[2 * layer + 2 : 2 * layer + 3, :]).astype(BF16))
        if j == CHUNKS - 2:
            at_last()
    for j in range(CHUNKS):
        share_next.arrived(j)
    for part in (first, second, share, share_next):
        part.close()


def layer_outs(seq_len, width, heads_width):
    return [
        jax.ShapeDtypeStruct((3, seq_len, heads_width), BF16),
        jax.ShapeDtypeStruct((seq_len, heads_width), BF16),
        jax.ShapeDtypeStruct((seq_len // 2, width), F32),
        jax.ShapeDtypeStruct((seq_len, width), BF16),
    ]


def layer_scratch(seq_len, width, heads_width):
    half, chunk = seq_len // 2, seq_len // 2 // CHUNKS
    block = max(chunk, min(QUERY_BLOCK, half))
    return (
        [pltpu.VMEM((seq_len, block), F32), pltpu.VMEM((heads_width, seq_len), BF16)]
        + Exchange.scratch(chunk, width, FORWARD_KIND)
        + Exchange.scratch(chunk, width, FORWARD_KIND)
        + [pltpu.VMEM((CHUNKS, chunk, width), F32)]
        + sems(6)
    )


LAYER_SCRATCH = 13


def front_kernel(
    ids, counted, gains, extra, table, key_seg, query_seg,
    resid, normed, gain_all, count_all, ids_all, projected, mixed, middle, normed_two, result, normed_next,
    *scratch, carry,
):
    embed_part(
        ids, counted, gains, extra, table, resid, normed, gain_all, count_all, ids_all,
        *scratch[:-LAYER_SCRATCH], carry,
    )
    carry.end(0, 1)
    later = list(carry.all())[4:]

    def at_half():
        carry.hand_on(3)
        carry.begin(*later[:2])

    def at_feed():
        carry.end(2, 3)
        carry.begin(*later[2:])

    forward_part(
        0,
        [carry.loads[0].value] + [load.value for load in carry.loads[1:4]],
        (at_half, at_feed, lambda: carry.hand_on(*later[:2]), lambda: carry.hand_on(*later[2:3])),
        normed, key_seg, query_seg, resid, gain_all,
        projected, mixed, middle, normed_two, result, normed_next, *scratch[-LAYER_SCRATCH:],
    )
    carry.end(*later)


def front(ids, counted, gains, extra, tables, key_seg, query_seg, owners, heads_width, collective_id, loads):
    seq_len = ids.size
    half, width = extra.shape
    share, vocab = tables.shape[1:]
    dma = pltpu.SemaphoreType.DMA
    return run(
        front_kernel,
        "front",
        [ids, counted, gains, extra, tables, key_seg, query_seg],
        [
            jax.ShapeDtypeStruct((half, width), F32),
            jax.ShapeDtypeStruct((seq_len, width), BF16),
            jax.ShapeDtypeStruct((8, width), F32),
            jax.ShapeDtypeStruct((8, LANES), F32),
            jax.ShapeDtypeStruct((owners,) + ids.shape, jnp.int32),
        ]
        + layer_outs(seq_len, width, heads_width)
        + [jax.ShapeDtypeStruct((half, width), F32), jax.ShapeDtypeStruct((seq_len, width), BF16)],
        [
            pltpu.VMEM((vocab, LANES), BF16),
            pltpu.VMEM((half, vocab), BF16),
            pltpu.VMEM((owners, 8, LANES), F32),
            pltpu.VMEM((owners, half, LANES), BF16),
            pltpu.VMEM((owners, half, LANES), BF16),
            pltpu.VMEM((owners, half, LANES), BF16),
            pltpu.VMEM((owners, half // 2, LANES), BF16),
            pltpu.VMEM((owners, half // 2, LANES), BF16),
            pltpu.VMEM((owners, half // 2, LANES), BF16),
            pltpu.VMEM((owners, half // 2, LANES), BF16),
            pltpu.VMEM((half // 2, width), BF16),
            pltpu.VMEM((half // 2, width), BF16),
        ]
        + [dma((owners,))] * 10
        + [dma((half // 2 // LANES,))] * 2
        + [dma((1, half // LANES))] * 2
        + layer_scratch(seq_len, width, heads_width),
        collective_id,
        loads,
    )


TILE = 256


def weight_grad(left_t, right, out):
    columns = right.shape[1]
    tile = TILE if columns % TILE == 0 else columns

    def put(where):
        value = dot_nn(left_t[...], right[:, where]).astype(out.dtype)
        if len(out.shape) == 3:
            out[:, :, where] = value.reshape(out.shape[:2] + (tile,))
        else:
            out[:, where] = value

    def step(i, _):
        put(pl.ds(pl.multiple_of(i * tile, tile), tile))
        return 0

    if tile == columns:
        put(slice(None))
    else:
        lax.fori_loop(0, columns // tile, step, 0)


def head_lanes(value, head, size):
    lanes = lax.broadcasted_iota(jnp.int32, value.shape, 1)
    inside = (lanes >= head * size) & (lanes < (head + 1) * size)
    return jnp.where(inside, value, jnp.zeros_like(value))


def backward_kernel(
    layer, scale, points, grad, branch, w_red, w_in, w_out, normed_two, middle, gains, mixed,
    projected, key_seg, query_seg, w_query, resid, normed,
    grad_out, branch_out, d_out, d_query, gain_two, gain_one,
    d_red, d_in, grad_middle, grad_attn, grad_mixed, grad_projected, grad_before, after, turned,
    bias, keys_t, grad_keys, grad_values,
    near_out, near_in, far_out, far_in, far_out2, far_in2, send, recv, loaded, carry,
):
    at_start, at_made, at_summed, at_attended, at_sent = points
    seq_len, width = normed_two.shape
    chunk = seq_len // 2 // CHUNKS
    sibling, partner, mine, other = group_places(seq_len)
    greet([sibling, partner] + carry.peers())
    at_start(carry, d_red, d_in)
    pair = (send, recv)
    trade = Exchange((near_out, near_in, far_out, far_in), pair, 0, sibling, partner)
    share = Share(grad_attn, pair, 2, sibling, mine, chunk)

    def ffn_partial(start, j):
        rows = rows_at(start, j, chunk)
        pre = dot_nn(normed_two[rows, :], w_in[...])
        after[rows, :] = gelu_of(pre).astype(BF16)
        low = (dot_nn(branch[rows, :], w_red[...]) * gelu_slope(pre)).astype(BF16)
        grad_before[rows, :] = low
        return dot_nt(low, w_in[...])

    trade.give(0, ffn_partial(other, 0))
    for j in range(CHUNKS):
        if j + 1 < CHUNKS:
            trade.give(j + 1, ffn_partial(other, j + 1))
        trade.pass_on(j, ffn_partial(mine, j))
    turned[...] = jnp.transpose(branch[...])
    weight_grad(turned, after, d_red)
    turned[...] = jnp.transpose(normed_two[...])
    weight_grad(turned, grad_before, d_in)
    at_made(carry)
    fetch = pltpu.make_async_copy(normed, after, loaded)
    fetch.start()
    total = jnp.zeros((1, width), F32)
    for j in range(CHUNKS):
        rows = rows_at(0, j, chunk)
        back, part = norm_back(trade.take(j), middle[rows, :], gains[2 * layer + 1 : 2 * layer + 2, :])
        total = total + part
        back = back + grad[rows, :]
        grad_middle[rows, :] = back
        share.put(j, back.astype(BF16))
        here = rows_at(mine, j, chunk)
        grad_mixed[here, :] = dot_nn(grad_attn[here, :], w_out[...]).astype(BF16)
    gain_two[...] = total
    for j in range(CHUNKS):
        share.arrived(j)
        here = rows_at(other, j, chunk)
        grad_mixed[here, :] = dot_nn(grad_attn[here, :], w_out[...]).astype(BF16)
    trade.close()
    share.close()
    at_summed(carry)

    block = bias.shape[1]
    heads = grad_mixed.shape[1] // HD
    keys_t[...] = jnp.transpose(projected[1])
    grad_keys[...] = jnp.zeros(grad_keys.shape, F32)
    grad_values[...] = jnp.zeros(grad_values.shape, F32)

    def queries(i, _):
        rows = rows_at(0, i, block)
        bias[...] = jnp.where(key_seg[...] == query_seg[:, rows], 0.0, -1e30)
        asked = projected[0, rows, :] * HD ** (-0.5)
        given = grad_mixed[rows, :]
        parts = []
        for head in range(heads):
            query = head_lanes(asked, head, HD)
            wanted = head_lanes(given, head, HD)
            scores = dot_nt(projected[1], query) + bias[...]
            powers = jnp.exp(scores - jnp.max(scores, axis=0, keepdims=True))
            probs = powers * (1.0 / jnp.sum(powers, axis=0, keepdims=True))
            grad_probs = dot_nt(projected[2], wanted)
            centre = jnp.sum(probs * grad_probs, axis=0, keepdims=True)
            grad_scores = (probs * (grad_probs - centre)).astype(BF16)
            parts.append(dot_nn(keys_t[head * HD : (head + 1) * HD, :], grad_scores))
            grad_keys[...] += dot_nn(grad_scores, query)
            grad_values[...] += dot_nn(probs.astype(BF16), wanted)
        grad_projected[0, rows, :] = (jnp.transpose(jnp.concatenate(parts, axis=0)) * HD ** (-0.5)).astype(BF16)
        return 0

    lax.fori_loop(0, seq_len // block, queries, 0)
    grad_projected[1] = grad_keys[...].astype(BF16)
    grad_projected[2] = grad_values[...].astype(BF16)
    at_attended(carry)

    trade = Exchange((near_out, near_in, far_out2, far_in2), pair, 3, sibling, partner)
    share = Share(branch_out, pair, 5, sibling, mine, chunk)

    def query_partial(start, j):
        rows = rows_at(start, j, chunk)
        found = None
        for which in range(3):
            part = dot_nt(grad_projected[which, rows, :], w_query[which])
            found = part if found is None else found + part
        return found

    trade.give(0, query_partial(other, 0))
    for j in range(CHUNKS):
        if j + 1 < CHUNKS:
            trade.give(j + 1, query_partial(other, j + 1))
        trade.pass_on(j, query_partial(mine, j))
    turned[...] = jnp.transpose(grad_attn[...])
    weight_grad(turned, mixed, d_out)
    fetch.wait()
    turned[...] = jnp.transpose(after[...])
    for which in range(3):
        weight_grad(turned, grad_projected.at[which], d_query.at[which])
    at_sent(carry, d_out)
    total = jnp.zeros((1, width), F32)
    for j in range(CHUNKS):
        rows = rows_at(0, j, chunk)
        back, part = norm_back(trade.take(j), resid[rows, :], gains[2 * layer : 2 * layer + 1, :])
        total = total + part
        back = back + grad_middle[rows, :]
        grad_out[rows, :] = back
        share.put(j, (back if scale is None else scale * back).astype(BF16))
    gain_one[...] = total
    for j in range(CHUNKS):
        share.arrived(j)
    trade.close()
    share.close()
    carry.end(*carry.all())


def backward_block(
    layer, scale, points, grad, branch, w_red, w_in, w_out, normed_two, middle, gains, mixed,
    projected, key_seg, query_seg, w_query, resid, normed, owners, collective_id, loads,
):
    seq_len, width = normed_two.shape
    hidden, heads_width = w_in.shape[1], w_query.shape[2]
    half, chunk = seq_len // 2, seq_len // 2 // CHUNKS
    block = min(QUERY_BLOCK, seq_len)
    far = pltpu.VMEM((CHUNKS, chunk, width), BACKWARD_KIND)
    return run(
        functools.partial(backward_kernel, layer, scale, points),
        "backward_block",
        [grad, branch, w_red, w_in, w_out, normed_two, middle, gains, mixed]
        + [projected, key_seg, query_seg, w_query, resid, normed],
        [
            jax.ShapeDtypeStruct((half, width), F32),
            jax.ShapeDtypeStruct((seq_len, width), BF16),
            jax.ShapeDtypeStruct((owners, width // owners, heads_width), BF16),
            jax.ShapeDtypeStruct((3, owners, width // owners, heads_width), BF16),
            jax.ShapeDtypeStruct((1, width), F32),
            jax.ShapeDtypeStruct((1, width), F32),
        ],
        [pltpu.VMEM((owners, width // owners, hidden), BF16)] * 2
        + [
            pltpu.VMEM((half, width), F32),
            pltpu.VMEM((seq_len, width), BF16),
            pltpu.VMEM((seq_len, heads_width), BF16),
            pltpu.VMEM((3, seq_len, heads_width), BF16),
            pltpu.VMEM((seq_len, hidden), BF16),
            pltpu.VMEM((seq_len, width), BF16),
            pltpu.VMEM((width, seq_len), BF16),
            pltpu.VMEM((seq_len, block), F32),
            pltpu.VMEM((heads_width, seq_len), BF16),
            pltpu.VMEM((seq_len, heads_width), F32),
            pltpu.VMEM((seq_len, heads_width), F32),
        ]
        + Exchange.scratch(chunk, width, BACKWARD_KIND)
        + [far, far]
        + sems(6)
        + [pltpu.SemaphoreType.DMA],
        collective_id,
        loads,
        far_operands=(14,),
    )


def to_rows(columns):
    lanes = lax.broadcasted_iota(jnp.int32, (LANES, LANES), 1)
    total = jnp.zeros((LANES, LANES), F32)
    for k, column in enumerate(columns):
        total = jnp.where(lanes == k, column, total)
    return jnp.transpose(total)[:8, :]


def loss_part(
    row, normed, info, value, gain, table_loads, grad_out, branch, d_gain, losses, d_tables,
    logits, grads, places, turned, stat_out, stat_in, sum_out, sum_in,
    stat_send, stat_recv, sum_send, sum_recv, near_out, near_in, far_out, far_in, send, recv,
):
    seq_len, width = normed.shape
    chunk = seq_len // 2 // CHUNKS
    piece_width = table_loads[0].out.shape[-1]
    vocab = piece_width * len(table_loads)
    tiles = vocab // LANES
    blocks = seq_len // LANES
    me = lax.axis_index(NARROW)
    sibling, partner, mine, other = group_places(seq_len)
    peers = [{NARROW: lax.rem(me + k, 4)} for k in range(1, 4)]
    sems = (send, recv)
    trade = Exchange((near_out, near_in, far_out, far_in), sems, 0, sibling, partner)
    share = Share(branch, sems, 2, sibling, mine, chunk)
    first = (me * vocab).astype(F32)
    whole = 4.0 * vocab
    lanes = lax.broadcasted_iota(jnp.int32, (LANES, LANES), 1).astype(F32)

    def stat_copy(b, k):
        return remote(stat_out.at[b], stat_in.at[k, b], stat_send.at[k, b], stat_recv.at[k, b], peers[k])

    def sum_copy(b, k):
        return remote(sum_out.at[b], sum_in.at[k, b], sum_send.at[k, b], sum_recv.at[k, b], peers[k])

    def tile_at(t):
        return pl.ds(pl.multiple_of(t * LANES, LANES), LANES)

    def ask(b, _):
        rows = rows_at(0, b, LANES)
        here = info[:, rows]
        at_noised = spread(here[0:1] - first)
        at_clean = spread(here[1:2] - first)
        places[b, 0] = at_noised
        places[b, 1] = at_clean

        def top_step(t, top):
            return jnp.maximum(top, logits[rows, tile_at(t)])

        top = lax.fori_loop(1, tiles, top_step, logits[rows, tile_at(0)], unroll=4)
        top = jnp.max(top, axis=1, keepdims=True)
        top_wide = jnp.broadcast_to(top, (LANES, LANES))

        def sum_step(t, totals):
            powers, noised, clean = totals
            piece = logits[rows, tile_at(t)]
            column = lanes + (t * LANES).astype(F32)
            return (
                powers + jnp.exp(piece - top_wide),
                noised + jnp.where(column == at_noised, piece, 0.0),
                clean + jnp.where(column == at_clean, piece, 0.0),
            )

        zero = jnp.zeros((LANES, LANES), F32)
        totals = lax.fori_loop(0, tiles, sum_step, (zero, zero, zero), unroll=2)
        stat_out[b] = to_rows([top] + [jnp.sum(total, axis=1, keepdims=True) for total in totals])
        for k in range(3):
            stat_copy(b, k).start()
        return 0

    for k, table in enumerate(table_loads):
        if k == len(table_loads) - 1:
            table.finish()

        def product(i, _):
            rows = rows_at(0, i, TILE)
            logits[rows, k * piece_width : (k + 1) * piece_width] = dot_nn(normed[rows, :], table.value())
            return 0

        lax.fori_loop(0, seq_len // TILE, product, 0)
    lax.fori_loop(0, blocks, ask, 0)

    def scalars(b):
        here = info[:, rows_at(0, b, LANES)]
        step = jnp.maximum(here[2:3], 2.0)
        left = STEPS - step + 1.0
        beta = 1.0 / left
        keep = left / STEPS
        rest = (step - 1.0) / (STEPS * whole)
        own = stat_out[b]
        others = [stat_in[k, b] for k in range(3)]
        top = own[0:1]
        for stat in others:
            top = jnp.maximum(top, stat[0:1])
        total = own[1:2] * jnp.exp(own[0:1] - top)
        noised, clean = own[2:3], own[3:4]
        for stat in others:
            total = total + stat[1:2] * jnp.exp(stat[0:1] - top)
            noised, clean = noised + stat[2:3], clean + stat[3:4]
        return here, beta, keep, rest, top + jnp.log(total), noised, clean

    def measure(b, _):
        rows = rows_at(0, b, LANES)
        for k in range(3):
            stat_copy(b, k).wait_recv()
        _, _, keep, rest, log_total, _, _ = scalars(b)
        log_wide = spread(log_total)
        ratio = spread(keep / rest)

        def step(t, totals):
            logs, shares = totals
            probs = jnp.exp(logits[rows, tile_at(t)] - log_wide)
            logits[rows, tile_at(t)] = probs
            grown = 1.0 + probs * ratio
            return (logs + jnp.log(grown), shares + probs / grown)

        zero = jnp.zeros((LANES, LANES), F32)
        totals = lax.fori_loop(0, tiles, step, (zero, zero), unroll=2)
        sum_out[b] = to_rows([jnp.sum(total, axis=1, keepdims=True) for total in totals])
        for k in range(3):
            sum_copy(b, k).start()
        return 0

    lax.fori_loop(0, blocks, measure, 0)

    def pull(b):
        rows = rows_at(0, b, LANES)
        for k in range(3):
            sum_copy(b, k).wait_recv()
        here, beta, keep, rest, log_total, noised, clean = scalars(b)
        sums = sum_out[b] + sum_in[0, b] + sum_in[1, b] + sum_in[2, b]
        log_sum, share_sum = sums[0:1], sums[1:2] / rest
        same = here[0:1] == here[1:2]
        first_step = here[2:3] == 1.0
        base_a, more_a = beta / whole, 1.0 - beta
        base_w = base_a * rest
        joint = whole * base_w + more_a * rest + base_a * keep + jnp.where(same, more_a * keep, 0.0)
        ratio = keep / rest
        prob_n, prob_c = jnp.exp(noised - log_total), jnp.exp(clean - log_total)
        grown_n, grown_c = 1.0 + prob_n * ratio, 1.0 + prob_c * ratio
        marginal_n, marginal_c = rest * grown_n, rest * grown_c
        log_n, log_c = jnp.log(grown_n), jnp.log(grown_c)
        weight_n = jnp.where(same, 0.0, more_a * rest)
        weight_c = jnp.where(same, more_a * rest + base_a * keep + more_a * keep, base_a * keep)
        lift = jnp.log((keep + rest) / rest)
        cross = -base_w * log_sum - weight_n * log_n - weight_c * log_c + (base_w + weight_c) * lift
        model = base_a * (keep + whole * rest) + more_a * marginal_n
        divergence = cross / joint - jnp.log(joint) + jnp.log(model)
        loss = jnp.where(first_step, log_total - clean, divergence)
        losses[:, rows] = here[4:5] * loss
        weighted = base_w * share_sum + weight_n * prob_n / marginal_n + weight_c * prob_c / marginal_c
        aligned = base_a + more_a * prob_n
        centre = keep * (aligned / model - weighted / joint)
        scale = here[3:4]
        zero = jnp.zeros_like(scale)
        even = scale * jnp.where(first_step, 1.0, keep * base_a / model - centre)
        bent = scale * jnp.where(first_step, zero, -keep * base_w / joint / rest)
        at_n = prob_n * keep * (more_a / model - weight_n / joint / marginal_n)
        at_c = -prob_c * keep * (weight_c / joint / marginal_c)
        extra_n = spread(scale * jnp.where(first_step, zero, at_n))
        extra_c = spread(scale * jnp.where(first_step, -1.0, at_c))
        even, bent, ratio = spread(even), spread(bent), spread(ratio)
        at_noised, at_clean = places[b, 0], places[b, 1]

        def step(t, _):
            probs = logits[rows, tile_at(t)]
            column = lanes + (t * LANES).astype(F32)
            grad = probs * (even + bent / (1.0 + probs * ratio))
            grad = grad + jnp.where(column == at_noised, extra_n, 0.0)
            grad = grad + jnp.where(column == at_clean, extra_c, 0.0)
            grads[rows, tile_at(t)] = grad.astype(BF16)
            return 0

        lax.fori_loop(0, tiles, step, 0, unroll=2)

    def partial(start, j):
        base = start // LANES + j * (chunk // LANES)
        for b in range(chunk // LANES):
            pull(base + b)
        total = None
        for k, table in enumerate(table_loads):
            part = dot_nt(grads[rows_at(start, j, chunk), k * piece_width : (k + 1) * piece_width], table.value())
            total = part if total is None else total + part
        return total

    trade.give(0, partial(other, 0))
    for j in range(CHUNKS):
        if j + 1 < CHUNKS:
            trade.give(j + 1, partial(other, j + 1))
        trade.pass_on(j, partial(mine, j))
    turned[...] = jnp.transpose(normed[...])
    for k, d_table in enumerate(d_tables):
        weight_grad(turned, grads.at[:, k * piece_width : (k + 1) * piece_width], d_table)
    gain_total = jnp.zeros((1, gain.shape[1]), F32)
    for j in range(CHUNKS):
        rows = rows_at(0, j, chunk)
        back, gain_part = norm_back(trade.take(j), value[rows, :], gain[row : row + 1, :])
        gain_total = gain_total + gain_part
        grad_out[rows, :] = back
        share.put(j, back.astype(BF16))
    d_gain[...] = gain_total
    for j in range(CHUNKS):
        share.arrived(j)
    trade.close()
    share.close()

    def finish(b, _):
        for k in range(3):
            stat_copy(b, k).wait_send()
            sum_copy(b, k).wait_send()
        return 0

    lax.fori_loop(0, blocks, finish, 0)


def back_kernel(
    layer, normed, key_seg, query_seg, resid, w_query, w_out, w_in, gains, info,
    projected, mixed, middle, normed_two, grad_out, branch, d_gain, losses, *refs, carry,
):
    pieces = len(carry.loads) - 1
    d_tables, refs = refs[:pieces], refs[pieces:]
    (result, normed_next), refs = refs[:2], refs[2:]
    loss_scratch, layer_refs = refs[:-LAYER_SCRATCH], refs[-LAYER_SCRATCH:]
    me = lax.axis_index(NARROW)
    greet([{NARROW: lax.rem(me + k, 4)} for k in range(1, 4)] + carry.peers())
    carry.begin(0, 1)

    def at_half():
        carry.begin(2)

    def at_feed():
        carry.end(0)
        carry.hand_on(1)
        carry.begin(3)

    def at_sent():
        carry.hand_on(2)
        carry.begin(4)

    def at_last():
        carry.hand_on(3)

    forward_part(
        layer,
        [lambda which: w_query[which], lambda: w_out[...], lambda: w_in[...], carry.loads[0].value],
        (at_half, at_feed, at_sent, at_last),
        normed, key_seg, query_seg, resid, gains,
        projected, mixed, middle, normed_two, result, normed_next, *layer_refs,
    )
    carry.hand_on(4)
    carry.end(1, 2, 3)
    loss_part(
        2 * layer + 2, normed_next, info, result, gains, carry.loads[1:], grad_out, branch, d_gain, losses, d_tables,
        *loss_scratch, *layer_refs[2:6], *layer_refs[-2:],
    )


def last_and_loss(
    layer, normed, key_seg, query_seg, resid, w_query, w_out, w_in, gains, info, vocab, collective_id, loads
):
    seq_len, width = normed.shape
    heads_width = w_query.shape[2]
    half, blocks = seq_len // 2, seq_len // LANES
    pieces = len(loads) - 1
    return run(
        functools.partial(back_kernel, layer),
        "last_and_loss",
        [normed, key_seg, query_seg, resid, w_query, w_out, w_in, gains, info],
        layer_outs(seq_len, width, heads_width)
        + [
            jax.ShapeDtypeStruct((half, width), F32),
            jax.ShapeDtypeStruct((seq_len, width), BF16),
            jax.ShapeDtypeStruct((1, width), F32),
            jax.ShapeDtypeStruct((1, seq_len), F32),
        ]
        + [jax.ShapeDtypeStruct((width, vocab // pieces), BF16)] * pieces,
        [
            pltpu.VMEM((half, width), F32),
            pltpu.VMEM((seq_len, width), BF16),
            pltpu.VMEM((seq_len, vocab), F32),
            pltpu.VMEM((seq_len, vocab), BF16),
            pltpu.VMEM((blocks, 2, LANES, LANES), F32),
            pltpu.VMEM((width, seq_len), BF16),
            pltpu.VMEM((blocks, 8, LANES), F32),
            pltpu.VMEM((3, blocks, 8, LANES), F32),
            pltpu.VMEM((blocks, 8, LANES), F32),
            pltpu.VMEM((3, blocks, 8, LANES), F32),
        ]
        + [pltpu.SemaphoreType.DMA((3, blocks))] * 4
        + layer_scratch(seq_len, width, heads_width),
        collective_id,
        loads,
    )


def sum_ways(place, me, slow, fast, slows, group):
    near = [{NARROW: lax.rem(place + step, group)} for step in range(1, group)]
    return near, {WIDE: me + 1 - 2 * fast}


def tail_kernel(
    layers, branch, ids_all, losses, full, *refs, carry,
):
    gain_parts, refs = refs[: 2 * layers + 1], refs[2 * layers + 1 :]
    squares, refs = refs[: len(refs) - 32], refs[len(refs) - 32 :]
    tail_body(branch, ids_all, losses, full, gain_parts, squares, *refs, carry)


def tail_body(
    branch, ids_all, losses, full, gain_parts, squares,
    d_table, d_full, d_small, scalars,
    out_blocks, all_in, masked, picks, total, gains_out, gains_in, blocks, block_in, line_out, line_in,
    fast_in, sums, slow_in, near, along, across,
    wide_send, wide_recv, far_send, far_recv, near_send, near_recv,
    pair_send, pair_recv, line_send, line_recv, sum_sems,
    carry,
):
    seq_len, width = branch.shape
    quarter, half = seq_len // 4, seq_len // 2
    owners = ids_all.shape[0]
    share, vocab = d_table.shape
    sibling, partner, mine, other = group_places(seq_len)
    place = lax.axis_index(NARROW)
    side = lax.div(place, 2)
    me, slow, fast, slows = wide_places(owners)
    beside = {WIDE: me + 1 - 2 * fast}
    group = near.shape[0]
    first = place * vocab
    around = [lax.rem(me + step, owners) for step in range(owners)]
    at_quarter = pl.multiple_of(mine + side * quarter, quarter)
    across_quarter = pl.multiple_of(mine + (1 - side) * quarter, quarter)

    def along_way(step):
        return {WIDE: 2 * lax.rem(slow + step, slows) + fast}

    def wide_copy(step):
        return remote(
            out_blocks.at[around[step]], all_in.at[me, pl.ds(at_quarter, quarter)],
            wide_send.at[step], wide_recv.at[step], {WIDE: around[step]},
        )

    def far_copy(step):
        rows = all_in.at[around[step], pl.ds(at_quarter, quarter)]
        return remote(rows, rows, far_send.at[step], far_recv.at[step], partner)

    def near_copy(step):
        rows = all_in.at[around[step], pl.ds(mine, half)]
        return remote(rows, rows, near_send.at[step], near_recv.at[step], sibling)

    def block(owner):
        return full.at[:, owner]

    def pair_copy(step):
        return remote(
            block(2 * lax.rem(slow + step, slows) + 1 - fast), fast_in.at[step],
            pair_send.at[step], pair_recv.at[step], beside,
        )

    def line_copy(step):
        return remote(sums.at[step], slow_in.at[step], line_send.at[step], line_recv.at[step], along_way(step))

    def gain_near():
        return remote(gains_out, gains_in, sum_sems.at[0, 0], sum_sems.at[1, 0], sibling)

    def gain_pair(step):
        return remote(
            blocks.at[2 * lax.rem(slow + step, slows) + 1 - fast], block_in.at[step],
            sum_sems.at[2, step], sum_sems.at[3, step], beside,
        )

    def gain_line(step):
        return remote(line_out.at[step], line_in.at[step], sum_sems.at[4, step], sum_sems.at[5, step], along_way(step))

    near_ways = [{NARROW: lax.rem(place + step, group)} for step in range(1, group)]
    greet([{WIDE: device} for device in around[1:]] + near_ways)
    for step in range(slows):
        pair_copy(step).start()
    gains_out[...] = jnp.zeros(gains_out.shape, F32)
    for row, part in enumerate(gain_parts):
        gains_out[row : row + 1, :] = part[...]
    gain_near().start()
    for owner in range(owners):
        out_blocks[owner] = dot_nt(
            branch[pl.ds(at_quarter, quarter), :], feature_places(owner, width, share)
        ).astype(BF16)
    for step in range(1, owners):
        wide_copy(step).start()
    all_in[me, pl.ds(at_quarter, quarter), :] = out_blocks[me]
    carry.begin(*carry.all())
    gain_near().wait_recv()
    both = gains_out[...] + gains_in[...]
    for owner in range(owners):
        blocks[owner] = lax.dot_general(
            both, feature_places(owner, width, share).astype(F32), (((1,), (1,)), ((), ())),
            precision=lax.Precision.HIGHEST, preferred_element_type=F32,
        )
    for step in range(slows):
        gain_pair(step).start()

    def hand_on(step):
        if step:
            wide_copy(owners - step).wait_recv()
        far_copy(step).start()

    def hand_over(step):
        far_copy(step).wait_recv()
        near_copy(step).start()

    def gather_grad(step, first_turn):
        near_copy(step).wait_recv()
        row = around[step]

        def make(b, _):
            rows = rows_at(0, b, LANES)
            here = ids_all[row, pl.ds(b, 1), :] - first
            high = lax.shift_right_arithmetic(here, 7)
            rest = spread((here - high * LANES).astype(F32))
            lane = lax.broadcasted_iota(jnp.int32, (LANES, LANES), 1).astype(F32)
            picks[rows, :] = jnp.where(rest == lane, 1.0, 0.0).astype(BF16)
            turned = jnp.transpose(all_in[row, rows, :])
            for t in range(vocab // LANES):
                inside = jnp.where(high == t, 1.0, 0.0).astype(BF16)
                masked[t * LANES : (t + 1) * LANES, rows] = turned * inside
            return 0

        lax.fori_loop(0, seq_len // LANES, make, 0)
        span = 2 * TILE

        def some(i, _):
            rows = rows_at(0, i, span)
            part = dot_nn(masked[rows, :], picks[...])
            total[rows, :] = part if first_turn else total[rows, :] + part
            return 0

        lax.fori_loop(0, vocab // span, some, 0)

    order = [0] + list(range(1, owners))
    for turn in range(owners + 2):
        if turn < owners:
            hand_on(order[turn])
        if 1 <= turn < owners + 1:
            hand_over(order[turn - 1])
        if turn == 1:
            for step in list(range(1, slows)) + [0]:
                pair_copy(step).wait_recv()
                owner = 2 * lax.rem(slow + step, slows) + fast
                sums[step] = (block(owner)[...].astype(F32) + fast_in[step].astype(F32)).astype(BF16)
                if step:
                    line_copy(step).start()
            for step in list(range(1, slows)) + [0]:
                gain_pair(step).wait_recv()
                line_out[step] = blocks[2 * lax.rem(slow + step, slows) + fast] + block_in[step]
                if step:
                    gain_line(step).start()
        if turn >= 2:
            gather_grad(order[turn - 2], turn == 2)
    for t in range(vocab // LANES):
        d_table[:, t * LANES : (t + 1) * LANES] = total[t * LANES : t * LANES + share, :]
    result = sums[0].astype(F32)
    small = line_out[0]
    for step in range(1, slows):
        line_copy(step).wait_recv()
        result = result + slow_in[step].astype(F32)
        gain_line(step).wait_recv()
        small = small + line_in[step]
    d_full[...] = result
    d_small[...] = small
    carry.end(*carry.all())
    square = jnp.sum(result * result) + jnp.sum(d_table[...] * d_table[...])
    for part in squares:
        square = square + part[0, 0]
    for load in carry.loads:
        square = square + load.squares[0, 0]
    lead = (place == 0).astype(F32)
    square = square + lead * jnp.sum(small * small)
    lanes = lax.broadcasted_iota(jnp.int32, (8, LANES), 1)
    given = jnp.where(lanes == 0, square, jnp.where(lanes == 1, lead * jnp.sum(losses[...]), 0.0))

    def scalar_near(step):
        return remote(near.at[place], near.at[place], sum_sems.at[6, step], sum_sems.at[7, step], near_ways[step - 1])

    def scalar_line(step):
        return remote(along.at[slow], along.at[slow], sum_sems.at[8, step], sum_sems.at[9, step], along_way(step))

    near[place] = given
    for step in range(1, group):
        scalar_near(step).start()
    for step in range(1, group):
        scalar_near(step).wait()
    along[slow] = jnp.sum(near[...], axis=0)
    for step in range(1, slows):
        scalar_line(step).start()
    for step in range(1, slows):
        scalar_line(step).wait()
    across[0] = jnp.sum(along[...], axis=0)
    last = remote(across.at[0], across.at[1], sum_sems.at[10, 0], sum_sems.at[11, 0], beside)
    last.start()
    last.wait()
    scalars[...] = across[0] + across[1]
    gain_near().wait_send()
    for step in range(owners):
        far_copy(step).wait_send()
        near_copy(step).wait_send()
        if step:
            wide_copy(step).wait_send()
    for step in range(slows):
        pair_copy(step).wait_send()
        gain_pair(step).wait_send()
        if step:
            line_copy(step).wait_send()
            gain_line(step).wait_send()


def tail(branch, ids_all, losses, full, gain_parts, squares, share, vocab, group, collective_id, loads):
    seq_len, width = branch.shape
    owners = ids_all.shape[0]
    slows = owners // 2
    shape = full.shape[:1] + full.shape[2:]
    dma = pltpu.SemaphoreType.DMA
    small = (8, LANES)
    return run(
        functools.partial(tail_kernel, (len(gain_parts) - 1) // 2),
        "tail",
        [branch, ids_all, losses, full, *gain_parts, *squares],
        [
            jax.ShapeDtypeStruct((share, vocab), F32),
            jax.ShapeDtypeStruct(shape, F32),
            jax.ShapeDtypeStruct(small, F32),
            jax.ShapeDtypeStruct(small, F32),
        ],
        [
            pltpu.VMEM((owners, seq_len // 4, LANES), BF16),
            pltpu.VMEM((owners, seq_len, LANES), BF16),
            pltpu.VMEM((vocab, seq_len), BF16),
            pltpu.VMEM((seq_len, LANES), BF16),
            pltpu.VMEM((vocab, LANES), F32),
            pltpu.VMEM((8, width), F32),
            pltpu.VMEM((8, width), F32),
            pltpu.VMEM((owners,) + small, F32),
            pltpu.VMEM((slows,) + small, F32),
            pltpu.VMEM((slows,) + small, F32),
            pltpu.VMEM((slows,) + small, F32),
            pltpu.VMEM((slows,) + shape, BF16),
            pltpu.VMEM((slows,) + shape, BF16),
            pltpu.VMEM((slows,) + shape, BF16),
            pltpu.VMEM((group,) + small, F32),
            pltpu.VMEM((slows,) + small, F32),
            pltpu.VMEM((2,) + small, F32),
        ]
        + [dma((owners,))] * 6
        + [dma((slows,))] * 4
        + [dma((12, max(slows, group)))],
        collective_id,
        loads,
    )


PIECES = 4
TABLE, ATTN_IN, ATTN_OUT, FFN_IN, FFN_OUT = range(5)


def shares_tile(wide, narrow, noised, attn_out, ffn_in, tables):
    rows, seq_len = noised.shape
    return (
        attn_out.shape[0] == 2
        and narrow == 4
        and wide % 2 == 0
        and rows == 1
        and seq_len % (2 * CHUNKS * 128) == 0
        and attn_out.shape[1] % 16 == 0
        and attn_out.shape[1] <= LANES
        and ffn_in.shape[2] % 128 == 0
        and tables.shape[1] == attn_out.shape[1]
        and tables.shape[2] % (PIECES * TILE) == 0
    )


def per_device(wide, narrow, *arrays):
    noised, attn_out, ffn_in, tables = arrays[0], arrays[6], arrays[7], arrays[9]
    if shares_tile(wide, narrow, noised, attn_out, ffn_in, tables):
        return tiled_device(wide, *arrays)
    return general_device(*arrays)


def tiled_device(
    wide,
    noised,
    clean,
    timesteps,
    segments,
    counted,
    attn_in,
    attn_out,
    ffn_in,
    ffn_out,
    tables,
    gains,
    attn_in_mean,
    attn_out_mean,
    ffn_in_mean,
    ffn_out_mean,
    tables_mean,
    gains_mean,
    attn_in_square,
    attn_out_square,
    ffn_in_square,
    ffn_out_square,
    tables_square,
    gains_square,
):
    layers = attn_in.shape[0]
    gain_rows, gain_cols = gains.shape
    mask = counted.reshape(-1).astype(jnp.float32)
    seq_len = mask.shape[0]
    half = seq_len // 2
    core = lax.rem(lax.axis_index(NARROW), 2)
    share, vocab = tables.shape[1:]
    leads = (1, 0, 0, 0)
    four = (attn_in, attn_out, ffn_in, ffn_out)

    def joined(value, lead):
        return value.reshape(value.shape[:lead] + (-1,) + value.shape[lead + 2 :])

    step_flat = timesteps.reshape(-1)
    extra = time_features(lax.dynamic_slice(step_flat, (core * half,), (half,)))
    ids = noised.reshape(-1, LANES)
    quarter = vocab // PIECES
    windows = [(k * quarter, quarter) for k in range(PIECES)]
    key_seg, query_seg = segments.reshape(-1, 1), segments.reshape(1, -1)
    weights = (attn_in, attn_out, ffn_in, ffn_out)
    (residual, normed, gain_w, counts, ids_all, projected, mixed, middle, normed_two, result, normed_next), carried = front(
        ids, counted, gains, extra, tables, key_seg, query_seg, wide, attn_out.shape[2], 0,
        [GatherLoad(value, 0, lead, wide, place=KEPT) for value, lead in zip(weights, leads)]
        + [GatherLoad(value, 1, lead, wide) for value, lead in zip(weights[:3], leads)]
        + [SlowLoad(ffn_out, 1, 0, wide)],
    )
    token_total = counts[gain_rows, 0]
    first_w = [joined(value, lead) for value, lead in zip(carried[:4], leads)]
    query_w, output_w, expand_w = [joined(value, lead) for value, lead in zip(carried[4:7], leads)]
    kept = [(residual, normed, projected, mixed, middle, normed_two, *first_w)]
    noised_flat, clean_flat = noised.reshape(-1), clean.reshape(-1)
    info = jnp.stack(
        [noised_flat.astype(F32), clean_flat.astype(F32), step_flat.astype(F32), mask / token_total, mask]
        + [jnp.zeros_like(mask)] * 3
    )
    (projected, mixed, middle, normed_two, grad, branch, gain_final, losses, *d_last), (reduce_w,) = last_and_loss(
        1, normed_next, key_seg, query_seg, result, query_w, output_w, expand_w, gain_w, info, vocab, 1,
        [FastLoad(carried[7], 0, wide)]
        + [GatherLoad(tables, 1, 0, wide, window, place=LOCAL) for window in windows],
    )
    kept.append(
        (result, normed_next, projected, mixed, middle, normed_two, query_w, output_w, expand_w, joined(reduce_w, 0))
    )
    own, squares = {}, []

    def by_owner(value, lead):
        shape = value.shape
        return value.reshape(shape[:lead] + (wide, shape[lead] // wide) + shape[lead + 1 :])

    def landed(key, results):
        own[key] = results[0]
        squares.append(results[1])
        return results[2:]

    hidden = ffn_in.shape[2]
    made = jax.ShapeDtypeStruct((wide, share, hidden), BF16)
    made_out = jax.ShapeDtypeStruct((wide, share, attn_out.shape[2]), BF16)

    def start_last(carry, d_red, d_in):
        carry.loads[PIECES].full, carry.loads[PIECES + 1].full = d_red, d_in
        carry.begin(*range(PIECES))

    half_pieces = PIECES // 2
    points = (
        start_last,
        lambda carry: carry.begin(PIECES, PIECES + 1),
        lambda carry: carry.hand_on(*range(half_pieces)),
        lambda carry: carry.hand_on(*range(half_pieces, PIECES)),
        lambda carry, d_out: None,
    )
    residual, normed, projected, mixed, middle, normed_two, query_w, output_w, expand_w, reduce_w = kept[1]
    (grad, branch, d_out, d_query, gain_two, gain_one), carried = backward_block(
        1, None, points, grad, branch, reduce_w, expand_w, output_w, normed_two, middle, gain_w, mixed,
        projected, key_seg, query_seg, query_w, residual, normed, wide, 2,
        [ReduceLoad(by_owner(piece, 0), 0) for piece in d_last]
        + [PairLoad(made, 0, True), PairLoad(made, 0, True)],
    )
    for k in range(PIECES):
        carried = landed((TABLE, k), carried)
    red_sums, in_sums = carried
    gain_grads = [None, None, gain_one, gain_two, gain_final]

    def start_first(carry, d_red, d_in):
        carry.loads[4].full, carry.loads[5].full = d_red, d_in
        carry.begin(0, 1, 2, 3)

    def sent_first(carry, d_out):
        carry.loads[6].full = d_out
        carry.begin(6)

    points = (
        start_first,
        lambda carry: carry.begin(4, 5),
        lambda carry: carry.hand_on(2, 3),
        lambda carry: carry.hand_on(4),
        sent_first,
    )
    residual, normed, projected, mixed, middle, normed_two, query_w, output_w, expand_w, reduce_w = kept[0]
    (grad, branch, _, d_query, gain_two, gain_one), carried = backward_block(
        0, math.sqrt(D), points, grad, branch, reduce_w, expand_w, output_w, normed_two, middle, gain_w, mixed,
        projected, key_seg, query_seg, query_w, residual, normed, wide, 3,
        [LineLoad(red_sums, wide), LineLoad(in_sums, wide), ReduceLoad(d_out, 0), ReduceLoad(d_query, 1)]
        + [ReduceLoad(made, 0, True), PairLoad(made, 0, True), PairLoad(made_out, 0, True)],
    )
    for key in ((FFN_OUT, 1), (FFN_IN, 1), (ATTN_OUT, 1), (ATTN_IN, 1), (FFN_OUT, 0)):
        carried = landed(key, carried)
    in_sums, out_sums = carried
    gain_grads[:2] = gain_one, gain_two

    (own_first, own[ATTN_IN, 0], total_small, scalars), carried = tail(
        branch, ids_all, losses, d_query, gain_grads, squares, share, vocab, 4, 4,
        [LineLoad(in_sums, wide), LineLoad(out_sums, wide)],
    )
    own[FFN_IN, 0], own[ATTN_OUT, 0] = carried[0], carried[2]
    grad_attn_in, grad_attn_out, grad_ffn_in, grad_ffn_out = [
        jnp.stack([own[name, index] for index in range(layers)]) for name in (ATTN_IN, ATTN_OUT, FFN_IN, FFN_OUT)
    ]
    grad_tables = jnp.stack([own_first, jnp.concatenate([own[TABLE, k] for k in range(PIECES)], axis=1)])
    grad_gains = total_small[:gain_rows, :gain_cols]
    total_square, loss_sum = scalars[0, 0], scalars[0, 1]
    grad_norm = jnp.sqrt(total_square)
    factor = jnp.minimum(1.0, CLIP_NORM / (grad_norm + 1e-06))
    results = [loss_sum, token_total, grad_norm]
    for weight, gradient, first, second, decay, rate in (
        (attn_in, grad_attn_in, attn_in_mean, attn_in_square, WEIGHT_DECAY, LEARN_RATE),
        (attn_out, grad_attn_out, attn_out_mean, attn_out_square, WEIGHT_DECAY, LEARN_RATE),
        (ffn_in, grad_ffn_in, ffn_in_mean, ffn_in_square, WEIGHT_DECAY, LEARN_RATE),
        (ffn_out, grad_ffn_out, ffn_out_mean, ffn_out_square, WEIGHT_DECAY, LEARN_RATE),
        (tables, grad_tables, tables_mean, tables_square, WEIGHT_DECAY, LEARN_RATE),
        (gains, grad_gains, gains_mean, gains_square, 0.0, GAIN_RATE),
    ):
        results += adam(weight, factor * gradient, first, second, decay, rate)
    return tuple(results)


def solution(mesh):
    wide, narrow = mesh.shape[WIDE], mesh.shape[NARROW]
    placed = (
        P(WIDE, None),
        P(WIDE, None),
        P(WIDE, None),
        P(WIDE, None),
        P(WIDE, None),
        P(None, None, WIDE, NARROW),
        P(None, WIDE, NARROW),
        P(None, WIDE, NARROW),
        P(None, WIDE, NARROW),
        P(None, WIDE, NARROW),
        P(None, WIDE),
        P(None, None, WIDE, NARROW),
        P(None, WIDE, NARROW),
        P(None, WIDE, NARROW),
        P(None, WIDE, NARROW),
        P(None, WIDE, NARROW),
        P(None, WIDE),
        P(None, None, WIDE, NARROW),
        P(None, WIDE, NARROW),
        P(None, WIDE, NARROW),
        P(None, WIDE, NARROW),
        P(None, WIDE, NARROW),
        P(None, WIDE),
    )
    return jax.shard_map(
        functools.partial(per_device, wide, narrow),
        mesh=mesh,
        in_specs=placed,
        out_specs=(
            P(),
            P(),
            P(),
            P(None, None, WIDE, NARROW),
            P(None, None, WIDE, NARROW),
            P(None, None, WIDE, NARROW),
            P(None, None, WIDE, NARROW),
            P(None, WIDE, NARROW),
            P(None, WIDE, NARROW),
            P(None, WIDE, NARROW),
            P(None, WIDE, NARROW),
            P(None, WIDE, NARROW),
            P(None, WIDE, NARROW),
            P(None, WIDE, NARROW),
            P(None, WIDE, NARROW),
            P(None, WIDE, NARROW),
            P(None, WIDE, NARROW),
            P(None, WIDE, NARROW),
            P(None, WIDE, NARROW),
            P(None, WIDE, NARROW),
            P(None, WIDE, NARROW),
            P(None, WIDE, NARROW),
            P(None, WIDE, NARROW),
            P(None, WIDE),
            P(None, WIDE),
            P(None, WIDE),
            P(None, WIDE),
        ),
        check_vma=False,
    )
```

```python
import functools
import math

import jax
import jax.numpy as jnp
from jax import lax
from jax.experimental import pallas as pl
from jax.experimental.pallas import tpu as pltpu
from jax.sharding import PartitionSpec as P

D = 768
HD = 64
V = 8192
STEPS = 1000
ADAM_STEP = 10


NORM_EPS = 1e-05
LEARN_RATE = 0.05
GAIN_RATE = 0.75
FIRST_DECAY = 0.9
SECOND_DECAY = 0.999
ADAM_EPS = 1e-08
WEIGHT_DECAY = 0.01
CLIP_NORM = 0.005
WIDE, NARROW = "wide", "narrow"


def add_heads(partial_value):
    return lax.psum(partial_value, NARROW)


def back_heads(partial_value):
    return lax.psum(partial_value, NARROW)


def rms_forward(value, gain):
    scale_row = lax.rsqrt(jnp.mean(value * value, axis=-1, keepdims=True) + NORM_EPS)
    return (value * scale_row * gain, scale_row)


def rms_backward(grad, value, scale_row, gain):
    unit = value * scale_row
    scaled = grad * gain
    back = scale_row * (scaled - unit * jnp.mean(scaled * unit, axis=-1, keepdims=True))
    return (back, jnp.sum(grad * unit, axis=0))


def time_features(timestep_row):
    half_width = D // 2
    rates = jnp.exp(-math.log(10000.0) * jnp.arange(half_width, dtype=jnp.float32) / half_width)
    angles = timestep_row.astype(jnp.float32)[:, None] * rates[None, :]
    return jnp.concatenate([jnp.sin(angles), jnp.cos(angles)], axis=1)


def masked_scores(queries, key_rows, segment):
    scores = jnp.einsum(
        "qhd,khd->hqk", queries, key_rows, preferred_element_type=jnp.float32
    ) * HD ** (-0.5)
    return jnp.where((segment[:, None] == segment[None, :])[None], scores, -1e30)


def attend(entry):
    queries, key_rows, values, segment = entry
    scores = masked_scores(queries, key_rows, segment)
    row_top = jnp.max(scores, axis=-1, keepdims=True)
    log_total = row_top + jnp.log(jnp.sum(jnp.exp(scores - row_top), axis=-1, keepdims=True))
    probs = jnp.exp(scores - log_total).astype(jnp.bfloat16)
    mixed = jnp.einsum("hqk,khd->qhd", probs, values, preferred_element_type=jnp.float32)
    return (mixed.astype(jnp.bfloat16), log_total)


def attend_back(entry):
    queries, key_rows, values, segment, log_total, grad_mixed = entry
    probs = jnp.exp(masked_scores(queries, key_rows, segment) - log_total)
    grad_probs = jnp.einsum("qhd,khd->hqk", grad_mixed, values, preferred_element_type=jnp.float32)
    grad_scores = (
        probs * (grad_probs - jnp.sum(probs * grad_probs, axis=-1, keepdims=True))
    ).astype(jnp.bfloat16)
    grad_query = jnp.einsum(
        "hqk,khd->qhd", grad_scores, key_rows, preferred_element_type=jnp.float32
    ) * HD ** (-0.5)
    grad_key = jnp.einsum(
        "hqk,qhd->khd", grad_scores, queries, preferred_element_type=jnp.float32
    ) * HD ** (-0.5)
    grad_value = jnp.einsum(
        "hqk,qhd->khd", probs.astype(jnp.bfloat16), grad_mixed, preferred_element_type=jnp.float32
    )
    return (grad_query, grad_key, grad_value)


def layer_forward(residual, segments, query_w, output_w, expand_w, reduce_w, gain_attn, gain_ffn):
    seq_count, seq_len = segments.shape
    normed, scale_one = rms_forward(residual, gain_attn)
    normed = normed.astype(jnp.bfloat16)
    projected = jnp.einsum(
        "sd,cde->cse", normed, query_w, preferred_element_type=jnp.float32
    ).astype(jnp.bfloat16)
    heads = projected.reshape(3, seq_count, seq_len, -1, HD)
    mixed, log_total = lax.map(attend, (heads[0], heads[1], heads[2], segments))
    mixed = mixed.reshape(seq_count * seq_len, -1)
    middle = residual + add_heads(
        jnp.einsum("se,de->sd", mixed, output_w, preferred_element_type=jnp.float32)
    )
    normed_two, scale_two = rms_forward(middle, gain_ffn)
    normed_two = normed_two.astype(jnp.bfloat16)
    before = jnp.dot(normed_two, expand_w, preferred_element_type=jnp.float32)
    after = jax.nn.gelu(before).astype(jnp.bfloat16)
    result = middle + add_heads(
        jnp.einsum("sf,df->sd", after, reduce_w, preferred_element_type=jnp.float32)
    )
    return (
        result,
        (
            residual,
            scale_one,
            normed,
            projected,
            log_total,
            mixed,
            middle,
            scale_two,
            normed_two,
            before,
            after,
        ),
    )


def layer_backward(
    grad, kept, segments, query_w, output_w, expand_w, reduce_w, gain_attn, gain_ffn
):
    (
        residual,
        scale_one,
        normed,
        projected,
        log_total,
        mixed,
        middle,
        scale_two,
        normed_two,
        before,
        after,
    ) = kept
    seq_count, seq_len = segments.shape
    grad_branch = grad.astype(jnp.bfloat16)
    grad_after = jnp.dot(grad_branch, reduce_w, preferred_element_type=jnp.float32)
    grad_reduce = jnp.einsum("sd,sf->df", grad_branch, after, preferred_element_type=jnp.float32)
    _, gelu_pull = jax.vjp(jax.nn.gelu, before)
    grad_before = gelu_pull(grad_after)[0].astype(jnp.bfloat16)
    grad_expand = jnp.einsum(
        "sd,sf->df", normed_two, grad_before, preferred_element_type=jnp.float32
    )
    grad_normed_two = back_heads(
        jnp.einsum("sf,df->sd", grad_before, expand_w, preferred_element_type=jnp.float32)
    )
    grad_middle, grad_gain_ffn = rms_backward(grad_normed_two, middle, scale_two, gain_ffn)
    grad_middle = grad_middle + grad
    grad_attn = grad_middle.astype(jnp.bfloat16)
    grad_mixed = jnp.dot(grad_attn, output_w, preferred_element_type=jnp.float32).astype(
        jnp.bfloat16
    )
    grad_output = jnp.einsum("sd,se->de", grad_attn, mixed, preferred_element_type=jnp.float32)
    heads = projected.reshape(3, seq_count, seq_len, -1, HD)
    grad_query, grad_key, grad_value = lax.map(
        attend_back,
        (
            heads[0],
            heads[1],
            heads[2],
            segments,
            log_total,
            grad_mixed.reshape(seq_count, seq_len, -1, HD),
        ),
    )
    grad_projected = (
        jnp.stack([grad_query, grad_key, grad_value])
        .reshape(3, seq_count * seq_len, -1)
        .astype(jnp.bfloat16)
    )
    grad_query_w = jnp.einsum(
        "sd,cse->cde", normed, grad_projected, preferred_element_type=jnp.float32
    )
    grad_normed = back_heads(
        jnp.einsum("cse,cde->sd", grad_projected, query_w, preferred_element_type=jnp.float32)
    )
    grad_input, grad_gain_attn = rms_backward(grad_normed, residual, scale_one, gain_attn)
    return (
        grad_input + grad_middle,
        (
            grad_query_w,
            grad_output,
            grad_expand,
            grad_reduce,
            jnp.stack([grad_gain_attn, grad_gain_ffn]),
        ),
    )


def adam(weight, grad, first, second, decay, rate):
    first_new = FIRST_DECAY * first + (1.0 - FIRST_DECAY) * grad
    second_new = SECOND_DECAY * second + (1.0 - SECOND_DECAY) * grad * grad
    first_hat = first_new / (1.0 - FIRST_DECAY**ADAM_STEP)
    second_hat = second_new / (1.0 - SECOND_DECAY**ADAM_STEP)
    weight_new = weight - rate * (first_hat / (jnp.sqrt(second_hat) + ADAM_EPS) + decay * weight)
    return (weight_new, first_new, second_new, weight_new.astype(jnp.bfloat16))


def general_device(
    noised,
    clean,
    timesteps,
    segments,
    counted,
    attn_in,
    attn_out,
    ffn_in,
    ffn_out,
    tables,
    gains,
    attn_in_mean,
    attn_out_mean,
    ffn_in_mean,
    ffn_out_mean,
    tables_mean,
    gains_mean,
    attn_in_square,
    attn_out_square,
    ffn_in_square,
    ffn_out_square,
    tables_square,
    gains_square,
):
    layers = attn_in.shape[0]
    mask = counted.reshape(-1).astype(jnp.float32)
    token_total = lax.psum(jnp.sum(mask), WIDE)
    query_w, output_w, expand_w, reduce_w, table_w, gain_low = (
        lax.all_gather(attn_in.astype(jnp.bfloat16), WIDE, axis=2, tiled=True),
        lax.all_gather(attn_out.astype(jnp.bfloat16), WIDE, axis=1, tiled=True),
        lax.all_gather(ffn_in.astype(jnp.bfloat16), WIDE, axis=1, tiled=True),
        lax.all_gather(ffn_out.astype(jnp.bfloat16), WIDE, axis=1, tiled=True),
        lax.all_gather(tables.astype(jnp.bfloat16), WIDE, axis=1, tiled=True),
        lax.all_gather(gains.astype(jnp.bfloat16), WIDE, axis=1, tiled=True),
    )
    gain_w = gain_low.astype(jnp.float32)
    noised_flat = noised.reshape(-1)
    clean_flat = clean.reshape(-1)
    step_flat = timesteps.reshape(-1)
    vocab_local = table_w.shape[2]
    vocab_ids = lax.axis_index(NARROW) * vocab_local + jnp.arange(vocab_local, dtype=jnp.int32)
    picks = (noised_flat[:, None] == vocab_ids[None, :]).astype(jnp.bfloat16)
    looked = add_heads(
        jnp.einsum("sv,dv->sd", picks, table_w[0], preferred_element_type=jnp.float32)
    )
    residual = math.sqrt(D) * looked + time_features(step_flat)
    kept_layers = []
    for layer_index in range(layers):
        residual, kept = layer_forward(
            residual,
            segments,
            query_w[layer_index],
            output_w[layer_index],
            expand_w[layer_index],
            reduce_w[layer_index],
            gain_w[2 * layer_index],
            gain_w[2 * layer_index + 1],
        )
        kept_layers.append(kept)
    final, scale_final = rms_forward(residual, gain_w[2 * layers])
    final_low = final.astype(jnp.bfloat16)
    logits = jnp.dot(final_low, table_w[1], preferred_element_type=jnp.float32)
    local_top = jnp.max(logits, axis=1)
    row_top = lax.pmax(local_top, NARROW)
    row_total = lax.psum(jnp.sum(jnp.exp(logits - row_top[:, None]), axis=1), NARROW)
    log_probs = logits - (row_top + jnp.log(row_total))[:, None]
    probs = jnp.exp(log_probs)
    clamped = jnp.maximum(step_flat, 2).astype(jnp.float32)[:, None]
    beta = 1.0 / (STEPS - clamped + 1.0)
    retain = (STEPS - clamped + 1.0) / STEPS
    spread = (clamped - 1.0) / (STEPS * V)
    at_noised = (vocab_ids[None, :] == noised_flat[:, None]).astype(jnp.float32)
    at_clean = (vocab_ids[None, :] == clean_flat[:, None]).astype(jnp.float32)
    forward_fac = beta / V + (1.0 - beta) * at_noised
    backward_fac = retain * at_clean + spread
    joint = forward_fac * backward_fac
    marginal = retain * probs + spread
    joint_total, cross, model_total, weighted, aligned, clean_logp = lax.psum(
        (
            jnp.sum(joint, axis=1),
            jnp.sum(joint * (jnp.log(backward_fac) - jnp.log(marginal)), axis=1),
            jnp.sum(forward_fac * marginal, axis=1),
            jnp.sum(probs * joint / marginal, axis=1),
            jnp.sum(forward_fac * probs, axis=1),
            jnp.sum(at_clean * log_probs, axis=1),
        ),
        NARROW,
    )
    divergence = cross / joint_total - jnp.log(joint_total) + jnp.log(model_total)
    first_step = step_flat == 1
    losses = jnp.where(first_step, -clean_logp, divergence)
    pull = retain * (
        -(joint / joint_total[:, None]) / marginal + forward_fac / model_total[:, None]
    )
    centre = retain[:, 0] * (-weighted / joint_total + aligned / model_total)
    grad_kl = probs * (pull - centre[:, None])
    grad_recon = probs - at_clean
    grad_logits = (
        (mask / token_total)[:, None] * jnp.where(first_step[:, None], grad_recon, grad_kl)
    ).astype(jnp.bfloat16)
    grad_table_out = jnp.einsum(
        "sd,sv->dv", final_low, grad_logits, preferred_element_type=jnp.float32
    )
    grad_final = back_heads(
        jnp.einsum("sv,dv->sd", grad_logits, table_w[1], preferred_element_type=jnp.float32)
    )
    grad_x, grad_gain_final = rms_backward(grad_final, residual, scale_final, gain_w[2 * layers])
    layer_grads = [None] * layers
    for layer_index in reversed(range(layers)):
        grad_x, produced = layer_backward(
            grad_x,
            kept_layers[layer_index],
            segments,
            query_w[layer_index],
            output_w[layer_index],
            expand_w[layer_index],
            reduce_w[layer_index],
            gain_w[2 * layer_index],
            gain_w[2 * layer_index + 1],
        )
        layer_grads[layer_index] = produced
    grad_look = (math.sqrt(D) * grad_x).astype(jnp.bfloat16)
    grad_table_in = jnp.einsum("sd,sv->dv", grad_look, picks, preferred_element_type=jnp.float32)
    stacked = [jnp.stack([entry[which] for entry in layer_grads]) for which in range(5)]
    gain_layers = stacked[4].reshape(2 * layers, -1)
    grad_tables_all = jnp.stack([grad_table_in, grad_table_out])
    grad_attn_in, grad_attn_out, grad_ffn_in, grad_ffn_out, grad_tables, grad_gains = (
        lax.psum_scatter(stacked[0], WIDE, scatter_dimension=2, tiled=True),
        lax.psum_scatter(stacked[1], WIDE, scatter_dimension=1, tiled=True),
        lax.psum_scatter(stacked[2], WIDE, scatter_dimension=1, tiled=True),
        lax.psum_scatter(stacked[3], WIDE, scatter_dimension=1, tiled=True),
        lax.psum_scatter(grad_tables_all, WIDE, scatter_dimension=1, tiled=True),
        lax.psum_scatter(
            jnp.concatenate([gain_layers, grad_gain_final[None, :]], axis=0),
            WIDE,
            scatter_dimension=1,
            tiled=True,
        ),
    )
    narrow_first = (lax.axis_index(NARROW) == 0).astype(jnp.float32)
    squares = (
        jnp.sum(grad_attn_in * grad_attn_in)
        + jnp.sum(grad_attn_out * grad_attn_out)
        + jnp.sum(grad_ffn_in * grad_ffn_in)
        + jnp.sum(grad_ffn_out * grad_ffn_out)
        + jnp.sum(grad_tables * grad_tables)
        + narrow_first * jnp.sum(grad_gains * grad_gains)
    )
    squares, loss_sum = lax.psum(
        (squares, narrow_first * jnp.sum(mask * losses)), (WIDE, NARROW)
    )
    grad_norm = jnp.sqrt(squares)
    factor = jnp.minimum(1.0, CLIP_NORM / (grad_norm + 1e-06))
    attn_in_next, attn_in_mean_next, attn_in_square_next, attn_in_copy = adam(
        attn_in, factor * grad_attn_in, attn_in_mean, attn_in_square, WEIGHT_DECAY, LEARN_RATE
    )
    attn_out_next, attn_out_mean_next, attn_out_square_next, attn_out_copy = adam(
        attn_out, factor * grad_attn_out, attn_out_mean, attn_out_square, WEIGHT_DECAY, LEARN_RATE
    )
    ffn_in_next, ffn_in_mean_next, ffn_in_square_next, ffn_in_copy = adam(
        ffn_in, factor * grad_ffn_in, ffn_in_mean, ffn_in_square, WEIGHT_DECAY, LEARN_RATE
    )
    ffn_out_next, ffn_out_mean_next, ffn_out_square_next, ffn_out_copy = adam(
        ffn_out, factor * grad_ffn_out, ffn_out_mean, ffn_out_square, WEIGHT_DECAY, LEARN_RATE
    )
    tables_next, tables_mean_next, tables_square_next, tables_copy = adam(
        tables, factor * grad_tables, tables_mean, tables_square, WEIGHT_DECAY, LEARN_RATE
    )
    gains_next, gains_mean_next, gains_square_next, gains_copy = adam(
        gains, factor * grad_gains, gains_mean, gains_square, 0.0, GAIN_RATE
    )
    return (
        loss_sum,
        token_total,
        grad_norm,
        attn_in_next,
        attn_in_mean_next,
        attn_in_square_next,
        attn_in_copy,
        attn_out_next,
        attn_out_mean_next,
        attn_out_square_next,
        attn_out_copy,
        ffn_in_next,
        ffn_in_mean_next,
        ffn_in_square_next,
        ffn_in_copy,
        ffn_out_next,
        ffn_out_mean_next,
        ffn_out_square_next,
        ffn_out_copy,
        tables_next,
        tables_mean_next,
        tables_square_next,
        tables_copy,
        gains_next,
        gains_mean_next,
        gains_square_next,
        gains_copy,
    )


MESH = pl.DeviceIdType.MESH
SLOW, FAST = 1, 2
HBM, KEPT, LOCAL = 1, 2, 3
F32 = jnp.float32
BF16 = jnp.bfloat16
CHUNKS = 4
VMEM_LIMIT = 61 * 1024 * 1024
FORWARD_KIND = BF16
BACKWARD_KIND = BF16


def whole_vmem():
    return pl.BlockSpec(memory_space=pltpu.VMEM)


def dot_nn(a, b):
    return lax.dot_general(a, b, (((1,), (0,)), ((), ())), preferred_element_type=F32)


def dot_nt(a, b):
    return lax.dot_general(a, b, (((1,), (1,)), ((), ())), preferred_element_type=F32)


def remote(src, dst, send_sem, recv_sem, device):
    return pltpu.make_async_remote_copy(
        src_ref=src,
        dst_ref=dst,
        send_sem=send_sem,
        recv_sem=recv_sem,
        device_id=device,
        device_id_type=MESH,
    )


def greet(devices):
    barrier = pltpu.get_barrier_semaphore()
    for device in devices:
        pl.semaphore_signal(barrier, inc=1, device_id=device, device_id_type=MESH)
    pl.semaphore_wait(barrier, len(devices))


def group_places(seq_len):
    me = lax.axis_index(NARROW)
    core = lax.rem(me, 2)
    half = seq_len // 2
    mine = pl.multiple_of(core * half, half)
    other = pl.multiple_of((1 - core) * half, half)
    return ({NARROW: me + 1 - 2 * core}, {NARROW: lax.rem(me + 2, 4)}, mine, other)


class Exchange:
    def __init__(self, refs, sems, base, sibling, partner):
        self.near_out, self.near_in, self.far_out, self.far_in = refs
        self.send, self.recv = sems
        self.base, self.sibling, self.partner = base, sibling, partner

    def near(self, j):
        return remote(
            self.near_out.at[j],
            self.near_in.at[j],
            self.send.at[self.base, j],
            self.recv.at[self.base, j],
            self.sibling,
        )

    def far(self, j):
        return remote(
            self.far_out.at[j],
            self.far_in.at[j],
            self.send.at[self.base + 1, j],
            self.recv.at[self.base + 1, j],
            self.partner,
        )

    def give(self, j, value):
        self.near_out[j] = value
        self.near(j).start()

    def pass_on(self, j, value):
        self.near(j).wait_recv()
        self.far_out[j] = (value + self.near_in[j]).astype(self.far_out.dtype)
        self.far(j).start()

    def take(self, j):
        self.far(j).wait_recv()
        return self.far_out[j].astype(F32) + self.far_in[j].astype(F32)

    def close(self):
        for j in range(CHUNKS):
            self.near(j).wait_send()
            self.far(j).wait_send()

    @staticmethod
    def scratch(chunk, width, kind):
        return [
            pltpu.VMEM((CHUNKS, chunk, width), F32),
            pltpu.VMEM((CHUNKS, chunk, width), F32),
            pltpu.VMEM((CHUNKS, chunk, width), kind),
            pltpu.VMEM((CHUNKS, chunk, width), kind),
        ]


class Share:
    def __init__(self, ref, sems, base, sibling, mine, chunk):
        self.ref, self.base, self.sibling, self.mine, self.chunk = ref, base, sibling, mine, chunk
        self.send, self.recv = sems

    def piece(self, j):
        rows = self.ref.at[pl.ds(pl.multiple_of(self.mine + j * self.chunk, self.chunk), self.chunk)]
        return remote(rows, rows, self.send.at[self.base, j], self.recv.at[self.base, j], self.sibling)

    def put(self, j, value):
        self.ref[pl.ds(pl.multiple_of(self.mine + j * self.chunk, self.chunk), self.chunk), :] = value
        self.piece(j).start()

    def arrived(self, j):
        self.piece(j).wait_recv()

    def close(self):
        for j in range(CHUNKS):
            self.piece(j).wait_send()


def wide_places(count):
    me = lax.axis_index(WIDE)
    fast = lax.rem(me, 2)
    slow = me // 2
    return (me, slow, fast, count // 2)


class Carry:
    def __init__(self, loads):
        self.loads = loads

    def peers(self):
        ways = []
        for load in self.loads:
            ways += [way for way in load.ways if way not in ways]
        me, slow, fast, slows = wide_places(self.loads[0].count) if self.loads else (0, 0, 0, 0)
        found = []
        if SLOW in ways:
            found += [{WIDE: 2 * lax.rem(slow + step, slows) + fast} for step in range(1, slows)]
        if FAST in ways:
            found.append({WIDE: me + 1 - 2 * fast})
        return found

    def begin(self, *which):
        for k in which:
            self.loads[k].start()

    def hand_on(self, *which):
        for k in which:
            self.loads[k].relay()

    def end(self, *which):
        for k in which:
            self.loads[k].finish()

    def all(self):
        return range(len(self.loads))


def part_of(weights, index, window):
    shape = weights.shape[1:]
    return shape if window is None else shape[:-1] + (window[1],)


class SlowLoad:
    ways = (SLOW,)

    def __init__(self, weights, index, lead, count, window=None):
        self.index, self.lead, self.count, self.window = index, lead, count, window
        shape, slows = part_of(weights, index, window), count // 2
        self.operands, self.in_specs = [weights], [whole_vmem()]
        self.outs = [jax.ShapeDtypeStruct((slows,) + shape, BF16)]
        self.out_specs = [pl.BlockSpec(memory_space=pl.ANY)]
        self.scratch = [pltpu.VMEM(shape, BF16), pltpu.SemaphoreType.DMA] + [pltpu.SemaphoreType.DMA((slows,))] * 2

    def bind(self, given, out, scratch):
        self.shard, self.out = given[0], out[0]
        self.low, self.local, self.send, self.recv = scratch
        self.me, self.slow, self.fast, self.slows = wide_places(self.count)

    def cast(self):
        if self.window is None:
            self.low[...] = self.shard[self.index].astype(BF16)
        else:
            self.low[...] = self.shard[self.index, :, self.window[0] : self.window[0] + self.window[1]].astype(BF16)

    def target(self):
        return self.out.at[self.slow]

    def slow_copy(self, step):
        return remote(
            self.low, self.target(), self.send.at[step], self.recv.at[step],
            {WIDE: 2 * lax.rem(self.slow + step, self.slows) + self.fast},
        )

    def own_copy(self):
        return pltpu.make_async_copy(self.low, self.target(), self.local)

    def start(self):
        self.cast()
        for step in range(1, self.slows):
            self.slow_copy(step).start()
        self.own_copy().start()

    def finish(self):
        for step in range(1, self.slows):
            self.slow_copy(step).wait()
        self.own_copy().wait()


class FastLoad:
    ways = (FAST,)

    def __init__(self, blocks, lead, count):
        self.lead, self.count = lead, count
        shape, slows = blocks.shape[1:], count // 2
        self.operands, self.in_specs = [blocks], [pl.BlockSpec(memory_space=pl.ANY)]
        self.outs = [jax.ShapeDtypeStruct(shape[:lead] + (count,) + shape[lead:], BF16)]
        self.out_specs = [whole_vmem()]
        self.scratch = [pltpu.SemaphoreType.DMA((slows,))] * 3

    def value(self):
        return self.out[...].reshape((-1, self.out.shape[-1]))

    def bind(self, given, out, scratch):
        self.blocks, self.out = given[0], out[0]
        self.local, self.send, self.recv = scratch
        self.me, self.slow, self.fast, self.slows = wide_places(self.count)

    def copies(self, step):
        target = self.out.at[(slice(None),) * self.lead + (2 * step + self.fast,)]
        return (
            remote(
                self.blocks.at[step], target, self.send.at[step], self.recv.at[step],
                {WIDE: self.me + 1 - 2 * self.fast},
            ),
            pltpu.make_async_copy(self.blocks.at[step], target, self.local.at[step]),
        )

    def start(self):
        for step in range(self.slows):
            for copy in self.copies(step):
                copy.start()

    def finish(self):
        for step in range(self.slows):
            for copy in self.copies(step):
                copy.wait()


class GatherLoad(SlowLoad):
    ways = (SLOW, FAST)

    def __init__(self, weights, index, lead, count, window=None, place=HBM):
        super().__init__(weights, index, lead, count, window)
        shape, slows = part_of(weights, index, window), count // 2
        whole = shape[:lead] + (count,) + shape[lead:]
        self.outs = [jax.ShapeDtypeStruct(whole, BF16)]
        self.scratch = self.scratch + [pltpu.SemaphoreType.DMA((slows,))] * 2
        if place == KEPT:
            self.out_specs = [whole_vmem()]
        self.local_out = place == LOCAL
        if self.local_out:
            self.outs, self.out_specs = [], []
            self.scratch = self.scratch + [pltpu.VMEM(whole, BF16)]

    def bind(self, given, out, scratch):
        if self.local_out:
            out, scratch = scratch[-1:], scratch[:-1]
        super().bind(given, out, scratch[:-2])
        self.fast_send, self.fast_recv = scratch[-2:]

    def value(self, *index):
        found = self.out[index] if index else self.out[...]
        return found.reshape((-1, found.shape[-1]))

    def at(self, owner):
        return self.out.at[(slice(None),) * self.lead + (owner,)]

    def target(self):
        return self.at(self.me)

    def fast_copy(self, step):
        block = self.at(2 * lax.rem(self.slow + self.slows - step, self.slows) + self.fast)
        return remote(
            self.low if step == 0 else block, block, self.fast_send.at[step], self.fast_recv.at[step],
            {WIDE: self.me + 1 - 2 * self.fast},
        )

    def start(self):
        super().start()
        self.fast_copy(0).start()

    def relay(self):
        for step in range(1, self.slows):
            self.slow_copy(step).wait_recv()
            self.fast_copy(step).start()

    def finish(self):
        for step in range(self.slows):
            self.fast_copy(step).wait()
            if step:
                self.slow_copy(step).wait_send()
        self.own_copy().wait()


class PairLoad:
    ways = (FAST,)

    def __init__(self, full, lead, inside=False):
        self.lead, self.count, self.inside = lead, full.shape[lead], inside
        self.shape, self.slows = full.shape[:lead] + full.shape[lead + 1 :], self.count // 2
        self.operands, self.in_specs = ([], []) if inside else ([full], [whole_vmem()])
        self.outs, self.out_specs = [jax.ShapeDtypeStruct((self.slows,) + self.shape, BF16)], [whole_vmem()]
        self.scratch = [pltpu.VMEM((self.slows,) + self.shape, BF16)] + [pltpu.SemaphoreType.DMA((self.slows,))] * 2

    def bind(self, given, out, scratch):
        self.full = None if self.inside else given[0]
        self.out = out[0]
        self.came, self.send, self.recv = scratch
        self.me, self.slow, self.fast, self.slows = wide_places(self.count)

    def block(self, step, fast):
        owner = 2 * lax.rem(self.slow + step, self.slows) + fast
        return self.full.at[(slice(None),) * self.lead + (owner,)]

    def copy(self, step):
        return remote(
            self.block(step, 1 - self.fast), self.came.at[step], self.send.at[step], self.recv.at[step],
            {WIDE: self.me + 1 - 2 * self.fast},
        )

    def start(self):
        for step in list(range(1, self.slows)) + [0]:
            self.copy(step).start()

    def finish(self):
        for step in range(self.slows):
            self.copy(step).wait()
            total = self.block(step, self.fast)[...].astype(F32) + self.came[step].astype(F32)
            self.out[step] = total.astype(BF16)


class ReduceLoad(PairLoad):
    ways = (SLOW, FAST)

    def __init__(self, full, lead, inside=False):
        super().__init__(full, lead, inside)
        self.outs = [jax.ShapeDtypeStruct(self.shape, F32), jax.ShapeDtypeStruct((8, 128), F32)]
        self.out_specs = [whole_vmem()] * 2
        self.scratch = (
            self.scratch
            + [pltpu.VMEM((self.slows - 1,) + self.shape, BF16)]
            + [pltpu.SemaphoreType.DMA((self.slows,))] * 2
        )

    def bind(self, given, out, scratch):
        super().bind(given, out[:1], scratch[:3])
        self.squares = out[1]
        self.landed, self.line_send, self.line_recv = scratch[3:]

    def line_copy(self, step):
        return remote(
            self.came.at[step], self.landed.at[step - 1], self.line_send.at[step], self.line_recv.at[step],
            {WIDE: 2 * lax.rem(self.slow + step, self.slows) + self.fast},
        )

    def relay(self):
        for step in list(range(1, self.slows)) + [0]:
            self.copy(step).wait()
            total = self.block(step, self.fast)[...].astype(F32) + self.came[step].astype(F32)
            self.came[step] = total.astype(BF16)
            if step:
                self.line_copy(step).start()

    def finish(self):
        total = self.came[0].astype(F32)
        for step in range(1, self.slows):
            self.line_copy(step).wait()
            total = total + self.landed[step - 1].astype(F32)
        self.out[...] = total
        self.squares[...] = jnp.full(self.squares.shape, jnp.sum(total * total), F32)


class LineLoad:
    ways = (SLOW,)

    def __init__(self, sums, count):
        self.count = count
        slows = count // 2
        self.operands, self.in_specs = [sums], [whole_vmem()]
        self.outs = [jax.ShapeDtypeStruct(sums.shape[1:], F32), jax.ShapeDtypeStruct((8, 128), F32)]
        self.out_specs = [whole_vmem()] * 2
        self.scratch = [pltpu.VMEM(sums.shape, BF16)] + [pltpu.SemaphoreType.DMA((slows,))] * 2

    def bind(self, given, out, scratch):
        self.sums, (self.out, self.squares) = given[0], out
        self.came, self.send, self.recv = scratch
        self.me, self.slow, self.fast, self.slows = wide_places(self.count)

    def copy(self, step):
        return remote(
            self.sums.at[step], self.came.at[step], self.send.at[step], self.recv.at[step],
            {WIDE: 2 * lax.rem(self.slow + step, self.slows) + self.fast},
        )

    def start(self):
        for step in range(1, self.slows):
            self.copy(step).start()

    def finish(self):
        total = self.sums[0].astype(F32)
        for step in range(1, self.slows):
            self.copy(step).wait()
            total = total + self.came[step].astype(F32)
        self.out[...] = total
        self.squares[...] = jnp.full(self.squares.shape, jnp.sum(total * total), F32)


def run(body, name, operands, outs, scratch, collective_id=None, loads=(), far_operands=()):
    given, taken = list(operands), []
    in_specs = [
        pl.BlockSpec(memory_space=pl.ANY) if k in far_operands else whole_vmem() for k in range(len(operands))
    ]
    for load in loads:
        places = []
        for operand, spec in zip(load.operands, load.in_specs):
            known = [k for k, other in enumerate(given) if other is operand]
            if not known:
                known = [len(given)]
                given.append(operand)
                in_specs.append(spec)
            places.append(known[0])
        taken.append(places)
    counts = [len(given), len(outs)] + [len(load.outs) for load in loads]
    counts += [len(scratch)] + [len(load.scratch) for load in loads]
    parts = 1 + len(loads)

    def kernel(*refs):
        groups, place = [], 0
        for count in counts:
            groups.append(refs[place : place + count])
            place += count
        for k, load in enumerate(loads):
            load.bind([groups[0][p] for p in taken[k]], groups[2 + k], groups[2 + parts + k])
        body(*groups[0][: len(operands)], *groups[1], *groups[1 + parts], carry=Carry(list(loads)))

    results = pl.pallas_call(
        kernel,
        out_shape=tuple(outs) + tuple(out for load in loads for out in load.outs),
        in_specs=in_specs,
        out_specs=(whole_vmem(),) * len(outs) + tuple(spec for load in loads for spec in load.out_specs),
        scratch_shapes=list(scratch) + [s for load in loads for s in load.scratch],
        compiler_params=pltpu.CompilerParams(
            collective_id=collective_id,
            has_side_effects=collective_id is not None,
            vmem_limit_bytes=VMEM_LIMIT,
        ),
        name=name,
    )(*given)
    return results[: len(outs)], results[len(outs) :]


def sems(kinds):
    return [pltpu.SemaphoreType.DMA((kinds, CHUNKS)), pltpu.SemaphoreType.DMA((kinds, CHUNKS))]


def norm_of(value, gain):
    scale = lax.rsqrt(jnp.mean(value * value, axis=-1, keepdims=True) + NORM_EPS)
    return value * scale * gain


def norm_back(grad, value, gain):
    scale = lax.rsqrt(jnp.mean(value * value, axis=-1, keepdims=True) + NORM_EPS)
    unit = value * scale
    scaled = grad * gain
    back = scale * (scaled - unit * jnp.mean(scaled * unit, axis=-1, keepdims=True))
    return (back, jnp.sum(grad * unit, axis=0, keepdims=True))


GELU_A = math.sqrt(2.0 / math.pi)
GELU_B = 0.044715


def gelu_of(x):
    return 0.5 * x * (1.0 + jnp.tanh(GELU_A * (x + GELU_B * (x * x * x))))


def gelu_slope(x):
    square = x * x
    t = jnp.tanh(GELU_A * (x + GELU_B * (x * square)))
    return 0.5 * (1.0 + t) + 0.5 * x * (1.0 - t * t) * (GELU_A * (1.0 + 3.0 * GELU_B * square))


def rows_at(start, j, chunk):
    return pl.ds(pl.multiple_of(start + j * chunk, chunk), chunk)


LANES = 128


def spread(row):
    return jnp.transpose(jnp.broadcast_to(row, (LANES, LANES)))


def feature_places(owner, width, share):
    lane = lax.broadcasted_iota(jnp.int32, (LANES, width), 0)
    feature = lax.broadcasted_iota(jnp.int32, (LANES, width), 1)
    return ((feature == lane + owner * share) & (lane < share)).astype(F32).astype(BF16)


def token_parts(ids, first):
    here = ids - first
    high = lax.shift_right_arithmetic(here, 7)
    place = lax.broadcasted_iota(jnp.int32, (LANES, ids.shape[1]), 0)
    return high, jnp.where(place == here - high * LANES, 1.0, 0.0).astype(BF16)


def embed_part(
    ids, counted, gains, steps, rates, table,
    resid, normed, gain_all, count_all, ids_all,
    low, extra, small, near_out, near_in, own, far_out, far_in, wide_out, wide_in, part_out, part_in,
    id_send, id_recv, small_send, small_recv, near_send, near_recv, far_send, far_recv, wide_send, wide_recv,
    part_send, part_recv, send, recv, carry,
):
    seq_len, width = normed.shape
    chunk = seq_len // 2 // CHUNKS
    quarter = seq_len // 4
    share, vocab = table.shape[1:]
    owners = ids_all.shape[0]
    sibling, partner, mine, other = group_places(seq_len)
    place = lax.axis_index(NARROW)
    side = lax.div(place, 2)
    me = lax.axis_index(WIDE)
    first = place * vocab
    around = [lax.rem(me + step, owners) for step in range(owners)]

    def id_copy(step):
        return remote(ids_all.at[me], ids_all.at[me], id_send.at[step], id_recv.at[step], {WIDE: around[step]})

    def small_copy(step):
        return remote(small.at[me], small.at[me], small_send.at[step], small_recv.at[step], {WIDE: around[step]})

    def near_copy(step):
        return remote(near_out.at[step], near_in.at[step], near_send.at[step], near_recv.at[step], sibling)

    def far_copy(step):
        return remote(far_out.at[step], far_in.at[step], far_send.at[step], far_recv.at[step], partner)

    def wide_copy(step):
        return remote(wide_out.at[step], wide_in.at[me], wide_send.at[step], wide_recv.at[step], {WIDE: around[step]})

    def part_copy(piece):
        rows = pl.ds(piece * LANES, LANES)
        return remote(part_out.at[rows], part_in.at[rows], part_send.at[piece], part_recv.at[piece], partner)

    ids_all[me] = ids[...]
    small[me] = jnp.zeros(small.shape[1:], F32)
    small[me, : gains.shape[0], : gains.shape[1]] = gains[...].astype(BF16).astype(F32)
    count = jnp.sum(counted[...].astype(F32), keepdims=True)
    small[me, gains.shape[0] : gains.shape[0] + 1, :] = jnp.broadcast_to(count, (1, small.shape[2]))
    greet([{WIDE: device} for device in around[1:]] + [sibling, partner])
    for step in range(1, owners):
        id_copy(step).start()
    for step in range(1, owners):
        small_copy(step).start()
    carry.begin(0, 1)
    parts = vocab // LANES
    for part in range(parts):
        low[part * share : (part + 1) * share, :] = table[0, :, part * LANES : (part + 1) * LANES].astype(BF16)
    core = lax.rem(place, 2)

    def look_up(step):
        row = lax.rem(me + step, owners)

        def find(which):
            high, picks = token_parts(ids_all[row, pl.ds(which, 1), :], first)
            found = dot_nn(low[...], picks)
            total = jnp.zeros((share, quarter), F32)
            for part in range(parts):
                total = total + jnp.where(high == part, found[part * share : (part + 1) * share, :], 0.0)
            return total.astype(BF16)

        for k in range(2):
            near_out[step, k] = find(2 * (1 - core) + k)
        near_copy(step).start()
        for k in range(2):
            own[step, k] = find(2 * core + k)

    def halve(step):
        near_copy(step).wait_recv()
        own[step] = own[step] + near_in[step]
        far_out[step] = own[step, 1 - side]
        far_copy(step).start()

    def deliver(step):
        far_copy(step).wait_recv()
        total = own[step, side] + far_in[step]
        if step % owners == 0:
            wide_in[me] = total
        else:
            wide_out[step] = total
            wide_copy(step).start()

    order = list(range(1, owners)) + [0]
    for turn in range(owners + 2):
        if turn < owners:
            if order[turn]:
                id_copy(owners - order[turn]).wait_recv()
            look_up(order[turn])
        if 1 <= turn < owners + 1:
            halve(order[turn - 1])
        if turn >= 2:
            deliver(order[turn - 2])
        if turn == 1:
            carry.begin(2)
    carry.begin(3)
    carry.hand_on(0, 1)
    for step in range(1, owners):
        small_copy(step).wait_recv()
    total = None
    for owner in range(owners):
        part = dot_nn(small[owner].astype(BF16), feature_places(owner, width, share))
        total = part if total is None else total + part
    gain_all[...] = total
    count_all[...] = jnp.sum(small[...], axis=0)
    half_width = width // 2
    for k in range(seq_len // 2 // LANES):
        when = spread(steps[pl.ds(mine // LANES + k, 1), :].astype(F32))
        for t in range(half_width // LANES):
            columns = slice(t * LANES, (t + 1) * LANES)
            angles = when * rates[:, columns]
            rows = slice(k * LANES, (k + 1) * LANES)
            extra[rows, t * LANES : (t + 1) * LANES] = jnp.sin(angles)
            extra[rows, half_width + t * LANES : half_width + (t + 1) * LANES] = jnp.cos(angles)
    for step in range(1, owners):
        wide_copy(step).wait_recv()
    found = jnp.transpose(wide_in[...].reshape(width, quarter))
    pieces = quarter // LANES
    at_side = pl.multiple_of(side * quarter, quarter)
    at_other = pl.multiple_of((1 - side) * quarter, quarter)
    for piece in range(pieces):
        rows = pl.ds(piece * LANES, LANES)
        part_out[rows, :] = found[piece * LANES : (piece + 1) * LANES, :]
        part_copy(piece).start()

    def finish(start, source, piece):
        rows = rows_at(start, piece, LANES)
        x = math.sqrt(width) * source[pl.ds(piece * LANES, LANES), :].astype(F32) + extra[rows, :]
        resid[rows, :] = x
        here = rows_at(mine + start, piece, LANES)
        normed[here, :] = norm_of(x, gain_all[0:1, :]).astype(BF16)
        give_rows(here, piece if source is part_out else pieces + piece).start()

    def give_rows(here, k):
        return remote(normed.at[here], normed.at[here], send.at[0, k], recv.at[0, k], sibling)

    for piece in range(pieces):
        finish(at_side, part_out, piece)
    for piece in range(pieces):
        part_copy(piece).wait_recv()
        finish(at_other, part_in, piece)
    carry.hand_on(2)
    for k in range(2 * pieces):
        give_rows(rows_at(mine, k % pieces, LANES), k).wait()
    for step in range(owners):
        near_copy(step).wait_send()
        far_copy(step).wait_send()
        if step:
            id_copy(step).wait_send()
            small_copy(step).wait_send()
            wide_copy(step).wait_send()
    for piece in range(pieces):
        part_copy(piece).wait_send()


QUERY_BLOCK = 256


def forward_part(
    layer, weights, points, normed, key_seg, query_seg, resid, gains,
    projected, mixed, middle, normed_two, result, normed_next,
    bias, values_t, near_out, near_in, far_out, far_in, near_out2, near_in2, far_out2, far_in2, own2, send, recv,
):
    w_query, w_out, w_in, w_red = weights
    at_half, at_feed, at_sent, at_last = points
    seq_len, width = normed.shape
    chunk = seq_len // 2 // CHUNKS
    block = bias.shape[1]
    heads = mixed.shape[1] // HD
    sibling, partner, mine, other = group_places(seq_len)
    pair = (send, recv)
    first = Exchange((near_out, near_in, far_out, far_in), pair, 0, sibling, partner)
    second = Exchange((near_out2, near_in2, far_out2, far_in2), pair, 2, sibling, partner)
    share = Share(normed_two, pair, 4, sibling, mine, chunk)
    share_next = Share(normed_next, pair, 5, sibling, mine, chunk)

    def ask(i, _):
        rows = rows_at(0, i, block)
        for which in range(3):
            projected[which, rows, :] = dot_nn(normed[rows, :], w_query(which)).astype(BF16)
        return 0

    lax.fori_loop(0, seq_len // block, ask, 0)
    values_t[...] = jnp.transpose(projected[2])

    def attend_rows(start):
        rows = pl.ds(pl.multiple_of(start, block), block)
        bias[...] = jnp.where(key_seg[...] == query_seg[:, rows], 0.0, -1e30)
        asked = projected[0, rows, :] * HD ** (-0.5)
        parts = []
        for head in range(heads):
            scores = dot_nt(projected[1], head_lanes(asked, head, HD)) + bias[...]
            powers = jnp.exp(scores - jnp.max(scores, axis=0, keepdims=True))
            probs = (powers * (1.0 / jnp.sum(powers, axis=0, keepdims=True))).astype(BF16)
            parts.append(dot_nn(values_t[head * HD : (head + 1) * HD, :], probs))
        mixed[rows, :] = jnp.transpose(jnp.concatenate(parts, axis=0)).astype(BF16)

    def project(start, j):
        return dot_nt(mixed[rows_at(start, j, chunk), :], w_out())

    def feed(rows):
        pre = dot_nn(normed_two[rows, :], w_in())
        return dot_nt(gelu_of(pre).astype(BF16), w_red())

    per_block = block // chunk
    for part in range(CHUNKS // per_block):

        def both(i, _):
            attend_rows(jnp.where(i == 0, other, mine) + part * block)
            return 0

        lax.fori_loop(0, 2, both, 0)
        for j in range(part * per_block, (part + 1) * per_block):
            first.give(j, project(other, j))
        if part == 0:
            at_half()
        for j in range(part * per_block, (part + 1) * per_block):
            first.pass_on(j, project(mine, j))
    at_feed()
    for j in range(CHUNKS):
        rows = rows_at(0, j, chunk)
        mid = resid[rows, :] + first.take(j)
        middle[rows, :] = mid
        share.put(j, norm_of(mid, gains[2 * layer + 1 : 2 * layer + 2, :]).astype(BF16))
        own2[j] = feed(rows_at(mine, j, chunk))
        share.arrived(j)
        second.give(j, feed(rows_at(other, j, chunk)))
        if j >= 1:
            second.pass_on(j - 1, own2[j - 1])
    second.pass_on(CHUNKS - 1, own2[CHUNKS - 1])
    at_sent()
    for j in range(CHUNKS):
        rows = rows_at(0, j, chunk)
        x = middle[rows, :] + second.take(j)
        result[rows, :] = x
        share_next.put(j, norm_of(x, gains[2 * layer + 2 : 2 * layer + 3, :]).astype(BF16))
        if j == CHUNKS - 2:
            at_last()
    for j in range(CHUNKS):
        share_next.arrived(j)
    for part in (first, second, share, share_next):
        part.close()


def layer_outs(seq_len, width, heads_width):
    return [
        jax.ShapeDtypeStruct((3, seq_len, heads_width), BF16),
        jax.ShapeDtypeStruct((seq_len, heads_width), BF16),
        jax.ShapeDtypeStruct((seq_len // 2, width), F32),
        jax.ShapeDtypeStruct((seq_len, width), BF16),
    ]


def layer_scratch(seq_len, width, heads_width):
    half, chunk = seq_len // 2, seq_len // 2 // CHUNKS
    block = max(chunk, min(QUERY_BLOCK, half))
    return (
        [pltpu.VMEM((seq_len, block), F32), pltpu.VMEM((heads_width, seq_len), BF16)]
        + Exchange.scratch(chunk, width, FORWARD_KIND)
        + Exchange.scratch(chunk, width, FORWARD_KIND)
        + [pltpu.VMEM((CHUNKS, chunk, width), F32)]
        + sems(6)
    )


LAYER_SCRATCH = 13


def front_kernel(
    ids, counted, gains, steps, rates, table, key_seg, query_seg,
    resid, normed, gain_all, count_all, ids_all, projected, mixed, middle, normed_two, result, normed_next,
    *scratch, carry,
):
    embed_part(
        ids, counted, gains, steps, rates, table, resid, normed, gain_all, count_all, ids_all,
        *scratch[:-LAYER_SCRATCH], carry,
    )
    carry.end(0, 1)
    later = list(carry.all())[4:]

    def at_half():
        carry.hand_on(3)
        carry.begin(*later[:2])

    def at_feed():
        carry.end(2, 3)
        carry.begin(*later[2:])

    forward_part(
        0,
        [carry.loads[0].value] + [load.value for load in carry.loads[1:4]],
        (at_half, at_feed, lambda: carry.hand_on(*later[:2]), lambda: carry.hand_on(*later[2:3])),
        normed, key_seg, query_seg, resid, gain_all,
        projected, mixed, middle, normed_two, result, normed_next, *scratch[-LAYER_SCRATCH:],
    )
    carry.end(*later)


def front(ids, counted, gains, steps, rates, tables, key_seg, query_seg, owners, heads_width, collective_id, loads):
    seq_len = ids.size
    share, vocab = tables.shape[1:]
    half, width = seq_len // 2, owners * share
    dma = pltpu.SemaphoreType.DMA
    return run(
        front_kernel,
        "front",
        [ids, counted, gains, steps, rates, tables, key_seg, query_seg],
        [
            jax.ShapeDtypeStruct((half, width), F32),
            jax.ShapeDtypeStruct((seq_len, width), BF16),
            jax.ShapeDtypeStruct((8, width), F32),
            jax.ShapeDtypeStruct((8, LANES), F32),
            jax.ShapeDtypeStruct((owners,) + ids.shape, jnp.int32),
        ]
        + layer_outs(seq_len, width, heads_width)
        + [jax.ShapeDtypeStruct((half, width), F32), jax.ShapeDtypeStruct((seq_len, width), BF16)],
        [
            pltpu.VMEM((vocab // LANES * share, LANES), BF16),
            pltpu.VMEM((half, width), F32),
            pltpu.VMEM((owners, 8, LANES), F32),
        ]
        + [pltpu.VMEM((owners, 2, share, half // 2), BF16)] * 3
        + [pltpu.VMEM((owners, share, half // 2), BF16)] * 4
        + [
            pltpu.VMEM((half // 2, width), BF16),
            pltpu.VMEM((half // 2, width), BF16),
        ]
        + [dma((owners,))] * 10
        + [dma((half // 2 // LANES,))] * 2
        + [dma((1, half // LANES))] * 2
        + layer_scratch(seq_len, width, heads_width),
        collective_id,
        loads,
    )


TILE = 256


def weight_grad(left_t, right, out):
    columns = right.shape[1]
    tile = TILE if columns % TILE == 0 else columns

    def put(where):
        value = dot_nn(left_t[...], right[:, where]).astype(out.dtype)
        if len(out.shape) == 3:
            out[:, :, where] = value.reshape(out.shape[:2] + (tile,))
        else:
            out[:, where] = value

    def step(i, _):
        put(pl.ds(pl.multiple_of(i * tile, tile), tile))
        return 0

    if tile == columns:
        put(slice(None))
    else:
        lax.fori_loop(0, columns // tile, step, 0)


def head_lanes(value, head, size):
    lanes = lax.broadcasted_iota(jnp.int32, value.shape, 1)
    inside = (lanes >= head * size) & (lanes < (head + 1) * size)
    return jnp.where(inside, value, jnp.zeros_like(value))


def backward_kernel(
    layer, scale, points, grad, branch, w_red, w_in, w_out, normed_two, middle, gains, mixed,
    projected, key_seg, query_seg, w_query, resid, normed,
    grad_out, branch_out, d_out, d_query, gain_two, gain_one,
    d_red, d_in, grad_middle, grad_attn, grad_mixed, grad_projected, grad_before, after, turned,
    bias, keys_t, grad_keys, grad_values,
    near_out, near_in, far_out, far_in, far_out2, far_in2, send, recv, loaded, carry,
):
    at_start, at_made, at_summed, at_attended, at_sent = points
    seq_len, width = normed_two.shape
    chunk = seq_len // 2 // CHUNKS
    sibling, partner, mine, other = group_places(seq_len)
    greet([sibling, partner] + carry.peers())
    at_start(carry, d_red, d_in)
    pair = (send, recv)
    trade = Exchange((near_out, near_in, far_out, far_in), pair, 0, sibling, partner)
    share = Share(grad_attn, pair, 2, sibling, mine, chunk)

    def ffn_partial(start, j):
        rows = rows_at(start, j, chunk)
        pre = dot_nn(normed_two[rows, :], w_in[...])
        after[rows, :] = gelu_of(pre).astype(BF16)
        low = (dot_nn(branch[rows, :], w_red[...]) * gelu_slope(pre)).astype(BF16)
        grad_before[rows, :] = low
        return dot_nt(low, w_in[...])

    trade.give(0, ffn_partial(other, 0))
    for j in range(CHUNKS):
        if j + 1 < CHUNKS:
            trade.give(j + 1, ffn_partial(other, j + 1))
        trade.pass_on(j, ffn_partial(mine, j))
    turned[...] = jnp.transpose(branch[...])
    weight_grad(turned, after, d_red)
    turned[...] = jnp.transpose(normed_two[...])
    weight_grad(turned, grad_before, d_in)
    at_made(carry)
    fetch = pltpu.make_async_copy(normed, after, loaded)
    fetch.start()
    total = jnp.zeros((1, width), F32)
    for j in range(CHUNKS):
        rows = rows_at(0, j, chunk)
        back, part = norm_back(trade.take(j), middle[rows, :], gains[2 * layer + 1 : 2 * layer + 2, :])
        total = total + part
        back = back + grad[rows, :]
        grad_middle[rows, :] = back
        share.put(j, back.astype(BF16))
        here = rows_at(mine, j, chunk)
        grad_mixed[here, :] = dot_nn(grad_attn[here, :], w_out[...]).astype(BF16)
    gain_two[...] = total
    for j in range(CHUNKS):
        share.arrived(j)
        here = rows_at(other, j, chunk)
        grad_mixed[here, :] = dot_nn(grad_attn[here, :], w_out[...]).astype(BF16)
    trade.close()
    share.close()
    at_summed(carry)

    block = bias.shape[1]
    heads = grad_mixed.shape[1] // HD
    keys_t[...] = jnp.transpose(projected[1])
    grad_keys[...] = jnp.zeros(grad_keys.shape, F32)
    grad_values[...] = jnp.zeros(grad_values.shape, F32)

    def queries(i, _):
        rows = rows_at(0, i, block)
        bias[...] = jnp.where(key_seg[...] == query_seg[:, rows], 0.0, -1e30)
        asked = projected[0, rows, :] * HD ** (-0.5)
        given = grad_mixed[rows, :]
        parts = []
        for head in range(heads):
            query = head_lanes(asked, head, HD)
            wanted = head_lanes(given, head, HD)
            scores = dot_nt(projected[1], query) + bias[...]
            powers = jnp.exp(scores - jnp.max(scores, axis=0, keepdims=True))
            probs = powers * (1.0 / jnp.sum(powers, axis=0, keepdims=True))
            grad_probs = dot_nt(projected[2], wanted)
            centre = jnp.sum(probs * grad_probs, axis=0, keepdims=True)
            grad_scores = (probs * (grad_probs - centre)).astype(BF16)
            parts.append(dot_nn(keys_t[head * HD : (head + 1) * HD, :], grad_scores))
            grad_keys[...] += dot_nn(grad_scores, query)
            grad_values[...] += dot_nn(probs.astype(BF16), wanted)
        grad_projected[0, rows, :] = (jnp.transpose(jnp.concatenate(parts, axis=0)) * HD ** (-0.5)).astype(BF16)
        return 0

    lax.fori_loop(0, seq_len // block, queries, 0)
    grad_projected[1] = grad_keys[...].astype(BF16)
    grad_projected[2] = grad_values[...].astype(BF16)
    at_attended(carry)

    trade = Exchange((near_out, near_in, far_out2, far_in2), pair, 3, sibling, partner)
    share = Share(branch_out, pair, 5, sibling, mine, chunk)

    def query_partial(start, j):
        rows = rows_at(start, j, chunk)
        found = None
        for which in range(3):
            part = dot_nt(grad_projected[which, rows, :], w_query[which])
            found = part if found is None else found + part
        return found

    trade.give(0, query_partial(other, 0))
    for j in range(CHUNKS):
        if j + 1 < CHUNKS:
            trade.give(j + 1, query_partial(other, j + 1))
        trade.pass_on(j, query_partial(mine, j))
    turned[...] = jnp.transpose(grad_attn[...])
    weight_grad(turned, mixed, d_out)
    fetch.wait()
    turned[...] = jnp.transpose(after[...])
    for which in range(3):
        weight_grad(turned, grad_projected.at[which], d_query.at[which])
    at_sent(carry, d_out)
    total = jnp.zeros((1, width), F32)
    for j in range(CHUNKS):
        rows = rows_at(0, j, chunk)
        back, part = norm_back(trade.take(j), resid[rows, :], gains[2 * layer : 2 * layer + 1, :])
        total = total + part
        back = back + grad_middle[rows, :]
        grad_out[rows, :] = back
        share.put(j, (back if scale is None else scale * back).astype(BF16))
    gain_one[...] = total
    for j in range(CHUNKS):
        share.arrived(j)
    trade.close()
    share.close()
    carry.end(*carry.all())


def backward_block(
    layer, scale, points, grad, branch, w_red, w_in, w_out, normed_two, middle, gains, mixed,
    projected, key_seg, query_seg, w_query, resid, normed, owners, collective_id, loads,
):
    seq_len, width = normed_two.shape
    hidden, heads_width = w_in.shape[1], w_query.shape[2]
    half, chunk = seq_len // 2, seq_len // 2 // CHUNKS
    block = min(QUERY_BLOCK, seq_len)
    far = pltpu.VMEM((CHUNKS, chunk, width), BACKWARD_KIND)
    return run(
        functools.partial(backward_kernel, layer, scale, points),
        "backward_block",
        [grad, branch, w_red, w_in, w_out, normed_two, middle, gains, mixed]
        + [projected, key_seg, query_seg, w_query, resid, normed],
        [
            jax.ShapeDtypeStruct((half, width), F32),
            jax.ShapeDtypeStruct((seq_len, width), BF16),
            jax.ShapeDtypeStruct((owners, width // owners, heads_width), BF16),
            jax.ShapeDtypeStruct((3, owners, width // owners, heads_width), BF16),
            jax.ShapeDtypeStruct((1, width), F32),
            jax.ShapeDtypeStruct((1, width), F32),
        ],
        [pltpu.VMEM((owners, width // owners, hidden), BF16)] * 2
        + [
            pltpu.VMEM((half, width), F32),
            pltpu.VMEM((seq_len, width), BF16),
            pltpu.VMEM((seq_len, heads_width), BF16),
            pltpu.VMEM((3, seq_len, heads_width), BF16),
            pltpu.VMEM((seq_len, hidden), BF16),
            pltpu.VMEM((seq_len, width), BF16),
            pltpu.VMEM((width, seq_len), BF16),
            pltpu.VMEM((seq_len, block), F32),
            pltpu.VMEM((heads_width, seq_len), BF16),
            pltpu.VMEM((seq_len, heads_width), F32),
            pltpu.VMEM((seq_len, heads_width), F32),
        ]
        + Exchange.scratch(chunk, width, BACKWARD_KIND)
        + [far, far]
        + sems(6)
        + [pltpu.SemaphoreType.DMA],
        collective_id,
        loads,
        far_operands=(14,),
    )


def to_rows(columns):
    lanes = lax.broadcasted_iota(jnp.int32, (LANES, LANES), 1)
    total = jnp.zeros((LANES, LANES), F32)
    for k, column in enumerate(columns):
        total = jnp.where(lanes == k, column, total)
    return jnp.transpose(total)[:8, :]


def loss_part(
    row, normed, info, value, gain, table_loads, grad_out, branch, d_gain, losses, d_tables,
    logits, grads, places, turned, stat_out, stat_in, sum_out, sum_in,
    stat_send, stat_recv, sum_send, sum_recv, near_out, near_in, far_out, far_in, send, recv,
):
    seq_len, width = normed.shape
    chunk = seq_len // 2 // CHUNKS
    piece_width = table_loads[0].out.shape[-1]
    vocab = piece_width * len(table_loads)
    tiles = vocab // LANES
    blocks = seq_len // LANES
    me = lax.axis_index(NARROW)
    sibling, partner, mine, other = group_places(seq_len)
    peers = [{NARROW: lax.rem(me + k, 4)} for k in range(1, 4)]
    sems = (send, recv)
    trade = Exchange((near_out, near_in, far_out, far_in), sems, 0, sibling, partner)
    share = Share(branch, sems, 2, sibling, mine, chunk)
    first = (me * vocab).astype(F32)
    whole = 4.0 * vocab
    lanes = lax.broadcasted_iota(jnp.int32, (LANES, LANES), 1).astype(F32)

    def stat_copy(b, k):
        return remote(stat_out.at[b], stat_in.at[k, b], stat_send.at[k, b], stat_recv.at[k, b], peers[k])

    def sum_copy(b, k):
        return remote(sum_out.at[b], sum_in.at[k, b], sum_send.at[k, b], sum_recv.at[k, b], peers[k])

    def tile_at(t):
        return pl.ds(pl.multiple_of(t * LANES, LANES), LANES)

    def ask(b, _):
        rows = rows_at(0, b, LANES)
        here = info[:, rows]
        at_noised = spread(here[0:1] - first)
        at_clean = spread(here[1:2] - first)
        places[b, 0] = at_noised
        places[b, 1] = at_clean

        def top_step(t, top):
            return jnp.maximum(top, logits[rows, tile_at(t)])

        top = lax.fori_loop(1, tiles, top_step, logits[rows, tile_at(0)], unroll=4)
        top = jnp.max(top, axis=1, keepdims=True)
        top_wide = jnp.broadcast_to(top, (LANES, LANES))

        def sum_step(t, totals):
            powers, noised, clean = totals
            piece = logits[rows, tile_at(t)]
            column = lanes + (t * LANES).astype(F32)
            return (
                powers + jnp.exp(piece - top_wide),
                noised + jnp.where(column == at_noised, piece, 0.0),
                clean + jnp.where(column == at_clean, piece, 0.0),
            )

        zero = jnp.zeros((LANES, LANES), F32)
        totals = lax.fori_loop(0, tiles, sum_step, (zero, zero, zero), unroll=2)
        stat_out[b] = to_rows([top] + [jnp.sum(total, axis=1, keepdims=True) for total in totals])
        for k in range(3):
            stat_copy(b, k).start()
        return 0

    for k, table in enumerate(table_loads):
        if k == len(table_loads) - 1:
            table.finish()

        def product(i, _):
            rows = rows_at(0, i, TILE)
            logits[rows, k * piece_width : (k + 1) * piece_width] = dot_nn(normed[rows, :], table.value())
            return 0

        lax.fori_loop(0, seq_len // TILE, product, 0)
    lax.fori_loop(0, blocks, ask, 0)

    def scalars(b):
        here = info[:, rows_at(0, b, LANES)]
        step = jnp.maximum(here[2:3], 2.0)
        left = STEPS - step + 1.0
        beta = 1.0 / left
        keep = left / STEPS
        rest = (step - 1.0) / (STEPS * whole)
        own = stat_out[b]
        others = [stat_in[k, b] for k in range(3)]
        top = own[0:1]
        for stat in others:
            top = jnp.maximum(top, stat[0:1])
        total = own[1:2] * jnp.exp(own[0:1] - top)
        noised, clean = own[2:3], own[3:4]
        for stat in others:
            total = total + stat[1:2] * jnp.exp(stat[0:1] - top)
            noised, clean = noised + stat[2:3], clean + stat[3:4]
        return here, beta, keep, rest, top + jnp.log(total), noised, clean

    def measure(b, _):
        rows = rows_at(0, b, LANES)
        for k in range(3):
            stat_copy(b, k).wait_recv()
        _, _, keep, rest, log_total, _, _ = scalars(b)
        log_wide = spread(log_total)
        ratio = spread(keep / rest)

        def step(t, totals):
            logs, shares = totals
            probs = jnp.exp(logits[rows, tile_at(t)] - log_wide)
            logits[rows, tile_at(t)] = probs
            grown = 1.0 + probs * ratio
            return (logs + jnp.log(grown), shares + probs / grown)

        zero = jnp.zeros((LANES, LANES), F32)
        totals = lax.fori_loop(0, tiles, step, (zero, zero), unroll=2)
        sum_out[b] = to_rows([jnp.sum(total, axis=1, keepdims=True) for total in totals])
        for k in range(3):
            sum_copy(b, k).start()
        return 0

    lax.fori_loop(0, blocks, measure, 0)

    def pull(b):
        rows = rows_at(0, b, LANES)
        for k in range(3):
            sum_copy(b, k).wait_recv()
        here, beta, keep, rest, log_total, noised, clean = scalars(b)
        sums = sum_out[b] + sum_in[0, b] + sum_in[1, b] + sum_in[2, b]
        log_sum, share_sum = sums[0:1], sums[1:2] / rest
        same = here[0:1] == here[1:2]
        first_step = here[2:3] == 1.0
        base_a, more_a = beta / whole, 1.0 - beta
        base_w = base_a * rest
        joint = whole * base_w + more_a * rest + base_a * keep + jnp.where(same, more_a * keep, 0.0)
        ratio = keep / rest
        prob_n, prob_c = jnp.exp(noised - log_total), jnp.exp(clean - log_total)
        grown_n, grown_c = 1.0 + prob_n * ratio, 1.0 + prob_c * ratio
        marginal_n, marginal_c = rest * grown_n, rest * grown_c
        log_n, log_c = jnp.log(grown_n), jnp.log(grown_c)
        weight_n = jnp.where(same, 0.0, more_a * rest)
        weight_c = jnp.where(same, more_a * rest + base_a * keep + more_a * keep, base_a * keep)
        lift = jnp.log((keep + rest) / rest)
        cross = -base_w * log_sum - weight_n * log_n - weight_c * log_c + (base_w + weight_c) * lift
        model = base_a * (keep + whole * rest) + more_a * marginal_n
        divergence = cross / joint - jnp.log(joint) + jnp.log(model)
        loss = jnp.where(first_step, log_total - clean, divergence)
        losses[:, rows] = here[4:5] * loss
        weighted = base_w * share_sum + weight_n * prob_n / marginal_n + weight_c * prob_c / marginal_c
        aligned = base_a + more_a * prob_n
        centre = keep * (aligned / model - weighted / joint)
        scale = here[3:4]
        zero = jnp.zeros_like(scale)
        even = scale * jnp.where(first_step, 1.0, keep * base_a / model - centre)
        bent = scale * jnp.where(first_step, zero, -keep * base_w / joint / rest)
        at_n = prob_n * keep * (more_a / model - weight_n / joint / marginal_n)
        at_c = -prob_c * keep * (weight_c / joint / marginal_c)
        extra_n = spread(scale * jnp.where(first_step, zero, at_n))
        extra_c = spread(scale * jnp.where(first_step, -1.0, at_c))
        even, bent, ratio = spread(even), spread(bent), spread(ratio)
        at_noised, at_clean = places[b, 0], places[b, 1]

        def step(t, _):
            probs = logits[rows, tile_at(t)]
            column = lanes + (t * LANES).astype(F32)
            grad = probs * (even + bent / (1.0 + probs * ratio))
            grad = grad + jnp.where(column == at_noised, extra_n, 0.0)
            grad = grad + jnp.where(column == at_clean, extra_c, 0.0)
            grads[rows, tile_at(t)] = grad.astype(BF16)
            return 0

        lax.fori_loop(0, tiles, step, 0, unroll=2)

    def partial(start, j):
        base = start // LANES + j * (chunk // LANES)
        for b in range(chunk // LANES):
            pull(base + b)
        total = None
        for k, table in enumerate(table_loads):
            part = dot_nt(grads[rows_at(start, j, chunk), k * piece_width : (k + 1) * piece_width], table.value())
            total = part if total is None else total + part
        return total

    trade.give(0, partial(other, 0))
    for j in range(CHUNKS):
        if j + 1 < CHUNKS:
            trade.give(j + 1, partial(other, j + 1))
        trade.pass_on(j, partial(mine, j))
    turned[...] = jnp.transpose(normed[...])
    for k, d_table in enumerate(d_tables):
        weight_grad(turned, grads.at[:, k * piece_width : (k + 1) * piece_width], d_table)
    gain_total = jnp.zeros((1, gain.shape[1]), F32)
    for j in range(CHUNKS):
        rows = rows_at(0, j, chunk)
        back, gain_part = norm_back(trade.take(j), value[rows, :], gain[row : row + 1, :])
        gain_total = gain_total + gain_part
        grad_out[rows, :] = back
        share.put(j, back.astype(BF16))
    d_gain[...] = gain_total
    for j in range(CHUNKS):
        share.arrived(j)
    trade.close()
    share.close()

    def finish(b, _):
        for k in range(3):
            stat_copy(b, k).wait_send()
            sum_copy(b, k).wait_send()
        return 0

    lax.fori_loop(0, blocks, finish, 0)


def back_kernel(
    layer, normed, key_seg, query_seg, resid, w_query, w_out, w_in, gains, info,
    projected, mixed, middle, normed_two, grad_out, branch, d_gain, losses, *refs, carry,
):
    pieces = len(carry.loads) - 1
    d_tables, refs = refs[:pieces], refs[pieces:]
    (result, normed_next), refs = refs[:2], refs[2:]
    loss_scratch, layer_refs = refs[:-LAYER_SCRATCH], refs[-LAYER_SCRATCH:]
    me = lax.axis_index(NARROW)
    greet([{NARROW: lax.rem(me + k, 4)} for k in range(1, 4)] + carry.peers())
    carry.begin(0, 1)

    def at_half():
        carry.begin(2)

    def at_feed():
        carry.end(0)
        carry.hand_on(1)
        carry.begin(3)

    def at_sent():
        carry.hand_on(2)
        carry.begin(4)

    def at_last():
        carry.hand_on(3)

    forward_part(
        layer,
        [lambda which: w_query[which], lambda: w_out[...], lambda: w_in[...], carry.loads[0].value],
        (at_half, at_feed, at_sent, at_last),
        normed, key_seg, query_seg, resid, gains,
        projected, mixed, middle, normed_two, result, normed_next, *layer_refs,
    )
    carry.hand_on(4)
    carry.end(1, 2, 3)
    loss_part(
        2 * layer + 2, normed_next, info, result, gains, carry.loads[1:], grad_out, branch, d_gain, losses, d_tables,
        *loss_scratch, *layer_refs[2:6], *layer_refs[-2:],
    )


def last_and_loss(
    layer, normed, key_seg, query_seg, resid, w_query, w_out, w_in, gains, info, vocab, collective_id, loads
):
    seq_len, width = normed.shape
    heads_width = w_query.shape[2]
    half, blocks = seq_len // 2, seq_len // LANES
    pieces = len(loads) - 1
    return run(
        functools.partial(back_kernel, layer),
        "last_and_loss",
        [normed, key_seg, query_seg, resid, w_query, w_out, w_in, gains, info],
        layer_outs(seq_len, width, heads_width)
        + [
            jax.ShapeDtypeStruct((half, width), F32),
            jax.ShapeDtypeStruct((seq_len, width), BF16),
            jax.ShapeDtypeStruct((1, width), F32),
            jax.ShapeDtypeStruct((1, seq_len), F32),
        ]
        + [jax.ShapeDtypeStruct((width, vocab // pieces), BF16)] * pieces,
        [
            pltpu.VMEM((half, width), F32),
            pltpu.VMEM((seq_len, width), BF16),
            pltpu.VMEM((seq_len, vocab), F32),
            pltpu.VMEM((seq_len, vocab), BF16),
            pltpu.VMEM((blocks, 2, LANES, LANES), F32),
            pltpu.VMEM((width, seq_len), BF16),
            pltpu.VMEM((blocks, 8, LANES), F32),
            pltpu.VMEM((3, blocks, 8, LANES), F32),
            pltpu.VMEM((blocks, 8, LANES), F32),
            pltpu.VMEM((3, blocks, 8, LANES), F32),
        ]
        + [pltpu.SemaphoreType.DMA((3, blocks))] * 4
        + layer_scratch(seq_len, width, heads_width),
        collective_id,
        loads,
    )


def sum_ways(place, me, slow, fast, slows, group):
    near = [{NARROW: lax.rem(place + step, group)} for step in range(1, group)]
    return near, {WIDE: me + 1 - 2 * fast}


def tail_kernel(
    layers, branch, ids_all, losses, full, *refs, carry,
):
    gain_parts, refs = refs[: 2 * layers + 1], refs[2 * layers + 1 :]
    squares, refs = refs[: len(refs) - 32], refs[len(refs) - 32 :]
    tail_body(branch, ids_all, losses, full, gain_parts, squares, *refs, carry)


def tail_body(
    branch, ids_all, losses, full, gain_parts, squares,
    d_table, d_full, d_small, scalars,
    out_blocks, all_in, masked, picks, total, gains_out, gains_in, blocks, block_in, line_out, line_in,
    fast_in, sums, slow_in, near, along, across,
    wide_send, wide_recv, far_send, far_recv, near_send, near_recv,
    pair_send, pair_recv, line_send, line_recv, sum_sems,
    carry,
):
    seq_len, width = branch.shape
    quarter, half = seq_len // 4, seq_len // 2
    owners = ids_all.shape[0]
    share, vocab = d_table.shape
    sibling, partner, mine, other = group_places(seq_len)
    place = lax.axis_index(NARROW)
    side = lax.div(place, 2)
    me, slow, fast, slows = wide_places(owners)
    beside = {WIDE: me + 1 - 2 * fast}
    group = near.shape[0]
    first = place * vocab
    around = [lax.rem(me + step, owners) for step in range(owners)]
    at_quarter = pl.multiple_of(mine + side * quarter, quarter)
    held = 2 * lax.rem(place, 2) + side

    def along_way(step):
        return {WIDE: 2 * lax.rem(slow + step, slows) + fast}

    def wide_copy(step):
        return remote(
            out_blocks.at[around[step]], all_in.at[me, held],
            wide_send.at[step], wide_recv.at[step], {WIDE: around[step]},
        )

    def far_copy(step):
        rows = all_in.at[around[step], held]
        return remote(rows, rows, far_send.at[step], far_recv.at[step], partner)

    def near_copy(step):
        rows = all_in.at[around[step], pl.ds(2 * lax.rem(place, 2), 2)]
        return remote(rows, rows, near_send.at[step], near_recv.at[step], sibling)

    def block(owner):
        return full.at[:, owner]

    def pair_copy(step):
        return remote(
            block(2 * lax.rem(slow + step, slows) + 1 - fast), fast_in.at[step],
            pair_send.at[step], pair_recv.at[step], beside,
        )

    def line_copy(step):
        return remote(sums.at[step], slow_in.at[step], line_send.at[step], line_recv.at[step], along_way(step))

    def gain_near():
        return remote(gains_out, gains_in, sum_sems.at[0, 0], sum_sems.at[1, 0], sibling)

    def gain_pair(step):
        return remote(
            blocks.at[2 * lax.rem(slow + step, slows) + 1 - fast], block_in.at[step],
            sum_sems.at[2, step], sum_sems.at[3, step], beside,
        )

    def gain_line(step):
        return remote(line_out.at[step], line_in.at[step], sum_sems.at[4, step], sum_sems.at[5, step], along_way(step))

    near_ways = [{NARROW: lax.rem(place + step, group)} for step in range(1, group)]
    greet([{WIDE: device} for device in around[1:]] + near_ways)
    for step in range(slows):
        pair_copy(step).start()
    gains_out[...] = jnp.zeros(gains_out.shape, F32)
    for row, part in enumerate(gain_parts):
        gains_out[row : row + 1, :] = part[...]
    gain_near().start()
    out_blocks[...] = jnp.transpose(branch[pl.ds(at_quarter, quarter), :]).reshape(out_blocks.shape)
    for step in range(1, owners):
        wide_copy(step).start()
    all_in[me, held] = out_blocks[me]
    carry.begin(*carry.all())
    gain_near().wait_recv()
    both = gains_out[...] + gains_in[...]
    for owner in range(owners):
        blocks[owner] = lax.dot_general(
            both, feature_places(owner, width, share).astype(F32), (((1,), (1,)), ((), ())),
            precision=lax.Precision.HIGHEST, preferred_element_type=F32,
        )
    for step in range(slows):
        gain_pair(step).start()

    def hand_on(step):
        if step:
            wide_copy(owners - step).wait_recv()
        far_copy(step).start()

    def hand_over(step):
        far_copy(step).wait_recv()
        near_copy(step).start()

    def gather_grad(step, first_turn):
        near_copy(step).wait_recv()
        row = around[step]

        for k in range(seq_len // quarter):
            columns = slice(k * quarter, (k + 1) * quarter)
            high, found = token_parts(ids_all[row, k : k + 1, :], first)
            picks[:, columns] = found
            grads = all_in[row, k]
            for part in range(vocab // LANES):
                inside = jnp.where(high == part, 1.0, 0.0).astype(BF16)
                masked[part * share : (part + 1) * share, columns] = grads * inside
        span = 4 * share

        def some(i, _):
            rows = rows_at(0, i, span)
            part = dot_nt(masked[rows, :], picks[...])
            total[rows, :] = part if first_turn else total[rows, :] + part
            return 0

        lax.fori_loop(0, total.shape[0] // span, some, 0)

    order = [0] + list(range(1, owners))
    for turn in range(owners + 2):
        if turn < owners:
            hand_on(order[turn])
        if 1 <= turn < owners + 1:
            hand_over(order[turn - 1])
        if turn == 1:
            for step in list(range(1, slows)) + [0]:
                pair_copy(step).wait_recv()
                owner = 2 * lax.rem(slow + step, slows) + fast
                sums[step] = (block(owner)[...].astype(F32) + fast_in[step].astype(F32)).astype(BF16)
                if step:
                    line_copy(step).start()
            for step in list(range(1, slows)) + [0]:
                gain_pair(step).wait_recv()
                line_out[step] = blocks[2 * lax.rem(slow + step, slows) + fast] + block_in[step]
                if step:
                    gain_line(step).start()
        if turn >= 2:
            gather_grad(order[turn - 2], turn == 2)
    for t in range(vocab // LANES):
        d_table[:, t * LANES : (t + 1) * LANES] = total[t * share : (t + 1) * share, :]
    result = sums[0].astype(F32)
    small = line_out[0]
    for step in range(1, slows):
        line_copy(step).wait_recv()
        result = result + slow_in[step].astype(F32)
        gain_line(step).wait_recv()
        small = small + line_in[step]
    d_full[...] = result
    d_small[...] = small
    carry.end(*carry.all())
    square = jnp.sum(result * result) + jnp.sum(d_table[...] * d_table[...])
    for part in squares:
        square = square + part[0, 0]
    for load in carry.loads:
        square = square + load.squares[0, 0]
    lead = (place == 0).astype(F32)
    square = square + lead * jnp.sum(small * small)
    lanes = lax.broadcasted_iota(jnp.int32, (8, LANES), 1)
    given = jnp.where(lanes == 0, square, jnp.where(lanes == 1, lead * jnp.sum(losses[...]), 0.0))

    def scalar_near(step):
        return remote(near.at[place], near.at[place], sum_sems.at[6, step], sum_sems.at[7, step], near_ways[step - 1])

    def scalar_line(step):
        return remote(along.at[slow], along.at[slow], sum_sems.at[8, step], sum_sems.at[9, step], along_way(step))

    near[place] = given
    for step in range(1, group):
        scalar_near(step).start()
    for step in range(1, group):
        scalar_near(step).wait()
    along[slow] = jnp.sum(near[...], axis=0)
    for step in range(1, slows):
        scalar_line(step).start()
    for step in range(1, slows):
        scalar_line(step).wait()
    across[0] = jnp.sum(along[...], axis=0)
    last = remote(across.at[0], across.at[1], sum_sems.at[10, 0], sum_sems.at[11, 0], beside)
    last.start()
    last.wait()
    scalars[...] = across[0] + across[1]
    gain_near().wait_send()
    for step in range(owners):
        far_copy(step).wait_send()
        near_copy(step).wait_send()
        if step:
            wide_copy(step).wait_send()
    for step in range(slows):
        pair_copy(step).wait_send()
        gain_pair(step).wait_send()
        if step:
            line_copy(step).wait_send()
            gain_line(step).wait_send()


def tail(branch, ids_all, losses, full, gain_parts, squares, share, vocab, group, collective_id, loads):
    seq_len, width = branch.shape
    owners = ids_all.shape[0]
    slows = owners // 2
    shape = full.shape[:1] + full.shape[2:]
    dma = pltpu.SemaphoreType.DMA
    small = (8, LANES)
    return run(
        functools.partial(tail_kernel, (len(gain_parts) - 1) // 2),
        "tail",
        [branch, ids_all, losses, full, *gain_parts, *squares],
        [
            jax.ShapeDtypeStruct((share, vocab), F32),
            jax.ShapeDtypeStruct(shape, F32),
            jax.ShapeDtypeStruct(small, F32),
            jax.ShapeDtypeStruct(small, F32),
        ],
        [
            pltpu.VMEM((owners, share, seq_len // 4), BF16),
            pltpu.VMEM((owners, 4, share, seq_len // 4), BF16),
            pltpu.VMEM((vocab // LANES * share, seq_len), BF16),
            pltpu.VMEM((LANES, seq_len), BF16),
            pltpu.VMEM((vocab // LANES * share, LANES), F32),
            pltpu.VMEM((8, width), F32),
            pltpu.VMEM((8, width), F32),
            pltpu.VMEM((owners,) + small, F32),
            pltpu.VMEM((slows,) + small, F32),
            pltpu.VMEM((slows,) + small, F32),
            pltpu.VMEM((slows,) + small, F32),
            pltpu.VMEM((slows,) + shape, BF16),
            pltpu.VMEM((slows,) + shape, BF16),
            pltpu.VMEM((slows,) + shape, BF16),
            pltpu.VMEM((group,) + small, F32),
            pltpu.VMEM((slows,) + small, F32),
            pltpu.VMEM((2,) + small, F32),
        ]
        + [dma((owners,))] * 6
        + [dma((slows,))] * 4
        + [dma((12, max(slows, group)))],
        collective_id,
        loads,
    )


PIECES = 4
TABLE, ATTN_IN, ATTN_OUT, FFN_IN, FFN_OUT = range(5)


def shares_tile(wide, narrow, noised, attn_out, ffn_in, tables):
    rows, seq_len = noised.shape
    return (
        attn_out.shape[0] == 2
        and narrow == 4
        and wide % 2 == 0
        and rows == 1
        and seq_len % (2 * CHUNKS * 128) == 0
        and tables.shape[1] * wide % 256 == 0
        and attn_out.shape[1] % 16 == 0
        and attn_out.shape[1] <= LANES
        and ffn_in.shape[2] % 128 == 0
        and tables.shape[1] == attn_out.shape[1]
        and tables.shape[2] % (PIECES * TILE) == 0
    )


def per_device(wide, narrow, *arrays):
    noised, attn_out, ffn_in, tables = arrays[0], arrays[6], arrays[7], arrays[9]
    if shares_tile(wide, narrow, noised, attn_out, ffn_in, tables):
        return tiled_device(wide, *arrays)
    return general_device(*arrays)


def tiled_device(
    wide,
    noised,
    clean,
    timesteps,
    segments,
    counted,
    attn_in,
    attn_out,
    ffn_in,
    ffn_out,
    tables,
    gains,
    attn_in_mean,
    attn_out_mean,
    ffn_in_mean,
    ffn_out_mean,
    tables_mean,
    gains_mean,
    attn_in_square,
    attn_out_square,
    ffn_in_square,
    ffn_out_square,
    tables_square,
    gains_square,
):
    layers = attn_in.shape[0]
    gain_rows, gain_cols = gains.shape
    mask = counted.reshape(-1).astype(jnp.float32)
    seq_len = mask.shape[0]
    half = seq_len // 2
    core = lax.rem(lax.axis_index(NARROW), 2)
    share, vocab = tables.shape[1:]
    leads = (1, 0, 0, 0)
    four = (attn_in, attn_out, ffn_in, ffn_out)

    def joined(value, lead):
        return value.reshape(value.shape[:lead] + (-1,) + value.shape[lead + 2 :])

    step_flat = timesteps.reshape(-1)
    ids = noised.reshape(4, -1)
    steps = timesteps.reshape(-1, LANES)
    half_width = D // 2
    rates = jnp.exp(-math.log(10000.0) * jnp.arange(half_width, dtype=F32) / half_width)[None, :]
    quarter = vocab // PIECES
    windows = [(k * quarter, quarter) for k in range(PIECES)]
    key_seg, query_seg = segments.reshape(-1, 1), segments.reshape(1, -1)
    weights = (attn_in, attn_out, ffn_in, ffn_out)
    (residual, normed, gain_w, counts, ids_all, projected, mixed, middle, normed_two, result, normed_next), carried = front(
        ids, counted, gains, steps, rates, tables, key_seg, query_seg, wide, attn_out.shape[2], 0,
        [GatherLoad(value, 0, lead, wide, place=KEPT) for value, lead in zip(weights, leads)]
        + [GatherLoad(value, 1, lead, wide) for value, lead in zip(weights[:3], leads)]
        + [SlowLoad(ffn_out, 1, 0, wide)],
    )
    token_total = counts[gain_rows, 0]
    first_w = [joined(value, lead) for value, lead in zip(carried[:4], leads)]
    query_w, output_w, expand_w = [joined(value, lead) for value, lead in zip(carried[4:7], leads)]
    kept = [(residual, normed, projected, mixed, middle, normed_two, *first_w)]
    noised_flat, clean_flat = noised.reshape(-1), clean.reshape(-1)
    info = jnp.stack(
        [noised_flat.astype(F32), clean_flat.astype(F32), step_flat.astype(F32), mask / token_total, mask]
        + [jnp.zeros_like(mask)] * 3
    )
    (projected, mixed, middle, normed_two, grad, branch, gain_final, losses, *d_last), (reduce_w,) = last_and_loss(
        1, normed_next, key_seg, query_seg, result, query_w, output_w, expand_w, gain_w, info, vocab, 1,
        [FastLoad(carried[7], 0, wide)]
        + [GatherLoad(tables, 1, 0, wide, window, place=LOCAL) for window in windows],
    )
    kept.append(
        (result, normed_next, projected, mixed, middle, normed_two, query_w, output_w, expand_w, joined(reduce_w, 0))
    )
    own, squares = {}, []

    def by_owner(value, lead):
        shape = value.shape
        return value.reshape(shape[:lead] + (wide, shape[lead] // wide) + shape[lead + 1 :])

    def landed(key, results):
        own[key] = results[0]
        squares.append(results[1])
        return results[2:]

    hidden = ffn_in.shape[2]
    made = jax.ShapeDtypeStruct((wide, share, hidden), BF16)
    made_out = jax.ShapeDtypeStruct((wide, share, attn_out.shape[2]), BF16)

    def start_last(carry, d_red, d_in):
        carry.loads[PIECES].full, carry.loads[PIECES + 1].full = d_red, d_in
        carry.begin(*range(PIECES))

    half_pieces = PIECES // 2
    points = (
        start_last,
        lambda carry: carry.begin(PIECES, PIECES + 1),
        lambda carry: carry.hand_on(*range(half_pieces)),
        lambda carry: carry.hand_on(*range(half_pieces, PIECES)),
        lambda carry, d_out: None,
    )
    residual, normed, projected, mixed, middle, normed_two, query_w, output_w, expand_w, reduce_w = kept[1]
    (grad, branch, d_out, d_query, gain_two, gain_one), carried = backward_block(
        1, None, points, grad, branch, reduce_w, expand_w, output_w, normed_two, middle, gain_w, mixed,
        projected, key_seg, query_seg, query_w, residual, normed, wide, 2,
        [ReduceLoad(by_owner(piece, 0), 0) for piece in d_last]
        + [PairLoad(made, 0, True), PairLoad(made, 0, True)],
    )
    for k in range(PIECES):
        carried = landed((TABLE, k), carried)
    red_sums, in_sums = carried
    gain_grads = [None, None, gain_one, gain_two, gain_final]

    def start_first(carry, d_red, d_in):
        carry.loads[4].full, carry.loads[5].full = d_red, d_in
        carry.begin(0, 1, 2, 3)

    def sent_first(carry, d_out):
        carry.loads[6].full = d_out
        carry.begin(6)

    points = (
        start_first,
        lambda carry: carry.begin(4, 5),
        lambda carry: carry.hand_on(2, 3),
        lambda carry: carry.hand_on(4),
        sent_first,
    )
    residual, normed, projected, mixed, middle, normed_two, query_w, output_w, expand_w, reduce_w = kept[0]
    (grad, branch, _, d_query, gain_two, gain_one), carried = backward_block(
        0, math.sqrt(D), points, grad, branch, reduce_w, expand_w, output_w, normed_two, middle, gain_w, mixed,
        projected, key_seg, query_seg, query_w, residual, normed, wide, 3,
        [LineLoad(red_sums, wide), LineLoad(in_sums, wide), ReduceLoad(d_out, 0), ReduceLoad(d_query, 1)]
        + [ReduceLoad(made, 0, True), PairLoad(made, 0, True), PairLoad(made_out, 0, True)],
    )
    for key in ((FFN_OUT, 1), (FFN_IN, 1), (ATTN_OUT, 1), (ATTN_IN, 1), (FFN_OUT, 0)):
        carried = landed(key, carried)
    in_sums, out_sums = carried
    gain_grads[:2] = gain_one, gain_two

    (own_first, own[ATTN_IN, 0], total_small, scalars), carried = tail(
        branch, ids_all, losses, d_query, gain_grads, squares, share, vocab, 4, 4,
        [LineLoad(in_sums, wide), LineLoad(out_sums, wide)],
    )
    own[FFN_IN, 0], own[ATTN_OUT, 0] = carried[0], carried[2]
    grad_attn_in, grad_attn_out, grad_ffn_in, grad_ffn_out = [
        jnp.stack([own[name, index] for index in range(layers)]) for name in (ATTN_IN, ATTN_OUT, FFN_IN, FFN_OUT)
    ]
    grad_tables = jnp.stack([own_first, jnp.concatenate([own[TABLE, k] for k in range(PIECES)], axis=1)])
    grad_gains = total_small[:gain_rows, :gain_cols]
    total_square, loss_sum = scalars[0, 0], scalars[0, 1]
    grad_norm = jnp.sqrt(total_square)
    factor = jnp.minimum(1.0, CLIP_NORM / (grad_norm + 1e-06))
    results = [loss_sum, token_total, grad_norm]
    for weight, gradient, first, second, decay, rate in (
        (attn_in, grad_attn_in, attn_in_mean, attn_in_square, WEIGHT_DECAY, LEARN_RATE),
        (attn_out, grad_attn_out, attn_out_mean, attn_out_square, WEIGHT_DECAY, LEARN_RATE),
        (ffn_in, grad_ffn_in, ffn_in_mean, ffn_in_square, WEIGHT_DECAY, LEARN_RATE),
        (ffn_out, grad_ffn_out, ffn_out_mean, ffn_out_square, WEIGHT_DECAY, LEARN_RATE),
        (tables, grad_tables, tables_mean, tables_square, WEIGHT_DECAY, LEARN_RATE),
        (gains, grad_gains, gains_mean, gains_square, 0.0, GAIN_RATE),
    ):
        results += adam(weight, factor * gradient, first, second, decay, rate)
    return tuple(results)


def solution(mesh):
    wide, narrow = mesh.shape[WIDE], mesh.shape[NARROW]
    placed = (
        P(WIDE, None),
        P(WIDE, None),
        P(WIDE, None),
        P(WIDE, None),
        P(WIDE, None),
        P(None, None, WIDE, NARROW),
        P(None, WIDE, NARROW),
        P(None, WIDE, NARROW),
        P(None, WIDE, NARROW),
        P(None, WIDE, NARROW),
        P(None, WIDE),
        P(None, None, WIDE, NARROW),
        P(None, WIDE, NARROW),
        P(None, WIDE, NARROW),
        P(None, WIDE, NARROW),
        P(None, WIDE, NARROW),
        P(None, WIDE),
        P(None, None, WIDE, NARROW),
        P(None, WIDE, NARROW),
        P(None, WIDE, NARROW),
        P(None, WIDE, NARROW),
        P(None, WIDE, NARROW),
        P(None, WIDE),
    )
    return jax.shard_map(
        functools.partial(per_device, wide, narrow),
        mesh=mesh,
        in_specs=placed,
        out_specs=(
            P(),
            P(),
            P(),
            P(None, None, WIDE, NARROW),
            P(None, None, WIDE, NARROW),
            P(None, None, WIDE, NARROW),
            P(None, None, WIDE, NARROW),
            P(None, WIDE, NARROW),
            P(None, WIDE, NARROW),
            P(None, WIDE, NARROW),
            P(None, WIDE, NARROW),
            P(None, WIDE, NARROW),
            P(None, WIDE, NARROW),
            P(None, WIDE, NARROW),
            P(None, WIDE, NARROW),
            P(None, WIDE, NARROW),
            P(None, WIDE, NARROW),
            P(None, WIDE, NARROW),
            P(None, WIDE, NARROW),
            P(None, WIDE, NARROW),
            P(None, WIDE, NARROW),
            P(None, WIDE, NARROW),
            P(None, WIDE, NARROW),
            P(None, WIDE),
            P(None, WIDE),
            P(None, WIDE),
            P(None, WIDE),
        ),
        check_vma=False,
    )
```

```python
import functools
import math

import jax
import jax.numpy as jnp
from jax import lax
from jax.experimental import pallas as pl
from jax.experimental.pallas import tpu as pltpu
from jax.sharding import PartitionSpec as P

D = 768
HD = 64
V = 8192
STEPS = 1000
ADAM_STEP = 10


NORM_EPS = 1e-05
LEARN_RATE = 0.05
GAIN_RATE = 0.75
FIRST_DECAY = 0.9
SECOND_DECAY = 0.999
ADAM_EPS = 1e-08
WEIGHT_DECAY = 0.01
CLIP_NORM = 0.005
WIDE, NARROW = "wide", "narrow"


def add_heads(partial_value):
    return lax.psum(partial_value, NARROW)


def back_heads(partial_value):
    return lax.psum(partial_value, NARROW)


def rms_forward(value, gain):
    scale_row = lax.rsqrt(jnp.mean(value * value, axis=-1, keepdims=True) + NORM_EPS)
    return (value * scale_row * gain, scale_row)


def rms_backward(grad, value, scale_row, gain):
    unit = value * scale_row
    scaled = grad * gain
    back = scale_row * (scaled - unit * jnp.mean(scaled * unit, axis=-1, keepdims=True))
    return (back, jnp.sum(grad * unit, axis=0))


def time_features(timestep_row):
    half_width = D // 2
    rates = jnp.exp(-math.log(10000.0) * jnp.arange(half_width, dtype=jnp.float32) / half_width)
    angles = timestep_row.astype(jnp.float32)[:, None] * rates[None, :]
    return jnp.concatenate([jnp.sin(angles), jnp.cos(angles)], axis=1)


def masked_scores(queries, key_rows, segment):
    scores = jnp.einsum(
        "qhd,khd->hqk", queries, key_rows, preferred_element_type=jnp.float32
    ) * HD ** (-0.5)
    return jnp.where((segment[:, None] == segment[None, :])[None], scores, -1e30)


def attend(entry):
    queries, key_rows, values, segment = entry
    scores = masked_scores(queries, key_rows, segment)
    row_top = jnp.max(scores, axis=-1, keepdims=True)
    log_total = row_top + jnp.log(jnp.sum(jnp.exp(scores - row_top), axis=-1, keepdims=True))
    probs = jnp.exp(scores - log_total).astype(jnp.bfloat16)
    mixed = jnp.einsum("hqk,khd->qhd", probs, values, preferred_element_type=jnp.float32)
    return (mixed.astype(jnp.bfloat16), log_total)


def attend_back(entry):
    queries, key_rows, values, segment, log_total, grad_mixed = entry
    probs = jnp.exp(masked_scores(queries, key_rows, segment) - log_total)
    grad_probs = jnp.einsum("qhd,khd->hqk", grad_mixed, values, preferred_element_type=jnp.float32)
    grad_scores = (
        probs * (grad_probs - jnp.sum(probs * grad_probs, axis=-1, keepdims=True))
    ).astype(jnp.bfloat16)
    grad_query = jnp.einsum(
        "hqk,khd->qhd", grad_scores, key_rows, preferred_element_type=jnp.float32
    ) * HD ** (-0.5)
    grad_key = jnp.einsum(
        "hqk,qhd->khd", grad_scores, queries, preferred_element_type=jnp.float32
    ) * HD ** (-0.5)
    grad_value = jnp.einsum(
        "hqk,qhd->khd", probs.astype(jnp.bfloat16), grad_mixed, preferred_element_type=jnp.float32
    )
    return (grad_query, grad_key, grad_value)


def layer_forward(residual, segments, query_w, output_w, expand_w, reduce_w, gain_attn, gain_ffn):
    seq_count, seq_len = segments.shape
    normed, scale_one = rms_forward(residual, gain_attn)
    normed = normed.astype(jnp.bfloat16)
    projected = jnp.einsum(
        "sd,cde->cse", normed, query_w, preferred_element_type=jnp.float32
    ).astype(jnp.bfloat16)
    heads = projected.reshape(3, seq_count, seq_len, -1, HD)
    mixed, log_total = lax.map(attend, (heads[0], heads[1], heads[2], segments))
    mixed = mixed.reshape(seq_count * seq_len, -1)
    middle = residual + add_heads(
        jnp.einsum("se,de->sd", mixed, output_w, preferred_element_type=jnp.float32)
    )
    normed_two, scale_two = rms_forward(middle, gain_ffn)
    normed_two = normed_two.astype(jnp.bfloat16)
    before = jnp.dot(normed_two, expand_w, preferred_element_type=jnp.float32)
    after = jax.nn.gelu(before).astype(jnp.bfloat16)
    result = middle + add_heads(
        jnp.einsum("sf,df->sd", after, reduce_w, preferred_element_type=jnp.float32)
    )
    return (
        result,
        (
            residual,
            scale_one,
            normed,
            projected,
            log_total,
            mixed,
            middle,
            scale_two,
            normed_two,
            before,
            after,
        ),
    )


def layer_backward(
    grad, kept, segments, query_w, output_w, expand_w, reduce_w, gain_attn, gain_ffn
):
    (
        residual,
        scale_one,
        normed,
        projected,
        log_total,
        mixed,
        middle,
        scale_two,
        normed_two,
        before,
        after,
    ) = kept
    seq_count, seq_len = segments.shape
    grad_branch = grad.astype(jnp.bfloat16)
    grad_after = jnp.dot(grad_branch, reduce_w, preferred_element_type=jnp.float32)
    grad_reduce = jnp.einsum("sd,sf->df", grad_branch, after, preferred_element_type=jnp.float32)
    _, gelu_pull = jax.vjp(jax.nn.gelu, before)
    grad_before = gelu_pull(grad_after)[0].astype(jnp.bfloat16)
    grad_expand = jnp.einsum(
        "sd,sf->df", normed_two, grad_before, preferred_element_type=jnp.float32
    )
    grad_normed_two = back_heads(
        jnp.einsum("sf,df->sd", grad_before, expand_w, preferred_element_type=jnp.float32)
    )
    grad_middle, grad_gain_ffn = rms_backward(grad_normed_two, middle, scale_two, gain_ffn)
    grad_middle = grad_middle + grad
    grad_attn = grad_middle.astype(jnp.bfloat16)
    grad_mixed = jnp.dot(grad_attn, output_w, preferred_element_type=jnp.float32).astype(
        jnp.bfloat16
    )
    grad_output = jnp.einsum("sd,se->de", grad_attn, mixed, preferred_element_type=jnp.float32)
    heads = projected.reshape(3, seq_count, seq_len, -1, HD)
    grad_query, grad_key, grad_value = lax.map(
        attend_back,
        (
            heads[0],
            heads[1],
            heads[2],
            segments,
            log_total,
            grad_mixed.reshape(seq_count, seq_len, -1, HD),
        ),
    )
    grad_projected = (
        jnp.stack([grad_query, grad_key, grad_value])
        .reshape(3, seq_count * seq_len, -1)
        .astype(jnp.bfloat16)
    )
    grad_query_w = jnp.einsum(
        "sd,cse->cde", normed, grad_projected, preferred_element_type=jnp.float32
    )
    grad_normed = back_heads(
        jnp.einsum("cse,cde->sd", grad_projected, query_w, preferred_element_type=jnp.float32)
    )
    grad_input, grad_gain_attn = rms_backward(grad_normed, residual, scale_one, gain_attn)
    return (
        grad_input + grad_middle,
        (
            grad_query_w,
            grad_output,
            grad_expand,
            grad_reduce,
            jnp.stack([grad_gain_attn, grad_gain_ffn]),
        ),
    )


def adam(weight, grad, first, second, decay, rate):
    first_new = FIRST_DECAY * first + (1.0 - FIRST_DECAY) * grad
    second_new = SECOND_DECAY * second + (1.0 - SECOND_DECAY) * grad * grad
    first_hat = first_new / (1.0 - FIRST_DECAY**ADAM_STEP)
    second_hat = second_new / (1.0 - SECOND_DECAY**ADAM_STEP)
    weight_new = weight - rate * (first_hat / (jnp.sqrt(second_hat) + ADAM_EPS) + decay * weight)
    return (weight_new, first_new, second_new, weight_new.astype(jnp.bfloat16))


def general_device(
    noised,
    clean,
    timesteps,
    segments,
    counted,
    attn_in,
    attn_out,
    ffn_in,
    ffn_out,
    tables,
    gains,
    attn_in_mean,
    attn_out_mean,
    ffn_in_mean,
    ffn_out_mean,
    tables_mean,
    gains_mean,
    attn_in_square,
    attn_out_square,
    ffn_in_square,
    ffn_out_square,
    tables_square,
    gains_square,
):
    layers = attn_in.shape[0]
    mask = counted.reshape(-1).astype(jnp.float32)
    token_total = lax.psum(jnp.sum(mask), WIDE)
    query_w, output_w, expand_w, reduce_w, table_w, gain_low = (
        lax.all_gather(attn_in.astype(jnp.bfloat16), WIDE, axis=2, tiled=True),
        lax.all_gather(attn_out.astype(jnp.bfloat16), WIDE, axis=1, tiled=True),
        lax.all_gather(ffn_in.astype(jnp.bfloat16), WIDE, axis=1, tiled=True),
        lax.all_gather(ffn_out.astype(jnp.bfloat16), WIDE, axis=1, tiled=True),
        lax.all_gather(tables.astype(jnp.bfloat16), WIDE, axis=1, tiled=True),
        lax.all_gather(gains.astype(jnp.bfloat16), WIDE, axis=1, tiled=True),
    )
    gain_w = gain_low.astype(jnp.float32)
    noised_flat = noised.reshape(-1)
    clean_flat = clean.reshape(-1)
    step_flat = timesteps.reshape(-1)
    vocab_local = table_w.shape[2]
    vocab_ids = lax.axis_index(NARROW) * vocab_local + jnp.arange(vocab_local, dtype=jnp.int32)
    picks = (noised_flat[:, None] == vocab_ids[None, :]).astype(jnp.bfloat16)
    looked = add_heads(
        jnp.einsum("sv,dv->sd", picks, table_w[0], preferred_element_type=jnp.float32)
    )
    residual = math.sqrt(D) * looked + time_features(step_flat)
    kept_layers = []
    for layer_index in range(layers):
        residual, kept = layer_forward(
            residual,
            segments,
            query_w[layer_index],
            output_w[layer_index],
            expand_w[layer_index],
            reduce_w[layer_index],
            gain_w[2 * layer_index],
            gain_w[2 * layer_index + 1],
        )
        kept_layers.append(kept)
    final, scale_final = rms_forward(residual, gain_w[2 * layers])
    final_low = final.astype(jnp.bfloat16)
    logits = jnp.dot(final_low, table_w[1], preferred_element_type=jnp.float32)
    local_top = jnp.max(logits, axis=1)
    row_top = lax.pmax(local_top, NARROW)
    row_total = lax.psum(jnp.sum(jnp.exp(logits - row_top[:, None]), axis=1), NARROW)
    log_probs = logits - (row_top + jnp.log(row_total))[:, None]
    probs = jnp.exp(log_probs)
    clamped = jnp.maximum(step_flat, 2).astype(jnp.float32)[:, None]
    beta = 1.0 / (STEPS - clamped + 1.0)
    retain = (STEPS - clamped + 1.0) / STEPS
    spread = (clamped - 1.0) / (STEPS * V)
    at_noised = (vocab_ids[None, :] == noised_flat[:, None]).astype(jnp.float32)
    at_clean = (vocab_ids[None, :] == clean_flat[:, None]).astype(jnp.float32)
    forward_fac = beta / V + (1.0 - beta) * at_noised
    backward_fac = retain * at_clean + spread
    joint = forward_fac * backward_fac
    marginal = retain * probs + spread
    joint_total, cross, model_total, weighted, aligned, clean_logp = lax.psum(
        (
            jnp.sum(joint, axis=1),
            jnp.sum(joint * (jnp.log(backward_fac) - jnp.log(marginal)), axis=1),
            jnp.sum(forward_fac * marginal, axis=1),
            jnp.sum(probs * joint / marginal, axis=1),
            jnp.sum(forward_fac * probs, axis=1),
            jnp.sum(at_clean * log_probs, axis=1),
        ),
        NARROW,
    )
    divergence = cross / joint_total - jnp.log(joint_total) + jnp.log(model_total)
    first_step = step_flat == 1
    losses = jnp.where(first_step, -clean_logp, divergence)
    pull = retain * (
        -(joint / joint_total[:, None]) / marginal + forward_fac / model_total[:, None]
    )
    centre = retain[:, 0] * (-weighted / joint_total + aligned / model_total)
    grad_kl = probs * (pull - centre[:, None])
    grad_recon = probs - at_clean
    grad_logits = (
        (mask / token_total)[:, None] * jnp.where(first_step[:, None], grad_recon, grad_kl)
    ).astype(jnp.bfloat16)
    grad_table_out = jnp.einsum(
        "sd,sv->dv", final_low, grad_logits, preferred_element_type=jnp.float32
    )
    grad_final = back_heads(
        jnp.einsum("sv,dv->sd", grad_logits, table_w[1], preferred_element_type=jnp.float32)
    )
    grad_x, grad_gain_final = rms_backward(grad_final, residual, scale_final, gain_w[2 * layers])
    layer_grads = [None] * layers
    for layer_index in reversed(range(layers)):
        grad_x, produced = layer_backward(
            grad_x,
            kept_layers[layer_index],
            segments,
            query_w[layer_index],
            output_w[layer_index],
            expand_w[layer_index],
            reduce_w[layer_index],
            gain_w[2 * layer_index],
            gain_w[2 * layer_index + 1],
        )
        layer_grads[layer_index] = produced
    grad_look = (math.sqrt(D) * grad_x).astype(jnp.bfloat16)
    grad_table_in = jnp.einsum("sd,sv->dv", grad_look, picks, preferred_element_type=jnp.float32)
    stacked = [jnp.stack([entry[which] for entry in layer_grads]) for which in range(5)]
    gain_layers = stacked[4].reshape(2 * layers, -1)
    grad_tables_all = jnp.stack([grad_table_in, grad_table_out])
    grad_attn_in, grad_attn_out, grad_ffn_in, grad_ffn_out, grad_tables, grad_gains = (
        lax.psum_scatter(stacked[0], WIDE, scatter_dimension=2, tiled=True),
        lax.psum_scatter(stacked[1], WIDE, scatter_dimension=1, tiled=True),
        lax.psum_scatter(stacked[2], WIDE, scatter_dimension=1, tiled=True),
        lax.psum_scatter(stacked[3], WIDE, scatter_dimension=1, tiled=True),
        lax.psum_scatter(grad_tables_all, WIDE, scatter_dimension=1, tiled=True),
        lax.psum_scatter(
            jnp.concatenate([gain_layers, grad_gain_final[None, :]], axis=0),
            WIDE,
            scatter_dimension=1,
            tiled=True,
        ),
    )
    narrow_first = (lax.axis_index(NARROW) == 0).astype(jnp.float32)
    squares = (
        jnp.sum(grad_attn_in * grad_attn_in)
        + jnp.sum(grad_attn_out * grad_attn_out)
        + jnp.sum(grad_ffn_in * grad_ffn_in)
        + jnp.sum(grad_ffn_out * grad_ffn_out)
        + jnp.sum(grad_tables * grad_tables)
        + narrow_first * jnp.sum(grad_gains * grad_gains)
    )
    squares, loss_sum = lax.psum(
        (squares, narrow_first * jnp.sum(mask * losses)), (WIDE, NARROW)
    )
    grad_norm = jnp.sqrt(squares)
    factor = jnp.minimum(1.0, CLIP_NORM / (grad_norm + 1e-06))
    attn_in_next, attn_in_mean_next, attn_in_square_next, attn_in_copy = adam(
        attn_in, factor * grad_attn_in, attn_in_mean, attn_in_square, WEIGHT_DECAY, LEARN_RATE
    )
    attn_out_next, attn_out_mean_next, attn_out_square_next, attn_out_copy = adam(
        attn_out, factor * grad_attn_out, attn_out_mean, attn_out_square, WEIGHT_DECAY, LEARN_RATE
    )
    ffn_in_next, ffn_in_mean_next, ffn_in_square_next, ffn_in_copy = adam(
        ffn_in, factor * grad_ffn_in, ffn_in_mean, ffn_in_square, WEIGHT_DECAY, LEARN_RATE
    )
    ffn_out_next, ffn_out_mean_next, ffn_out_square_next, ffn_out_copy = adam(
        ffn_out, factor * grad_ffn_out, ffn_out_mean, ffn_out_square, WEIGHT_DECAY, LEARN_RATE
    )
    tables_next, tables_mean_next, tables_square_next, tables_copy = adam(
        tables, factor * grad_tables, tables_mean, tables_square, WEIGHT_DECAY, LEARN_RATE
    )
    gains_next, gains_mean_next, gains_square_next, gains_copy = adam(
        gains, factor * grad_gains, gains_mean, gains_square, 0.0, GAIN_RATE
    )
    return (
        loss_sum,
        token_total,
        grad_norm,
        attn_in_next,
        attn_in_mean_next,
        attn_in_square_next,
        attn_in_copy,
        attn_out_next,
        attn_out_mean_next,
        attn_out_square_next,
        attn_out_copy,
        ffn_in_next,
        ffn_in_mean_next,
        ffn_in_square_next,
        ffn_in_copy,
        ffn_out_next,
        ffn_out_mean_next,
        ffn_out_square_next,
        ffn_out_copy,
        tables_next,
        tables_mean_next,
        tables_square_next,
        tables_copy,
        gains_next,
        gains_mean_next,
        gains_square_next,
        gains_copy,
    )


MESH = pl.DeviceIdType.MESH
SLOW, FAST = 1, 2
HBM, KEPT, LOCAL = 1, 2, 3
F32 = jnp.float32
BF16 = jnp.bfloat16
CHUNKS = 4
VMEM_LIMIT = 61 * 1024 * 1024
FORWARD_KIND = BF16
BACKWARD_KIND = BF16


def whole_vmem():
    return pl.BlockSpec(memory_space=pltpu.VMEM)


def dot_nn(a, b):
    return lax.dot_general(a, b, (((1,), (0,)), ((), ())), preferred_element_type=F32)


def dot_nt(a, b):
    return lax.dot_general(a, b, (((1,), (1,)), ((), ())), preferred_element_type=F32)


def remote(src, dst, send_sem, recv_sem, device):
    return pltpu.make_async_remote_copy(
        src_ref=src,
        dst_ref=dst,
        send_sem=send_sem,
        recv_sem=recv_sem,
        device_id=device,
        device_id_type=MESH,
    )


def greet(devices):
    barrier = pltpu.get_barrier_semaphore()
    for device in devices:
        pl.semaphore_signal(barrier, inc=1, device_id=device, device_id_type=MESH)
    pl.semaphore_wait(barrier, len(devices))


def group_places(seq_len):
    me = lax.axis_index(NARROW)
    core = lax.rem(me, 2)
    half = seq_len // 2
    mine = pl.multiple_of(core * half, half)
    other = pl.multiple_of((1 - core) * half, half)
    return ({NARROW: me + 1 - 2 * core}, {NARROW: lax.rem(me + 2, 4)}, mine, other)


class Exchange:
    def __init__(self, refs, sems, base, sibling, partner):
        self.near_out, self.near_in, self.far_out, self.far_in = refs
        self.send, self.recv = sems
        self.base, self.sibling, self.partner = base, sibling, partner

    def near(self, j):
        return remote(
            self.near_out.at[j],
            self.near_in.at[j],
            self.send.at[self.base, j],
            self.recv.at[self.base, j],
            self.sibling,
        )

    def far(self, j):
        return remote(
            self.far_out.at[j],
            self.far_in.at[j],
            self.send.at[self.base + 1, j],
            self.recv.at[self.base + 1, j],
            self.partner,
        )

    def give(self, j, value):
        self.near_out[j] = value
        self.near(j).start()

    def pass_on(self, j, value):
        self.near(j).wait_recv()
        self.far_out[j] = (value + self.near_in[j]).astype(self.far_out.dtype)
        self.far(j).start()

    def take(self, j):
        self.far(j).wait_recv()
        return self.far_out[j].astype(F32) + self.far_in[j].astype(F32)

    def close(self):
        for j in range(CHUNKS):
            self.near(j).wait_send()
            self.far(j).wait_send()

    @staticmethod
    def scratch(chunk, width, kind):
        return [
            pltpu.VMEM((CHUNKS, chunk, width), F32),
            pltpu.VMEM((CHUNKS, chunk, width), F32),
            pltpu.VMEM((CHUNKS, chunk, width), kind),
            pltpu.VMEM((CHUNKS, chunk, width), kind),
        ]


class Share:
    def __init__(self, ref, sems, base, sibling, mine, chunk):
        self.ref, self.base, self.sibling, self.mine, self.chunk = ref, base, sibling, mine, chunk
        self.send, self.recv = sems

    def piece(self, j):
        rows = self.ref.at[pl.ds(pl.multiple_of(self.mine + j * self.chunk, self.chunk), self.chunk)]
        return remote(rows, rows, self.send.at[self.base, j], self.recv.at[self.base, j], self.sibling)

    def put(self, j, value):
        self.ref[pl.ds(pl.multiple_of(self.mine + j * self.chunk, self.chunk), self.chunk), :] = value
        self.piece(j).start()

    def arrived(self, j):
        self.piece(j).wait_recv()

    def close(self):
        for j in range(CHUNKS):
            self.piece(j).wait_send()


def wide_places(count):
    me = lax.axis_index(WIDE)
    fast = lax.rem(me, 2)
    slow = me // 2
    return (me, slow, fast, count // 2)


class Carry:
    def __init__(self, loads, fetches, leaves):
        self.loads, self.fetches, self.leaves = loads, fetches, leaves
        self.left = []

    def fetch(self):
        for copy in self.fetches:
            copy.start()

    def fetched(self):
        for copy in self.fetches:
            copy.wait()

    def leave(self, *which):
        for k in which:
            self.leaves[k].start()
            self.left.append(k)

    def gone(self):
        self.leave(*[k for k in self.leaves if k not in self.left])
        for k in self.left:
            self.leaves[k].wait()

    def peers(self):
        ways = []
        for load in self.loads:
            ways += [way for way in load.ways if way not in ways]
        me, slow, fast, slows = wide_places(self.loads[0].count) if self.loads else (0, 0, 0, 0)
        found = []
        if SLOW in ways:
            found += [{WIDE: 2 * lax.rem(slow + step, slows) + fast} for step in range(1, slows)]
        if FAST in ways:
            found.append({WIDE: me + 1 - 2 * fast})
        return found

    def begin(self, *which):
        for k in which:
            self.loads[k].start()

    def hand_on(self, *which):
        for k in which:
            self.loads[k].relay()

    def end(self, *which):
        for k in which:
            self.loads[k].finish()

    def all(self):
        return range(len(self.loads))


def part_of(weights, index, window):
    shape = weights.shape[1:]
    return shape if window is None else shape[:-1] + (window[1],)


class SlowLoad:
    ways = (SLOW,)

    def __init__(self, weights, index, lead, count, window=None):
        self.index, self.lead, self.count, self.window = index, lead, count, window
        shape, slows = part_of(weights, index, window), count // 2
        self.operands, self.in_specs = [weights], [whole_vmem()]
        self.outs = [jax.ShapeDtypeStruct((slows,) + shape, BF16)]
        self.out_specs = [pl.BlockSpec(memory_space=pl.ANY)]
        self.scratch = [pltpu.VMEM(shape, BF16), pltpu.SemaphoreType.DMA] + [pltpu.SemaphoreType.DMA((slows,))] * 2

    def bind(self, given, out, scratch):
        self.shard, self.out = given[0], out[0]
        self.low, self.local, self.send, self.recv = scratch
        self.me, self.slow, self.fast, self.slows = wide_places(self.count)

    def cast(self):
        if self.window is None:
            self.low[...] = self.shard[self.index].astype(BF16)
        else:
            self.low[...] = self.shard[self.index, :, self.window[0] : self.window[0] + self.window[1]].astype(BF16)

    def target(self):
        return self.out.at[self.slow]

    def slow_copy(self, step):
        return remote(
            self.low, self.target(), self.send.at[step], self.recv.at[step],
            {WIDE: 2 * lax.rem(self.slow + step, self.slows) + self.fast},
        )

    def own_copy(self):
        return pltpu.make_async_copy(self.low, self.target(), self.local)

    def start(self):
        self.cast()
        for step in range(1, self.slows):
            self.slow_copy(step).start()
        self.own_copy().start()

    def finish(self):
        for step in range(1, self.slows):
            self.slow_copy(step).wait()
        self.own_copy().wait()


class FastLoad:
    ways = (FAST,)

    def __init__(self, blocks, lead, count):
        self.lead, self.count = lead, count
        shape, slows = blocks.shape[1:], count // 2
        self.operands, self.in_specs = [blocks], [pl.BlockSpec(memory_space=pl.ANY)]
        self.outs = [jax.ShapeDtypeStruct(shape[:lead] + (count,) + shape[lead:], BF16)]
        self.out_specs = [whole_vmem()]
        self.scratch = [pltpu.SemaphoreType.DMA((slows,))] * 3

    def value(self):
        return self.out[...].reshape((-1, self.out.shape[-1]))

    def bind(self, given, out, scratch):
        self.blocks, self.out = given[0], out[0]
        self.local, self.send, self.recv = scratch
        self.me, self.slow, self.fast, self.slows = wide_places(self.count)

    def copies(self, step):
        target = self.out.at[(slice(None),) * self.lead + (2 * step + self.fast,)]
        return (
            remote(
                self.blocks.at[step], target, self.send.at[step], self.recv.at[step],
                {WIDE: self.me + 1 - 2 * self.fast},
            ),
            pltpu.make_async_copy(self.blocks.at[step], target, self.local.at[step]),
        )

    def start(self):
        for step in range(self.slows):
            for copy in self.copies(step):
                copy.start()

    def finish(self):
        for step in range(self.slows):
            for copy in self.copies(step):
                copy.wait()


class GatherLoad(SlowLoad):
    ways = (SLOW, FAST)

    def __init__(self, weights, index, lead, count, window=None, place=HBM):
        super().__init__(weights, index, lead, count, window)
        shape, slows = part_of(weights, index, window), count // 2
        whole = shape[:lead] + (count,) + shape[lead:]
        self.outs = [jax.ShapeDtypeStruct(whole, BF16)]
        self.scratch = self.scratch + [pltpu.SemaphoreType.DMA((slows,))] * 2
        if place == KEPT:
            self.out_specs = [whole_vmem()]
        self.local_out = place == LOCAL
        if self.local_out:
            self.outs, self.out_specs = [], []
            self.scratch = self.scratch + [pltpu.VMEM(whole, BF16)]

    def bind(self, given, out, scratch):
        if self.local_out:
            out, scratch = scratch[-1:], scratch[:-1]
        super().bind(given, out, scratch[:-2])
        self.fast_send, self.fast_recv = scratch[-2:]

    def value(self, *index):
        found = self.out[index] if index else self.out[...]
        return found.reshape((-1, found.shape[-1]))

    def at(self, owner):
        return self.out.at[(slice(None),) * self.lead + (owner,)]

    def target(self):
        return self.at(self.me)

    def fast_copy(self, step):
        block = self.at(2 * lax.rem(self.slow + self.slows - step, self.slows) + self.fast)
        return remote(
            self.low if step == 0 else block, block, self.fast_send.at[step], self.fast_recv.at[step],
            {WIDE: self.me + 1 - 2 * self.fast},
        )

    def start(self):
        super().start()
        self.fast_copy(0).start()

    def relay(self):
        for step in range(1, self.slows):
            self.slow_copy(step).wait_recv()
            self.fast_copy(step).start()

    def finish(self):
        for step in range(self.slows):
            self.fast_copy(step).wait()
            if step:
                self.slow_copy(step).wait_send()
        self.own_copy().wait()


class PairLoad:
    ways = (FAST,)

    def __init__(self, full, lead, inside=False):
        self.lead, self.count, self.inside = lead, full.shape[lead], inside
        self.shape, self.slows = full.shape[:lead] + full.shape[lead + 1 :], self.count // 2
        self.operands, self.in_specs = ([], []) if inside else ([full], [whole_vmem()])
        self.outs, self.out_specs = [jax.ShapeDtypeStruct((self.slows,) + self.shape, BF16)], [whole_vmem()]
        self.scratch = [pltpu.VMEM((self.slows,) + self.shape, BF16)] + [pltpu.SemaphoreType.DMA((self.slows,))] * 2

    def bind(self, given, out, scratch):
        self.full = None if self.inside else given[0]
        self.out = out[0]
        self.came, self.send, self.recv = scratch
        self.me, self.slow, self.fast, self.slows = wide_places(self.count)

    def block(self, step, fast):
        owner = 2 * lax.rem(self.slow + step, self.slows) + fast
        return self.full.at[(slice(None),) * self.lead + (owner,)]

    def copy(self, step):
        return remote(
            self.block(step, 1 - self.fast), self.came.at[step], self.send.at[step], self.recv.at[step],
            {WIDE: self.me + 1 - 2 * self.fast},
        )

    def start(self):
        for step in list(range(1, self.slows)) + [0]:
            self.copy(step).start()

    def finish(self):
        for step in range(self.slows):
            self.copy(step).wait()
            total = self.block(step, self.fast)[...].astype(F32) + self.came[step].astype(F32)
            self.out[step] = total.astype(BF16)


class ReduceLoad(PairLoad):
    ways = (SLOW, FAST)

    def __init__(self, full, lead, inside=False):
        super().__init__(full, lead, inside)
        self.outs = [jax.ShapeDtypeStruct(self.shape, F32), jax.ShapeDtypeStruct((8, 128), F32)]
        self.out_specs = [whole_vmem()] * 2
        self.scratch = (
            self.scratch
            + [pltpu.VMEM((self.slows - 1,) + self.shape, BF16)]
            + [pltpu.SemaphoreType.DMA((self.slows,))] * 2
        )

    def bind(self, given, out, scratch):
        super().bind(given, out[:1], scratch[:3])
        self.squares = out[1]
        self.landed, self.line_send, self.line_recv = scratch[3:]

    def line_copy(self, step):
        return remote(
            self.came.at[step], self.landed.at[step - 1], self.line_send.at[step], self.line_recv.at[step],
            {WIDE: 2 * lax.rem(self.slow + step, self.slows) + self.fast},
        )

    def relay(self):
        for step in list(range(1, self.slows)) + [0]:
            self.copy(step).wait()
            total = self.block(step, self.fast)[...].astype(F32) + self.came[step].astype(F32)
            self.came[step] = total.astype(BF16)
            if step:
                self.line_copy(step).start()

    def finish(self):
        total = self.came[0].astype(F32)
        for step in range(1, self.slows):
            self.line_copy(step).wait()
            total = total + self.landed[step - 1].astype(F32)
        self.out[...] = total
        self.squares[...] = jnp.full(self.squares.shape, jnp.sum(total * total), F32)


class LineLoad:
    ways = (SLOW,)

    def __init__(self, sums, count):
        self.count = count
        slows = count // 2
        self.operands, self.in_specs = [sums], [whole_vmem()]
        self.outs = [jax.ShapeDtypeStruct(sums.shape[1:], F32), jax.ShapeDtypeStruct((8, 128), F32)]
        self.out_specs = [whole_vmem()] * 2
        self.scratch = [pltpu.VMEM(sums.shape, BF16)] + [pltpu.SemaphoreType.DMA((slows,))] * 2

    def bind(self, given, out, scratch):
        self.sums, (self.out, self.squares) = given[0], out
        self.came, self.send, self.recv = scratch
        self.me, self.slow, self.fast, self.slows = wide_places(self.count)

    def copy(self, step):
        return remote(
            self.sums.at[step], self.came.at[step], self.send.at[step], self.recv.at[step],
            {WIDE: 2 * lax.rem(self.slow + step, self.slows) + self.fast},
        )

    def start(self):
        for step in range(1, self.slows):
            self.copy(step).start()

    def finish(self):
        total = self.sums[0].astype(F32)
        for step in range(1, self.slows):
            self.copy(step).wait()
            total = total + self.came[step].astype(F32)
        self.out[...] = total
        self.squares[...] = jnp.full(self.squares.shape, jnp.sum(total * total), F32)


def run(body, name, operands, outs, scratch, collective_id=None, loads=(), away=(), lazy=(), early=()):
    any_place = pl.BlockSpec(memory_space=pl.ANY)
    given, taken = list(operands), []
    in_specs = [any_place if k in away or k in lazy else whole_vmem() for k in range(len(operands))]
    for load in loads:
        places = []
        for operand, spec in zip(load.operands, load.in_specs):
            known = [k for k, other in enumerate(given) if other is operand]
            if not known:
                known = [len(given)]
                given.append(operand)
                in_specs.append(spec)
            places.append(known[0])
        taken.append(places)
    moved = [operands[k] for k in lazy] + [outs[k] for k in early]
    counts = [len(given), len(outs)] + [len(load.outs) for load in loads]
    counts += [len(scratch)] + [len(load.scratch) for load in loads] + [len(moved), len(moved)]
    parts = 1 + len(loads)

    def kernel(*refs):
        groups, place = [], 0
        for count in counts:
            groups.append(refs[place : place + count])
            place += count
        for k, load in enumerate(loads):
            load.bind([groups[0][p] for p in taken[k]], groups[2 + k], groups[2 + parts + k])
        mine, results = list(groups[0][: len(operands)]), list(groups[1])
        fetches, leaves = [], {}
        for k, buffer, sem in zip(lazy, groups[-2], groups[-1]):
            fetches.append(pltpu.make_async_copy(mine[k], buffer, sem))
            mine[k] = buffer
        for k, buffer, sem in zip(early, groups[-2][len(lazy) :], groups[-1][len(lazy) :]):
            leaves[k] = pltpu.make_async_copy(buffer, results[k], sem)
            results[k] = buffer
        body(*mine, *results, *groups[1 + parts], carry=Carry(list(loads), fetches, leaves))

    results = pl.pallas_call(
        kernel,
        out_shape=tuple(outs) + tuple(out for load in loads for out in load.outs),
        in_specs=in_specs,
        out_specs=tuple(any_place if k in early else whole_vmem() for k in range(len(outs)))
        + tuple(spec for load in loads for spec in load.out_specs),
        scratch_shapes=list(scratch)
        + [s for load in loads for s in load.scratch]
        + [pltpu.VMEM(value.shape, value.dtype) for value in moved]
        + [pltpu.SemaphoreType.DMA] * len(moved),
        compiler_params=pltpu.CompilerParams(
            collective_id=collective_id,
            has_side_effects=collective_id is not None,
            vmem_limit_bytes=VMEM_LIMIT,
        ),
        name=name,
    )(*given)
    return results[: len(outs)], results[len(outs) :]


def sems(kinds):
    return [pltpu.SemaphoreType.DMA((kinds, CHUNKS)), pltpu.SemaphoreType.DMA((kinds, CHUNKS))]


def norm_of(value, gain):
    scale = lax.rsqrt(jnp.mean(value * value, axis=-1, keepdims=True) + NORM_EPS)
    return value * scale * gain


def norm_back(grad, value, gain):
    scale = lax.rsqrt(jnp.mean(value * value, axis=-1, keepdims=True) + NORM_EPS)
    unit = value * scale
    scaled = grad * gain
    back = scale * (scaled - unit * jnp.mean(scaled * unit, axis=-1, keepdims=True))
    return (back, jnp.sum(grad * unit, axis=0, keepdims=True))


GELU_A = math.sqrt(2.0 / math.pi)
GELU_B = 0.044715


def gelu_of(x):
    return 0.5 * x * (1.0 + jnp.tanh(GELU_A * (x + GELU_B * (x * x * x))))


def gelu_slope(x):
    square = x * x
    t = jnp.tanh(GELU_A * (x + GELU_B * (x * square)))
    return 0.5 * (1.0 + t) + 0.5 * x * (1.0 - t * t) * (GELU_A * (1.0 + 3.0 * GELU_B * square))


def rows_at(start, j, chunk):
    return pl.ds(pl.multiple_of(start + j * chunk, chunk), chunk)


LANES = 128


def spread(row):
    return jnp.transpose(jnp.broadcast_to(row, (LANES, LANES)))


def feature_places(owner, width, share):
    lane = lax.broadcasted_iota(jnp.int32, (LANES, width), 0)
    feature = lax.broadcasted_iota(jnp.int32, (LANES, width), 1)
    return ((feature == lane + owner * share) & (lane < share)).astype(F32).astype(BF16)


def token_parts(ids, first):
    here = ids - first
    high = lax.shift_right_arithmetic(here, 7)
    place = lax.broadcasted_iota(jnp.int32, (LANES, ids.shape[1]), 0)
    return high, jnp.where(place == here - high * LANES, 1.0, 0.0).astype(BF16)


def embed_part(
    ids, counted, gains, steps, rates, table,
    resid, normed, gain_all, count_all, ids_all,
    low, extra, small, near_out, near_in, own, far_out, far_in, wide_out, wide_in, part_out, part_in,
    id_send, id_recv, small_send, small_recv, near_send, near_recv, far_send, far_recv, wide_send, wide_recv,
    part_send, part_recv, send, recv, carry,
):
    seq_len, width = normed.shape
    chunk = seq_len // 2 // CHUNKS
    quarter = seq_len // 4
    share, vocab = table.shape[1:]
    owners = ids_all.shape[0]
    sibling, partner, mine, other = group_places(seq_len)
    place = lax.axis_index(NARROW)
    side = lax.div(place, 2)
    me = lax.axis_index(WIDE)
    first = place * vocab
    around = [lax.rem(me + step, owners) for step in range(owners)]

    def id_copy(step):
        return remote(ids_all.at[me], ids_all.at[me], id_send.at[step], id_recv.at[step], {WIDE: around[step]})

    def small_copy(step):
        return remote(small.at[me], small.at[me], small_send.at[step], small_recv.at[step], {WIDE: around[step]})

    def near_copy(step):
        return remote(near_out.at[step], near_in.at[step], near_send.at[step], near_recv.at[step], sibling)

    def far_copy(step):
        return remote(far_out.at[step], far_in.at[step], far_send.at[step], far_recv.at[step], partner)

    def wide_copy(step):
        return remote(wide_out.at[step], wide_in.at[me], wide_send.at[step], wide_recv.at[step], {WIDE: around[step]})

    def part_copy(piece):
        rows = pl.ds(piece * LANES, LANES)
        return remote(part_out.at[rows], part_in.at[rows], part_send.at[piece], part_recv.at[piece], partner)

    ids_all[me] = ids[...]
    small[me] = jnp.zeros(small.shape[1:], F32)
    small[me, : gains.shape[0], : gains.shape[1]] = gains[...].astype(BF16).astype(F32)
    count = jnp.sum(counted[...].astype(F32), keepdims=True)
    small[me, COUNT_ROW : COUNT_ROW + 1, :] = jnp.broadcast_to(count, (1, small.shape[2]))
    greet([{WIDE: device} for device in around[1:]] + [sibling, partner])
    for step in range(1, owners):
        id_copy(step).start()
    for step in range(1, owners):
        small_copy(step).start()
    carry.begin(0, 1)
    parts = vocab // LANES
    for part in range(parts):
        low[part * share : (part + 1) * share, :] = table[0, :, part * LANES : (part + 1) * LANES].astype(BF16)
    core = lax.rem(place, 2)

    def look_up(step):
        row = lax.rem(me + step, owners)

        def find(which):
            high, picks = token_parts(ids_all[row, pl.ds(which, 1), :], first)
            found = dot_nn(low[...], picks)
            total = jnp.zeros((share, quarter), F32)
            for part in range(parts):
                total = total + jnp.where(high == part, found[part * share : (part + 1) * share, :], 0.0)
            return total.astype(BF16)

        for k in range(2):
            near_out[step, k] = find(2 * (1 - core) + k)
        near_copy(step).start()
        for k in range(2):
            own[step, k] = find(2 * core + k)

    def halve(step):
        near_copy(step).wait_recv()
        own[step] = own[step] + near_in[step]
        far_out[step] = own[step, 1 - side]
        far_copy(step).start()

    def deliver(step):
        far_copy(step).wait_recv()
        total = own[step, side] + far_in[step]
        if step % owners == 0:
            wide_in[me] = total
        else:
            wide_out[step] = total
            wide_copy(step).start()

    order = list(range(1, owners)) + [0]
    for turn in range(owners + 2):
        if turn < owners:
            if order[turn]:
                id_copy(owners - order[turn]).wait_recv()
            look_up(order[turn])
        if 1 <= turn < owners + 1:
            halve(order[turn - 1])
        if turn >= 2:
            deliver(order[turn - 2])
    carry.begin(2, 3)
    carry.hand_on(0, 1)
    for step in range(1, owners):
        small_copy(step).wait_recv()
    total = None
    for owner in range(owners):
        part = dot_nn(small[owner].astype(BF16), feature_places(owner, width, share))
        total = part if total is None else total + part
    gain_all[...] = total
    count_all[...] = jnp.sum(small[...], axis=0)
    half_width = width // 2
    for k in range(seq_len // 2 // LANES):
        when = spread(steps[pl.ds(mine // LANES + k, 1), :].astype(F32))
        for t in range(half_width // LANES):
            columns = slice(t * LANES, (t + 1) * LANES)
            angles = when * rates[:, columns]
            rows = slice(k * LANES, (k + 1) * LANES)
            extra[rows, t * LANES : (t + 1) * LANES] = jnp.sin(angles)
            extra[rows, half_width + t * LANES : half_width + (t + 1) * LANES] = jnp.cos(angles)
    for step in range(1, owners):
        wide_copy(step).wait_recv()
    found = jnp.transpose(wide_in[...].reshape(width, quarter))
    pieces = quarter // LANES
    at_side = pl.multiple_of(side * quarter, quarter)
    at_other = pl.multiple_of((1 - side) * quarter, quarter)
    for piece in range(pieces):
        rows = pl.ds(piece * LANES, LANES)
        part_out[rows, :] = found[piece * LANES : (piece + 1) * LANES, :]
        part_copy(piece).start()

    def finish(start, source, piece):
        rows = rows_at(start, piece, LANES)
        x = math.sqrt(width) * source[pl.ds(piece * LANES, LANES), :].astype(F32) + extra[rows, :]
        resid[rows, :] = x
        here = rows_at(mine + start, piece, LANES)
        normed[here, :] = norm_of(x, gain_all[0:1, :]).astype(BF16)
        give_rows(here, piece if source is part_out else pieces + piece).start()

    def give_rows(here, k):
        return remote(normed.at[here], normed.at[here], send.at[0, k], recv.at[0, k], sibling)

    for piece in range(pieces):
        finish(at_side, part_out, piece)
    for piece in range(pieces):
        part_copy(piece).wait_recv()
        finish(at_other, part_in, piece)
    carry.hand_on(2)
    for k in range(2 * pieces):
        give_rows(rows_at(mine, k % pieces, LANES), k).wait()
    for step in range(owners):
        near_copy(step).wait_send()
        far_copy(step).wait_send()
        if step:
            id_copy(step).wait_send()
            small_copy(step).wait_send()
            wide_copy(step).wait_send()
    for piece in range(pieces):
        part_copy(piece).wait_send()


QUERY_BLOCK = 256


def forward_part(
    layer, weights, points, normed, key_seg, query_seg, resid, gains,
    projected, mixed, middle, normed_two, result, normed_next,
    bias, values_t, near_out, near_in, far_out, far_in, near_out2, near_in2, far_out2, far_in2, own2, send, recv,
):
    w_query, w_out, w_in, w_red = weights
    at_half, at_feed, at_sent, at_last = points
    seq_len, width = normed.shape
    chunk = seq_len // 2 // CHUNKS
    block = bias.shape[1]
    heads = mixed.shape[1] // HD
    sibling, partner, mine, other = group_places(seq_len)
    pair = (send, recv)
    first = Exchange((near_out, near_in, far_out, far_in), pair, 0, sibling, partner)
    second = Exchange((near_out2, near_in2, far_out2, far_in2), pair, 2, sibling, partner)
    share = Share(normed_two, pair, 4, sibling, mine, chunk)
    share_next = Share(normed_next, pair, 5, sibling, mine, chunk)

    def ask(i, _):
        rows = rows_at(0, i, block)
        for which in range(3):
            projected[which, rows, :] = dot_nn(normed[rows, :], w_query(which)).astype(BF16)
        return 0

    lax.fori_loop(0, seq_len // block, ask, 0)
    values_t[...] = jnp.transpose(projected[2])

    def attend_rows(start):
        rows = pl.ds(pl.multiple_of(start, block), block)
        bias[...] = jnp.where(key_seg[...] == query_seg[:, rows], 0.0, -1e30)
        asked = projected[0, rows, :] * HD ** (-0.5)
        parts = []
        for head in range(heads):
            scores = dot_nt(projected[1], head_lanes(asked, head, HD)) + bias[...]
            powers = jnp.exp(scores - jnp.max(scores, axis=0, keepdims=True))
            probs = (powers * (1.0 / jnp.sum(powers, axis=0, keepdims=True))).astype(BF16)
            parts.append(dot_nn(values_t[head * HD : (head + 1) * HD, :], probs))
        mixed[rows, :] = jnp.transpose(jnp.concatenate(parts, axis=0)).astype(BF16)

    def project(start, j):
        return dot_nt(mixed[rows_at(start, j, chunk), :], w_out())

    def feed(rows):
        pre = dot_nn(normed_two[rows, :], w_in())
        return dot_nt(gelu_of(pre).astype(BF16), w_red())

    per_block = block // chunk
    for part in range(CHUNKS // per_block):

        def both(i, _):
            attend_rows(jnp.where(i == 0, other, mine) + part * block)
            return 0

        lax.fori_loop(0, 2, both, 0)
        for j in range(part * per_block, (part + 1) * per_block):
            first.give(j, project(other, j))
        if part == 0:
            at_half()
        for j in range(part * per_block, (part + 1) * per_block):
            first.pass_on(j, project(mine, j))
    at_feed()
    for j in range(CHUNKS):
        rows = rows_at(0, j, chunk)
        mid = resid[rows, :] + first.take(j)
        middle[rows, :] = mid
        share.put(j, norm_of(mid, gains[2 * layer + 1 : 2 * layer + 2, :]).astype(BF16))
        own2[j] = feed(rows_at(mine, j, chunk))
        share.arrived(j)
        second.give(j, feed(rows_at(other, j, chunk)))
        if j >= 1:
            second.pass_on(j - 1, own2[j - 1])
    second.pass_on(CHUNKS - 1, own2[CHUNKS - 1])
    at_sent()
    for j in range(CHUNKS):
        rows = rows_at(0, j, chunk)
        x = middle[rows, :] + second.take(j)
        result[rows, :] = x
        share_next.put(j, norm_of(x, gains[2 * layer + 2 : 2 * layer + 3, :]).astype(BF16))
        if j == CHUNKS - 2:
            at_last()
    for j in range(CHUNKS):
        share_next.arrived(j)
    for part in (first, second, share, share_next):
        part.close()


def layer_outs(seq_len, width, heads_width):
    return [
        jax.ShapeDtypeStruct((3, seq_len, heads_width), BF16),
        jax.ShapeDtypeStruct((seq_len, heads_width), BF16),
        jax.ShapeDtypeStruct((seq_len // 2, width), F32),
        jax.ShapeDtypeStruct((seq_len, width), BF16),
    ]


def layer_scratch(seq_len, width, heads_width):
    half, chunk = seq_len // 2, seq_len // 2 // CHUNKS
    block = max(chunk, min(QUERY_BLOCK, half))
    return (
        [pltpu.VMEM((seq_len, block), F32), pltpu.VMEM((heads_width, seq_len), BF16)]
        + Exchange.scratch(chunk, width, FORWARD_KIND)
        + Exchange.scratch(chunk, width, FORWARD_KIND)
        + [pltpu.VMEM((CHUNKS, chunk, width), F32)]
        + sems(6)
    )


LAYER_SCRATCH = 13
COUNT_ROW = 5


def front_kernel(
    ids, counted, gains, steps, rates, table, key_seg, query_seg,
    resid, normed, gain_all, count_all, ids_all, projected, mixed, middle, normed_two, result, normed_next,
    *scratch, carry,
):
    embed_part(
        ids, counted, gains, steps, rates, table, resid, normed, gain_all, count_all, ids_all,
        *scratch[:-LAYER_SCRATCH], carry,
    )
    carry.end(0, 1)
    later = list(carry.all())[4:]

    def at_half():
        carry.hand_on(3)
        carry.begin(*later[:2])

    def at_feed():
        carry.end(2, 3)
        carry.begin(*later[2:])
        carry.leave(0, 1, 5, 6)

    def at_sent():
        carry.hand_on(*later[:2])
        carry.leave(7, 8)

    forward_part(
        0,
        [carry.loads[0].value] + [load.value for load in carry.loads[1:4]],
        (at_half, at_feed, at_sent, lambda: carry.hand_on(*later[2:3])),
        normed, key_seg, query_seg, resid, gain_all,
        projected, mixed, middle, normed_two, result, normed_next, *scratch[-LAYER_SCRATCH:],
    )
    carry.end(*later)
    carry.gone()


def front(ids, counted, gains, steps, rates, tables, key_seg, query_seg, owners, heads_width, collective_id, loads):
    seq_len = ids.size
    share, vocab = tables.shape[1:]
    half, width = seq_len // 2, owners * share
    dma = pltpu.SemaphoreType.DMA
    return run(
        front_kernel,
        "front",
        [ids, counted, gains, steps, rates, tables, key_seg, query_seg],
        [
            jax.ShapeDtypeStruct((half, width), F32),
            jax.ShapeDtypeStruct((seq_len, width), BF16),
            jax.ShapeDtypeStruct((8, width), F32),
            jax.ShapeDtypeStruct((8, LANES), F32),
            jax.ShapeDtypeStruct((owners,) + ids.shape, jnp.int32),
        ]
        + layer_outs(seq_len, width, heads_width)
        + [jax.ShapeDtypeStruct((half, width), F32), jax.ShapeDtypeStruct((seq_len, width), BF16)],
        [
            pltpu.VMEM((vocab // LANES * share, LANES), BF16),
            pltpu.VMEM((half, width), F32),
            pltpu.VMEM((owners, 8, LANES), F32),
        ]
        + [pltpu.VMEM((owners, 2, share, half // 2), BF16)] * 3
        + [pltpu.VMEM((owners, share, half // 2), BF16)] * 4
        + [
            pltpu.VMEM((half // 2, width), BF16),
            pltpu.VMEM((half // 2, width), BF16),
        ]
        + [dma((owners,))] * 10
        + [dma((half // 2 // LANES,))] * 2
        + [dma((1, half // LANES))] * 2
        + layer_scratch(seq_len, width, heads_width),
        collective_id,
        loads,
        early=(0, 1, 5, 6, 7, 8),
    )


TILE = 256


def weight_grad(left_t, right, out):
    columns = right.shape[1]
    tile = TILE if columns % TILE == 0 else columns

    def put(where):
        value = dot_nn(left_t[...], right[:, where]).astype(out.dtype)
        if len(out.shape) == 3:
            out[:, :, where] = value.reshape(out.shape[:2] + (tile,))
        else:
            out[:, where] = value

    def step(i, _):
        put(pl.ds(pl.multiple_of(i * tile, tile), tile))
        return 0

    if tile == columns:
        put(slice(None))
    else:
        lax.fori_loop(0, columns // tile, step, 0)


def head_lanes(value, head, size):
    lanes = lax.broadcasted_iota(jnp.int32, value.shape, 1)
    inside = (lanes >= head * size) & (lanes < (head + 1) * size)
    return jnp.where(inside, value, jnp.zeros_like(value))


def backward_kernel(
    layer, scale, points, grad, branch, w_red, w_in, w_out, normed_two, middle, gains, mixed,
    projected, key_seg, query_seg, w_query, resid, normed,
    grad_out, branch_out, d_out, d_query, gain_two, gain_one,
    d_red, d_in, grad_middle, grad_attn, grad_mixed, grad_projected, grad_before, after, turned,
    bias, keys_t, grad_keys, grad_values,
    near_out, near_in, far_out, far_in, far_out2, far_in2, send, recv, loaded, carry,
):
    at_start, at_made, at_summed, at_attended, at_sent = points
    seq_len, width = normed_two.shape
    chunk = seq_len // 2 // CHUNKS
    sibling, partner, mine, other = group_places(seq_len)
    carry.fetch()
    greet([sibling, partner] + carry.peers())
    at_start(carry, d_red, d_in)
    pair = (send, recv)
    trade = Exchange((near_out, near_in, far_out, far_in), pair, 0, sibling, partner)
    share = Share(grad_attn, pair, 2, sibling, mine, chunk)

    def ffn_partial(start, j):
        rows = rows_at(start, j, chunk)
        pre = dot_nn(normed_two[rows, :], w_in[...])
        after[rows, :] = gelu_of(pre).astype(BF16)
        low = (dot_nn(branch[rows, :], w_red[...]) * gelu_slope(pre)).astype(BF16)
        grad_before[rows, :] = low
        return dot_nt(low, w_in[...])

    trade.give(0, ffn_partial(other, 0))
    for j in range(CHUNKS):
        if j + 1 < CHUNKS:
            trade.give(j + 1, ffn_partial(other, j + 1))
        trade.pass_on(j, ffn_partial(mine, j))
    turned[...] = jnp.transpose(branch[...])
    weight_grad(turned, after, d_red)
    turned[...] = jnp.transpose(normed_two[...])
    weight_grad(turned, grad_before, d_in)
    at_made(carry)
    fetch = pltpu.make_async_copy(normed, after, loaded)
    fetch.start()
    carry.fetched()
    total = jnp.zeros((1, width), F32)
    for j in range(CHUNKS):
        rows = rows_at(0, j, chunk)
        back, part = norm_back(trade.take(j), middle[rows, :], gains[2 * layer + 1 : 2 * layer + 2, :])
        total = total + part
        back = back + grad[rows, :]
        grad_middle[rows, :] = back
        share.put(j, back.astype(BF16))
        here = rows_at(mine, j, chunk)
        grad_mixed[here, :] = dot_nn(grad_attn[here, :], w_out[...]).astype(BF16)
    gain_two[...] = total
    for j in range(CHUNKS):
        share.arrived(j)
        here = rows_at(other, j, chunk)
        grad_mixed[here, :] = dot_nn(grad_attn[here, :], w_out[...]).astype(BF16)
    trade.close()
    share.close()
    at_summed(carry)

    block = bias.shape[1]
    heads = grad_mixed.shape[1] // HD
    keys_t[...] = jnp.transpose(projected[1])
    grad_keys[...] = jnp.zeros(grad_keys.shape, F32)
    grad_values[...] = jnp.zeros(grad_values.shape, F32)

    def queries(i, _):
        rows = rows_at(0, i, block)
        bias[...] = jnp.where(key_seg[...] == query_seg[:, rows], 0.0, -1e30)
        asked = projected[0, rows, :] * HD ** (-0.5)
        given = grad_mixed[rows, :]
        parts = []
        for head in range(heads):
            query = head_lanes(asked, head, HD)
            wanted = head_lanes(given, head, HD)
            scores = dot_nt(projected[1], query) + bias[...]
            powers = jnp.exp(scores - jnp.max(scores, axis=0, keepdims=True))
            probs = powers * (1.0 / jnp.sum(powers, axis=0, keepdims=True))
            grad_probs = dot_nt(projected[2], wanted)
            centre = jnp.sum(probs * grad_probs, axis=0, keepdims=True)
            grad_scores = (probs * (grad_probs - centre)).astype(BF16)
            parts.append(dot_nn(keys_t[head * HD : (head + 1) * HD, :], grad_scores))
            grad_keys[...] += dot_nn(grad_scores, query)
            grad_values[...] += dot_nn(probs.astype(BF16), wanted)
        grad_projected[0, rows, :] = (jnp.transpose(jnp.concatenate(parts, axis=0)) * HD ** (-0.5)).astype(BF16)
        return 0

    lax.fori_loop(0, seq_len // block, queries, 0)
    grad_projected[1] = grad_keys[...].astype(BF16)
    grad_projected[2] = grad_values[...].astype(BF16)
    at_attended(carry)

    trade = Exchange((near_out, near_in, far_out2, far_in2), pair, 3, sibling, partner)
    share = Share(branch_out, pair, 5, sibling, mine, chunk)

    def query_partial(start, j):
        rows = rows_at(start, j, chunk)
        found = None
        for which in range(3):
            part = dot_nt(grad_projected[which, rows, :], w_query[which])
            found = part if found is None else found + part
        return found

    trade.give(0, query_partial(other, 0))
    for j in range(CHUNKS):
        if j + 1 < CHUNKS:
            trade.give(j + 1, query_partial(other, j + 1))
        trade.pass_on(j, query_partial(mine, j))
    turned[...] = jnp.transpose(grad_attn[...])
    weight_grad(turned, mixed, d_out)
    fetch.wait()
    turned[...] = jnp.transpose(after[...])
    for which in range(3):
        weight_grad(turned, grad_projected.at[which], d_query.at[which])
    at_sent(carry, d_out, d_query)
    total = jnp.zeros((1, width), F32)
    for j in range(CHUNKS):
        rows = rows_at(0, j, chunk)
        back, part = norm_back(trade.take(j), resid[rows, :], gains[2 * layer : 2 * layer + 1, :])
        total = total + part
        back = back + grad_middle[rows, :]
        grad_out[rows, :] = back
        share.put(j, (back if scale is None else scale * back).astype(BF16))
    gain_one[...] = total
    for j in range(CHUNKS):
        share.arrived(j)
    trade.close()
    share.close()
    carry.end(*carry.all())


def backward_block(
    layer, scale, points, grad, branch, w_red, w_in, w_out, normed_two, middle, gains, mixed,
    projected, key_seg, query_seg, w_query, resid, normed, owners, collective_id, loads,
):
    seq_len, width = normed_two.shape
    hidden, heads_width = w_in.shape[1], w_query.shape[2]
    half, chunk = seq_len // 2, seq_len // 2 // CHUNKS
    block = min(QUERY_BLOCK, seq_len)
    far = pltpu.VMEM((CHUNKS, chunk, width), BACKWARD_KIND)
    return run(
        functools.partial(backward_kernel, layer, scale, points),
        "backward_block",
        [grad, branch, w_red, w_in, w_out, normed_two, middle, gains, mixed]
        + [projected, key_seg, query_seg, w_query, resid, normed],
        [
            jax.ShapeDtypeStruct((half, width), F32),
            jax.ShapeDtypeStruct((seq_len, width), BF16),
            jax.ShapeDtypeStruct((owners, width // owners, heads_width), BF16),
            jax.ShapeDtypeStruct((3, owners, width // owners, heads_width), BF16),
            jax.ShapeDtypeStruct((1, width), F32),
            jax.ShapeDtypeStruct((1, width), F32),
        ],
        [pltpu.VMEM((owners, width // owners, hidden), BF16)] * 2
        + [
            pltpu.VMEM((half, width), F32),
            pltpu.VMEM((seq_len, width), BF16),
            pltpu.VMEM((seq_len, heads_width), BF16),
            pltpu.VMEM((3, seq_len, heads_width), BF16),
            pltpu.VMEM((seq_len, hidden), BF16),
            pltpu.VMEM((seq_len, width), BF16),
            pltpu.VMEM((width, seq_len), BF16),
            pltpu.VMEM((seq_len, block), F32),
            pltpu.VMEM((heads_width, seq_len), BF16),
            pltpu.VMEM((seq_len, heads_width), F32),
            pltpu.VMEM((seq_len, heads_width), F32),
        ]
        + Exchange.scratch(chunk, width, BACKWARD_KIND)
        + [far, far]
        + sems(6)
        + [pltpu.SemaphoreType.DMA],
        collective_id,
        loads,
        away=(14,),
        lazy=(0, 4, 6, 8, 9, 10, 12, 13),
    )


def to_rows(columns):
    lanes = lax.broadcasted_iota(jnp.int32, (LANES, LANES), 1)
    total = jnp.zeros((LANES, LANES), F32)
    for k, column in enumerate(columns):
        total = jnp.where(lanes == k, column, total)
    return jnp.transpose(total)[:8, :]


def loss_part(
    row, normed, info, value, gain, table_loads, grad_out, branch, d_gain, losses, d_tables,
    logits, grads, places, turned, stat_out, stat_in, sum_out, sum_in,
    stat_send, stat_recv, sum_send, sum_recv, near_out, near_in, far_out, far_in, send, recv, made,
):
    seq_len, width = normed.shape
    chunk = seq_len // 2 // CHUNKS
    piece_width = table_loads[0].out.shape[-1]
    vocab = piece_width * len(table_loads)
    tiles = vocab // LANES
    blocks = seq_len // LANES
    me = lax.axis_index(NARROW)
    sibling, partner, mine, other = group_places(seq_len)
    peers = [{NARROW: lax.rem(me + k, 4)} for k in range(1, 4)]
    sems = (send, recv)
    trade = Exchange((near_out, near_in, far_out, far_in), sems, 0, sibling, partner)
    share = Share(branch, sems, 2, sibling, mine, chunk)
    first = (me * vocab).astype(F32)
    whole = 4.0 * vocab
    lanes = lax.broadcasted_iota(jnp.int32, (LANES, LANES), 1).astype(F32)

    def stat_copy(b, k):
        return remote(stat_out.at[b], stat_in.at[k, b], stat_send.at[k, b], stat_recv.at[k, b], peers[k])

    def sum_copy(b, k):
        return remote(sum_out.at[b], sum_in.at[k, b], sum_send.at[k, b], sum_recv.at[k, b], peers[k])

    def tile_at(t):
        return pl.ds(pl.multiple_of(t * LANES, LANES), LANES)

    def ask(b, _):
        rows = rows_at(0, b, LANES)
        here = info[:, rows]
        at_noised = spread(here[0:1] - first)
        at_clean = spread(here[1:2] - first)
        places[b, 0] = at_noised
        places[b, 1] = at_clean

        def top_step(t, top):
            return jnp.maximum(top, logits[rows, tile_at(t)])

        top = lax.fori_loop(1, tiles, top_step, logits[rows, tile_at(0)], unroll=4)
        top = jnp.max(top, axis=1, keepdims=True)
        top_wide = jnp.broadcast_to(top, (LANES, LANES))

        def sum_step(t, totals):
            powers, noised, clean = totals
            piece = logits[rows, tile_at(t)]
            column = lanes + (t * LANES).astype(F32)
            return (
                powers + jnp.exp(piece - top_wide),
                noised + jnp.where(column == at_noised, piece, 0.0),
                clean + jnp.where(column == at_clean, piece, 0.0),
            )

        zero = jnp.zeros((LANES, LANES), F32)
        totals = lax.fori_loop(0, tiles, sum_step, (zero, zero, zero), unroll=2)
        stat_out[b] = to_rows([top] + [jnp.sum(total, axis=1, keepdims=True) for total in totals])
        for k in range(3):
            stat_copy(b, k).start()
        return 0

    for k, table in enumerate(table_loads):
        if k == len(table_loads) - 1:
            table.finish()

        def product(i, _):
            rows = rows_at(0, i, TILE)
            logits[rows, k * piece_width : (k + 1) * piece_width] = dot_nn(normed[rows, :], table.value())
            return 0

        lax.fori_loop(0, seq_len // TILE, product, 0)
    lax.fori_loop(0, blocks, ask, 0)

    def scalars(b):
        here = info[:, rows_at(0, b, LANES)]
        step = jnp.maximum(here[2:3], 2.0)
        left = STEPS - step + 1.0
        beta = 1.0 / left
        keep = left / STEPS
        rest = (step - 1.0) / (STEPS * whole)
        own = stat_out[b]
        others = [stat_in[k, b] for k in range(3)]
        top = own[0:1]
        for stat in others:
            top = jnp.maximum(top, stat[0:1])
        total = own[1:2] * jnp.exp(own[0:1] - top)
        noised, clean = own[2:3], own[3:4]
        for stat in others:
            total = total + stat[1:2] * jnp.exp(stat[0:1] - top)
            noised, clean = noised + stat[2:3], clean + stat[3:4]
        return here, beta, keep, rest, top + jnp.log(total), noised, clean

    def measure(b, _):
        rows = rows_at(0, b, LANES)
        for k in range(3):
            stat_copy(b, k).wait_recv()
        _, _, keep, rest, log_total, _, _ = scalars(b)
        log_wide = spread(log_total)
        ratio = spread(keep / rest)

        def step(t, totals):
            logs, shares = totals
            probs = jnp.exp(logits[rows, tile_at(t)] - log_wide)
            logits[rows, tile_at(t)] = probs
            grown = 1.0 + probs * ratio
            return (logs + jnp.log(grown), shares + probs / grown)

        zero = jnp.zeros((LANES, LANES), F32)
        totals = lax.fori_loop(0, tiles, step, (zero, zero), unroll=2)
        sum_out[b] = to_rows([jnp.sum(total, axis=1, keepdims=True) for total in totals])
        for k in range(3):
            sum_copy(b, k).start()
        return 0

    lax.fori_loop(0, blocks, measure, 0)

    def pull(b):
        rows = rows_at(0, b, LANES)
        for k in range(3):
            sum_copy(b, k).wait_recv()
        here, beta, keep, rest, log_total, noised, clean = scalars(b)
        sums = sum_out[b] + sum_in[0, b] + sum_in[1, b] + sum_in[2, b]
        log_sum, share_sum = sums[0:1], sums[1:2] / rest
        same = here[0:1] == here[1:2]
        first_step = here[2:3] == 1.0
        base_a, more_a = beta / whole, 1.0 - beta
        base_w = base_a * rest
        joint = whole * base_w + more_a * rest + base_a * keep + jnp.where(same, more_a * keep, 0.0)
        ratio = keep / rest
        prob_n, prob_c = jnp.exp(noised - log_total), jnp.exp(clean - log_total)
        grown_n, grown_c = 1.0 + prob_n * ratio, 1.0 + prob_c * ratio
        marginal_n, marginal_c = rest * grown_n, rest * grown_c
        log_n, log_c = jnp.log(grown_n), jnp.log(grown_c)
        weight_n = jnp.where(same, 0.0, more_a * rest)
        weight_c = jnp.where(same, more_a * rest + base_a * keep + more_a * keep, base_a * keep)
        lift = jnp.log((keep + rest) / rest)
        cross = -base_w * log_sum - weight_n * log_n - weight_c * log_c + (base_w + weight_c) * lift
        model = base_a * (keep + whole * rest) + more_a * marginal_n
        divergence = cross / joint - jnp.log(joint) + jnp.log(model)
        loss = jnp.where(first_step, log_total - clean, divergence)
        losses[:, rows] = here[4:5] * loss
        weighted = base_w * share_sum + weight_n * prob_n / marginal_n + weight_c * prob_c / marginal_c
        aligned = base_a + more_a * prob_n
        centre = keep * (aligned / model - weighted / joint)
        scale = here[3:4]
        zero = jnp.zeros_like(scale)
        even = scale * jnp.where(first_step, 1.0, keep * base_a / model - centre)
        bent = scale * jnp.where(first_step, zero, -keep * base_w / joint / rest)
        at_n = prob_n * keep * (more_a / model - weight_n / joint / marginal_n)
        at_c = -prob_c * keep * (weight_c / joint / marginal_c)
        extra_n = spread(scale * jnp.where(first_step, zero, at_n))
        extra_c = spread(scale * jnp.where(first_step, -1.0, at_c))
        even, bent, ratio = spread(even), spread(bent), spread(ratio)
        at_noised, at_clean = places[b, 0], places[b, 1]

        def step(t, _):
            probs = logits[rows, tile_at(t)]
            column = lanes + (t * LANES).astype(F32)
            grad = probs * (even + bent / (1.0 + probs * ratio))
            grad = grad + jnp.where(column == at_noised, extra_n, 0.0)
            grad = grad + jnp.where(column == at_clean, extra_c, 0.0)
            grads[rows, tile_at(t)] = grad.astype(BF16)
            return 0

        lax.fori_loop(0, tiles, step, 0, unroll=2)

    def partial(start, j):
        base = start // LANES + j * (chunk // LANES)
        for b in range(chunk // LANES):
            pull(base + b)
        total = None
        for k, table in enumerate(table_loads):
            part = dot_nt(grads[rows_at(start, j, chunk), k * piece_width : (k + 1) * piece_width], table.value())
            total = part if total is None else total + part
        return total

    trade.give(0, partial(other, 0))
    for j in range(CHUNKS):
        if j + 1 < CHUNKS:
            trade.give(j + 1, partial(other, j + 1))
        trade.pass_on(j, partial(mine, j))
    turned[...] = jnp.transpose(normed[...])
    for k, d_table in enumerate(d_tables):
        weight_grad(turned, grads.at[:, k * piece_width : (k + 1) * piece_width], d_table)
    made()
    gain_total = jnp.zeros((1, gain.shape[1]), F32)
    for j in range(CHUNKS):
        rows = rows_at(0, j, chunk)
        back, gain_part = norm_back(trade.take(j), value[rows, :], gain[row : row + 1, :])
        gain_total = gain_total + gain_part
        grad_out[rows, :] = back
        share.put(j, back.astype(BF16))
    d_gain[...] = gain_total
    for j in range(CHUNKS):
        share.arrived(j)
    trade.close()
    share.close()

    def finish(b, _):
        for k in range(3):
            stat_copy(b, k).wait_send()
            sum_copy(b, k).wait_send()
        return 0

    lax.fori_loop(0, blocks, finish, 0)


def back_kernel(
    layer, normed, key_seg, query_seg, resid, w_query, w_out, w_in, gains, noised, clean, steps, counted, counts,
    projected, mixed, middle, normed_two, grad_out, branch, d_gain, losses, *refs, carry,
):
    pieces = len(carry.loads) - 1
    d_tables, refs = refs[:pieces], refs[pieces:]
    (result, normed_next, info), refs = refs[:3], refs[3:]
    loss_scratch, layer_refs = refs[:-LAYER_SCRATCH], refs[-LAYER_SCRATCH:]
    me = lax.axis_index(NARROW)
    carry.fetch()
    info[...] = jnp.zeros(info.shape, F32)
    mask = counted[...].astype(F32)
    for row, value in enumerate((noised[...], clean[...], steps[...])):
        info[row : row + 1, :] = value.astype(F32)
    info[3:4, :] = mask / counts[COUNT_ROW : COUNT_ROW + 1, 0:1]
    info[4:5, :] = mask
    greet([{NARROW: lax.rem(me + k, 4)} for k in range(1, 4)] + carry.peers())
    carry.begin(0, 1)

    def at_half():
        carry.begin(2)

    def at_feed():
        carry.fetched()
        carry.end(0)
        carry.hand_on(1)
        carry.begin(3)

    def at_sent():
        carry.leave(0, 1, 2, 3)
        carry.hand_on(2)
        carry.begin(4)

    def at_last():
        carry.hand_on(3)

    forward_part(
        layer,
        [lambda which: w_query[which], lambda: w_out[...], lambda: w_in[...], carry.loads[0].value],
        (at_half, at_feed, at_sent, at_last),
        normed, key_seg, query_seg, resid, gains,
        projected, mixed, middle, normed_two, result, normed_next, *layer_refs,
    )
    carry.hand_on(4)
    carry.end(1, 2, 3)
    loss_part(
        2 * layer + 2, normed_next, info, result, gains, carry.loads[1:], grad_out, branch, d_gain, losses, d_tables,
        *loss_scratch, *layer_refs[2:6], *layer_refs[-2:], made=lambda: carry.leave(*range(8, 8 + pieces)),
    )
    carry.gone()


def last_and_loss(
    layer, normed, key_seg, query_seg, resid, w_query, w_out, w_in, gains, tokens, counts, vocab, collective_id, loads
):
    seq_len, width = normed.shape
    heads_width = w_query.shape[2]
    half, blocks = seq_len // 2, seq_len // LANES
    pieces = len(loads) - 1
    return run(
        functools.partial(back_kernel, layer),
        "last_and_loss",
        [normed, key_seg, query_seg, resid, w_query, w_out, w_in, gains, *tokens, counts],
        layer_outs(seq_len, width, heads_width)
        + [
            jax.ShapeDtypeStruct((half, width), F32),
            jax.ShapeDtypeStruct((seq_len, width), BF16),
            jax.ShapeDtypeStruct((1, width), F32),
            jax.ShapeDtypeStruct((1, seq_len), F32),
        ]
        + [jax.ShapeDtypeStruct((width, vocab // pieces), BF16)] * pieces,
        [
            pltpu.VMEM((half, width), F32),
            pltpu.VMEM((seq_len, width), BF16),
            pltpu.VMEM((8, seq_len), F32),
            pltpu.VMEM((seq_len, vocab), F32),
            pltpu.VMEM((seq_len, vocab), BF16),
            pltpu.VMEM((blocks, 2, LANES, LANES), F32),
            pltpu.VMEM((width, seq_len), BF16),
            pltpu.VMEM((blocks, 8, LANES), F32),
            pltpu.VMEM((3, blocks, 8, LANES), F32),
            pltpu.VMEM((blocks, 8, LANES), F32),
            pltpu.VMEM((3, blocks, 8, LANES), F32),
        ]
        + [pltpu.SemaphoreType.DMA((3, blocks))] * 4
        + layer_scratch(seq_len, width, heads_width),
        collective_id,
        loads,
        lazy=(3, 6),
        early=(0, 1, 2, 3) + tuple(range(8, 8 + pieces)),
    )


def sum_ways(place, me, slow, fast, slows, group):
    near = [{NARROW: lax.rem(place + step, group)} for step in range(1, group)]
    return near, {WIDE: me + 1 - 2 * fast}


def tail_kernel(
    layers, branch, ids_all, losses, *refs, carry,
):
    gain_parts, refs = refs[: 2 * layers + 1], refs[2 * layers + 1 :]
    squares, refs = refs[: len(refs) - 24], refs[len(refs) - 24 :]
    tail_body(branch, ids_all, losses, gain_parts, squares, *refs, carry)


def tail_body(
    branch, ids_all, losses, gain_parts, squares,
    d_table, d_small, scalars,
    out_blocks, all_in, masked, picks, total, gains_out, gains_in, blocks, block_in, line_out, line_in,
    near, along, across,
    wide_send, wide_recv, far_send, far_recv, near_send, near_recv,
    sum_sems,
    carry,
):
    seq_len, width = branch.shape
    quarter, half = seq_len // 4, seq_len // 2
    owners = ids_all.shape[0]
    share, vocab = d_table.shape
    sibling, partner, mine, other = group_places(seq_len)
    place = lax.axis_index(NARROW)
    side = lax.div(place, 2)
    me, slow, fast, slows = wide_places(owners)
    beside = {WIDE: me + 1 - 2 * fast}
    group = near.shape[0]
    first = place * vocab
    around = [lax.rem(me + step, owners) for step in range(owners)]
    at_quarter = pl.multiple_of(mine + side * quarter, quarter)
    held = 2 * lax.rem(place, 2) + side

    def along_way(step):
        return {WIDE: 2 * lax.rem(slow + step, slows) + fast}

    def wide_copy(step):
        return remote(
            out_blocks.at[around[step]], all_in.at[me, held],
            wide_send.at[step], wide_recv.at[step], {WIDE: around[step]},
        )

    def far_copy(step):
        rows = all_in.at[around[step], held]
        return remote(rows, rows, far_send.at[step], far_recv.at[step], partner)

    def near_copy(step):
        rows = all_in.at[around[step], pl.ds(2 * lax.rem(place, 2), 2)]
        return remote(rows, rows, near_send.at[step], near_recv.at[step], sibling)

    def gain_near():
        return remote(gains_out, gains_in, sum_sems.at[0, 0], sum_sems.at[1, 0], sibling)

    def gain_pair(step):
        return remote(
            blocks.at[2 * lax.rem(slow + step, slows) + 1 - fast], block_in.at[step],
            sum_sems.at[2, step], sum_sems.at[3, step], beside,
        )

    def gain_line(step):
        return remote(line_out.at[step], line_in.at[step], sum_sems.at[4, step], sum_sems.at[5, step], along_way(step))

    near_ways = [{NARROW: lax.rem(place + step, group)} for step in range(1, group)]
    greet([{WIDE: device} for device in around[1:]] + near_ways)
    gains_out[...] = jnp.zeros(gains_out.shape, F32)
    for row, part in enumerate(gain_parts):
        gains_out[row : row + 1, :] = part[...]
    gain_near().start()
    out_blocks[...] = jnp.transpose(branch[pl.ds(at_quarter, quarter), :]).reshape(out_blocks.shape)
    for step in range(1, owners):
        wide_copy(step).start()
    all_in[me, held] = out_blocks[me]
    carry.begin(*carry.all())
    gain_near().wait_recv()
    both = gains_out[...] + gains_in[...]
    for owner in range(owners):
        blocks[owner] = lax.dot_general(
            both, feature_places(owner, width, share).astype(F32), (((1,), (1,)), ((), ())),
            precision=lax.Precision.HIGHEST, preferred_element_type=F32,
        )
    for step in range(slows):
        gain_pair(step).start()

    def hand_on(step):
        if step:
            wide_copy(owners - step).wait_recv()
        far_copy(step).start()

    def hand_over(step):
        far_copy(step).wait_recv()
        near_copy(step).start()

    def gather_grad(step, first_turn):
        near_copy(step).wait_recv()
        row = around[step]

        for k in range(seq_len // quarter):
            columns = slice(k * quarter, (k + 1) * quarter)
            high, found = token_parts(ids_all[row, k : k + 1, :], first)
            picks[:, columns] = found
            grads = all_in[row, k]
            for part in range(vocab // LANES):
                inside = jnp.where(high == part, 1.0, 0.0).astype(BF16)
                masked[part * share : (part + 1) * share, columns] = grads * inside
        span = 4 * share

        def some(i, _):
            rows = rows_at(0, i, span)
            part = dot_nt(masked[rows, :], picks[...])
            total[rows, :] = part if first_turn else total[rows, :] + part
            return 0

        lax.fori_loop(0, total.shape[0] // span, some, 0)

    order = [0] + list(range(1, owners))
    for turn in range(owners + 2):
        if turn < owners:
            hand_on(order[turn])
        if 1 <= turn < owners + 1:
            hand_over(order[turn - 1])
        if turn == 1:
            for step in list(range(1, slows)) + [0]:
                gain_pair(step).wait_recv()
                line_out[step] = blocks[2 * lax.rem(slow + step, slows) + fast] + block_in[step]
                if step:
                    gain_line(step).start()
        if turn >= 2:
            gather_grad(order[turn - 2], turn == 2)
    for t in range(vocab // LANES):
        d_table[:, t * LANES : (t + 1) * LANES] = total[t * share : (t + 1) * share, :]
    small = line_out[0]
    for step in range(1, slows):
        gain_line(step).wait_recv()
        small = small + line_in[step]
    d_small[...] = small
    carry.end(*carry.all())
    square = jnp.sum(d_table[...] * d_table[...])
    for part in squares:
        square = square + part[0, 0]
    for load in carry.loads:
        square = square + load.squares[0, 0]
    lead = (place == 0).astype(F32)
    square = square + lead * jnp.sum(small * small)
    lanes = lax.broadcasted_iota(jnp.int32, (8, LANES), 1)
    given = jnp.where(lanes == 0, square, jnp.where(lanes == 1, lead * jnp.sum(losses[...]), 0.0))

    def scalar_near(step):
        return remote(near.at[place], near.at[place], sum_sems.at[6, step], sum_sems.at[7, step], near_ways[step - 1])

    def scalar_line(step):
        return remote(along.at[slow], along.at[slow], sum_sems.at[8, step], sum_sems.at[9, step], along_way(step))

    near[place] = given
    for step in range(1, group):
        scalar_near(step).start()
    for step in range(1, group):
        scalar_near(step).wait()
    along[slow] = jnp.sum(near[...], axis=0)
    for step in range(1, slows):
        scalar_line(step).start()
    for step in range(1, slows):
        scalar_line(step).wait()
    across[0] = jnp.sum(along[...], axis=0)
    last = remote(across.at[0], across.at[1], sum_sems.at[10, 0], sum_sems.at[11, 0], beside)
    last.start()
    last.wait()
    scalars[...] = across[0] + across[1]
    gain_near().wait_send()
    for step in range(owners):
        far_copy(step).wait_send()
        near_copy(step).wait_send()
        if step:
            wide_copy(step).wait_send()
    for step in range(slows):
        gain_pair(step).wait_send()
        if step:
            gain_line(step).wait_send()


def tail(branch, ids_all, losses, gain_parts, squares, share, vocab, group, collective_id, loads):
    seq_len, width = branch.shape
    owners = ids_all.shape[0]
    slows = owners // 2
    dma = pltpu.SemaphoreType.DMA
    small = (8, LANES)
    return run(
        functools.partial(tail_kernel, (len(gain_parts) - 1) // 2),
        "tail",
        [branch, ids_all, losses, *gain_parts, *squares],
        [
            jax.ShapeDtypeStruct((share, vocab), F32),
            jax.ShapeDtypeStruct(small, F32),
            jax.ShapeDtypeStruct(small, F32),
        ],
        [
            pltpu.VMEM((owners, share, seq_len // 4), BF16),
            pltpu.VMEM((owners, 4, share, seq_len // 4), BF16),
            pltpu.VMEM((vocab // LANES * share, seq_len), BF16),
            pltpu.VMEM((LANES, seq_len), BF16),
            pltpu.VMEM((vocab // LANES * share, LANES), F32),
            pltpu.VMEM((8, width), F32),
            pltpu.VMEM((8, width), F32),
            pltpu.VMEM((owners,) + small, F32),
            pltpu.VMEM((slows,) + small, F32),
            pltpu.VMEM((slows,) + small, F32),
            pltpu.VMEM((slows,) + small, F32),
            pltpu.VMEM((group,) + small, F32),
            pltpu.VMEM((slows,) + small, F32),
            pltpu.VMEM((2,) + small, F32),
        ]
        + [dma((owners,))] * 6
        + [dma((12, max(slows, group)))],
        collective_id,
        loads,
    )


PIECES = 4
TABLE, ATTN_IN, ATTN_OUT, FFN_IN, FFN_OUT = range(5)


def shares_tile(wide, narrow, noised, attn_out, ffn_in, tables):
    rows, seq_len = noised.shape
    return (
        attn_out.shape[0] == 2
        and narrow == 4
        and wide % 2 == 0
        and rows == 1
        and seq_len % (2 * CHUNKS * 128) == 0
        and tables.shape[1] * wide % 256 == 0
        and attn_out.shape[1] % 16 == 0
        and attn_out.shape[1] <= LANES
        and ffn_in.shape[2] % 128 == 0
        and tables.shape[1] == attn_out.shape[1]
        and tables.shape[2] % (PIECES * TILE) == 0
    )


def per_device(wide, narrow, *arrays):
    noised, attn_out, ffn_in, tables = arrays[0], arrays[6], arrays[7], arrays[9]
    if shares_tile(wide, narrow, noised, attn_out, ffn_in, tables):
        return tiled_device(wide, *arrays)
    return general_device(*arrays)


def tiled_device(
    wide,
    noised,
    clean,
    timesteps,
    segments,
    counted,
    attn_in,
    attn_out,
    ffn_in,
    ffn_out,
    tables,
    gains,
    attn_in_mean,
    attn_out_mean,
    ffn_in_mean,
    ffn_out_mean,
    tables_mean,
    gains_mean,
    attn_in_square,
    attn_out_square,
    ffn_in_square,
    ffn_out_square,
    tables_square,
    gains_square,
):
    layers = attn_in.shape[0]
    gain_rows, gain_cols = gains.shape
    share, vocab = tables.shape[1:]
    leads = (1, 0, 0, 0)
    four = (attn_in, attn_out, ffn_in, ffn_out)

    def joined(value, lead):
        return value.reshape(value.shape[:lead] + (-1,) + value.shape[lead + 2 :])

    ids = noised.reshape(4, -1)
    steps = timesteps.reshape(-1, LANES)
    half_width = D // 2
    rates = jnp.exp(-math.log(10000.0) * jnp.arange(half_width, dtype=F32) / half_width)[None, :]
    quarter = vocab // PIECES
    windows = [(k * quarter, quarter) for k in range(PIECES)]
    key_seg, query_seg = segments.reshape(-1, 1), segments.reshape(1, -1)
    weights = (attn_in, attn_out, ffn_in, ffn_out)
    (residual, normed, gain_w, counts, ids_all, projected, mixed, middle, normed_two, result, normed_next), carried = front(
        ids, counted, gains, steps, rates, tables, key_seg, query_seg, wide, attn_out.shape[2], 0,
        [GatherLoad(value, 0, lead, wide, place=KEPT) for value, lead in zip(weights, leads)]
        + [GatherLoad(value, 1, lead, wide) for value, lead in zip(weights[:3], leads)]
        + [SlowLoad(ffn_out, 1, 0, wide)],
    )
    token_total = counts[gain_rows, 0]
    first_w = [joined(value, lead) for value, lead in zip(carried[:4], leads)]
    query_w, output_w, expand_w = [joined(value, lead) for value, lead in zip(carried[4:7], leads)]
    kept = [(residual, normed, projected, mixed, middle, normed_two, *first_w)]
    (projected, mixed, middle, normed_two, grad, branch, gain_final, losses, *d_last), (reduce_w,) = last_and_loss(
        1, normed_next, key_seg, query_seg, result, query_w, output_w, expand_w, gain_w,
        (noised, clean, timesteps, counted), counts, vocab, 1,
        [FastLoad(carried[7], 0, wide)]
        + [GatherLoad(tables, 1, 0, wide, window, place=LOCAL) for window in windows],
    )
    kept.append(
        (result, normed_next, projected, mixed, middle, normed_two, query_w, output_w, expand_w, joined(reduce_w, 0))
    )
    own, squares = {}, []

    def by_owner(value, lead):
        shape = value.shape
        return value.reshape(shape[:lead] + (wide, shape[lead] // wide) + shape[lead + 1 :])

    def landed(key, results):
        own[key] = results[0]
        squares.append(results[1])
        return results[2:]

    hidden = ffn_in.shape[2]
    made = jax.ShapeDtypeStruct((wide, share, hidden), BF16)
    made_in = jax.ShapeDtypeStruct((3, wide, share, attn_in.shape[3]), BF16)
    made_out = jax.ShapeDtypeStruct((wide, share, attn_out.shape[2]), BF16)

    def start_last(carry, d_red, d_in):
        carry.loads[PIECES].full, carry.loads[PIECES + 1].full = d_red, d_in
        carry.begin(*range(PIECES))

    half_pieces = PIECES // 2
    points = (
        start_last,
        lambda carry: carry.begin(PIECES, PIECES + 1),
        lambda carry: carry.hand_on(*range(half_pieces)),
        lambda carry: carry.hand_on(*range(half_pieces, PIECES)),
        lambda carry, d_out, d_query: None,
    )
    residual, normed, projected, mixed, middle, normed_two, query_w, output_w, expand_w, reduce_w = kept[1]
    (grad, branch, d_out, d_query, gain_two, gain_one), carried = backward_block(
        1, None, points, grad, branch, reduce_w, expand_w, output_w, normed_two, middle, gain_w, mixed,
        projected, key_seg, query_seg, query_w, residual, normed, wide, 2,
        [ReduceLoad(by_owner(piece, 0), 0) for piece in d_last]
        + [PairLoad(made, 0, True), PairLoad(made, 0, True)],
    )
    for k in range(PIECES):
        carried = landed((TABLE, k), carried)
    red_sums, in_sums = carried
    gain_grads = [None, None, gain_one, gain_two, gain_final]

    def start_first(carry, d_red, d_in):
        carry.loads[4].full, carry.loads[5].full = d_red, d_in
        carry.begin(0, 1, 2, 3)

    def sent_first(carry, d_out, d_query):
        carry.hand_on(5)
        carry.loads[6].full, carry.loads[7].full = d_out, d_query
        carry.begin(6, 7)

    points = (
        start_first,
        lambda carry: carry.begin(4, 5),
        lambda carry: carry.hand_on(2, 3),
        lambda carry: carry.hand_on(4),
        sent_first,
    )
    residual, normed, projected, mixed, middle, normed_two, query_w, output_w, expand_w, reduce_w = kept[0]
    (grad, branch, _, d_query, gain_two, gain_one), carried = backward_block(
        0, math.sqrt(D), points, grad, branch, reduce_w, expand_w, output_w, normed_two, middle, gain_w, mixed,
        projected, key_seg, query_seg, query_w, residual, normed, wide, 3,
        [LineLoad(red_sums, wide), LineLoad(in_sums, wide), ReduceLoad(d_out, 0), ReduceLoad(d_query, 1)]
        + [ReduceLoad(made, 0, True), ReduceLoad(made, 0, True), PairLoad(made_out, 0, True), PairLoad(made_in, 1, True)],
    )
    for key in ((FFN_OUT, 1), (FFN_IN, 1), (ATTN_OUT, 1), (ATTN_IN, 1), (FFN_OUT, 0), (FFN_IN, 0)):
        carried = landed(key, carried)
    out_sums, in_sums = carried
    gain_grads[:2] = gain_one, gain_two

    (own_first, total_small, scalars), carried = tail(
        branch, ids_all, losses, gain_grads, squares, share, vocab, 4, 4,
        [LineLoad(out_sums, wide), LineLoad(in_sums, wide)],
    )
    own[ATTN_OUT, 0], own[ATTN_IN, 0] = carried[0], carried[2]
    grad_attn_in, grad_attn_out, grad_ffn_in, grad_ffn_out = [
        jnp.stack([own[name, index] for index in range(layers)]) for name in (ATTN_IN, ATTN_OUT, FFN_IN, FFN_OUT)
    ]
    grad_tables = jnp.stack([own_first, jnp.concatenate([own[TABLE, k] for k in range(PIECES)], axis=1)])
    grad_gains = total_small[:gain_rows, :gain_cols]
    total_square, loss_sum = scalars[0, 0], scalars[0, 1]
    grad_norm = jnp.sqrt(total_square)
    factor = jnp.minimum(1.0, CLIP_NORM / (grad_norm + 1e-06))
    results = [loss_sum, token_total, grad_norm]
    for weight, gradient, first, second, decay, rate in (
        (attn_in, grad_attn_in, attn_in_mean, attn_in_square, WEIGHT_DECAY, LEARN_RATE),
        (attn_out, grad_attn_out, attn_out_mean, attn_out_square, WEIGHT_DECAY, LEARN_RATE),
        (ffn_in, grad_ffn_in, ffn_in_mean, ffn_in_square, WEIGHT_DECAY, LEARN_RATE),
        (ffn_out, grad_ffn_out, ffn_out_mean, ffn_out_square, WEIGHT_DECAY, LEARN_RATE),
        (tables, grad_tables, tables_mean, tables_square, WEIGHT_DECAY, LEARN_RATE),
        (gains, grad_gains, gains_mean, gains_square, 0.0, GAIN_RATE),
    ):
        results += adam(weight, factor * gradient, first, second, decay, rate)
    return tuple(results)


def solution(mesh):
    wide, narrow = mesh.shape[WIDE], mesh.shape[NARROW]
    placed = (
        P(WIDE, None),
        P(WIDE, None),
        P(WIDE, None),
        P(WIDE, None),
        P(WIDE, None),
        P(None, None, WIDE, NARROW),
        P(None, WIDE, NARROW),
        P(None, WIDE, NARROW),
        P(None, WIDE, NARROW),
        P(None, WIDE, NARROW),
        P(None, WIDE),
        P(None, None, WIDE, NARROW),
        P(None, WIDE, NARROW),
        P(None, WIDE, NARROW),
        P(None, WIDE, NARROW),
        P(None, WIDE, NARROW),
        P(None, WIDE),
        P(None, None, WIDE, NARROW),
        P(None, WIDE, NARROW),
        P(None, WIDE, NARROW),
        P(None, WIDE, NARROW),
        P(None, WIDE, NARROW),
        P(None, WIDE),
    )
    return jax.shard_map(
        functools.partial(per_device, wide, narrow),
        mesh=mesh,
        in_specs=placed,
        out_specs=(
            P(),
            P(),
            P(),
            P(None, None, WIDE, NARROW),
            P(None, None, WIDE, NARROW),
            P(None, None, WIDE, NARROW),
            P(None, None, WIDE, NARROW),
            P(None, WIDE, NARROW),
            P(None, WIDE, NARROW),
            P(None, WIDE, NARROW),
            P(None, WIDE, NARROW),
            P(None, WIDE, NARROW),
            P(None, WIDE, NARROW),
            P(None, WIDE, NARROW),
            P(None, WIDE, NARROW),
            P(None, WIDE, NARROW),
            P(None, WIDE, NARROW),
            P(None, WIDE, NARROW),
            P(None, WIDE, NARROW),
            P(None, WIDE, NARROW),
            P(None, WIDE, NARROW),
            P(None, WIDE, NARROW),
            P(None, WIDE, NARROW),
            P(None, WIDE),
            P(None, WIDE),
            P(None, WIDE),
            P(None, WIDE),
        ),
        check_vma=False,
    )
```

```python
import functools
import math

import jax
import jax.numpy as jnp
from jax import lax
from jax.experimental import pallas as pl
from jax.experimental.pallas import tpu as pltpu
from jax.sharding import PartitionSpec as P

D = 768
HD = 64
V = 8192
STEPS = 1000
ADAM_STEP = 10


NORM_EPS = 1e-05
LEARN_RATE = 0.05
GAIN_RATE = 0.75
FIRST_DECAY = 0.9
SECOND_DECAY = 0.999
ADAM_EPS = 1e-08
WEIGHT_DECAY = 0.01
CLIP_NORM = 0.005
WIDE, NARROW = "wide", "narrow"


def add_heads(partial_value):
    return lax.psum(partial_value, NARROW)


def back_heads(partial_value):
    return lax.psum(partial_value, NARROW)


def rms_forward(value, gain):
    scale_row = lax.rsqrt(jnp.mean(value * value, axis=-1, keepdims=True) + NORM_EPS)
    return (value * scale_row * gain, scale_row)


def rms_backward(grad, value, scale_row, gain):
    unit = value * scale_row
    scaled = grad * gain
    back = scale_row * (scaled - unit * jnp.mean(scaled * unit, axis=-1, keepdims=True))
    return (back, jnp.sum(grad * unit, axis=0))


def time_features(timestep_row):
    half_width = D // 2
    rates = jnp.exp(-math.log(10000.0) * jnp.arange(half_width, dtype=jnp.float32) / half_width)
    angles = timestep_row.astype(jnp.float32)[:, None] * rates[None, :]
    return jnp.concatenate([jnp.sin(angles), jnp.cos(angles)], axis=1)


def masked_scores(queries, key_rows, segment):
    scores = jnp.einsum(
        "qhd,khd->hqk", queries, key_rows, preferred_element_type=jnp.float32
    ) * HD ** (-0.5)
    return jnp.where((segment[:, None] == segment[None, :])[None], scores, -1e30)


def attend(entry):
    queries, key_rows, values, segment = entry
    scores = masked_scores(queries, key_rows, segment)
    row_top = jnp.max(scores, axis=-1, keepdims=True)
    log_total = row_top + jnp.log(jnp.sum(jnp.exp(scores - row_top), axis=-1, keepdims=True))
    probs = jnp.exp(scores - log_total).astype(jnp.bfloat16)
    mixed = jnp.einsum("hqk,khd->qhd", probs, values, preferred_element_type=jnp.float32)
    return (mixed.astype(jnp.bfloat16), log_total)


def attend_back(entry):
    queries, key_rows, values, segment, log_total, grad_mixed = entry
    probs = jnp.exp(masked_scores(queries, key_rows, segment) - log_total)
    grad_probs = jnp.einsum("qhd,khd->hqk", grad_mixed, values, preferred_element_type=jnp.float32)
    grad_scores = (
        probs * (grad_probs - jnp.sum(probs * grad_probs, axis=-1, keepdims=True))
    ).astype(jnp.bfloat16)
    grad_query = jnp.einsum(
        "hqk,khd->qhd", grad_scores, key_rows, preferred_element_type=jnp.float32
    ) * HD ** (-0.5)
    grad_key = jnp.einsum(
        "hqk,qhd->khd", grad_scores, queries, preferred_element_type=jnp.float32
    ) * HD ** (-0.5)
    grad_value = jnp.einsum(
        "hqk,qhd->khd", probs.astype(jnp.bfloat16), grad_mixed, preferred_element_type=jnp.float32
    )
    return (grad_query, grad_key, grad_value)


def layer_forward(residual, segments, query_w, output_w, expand_w, reduce_w, gain_attn, gain_ffn):
    seq_count, seq_len = segments.shape
    normed, scale_one = rms_forward(residual, gain_attn)
    normed = normed.astype(jnp.bfloat16)
    projected = jnp.einsum(
        "sd,cde->cse", normed, query_w, preferred_element_type=jnp.float32
    ).astype(jnp.bfloat16)
    heads = projected.reshape(3, seq_count, seq_len, -1, HD)
    mixed, log_total = lax.map(attend, (heads[0], heads[1], heads[2], segments))
    mixed = mixed.reshape(seq_count * seq_len, -1)
    middle = residual + add_heads(
        jnp.einsum("se,de->sd", mixed, output_w, preferred_element_type=jnp.float32)
    )
    normed_two, scale_two = rms_forward(middle, gain_ffn)
    normed_two = normed_two.astype(jnp.bfloat16)
    before = jnp.dot(normed_two, expand_w, preferred_element_type=jnp.float32)
    after = jax.nn.gelu(before).astype(jnp.bfloat16)
    result = middle + add_heads(
        jnp.einsum("sf,df->sd", after, reduce_w, preferred_element_type=jnp.float32)
    )
    return (
        result,
        (
            residual,
            scale_one,
            normed,
            projected,
            log_total,
            mixed,
            middle,
            scale_two,
            normed_two,
            before,
            after,
        ),
    )


def layer_backward(
    grad, kept, segments, query_w, output_w, expand_w, reduce_w, gain_attn, gain_ffn
):
    (
        residual,
        scale_one,
        normed,
        projected,
        log_total,
        mixed,
        middle,
        scale_two,
        normed_two,
        before,
        after,
    ) = kept
    seq_count, seq_len = segments.shape
    grad_branch = grad.astype(jnp.bfloat16)
    grad_after = jnp.dot(grad_branch, reduce_w, preferred_element_type=jnp.float32)
    grad_reduce = jnp.einsum("sd,sf->df", grad_branch, after, preferred_element_type=jnp.float32)
    _, gelu_pull = jax.vjp(jax.nn.gelu, before)
    grad_before = gelu_pull(grad_after)[0].astype(jnp.bfloat16)
    grad_expand = jnp.einsum(
        "sd,sf->df", normed_two, grad_before, preferred_element_type=jnp.float32
    )
    grad_normed_two = back_heads(
        jnp.einsum("sf,df->sd", grad_before, expand_w, preferred_element_type=jnp.float32)
    )
    grad_middle, grad_gain_ffn = rms_backward(grad_normed_two, middle, scale_two, gain_ffn)
    grad_middle = grad_middle + grad
    grad_attn = grad_middle.astype(jnp.bfloat16)
    grad_mixed = jnp.dot(grad_attn, output_w, preferred_element_type=jnp.float32).astype(
        jnp.bfloat16
    )
    grad_output = jnp.einsum("sd,se->de", grad_attn, mixed, preferred_element_type=jnp.float32)
    heads = projected.reshape(3, seq_count, seq_len, -1, HD)
    grad_query, grad_key, grad_value = lax.map(
        attend_back,
        (
            heads[0],
            heads[1],
            heads[2],
            segments,
            log_total,
            grad_mixed.reshape(seq_count, seq_len, -1, HD),
        ),
    )
    grad_projected = (
        jnp.stack([grad_query, grad_key, grad_value])
        .reshape(3, seq_count * seq_len, -1)
        .astype(jnp.bfloat16)
    )
    grad_query_w = jnp.einsum(
        "sd,cse->cde", normed, grad_projected, preferred_element_type=jnp.float32
    )
    grad_normed = back_heads(
        jnp.einsum("cse,cde->sd", grad_projected, query_w, preferred_element_type=jnp.float32)
    )
    grad_input, grad_gain_attn = rms_backward(grad_normed, residual, scale_one, gain_attn)
    return (
        grad_input + grad_middle,
        (
            grad_query_w,
            grad_output,
            grad_expand,
            grad_reduce,
            jnp.stack([grad_gain_attn, grad_gain_ffn]),
        ),
    )


def adam(weight, grad, first, second, decay, rate):
    first_new = FIRST_DECAY * first + (1.0 - FIRST_DECAY) * grad
    second_new = SECOND_DECAY * second + (1.0 - SECOND_DECAY) * grad * grad
    first_hat = first_new / (1.0 - FIRST_DECAY**ADAM_STEP)
    second_hat = second_new / (1.0 - SECOND_DECAY**ADAM_STEP)
    weight_new = weight - rate * (first_hat / (jnp.sqrt(second_hat) + ADAM_EPS) + decay * weight)
    return (weight_new, first_new, second_new, weight_new.astype(jnp.bfloat16))


def general_device(
    noised,
    clean,
    timesteps,
    segments,
    counted,
    attn_in,
    attn_out,
    ffn_in,
    ffn_out,
    tables,
    gains,
    attn_in_mean,
    attn_out_mean,
    ffn_in_mean,
    ffn_out_mean,
    tables_mean,
    gains_mean,
    attn_in_square,
    attn_out_square,
    ffn_in_square,
    ffn_out_square,
    tables_square,
    gains_square,
):
    layers = attn_in.shape[0]
    mask = counted.reshape(-1).astype(jnp.float32)
    token_total = lax.psum(jnp.sum(mask), WIDE)
    query_w, output_w, expand_w, reduce_w, table_w, gain_low = (
        lax.all_gather(attn_in.astype(jnp.bfloat16), WIDE, axis=2, tiled=True),
        lax.all_gather(attn_out.astype(jnp.bfloat16), WIDE, axis=1, tiled=True),
        lax.all_gather(ffn_in.astype(jnp.bfloat16), WIDE, axis=1, tiled=True),
        lax.all_gather(ffn_out.astype(jnp.bfloat16), WIDE, axis=1, tiled=True),
        lax.all_gather(tables.astype(jnp.bfloat16), WIDE, axis=1, tiled=True),
        lax.all_gather(gains.astype(jnp.bfloat16), WIDE, axis=1, tiled=True),
    )
    gain_w = gain_low.astype(jnp.float32)
    noised_flat = noised.reshape(-1)
    clean_flat = clean.reshape(-1)
    step_flat = timesteps.reshape(-1)
    vocab_local = table_w.shape[2]
    vocab_ids = lax.axis_index(NARROW) * vocab_local + jnp.arange(vocab_local, dtype=jnp.int32)
    picks = (noised_flat[:, None] == vocab_ids[None, :]).astype(jnp.bfloat16)
    looked = add_heads(
        jnp.einsum("sv,dv->sd", picks, table_w[0], preferred_element_type=jnp.float32)
    )
    residual = math.sqrt(D) * looked + time_features(step_flat)
    kept_layers = []
    for layer_index in range(layers):
        residual, kept = layer_forward(
            residual,
            segments,
            query_w[layer_index],
            output_w[layer_index],
            expand_w[layer_index],
            reduce_w[layer_index],
            gain_w[2 * layer_index],
            gain_w[2 * layer_index + 1],
        )
        kept_layers.append(kept)
    final, scale_final = rms_forward(residual, gain_w[2 * layers])
    final_low = final.astype(jnp.bfloat16)
    logits = jnp.dot(final_low, table_w[1], preferred_element_type=jnp.float32)
    local_top = jnp.max(logits, axis=1)
    row_top = lax.pmax(local_top, NARROW)
    row_total = lax.psum(jnp.sum(jnp.exp(logits - row_top[:, None]), axis=1), NARROW)
    log_probs = logits - (row_top + jnp.log(row_total))[:, None]
    probs = jnp.exp(log_probs)
    clamped = jnp.maximum(step_flat, 2).astype(jnp.float32)[:, None]
    beta = 1.0 / (STEPS - clamped + 1.0)
    retain = (STEPS - clamped + 1.0) / STEPS
    spread = (clamped - 1.0) / (STEPS * V)
    at_noised = (vocab_ids[None, :] == noised_flat[:, None]).astype(jnp.float32)
    at_clean = (vocab_ids[None, :] == clean_flat[:, None]).astype(jnp.float32)
    forward_fac = beta / V + (1.0 - beta) * at_noised
    backward_fac = retain * at_clean + spread
    joint = forward_fac * backward_fac
    marginal = retain * probs + spread
    joint_total, cross, model_total, weighted, aligned, clean_logp = lax.psum(
        (
            jnp.sum(joint, axis=1),
            jnp.sum(joint * (jnp.log(backward_fac) - jnp.log(marginal)), axis=1),
            jnp.sum(forward_fac * marginal, axis=1),
            jnp.sum(probs * joint / marginal, axis=1),
            jnp.sum(forward_fac * probs, axis=1),
            jnp.sum(at_clean * log_probs, axis=1),
        ),
        NARROW,
    )
    divergence = cross / joint_total - jnp.log(joint_total) + jnp.log(model_total)
    first_step = step_flat == 1
    losses = jnp.where(first_step, -clean_logp, divergence)
    pull = retain * (
        -(joint / joint_total[:, None]) / marginal + forward_fac / model_total[:, None]
    )
    centre = retain[:, 0] * (-weighted / joint_total + aligned / model_total)
    grad_kl = probs * (pull - centre[:, None])
    grad_recon = probs - at_clean
    grad_logits = (
        (mask / token_total)[:, None] * jnp.where(first_step[:, None], grad_recon, grad_kl)
    ).astype(jnp.bfloat16)
    grad_table_out = jnp.einsum(
        "sd,sv->dv", final_low, grad_logits, preferred_element_type=jnp.float32
    )
    grad_final = back_heads(
        jnp.einsum("sv,dv->sd", grad_logits, table_w[1], preferred_element_type=jnp.float32)
    )
    grad_x, grad_gain_final = rms_backward(grad_final, residual, scale_final, gain_w[2 * layers])
    layer_grads = [None] * layers
    for layer_index in reversed(range(layers)):
        grad_x, produced = layer_backward(
            grad_x,
            kept_layers[layer_index],
            segments,
            query_w[layer_index],
            output_w[layer_index],
            expand_w[layer_index],
            reduce_w[layer_index],
            gain_w[2 * layer_index],
            gain_w[2 * layer_index + 1],
        )
        layer_grads[layer_index] = produced
    grad_look = (math.sqrt(D) * grad_x).astype(jnp.bfloat16)
    grad_table_in = jnp.einsum("sd,sv->dv", grad_look, picks, preferred_element_type=jnp.float32)
    stacked = [jnp.stack([entry[which] for entry in layer_grads]) for which in range(5)]
    gain_layers = stacked[4].reshape(2 * layers, -1)
    grad_tables_all = jnp.stack([grad_table_in, grad_table_out])
    grad_attn_in, grad_attn_out, grad_ffn_in, grad_ffn_out, grad_tables, grad_gains = (
        lax.psum_scatter(stacked[0], WIDE, scatter_dimension=2, tiled=True),
        lax.psum_scatter(stacked[1], WIDE, scatter_dimension=1, tiled=True),
        lax.psum_scatter(stacked[2], WIDE, scatter_dimension=1, tiled=True),
        lax.psum_scatter(stacked[3], WIDE, scatter_dimension=1, tiled=True),
        lax.psum_scatter(grad_tables_all, WIDE, scatter_dimension=1, tiled=True),
        lax.psum_scatter(
            jnp.concatenate([gain_layers, grad_gain_final[None, :]], axis=0),
            WIDE,
            scatter_dimension=1,
            tiled=True,
        ),
    )
    narrow_first = (lax.axis_index(NARROW) == 0).astype(jnp.float32)
    squares = (
        jnp.sum(grad_attn_in * grad_attn_in)
        + jnp.sum(grad_attn_out * grad_attn_out)
        + jnp.sum(grad_ffn_in * grad_ffn_in)
        + jnp.sum(grad_ffn_out * grad_ffn_out)
        + jnp.sum(grad_tables * grad_tables)
        + narrow_first * jnp.sum(grad_gains * grad_gains)
    )
    squares, loss_sum = lax.psum(
        (squares, narrow_first * jnp.sum(mask * losses)), (WIDE, NARROW)
    )
    grad_norm = jnp.sqrt(squares)
    factor = jnp.minimum(1.0, CLIP_NORM / (grad_norm + 1e-06))
    attn_in_next, attn_in_mean_next, attn_in_square_next, attn_in_copy = adam(
        attn_in, factor * grad_attn_in, attn_in_mean, attn_in_square, WEIGHT_DECAY, LEARN_RATE
    )
    attn_out_next, attn_out_mean_next, attn_out_square_next, attn_out_copy = adam(
        attn_out, factor * grad_attn_out, attn_out_mean, attn_out_square, WEIGHT_DECAY, LEARN_RATE
    )
    ffn_in_next, ffn_in_mean_next, ffn_in_square_next, ffn_in_copy = adam(
        ffn_in, factor * grad_ffn_in, ffn_in_mean, ffn_in_square, WEIGHT_DECAY, LEARN_RATE
    )
    ffn_out_next, ffn_out_mean_next, ffn_out_square_next, ffn_out_copy = adam(
        ffn_out, factor * grad_ffn_out, ffn_out_mean, ffn_out_square, WEIGHT_DECAY, LEARN_RATE
    )
    tables_next, tables_mean_next, tables_square_next, tables_copy = adam(
        tables, factor * grad_tables, tables_mean, tables_square, WEIGHT_DECAY, LEARN_RATE
    )
    gains_next, gains_mean_next, gains_square_next, gains_copy = adam(
        gains, factor * grad_gains, gains_mean, gains_square, 0.0, GAIN_RATE
    )
    return (
        loss_sum,
        token_total,
        grad_norm,
        attn_in_next,
        attn_in_mean_next,
        attn_in_square_next,
        attn_in_copy,
        attn_out_next,
        attn_out_mean_next,
        attn_out_square_next,
        attn_out_copy,
        ffn_in_next,
        ffn_in_mean_next,
        ffn_in_square_next,
        ffn_in_copy,
        ffn_out_next,
        ffn_out_mean_next,
        ffn_out_square_next,
        ffn_out_copy,
        tables_next,
        tables_mean_next,
        tables_square_next,
        tables_copy,
        gains_next,
        gains_mean_next,
        gains_square_next,
        gains_copy,
    )


MESH = pl.DeviceIdType.MESH
SLOW, FAST = 1, 2
HBM, KEPT, LOCAL = 1, 2, 3
F32 = jnp.float32
BF16 = jnp.bfloat16
CHUNKS = 4
SPAN = 2
VMEM_LIMIT = 61 * 1024 * 1024
FORWARD_KIND = BF16
BACKWARD_KIND = BF16


def whole_vmem():
    return pl.BlockSpec(memory_space=pltpu.VMEM)


def dot_nn(a, b):
    return lax.dot_general(a, b, (((1,), (0,)), ((), ())), preferred_element_type=F32)


def dot_nt(a, b):
    return lax.dot_general(a, b, (((1,), (1,)), ((), ())), preferred_element_type=F32)


def remote(src, dst, send_sem, recv_sem, device):
    return pltpu.make_async_remote_copy(
        src_ref=src,
        dst_ref=dst,
        send_sem=send_sem,
        recv_sem=recv_sem,
        device_id=device,
        device_id_type=MESH,
    )


def greet(devices):
    barrier = pltpu.get_barrier_semaphore()
    for device in devices:
        pl.semaphore_signal(barrier, inc=1, device_id=device, device_id_type=MESH)
    pl.semaphore_wait(barrier, len(devices))


def group_places(seq_len):
    me = lax.axis_index(NARROW)
    core = lax.rem(me, 2)
    half = seq_len // 2
    mine = pl.multiple_of(core * half, half)
    other = pl.multiple_of((1 - core) * half, half)
    return ({NARROW: me + 1 - 2 * core}, {NARROW: lax.rem(me + 2, 4)}, mine, other)


class Exchange:
    def __init__(self, refs, sems, base, sibling, partner):
        self.near_out, self.near_in, self.far_out, self.far_in = refs
        self.send, self.recv = sems
        self.base, self.sibling, self.partner = base, sibling, partner

    def near(self, j):
        return remote(
            self.near_out.at[j],
            self.near_in.at[j],
            self.send.at[self.base, j],
            self.recv.at[self.base, j],
            self.sibling,
        )

    def far(self, j):
        return remote(
            self.far_out.at[j],
            self.far_in.at[j],
            self.send.at[self.base + 1, j],
            self.recv.at[self.base + 1, j],
            self.partner,
        )

    def give(self, j, value):
        self.near_out[j] = value
        self.near(j).start()

    def give_span(self, k, value):
        chunk = self.near_out.shape[1]
        for i in range(SPAN):
            self.give(SPAN * k + i, value[i * chunk : (i + 1) * chunk, :])

    def pass_on_span(self, k, value):
        chunk = self.near_out.shape[1]
        for i in range(SPAN):
            self.pass_on(SPAN * k + i, value[i * chunk : (i + 1) * chunk, :])

    def pass_on(self, j, value):
        self.near(j).wait_recv()
        self.far_out[j] = (value + self.near_in[j]).astype(self.far_out.dtype)
        self.far(j).start()

    def take(self, j):
        self.far(j).wait_recv()
        return self.far_out[j].astype(F32) + self.far_in[j].astype(F32)

    def close(self):
        for j in range(CHUNKS):
            self.near(j).wait_send()
            self.far(j).wait_send()

    @staticmethod
    def scratch(chunk, width, kind):
        return [
            pltpu.VMEM((CHUNKS, chunk, width), F32),
            pltpu.VMEM((CHUNKS, chunk, width), F32),
            pltpu.VMEM((CHUNKS, chunk, width), kind),
            pltpu.VMEM((CHUNKS, chunk, width), kind),
        ]


class Share:
    def __init__(self, ref, sems, base, sibling, mine, chunk):
        self.ref, self.base, self.sibling, self.mine, self.chunk = ref, base, sibling, mine, chunk
        self.send, self.recv = sems

    def piece(self, j):
        rows = self.ref.at[pl.ds(pl.multiple_of(self.mine + j * self.chunk, self.chunk), self.chunk)]
        return remote(rows, rows, self.send.at[self.base, j], self.recv.at[self.base, j], self.sibling)

    def put(self, j, value):
        self.ref[pl.ds(pl.multiple_of(self.mine + j * self.chunk, self.chunk), self.chunk), :] = value
        self.piece(j).start()

    def arrived(self, j):
        self.piece(j).wait_recv()

    def close(self):
        for j in range(CHUNKS):
            self.piece(j).wait_send()


def wide_places(count):
    me = lax.axis_index(WIDE)
    fast = lax.rem(me, 2)
    slow = me // 2
    return (me, slow, fast, count // 2)


class Carry:
    def __init__(self, loads, fetches, leaves):
        self.loads, self.fetches, self.leaves = loads, fetches, leaves
        self.left = []

    def fetch(self):
        for copy in self.fetches:
            copy.start()

    def fetched(self):
        for copy in self.fetches:
            copy.wait()

    def leave(self, *which):
        for k in which:
            self.leaves[k].start()
            self.left.append(k)

    def gone(self):
        self.leave(*[k for k in self.leaves if k not in self.left])
        for k in self.left:
            self.leaves[k].wait()

    def peers(self):
        ways = []
        for load in self.loads:
            ways += [way for way in load.ways if way not in ways]
        me, slow, fast, slows = wide_places(self.loads[0].count) if self.loads else (0, 0, 0, 0)
        found = []
        if SLOW in ways:
            found += [{WIDE: 2 * lax.rem(slow + step, slows) + fast} for step in range(1, slows)]
        if FAST in ways:
            found.append({WIDE: me + 1 - 2 * fast})
        return found

    def begin(self, *which):
        for k in which:
            self.loads[k].start()

    def hand_on(self, *which):
        for k in which:
            self.loads[k].relay()

    def end(self, *which):
        for k in which:
            self.loads[k].finish()

    def all(self):
        return range(len(self.loads))


def part_of(weights, index, window):
    shape = weights.shape[1:]
    return shape if window is None else shape[:-1] + (window[1],)


class SlowLoad:
    ways = (SLOW,)

    def __init__(self, weights, index, lead, count, window=None):
        self.index, self.lead, self.count, self.window = index, lead, count, window
        shape, slows = part_of(weights, index, window), count // 2
        self.operands, self.in_specs = [weights], [whole_vmem()]
        self.outs = [jax.ShapeDtypeStruct((slows,) + shape, BF16)]
        self.out_specs = [pl.BlockSpec(memory_space=pl.ANY)]
        self.scratch = [pltpu.VMEM(shape, BF16), pltpu.SemaphoreType.DMA] + [pltpu.SemaphoreType.DMA((slows,))] * 2

    def bind(self, given, out, scratch):
        self.shard, self.out = given[0], out[0]
        self.low, self.local, self.send, self.recv = scratch
        self.me, self.slow, self.fast, self.slows = wide_places(self.count)

    def cast(self):
        if self.window is None:
            self.low[...] = self.shard[self.index].astype(BF16)
        else:
            self.low[...] = self.shard[self.index, :, self.window[0] : self.window[0] + self.window[1]].astype(BF16)

    def target(self):
        return self.out.at[self.slow]

    def slow_copy(self, step):
        return remote(
            self.low, self.target(), self.send.at[step], self.recv.at[step],
            {WIDE: 2 * lax.rem(self.slow + step, self.slows) + self.fast},
        )

    def own_copy(self):
        return pltpu.make_async_copy(self.low, self.target(), self.local)

    def start(self):
        self.cast()
        for step in range(1, self.slows):
            self.slow_copy(step).start()
        self.own_copy().start()

    def finish(self):
        for step in range(1, self.slows):
            self.slow_copy(step).wait()
        self.own_copy().wait()


class FastLoad:
    ways = (FAST,)

    def __init__(self, blocks, lead, count):
        self.lead, self.count = lead, count
        shape, slows = blocks.shape[1:], count // 2
        self.operands, self.in_specs = [blocks], [pl.BlockSpec(memory_space=pl.ANY)]
        self.outs = [jax.ShapeDtypeStruct(shape[:lead] + (count,) + shape[lead:], BF16)]
        self.out_specs = [whole_vmem()]
        self.scratch = [pltpu.SemaphoreType.DMA((slows,))] * 3

    def value(self):
        return self.out[...].reshape((-1, self.out.shape[-1]))

    def bind(self, given, out, scratch):
        self.blocks, self.out = given[0], out[0]
        self.local, self.send, self.recv = scratch
        self.me, self.slow, self.fast, self.slows = wide_places(self.count)

    def copies(self, step):
        target = self.out.at[(slice(None),) * self.lead + (2 * step + self.fast,)]
        return (
            remote(
                self.blocks.at[step], target, self.send.at[step], self.recv.at[step],
                {WIDE: self.me + 1 - 2 * self.fast},
            ),
            pltpu.make_async_copy(self.blocks.at[step], target, self.local.at[step]),
        )

    def start(self):
        for step in range(self.slows):
            for copy in self.copies(step):
                copy.start()

    def finish(self):
        for step in range(self.slows):
            for copy in self.copies(step):
                copy.wait()


class GatherLoad(SlowLoad):
    ways = (SLOW, FAST)

    def __init__(self, weights, index, lead, count, window=None, place=HBM):
        super().__init__(weights, index, lead, count, window)
        shape, slows = part_of(weights, index, window), count // 2
        whole = shape[:lead] + (count,) + shape[lead:]
        self.outs = [jax.ShapeDtypeStruct(whole, BF16)]
        self.scratch = self.scratch + [pltpu.SemaphoreType.DMA((slows,))] * 2
        if place == KEPT:
            self.out_specs = [whole_vmem()]
        self.local_out = place == LOCAL
        if self.local_out:
            self.outs, self.out_specs = [], []
            self.scratch = self.scratch + [pltpu.VMEM(whole, BF16)]

    def bind(self, given, out, scratch):
        if self.local_out:
            out, scratch = scratch[-1:], scratch[:-1]
        super().bind(given, out, scratch[:-2])
        self.fast_send, self.fast_recv = scratch[-2:]

    def value(self, *index):
        found = self.out[index] if index else self.out[...]
        return found.reshape((-1, found.shape[-1]))

    def at(self, owner):
        return self.out.at[(slice(None),) * self.lead + (owner,)]

    def target(self):
        return self.at(self.me)

    def fast_copy(self, step):
        block = self.at(2 * lax.rem(self.slow + self.slows - step, self.slows) + self.fast)
        return remote(
            self.low if step == 0 else block, block, self.fast_send.at[step], self.fast_recv.at[step],
            {WIDE: self.me + 1 - 2 * self.fast},
        )

    def start(self):
        super().start()
        self.fast_copy(0).start()

    def relay(self):
        for step in range(1, self.slows):
            self.slow_copy(step).wait_recv()
            self.fast_copy(step).start()

    def finish(self):
        for step in range(self.slows):
            self.fast_copy(step).wait()
            if step:
                self.slow_copy(step).wait_send()
        self.own_copy().wait()


class PairLoad:
    ways = (FAST,)

    def __init__(self, full, lead, inside=False):
        self.lead, self.count, self.inside = lead, full.shape[lead], inside
        self.shape, self.slows = full.shape[:lead] + full.shape[lead + 1 :], self.count // 2
        self.operands, self.in_specs = ([], []) if inside else ([full], [whole_vmem()])
        self.outs, self.out_specs = [jax.ShapeDtypeStruct((self.slows,) + self.shape, BF16)], [whole_vmem()]
        self.scratch = [pltpu.VMEM((self.slows,) + self.shape, BF16)] + [pltpu.SemaphoreType.DMA((self.slows,))] * 2

    def bind(self, given, out, scratch):
        self.full = None if self.inside else given[0]
        self.out = out[0]
        self.came, self.send, self.recv = scratch
        self.me, self.slow, self.fast, self.slows = wide_places(self.count)

    def block(self, step, fast):
        owner = 2 * lax.rem(self.slow + step, self.slows) + fast
        return self.full.at[(slice(None),) * self.lead + (owner,)]

    def copy(self, step):
        return remote(
            self.block(step, 1 - self.fast), self.came.at[step], self.send.at[step], self.recv.at[step],
            {WIDE: self.me + 1 - 2 * self.fast},
        )

    def start(self):
        for step in list(range(1, self.slows)) + [0]:
            self.copy(step).start()

    def finish(self):
        for step in range(self.slows):
            self.copy(step).wait()
            total = self.block(step, self.fast)[...].astype(F32) + self.came[step].astype(F32)
            self.out[step] = total.astype(BF16)


class ReduceLoad(PairLoad):
    ways = (SLOW, FAST)

    def __init__(self, full, lead, inside=False):
        super().__init__(full, lead, inside)
        self.outs = [jax.ShapeDtypeStruct(self.shape, F32), jax.ShapeDtypeStruct((8, 128), F32)]
        self.out_specs = [whole_vmem()] * 2
        self.scratch = (
            self.scratch
            + [pltpu.VMEM((self.slows - 1,) + self.shape, BF16)]
            + [pltpu.SemaphoreType.DMA((self.slows,))] * 2
        )

    def bind(self, given, out, scratch):
        super().bind(given, out[:1], scratch[:3])
        self.squares = out[1]
        self.landed, self.line_send, self.line_recv = scratch[3:]

    def line_copy(self, step):
        return remote(
            self.came.at[step], self.landed.at[step - 1], self.line_send.at[step], self.line_recv.at[step],
            {WIDE: 2 * lax.rem(self.slow + step, self.slows) + self.fast},
        )

    def relay(self):
        for step in list(range(1, self.slows)) + [0]:
            self.copy(step).wait()
            total = self.block(step, self.fast)[...].astype(F32) + self.came[step].astype(F32)
            self.came[step] = total.astype(BF16)
            if step:
                self.line_copy(step).start()

    def finish(self):
        total = self.came[0].astype(F32)
        for step in range(1, self.slows):
            self.line_copy(step).wait()
            total = total + self.landed[step - 1].astype(F32)
        self.out[...] = total
        self.squares[...] = jnp.full(self.squares.shape, jnp.sum(total * total), F32)


class LineLoad:
    ways = (SLOW,)

    def __init__(self, sums, count):
        self.count = count
        slows = count // 2
        self.operands, self.in_specs = [sums], [whole_vmem()]
        self.outs = [jax.ShapeDtypeStruct(sums.shape[1:], F32), jax.ShapeDtypeStruct((8, 128), F32)]
        self.out_specs = [whole_vmem()] * 2
        self.scratch = [pltpu.VMEM(sums.shape, BF16)] + [pltpu.SemaphoreType.DMA((slows,))] * 2

    def bind(self, given, out, scratch):
        self.sums, (self.out, self.squares) = given[0], out
        self.came, self.send, self.recv = scratch
        self.me, self.slow, self.fast, self.slows = wide_places(self.count)

    def copy(self, step):
        return remote(
            self.sums.at[step], self.came.at[step], self.send.at[step], self.recv.at[step],
            {WIDE: 2 * lax.rem(self.slow + step, self.slows) + self.fast},
        )

    def start(self):
        for step in range(1, self.slows):
            self.copy(step).start()

    def finish(self):
        total = self.sums[0].astype(F32)
        for step in range(1, self.slows):
            self.copy(step).wait()
            total = total + self.came[step].astype(F32)
        self.out[...] = total
        self.squares[...] = jnp.full(self.squares.shape, jnp.sum(total * total), F32)


def run(body, name, operands, outs, scratch, collective_id=None, loads=(), away=(), lazy=(), early=()):
    any_place = pl.BlockSpec(memory_space=pl.ANY)
    given, taken = list(operands), []
    in_specs = [any_place if k in away or k in lazy else whole_vmem() for k in range(len(operands))]
    for load in loads:
        places = []
        for operand, spec in zip(load.operands, load.in_specs):
            known = [k for k, other in enumerate(given) if other is operand]
            if not known:
                known = [len(given)]
                given.append(operand)
                in_specs.append(spec)
            places.append(known[0])
        taken.append(places)
    moved = [operands[k] for k in lazy] + [outs[k] for k in early]
    counts = [len(given), len(outs)] + [len(load.outs) for load in loads]
    counts += [len(scratch)] + [len(load.scratch) for load in loads] + [len(moved), len(moved)]
    parts = 1 + len(loads)

    def kernel(*refs):
        groups, place = [], 0
        for count in counts:
            groups.append(refs[place : place + count])
            place += count
        for k, load in enumerate(loads):
            load.bind([groups[0][p] for p in taken[k]], groups[2 + k], groups[2 + parts + k])
        mine, results = list(groups[0][: len(operands)]), list(groups[1])
        fetches, leaves = [], {}
        for k, buffer, sem in zip(lazy, groups[-2], groups[-1]):
            fetches.append(pltpu.make_async_copy(mine[k], buffer, sem))
            mine[k] = buffer
        for k, buffer, sem in zip(early, groups[-2][len(lazy) :], groups[-1][len(lazy) :]):
            leaves[k] = pltpu.make_async_copy(buffer, results[k], sem)
            results[k] = buffer
        body(*mine, *results, *groups[1 + parts], carry=Carry(list(loads), fetches, leaves))

    results = pl.pallas_call(
        kernel,
        out_shape=tuple(outs) + tuple(out for load in loads for out in load.outs),
        in_specs=in_specs,
        out_specs=tuple(any_place if k in early else whole_vmem() for k in range(len(outs)))
        + tuple(spec for load in loads for spec in load.out_specs),
        scratch_shapes=list(scratch)
        + [s for load in loads for s in load.scratch]
        + [pltpu.VMEM(value.shape, value.dtype) for value in moved]
        + [pltpu.SemaphoreType.DMA] * len(moved),
        compiler_params=pltpu.CompilerParams(
            collective_id=collective_id,
            has_side_effects=collective_id is not None,
            vmem_limit_bytes=VMEM_LIMIT,
        ),
        name=name,
    )(*given)
    return results[: len(outs)], results[len(outs) :]


def sems(kinds):
    return [pltpu.SemaphoreType.DMA((kinds, CHUNKS)), pltpu.SemaphoreType.DMA((kinds, CHUNKS))]


def norm_of(value, gain):
    scale = lax.rsqrt(jnp.mean(value * value, axis=-1, keepdims=True) + NORM_EPS)
    return value * scale * gain


def norm_back(grad, value, gain):
    scale = lax.rsqrt(jnp.mean(value * value, axis=-1, keepdims=True) + NORM_EPS)
    unit = value * scale
    scaled = grad * gain
    back = scale * (scaled - unit * jnp.mean(scaled * unit, axis=-1, keepdims=True))
    return (back, jnp.sum(grad * unit, axis=0, keepdims=True))


GELU_A = math.sqrt(2.0 / math.pi)
GELU_B = 0.044715


def gelu_of(x):
    return 0.5 * x * (1.0 + jnp.tanh(GELU_A * (x + GELU_B * (x * x * x))))


def gelu_slope(x):
    square = x * x
    t = jnp.tanh(GELU_A * (x + GELU_B * (x * square)))
    return 0.5 * (1.0 + t) + 0.5 * x * (1.0 - t * t) * (GELU_A * (1.0 + 3.0 * GELU_B * square))


def rows_at(start, j, chunk):
    return pl.ds(pl.multiple_of(start + j * chunk, chunk), chunk)


LANES = 128
SUB = 64


def spread(row):
    return jnp.transpose(jnp.broadcast_to(row, (LANES, LANES)))


def feature_places(owner, width, share):
    lane = lax.broadcasted_iota(jnp.int32, (LANES, width), 0)
    feature = lax.broadcasted_iota(jnp.int32, (LANES, width), 1)
    return ((feature == lane + owner * share) & (lane < share)).astype(F32).astype(BF16)


def token_parts(ids, first):
    here = ids - first
    high = lax.shift_right_arithmetic(here, 7)
    place = lax.broadcasted_iota(jnp.int32, (LANES, ids.shape[1]), 0)
    return high, jnp.where(place == here - high * LANES, 1.0, 0.0).astype(BF16)


def embed_part(
    ids, counted, gains, steps, rates, table,
    resid, normed, gain_all, count_all, ids_all,
    low, extra, small, near_out, near_in, own, far_out, far_in, wide_out, wide_in, part_out, part_in,
    id_send, id_recv, small_send, small_recv, near_send, near_recv, far_send, far_recv, wide_send, wide_recv,
    part_send, part_recv, send, recv, carry,
):
    seq_len, width = normed.shape
    chunk = seq_len // 2 // CHUNKS
    quarter = seq_len // 4
    share, vocab = table.shape[1:]
    owners = ids_all.shape[0]
    sibling, partner, mine, other = group_places(seq_len)
    place = lax.axis_index(NARROW)
    side = lax.div(place, 2)
    me = lax.axis_index(WIDE)
    first = place * vocab
    around = [lax.rem(me + step, owners) for step in range(owners)]

    def id_copy(step):
        return remote(ids_all.at[me], ids_all.at[me], id_send.at[step], id_recv.at[step], {WIDE: around[step]})

    def small_copy(step):
        return remote(small.at[me], small.at[me], small_send.at[step], small_recv.at[step], {WIDE: around[step]})

    def near_copy(step):
        return remote(near_out.at[step], near_in.at[step], near_send.at[step], near_recv.at[step], sibling)

    def far_copy(step):
        return remote(far_out.at[step], far_in.at[step], far_send.at[step], far_recv.at[step], partner)

    def wide_copy(step):
        return remote(wide_out.at[step], wide_in.at[me], wide_send.at[step], wide_recv.at[step], {WIDE: around[step]})

    def part_copy(piece):
        rows = pl.ds(piece * LANES, LANES)
        return remote(part_out.at[rows], part_in.at[rows], part_send.at[piece], part_recv.at[piece], partner)

    ids_all[me] = ids[...]
    small[me] = jnp.zeros(small.shape[1:], F32)
    small[me, : gains.shape[0], : gains.shape[1]] = gains[...].astype(BF16).astype(F32)
    count = jnp.sum(counted[...].astype(F32), keepdims=True)
    small[me, COUNT_ROW : COUNT_ROW + 1, :] = jnp.broadcast_to(count, (1, small.shape[2]))
    greet([{WIDE: device} for device in around[1:]] + [sibling, partner])
    for step in range(1, owners):
        id_copy(step).start()
    for step in range(1, owners):
        small_copy(step).start()
    carry.begin(0, 1)
    parts = vocab // LANES
    for part in range(parts):
        low[part * share : (part + 1) * share, :] = table[0, :, part * LANES : (part + 1) * LANES].astype(BF16)
    core = lax.rem(place, 2)

    def look_up(step):
        row = lax.rem(me + step, owners)

        def find(which):
            high, picks = token_parts(ids_all[row, pl.ds(which, 1), :], first)
            found = dot_nn(low[...], picks)
            total = jnp.zeros((share, quarter), F32)
            for part in range(parts):
                total = total + jnp.where(high == part, found[part * share : (part + 1) * share, :], 0.0)
            return total.astype(BF16)

        for k in range(2):
            near_out[step, k] = find(2 * (1 - core) + k)
        near_copy(step).start()
        for k in range(2):
            own[step, k] = find(2 * core + k)

    def halve(step):
        near_copy(step).wait_recv()
        own[step] = own[step] + near_in[step]
        far_out[step] = own[step, 1 - side]
        far_copy(step).start()

    def deliver(step):
        far_copy(step).wait_recv()
        total = own[step, side] + far_in[step]
        if step % owners == 0:
            wide_in[me] = total
        else:
            wide_out[step] = total
            wide_copy(step).start()

    order = list(range(1, owners)) + [0]
    for turn in range(owners + 2):
        if turn < owners:
            if order[turn]:
                id_copy(owners - order[turn]).wait_recv()
            look_up(order[turn])
        if 1 <= turn < owners + 1:
            halve(order[turn - 1])
        if turn >= 2:
            deliver(order[turn - 2])
    carry.begin(2, 3)
    carry.hand_on(0, 1)
    for step in range(1, owners):
        small_copy(step).wait_recv()
    total = None
    for owner in range(owners):
        part = dot_nn(small[owner].astype(BF16), feature_places(owner, width, share))
        total = part if total is None else total + part
    gain_all[...] = total
    count_all[...] = jnp.sum(small[...], axis=0)
    half_width = width // 2
    for k in range(seq_len // 2 // LANES):
        when = spread(steps[pl.ds(mine // LANES + k, 1), :].astype(F32))
        for t in range(half_width // LANES):
            columns = slice(t * LANES, (t + 1) * LANES)
            angles = when * rates[:, columns]
            rows = slice(k * LANES, (k + 1) * LANES)
            extra[rows, t * LANES : (t + 1) * LANES] = jnp.sin(angles)
            extra[rows, half_width + t * LANES : half_width + (t + 1) * LANES] = jnp.cos(angles)
    for step in range(1, owners):
        wide_copy(step).wait_recv()
    found = jnp.transpose(wide_in[...].reshape(width, quarter))
    pieces = quarter // LANES
    at_side = pl.multiple_of(side * quarter, quarter)
    at_other = pl.multiple_of((1 - side) * quarter, quarter)
    for piece in range(pieces):
        rows = pl.ds(piece * LANES, LANES)
        part_out[rows, :] = found[piece * LANES : (piece + 1) * LANES, :]
        part_copy(piece).start()

    def finish(start, source, piece):
        rows = rows_at(start, piece, LANES)
        x = math.sqrt(width) * source[pl.ds(piece * LANES, LANES), :].astype(F32) + extra[rows, :]
        resid[rows, :] = x
        here = rows_at(mine + start, piece, LANES)
        normed[here, :] = norm_of(x, gain_all[0:1, :]).astype(BF16)
        give_rows(here, piece if source is part_out else pieces + piece).start()

    def give_rows(here, k):
        return remote(normed.at[here], normed.at[here], send.at[0, k], recv.at[0, k], sibling)

    for piece in range(pieces):
        finish(at_side, part_out, piece)
    for piece in range(pieces):
        part_copy(piece).wait_recv()
        finish(at_other, part_in, piece)
    carry.hand_on(2)
    for k in range(2 * pieces):
        give_rows(rows_at(mine, k % pieces, LANES), k).wait()
    for step in range(owners):
        near_copy(step).wait_send()
        far_copy(step).wait_send()
        if step:
            id_copy(step).wait_send()
            small_copy(step).wait_send()
            wide_copy(step).wait_send()
    for piece in range(pieces):
        part_copy(piece).wait_send()


QUERY_BLOCK = 256


def forward_part(
    layer, weights, points, normed, key_seg, query_seg, resid, gains,
    projected, mixed, middle, normed_two, log_sums, result, normed_next,
    bias, values_t, near_out, near_in, far_out, far_in, near_out2, near_in2, far_out2, far_in2, send, recv,
):
    w_query, w_out, w_in, w_red = weights
    at_half, at_feed, at_sent, at_last = points
    seq_len, width = normed.shape
    chunk = seq_len // 2 // CHUNKS
    block = bias.shape[1]
    heads = mixed.shape[1] // HD
    sibling, partner, mine, other = group_places(seq_len)
    pair = (send, recv)
    first = Exchange((near_out, near_in, far_out, far_in), pair, 0, sibling, partner)
    second = Exchange((near_out2, near_in2, far_out2, far_in2), pair, 2, sibling, partner)
    share = Share(normed_two, pair, 4, sibling, mine, chunk)
    share_next = Share(normed_next, pair, 5, sibling, mine, chunk)

    def ask(i, _):
        rows = rows_at(0, i, block)
        for which in range(3):
            projected[which, rows, :] = dot_nn(normed[rows, :], w_query(which)).astype(BF16)
        return 0

    lax.fori_loop(0, seq_len // block, ask, 0)
    values_t[...] = jnp.transpose(projected[2])

    def attend_rows(start):
        rows = pl.ds(pl.multiple_of(start, block), block)
        bias[...] = jnp.where(key_seg[...] == query_seg[:, rows], 0.0, -1e30)
        asked = projected[0, rows, :] * HD ** (-0.5)
        parts = []
        for head in range(heads):
            scores = dot_nt(projected[1], head_lanes(asked, head, HD)) + bias[...]
            top = jnp.max(scores, axis=0, keepdims=True)
            powers = jnp.exp(scores - top)
            total = jnp.sum(powers, axis=0, keepdims=True)
            log_sums[head : head + 1, rows] = top + jnp.log(total)
            probs = (powers * (1.0 / total)).astype(BF16)
            parts.append(dot_nn(values_t[head * HD : (head + 1) * HD, :], probs))
        mixed[rows, :] = jnp.transpose(jnp.concatenate(parts, axis=0)).astype(BF16)

    def project(start, k):
        return dot_nt(mixed[rows_at(start, k, SPAN * chunk), :], w_out())

    def feed(rows):
        pre = dot_nn(normed_two[rows, :], w_in())
        return dot_nt(gelu_of(pre).astype(BF16), w_red())

    for part in range(CHUNKS // SPAN):

        def both(i, _):
            attend_rows(jnp.where(i == 0, other, mine) + part * block)
            return 0

        lax.fori_loop(0, 2, both, 0)
        first.give_span(part, project(other, part))
        if part == 0:
            at_half()
        first.pass_on_span(part, project(mine, part))
    at_feed()
    for k in range(CHUNKS // SPAN):
        for j in range(SPAN * k, SPAN * (k + 1)):
            rows = rows_at(0, j, chunk)
            mid = resid[rows, :] + first.take(j)
            middle[rows, :] = mid
            share.put(j, norm_of(mid, gains[2 * layer + 1 : 2 * layer + 2, :]).astype(BF16))
        kept = feed(rows_at(mine, k, SPAN * chunk))
        for j in range(SPAN * k, SPAN * (k + 1)):
            share.arrived(j)
        second.give_span(k, feed(rows_at(other, k, SPAN * chunk)))
        second.pass_on_span(k, kept)
    at_sent()
    for j in range(CHUNKS):
        rows = rows_at(0, j, chunk)
        x = middle[rows, :] + second.take(j)
        result[rows, :] = x
        share_next.put(j, norm_of(x, gains[2 * layer + 2 : 2 * layer + 3, :]).astype(BF16))
        if j == CHUNKS - 2:
            at_last()
    for j in range(CHUNKS):
        share_next.arrived(j)
    for part in (first, second, share, share_next):
        part.close()


def layer_outs(seq_len, width, heads_width):
    return [
        jax.ShapeDtypeStruct((3, seq_len, heads_width), BF16),
        jax.ShapeDtypeStruct((seq_len, heads_width), BF16),
        jax.ShapeDtypeStruct((seq_len // 2, width), F32),
        jax.ShapeDtypeStruct((seq_len, width), BF16),
        jax.ShapeDtypeStruct((8, seq_len), F32),
    ]


def layer_scratch(seq_len, width, heads_width):
    half, chunk = seq_len // 2, seq_len // 2 // CHUNKS
    block = SPAN * chunk
    return (
        [pltpu.VMEM((seq_len, block), F32), pltpu.VMEM((heads_width, seq_len), BF16)]
        + Exchange.scratch(chunk, width, FORWARD_KIND)
        + Exchange.scratch(chunk, width, FORWARD_KIND)
        + sems(6)
    )


LAYER_SCRATCH = 12
COUNT_ROW = 5


def front_kernel(
    ids, counted, gains, steps, rates, table, key_seg, query_seg,
    resid, normed, gain_all, count_all, ids_all, projected, mixed, middle, normed_two, log_sums, result, normed_next,
    *scratch, carry,
):
    embed_part(
        ids, counted, gains, steps, rates, table, resid, normed, gain_all, count_all, ids_all,
        *scratch[:-LAYER_SCRATCH], carry,
    )
    carry.end(0, 1)
    later = list(carry.all())[4:]

    def at_half():
        carry.hand_on(3)
        carry.begin(*later[:2])

    def at_feed():
        carry.end(2, 3)
        carry.begin(*later[2:])
        carry.leave(0, 1, 5, 6)

    def at_sent():
        carry.hand_on(*later[:2])
        carry.leave(7, 8)

    forward_part(
        0,
        [carry.loads[0].value] + [load.value for load in carry.loads[1:4]],
        (at_half, at_feed, at_sent, lambda: carry.hand_on(*later[2:3])),
        normed, key_seg, query_seg, resid, gain_all,
        projected, mixed, middle, normed_two, log_sums, result, normed_next, *scratch[-LAYER_SCRATCH:],
    )
    carry.end(*later)
    carry.gone()


def front(ids, counted, gains, steps, rates, tables, key_seg, query_seg, owners, heads_width, collective_id, loads):
    seq_len = ids.size
    share, vocab = tables.shape[1:]
    half, width = seq_len // 2, owners * share
    dma = pltpu.SemaphoreType.DMA
    return run(
        front_kernel,
        "front",
        [ids, counted, gains, steps, rates, tables, key_seg, query_seg],
        [
            jax.ShapeDtypeStruct((half, width), F32),
            jax.ShapeDtypeStruct((seq_len, width), BF16),
            jax.ShapeDtypeStruct((8, width), F32),
            jax.ShapeDtypeStruct((8, LANES), F32),
            jax.ShapeDtypeStruct((owners,) + ids.shape, jnp.int32),
        ]
        + layer_outs(seq_len, width, heads_width)
        + [jax.ShapeDtypeStruct((half, width), F32), jax.ShapeDtypeStruct((seq_len, width), BF16)],
        [
            pltpu.VMEM((vocab // LANES * share, LANES), BF16),
            pltpu.VMEM((half, width), F32),
            pltpu.VMEM((owners, 8, LANES), F32),
        ]
        + [pltpu.VMEM((owners, 2, share, half // 2), BF16)] * 3
        + [pltpu.VMEM((owners, share, half // 2), BF16)] * 4
        + [
            pltpu.VMEM((half // 2, width), BF16),
            pltpu.VMEM((half // 2, width), BF16),
        ]
        + [dma((owners,))] * 10
        + [dma((half // 2 // LANES,))] * 2
        + [dma((1, half // LANES))] * 2
        + layer_scratch(seq_len, width, heads_width),
        collective_id,
        loads,
        early=(0, 1, 5, 6, 7, 8),
    )


TILE = 256


def weight_grad(left_t, right, out):
    columns = right.shape[1]
    tile = TILE if columns % TILE == 0 else columns

    def put(where):
        value = dot_nn(left_t[...], right[:, where]).astype(out.dtype)
        if len(out.shape) == 3:
            out[:, :, where] = value.reshape(out.shape[:2] + (tile,))
        else:
            out[:, where] = value

    def step(i, _):
        put(pl.ds(pl.multiple_of(i * tile, tile), tile))
        return 0

    if tile == columns:
        put(slice(None))
    else:
        lax.fori_loop(0, columns // tile, step, 0)


def head_lanes(value, head, size):
    lanes = lax.broadcasted_iota(jnp.int32, value.shape, 1)
    inside = (lanes >= head * size) & (lanes < (head + 1) * size)
    return jnp.where(inside, value, jnp.zeros_like(value))


def backward_kernel(
    layer, scale, points, grad, branch, w_red, w_in, w_out, normed_two, middle, gains, mixed,
    projected, log_sums, key_seg, query_seg, w_query, resid, normed,
    grad_out, branch_out, d_out, d_query, gain_two, gain_one,
    d_red, d_in, grad_middle, grad_attn, grad_mixed, grad_projected, grad_before, after, turned,
    bias, keys_t, grad_keys, grad_values,
    near_out, near_in, far_out, far_in, far_out2, far_in2, send, recv, loaded, carry,
):
    at_start, at_made, at_summed, at_attended, at_sent = points
    seq_len, width = normed_two.shape
    chunk = seq_len // 2 // CHUNKS
    sibling, partner, mine, other = group_places(seq_len)
    carry.fetch()
    greet([sibling, partner] + carry.peers())
    at_start(carry, d_red, d_in)
    pair = (send, recv)
    trade = Exchange((near_out, near_in, far_out, far_in), pair, 0, sibling, partner)
    share = Share(grad_attn, pair, 2, sibling, mine, chunk)

    def ffn_partial(start, k):
        rows = rows_at(start, k, SPAN * chunk)
        pre = dot_nn(normed_two[rows, :], w_in[...])
        after[rows, :] = gelu_of(pre).astype(BF16)
        low = (dot_nn(branch[rows, :], w_red[...]) * gelu_slope(pre)).astype(BF16)
        grad_before[rows, :] = low
        return dot_nt(low, w_in[...])

    for k in range(CHUNKS // SPAN):
        trade.give_span(k, ffn_partial(other, k))
        trade.pass_on_span(k, ffn_partial(mine, k))
    turned[...] = jnp.transpose(branch[...])
    weight_grad(turned, after, d_red)
    turned[...] = jnp.transpose(normed_two[...])
    weight_grad(turned, grad_before, d_in)
    at_made(carry)
    fetch = pltpu.make_async_copy(normed, after, loaded)
    fetch.start()
    carry.fetched()
    total = jnp.zeros((1, width), F32)
    for j in range(CHUNKS):
        rows = rows_at(0, j, chunk)
        back, part = norm_back(trade.take(j), middle[rows, :], gains[2 * layer + 1 : 2 * layer + 2, :])
        total = total + part
        back = back + grad[rows, :]
        grad_middle[rows, :] = back
        share.put(j, back.astype(BF16))
        here = rows_at(mine, j, chunk)
        grad_mixed[here, :] = dot_nn(grad_attn[here, :], w_out[...]).astype(BF16)
    gain_two[...] = total
    for j in range(CHUNKS):
        share.arrived(j)
        here = rows_at(other, j, chunk)
        grad_mixed[here, :] = dot_nn(grad_attn[here, :], w_out[...]).astype(BF16)
    trade.close()
    share.close()
    at_summed(carry)

    block = bias.shape[1]
    heads = grad_mixed.shape[1] // HD
    keys_t[...] = jnp.transpose(projected[1])
    grad_keys[...] = jnp.zeros(grad_keys.shape, F32)
    grad_values[...] = jnp.zeros(grad_values.shape, F32)

    def queries(i, _):
        rows = rows_at(0, i, block)
        bias[...] = jnp.where(key_seg[...] == query_seg[:, rows], 0.0, -1e30)
        asked = projected[0, rows, :] * HD ** (-0.5)
        given = grad_mixed[rows, :]
        parts = []
        for head in range(heads):
            query = head_lanes(asked, head, HD)
            wanted = head_lanes(given, head, HD)
            scores = dot_nt(projected[1], query) + bias[...]
            probs = jnp.exp(scores - log_sums[head : head + 1, rows])
            grad_probs = dot_nt(projected[2], wanted)
            centre = jnp.sum(probs * grad_probs, axis=0, keepdims=True)
            grad_scores = (probs * (grad_probs - centre)).astype(BF16)
            parts.append(dot_nn(keys_t[head * HD : (head + 1) * HD, :], grad_scores))
            grad_keys[...] += dot_nn(grad_scores, query)
            grad_values[...] += dot_nn(probs.astype(BF16), wanted)
        grad_projected[0, rows, :] = (jnp.transpose(jnp.concatenate(parts, axis=0)) * HD ** (-0.5)).astype(BF16)
        return 0

    lax.fori_loop(0, seq_len // block, queries, 0)
    grad_projected[1] = grad_keys[...].astype(BF16)
    grad_projected[2] = grad_values[...].astype(BF16)
    at_attended(carry)

    trade = Exchange((near_out, near_in, far_out2, far_in2), pair, 3, sibling, partner)
    share = Share(branch_out, pair, 5, sibling, mine, chunk)

    def query_partial(start, k):
        rows = rows_at(start, k, SPAN * chunk)
        found = None
        for which in range(3):
            part = dot_nt(grad_projected[which, rows, :], w_query[which])
            found = part if found is None else found + part
        return found

    for k in range(CHUNKS // SPAN):
        trade.give_span(k, query_partial(other, k))
        trade.pass_on_span(k, query_partial(mine, k))
    turned[...] = jnp.transpose(grad_attn[...])
    weight_grad(turned, mixed, d_out)
    fetch.wait()
    turned[...] = jnp.transpose(after[...])
    for which in range(3):
        weight_grad(turned, grad_projected.at[which], d_query.at[which])
    at_sent(carry, d_out, d_query)
    total = jnp.zeros((1, width), F32)
    for j in range(CHUNKS):
        rows = rows_at(0, j, chunk)
        back, part = norm_back(trade.take(j), resid[rows, :], gains[2 * layer : 2 * layer + 1, :])
        total = total + part
        back = back + grad_middle[rows, :]
        grad_out[rows, :] = back
        share.put(j, (back if scale is None else scale * back).astype(BF16))
    gain_one[...] = total
    for j in range(CHUNKS):
        share.arrived(j)
    trade.close()
    share.close()
    carry.end(*carry.all())


def backward_block(
    layer, scale, points, grad, branch, w_red, w_in, w_out, normed_two, middle, gains, mixed,
    projected, log_sums, key_seg, query_seg, w_query, resid, normed, owners, collective_id, loads,
):
    seq_len, width = normed_two.shape
    hidden, heads_width = w_in.shape[1], w_query.shape[2]
    half, chunk = seq_len // 2, seq_len // 2 // CHUNKS
    block = min(QUERY_BLOCK, seq_len)
    far = pltpu.VMEM((CHUNKS, chunk, width), BACKWARD_KIND)
    return run(
        functools.partial(backward_kernel, layer, scale, points),
        "backward_block",
        [grad, branch, w_red, w_in, w_out, normed_two, middle, gains, mixed]
        + [projected, log_sums, key_seg, query_seg, w_query, resid, normed],
        [
            jax.ShapeDtypeStruct((half, width), F32),
            jax.ShapeDtypeStruct((seq_len, width), BF16),
            jax.ShapeDtypeStruct((owners, width // owners, heads_width), BF16),
            jax.ShapeDtypeStruct((3, owners, width // owners, heads_width), BF16),
            jax.ShapeDtypeStruct((1, width), F32),
            jax.ShapeDtypeStruct((1, width), F32),
        ],
        [pltpu.VMEM((owners, width // owners, hidden), BF16)] * 2
        + [
            pltpu.VMEM((half, width), F32),
            pltpu.VMEM((seq_len, width), BF16),
            pltpu.VMEM((seq_len, heads_width), BF16),
            pltpu.VMEM((3, seq_len, heads_width), BF16),
            pltpu.VMEM((seq_len, hidden), BF16),
            pltpu.VMEM((seq_len, width), BF16),
            pltpu.VMEM((width, seq_len), BF16),
            pltpu.VMEM((seq_len, block), F32),
            pltpu.VMEM((heads_width, seq_len), BF16),
            pltpu.VMEM((seq_len, heads_width), F32),
            pltpu.VMEM((seq_len, heads_width), F32),
        ]
        + Exchange.scratch(chunk, width, BACKWARD_KIND)
        + [far, far]
        + sems(6)
        + [pltpu.SemaphoreType.DMA],
        collective_id,
        loads,
        away=(15,),
        lazy=(0, 4, 6, 8, 9, 11, 13, 14),
    )


def to_rows(columns):
    lanes = lax.broadcasted_iota(jnp.int32, (LANES, LANES), 1)
    total = jnp.zeros((LANES, LANES), F32)
    for k, column in enumerate(columns):
        total = jnp.where(lanes == k, column, total)
    return jnp.transpose(total)[:8, :]


def loss_part(
    row, normed, info, value, gain, table_loads, grad_out, branch, d_gain, losses, d_tables,
    logits, grads, places, turned, stat_out, stat_in, sum_out, sum_in,
    stat_send, stat_recv, sum_send, sum_recv, near_out, near_in, far_out, far_in, send, recv, made,
):
    seq_len, width = normed.shape
    chunk = seq_len // 2 // CHUNKS
    piece_width = table_loads[0].out.shape[-1]
    vocab = piece_width * len(table_loads)
    tiles = vocab // LANES
    blocks = seq_len // LANES
    me = lax.axis_index(NARROW)
    sibling, partner, mine, other = group_places(seq_len)
    peers = [{NARROW: lax.rem(me + k, 4)} for k in range(1, 4)]
    sems = (send, recv)
    trade = Exchange((near_out, near_in, far_out, far_in), sems, 0, sibling, partner)
    share = Share(branch, sems, 2, sibling, mine, chunk)
    first = (me * vocab).astype(F32)
    whole = 4.0 * vocab
    lanes = lax.broadcasted_iota(jnp.int32, (LANES, LANES), 1).astype(F32)

    def stat_copy(b, k):
        return remote(stat_out.at[b], stat_in.at[k, b], stat_send.at[k, b], stat_recv.at[k, b], peers[k])

    def sum_copy(b, k):
        return remote(sum_out.at[b], sum_in.at[k, b], sum_send.at[k, b], sum_recv.at[k, b], peers[k])

    def tile_at(t):
        return pl.ds(pl.multiple_of(t * LANES, LANES), LANES)

    def ask(b, _):
        rows = rows_at(0, b, LANES)
        here = info[:, rows]
        at_noised = spread(here[0:1] - first)
        at_clean = spread(here[1:2] - first)
        places[b, 0] = at_noised
        places[b, 1] = at_clean

        tops, sums = [], [[], [], []]
        for k in range(LANES // SUB):
            part = pl.ds(pl.multiple_of(b * LANES + k * SUB, SUB), SUB)
            subset = slice(k * SUB, (k + 1) * SUB)

            def top_step(t, top):
                return jnp.maximum(top, logits[part, tile_at(t)])

            top = lax.fori_loop(1, tiles, top_step, logits[part, tile_at(0)], unroll=5)
            top = jnp.max(top, axis=1, keepdims=True)
            top_wide = jnp.broadcast_to(top, (SUB, LANES))
            noised_at, clean_at = at_noised[subset], at_clean[subset]

            def sum_step(t, totals):
                powers, noised, clean = totals
                piece = logits[part, tile_at(t)]
                column = lanes[subset] + (t * LANES).astype(F32)
                return (
                    powers + jnp.exp(piece - top_wide),
                    noised + jnp.where(column == noised_at, piece, 0.0),
                    clean + jnp.where(column == clean_at, piece, 0.0),
                )

            zero = jnp.zeros((SUB, LANES), F32)
            totals = lax.fori_loop(0, tiles, sum_step, (zero, zero, zero), unroll=4)
            tops.append(top)
            for found, total in zip(sums, totals):
                found.append(jnp.sum(total, axis=1, keepdims=True))
        stat_out[b] = to_rows([jnp.concatenate(found, axis=0) for found in [tops] + sums])
        for k in range(3):
            stat_copy(b, k).start()
        return 0

    for k, table in enumerate(table_loads):
        if k == len(table_loads) - 1:
            table.finish()

        def product(i, _):
            rows = rows_at(0, i, TILE)
            logits[rows, k * piece_width : (k + 1) * piece_width] = dot_nn(normed[rows, :], table.value())
            return 0

        lax.fori_loop(0, seq_len // TILE, product, 0)
    lax.fori_loop(0, blocks, ask, 0)

    def scalars(b):
        here = info[:, rows_at(0, b, LANES)]
        step = jnp.maximum(here[2:3], 2.0)
        left = STEPS - step + 1.0
        beta = 1.0 / left
        keep = left / STEPS
        rest = (step - 1.0) / (STEPS * whole)
        own = stat_out[b]
        others = [stat_in[k, b] for k in range(3)]
        top = own[0:1]
        for stat in others:
            top = jnp.maximum(top, stat[0:1])
        total = own[1:2] * jnp.exp(own[0:1] - top)
        noised, clean = own[2:3], own[3:4]
        for stat in others:
            total = total + stat[1:2] * jnp.exp(stat[0:1] - top)
            noised, clean = noised + stat[2:3], clean + stat[3:4]
        return here, beta, keep, rest, top + jnp.log(total), noised, clean

    def measure(b, _):
        rows = rows_at(0, b, LANES)
        for k in range(3):
            stat_copy(b, k).wait_recv()
        _, _, keep, rest, log_total, _, _ = scalars(b)
        log_wide = spread(log_total)
        ratio = spread(keep / rest)

        sums = [[], []]
        for k in range(LANES // SUB):
            part = pl.ds(pl.multiple_of(b * LANES + k * SUB, SUB), SUB)
            log_part, ratio_part = log_wide[k * SUB : (k + 1) * SUB], ratio[k * SUB : (k + 1) * SUB]

            def step(t, totals):
                logs, shares = totals
                probs = jnp.exp(logits[part, tile_at(t)] - log_part)
                logits[part, tile_at(t)] = probs
                grown = 1.0 + probs * ratio_part
                return (logs + jnp.log(grown), shares + probs / grown)

            zero = jnp.zeros((SUB, LANES), F32)
            totals = lax.fori_loop(0, tiles, step, (zero, zero), unroll=4)
            for found, total in zip(sums, totals):
                found.append(jnp.sum(total, axis=1, keepdims=True))
        sum_out[b] = to_rows([jnp.concatenate(found, axis=0) for found in sums])
        for k in range(3):
            sum_copy(b, k).start()
        return 0

    lax.fori_loop(0, blocks, measure, 0)

    def pull(b):
        rows = rows_at(0, b, LANES)
        for k in range(3):
            sum_copy(b, k).wait_recv()
        here, beta, keep, rest, log_total, noised, clean = scalars(b)
        sums = sum_out[b] + sum_in[0, b] + sum_in[1, b] + sum_in[2, b]
        log_sum, share_sum = sums[0:1], sums[1:2] / rest
        same = here[0:1] == here[1:2]
        first_step = here[2:3] == 1.0
        base_a, more_a = beta / whole, 1.0 - beta
        base_w = base_a * rest
        joint = whole * base_w + more_a * rest + base_a * keep + jnp.where(same, more_a * keep, 0.0)
        ratio = keep / rest
        prob_n, prob_c = jnp.exp(noised - log_total), jnp.exp(clean - log_total)
        grown_n, grown_c = 1.0 + prob_n * ratio, 1.0 + prob_c * ratio
        marginal_n, marginal_c = rest * grown_n, rest * grown_c
        log_n, log_c = jnp.log(grown_n), jnp.log(grown_c)
        weight_n = jnp.where(same, 0.0, more_a * rest)
        weight_c = jnp.where(same, more_a * rest + base_a * keep + more_a * keep, base_a * keep)
        lift = jnp.log((keep + rest) / rest)
        cross = -base_w * log_sum - weight_n * log_n - weight_c * log_c + (base_w + weight_c) * lift
        model = base_a * (keep + whole * rest) + more_a * marginal_n
        divergence = cross / joint - jnp.log(joint) + jnp.log(model)
        loss = jnp.where(first_step, log_total - clean, divergence)
        losses[:, rows] = here[4:5] * loss
        weighted = base_w * share_sum + weight_n * prob_n / marginal_n + weight_c * prob_c / marginal_c
        aligned = base_a + more_a * prob_n
        centre = keep * (aligned / model - weighted / joint)
        scale = here[3:4]
        zero = jnp.zeros_like(scale)
        even = scale * jnp.where(first_step, 1.0, keep * base_a / model - centre)
        bent = scale * jnp.where(first_step, zero, -keep * base_w / joint / rest)
        at_n = prob_n * keep * (more_a / model - weight_n / joint / marginal_n)
        at_c = -prob_c * keep * (weight_c / joint / marginal_c)
        extra_n = spread(scale * jnp.where(first_step, zero, at_n))
        extra_c = spread(scale * jnp.where(first_step, -1.0, at_c))
        even, bent, ratio = spread(even), spread(bent), spread(ratio)
        at_noised, at_clean = places[b, 0], places[b, 1]

        for k in range(LANES // SUB):
            part = pl.ds(pl.multiple_of(b * LANES + k * SUB, SUB), SUB)
            subset = slice(k * SUB, (k + 1) * SUB)
            even_at, bent_at, ratio_at = even[subset], bent[subset], ratio[subset]
            n_at, c_at, noised_at, clean_at = extra_n[subset], extra_c[subset], at_noised[subset], at_clean[subset]

            def step(t, _):
                probs = logits[part, tile_at(t)]
                column = lanes[subset] + (t * LANES).astype(F32)
                grad = probs * (even_at + bent_at / (1.0 + probs * ratio_at))
                grad = grad + jnp.where(column == noised_at, n_at, 0.0)
                grad = grad + jnp.where(column == clean_at, c_at, 0.0)
                grads[part, tile_at(t)] = grad.astype(BF16)
                return 0

            lax.fori_loop(0, tiles, step, 0, unroll=4)

    def partial(start, k):
        span = SPAN * chunk
        base = start // LANES + k * (span // LANES)
        for b in range(span // LANES):
            pull(base + b)
        total = None
        for k_table, table in enumerate(table_loads):
            part = dot_nt(
                grads[rows_at(start, k, span), k_table * piece_width : (k_table + 1) * piece_width], table.value()
            )
            total = part if total is None else total + part
        return total

    for k in range(CHUNKS // SPAN):
        trade.give_span(k, partial(other, k))
        trade.pass_on_span(k, partial(mine, k))
    turned[...] = jnp.transpose(normed[...])
    for k, d_table in enumerate(d_tables):
        weight_grad(turned, grads.at[:, k * piece_width : (k + 1) * piece_width], d_table)
    made()
    gain_total = jnp.zeros((1, gain.shape[1]), F32)
    for j in range(CHUNKS):
        rows = rows_at(0, j, chunk)
        back, gain_part = norm_back(trade.take(j), value[rows, :], gain[row : row + 1, :])
        gain_total = gain_total + gain_part
        grad_out[rows, :] = back
        share.put(j, back.astype(BF16))
    d_gain[...] = gain_total
    for j in range(CHUNKS):
        share.arrived(j)
    trade.close()
    share.close()

    def finish(b, _):
        for k in range(3):
            stat_copy(b, k).wait_send()
            sum_copy(b, k).wait_send()
        return 0

    lax.fori_loop(0, blocks, finish, 0)


def back_kernel(
    layer, normed, key_seg, query_seg, resid, w_query, w_out, w_in, gains, noised, clean, steps, counted, counts,
    projected, mixed, middle, normed_two, log_sums, grad_out, branch, d_gain, losses, *refs, carry,
):
    pieces = len(carry.loads) - 1
    d_tables, refs = refs[:pieces], refs[pieces:]
    (result, normed_next, info), refs = refs[:3], refs[3:]
    loss_scratch, layer_refs = refs[:-LAYER_SCRATCH], refs[-LAYER_SCRATCH:]
    me = lax.axis_index(NARROW)
    carry.fetch()
    info[...] = jnp.zeros(info.shape, F32)
    mask = counted[...].astype(F32)
    for row, value in enumerate((noised[...], clean[...], steps[...])):
        info[row : row + 1, :] = value.astype(F32)
    info[3:4, :] = mask / counts[COUNT_ROW : COUNT_ROW + 1, 0:1]
    info[4:5, :] = mask
    greet([{NARROW: lax.rem(me + k, 4)} for k in range(1, 4)] + carry.peers())
    carry.begin(0, 1)

    def at_half():
        carry.begin(2)

    def at_feed():
        carry.fetched()
        carry.end(0)
        carry.hand_on(1)
        carry.begin(3)

    def at_sent():
        carry.leave(0, 1, 2, 3)
        carry.hand_on(2)
        carry.begin(4)

    def at_last():
        carry.hand_on(3)

    forward_part(
        layer,
        [lambda which: w_query[which], lambda: w_out[...], lambda: w_in[...], carry.loads[0].value],
        (at_half, at_feed, at_sent, at_last),
        normed, key_seg, query_seg, resid, gains,
        projected, mixed, middle, normed_two, log_sums, result, normed_next, *layer_refs,
    )
    carry.hand_on(4)
    carry.end(1, 2, 3)
    loss_part(
        2 * layer + 2, normed_next, info, result, gains, carry.loads[1:], grad_out, branch, d_gain, losses, d_tables,
        *loss_scratch, *layer_refs[2:6], *layer_refs[-2:], made=lambda: carry.leave(*range(9, 9 + pieces)),
    )
    carry.gone()


def last_and_loss(
    layer, normed, key_seg, query_seg, resid, w_query, w_out, w_in, gains, tokens, counts, vocab, collective_id, loads
):
    seq_len, width = normed.shape
    heads_width = w_query.shape[2]
    half, blocks = seq_len // 2, seq_len // LANES
    pieces = len(loads) - 1
    return run(
        functools.partial(back_kernel, layer),
        "last_and_loss",
        [normed, key_seg, query_seg, resid, w_query, w_out, w_in, gains, *tokens, counts],
        layer_outs(seq_len, width, heads_width)
        + [
            jax.ShapeDtypeStruct((half, width), F32),
            jax.ShapeDtypeStruct((seq_len, width), BF16),
            jax.ShapeDtypeStruct((1, width), F32),
            jax.ShapeDtypeStruct((1, seq_len), F32),
        ]
        + [jax.ShapeDtypeStruct((width, vocab // pieces), BF16)] * pieces,
        [
            pltpu.VMEM((half, width), F32),
            pltpu.VMEM((seq_len, width), BF16),
            pltpu.VMEM((8, seq_len), F32),
            pltpu.VMEM((seq_len, vocab), F32),
            pltpu.VMEM((seq_len, vocab), BF16),
            pltpu.VMEM((blocks, 2, LANES, LANES), F32),
            pltpu.VMEM((width, seq_len), BF16),
            pltpu.VMEM((blocks, 8, LANES), F32),
            pltpu.VMEM((3, blocks, 8, LANES), F32),
            pltpu.VMEM((blocks, 8, LANES), F32),
            pltpu.VMEM((3, blocks, 8, LANES), F32),
        ]
        + [pltpu.SemaphoreType.DMA((3, blocks))] * 4
        + layer_scratch(seq_len, width, heads_width),
        collective_id,
        loads,
        lazy=(3, 6),
        early=(0, 1, 2, 3) + tuple(range(9, 9 + pieces)),
    )


def sum_ways(place, me, slow, fast, slows, group):
    near = [{NARROW: lax.rem(place + step, group)} for step in range(1, group)]
    return near, {WIDE: me + 1 - 2 * fast}


def tail_kernel(
    layers, branch, ids_all, losses, *refs, carry,
):
    gain_parts, refs = refs[: 2 * layers + 1], refs[2 * layers + 1 :]
    squares, refs = refs[: len(refs) - 25], refs[len(refs) - 25 :]
    tail_body(branch, ids_all, losses, gain_parts, squares, *refs, carry)


def tail_body(
    branch, ids_all, losses, gain_parts, squares,
    d_table, d_small, scalars,
    out_blocks, all_in, masked, picks, total, gains_out, gains_in, blocks, block_in, line_out, line_in,
    near, along,
    wide_send, wide_recv, far_send, far_recv, near_send, near_recv, all_send, all_recv,
    sum_sems,
    carry,
):
    seq_len, width = branch.shape
    quarter, half = seq_len // 4, seq_len // 2
    owners = ids_all.shape[0]
    share, vocab = d_table.shape
    sibling, partner, mine, other = group_places(seq_len)
    place = lax.axis_index(NARROW)
    side = lax.div(place, 2)
    me, slow, fast, slows = wide_places(owners)
    beside = {WIDE: me + 1 - 2 * fast}
    group = near.shape[0]
    first = place * vocab
    around = [lax.rem(me + step, owners) for step in range(owners)]
    at_quarter = pl.multiple_of(mine + side * quarter, quarter)
    held = 2 * lax.rem(place, 2) + side

    def along_way(step):
        return {WIDE: 2 * lax.rem(slow + step, slows) + fast}

    def wide_copy(step):
        return remote(
            out_blocks.at[around[step]], all_in.at[me, held],
            wide_send.at[step], wide_recv.at[step], {WIDE: around[step]},
        )

    def far_copy(step):
        rows = all_in.at[around[step], held]
        return remote(rows, rows, far_send.at[step], far_recv.at[step], partner)

    def near_copy(step):
        rows = all_in.at[around[step], pl.ds(2 * lax.rem(place, 2), 2)]
        return remote(rows, rows, near_send.at[step], near_recv.at[step], sibling)

    def gain_near():
        return remote(gains_out, gains_in, sum_sems.at[0, 0], sum_sems.at[1, 0], sibling)

    def gain_pair(step):
        return remote(
            blocks.at[2 * lax.rem(slow + step, slows) + 1 - fast], block_in.at[step],
            sum_sems.at[2, step], sum_sems.at[3, step], beside,
        )

    def gain_line(step):
        return remote(line_out.at[step], line_in.at[step], sum_sems.at[4, step], sum_sems.at[5, step], along_way(step))

    near_ways = [{NARROW: lax.rem(place + step, group)} for step in range(1, group)]
    greet([{WIDE: device} for device in around[1:]] + near_ways)
    gains_out[...] = jnp.zeros(gains_out.shape, F32)
    for row, part in enumerate(gain_parts):
        gains_out[row : row + 1, :] = part[...]
    gain_near().start()
    out_blocks[...] = jnp.transpose(branch[pl.ds(at_quarter, quarter), :]).reshape(out_blocks.shape)
    for step in range(1, owners):
        wide_copy(step).start()
    all_in[me, held] = out_blocks[me]
    carry.begin(*carry.all())
    gain_near().wait_recv()
    both = gains_out[...] + gains_in[...]
    for owner in range(owners):
        blocks[owner] = lax.dot_general(
            both, feature_places(owner, width, share).astype(F32), (((1,), (1,)), ((), ())),
            precision=lax.Precision.HIGHEST, preferred_element_type=F32,
        )
    for step in range(slows):
        gain_pair(step).start()

    def hand_on(step):
        if step:
            wide_copy(owners - step).wait_recv()
        far_copy(step).start()

    def hand_over(step):
        far_copy(step).wait_recv()
        near_copy(step).start()

    def gather_grad(step, first_turn):
        near_copy(step).wait_recv()
        row = around[step]

        for k in range(seq_len // quarter):
            columns = slice(k * quarter, (k + 1) * quarter)
            high, found = token_parts(ids_all[row, k : k + 1, :], first)
            picks[:, columns] = found
            grads = all_in[row, k]
            for part in range(vocab // LANES):
                inside = jnp.where(high == part, 1.0, 0.0).astype(BF16)
                masked[part * share : (part + 1) * share, columns] = grads * inside
        span = 8 * share

        def some(i, _):
            rows = rows_at(0, i, span)
            part = dot_nt(masked[rows, :], picks[...])
            total[rows, :] = part if first_turn else total[rows, :] + part
            return 0

        lax.fori_loop(0, total.shape[0] // span, some, 0)

    order = [0] + list(range(1, owners))
    for turn in range(owners + 2):
        if turn < owners:
            hand_on(order[turn])
        if 1 <= turn < owners + 1:
            hand_over(order[turn - 1])
        if turn == 1:
            for step in list(range(1, slows)) + [0]:
                gain_pair(step).wait_recv()
                line_out[step] = blocks[2 * lax.rem(slow + step, slows) + fast] + block_in[step]
                if step:
                    gain_line(step).start()
        if turn >= 2:
            gather_grad(order[turn - 2], turn == 2)
    for t in range(vocab // LANES):
        d_table[:, t * LANES : (t + 1) * LANES] = total[t * share : (t + 1) * share, :]
    small = line_out[0]
    for step in range(1, slows):
        gain_line(step).wait_recv()
        small = small + line_in[step]
    d_small[...] = small
    carry.end(*carry.all())
    square = jnp.sum(d_table[...] * d_table[...])
    for part in squares:
        square = square + part[0, 0]
    for load in carry.loads:
        square = square + load.squares[0, 0]
    lead = (place == 0).astype(F32)
    square = square + lead * jnp.sum(small * small)
    lanes = lax.broadcasted_iota(jnp.int32, (8, LANES), 1)
    given = jnp.where(lanes == 0, square, jnp.where(lanes == 1, lead * jnp.sum(losses[...]), 0.0))

    def scalar_near(step):
        return remote(near.at[place], near.at[place], sum_sems.at[6, step], sum_sems.at[7, step], near_ways[step - 1])

    def scalar_wide(step):
        return remote(along.at[me], along.at[me], all_send.at[step], all_recv.at[step], {WIDE: around[step]})

    near[place] = given
    for step in range(1, group):
        scalar_near(step).start()
    for step in range(1, group):
        scalar_near(step).wait()
    along[me] = jnp.sum(near[...], axis=0)
    for step in range(1, owners):
        scalar_wide(step).start()
    for step in range(1, owners):
        scalar_wide(step).wait()
    scalars[...] = jnp.sum(along[...], axis=0)
    gain_near().wait_send()
    for step in range(owners):
        far_copy(step).wait_send()
        near_copy(step).wait_send()
        if step:
            wide_copy(step).wait_send()
    for step in range(slows):
        gain_pair(step).wait_send()
        if step:
            gain_line(step).wait_send()


def tail(branch, ids_all, losses, gain_parts, squares, share, vocab, group, collective_id, loads):
    seq_len, width = branch.shape
    owners = ids_all.shape[0]
    slows = owners // 2
    dma = pltpu.SemaphoreType.DMA
    small = (8, LANES)
    return run(
        functools.partial(tail_kernel, (len(gain_parts) - 1) // 2),
        "tail",
        [branch, ids_all, losses, *gain_parts, *squares],
        [
            jax.ShapeDtypeStruct((share, vocab), F32),
            jax.ShapeDtypeStruct(small, F32),
            jax.ShapeDtypeStruct(small, F32),
        ],
        [
            pltpu.VMEM((owners, share, seq_len // 4), BF16),
            pltpu.VMEM((owners, 4, share, seq_len // 4), BF16),
            pltpu.VMEM((vocab // LANES * share, seq_len), BF16),
            pltpu.VMEM((LANES, seq_len), BF16),
            pltpu.VMEM((vocab // LANES * share, LANES), F32),
            pltpu.VMEM((8, width), F32),
            pltpu.VMEM((8, width), F32),
            pltpu.VMEM((owners,) + small, F32),
            pltpu.VMEM((slows,) + small, F32),
            pltpu.VMEM((slows,) + small, F32),
            pltpu.VMEM((slows,) + small, F32),
            pltpu.VMEM((group,) + small, F32),
            pltpu.VMEM((owners,) + small, F32),
        ]
        + [dma((owners,))] * 8
        + [dma((12, max(slows, group)))],
        collective_id,
        loads,
    )


PIECES = 4
TABLE, ATTN_IN, ATTN_OUT, FFN_IN, FFN_OUT = range(5)


def shares_tile(wide, narrow, noised, attn_out, ffn_in, tables):
    rows, seq_len = noised.shape
    return (
        attn_out.shape[0] == 2
        and narrow == 4
        and wide % 2 == 0
        and rows == 1
        and seq_len % (2 * CHUNKS * 128) == 0
        and tables.shape[1] * wide % 256 == 0
        and attn_out.shape[1] % 16 == 0
        and attn_out.shape[1] <= LANES
        and ffn_in.shape[2] % 128 == 0
        and tables.shape[1] == attn_out.shape[1]
        and tables.shape[2] % (PIECES * TILE) == 0
    )


def per_device(wide, narrow, *arrays):
    noised, attn_out, ffn_in, tables = arrays[0], arrays[6], arrays[7], arrays[9]
    if shares_tile(wide, narrow, noised, attn_out, ffn_in, tables):
        return tiled_device(wide, *arrays)
    return general_device(*arrays)


def tiled_device(
    wide,
    noised,
    clean,
    timesteps,
    segments,
    counted,
    attn_in,
    attn_out,
    ffn_in,
    ffn_out,
    tables,
    gains,
    attn_in_mean,
    attn_out_mean,
    ffn_in_mean,
    ffn_out_mean,
    tables_mean,
    gains_mean,
    attn_in_square,
    attn_out_square,
    ffn_in_square,
    ffn_out_square,
    tables_square,
    gains_square,
):
    layers = attn_in.shape[0]
    gain_rows, gain_cols = gains.shape
    share, vocab = tables.shape[1:]
    leads = (1, 0, 0, 0)
    four = (attn_in, attn_out, ffn_in, ffn_out)

    def joined(value, lead):
        return value.reshape(value.shape[:lead] + (-1,) + value.shape[lead + 2 :])

    ids = noised.reshape(4, -1)
    steps = timesteps.reshape(-1, LANES)
    half_width = D // 2
    rates = jnp.exp(-math.log(10000.0) * jnp.arange(half_width, dtype=F32) / half_width)[None, :]
    quarter = vocab // PIECES
    windows = [(k * quarter, quarter) for k in range(PIECES)]
    key_seg, query_seg = segments.reshape(-1, 1), segments.reshape(1, -1)
    weights = (attn_in, attn_out, ffn_in, ffn_out)
    (residual, normed, gain_w, counts, ids_all, projected, mixed, middle, normed_two, log_sums, result, normed_next), carried = front(
        ids, counted, gains, steps, rates, tables, key_seg, query_seg, wide, attn_out.shape[2], 0,
        [GatherLoad(value, 0, lead, wide, place=KEPT) for value, lead in zip(weights, leads)]
        + [GatherLoad(value, 1, lead, wide) for value, lead in zip(weights[:3], leads)]
        + [SlowLoad(ffn_out, 1, 0, wide)],
    )
    token_total = counts[gain_rows, 0]
    first_w = [joined(value, lead) for value, lead in zip(carried[:4], leads)]
    query_w, output_w, expand_w = [joined(value, lead) for value, lead in zip(carried[4:7], leads)]
    kept = [(residual, normed, projected, mixed, middle, normed_two, log_sums, *first_w)]
    (projected, mixed, middle, normed_two, log_sums, grad, branch, gain_final, losses, *d_last), (reduce_w,) = last_and_loss(
        1, normed_next, key_seg, query_seg, result, query_w, output_w, expand_w, gain_w,
        (noised, clean, timesteps, counted), counts, vocab, 1,
        [FastLoad(carried[7], 0, wide)]
        + [GatherLoad(tables, 1, 0, wide, window, place=LOCAL) for window in windows],
    )
    kept.append(
        (result, normed_next, projected, mixed, middle, normed_two, log_sums)
        + (query_w, output_w, expand_w, joined(reduce_w, 0))
    )
    own, squares = {}, []

    def by_owner(value, lead):
        shape = value.shape
        return value.reshape(shape[:lead] + (wide, shape[lead] // wide) + shape[lead + 1 :])

    def landed(key, results):
        own[key] = results[0]
        squares.append(results[1])
        return results[2:]

    hidden = ffn_in.shape[2]
    made = jax.ShapeDtypeStruct((wide, share, hidden), BF16)
    made_in = jax.ShapeDtypeStruct((3, wide, share, attn_in.shape[3]), BF16)
    made_out = jax.ShapeDtypeStruct((wide, share, attn_out.shape[2]), BF16)

    def start_last(carry, d_red, d_in):
        carry.loads[PIECES].full, carry.loads[PIECES + 1].full = d_red, d_in
        carry.begin(*range(PIECES))

    half_pieces = PIECES // 2
    points = (
        start_last,
        lambda carry: carry.begin(PIECES, PIECES + 1),
        lambda carry: carry.hand_on(*range(half_pieces)),
        lambda carry: carry.hand_on(*range(half_pieces, PIECES)),
        lambda carry, d_out, d_query: None,
    )
    residual, normed, projected, mixed, middle, normed_two, log_sums, *four_w = kept[1]
    query_w, output_w, expand_w, reduce_w = four_w
    (grad, branch, d_out, d_query, gain_two, gain_one), carried = backward_block(
        1, None, points, grad, branch, reduce_w, expand_w, output_w, normed_two, middle, gain_w, mixed,
        projected, log_sums, key_seg, query_seg, query_w, residual, normed, wide, 2,
        [ReduceLoad(by_owner(piece, 0), 0) for piece in d_last]
        + [PairLoad(made, 0, True), PairLoad(made, 0, True)],
    )
    for k in range(PIECES):
        carried = landed((TABLE, k), carried)
    red_sums, in_sums = carried
    gain_grads = [None, None, gain_one, gain_two, gain_final]

    def start_first(carry, d_red, d_in):
        carry.loads[4].full, carry.loads[5].full = d_red, d_in
        carry.begin(0, 1, 2, 3)

    def sent_first(carry, d_out, d_query):
        carry.hand_on(5)
        carry.loads[6].full, carry.loads[7].full = d_out, d_query
        carry.begin(6, 7)

    points = (
        start_first,
        lambda carry: carry.begin(4, 5),
        lambda carry: carry.hand_on(2, 3),
        lambda carry: carry.hand_on(4),
        sent_first,
    )
    residual, normed, projected, mixed, middle, normed_two, log_sums, *four_w = kept[0]
    query_w, output_w, expand_w, reduce_w = four_w
    (grad, branch, _, d_query, gain_two, gain_one), carried = backward_block(
        0, math.sqrt(D), points, grad, branch, reduce_w, expand_w, output_w, normed_two, middle, gain_w, mixed,
        projected, log_sums, key_seg, query_seg, query_w, residual, normed, wide, 3,
        [LineLoad(red_sums, wide), LineLoad(in_sums, wide), ReduceLoad(d_out, 0), ReduceLoad(d_query, 1)]
        + [ReduceLoad(made, 0, True), ReduceLoad(made, 0, True), PairLoad(made_out, 0, True), PairLoad(made_in, 1, True)],
    )
    for key in ((FFN_OUT, 1), (FFN_IN, 1), (ATTN_OUT, 1), (ATTN_IN, 1), (FFN_OUT, 0), (FFN_IN, 0)):
        carried = landed(key, carried)
    out_sums, in_sums = carried
    gain_grads[:2] = gain_one, gain_two

    (own_first, total_small, scalars), carried = tail(
        branch, ids_all, losses, gain_grads, squares, share, vocab, 4, 4,
        [LineLoad(out_sums, wide), LineLoad(in_sums, wide)],
    )
    own[ATTN_OUT, 0], own[ATTN_IN, 0] = carried[0], carried[2]
    grad_attn_in, grad_attn_out, grad_ffn_in, grad_ffn_out = [
        jnp.stack([own[name, index] for index in range(layers)]) for name in (ATTN_IN, ATTN_OUT, FFN_IN, FFN_OUT)
    ]
    grad_tables = jnp.stack([own_first, jnp.concatenate([own[TABLE, k] for k in range(PIECES)], axis=1)])
    grad_gains = total_small[:gain_rows, :gain_cols]
    total_square, loss_sum = scalars[0, 0], scalars[0, 1]
    grad_norm = jnp.sqrt(total_square)
    factor = jnp.minimum(1.0, CLIP_NORM / (grad_norm + 1e-06))
    results = [loss_sum, token_total, grad_norm]
    for weight, gradient, first, second, decay, rate in (
        (attn_in, grad_attn_in, attn_in_mean, attn_in_square, WEIGHT_DECAY, LEARN_RATE),
        (attn_out, grad_attn_out, attn_out_mean, attn_out_square, WEIGHT_DECAY, LEARN_RATE),
        (ffn_in, grad_ffn_in, ffn_in_mean, ffn_in_square, WEIGHT_DECAY, LEARN_RATE),
        (ffn_out, grad_ffn_out, ffn_out_mean, ffn_out_square, WEIGHT_DECAY, LEARN_RATE),
        (tables, grad_tables, tables_mean, tables_square, WEIGHT_DECAY, LEARN_RATE),
        (gains, grad_gains, gains_mean, gains_square, 0.0, GAIN_RATE),
    ):
        results += adam(weight, factor * gradient, first, second, decay, rate)
    return tuple(results)


def solution(mesh):
    wide, narrow = mesh.shape[WIDE], mesh.shape[NARROW]
    placed = (
        P(WIDE, None),
        P(WIDE, None),
        P(WIDE, None),
        P(WIDE, None),
        P(WIDE, None),
        P(None, None, WIDE, NARROW),
        P(None, WIDE, NARROW),
        P(None, WIDE, NARROW),
        P(None, WIDE, NARROW),
        P(None, WIDE, NARROW),
        P(None, WIDE),
        P(None, None, WIDE, NARROW),
        P(None, WIDE, NARROW),
        P(None, WIDE, NARROW),
        P(None, WIDE, NARROW),
        P(None, WIDE, NARROW),
        P(None, WIDE),
        P(None, None, WIDE, NARROW),
        P(None, WIDE, NARROW),
        P(None, WIDE, NARROW),
        P(None, WIDE, NARROW),
        P(None, WIDE, NARROW),
        P(None, WIDE),
    )
    return jax.shard_map(
        functools.partial(per_device, wide, narrow),
        mesh=mesh,
        in_specs=placed,
        out_specs=(
            P(),
            P(),
            P(),
            P(None, None, WIDE, NARROW),
            P(None, None, WIDE, NARROW),
            P(None, None, WIDE, NARROW),
            P(None, None, WIDE, NARROW),
            P(None, WIDE, NARROW),
            P(None, WIDE, NARROW),
            P(None, WIDE, NARROW),
            P(None, WIDE, NARROW),
            P(None, WIDE, NARROW),
            P(None, WIDE, NARROW),
            P(None, WIDE, NARROW),
            P(None, WIDE, NARROW),
            P(None, WIDE, NARROW),
            P(None, WIDE, NARROW),
            P(None, WIDE, NARROW),
            P(None, WIDE, NARROW),
            P(None, WIDE, NARROW),
            P(None, WIDE, NARROW),
            P(None, WIDE, NARROW),
            P(None, WIDE, NARROW),
            P(None, WIDE),
            P(None, WIDE),
            P(None, WIDE),
            P(None, WIDE),
        ),
        check_vma=False,
    )
```

```python
import functools
import math

import jax
import jax.numpy as jnp
from jax import lax
from jax.experimental import pallas as pl
from jax.experimental.pallas import tpu as pltpu
from jax.sharding import PartitionSpec as P

D = 768
HD = 64
V = 8192
STEPS = 1000
ADAM_STEP = 10


NORM_EPS = 1e-05
LEARN_RATE = 0.05
GAIN_RATE = 0.75
FIRST_DECAY = 0.9
SECOND_DECAY = 0.999
ADAM_EPS = 1e-08
WEIGHT_DECAY = 0.01
CLIP_NORM = 0.005
WIDE, NARROW = "wide", "narrow"


def add_heads(partial_value):
    return lax.psum(partial_value, NARROW)


def back_heads(partial_value):
    return lax.psum(partial_value, NARROW)


def rms_forward(value, gain):
    scale_row = lax.rsqrt(jnp.mean(value * value, axis=-1, keepdims=True) + NORM_EPS)
    return (value * scale_row * gain, scale_row)


def rms_backward(grad, value, scale_row, gain):
    unit = value * scale_row
    scaled = grad * gain
    back = scale_row * (scaled - unit * jnp.mean(scaled * unit, axis=-1, keepdims=True))
    return (back, jnp.sum(grad * unit, axis=0))


def time_features(timestep_row):
    half_width = D // 2
    rates = jnp.exp(-math.log(10000.0) * jnp.arange(half_width, dtype=jnp.float32) / half_width)
    angles = timestep_row.astype(jnp.float32)[:, None] * rates[None, :]
    return jnp.concatenate([jnp.sin(angles), jnp.cos(angles)], axis=1)


def masked_scores(queries, key_rows, segment):
    scores = jnp.einsum(
        "qhd,khd->hqk", queries, key_rows, preferred_element_type=jnp.float32
    ) * HD ** (-0.5)
    return jnp.where((segment[:, None] == segment[None, :])[None], scores, -1e30)


def attend(entry):
    queries, key_rows, values, segment = entry
    scores = masked_scores(queries, key_rows, segment)
    row_top = jnp.max(scores, axis=-1, keepdims=True)
    log_total = row_top + jnp.log(jnp.sum(jnp.exp(scores - row_top), axis=-1, keepdims=True))
    probs = jnp.exp(scores - log_total).astype(jnp.bfloat16)
    mixed = jnp.einsum("hqk,khd->qhd", probs, values, preferred_element_type=jnp.float32)
    return (mixed.astype(jnp.bfloat16), log_total)


def attend_back(entry):
    queries, key_rows, values, segment, log_total, grad_mixed = entry
    probs = jnp.exp(masked_scores(queries, key_rows, segment) - log_total)
    grad_probs = jnp.einsum("qhd,khd->hqk", grad_mixed, values, preferred_element_type=jnp.float32)
    grad_scores = (
        probs * (grad_probs - jnp.sum(probs * grad_probs, axis=-1, keepdims=True))
    ).astype(jnp.bfloat16)
    grad_query = jnp.einsum(
        "hqk,khd->qhd", grad_scores, key_rows, preferred_element_type=jnp.float32
    ) * HD ** (-0.5)
    grad_key = jnp.einsum(
        "hqk,qhd->khd", grad_scores, queries, preferred_element_type=jnp.float32
    ) * HD ** (-0.5)
    grad_value = jnp.einsum(
        "hqk,qhd->khd", probs.astype(jnp.bfloat16), grad_mixed, preferred_element_type=jnp.float32
    )
    return (grad_query, grad_key, grad_value)


def layer_forward(residual, segments, query_w, output_w, expand_w, reduce_w, gain_attn, gain_ffn):
    seq_count, seq_len = segments.shape
    normed, scale_one = rms_forward(residual, gain_attn)
    normed = normed.astype(jnp.bfloat16)
    projected = jnp.einsum(
        "sd,cde->cse", normed, query_w, preferred_element_type=jnp.float32
    ).astype(jnp.bfloat16)
    heads = projected.reshape(3, seq_count, seq_len, -1, HD)
    mixed, log_total = lax.map(attend, (heads[0], heads[1], heads[2], segments))
    mixed = mixed.reshape(seq_count * seq_len, -1)
    middle = residual + add_heads(
        jnp.einsum("se,de->sd", mixed, output_w, preferred_element_type=jnp.float32)
    )
    normed_two, scale_two = rms_forward(middle, gain_ffn)
    normed_two = normed_two.astype(jnp.bfloat16)
    before = jnp.dot(normed_two, expand_w, preferred_element_type=jnp.float32)
    after = jax.nn.gelu(before).astype(jnp.bfloat16)
    result = middle + add_heads(
        jnp.einsum("sf,df->sd", after, reduce_w, preferred_element_type=jnp.float32)
    )
    return (
        result,
        (
            residual,
            scale_one,
            normed,
            projected,
            log_total,
            mixed,
            middle,
            scale_two,
            normed_two,
            before,
            after,
        ),
    )


def layer_backward(
    grad, kept, segments, query_w, output_w, expand_w, reduce_w, gain_attn, gain_ffn
):
    (
        residual,
        scale_one,
        normed,
        projected,
        log_total,
        mixed,
        middle,
        scale_two,
        normed_two,
        before,
        after,
    ) = kept
    seq_count, seq_len = segments.shape
    grad_branch = grad.astype(jnp.bfloat16)
    grad_after = jnp.dot(grad_branch, reduce_w, preferred_element_type=jnp.float32)
    grad_reduce = jnp.einsum("sd,sf->df", grad_branch, after, preferred_element_type=jnp.float32)
    _, gelu_pull = jax.vjp(jax.nn.gelu, before)
    grad_before = gelu_pull(grad_after)[0].astype(jnp.bfloat16)
    grad_expand = jnp.einsum(
        "sd,sf->df", normed_two, grad_before, preferred_element_type=jnp.float32
    )
    grad_normed_two = back_heads(
        jnp.einsum("sf,df->sd", grad_before, expand_w, preferred_element_type=jnp.float32)
    )
    grad_middle, grad_gain_ffn = rms_backward(grad_normed_two, middle, scale_two, gain_ffn)
    grad_middle = grad_middle + grad
    grad_attn = grad_middle.astype(jnp.bfloat16)
    grad_mixed = jnp.dot(grad_attn, output_w, preferred_element_type=jnp.float32).astype(
        jnp.bfloat16
    )
    grad_output = jnp.einsum("sd,se->de", grad_attn, mixed, preferred_element_type=jnp.float32)
    heads = projected.reshape(3, seq_count, seq_len, -1, HD)
    grad_query, grad_key, grad_value = lax.map(
        attend_back,
        (
            heads[0],
            heads[1],
            heads[2],
            segments,
            log_total,
            grad_mixed.reshape(seq_count, seq_len, -1, HD),
        ),
    )
    grad_projected = (
        jnp.stack([grad_query, grad_key, grad_value])
        .reshape(3, seq_count * seq_len, -1)
        .astype(jnp.bfloat16)
    )
    grad_query_w = jnp.einsum(
        "sd,cse->cde", normed, grad_projected, preferred_element_type=jnp.float32
    )
    grad_normed = back_heads(
        jnp.einsum("cse,cde->sd", grad_projected, query_w, preferred_element_type=jnp.float32)
    )
    grad_input, grad_gain_attn = rms_backward(grad_normed, residual, scale_one, gain_attn)
    return (
        grad_input + grad_middle,
        (
            grad_query_w,
            grad_output,
            grad_expand,
            grad_reduce,
            jnp.stack([grad_gain_attn, grad_gain_ffn]),
        ),
    )


def adam(weight, grad, first, second, decay, rate):
    first_new = FIRST_DECAY * first + (1.0 - FIRST_DECAY) * grad
    second_new = SECOND_DECAY * second + (1.0 - SECOND_DECAY) * grad * grad
    first_hat = first_new / (1.0 - FIRST_DECAY**ADAM_STEP)
    second_hat = second_new / (1.0 - SECOND_DECAY**ADAM_STEP)
    weight_new = weight - rate * (first_hat / (jnp.sqrt(second_hat) + ADAM_EPS) + decay * weight)
    return (weight_new, first_new, second_new, weight_new.astype(jnp.bfloat16))


def general_device(
    noised,
    clean,
    timesteps,
    segments,
    counted,
    attn_in,
    attn_out,
    ffn_in,
    ffn_out,
    tables,
    gains,
    attn_in_mean,
    attn_out_mean,
    ffn_in_mean,
    ffn_out_mean,
    tables_mean,
    gains_mean,
    attn_in_square,
    attn_out_square,
    ffn_in_square,
    ffn_out_square,
    tables_square,
    gains_square,
):
    layers = attn_in.shape[0]
    mask = counted.reshape(-1).astype(jnp.float32)
    token_total = lax.psum(jnp.sum(mask), WIDE)
    query_w, output_w, expand_w, reduce_w, table_w, gain_low = (
        lax.all_gather(attn_in.astype(jnp.bfloat16), WIDE, axis=2, tiled=True),
        lax.all_gather(attn_out.astype(jnp.bfloat16), WIDE, axis=1, tiled=True),
        lax.all_gather(ffn_in.astype(jnp.bfloat16), WIDE, axis=1, tiled=True),
        lax.all_gather(ffn_out.astype(jnp.bfloat16), WIDE, axis=1, tiled=True),
        lax.all_gather(tables.astype(jnp.bfloat16), WIDE, axis=1, tiled=True),
        lax.all_gather(gains.astype(jnp.bfloat16), WIDE, axis=1, tiled=True),
    )
    gain_w = gain_low.astype(jnp.float32)
    noised_flat = noised.reshape(-1)
    clean_flat = clean.reshape(-1)
    step_flat = timesteps.reshape(-1)
    vocab_local = table_w.shape[2]
    vocab_ids = lax.axis_index(NARROW) * vocab_local + jnp.arange(vocab_local, dtype=jnp.int32)
    picks = (noised_flat[:, None] == vocab_ids[None, :]).astype(jnp.bfloat16)
    looked = add_heads(
        jnp.einsum("sv,dv->sd", picks, table_w[0], preferred_element_type=jnp.float32)
    )
    residual = math.sqrt(D) * looked + time_features(step_flat)
    kept_layers = []
    for layer_index in range(layers):
        residual, kept = layer_forward(
            residual,
            segments,
            query_w[layer_index],
            output_w[layer_index],
            expand_w[layer_index],
            reduce_w[layer_index],
            gain_w[2 * layer_index],
            gain_w[2 * layer_index + 1],
        )
        kept_layers.append(kept)
    final, scale_final = rms_forward(residual, gain_w[2 * layers])
    final_low = final.astype(jnp.bfloat16)
    logits = jnp.dot(final_low, table_w[1], preferred_element_type=jnp.float32)
    local_top = jnp.max(logits, axis=1)
    row_top = lax.pmax(local_top, NARROW)
    row_total = lax.psum(jnp.sum(jnp.exp(logits - row_top[:, None]), axis=1), NARROW)
    log_probs = logits - (row_top + jnp.log(row_total))[:, None]
    probs = jnp.exp(log_probs)
    clamped = jnp.maximum(step_flat, 2).astype(jnp.float32)[:, None]
    beta = 1.0 / (STEPS - clamped + 1.0)
    retain = (STEPS - clamped + 1.0) / STEPS
    spread = (clamped - 1.0) / (STEPS * V)
    at_noised = (vocab_ids[None, :] == noised_flat[:, None]).astype(jnp.float32)
    at_clean = (vocab_ids[None, :] == clean_flat[:, None]).astype(jnp.float32)
    forward_fac = beta / V + (1.0 - beta) * at_noised
    backward_fac = retain * at_clean + spread
    joint = forward_fac * backward_fac
    marginal = retain * probs + spread
    joint_total, cross, model_total, weighted, aligned, clean_logp = lax.psum(
        (
            jnp.sum(joint, axis=1),
            jnp.sum(joint * (jnp.log(backward_fac) - jnp.log(marginal)), axis=1),
            jnp.sum(forward_fac * marginal, axis=1),
            jnp.sum(probs * joint / marginal, axis=1),
            jnp.sum(forward_fac * probs, axis=1),
            jnp.sum(at_clean * log_probs, axis=1),
        ),
        NARROW,
    )
    divergence = cross / joint_total - jnp.log(joint_total) + jnp.log(model_total)
    first_step = step_flat == 1
    losses = jnp.where(first_step, -clean_logp, divergence)
    pull = retain * (
        -(joint / joint_total[:, None]) / marginal + forward_fac / model_total[:, None]
    )
    centre = retain[:, 0] * (-weighted / joint_total + aligned / model_total)
    grad_kl = probs * (pull - centre[:, None])
    grad_recon = probs - at_clean
    grad_logits = (
        (mask / token_total)[:, None] * jnp.where(first_step[:, None], grad_recon, grad_kl)
    ).astype(jnp.bfloat16)
    grad_table_out = jnp.einsum(
        "sd,sv->dv", final_low, grad_logits, preferred_element_type=jnp.float32
    )
    grad_final = back_heads(
        jnp.einsum("sv,dv->sd", grad_logits, table_w[1], preferred_element_type=jnp.float32)
    )
    grad_x, grad_gain_final = rms_backward(grad_final, residual, scale_final, gain_w[2 * layers])
    layer_grads = [None] * layers
    for layer_index in reversed(range(layers)):
        grad_x, produced = layer_backward(
            grad_x,
            kept_layers[layer_index],
            segments,
            query_w[layer_index],
            output_w[layer_index],
            expand_w[layer_index],
            reduce_w[layer_index],
            gain_w[2 * layer_index],
            gain_w[2 * layer_index + 1],
        )
        layer_grads[layer_index] = produced
    grad_look = (math.sqrt(D) * grad_x).astype(jnp.bfloat16)
    grad_table_in = jnp.einsum("sd,sv->dv", grad_look, picks, preferred_element_type=jnp.float32)
    stacked = [jnp.stack([entry[which] for entry in layer_grads]) for which in range(5)]
    gain_layers = stacked[4].reshape(2 * layers, -1)
    grad_tables_all = jnp.stack([grad_table_in, grad_table_out])
    grad_attn_in, grad_attn_out, grad_ffn_in, grad_ffn_out, grad_tables, grad_gains = (
        lax.psum_scatter(stacked[0], WIDE, scatter_dimension=2, tiled=True),
        lax.psum_scatter(stacked[1], WIDE, scatter_dimension=1, tiled=True),
        lax.psum_scatter(stacked[2], WIDE, scatter_dimension=1, tiled=True),
        lax.psum_scatter(stacked[3], WIDE, scatter_dimension=1, tiled=True),
        lax.psum_scatter(grad_tables_all, WIDE, scatter_dimension=1, tiled=True),
        lax.psum_scatter(
            jnp.concatenate([gain_layers, grad_gain_final[None, :]], axis=0),
            WIDE,
            scatter_dimension=1,
            tiled=True,
        ),
    )
    narrow_first = (lax.axis_index(NARROW) == 0).astype(jnp.float32)
    squares = (
        jnp.sum(grad_attn_in * grad_attn_in)
        + jnp.sum(grad_attn_out * grad_attn_out)
        + jnp.sum(grad_ffn_in * grad_ffn_in)
        + jnp.sum(grad_ffn_out * grad_ffn_out)
        + jnp.sum(grad_tables * grad_tables)
        + narrow_first * jnp.sum(grad_gains * grad_gains)
    )
    squares, loss_sum = lax.psum(
        (squares, narrow_first * jnp.sum(mask * losses)), (WIDE, NARROW)
    )
    grad_norm = jnp.sqrt(squares)
    factor = jnp.minimum(1.0, CLIP_NORM / (grad_norm + 1e-06))
    attn_in_next, attn_in_mean_next, attn_in_square_next, attn_in_copy = adam(
        attn_in, factor * grad_attn_in, attn_in_mean, attn_in_square, WEIGHT_DECAY, LEARN_RATE
    )
    attn_out_next, attn_out_mean_next, attn_out_square_next, attn_out_copy = adam(
        attn_out, factor * grad_attn_out, attn_out_mean, attn_out_square, WEIGHT_DECAY, LEARN_RATE
    )
    ffn_in_next, ffn_in_mean_next, ffn_in_square_next, ffn_in_copy = adam(
        ffn_in, factor * grad_ffn_in, ffn_in_mean, ffn_in_square, WEIGHT_DECAY, LEARN_RATE
    )
    ffn_out_next, ffn_out_mean_next, ffn_out_square_next, ffn_out_copy = adam(
        ffn_out, factor * grad_ffn_out, ffn_out_mean, ffn_out_square, WEIGHT_DECAY, LEARN_RATE
    )
    tables_next, tables_mean_next, tables_square_next, tables_copy = adam(
        tables, factor * grad_tables, tables_mean, tables_square, WEIGHT_DECAY, LEARN_RATE
    )
    gains_next, gains_mean_next, gains_square_next, gains_copy = adam(
        gains, factor * grad_gains, gains_mean, gains_square, 0.0, GAIN_RATE
    )
    return (
        loss_sum,
        token_total,
        grad_norm,
        attn_in_next,
        attn_in_mean_next,
        attn_in_square_next,
        attn_in_copy,
        attn_out_next,
        attn_out_mean_next,
        attn_out_square_next,
        attn_out_copy,
        ffn_in_next,
        ffn_in_mean_next,
        ffn_in_square_next,
        ffn_in_copy,
        ffn_out_next,
        ffn_out_mean_next,
        ffn_out_square_next,
        ffn_out_copy,
        tables_next,
        tables_mean_next,
        tables_square_next,
        tables_copy,
        gains_next,
        gains_mean_next,
        gains_square_next,
        gains_copy,
    )


MESH = pl.DeviceIdType.MESH
SLOW, FAST = 1, 2
HBM, KEPT, LOCAL = 1, 2, 3
F32 = jnp.float32
BF16 = jnp.bfloat16
CHUNKS = 4
SPAN = 2
VMEM_LIMIT = 61 * 1024 * 1024
FORWARD_KIND = BF16
BACKWARD_KIND = BF16


def whole_vmem():
    return pl.BlockSpec(memory_space=pltpu.VMEM)


def dot_nn(a, b):
    return lax.dot_general(a, b, (((1,), (0,)), ((), ())), preferred_element_type=F32)


def dot_nt(a, b):
    return lax.dot_general(a, b, (((1,), (1,)), ((), ())), preferred_element_type=F32)


def remote(src, dst, send_sem, recv_sem, device):
    return pltpu.make_async_remote_copy(
        src_ref=src,
        dst_ref=dst,
        send_sem=send_sem,
        recv_sem=recv_sem,
        device_id=device,
        device_id_type=MESH,
    )


def greet(devices):
    barrier = pltpu.get_barrier_semaphore()
    for device in devices:
        pl.semaphore_signal(barrier, inc=1, device_id=device, device_id_type=MESH)
    pl.semaphore_wait(barrier, len(devices))


def group_places(seq_len):
    me = lax.axis_index(NARROW)
    core = lax.rem(me, 2)
    half = seq_len // 2
    mine = pl.multiple_of(core * half, half)
    other = pl.multiple_of((1 - core) * half, half)
    return ({NARROW: me + 1 - 2 * core}, {NARROW: lax.rem(me + 2, 4)}, mine, other)


class Exchange:
    def __init__(self, refs, sems, base, sibling, partner):
        self.near_out, self.near_in, self.far_out, self.far_in = refs
        self.send, self.recv = sems
        self.base, self.sibling, self.partner = base, sibling, partner

    def near(self, j):
        return remote(
            self.near_out.at[j],
            self.near_in.at[j],
            self.send.at[self.base, j],
            self.recv.at[self.base, j],
            self.sibling,
        )

    def far(self, j):
        return remote(
            self.far_out.at[j],
            self.far_in.at[j],
            self.send.at[self.base + 1, j],
            self.recv.at[self.base + 1, j],
            self.partner,
        )

    def give(self, j, value):
        self.near_out[j] = value
        self.near(j).start()

    def give_span(self, k, value):
        chunk = self.near_out.shape[1]
        for i in range(SPAN):
            self.give(SPAN * k + i, value[i * chunk : (i + 1) * chunk, :])

    def pass_on_span(self, k, value):
        chunk = self.near_out.shape[1]
        for i in range(SPAN):
            self.pass_on(SPAN * k + i, value[i * chunk : (i + 1) * chunk, :])

    def pass_on(self, j, value):
        self.near(j).wait_recv()
        self.far_out[j] = (value + self.near_in[j]).astype(self.far_out.dtype)
        self.far(j).start()

    def take(self, j):
        self.far(j).wait_recv()
        return self.far_out[j].astype(F32) + self.far_in[j].astype(F32)

    def close(self):
        for j in range(CHUNKS):
            self.near(j).wait_send()
            self.far(j).wait_send()

    @staticmethod
    def scratch(chunk, width, kind):
        return [
            pltpu.VMEM((CHUNKS, chunk, width), F32),
            pltpu.VMEM((CHUNKS, chunk, width), F32),
            pltpu.VMEM((CHUNKS, chunk, width), kind),
            pltpu.VMEM((CHUNKS, chunk, width), kind),
        ]


class Share:
    def __init__(self, ref, sems, base, sibling, mine, chunk):
        self.ref, self.base, self.sibling, self.mine, self.chunk = ref, base, sibling, mine, chunk
        self.send, self.recv = sems

    def piece(self, j):
        rows = self.ref.at[pl.ds(pl.multiple_of(self.mine + j * self.chunk, self.chunk), self.chunk)]
        return remote(rows, rows, self.send.at[self.base, j], self.recv.at[self.base, j], self.sibling)

    def put(self, j, value):
        self.ref[pl.ds(pl.multiple_of(self.mine + j * self.chunk, self.chunk), self.chunk), :] = value
        self.piece(j).start()

    def arrived(self, j):
        self.piece(j).wait_recv()

    def close(self):
        for j in range(CHUNKS):
            self.piece(j).wait_send()


def wide_places(count):
    me = lax.axis_index(WIDE)
    fast = lax.rem(me, 2)
    slow = me // 2
    return (me, slow, fast, count // 2)


class Carry:
    def __init__(self, loads, fetches, leaves):
        self.loads, self.fetches, self.leaves = loads, fetches, leaves
        self.left = []

    def fetch(self):
        for copy in self.fetches:
            copy.start()

    def fetched(self):
        for copy in self.fetches:
            copy.wait()

    def leave(self, *which):
        for k in which:
            self.leaves[k].start()
            self.left.append(k)

    def gone(self):
        self.leave(*[k for k in self.leaves if k not in self.left])
        for k in self.left:
            self.leaves[k].wait()

    def peers(self):
        ways = []
        for load in self.loads:
            ways += [way for way in load.ways if way not in ways]
        me, slow, fast, slows = wide_places(self.loads[0].count) if self.loads else (0, 0, 0, 0)
        found = []
        if SLOW in ways:
            found += [{WIDE: 2 * lax.rem(slow + step, slows) + fast} for step in range(1, slows)]
        if FAST in ways:
            found.append({WIDE: me + 1 - 2 * fast})
        return found

    def begin(self, *which):
        for k in which:
            self.loads[k].start()

    def hand_on(self, *which):
        for k in which:
            self.loads[k].relay()

    def end(self, *which):
        for k in which:
            self.loads[k].finish()

    def all(self):
        return range(len(self.loads))


def part_of(weights, index, window):
    shape = weights.shape[1:]
    return shape if window is None else shape[:-1] + (window[1],)


class SlowLoad:
    ways = (SLOW,)

    def __init__(self, weights, index, lead, count, window=None):
        self.index, self.lead, self.count, self.window = index, lead, count, window
        shape, slows = part_of(weights, index, window), count // 2
        self.operands, self.in_specs = [weights], [whole_vmem()]
        self.outs = [jax.ShapeDtypeStruct((slows,) + shape, BF16)]
        self.out_specs = [pl.BlockSpec(memory_space=pl.ANY)]
        self.scratch = [pltpu.VMEM(shape, BF16), pltpu.SemaphoreType.DMA] + [pltpu.SemaphoreType.DMA((slows,))] * 2

    def bind(self, given, out, scratch):
        self.shard, self.out = given[0], out[0]
        self.low, self.local, self.send, self.recv = scratch
        self.me, self.slow, self.fast, self.slows = wide_places(self.count)

    def cast(self):
        if self.window is None:
            self.low[...] = self.shard[self.index].astype(BF16)
        else:
            self.low[...] = self.shard[self.index, :, self.window[0] : self.window[0] + self.window[1]].astype(BF16)

    def target(self):
        return self.out.at[self.slow]

    def slow_copy(self, step):
        return remote(
            self.low, self.target(), self.send.at[step], self.recv.at[step],
            {WIDE: 2 * lax.rem(self.slow + step, self.slows) + self.fast},
        )

    def own_copy(self):
        return pltpu.make_async_copy(self.low, self.target(), self.local)

    def start(self):
        self.cast()
        for step in range(1, self.slows):
            self.slow_copy(step).start()
        self.own_copy().start()

    def finish(self):
        for step in range(1, self.slows):
            self.slow_copy(step).wait()
        self.own_copy().wait()


class FastLoad:
    ways = (FAST,)

    def __init__(self, blocks, lead, count):
        self.lead, self.count = lead, count
        shape, slows = blocks.shape[1:], count // 2
        self.operands, self.in_specs = [blocks], [pl.BlockSpec(memory_space=pl.ANY)]
        self.outs = [jax.ShapeDtypeStruct(shape[:lead] + (count,) + shape[lead:], BF16)]
        self.out_specs = [whole_vmem()]
        self.scratch = [pltpu.SemaphoreType.DMA((slows,))] * 3

    def value(self):
        return self.out[...].reshape((-1, self.out.shape[-1]))

    def bind(self, given, out, scratch):
        self.blocks, self.out = given[0], out[0]
        self.local, self.send, self.recv = scratch
        self.me, self.slow, self.fast, self.slows = wide_places(self.count)

    def copies(self, step):
        target = self.out.at[(slice(None),) * self.lead + (2 * step + self.fast,)]
        return (
            remote(
                self.blocks.at[step], target, self.send.at[step], self.recv.at[step],
                {WIDE: self.me + 1 - 2 * self.fast},
            ),
            pltpu.make_async_copy(self.blocks.at[step], target, self.local.at[step]),
        )

    def start(self):
        for step in range(self.slows):
            for copy in self.copies(step):
                copy.start()

    def finish(self):
        for step in range(self.slows):
            for copy in self.copies(step):
                copy.wait()


class GatherLoad(SlowLoad):
    ways = (SLOW, FAST)

    def __init__(self, weights, index, lead, count, window=None, place=HBM):
        super().__init__(weights, index, lead, count, window)
        shape, slows = part_of(weights, index, window), count // 2
        whole = shape[:lead] + (count,) + shape[lead:]
        self.outs = [jax.ShapeDtypeStruct(whole, BF16)]
        self.scratch = self.scratch + [pltpu.SemaphoreType.DMA((slows,))] * 2
        if place == KEPT:
            self.out_specs = [whole_vmem()]
        self.local_out = place == LOCAL
        if self.local_out:
            self.outs, self.out_specs = [], []
            self.scratch = self.scratch + [pltpu.VMEM(whole, BF16)]

    def bind(self, given, out, scratch):
        if self.local_out:
            out, scratch = scratch[-1:], scratch[:-1]
        super().bind(given, out, scratch[:-2])
        self.fast_send, self.fast_recv = scratch[-2:]

    def value(self, *index):
        found = self.out[index] if index else self.out[...]
        return found.reshape((-1, found.shape[-1]))

    def at(self, owner):
        return self.out.at[(slice(None),) * self.lead + (owner,)]

    def target(self):
        return self.at(self.me)

    def fast_copy(self, step):
        block = self.at(2 * lax.rem(self.slow + self.slows - step, self.slows) + self.fast)
        return remote(
            self.low if step == 0 else block, block, self.fast_send.at[step], self.fast_recv.at[step],
            {WIDE: self.me + 1 - 2 * self.fast},
        )

    def start(self):
        super().start()
        self.fast_copy(0).start()

    def relay(self):
        for step in range(1, self.slows):
            self.slow_copy(step).wait_recv()
            self.fast_copy(step).start()

    def finish(self):
        for step in range(self.slows):
            self.fast_copy(step).wait()
            if step:
                self.slow_copy(step).wait_send()
        self.own_copy().wait()


class PairLoad:
    ways = (FAST,)

    def __init__(self, full, lead, inside=False):
        self.lead, self.count, self.inside = lead, full.shape[lead], inside
        self.shape, self.slows = full.shape[:lead] + full.shape[lead + 1 :], self.count // 2
        self.operands, self.in_specs = ([], []) if inside else ([full], [whole_vmem()])
        self.outs, self.out_specs = [jax.ShapeDtypeStruct((self.slows,) + self.shape, BF16)], [whole_vmem()]
        self.scratch = [pltpu.VMEM((self.slows,) + self.shape, BF16)] + [pltpu.SemaphoreType.DMA((self.slows,))] * 2

    def bind(self, given, out, scratch):
        self.full = None if self.inside else given[0]
        self.out = out[0]
        self.came, self.send, self.recv = scratch
        self.me, self.slow, self.fast, self.slows = wide_places(self.count)

    def block(self, step, fast):
        owner = 2 * lax.rem(self.slow + step, self.slows) + fast
        return self.full.at[(slice(None),) * self.lead + (owner,)]

    def copy(self, step):
        return remote(
            self.block(step, 1 - self.fast), self.came.at[step], self.send.at[step], self.recv.at[step],
            {WIDE: self.me + 1 - 2 * self.fast},
        )

    def start(self):
        for step in list(range(1, self.slows)) + [0]:
            self.copy(step).start()

    def finish(self):
        for step in range(self.slows):
            self.copy(step).wait()
            total = self.block(step, self.fast)[...].astype(F32) + self.came[step].astype(F32)
            self.out[step] = total.astype(BF16)


class ReduceLoad(PairLoad):
    ways = (SLOW, FAST)

    def __init__(self, full, lead, inside=False):
        super().__init__(full, lead, inside)
        self.outs = [jax.ShapeDtypeStruct(self.shape, F32), jax.ShapeDtypeStruct((8, 128), F32)]
        self.out_specs = [whole_vmem()] * 2
        self.scratch = (
            self.scratch
            + [pltpu.VMEM((self.slows - 1,) + self.shape, BF16)]
            + [pltpu.SemaphoreType.DMA((self.slows,))] * 2
        )

    def bind(self, given, out, scratch):
        super().bind(given, out[:1], scratch[:3])
        self.squares = out[1]
        self.landed, self.line_send, self.line_recv = scratch[3:]

    def line_copy(self, step):
        return remote(
            self.came.at[step], self.landed.at[step - 1], self.line_send.at[step], self.line_recv.at[step],
            {WIDE: 2 * lax.rem(self.slow + step, self.slows) + self.fast},
        )

    def relay(self):
        for step in list(range(1, self.slows)) + [0]:
            self.copy(step).wait()
            total = self.block(step, self.fast)[...].astype(F32) + self.came[step].astype(F32)
            self.came[step] = total.astype(BF16)
            if step:
                self.line_copy(step).start()

    def finish(self):
        total = self.came[0].astype(F32)
        for step in range(1, self.slows):
            self.line_copy(step).wait()
            total = total + self.landed[step - 1].astype(F32)
        self.out[...] = total
        self.squares[...] = jnp.full(self.squares.shape, jnp.sum(total * total), F32)


class LineLoad:
    ways = (SLOW,)

    def __init__(self, sums, count):
        self.count = count
        slows = count // 2
        self.operands, self.in_specs = [sums], [whole_vmem()]
        self.outs = [jax.ShapeDtypeStruct(sums.shape[1:], F32), jax.ShapeDtypeStruct((8, 128), F32)]
        self.out_specs = [whole_vmem()] * 2
        self.scratch = [pltpu.VMEM(sums.shape, BF16)] + [pltpu.SemaphoreType.DMA((slows,))] * 2

    def bind(self, given, out, scratch):
        self.sums, (self.out, self.squares) = given[0], out
        self.came, self.send, self.recv = scratch
        self.me, self.slow, self.fast, self.slows = wide_places(self.count)

    def copy(self, step):
        return remote(
            self.sums.at[step], self.came.at[step], self.send.at[step], self.recv.at[step],
            {WIDE: 2 * lax.rem(self.slow + step, self.slows) + self.fast},
        )

    def start(self):
        for step in range(1, self.slows):
            self.copy(step).start()

    def finish(self):
        total = self.sums[0].astype(F32)
        for step in range(1, self.slows):
            self.copy(step).wait()
            total = total + self.came[step].astype(F32)
        self.out[...] = total
        self.squares[...] = jnp.full(self.squares.shape, jnp.sum(total * total), F32)


def run(body, name, operands, outs, scratch, collective_id=None, loads=(), away=(), lazy=(), early=()):
    any_place = pl.BlockSpec(memory_space=pl.ANY)
    given, taken = list(operands), []
    in_specs = [any_place if k in away or k in lazy else whole_vmem() for k in range(len(operands))]
    for load in loads:
        places = []
        for operand, spec in zip(load.operands, load.in_specs):
            known = [k for k, other in enumerate(given) if other is operand]
            if not known:
                known = [len(given)]
                given.append(operand)
                in_specs.append(spec)
            places.append(known[0])
        taken.append(places)
    moved = [operands[k] for k in lazy] + [outs[k] for k in early]
    counts = [len(given), len(outs)] + [len(load.outs) for load in loads]
    counts += [len(scratch)] + [len(load.scratch) for load in loads] + [len(moved), len(moved)]
    parts = 1 + len(loads)

    def kernel(*refs):
        groups, place = [], 0
        for count in counts:
            groups.append(refs[place : place + count])
            place += count
        for k, load in enumerate(loads):
            load.bind([groups[0][p] for p in taken[k]], groups[2 + k], groups[2 + parts + k])
        mine, results = list(groups[0][: len(operands)]), list(groups[1])
        fetches, leaves = [], {}
        for k, buffer, sem in zip(lazy, groups[-2], groups[-1]):
            fetches.append(pltpu.make_async_copy(mine[k], buffer, sem))
            mine[k] = buffer
        for k, buffer, sem in zip(early, groups[-2][len(lazy) :], groups[-1][len(lazy) :]):
            leaves[k] = pltpu.make_async_copy(buffer, results[k], sem)
            results[k] = buffer
        body(*mine, *results, *groups[1 + parts], carry=Carry(list(loads), fetches, leaves))

    results = pl.pallas_call(
        kernel,
        out_shape=tuple(outs) + tuple(out for load in loads for out in load.outs),
        in_specs=in_specs,
        out_specs=tuple(any_place if k in early else whole_vmem() for k in range(len(outs)))
        + tuple(spec for load in loads for spec in load.out_specs),
        scratch_shapes=list(scratch)
        + [s for load in loads for s in load.scratch]
        + [pltpu.VMEM(value.shape, value.dtype) for value in moved]
        + [pltpu.SemaphoreType.DMA] * len(moved),
        compiler_params=pltpu.CompilerParams(
            collective_id=collective_id,
            has_side_effects=collective_id is not None,
            vmem_limit_bytes=VMEM_LIMIT,
        ),
        name=name,
    )(*given)
    return results[: len(outs)], results[len(outs) :]


def sems(kinds):
    return [pltpu.SemaphoreType.DMA((kinds, CHUNKS)), pltpu.SemaphoreType.DMA((kinds, CHUNKS))]


def norm_of(value, gain):
    scale = lax.rsqrt(jnp.mean(value * value, axis=-1, keepdims=True) + NORM_EPS)
    return value * scale * gain


def norm_back(grad, value, gain):
    scale = lax.rsqrt(jnp.mean(value * value, axis=-1, keepdims=True) + NORM_EPS)
    unit = value * scale
    scaled = grad * gain
    back = scale * (scaled - unit * jnp.mean(scaled * unit, axis=-1, keepdims=True))
    return (back, jnp.sum(grad * unit, axis=0, keepdims=True))


GELU_A = math.sqrt(2.0 / math.pi)
GELU_B = 0.044715


def gelu_of(x):
    return 0.5 * x * (1.0 + jnp.tanh(GELU_A * (x + GELU_B * (x * x * x))))


def gelu_slope(x):
    square = x * x
    t = jnp.tanh(GELU_A * (x + GELU_B * (x * square)))
    return 0.5 * (1.0 + t) + 0.5 * x * (1.0 - t * t) * (GELU_A * (1.0 + 3.0 * GELU_B * square))


def rows_at(start, j, chunk):
    return pl.ds(pl.multiple_of(start + j * chunk, chunk), chunk)


LANES = 128
SUB = 64


def spread(row):
    return jnp.transpose(jnp.broadcast_to(row, (LANES, LANES)))


def feature_places(owner, width, share):
    lane = lax.broadcasted_iota(jnp.int32, (LANES, width), 0)
    feature = lax.broadcasted_iota(jnp.int32, (LANES, width), 1)
    return ((feature == lane + owner * share) & (lane < share)).astype(F32).astype(BF16)


def token_parts(ids, first):
    here = ids - first
    high = lax.shift_right_arithmetic(here, 7)
    place = lax.broadcasted_iota(jnp.int32, (LANES, ids.shape[1]), 0)
    return high, jnp.where(place == here - high * LANES, 1.0, 0.0).astype(BF16)


def embed_part(
    ids, counted, gains, steps, rates, table,
    resid, normed, gain_all, count_all, ids_all,
    low, extra, small, near_out, near_in, own, far_out, far_in, wide_out, wide_in, part_out, part_in,
    id_send, id_recv, small_send, small_recv, near_send, near_recv, far_send, far_recv, wide_send, wide_recv,
    part_send, part_recv, send, recv, carry,
):
    seq_len, width = normed.shape
    chunk = seq_len // 2 // CHUNKS
    quarter = seq_len // 4
    share, vocab = table.shape[1:]
    owners = ids_all.shape[0]
    sibling, partner, mine, other = group_places(seq_len)
    place = lax.axis_index(NARROW)
    side = lax.div(place, 2)
    me = lax.axis_index(WIDE)
    first = place * vocab
    around = [lax.rem(me + step, owners) for step in range(owners)]

    def id_copy(step):
        return remote(ids_all.at[me], ids_all.at[me], id_send.at[step], id_recv.at[step], {WIDE: around[step]})

    def small_copy(step):
        return remote(small.at[me], small.at[me], small_send.at[step], small_recv.at[step], {WIDE: around[step]})

    def near_copy(step):
        return remote(near_out.at[step], near_in.at[step], near_send.at[step], near_recv.at[step], sibling)

    def far_copy(step):
        return remote(far_out.at[step], far_in.at[step], far_send.at[step], far_recv.at[step], partner)

    def wide_copy(step):
        return remote(wide_out.at[step], wide_in.at[me], wide_send.at[step], wide_recv.at[step], {WIDE: around[step]})

    def part_copy(piece):
        rows = pl.ds(piece * LANES, LANES)
        return remote(part_out.at[rows], part_in.at[rows], part_send.at[piece], part_recv.at[piece], partner)

    ids_all[me] = ids[...]
    small[me] = jnp.zeros(small.shape[1:], F32)
    small[me, : gains.shape[0], : gains.shape[1]] = gains[...].astype(BF16).astype(F32)
    count = jnp.sum(counted[...].astype(F32), keepdims=True)
    small[me, COUNT_ROW : COUNT_ROW + 1, :] = jnp.broadcast_to(count, (1, small.shape[2]))
    greet([{WIDE: device} for device in around[1:]] + [sibling, partner])
    for step in range(1, owners):
        id_copy(step).start()
    for step in range(1, owners):
        small_copy(step).start()
    carry.begin(0, 1)
    parts = vocab // LANES
    for part in range(parts):
        low[part * share : (part + 1) * share, :] = table[0, :, part * LANES : (part + 1) * LANES].astype(BF16)
    core = lax.rem(place, 2)

    def look_up(step):
        row = lax.rem(me + step, owners)

        def find(which):
            high, picks = token_parts(ids_all[row, pl.ds(which, 1), :], first)
            found = dot_nn(low[...], picks)
            total = jnp.zeros((share, quarter), F32)
            for part in range(parts):
                total = total + jnp.where(high == part, found[part * share : (part + 1) * share, :], 0.0)
            return total.astype(BF16)

        for k in range(2):
            near_out[step, k] = find(2 * (1 - core) + k)
        near_copy(step).start()
        for k in range(2):
            own[step, k] = find(2 * core + k)

    def halve(step):
        near_copy(step).wait_recv()
        own[step] = own[step] + near_in[step]
        far_out[step] = own[step, 1 - side]
        far_copy(step).start()

    def deliver(step):
        far_copy(step).wait_recv()
        total = own[step, side] + far_in[step]
        if step % owners == 0:
            wide_in[me] = total
        else:
            wide_out[step] = total
            wide_copy(step).start()

    order = list(range(1, owners)) + [0]
    for turn in range(owners + 2):
        if turn < owners:
            if order[turn]:
                id_copy(owners - order[turn]).wait_recv()
            look_up(order[turn])
        if 1 <= turn < owners + 1:
            halve(order[turn - 1])
        if turn >= 2:
            deliver(order[turn - 2])
    carry.begin(2, 3)
    carry.hand_on(0, 1)
    for step in range(1, owners):
        small_copy(step).wait_recv()
    total = None
    for owner in range(owners):
        part = dot_nn(small[owner].astype(BF16), feature_places(owner, width, share))
        total = part if total is None else total + part
    gain_all[...] = total
    count_all[...] = jnp.sum(small[...], axis=0)
    half_width = width // 2
    for k in range(seq_len // 2 // LANES):
        when = spread(steps[pl.ds(mine // LANES + k, 1), :].astype(F32))
        for t in range(half_width // LANES):
            columns = slice(t * LANES, (t + 1) * LANES)
            angles = when * rates[:, columns]
            rows = slice(k * LANES, (k + 1) * LANES)
            extra[rows, t * LANES : (t + 1) * LANES] = jnp.sin(angles)
            extra[rows, half_width + t * LANES : half_width + (t + 1) * LANES] = jnp.cos(angles)
    for step in range(1, owners):
        wide_copy(step).wait_recv()
    found = jnp.transpose(wide_in[...].reshape(width, quarter))
    pieces = quarter // LANES
    at_side = pl.multiple_of(side * quarter, quarter)
    at_other = pl.multiple_of((1 - side) * quarter, quarter)
    for piece in range(pieces):
        rows = pl.ds(piece * LANES, LANES)
        part_out[rows, :] = found[piece * LANES : (piece + 1) * LANES, :]
        part_copy(piece).start()

    def finish(start, source, piece):
        rows = rows_at(start, piece, LANES)
        x = math.sqrt(width) * source[pl.ds(piece * LANES, LANES), :].astype(F32) + extra[rows, :]
        resid[rows, :] = x
        here = rows_at(mine + start, piece, LANES)
        normed[here, :] = norm_of(x, gain_all[0:1, :]).astype(BF16)
        give_rows(here, piece if source is part_out else pieces + piece).start()

    def give_rows(here, k):
        return remote(normed.at[here], normed.at[here], send.at[0, k], recv.at[0, k], sibling)

    for piece in range(pieces):
        finish(at_side, part_out, piece)
    for piece in range(pieces):
        part_copy(piece).wait_recv()
        finish(at_other, part_in, piece)
    carry.hand_on(2)
    for k in range(2 * pieces):
        give_rows(rows_at(mine, k % pieces, LANES), k).wait()
    for step in range(owners):
        near_copy(step).wait_send()
        far_copy(step).wait_send()
        if step:
            id_copy(step).wait_send()
            small_copy(step).wait_send()
            wide_copy(step).wait_send()
    for piece in range(pieces):
        part_copy(piece).wait_send()


QUERY_BLOCK = 256


def forward_part(
    layer, weights, points, normed, key_seg, query_seg, resid, gains,
    projected, mixed, middle, normed_two, log_sums, result, normed_next,
    bias, values_t, near_out, near_in, far_out, far_in, near_out2, near_in2, far_out2, far_in2, send, recv,
):
    w_query, w_out, w_in, w_red = weights
    at_half, at_feed, at_sent, at_last = points
    seq_len, width = normed.shape
    chunk = seq_len // 2 // CHUNKS
    block = bias.shape[1]
    heads = mixed.shape[1] // HD
    sibling, partner, mine, other = group_places(seq_len)
    pair = (send, recv)
    first = Exchange((near_out, near_in, far_out, far_in), pair, 0, sibling, partner)
    second = Exchange((near_out2, near_in2, far_out2, far_in2), pair, 2, sibling, partner)
    share = Share(normed_two, pair, 4, sibling, mine, chunk)
    share_next = Share(normed_next, pair, 5, sibling, mine, chunk)

    def ask(i, _):
        rows = rows_at(0, i, block)
        for which in range(3):
            projected[which, rows, :] = dot_nn(normed[rows, :], w_query(which)).astype(BF16)
        return 0

    lax.fori_loop(0, seq_len // block, ask, 0)
    values_t[...] = jnp.transpose(projected[2])

    def attend_rows(start):
        rows = pl.ds(pl.multiple_of(start, block), block)
        bias[...] = jnp.where(key_seg[...] == query_seg[:, rows], 0.0, -1e30)
        asked = projected[0, rows, :] * HD ** (-0.5)
        parts = []
        for head in range(heads):
            scores = dot_nt(projected[1], head_lanes(asked, head, HD)) + bias[...]
            top = jnp.max(scores, axis=0, keepdims=True)
            powers = jnp.exp(scores - top)
            total = jnp.sum(powers, axis=0, keepdims=True)
            log_sums[head : head + 1, rows] = top + jnp.log(total)
            probs = (powers * (1.0 / total)).astype(BF16)
            parts.append(dot_nn(values_t[head * HD : (head + 1) * HD, :], probs))
        mixed[rows, :] = jnp.transpose(jnp.concatenate(parts, axis=0)).astype(BF16)

    def project(start, k):
        return dot_nt(mixed[rows_at(start, k, SPAN * chunk), :], w_out())

    def feed(rows):
        pre = dot_nn(normed_two[rows, :], w_in())
        return dot_nt(gelu_of(pre).astype(BF16), w_red())

    for part in range(CHUNKS // SPAN):

        def both(i, _):
            attend_rows(jnp.where(i == 0, other, mine) + part * block)
            return 0

        lax.fori_loop(0, 2, both, 0)
        first.give_span(part, project(other, part))
        if part == 0:
            at_half()
        first.pass_on_span(part, project(mine, part))
    at_feed()
    for k in range(CHUNKS // SPAN):
        for j in range(SPAN * k, SPAN * (k + 1)):
            rows = rows_at(0, j, chunk)
            mid = resid[rows, :] + first.take(j)
            middle[rows, :] = mid
            share.put(j, norm_of(mid, gains[2 * layer + 1 : 2 * layer + 2, :]).astype(BF16))
        kept = feed(rows_at(mine, k, SPAN * chunk))
        for j in range(SPAN * k, SPAN * (k + 1)):
            share.arrived(j)
        second.give_span(k, feed(rows_at(other, k, SPAN * chunk)))
        second.pass_on_span(k, kept)
    at_sent()
    for j in range(CHUNKS):
        rows = rows_at(0, j, chunk)
        x = middle[rows, :] + second.take(j)
        result[rows, :] = x
        share_next.put(j, norm_of(x, gains[2 * layer + 2 : 2 * layer + 3, :]).astype(BF16))
        if j == CHUNKS - 2:
            at_last()
    for j in range(CHUNKS):
        share_next.arrived(j)
    for part in (first, second, share, share_next):
        part.close()


def layer_outs(seq_len, width, heads_width):
    return [
        jax.ShapeDtypeStruct((3, seq_len, heads_width), BF16),
        jax.ShapeDtypeStruct((seq_len, heads_width), BF16),
        jax.ShapeDtypeStruct((seq_len // 2, width), F32),
        jax.ShapeDtypeStruct((seq_len, width), BF16),
        jax.ShapeDtypeStruct((8, seq_len), F32),
    ]


def layer_scratch(seq_len, width, heads_width):
    half, chunk = seq_len // 2, seq_len // 2 // CHUNKS
    block = SPAN * chunk
    return (
        [pltpu.VMEM((seq_len, block), F32), pltpu.VMEM((heads_width, seq_len), BF16)]
        + Exchange.scratch(chunk, width, FORWARD_KIND)
        + Exchange.scratch(chunk, width, FORWARD_KIND)
        + sems(6)
    )


LAYER_SCRATCH = 12
COUNT_ROW = 5


def front_kernel(
    ids, counted, gains, steps, rates, table, key_seg, query_seg,
    resid, normed, gain_all, count_all, ids_all, projected, mixed, middle, normed_two, log_sums, result, normed_next,
    *scratch, carry,
):
    embed_part(
        ids, counted, gains, steps, rates, table, resid, normed, gain_all, count_all, ids_all,
        *scratch[:-LAYER_SCRATCH], carry,
    )
    carry.end(0, 1)
    later = list(carry.all())[4:]

    def at_half():
        carry.hand_on(3)
        carry.begin(*later[:2])

    def at_feed():
        carry.end(2, 3)
        carry.begin(*later[2:])
        carry.leave(0, 1, 5, 6)

    def at_sent():
        carry.hand_on(*later[:2])
        carry.leave(7, 8)

    forward_part(
        0,
        [carry.loads[0].value] + [load.value for load in carry.loads[1:4]],
        (at_half, at_feed, at_sent, lambda: carry.hand_on(*later[2:3])),
        normed, key_seg, query_seg, resid, gain_all,
        projected, mixed, middle, normed_two, log_sums, result, normed_next, *scratch[-LAYER_SCRATCH:],
    )
    carry.end(*later)
    carry.gone()


def front(ids, counted, gains, steps, rates, tables, key_seg, query_seg, owners, heads_width, collective_id, loads):
    seq_len = ids.size
    share, vocab = tables.shape[1:]
    half, width = seq_len // 2, owners * share
    dma = pltpu.SemaphoreType.DMA
    return run(
        front_kernel,
        "front",
        [ids, counted, gains, steps, rates, tables, key_seg, query_seg],
        [
            jax.ShapeDtypeStruct((half, width), F32),
            jax.ShapeDtypeStruct((seq_len, width), BF16),
            jax.ShapeDtypeStruct((8, width), F32),
            jax.ShapeDtypeStruct((8, LANES), F32),
            jax.ShapeDtypeStruct((owners,) + ids.shape, jnp.int32),
        ]
        + layer_outs(seq_len, width, heads_width)
        + [jax.ShapeDtypeStruct((half, width), F32), jax.ShapeDtypeStruct((seq_len, width), BF16)],
        [
            pltpu.VMEM((vocab // LANES * share, LANES), BF16),
            pltpu.VMEM((half, width), F32),
            pltpu.VMEM((owners, 8, LANES), F32),
        ]
        + [pltpu.VMEM((owners, 2, share, half // 2), BF16)] * 3
        + [pltpu.VMEM((owners, share, half // 2), BF16)] * 4
        + [
            pltpu.VMEM((half // 2, width), BF16),
            pltpu.VMEM((half // 2, width), BF16),
        ]
        + [dma((owners,))] * 10
        + [dma((half // 2 // LANES,))] * 2
        + [dma((1, half // LANES))] * 2
        + layer_scratch(seq_len, width, heads_width),
        collective_id,
        loads,
        early=(0, 1, 5, 6, 7, 8),
    )


TILE = 256


def weight_grad(left_t, right, out):
    columns = right.shape[1]
    tile = TILE if columns % TILE == 0 else columns

    def put(where):
        value = dot_nn(left_t[...], right[:, where]).astype(out.dtype)
        if len(out.shape) == 3:
            out[:, :, where] = value.reshape(out.shape[:2] + (tile,))
        else:
            out[:, where] = value

    def step(i, _):
        put(pl.ds(pl.multiple_of(i * tile, tile), tile))
        return 0

    if tile == columns:
        put(slice(None))
    else:
        lax.fori_loop(0, columns // tile, step, 0)


def head_lanes(value, head, size):
    lanes = lax.broadcasted_iota(jnp.int32, value.shape, 1)
    inside = (lanes >= head * size) & (lanes < (head + 1) * size)
    return jnp.where(inside, value, jnp.zeros_like(value))


def backward_kernel(
    layer, scale, points, grad, branch, w_red, w_in, w_out, normed_two, middle, gains, mixed,
    projected, log_sums, key_seg, query_seg, w_query, resid, normed,
    grad_out, branch_out, d_out, d_query, gain_two, gain_one,
    d_red, d_in, grad_middle, grad_attn, grad_mixed, grad_projected, grad_before, after, turned,
    bias, keys_t, grad_keys, grad_values,
    near_out, near_in, far_out, far_in, far_out2, far_in2, send, recv, loaded, carry,
):
    at_start, at_made, at_summed, at_attended, at_sent = points
    seq_len, width = normed_two.shape
    chunk = seq_len // 2 // CHUNKS
    sibling, partner, mine, other = group_places(seq_len)
    carry.fetch()
    greet([sibling, partner] + carry.peers())
    at_start(carry, d_red, d_in)
    pair = (send, recv)
    trade = Exchange((near_out, near_in, far_out, far_in), pair, 0, sibling, partner)
    share = Share(grad_attn, pair, 2, sibling, mine, chunk)

    def ffn_partial(start, k):
        rows = rows_at(start, k, SPAN * chunk)
        pre = dot_nn(normed_two[rows, :], w_in[...])
        after[rows, :] = gelu_of(pre).astype(BF16)
        low = (dot_nn(branch[rows, :], w_red[...]) * gelu_slope(pre)).astype(BF16)
        grad_before[rows, :] = low
        return dot_nt(low, w_in[...])

    for k in range(CHUNKS // SPAN):
        trade.give_span(k, ffn_partial(other, k))
        trade.pass_on_span(k, ffn_partial(mine, k))
    turned[...] = jnp.transpose(branch[...])
    weight_grad(turned, after, d_red)
    turned[...] = jnp.transpose(normed_two[...])
    weight_grad(turned, grad_before, d_in)
    at_made(carry)
    fetch = pltpu.make_async_copy(normed, after, loaded)
    fetch.start()
    carry.fetched()
    total = jnp.zeros((1, width), F32)
    for j in range(CHUNKS):
        rows = rows_at(0, j, chunk)
        back, part = norm_back(trade.take(j), middle[rows, :], gains[2 * layer + 1 : 2 * layer + 2, :])
        total = total + part
        back = back + grad[rows, :]
        grad_middle[rows, :] = back
        share.put(j, back.astype(BF16))
        here = rows_at(mine, j, chunk)
        grad_mixed[here, :] = dot_nn(grad_attn[here, :], w_out[...]).astype(BF16)
    gain_two[...] = total
    for j in range(CHUNKS):
        share.arrived(j)
        here = rows_at(other, j, chunk)
        grad_mixed[here, :] = dot_nn(grad_attn[here, :], w_out[...]).astype(BF16)
    trade.close()
    share.close()
    at_summed(carry)

    block = bias.shape[1]
    heads = grad_mixed.shape[1] // HD
    keys_t[...] = jnp.transpose(projected[1])
    grad_keys[...] = jnp.zeros(grad_keys.shape, F32)
    grad_values[...] = jnp.zeros(grad_values.shape, F32)

    def queries(i, _):
        rows = rows_at(0, i, block)
        bias[...] = jnp.where(key_seg[...] == query_seg[:, rows], 0.0, -1e30)
        asked = projected[0, rows, :] * HD ** (-0.5)
        given = grad_mixed[rows, :]
        parts = []
        for head in range(heads):
            query = head_lanes(asked, head, HD)
            wanted = head_lanes(given, head, HD)
            scores = dot_nt(projected[1], query) + bias[...]
            probs = jnp.exp(scores - log_sums[head : head + 1, rows])
            grad_probs = dot_nt(projected[2], wanted)
            centre = jnp.sum(probs * grad_probs, axis=0, keepdims=True)
            grad_scores = (probs * (grad_probs - centre)).astype(BF16)
            parts.append(dot_nn(keys_t[head * HD : (head + 1) * HD, :], grad_scores))
            grad_keys[...] += dot_nn(grad_scores, query)
            grad_values[...] += dot_nn(probs.astype(BF16), wanted)
        grad_projected[0, rows, :] = (jnp.transpose(jnp.concatenate(parts, axis=0)) * HD ** (-0.5)).astype(BF16)
        return 0

    lax.fori_loop(0, seq_len // block, queries, 0)
    grad_projected[1] = grad_keys[...].astype(BF16)
    grad_projected[2] = grad_values[...].astype(BF16)
    at_attended(carry)

    trade = Exchange((near_out, near_in, far_out2, far_in2), pair, 3, sibling, partner)
    share = Share(branch_out, pair, 5, sibling, mine, chunk)

    def query_partial(start, k):
        rows = rows_at(start, k, SPAN * chunk)
        found = None
        for which in range(3):
            part = dot_nt(grad_projected[which, rows, :], w_query[which])
            found = part if found is None else found + part
        return found

    for k in range(CHUNKS // SPAN):
        trade.give_span(k, query_partial(other, k))
        trade.pass_on_span(k, query_partial(mine, k))
    turned[...] = jnp.transpose(grad_attn[...])
    weight_grad(turned, mixed, d_out)
    fetch.wait()
    turned[...] = jnp.transpose(after[...])
    for which in range(3):
        weight_grad(turned, grad_projected.at[which], d_query.at[which])
    at_sent(carry, d_out, d_query)
    total = jnp.zeros((1, width), F32)
    for j in range(CHUNKS):
        rows = rows_at(0, j, chunk)
        back, part = norm_back(trade.take(j), resid[rows, :], gains[2 * layer : 2 * layer + 1, :])
        total = total + part
        back = back + grad_middle[rows, :]
        grad_out[rows, :] = back
        share.put(j, (back if scale is None else scale * back).astype(BF16))
    gain_one[...] = total
    for j in range(CHUNKS):
        share.arrived(j)
    trade.close()
    share.close()
    carry.end(*carry.all())


def backward_block(
    layer, scale, points, grad, branch, w_red, w_in, w_out, normed_two, middle, gains, mixed,
    projected, log_sums, key_seg, query_seg, w_query, resid, normed, owners, collective_id, loads,
):
    seq_len, width = normed_two.shape
    hidden, heads_width = w_in.shape[1], w_query.shape[2]
    half, chunk = seq_len // 2, seq_len // 2 // CHUNKS
    block = min(QUERY_BLOCK, seq_len)
    far = pltpu.VMEM((CHUNKS, chunk, width), BACKWARD_KIND)
    return run(
        functools.partial(backward_kernel, layer, scale, points),
        "backward_block",
        [grad, branch, w_red, w_in, w_out, normed_two, middle, gains, mixed]
        + [projected, log_sums, key_seg, query_seg, w_query, resid, normed],
        [
            jax.ShapeDtypeStruct((half, width), F32),
            jax.ShapeDtypeStruct((seq_len, width), BF16),
            jax.ShapeDtypeStruct((owners, width // owners, heads_width), BF16),
            jax.ShapeDtypeStruct((3, owners, width // owners, heads_width), BF16),
            jax.ShapeDtypeStruct((1, width), F32),
            jax.ShapeDtypeStruct((1, width), F32),
        ],
        [pltpu.VMEM((owners, width // owners, hidden), BF16)] * 2
        + [
            pltpu.VMEM((half, width), F32),
            pltpu.VMEM((seq_len, width), BF16),
            pltpu.VMEM((seq_len, heads_width), BF16),
            pltpu.VMEM((3, seq_len, heads_width), BF16),
            pltpu.VMEM((seq_len, hidden), BF16),
            pltpu.VMEM((seq_len, width), BF16),
            pltpu.VMEM((width, seq_len), BF16),
            pltpu.VMEM((seq_len, block), F32),
            pltpu.VMEM((heads_width, seq_len), BF16),
            pltpu.VMEM((seq_len, heads_width), F32),
            pltpu.VMEM((seq_len, heads_width), F32),
        ]
        + Exchange.scratch(chunk, width, BACKWARD_KIND)
        + [far, far]
        + sems(6)
        + [pltpu.SemaphoreType.DMA],
        collective_id,
        loads,
        away=(15,),
        lazy=(0, 4, 6, 8, 9, 11, 13, 14),
    )


def to_rows(columns):
    lanes = lax.broadcasted_iota(jnp.int32, (LANES, LANES), 1)
    total = jnp.zeros((LANES, LANES), F32)
    for k, column in enumerate(columns):
        total = jnp.where(lanes == k, column, total)
    return jnp.transpose(total)[:8, :]


def loss_part(
    row, normed, info, value, gain, table_loads, grad_out, branch, d_gain, losses, d_tables,
    logits, grads, places, turned, stat_out, stat_in, sum_out, sum_in,
    stat_send, stat_recv, sum_send, sum_recv, near_out, near_in, far_out, far_in, send, recv, made,
):
    seq_len, width = normed.shape
    chunk = seq_len // 2 // CHUNKS
    piece_width = table_loads[0].out.shape[-1]
    vocab = piece_width * len(table_loads)
    tiles = vocab // LANES
    blocks = seq_len // LANES
    me = lax.axis_index(NARROW)
    sibling, partner, mine, other = group_places(seq_len)
    peers = [{NARROW: lax.rem(me + k, 4)} for k in range(1, 4)]
    sems = (send, recv)
    trade = Exchange((near_out, near_in, far_out, far_in), sems, 0, sibling, partner)
    share = Share(branch, sems, 2, sibling, mine, chunk)
    first = (me * vocab).astype(F32)
    whole = 4.0 * vocab
    lanes = lax.broadcasted_iota(jnp.int32, (LANES, LANES), 1).astype(F32)

    def stat_copy(b, k):
        return remote(stat_out.at[b], stat_in.at[k, b], stat_send.at[k, b], stat_recv.at[k, b], peers[k])

    def sum_copy(b, k):
        return remote(sum_out.at[b], sum_in.at[k, b], sum_send.at[k, b], sum_recv.at[k, b], peers[k])

    def tile_at(t):
        return pl.ds(pl.multiple_of(t * LANES, LANES), LANES)

    def ask(b, _):
        rows = rows_at(0, b, LANES)
        here = info[:, rows]
        at_noised = spread(here[0:1] - first)
        at_clean = spread(here[1:2] - first)
        places[b, 0] = at_noised
        places[b, 1] = at_clean

        tops, sums = [], [[], [], []]
        for k in range(LANES // SUB):
            part = pl.ds(pl.multiple_of(b * LANES + k * SUB, SUB), SUB)
            subset = slice(k * SUB, (k + 1) * SUB)

            def top_step(t, top):
                return jnp.maximum(top, logits[part, tile_at(t)])

            top = lax.fori_loop(1, tiles, top_step, logits[part, tile_at(0)], unroll=5)
            top = jnp.max(top, axis=1, keepdims=True)
            top_wide = jnp.broadcast_to(top, (SUB, LANES))
            noised_at, clean_at = at_noised[subset], at_clean[subset]

            def sum_step(t, totals):
                powers, noised, clean = totals
                piece = logits[part, tile_at(t)]
                column = lanes[subset] + (t * LANES).astype(F32)
                return (
                    powers + jnp.exp(piece - top_wide),
                    noised + jnp.where(column == noised_at, piece, 0.0),
                    clean + jnp.where(column == clean_at, piece, 0.0),
                )

            zero = jnp.zeros((SUB, LANES), F32)
            totals = lax.fori_loop(0, tiles, sum_step, (zero, zero, zero), unroll=4)
            tops.append(top)
            for found, total in zip(sums, totals):
                found.append(jnp.sum(total, axis=1, keepdims=True))
        stat_out[b] = to_rows([jnp.concatenate(found, axis=0) for found in [tops] + sums])
        for k in range(3):
            stat_copy(b, k).start()
        return 0

    for k, table in enumerate(table_loads):
        if k == len(table_loads) - 1:
            table.finish()

        def product(i, _):
            rows = rows_at(0, i, TILE)
            logits[rows, k * piece_width : (k + 1) * piece_width] = dot_nn(normed[rows, :], table.value())
            return 0

        lax.fori_loop(0, seq_len // TILE, product, 0)
    lax.fori_loop(0, blocks, ask, 0)

    def scalars(b):
        here = info[:, rows_at(0, b, LANES)]
        step = jnp.maximum(here[2:3], 2.0)
        left = STEPS - step + 1.0
        beta = 1.0 / left
        keep = left / STEPS
        rest = (step - 1.0) / (STEPS * whole)
        own = stat_out[b]
        others = [stat_in[k, b] for k in range(3)]
        top = own[0:1]
        for stat in others:
            top = jnp.maximum(top, stat[0:1])
        total = own[1:2] * jnp.exp(own[0:1] - top)
        noised, clean = own[2:3], own[3:4]
        for stat in others:
            total = total + stat[1:2] * jnp.exp(stat[0:1] - top)
            noised, clean = noised + stat[2:3], clean + stat[3:4]
        return here, beta, keep, rest, top + jnp.log(total), noised, clean

    def measure(b, _):
        rows = rows_at(0, b, LANES)
        for k in range(3):
            stat_copy(b, k).wait_recv()
        _, _, keep, rest, log_total, _, _ = scalars(b)
        log_wide = spread(log_total)
        ratio = spread(keep / rest)

        sums = [[], []]
        for k in range(LANES // SUB):
            part = pl.ds(pl.multiple_of(b * LANES + k * SUB, SUB), SUB)
            log_part, ratio_part = log_wide[k * SUB : (k + 1) * SUB], ratio[k * SUB : (k + 1) * SUB]

            def step(t, totals):
                logs, shares = totals
                probs = jnp.exp(logits[part, tile_at(t)] - log_part)
                logits[part, tile_at(t)] = probs
                grown = 1.0 + probs * ratio_part
                return (logs + jnp.log(grown), shares + probs / grown)

            zero = jnp.zeros((SUB, LANES), F32)
            totals = lax.fori_loop(0, tiles, step, (zero, zero), unroll=4)
            for found, total in zip(sums, totals):
                found.append(jnp.sum(total, axis=1, keepdims=True))
        sum_out[b] = to_rows([jnp.concatenate(found, axis=0) for found in sums])
        for k in range(3):
            sum_copy(b, k).start()
        return 0

    lax.fori_loop(0, blocks, measure, 0)

    def pull(b):
        rows = rows_at(0, b, LANES)
        for k in range(3):
            sum_copy(b, k).wait_recv()
        here, beta, keep, rest, log_total, noised, clean = scalars(b)
        sums = sum_out[b] + sum_in[0, b] + sum_in[1, b] + sum_in[2, b]
        log_sum, share_sum = sums[0:1], sums[1:2] / rest
        same = here[0:1] == here[1:2]
        first_step = here[2:3] == 1.0
        base_a, more_a = beta / whole, 1.0 - beta
        base_w = base_a * rest
        joint = whole * base_w + more_a * rest + base_a * keep + jnp.where(same, more_a * keep, 0.0)
        ratio = keep / rest
        prob_n, prob_c = jnp.exp(noised - log_total), jnp.exp(clean - log_total)
        grown_n, grown_c = 1.0 + prob_n * ratio, 1.0 + prob_c * ratio
        marginal_n, marginal_c = rest * grown_n, rest * grown_c
        log_n, log_c = jnp.log(grown_n), jnp.log(grown_c)
        weight_n = jnp.where(same, 0.0, more_a * rest)
        weight_c = jnp.where(same, more_a * rest + base_a * keep + more_a * keep, base_a * keep)
        lift = jnp.log((keep + rest) / rest)
        cross = -base_w * log_sum - weight_n * log_n - weight_c * log_c + (base_w + weight_c) * lift
        model = base_a * (keep + whole * rest) + more_a * marginal_n
        divergence = cross / joint - jnp.log(joint) + jnp.log(model)
        loss = jnp.where(first_step, log_total - clean, divergence)
        losses[:, rows] = here[4:5] * loss
        weighted = base_w * share_sum + weight_n * prob_n / marginal_n + weight_c * prob_c / marginal_c
        aligned = base_a + more_a * prob_n
        centre = keep * (aligned / model - weighted / joint)
        scale = here[3:4]
        zero = jnp.zeros_like(scale)
        even = scale * jnp.where(first_step, 1.0, keep * base_a / model - centre)
        bent = scale * jnp.where(first_step, zero, -keep * base_w / joint / rest)
        at_n = prob_n * keep * (more_a / model - weight_n / joint / marginal_n)
        at_c = -prob_c * keep * (weight_c / joint / marginal_c)
        extra_n = spread(scale * jnp.where(first_step, zero, at_n))
        extra_c = spread(scale * jnp.where(first_step, -1.0, at_c))
        even, bent, ratio = spread(even), spread(bent), spread(ratio)
        at_noised, at_clean = places[b, 0], places[b, 1]

        for k in range(LANES // SUB):
            part = pl.ds(pl.multiple_of(b * LANES + k * SUB, SUB), SUB)
            subset = slice(k * SUB, (k + 1) * SUB)
            even_at, bent_at, ratio_at = even[subset], bent[subset], ratio[subset]
            n_at, c_at, noised_at, clean_at = extra_n[subset], extra_c[subset], at_noised[subset], at_clean[subset]

            def step(t, _):
                probs = logits[part, tile_at(t)]
                column = lanes[subset] + (t * LANES).astype(F32)
                grad = probs * (even_at + bent_at / (1.0 + probs * ratio_at))
                grad = grad + jnp.where(column == noised_at, n_at, 0.0)
                grad = grad + jnp.where(column == clean_at, c_at, 0.0)
                grads[part, tile_at(t)] = grad.astype(BF16)
                return 0

            lax.fori_loop(0, tiles, step, 0, unroll=4)

    def partial(start, k):
        span = SPAN * chunk
        base = start // LANES + k * (span // LANES)
        for b in range(span // LANES):
            pull(base + b)
        total = None
        for k_table, table in enumerate(table_loads):
            part = dot_nt(
                grads[rows_at(start, k, span), k_table * piece_width : (k_table + 1) * piece_width], table.value()
            )
            total = part if total is None else total + part
        return total

    for k in range(CHUNKS // SPAN):
        trade.give_span(k, partial(other, k))
        trade.pass_on_span(k, partial(mine, k))
    turned[...] = jnp.transpose(normed[...])
    for k, d_table in enumerate(d_tables):
        weight_grad(turned, grads.at[:, k * piece_width : (k + 1) * piece_width], d_table)
        made(k)
    gain_total = jnp.zeros((1, gain.shape[1]), F32)
    for j in range(CHUNKS):
        rows = rows_at(0, j, chunk)
        back, gain_part = norm_back(trade.take(j), value[rows, :], gain[row : row + 1, :])
        gain_total = gain_total + gain_part
        grad_out[rows, :] = back
        share.put(j, back.astype(BF16))
    d_gain[...] = gain_total
    for j in range(CHUNKS):
        share.arrived(j)
    trade.close()
    share.close()

    def finish(b, _):
        for k in range(3):
            stat_copy(b, k).wait_send()
            sum_copy(b, k).wait_send()
        return 0

    lax.fori_loop(0, blocks, finish, 0)


def back_kernel(
    layer, pieces, normed, key_seg, query_seg, resid, w_query, w_out, w_in, gains, noised, clean, steps, counted, counts,
    projected, mixed, middle, normed_two, log_sums, grad_out, branch, d_gain, losses, *refs, carry,
):
    outs = 2 * pieces - (len(carry.loads) - 1)
    d_tables, refs = refs[:outs], refs[outs:]
    d_tables, refs = refs[: pieces - outs] + d_tables, refs[pieces - outs :]
    starting = range(pieces + 1, len(carry.loads))
    for k in starting:
        carry.loads[k].full = d_tables[k - pieces - 1]
    (result, normed_next, info), refs = refs[:3], refs[3:]
    loss_scratch, layer_refs = refs[:-LAYER_SCRATCH], refs[-LAYER_SCRATCH:]
    me = lax.axis_index(NARROW)
    carry.fetch()
    info[...] = jnp.zeros(info.shape, F32)
    mask = counted[...].astype(F32)
    for row, value in enumerate((noised[...], clean[...], steps[...])):
        info[row : row + 1, :] = value.astype(F32)
    info[3:4, :] = mask / counts[COUNT_ROW : COUNT_ROW + 1, 0:1]
    info[4:5, :] = mask
    greet([{NARROW: lax.rem(me + k, 4)} for k in range(1, 4)] + carry.peers())
    carry.begin(0, 1)

    def at_half():
        carry.begin(2)

    def at_feed():
        carry.fetched()
        carry.end(0)
        carry.hand_on(1)
        carry.begin(3)

    def at_sent():
        carry.leave(0, 1, 2, 3)
        carry.hand_on(2)
        carry.begin(4)

    def at_last():
        carry.hand_on(3)

    def made(piece):
        if piece == pieces - outs - 1:
            carry.begin(*starting)
        if piece == pieces - 1:
            carry.leave(*range(9, 9 + outs))

    forward_part(
        layer,
        [lambda which: w_query[which], lambda: w_out[...], lambda: w_in[...], carry.loads[0].value],
        (at_half, at_feed, at_sent, at_last),
        normed, key_seg, query_seg, resid, gains,
        projected, mixed, middle, normed_two, log_sums, result, normed_next, *layer_refs,
    )
    carry.hand_on(4)
    carry.end(1, 2, 3)
    loss_part(
        2 * layer + 2, normed_next, info, result, gains, carry.loads[1 : pieces + 1], grad_out, branch, d_gain, losses, d_tables,
        *loss_scratch, *layer_refs[2:6], *layer_refs[-2:], made=made,
    )
    carry.end(*starting)
    carry.gone()


def last_and_loss(
    layer, normed, key_seg, query_seg, resid, w_query, w_out, w_in, gains, tokens, counts, vocab, pieces, collective_id, loads
):
    seq_len, width = normed.shape
    heads_width = w_query.shape[2]
    half, blocks = seq_len // 2, seq_len // LANES
    outs = 2 * pieces - (len(loads) - 1)
    owners = loads[1].count
    table = (owners, width // owners, vocab // pieces)
    return run(
        functools.partial(back_kernel, layer, pieces),
        "last_and_loss",
        [normed, key_seg, query_seg, resid, w_query, w_out, w_in, gains, *tokens, counts],
        layer_outs(seq_len, width, heads_width)
        + [
            jax.ShapeDtypeStruct((half, width), F32),
            jax.ShapeDtypeStruct((seq_len, width), BF16),
            jax.ShapeDtypeStruct((1, width), F32),
            jax.ShapeDtypeStruct((1, seq_len), F32),
        ]
        + [jax.ShapeDtypeStruct(table, BF16)] * outs,
        [pltpu.VMEM(table, BF16)] * (pieces - outs)
        + [
            pltpu.VMEM((half, width), F32),
            pltpu.VMEM((seq_len, width), BF16),
            pltpu.VMEM((8, seq_len), F32),
            pltpu.VMEM((seq_len, vocab), F32),
            pltpu.VMEM((seq_len, vocab), BF16),
            pltpu.VMEM((blocks, 2, LANES, LANES), F32),
            pltpu.VMEM((width, seq_len), BF16),
            pltpu.VMEM((blocks, 8, LANES), F32),
            pltpu.VMEM((3, blocks, 8, LANES), F32),
            pltpu.VMEM((blocks, 8, LANES), F32),
            pltpu.VMEM((3, blocks, 8, LANES), F32),
        ]
        + [pltpu.SemaphoreType.DMA((3, blocks))] * 4
        + layer_scratch(seq_len, width, heads_width),
        collective_id,
        loads,
        lazy=(3, 6),
        early=(0, 1, 2, 3) + tuple(range(9, 9 + outs)),
    )


def sum_ways(place, me, slow, fast, slows, group):
    near = [{NARROW: lax.rem(place + step, group)} for step in range(1, group)]
    return near, {WIDE: me + 1 - 2 * fast}


def tail_kernel(
    layers, branch, ids_all, losses, *refs, carry,
):
    gain_parts, refs = refs[: 2 * layers + 1], refs[2 * layers + 1 :]
    squares, refs = refs[: len(refs) - 25], refs[len(refs) - 25 :]
    tail_body(branch, ids_all, losses, gain_parts, squares, *refs, carry)


def tail_body(
    branch, ids_all, losses, gain_parts, squares,
    d_table, d_small, scalars,
    out_blocks, all_in, masked, picks, total, gains_out, gains_in, blocks, block_in, line_out, line_in,
    near, along,
    wide_send, wide_recv, far_send, far_recv, near_send, near_recv, all_send, all_recv,
    sum_sems,
    carry,
):
    seq_len, width = branch.shape
    quarter, half = seq_len // 4, seq_len // 2
    owners = ids_all.shape[0]
    share, vocab = d_table.shape
    sibling, partner, mine, other = group_places(seq_len)
    place = lax.axis_index(NARROW)
    side = lax.div(place, 2)
    me, slow, fast, slows = wide_places(owners)
    beside = {WIDE: me + 1 - 2 * fast}
    group = near.shape[0]
    first = place * vocab
    around = [lax.rem(me + step, owners) for step in range(owners)]
    at_quarter = pl.multiple_of(mine + side * quarter, quarter)
    held = 2 * lax.rem(place, 2) + side

    def along_way(step):
        return {WIDE: 2 * lax.rem(slow + step, slows) + fast}

    def wide_copy(step):
        return remote(
            out_blocks.at[around[step]], all_in.at[me, held],
            wide_send.at[step], wide_recv.at[step], {WIDE: around[step]},
        )

    def far_copy(step):
        rows = all_in.at[around[step], held]
        return remote(rows, rows, far_send.at[step], far_recv.at[step], partner)

    def near_copy(step):
        rows = all_in.at[around[step], pl.ds(2 * lax.rem(place, 2), 2)]
        return remote(rows, rows, near_send.at[step], near_recv.at[step], sibling)

    def gain_near():
        return remote(gains_out, gains_in, sum_sems.at[0, 0], sum_sems.at[1, 0], sibling)

    def gain_pair(step):
        return remote(
            blocks.at[2 * lax.rem(slow + step, slows) + 1 - fast], block_in.at[step],
            sum_sems.at[2, step], sum_sems.at[3, step], beside,
        )

    def gain_line(step):
        return remote(line_out.at[step], line_in.at[step], sum_sems.at[4, step], sum_sems.at[5, step], along_way(step))

    near_ways = [{NARROW: lax.rem(place + step, group)} for step in range(1, group)]
    greet([{WIDE: device} for device in around[1:]] + near_ways)
    gains_out[...] = jnp.zeros(gains_out.shape, F32)
    for row, part in enumerate(gain_parts):
        gains_out[row : row + 1, :] = part[...]
    gain_near().start()
    out_blocks[...] = jnp.transpose(branch[pl.ds(at_quarter, quarter), :]).reshape(out_blocks.shape)
    for step in range(1, owners):
        wide_copy(step).start()
    all_in[me, held] = out_blocks[me]
    carry.begin(*carry.all())
    gain_near().wait_recv()
    both = gains_out[...] + gains_in[...]
    for owner in range(owners):
        blocks[owner] = lax.dot_general(
            both, feature_places(owner, width, share).astype(F32), (((1,), (1,)), ((), ())),
            precision=lax.Precision.HIGHEST, preferred_element_type=F32,
        )
    for step in range(slows):
        gain_pair(step).start()

    def hand_on(step):
        if step:
            wide_copy(owners - step).wait_recv()
        far_copy(step).start()

    def hand_over(step):
        far_copy(step).wait_recv()
        near_copy(step).start()

    def gather_grad(step, first_turn):
        near_copy(step).wait_recv()
        row = around[step]

        for k in range(seq_len // quarter):
            columns = slice(k * quarter, (k + 1) * quarter)
            high, found = token_parts(ids_all[row, k : k + 1, :], first)
            picks[:, columns] = found
            grads = all_in[row, k]
            for part in range(vocab // LANES):
                inside = jnp.where(high == part, 1.0, 0.0).astype(BF16)
                masked[part * share : (part + 1) * share, columns] = grads * inside
        span = 8 * share

        def some(i, _):
            rows = rows_at(0, i, span)
            part = dot_nt(masked[rows, :], picks[...])
            total[rows, :] = part if first_turn else total[rows, :] + part
            return 0

        lax.fori_loop(0, total.shape[0] // span, some, 0)

    order = [0] + list(range(1, owners))
    for turn in range(owners + 2):
        if turn < owners:
            hand_on(order[turn])
        if 1 <= turn < owners + 1:
            hand_over(order[turn - 1])
        if turn == 1:
            for step in list(range(1, slows)) + [0]:
                gain_pair(step).wait_recv()
                line_out[step] = blocks[2 * lax.rem(slow + step, slows) + fast] + block_in[step]
                if step:
                    gain_line(step).start()
        if turn >= 2:
            gather_grad(order[turn - 2], turn == 2)
    for t in range(vocab // LANES):
        d_table[:, t * LANES : (t + 1) * LANES] = total[t * share : (t + 1) * share, :]
    small = line_out[0]
    for step in range(1, slows):
        gain_line(step).wait_recv()
        small = small + line_in[step]
    d_small[...] = small
    carry.end(*carry.all())
    square = jnp.sum(d_table[...] * d_table[...])
    for part in squares:
        square = square + part[0, 0]
    for load in carry.loads:
        square = square + load.squares[0, 0]
    lead = (place == 0).astype(F32)
    square = square + lead * jnp.sum(small * small)
    lanes = lax.broadcasted_iota(jnp.int32, (8, LANES), 1)
    given = jnp.where(lanes == 0, square, jnp.where(lanes == 1, lead * jnp.sum(losses[...]), 0.0))

    def scalar_near(step):
        return remote(near.at[place], near.at[place], sum_sems.at[6, step], sum_sems.at[7, step], near_ways[step - 1])

    def scalar_wide(step):
        return remote(along.at[me], along.at[me], all_send.at[step], all_recv.at[step], {WIDE: around[step]})

    near[place] = given
    for step in range(1, group):
        scalar_near(step).start()
    for step in range(1, group):
        scalar_near(step).wait()
    along[me] = jnp.sum(near[...], axis=0)
    for step in range(1, owners):
        scalar_wide(step).start()
    for step in range(1, owners):
        scalar_wide(step).wait()
    scalars[...] = jnp.sum(along[...], axis=0)
    gain_near().wait_send()
    for step in range(owners):
        far_copy(step).wait_send()
        near_copy(step).wait_send()
        if step:
            wide_copy(step).wait_send()
    for step in range(slows):
        gain_pair(step).wait_send()
        if step:
            gain_line(step).wait_send()


def tail(branch, ids_all, losses, gain_parts, squares, share, vocab, group, collective_id, loads):
    seq_len, width = branch.shape
    owners = ids_all.shape[0]
    slows = owners // 2
    dma = pltpu.SemaphoreType.DMA
    small = (8, LANES)
    return run(
        functools.partial(tail_kernel, (len(gain_parts) - 1) // 2),
        "tail",
        [branch, ids_all, losses, *gain_parts, *squares],
        [
            jax.ShapeDtypeStruct((share, vocab), F32),
            jax.ShapeDtypeStruct(small, F32),
            jax.ShapeDtypeStruct(small, F32),
        ],
        [
            pltpu.VMEM((owners, share, seq_len // 4), BF16),
            pltpu.VMEM((owners, 4, share, seq_len // 4), BF16),
            pltpu.VMEM((vocab // LANES * share, seq_len), BF16),
            pltpu.VMEM((LANES, seq_len), BF16),
            pltpu.VMEM((vocab // LANES * share, LANES), F32),
            pltpu.VMEM((8, width), F32),
            pltpu.VMEM((8, width), F32),
            pltpu.VMEM((owners,) + small, F32),
            pltpu.VMEM((slows,) + small, F32),
            pltpu.VMEM((slows,) + small, F32),
            pltpu.VMEM((slows,) + small, F32),
            pltpu.VMEM((group,) + small, F32),
            pltpu.VMEM((owners,) + small, F32),
        ]
        + [dma((owners,))] * 8
        + [dma((12, max(slows, group)))],
        collective_id,
        loads,
    )


PIECES = 4
TABLE, ATTN_IN, ATTN_OUT, FFN_IN, FFN_OUT = range(5)


def shares_tile(wide, narrow, noised, attn_out, ffn_in, tables):
    rows, seq_len = noised.shape
    return (
        attn_out.shape[0] == 2
        and narrow == 4
        and wide % 2 == 0
        and rows == 1
        and seq_len % (2 * CHUNKS * 128) == 0
        and tables.shape[1] * wide % 256 == 0
        and attn_out.shape[1] % 16 == 0
        and attn_out.shape[1] <= LANES
        and ffn_in.shape[2] % 128 == 0
        and tables.shape[1] == attn_out.shape[1]
        and tables.shape[2] % (PIECES * TILE) == 0
    )


def per_device(wide, narrow, *arrays):
    noised, attn_out, ffn_in, tables = arrays[0], arrays[6], arrays[7], arrays[9]
    if shares_tile(wide, narrow, noised, attn_out, ffn_in, tables):
        return tiled_device(wide, *arrays)
    return general_device(*arrays)


def tiled_device(
    wide,
    noised,
    clean,
    timesteps,
    segments,
    counted,
    attn_in,
    attn_out,
    ffn_in,
    ffn_out,
    tables,
    gains,
    attn_in_mean,
    attn_out_mean,
    ffn_in_mean,
    ffn_out_mean,
    tables_mean,
    gains_mean,
    attn_in_square,
    attn_out_square,
    ffn_in_square,
    ffn_out_square,
    tables_square,
    gains_square,
):
    layers = attn_in.shape[0]
    gain_rows, gain_cols = gains.shape
    share, vocab = tables.shape[1:]
    leads = (1, 0, 0, 0)
    four = (attn_in, attn_out, ffn_in, ffn_out)

    def joined(value, lead):
        return value.reshape(value.shape[:lead] + (-1,) + value.shape[lead + 2 :])

    ids = noised.reshape(4, -1)
    steps = timesteps.reshape(-1, LANES)
    half_width = D // 2
    rates = jnp.exp(-math.log(10000.0) * jnp.arange(half_width, dtype=F32) / half_width)[None, :]
    quarter = vocab // PIECES
    windows = [(k * quarter, quarter) for k in range(PIECES)]
    key_seg, query_seg = segments.reshape(-1, 1), segments.reshape(1, -1)
    weights = (attn_in, attn_out, ffn_in, ffn_out)
    (residual, normed, gain_w, counts, ids_all, projected, mixed, middle, normed_two, log_sums, result, normed_next), carried = front(
        ids, counted, gains, steps, rates, tables, key_seg, query_seg, wide, attn_out.shape[2], 0,
        [GatherLoad(value, 0, lead, wide, place=KEPT) for value, lead in zip(weights, leads)]
        + [GatherLoad(value, 1, lead, wide) for value, lead in zip(weights[:3], leads)]
        + [SlowLoad(ffn_out, 1, 0, wide)],
    )
    token_total = counts[gain_rows, 0]
    first_w = [joined(value, lead) for value, lead in zip(carried[:4], leads)]
    query_w, output_w, expand_w = [joined(value, lead) for value, lead in zip(carried[4:7], leads)]
    kept = [(residual, normed, projected, mixed, middle, normed_two, log_sums, *first_w)]
    half_pieces = PIECES // 2
    piece_made = jax.ShapeDtypeStruct((wide, share, quarter), BF16)
    (projected, mixed, middle, normed_two, log_sums, grad, branch, gain_final, losses, *d_last), carried = last_and_loss(
        1, normed_next, key_seg, query_seg, result, query_w, output_w, expand_w, gain_w,
        (noised, clean, timesteps, counted), counts, vocab, PIECES, 1,
        [FastLoad(carried[7], 0, wide)]
        + [GatherLoad(tables, 1, 0, wide, window, place=LOCAL) for window in windows]
        + [PairLoad(piece_made, 0, True) for _ in range(half_pieces)],
    )
    reduce_w, *table_sums = carried
    kept.append(
        (result, normed_next, projected, mixed, middle, normed_two, log_sums)
        + (query_w, output_w, expand_w, joined(reduce_w, 0))
    )
    own, squares = {}, []

    def by_owner(value, lead):
        shape = value.shape
        return value.reshape(shape[:lead] + (wide, shape[lead] // wide) + shape[lead + 1 :])

    def landed(key, results):
        own[key] = results[0]
        squares.append(results[1])
        return results[2:]

    hidden = ffn_in.shape[2]
    made = jax.ShapeDtypeStruct((wide, share, hidden), BF16)
    made_in = jax.ShapeDtypeStruct((3, wide, share, attn_in.shape[3]), BF16)
    made_out = jax.ShapeDtypeStruct((wide, share, attn_out.shape[2]), BF16)

    def start_last(carry, d_red, d_in):
        carry.loads[PIECES].full, carry.loads[PIECES + 1].full = d_red, d_in
        carry.begin(*range(PIECES))

    points = (
        start_last,
        lambda carry: carry.begin(PIECES, PIECES + 1),
        lambda carry: carry.hand_on(*range(half_pieces, PIECES)),
        lambda carry: carry.hand_on(PIECES),
        lambda carry, d_out, d_query: None,
    )
    residual, normed, projected, mixed, middle, normed_two, log_sums, *four_w = kept[1]
    query_w, output_w, expand_w, reduce_w = four_w
    (grad, branch, d_out, d_query, gain_two, gain_one), carried = backward_block(
        1, None, points, grad, branch, reduce_w, expand_w, output_w, normed_two, middle, gain_w, mixed,
        projected, log_sums, key_seg, query_seg, query_w, residual, normed, wide, 2,
        [LineLoad(sums, wide) for sums in table_sums]
        + [ReduceLoad(piece, 0) for piece in d_last]
        + [ReduceLoad(made, 0, True), PairLoad(made, 0, True)],
    )
    for key in [(TABLE, k) for k in range(PIECES)] + [(FFN_OUT, 1)]:
        carried = landed(key, carried)
    (in_sums,) = carried
    gain_grads = [None, None, gain_one, gain_two, gain_final]

    def start_first(carry, d_red, d_in):
        carry.loads[3].full, carry.loads[4].full = d_red, d_in
        carry.begin(0, 1, 2)

    def sent_first(carry, d_out, d_query):
        carry.hand_on(4)
        carry.loads[5].full, carry.loads[6].full = d_out, d_query
        carry.begin(5, 6)

    points = (
        start_first,
        lambda carry: carry.begin(3, 4),
        lambda carry: carry.hand_on(1, 2),
        lambda carry: carry.hand_on(3),
        sent_first,
    )
    residual, normed, projected, mixed, middle, normed_two, log_sums, *four_w = kept[0]
    query_w, output_w, expand_w, reduce_w = four_w
    (grad, branch, _, _, gain_two, gain_one), carried = backward_block(
        0, math.sqrt(D), points, grad, branch, reduce_w, expand_w, output_w, normed_two, middle, gain_w, mixed,
        projected, log_sums, key_seg, query_seg, query_w, residual, normed, wide, 3,
        [LineLoad(in_sums, wide), ReduceLoad(d_out, 0), ReduceLoad(d_query, 1)]
        + [ReduceLoad(made, 0, True), ReduceLoad(made, 0, True), PairLoad(made_out, 0, True), PairLoad(made_in, 1, True)],
    )
    for key in ((FFN_IN, 1), (ATTN_OUT, 1), (ATTN_IN, 1), (FFN_OUT, 0), (FFN_IN, 0)):
        carried = landed(key, carried)
    out_sums, in_sums = carried
    gain_grads[:2] = gain_one, gain_two

    (own_first, total_small, scalars), carried = tail(
        branch, ids_all, losses, gain_grads, squares, share, vocab, 4, 4,
        [LineLoad(out_sums, wide), LineLoad(in_sums, wide)],
    )
    own[ATTN_OUT, 0], own[ATTN_IN, 0] = carried[0], carried[2]
    grad_attn_in, grad_attn_out, grad_ffn_in, grad_ffn_out = [
        jnp.stack([own[name, index] for index in range(layers)]) for name in (ATTN_IN, ATTN_OUT, FFN_IN, FFN_OUT)
    ]
    grad_tables = jnp.stack([own_first, jnp.concatenate([own[TABLE, k] for k in range(PIECES)], axis=1)])
    grad_gains = total_small[:gain_rows, :gain_cols]
    total_square, loss_sum = scalars[0, 0], scalars[0, 1]
    grad_norm = jnp.sqrt(total_square)
    factor = jnp.minimum(1.0, CLIP_NORM / (grad_norm + 1e-06))
    results = [loss_sum, token_total, grad_norm]
    for weight, gradient, first, second, decay, rate in (
        (attn_in, grad_attn_in, attn_in_mean, attn_in_square, WEIGHT_DECAY, LEARN_RATE),
        (attn_out, grad_attn_out, attn_out_mean, attn_out_square, WEIGHT_DECAY, LEARN_RATE),
        (ffn_in, grad_ffn_in, ffn_in_mean, ffn_in_square, WEIGHT_DECAY, LEARN_RATE),
        (ffn_out, grad_ffn_out, ffn_out_mean, ffn_out_square, WEIGHT_DECAY, LEARN_RATE),
        (tables, grad_tables, tables_mean, tables_square, WEIGHT_DECAY, LEARN_RATE),
        (gains, grad_gains, gains_mean, gains_square, 0.0, GAIN_RATE),
    ):
        results += adam(weight, factor * gradient, first, second, decay, rate)
    return tuple(results)


def solution(mesh):
    wide, narrow = mesh.shape[WIDE], mesh.shape[NARROW]
    placed = (
        P(WIDE, None),
        P(WIDE, None),
        P(WIDE, None),
        P(WIDE, None),
        P(WIDE, None),
        P(None, None, WIDE, NARROW),
        P(None, WIDE, NARROW),
        P(None, WIDE, NARROW),
        P(None, WIDE, NARROW),
        P(None, WIDE, NARROW),
        P(None, WIDE),
        P(None, None, WIDE, NARROW),
        P(None, WIDE, NARROW),
        P(None, WIDE, NARROW),
        P(None, WIDE, NARROW),
        P(None, WIDE, NARROW),
        P(None, WIDE),
        P(None, None, WIDE, NARROW),
        P(None, WIDE, NARROW),
        P(None, WIDE, NARROW),
        P(None, WIDE, NARROW),
        P(None, WIDE, NARROW),
        P(None, WIDE),
    )
    return jax.shard_map(
        functools.partial(per_device, wide, narrow),
        mesh=mesh,
        in_specs=placed,
        out_specs=(
            P(),
            P(),
            P(),
            P(None, None, WIDE, NARROW),
            P(None, None, WIDE, NARROW),
            P(None, None, WIDE, NARROW),
            P(None, None, WIDE, NARROW),
            P(None, WIDE, NARROW),
            P(None, WIDE, NARROW),
            P(None, WIDE, NARROW),
            P(None, WIDE, NARROW),
            P(None, WIDE, NARROW),
            P(None, WIDE, NARROW),
            P(None, WIDE, NARROW),
            P(None, WIDE, NARROW),
            P(None, WIDE, NARROW),
            P(None, WIDE, NARROW),
            P(None, WIDE, NARROW),
            P(None, WIDE, NARROW),
            P(None, WIDE, NARROW),
            P(None, WIDE, NARROW),
            P(None, WIDE, NARROW),
            P(None, WIDE, NARROW),
            P(None, WIDE),
            P(None, WIDE),
            P(None, WIDE),
            P(None, WIDE),
        ),
        check_vma=False,
    )
```

```python
import functools
import math

import jax
import jax.numpy as jnp
from jax import lax
from jax.experimental import pallas as pl
from jax.experimental.pallas import tpu as pltpu
from jax.sharding import PartitionSpec as P

D = 768
HD = 64
V = 8192
STEPS = 1000
ADAM_STEP = 10


NORM_EPS = 1e-05
LEARN_RATE = 0.05
GAIN_RATE = 0.75
FIRST_DECAY = 0.9
SECOND_DECAY = 0.999
ADAM_EPS = 1e-08
WEIGHT_DECAY = 0.01
CLIP_NORM = 0.005
WIDE, NARROW = "wide", "narrow"


def add_heads(partial_value):
    return lax.psum(partial_value, NARROW)


def back_heads(partial_value):
    return lax.psum(partial_value, NARROW)


def rms_forward(value, gain):
    scale_row = lax.rsqrt(jnp.mean(value * value, axis=-1, keepdims=True) + NORM_EPS)
    return (value * scale_row * gain, scale_row)


def rms_backward(grad, value, scale_row, gain):
    unit = value * scale_row
    scaled = grad * gain
    back = scale_row * (scaled - unit * jnp.mean(scaled * unit, axis=-1, keepdims=True))
    return (back, jnp.sum(grad * unit, axis=0))


def time_features(timestep_row):
    half_width = D // 2
    rates = jnp.exp(-math.log(10000.0) * jnp.arange(half_width, dtype=jnp.float32) / half_width)
    angles = timestep_row.astype(jnp.float32)[:, None] * rates[None, :]
    return jnp.concatenate([jnp.sin(angles), jnp.cos(angles)], axis=1)


def masked_scores(queries, key_rows, segment):
    scores = jnp.einsum(
        "qhd,khd->hqk", queries, key_rows, preferred_element_type=jnp.float32
    ) * HD ** (-0.5)
    return jnp.where((segment[:, None] == segment[None, :])[None], scores, -1e30)


def attend(entry):
    queries, key_rows, values, segment = entry
    scores = masked_scores(queries, key_rows, segment)
    row_top = jnp.max(scores, axis=-1, keepdims=True)
    log_total = row_top + jnp.log(jnp.sum(jnp.exp(scores - row_top), axis=-1, keepdims=True))
    probs = jnp.exp(scores - log_total).astype(jnp.bfloat16)
    mixed = jnp.einsum("hqk,khd->qhd", probs, values, preferred_element_type=jnp.float32)
    return (mixed.astype(jnp.bfloat16), log_total)


def attend_back(entry):
    queries, key_rows, values, segment, log_total, grad_mixed = entry
    probs = jnp.exp(masked_scores(queries, key_rows, segment) - log_total)
    grad_probs = jnp.einsum("qhd,khd->hqk", grad_mixed, values, preferred_element_type=jnp.float32)
    grad_scores = (
        probs * (grad_probs - jnp.sum(probs * grad_probs, axis=-1, keepdims=True))
    ).astype(jnp.bfloat16)
    grad_query = jnp.einsum(
        "hqk,khd->qhd", grad_scores, key_rows, preferred_element_type=jnp.float32
    ) * HD ** (-0.5)
    grad_key = jnp.einsum(
        "hqk,qhd->khd", grad_scores, queries, preferred_element_type=jnp.float32
    ) * HD ** (-0.5)
    grad_value = jnp.einsum(
        "hqk,qhd->khd", probs.astype(jnp.bfloat16), grad_mixed, preferred_element_type=jnp.float32
    )
    return (grad_query, grad_key, grad_value)


def layer_forward(residual, segments, query_w, output_w, expand_w, reduce_w, gain_attn, gain_ffn):
    seq_count, seq_len = segments.shape
    normed, scale_one = rms_forward(residual, gain_attn)
    normed = normed.astype(jnp.bfloat16)
    projected = jnp.einsum(
        "sd,cde->cse", normed, query_w, preferred_element_type=jnp.float32
    ).astype(jnp.bfloat16)
    heads = projected.reshape(3, seq_count, seq_len, -1, HD)
    mixed, log_total = lax.map(attend, (heads[0], heads[1], heads[2], segments))
    mixed = mixed.reshape(seq_count * seq_len, -1)
    middle = residual + add_heads(
        jnp.einsum("se,de->sd", mixed, output_w, preferred_element_type=jnp.float32)
    )
    normed_two, scale_two = rms_forward(middle, gain_ffn)
    normed_two = normed_two.astype(jnp.bfloat16)
    before = jnp.dot(normed_two, expand_w, preferred_element_type=jnp.float32)
    after = jax.nn.gelu(before).astype(jnp.bfloat16)
    result = middle + add_heads(
        jnp.einsum("sf,df->sd", after, reduce_w, preferred_element_type=jnp.float32)
    )
    return (
        result,
        (
            residual,
            scale_one,
            normed,
            projected,
            log_total,
            mixed,
            middle,
            scale_two,
            normed_two,
            before,
            after,
        ),
    )


def layer_backward(
    grad, kept, segments, query_w, output_w, expand_w, reduce_w, gain_attn, gain_ffn
):
    (
        residual,
        scale_one,
        normed,
        projected,
        log_total,
        mixed,
        middle,
        scale_two,
        normed_two,
        before,
        after,
    ) = kept
    seq_count, seq_len = segments.shape
    grad_branch = grad.astype(jnp.bfloat16)
    grad_after = jnp.dot(grad_branch, reduce_w, preferred_element_type=jnp.float32)
    grad_reduce = jnp.einsum("sd,sf->df", grad_branch, after, preferred_element_type=jnp.float32)
    _, gelu_pull = jax.vjp(jax.nn.gelu, before)
    grad_before = gelu_pull(grad_after)[0].astype(jnp.bfloat16)
    grad_expand = jnp.einsum(
        "sd,sf->df", normed_two, grad_before, preferred_element_type=jnp.float32
    )
    grad_normed_two = back_heads(
        jnp.einsum("sf,df->sd", grad_before, expand_w, preferred_element_type=jnp.float32)
    )
    grad_middle, grad_gain_ffn = rms_backward(grad_normed_two, middle, scale_two, gain_ffn)
    grad_middle = grad_middle + grad
    grad_attn = grad_middle.astype(jnp.bfloat16)
    grad_mixed = jnp.dot(grad_attn, output_w, preferred_element_type=jnp.float32).astype(
        jnp.bfloat16
    )
    grad_output = jnp.einsum("sd,se->de", grad_attn, mixed, preferred_element_type=jnp.float32)
    heads = projected.reshape(3, seq_count, seq_len, -1, HD)
    grad_query, grad_key, grad_value = lax.map(
        attend_back,
        (
            heads[0],
            heads[1],
            heads[2],
            segments,
            log_total,
            grad_mixed.reshape(seq_count, seq_len, -1, HD),
        ),
    )
    grad_projected = (
        jnp.stack([grad_query, grad_key, grad_value])
        .reshape(3, seq_count * seq_len, -1)
        .astype(jnp.bfloat16)
    )
    grad_query_w = jnp.einsum(
        "sd,cse->cde", normed, grad_projected, preferred_element_type=jnp.float32
    )
    grad_normed = back_heads(
        jnp.einsum("cse,cde->sd", grad_projected, query_w, preferred_element_type=jnp.float32)
    )
    grad_input, grad_gain_attn = rms_backward(grad_normed, residual, scale_one, gain_attn)
    return (
        grad_input + grad_middle,
        (
            grad_query_w,
            grad_output,
            grad_expand,
            grad_reduce,
            jnp.stack([grad_gain_attn, grad_gain_ffn]),
        ),
    )


def adam(weight, grad, first, second, decay, rate):
    first_new = FIRST_DECAY * first + (1.0 - FIRST_DECAY) * grad
    second_new = SECOND_DECAY * second + (1.0 - SECOND_DECAY) * grad * grad
    first_hat = first_new / (1.0 - FIRST_DECAY**ADAM_STEP)
    second_hat = second_new / (1.0 - SECOND_DECAY**ADAM_STEP)
    weight_new = weight - rate * (first_hat / (jnp.sqrt(second_hat) + ADAM_EPS) + decay * weight)
    return (weight_new, first_new, second_new, weight_new.astype(jnp.bfloat16))


def general_device(
    noised,
    clean,
    timesteps,
    segments,
    counted,
    attn_in,
    attn_out,
    ffn_in,
    ffn_out,
    tables,
    gains,
    attn_in_mean,
    attn_out_mean,
    ffn_in_mean,
    ffn_out_mean,
    tables_mean,
    gains_mean,
    attn_in_square,
    attn_out_square,
    ffn_in_square,
    ffn_out_square,
    tables_square,
    gains_square,
):
    layers = attn_in.shape[0]
    mask = counted.reshape(-1).astype(jnp.float32)
    token_total = lax.psum(jnp.sum(mask), WIDE)
    query_w, output_w, expand_w, reduce_w, table_w, gain_low = (
        lax.all_gather(attn_in.astype(jnp.bfloat16), WIDE, axis=2, tiled=True),
        lax.all_gather(attn_out.astype(jnp.bfloat16), WIDE, axis=1, tiled=True),
        lax.all_gather(ffn_in.astype(jnp.bfloat16), WIDE, axis=1, tiled=True),
        lax.all_gather(ffn_out.astype(jnp.bfloat16), WIDE, axis=1, tiled=True),
        lax.all_gather(tables.astype(jnp.bfloat16), WIDE, axis=1, tiled=True),
        lax.all_gather(gains.astype(jnp.bfloat16), WIDE, axis=1, tiled=True),
    )
    gain_w = gain_low.astype(jnp.float32)
    noised_flat = noised.reshape(-1)
    clean_flat = clean.reshape(-1)
    step_flat = timesteps.reshape(-1)
    vocab_local = table_w.shape[2]
    vocab_ids = lax.axis_index(NARROW) * vocab_local + jnp.arange(vocab_local, dtype=jnp.int32)
    picks = (noised_flat[:, None] == vocab_ids[None, :]).astype(jnp.bfloat16)
    looked = add_heads(
        jnp.einsum("sv,dv->sd", picks, table_w[0], preferred_element_type=jnp.float32)
    )
    residual = math.sqrt(D) * looked + time_features(step_flat)
    kept_layers = []
    for layer_index in range(layers):
        residual, kept = layer_forward(
            residual,
            segments,
            query_w[layer_index],
            output_w[layer_index],
            expand_w[layer_index],
            reduce_w[layer_index],
            gain_w[2 * layer_index],
            gain_w[2 * layer_index + 1],
        )
        kept_layers.append(kept)
    final, scale_final = rms_forward(residual, gain_w[2 * layers])
    final_low = final.astype(jnp.bfloat16)
    logits = jnp.dot(final_low, table_w[1], preferred_element_type=jnp.float32)
    local_top = jnp.max(logits, axis=1)
    row_top = lax.pmax(local_top, NARROW)
    row_total = lax.psum(jnp.sum(jnp.exp(logits - row_top[:, None]), axis=1), NARROW)
    log_probs = logits - (row_top + jnp.log(row_total))[:, None]
    probs = jnp.exp(log_probs)
    clamped = jnp.maximum(step_flat, 2).astype(jnp.float32)[:, None]
    beta = 1.0 / (STEPS - clamped + 1.0)
    retain = (STEPS - clamped + 1.0) / STEPS
    spread = (clamped - 1.0) / (STEPS * V)
    at_noised = (vocab_ids[None, :] == noised_flat[:, None]).astype(jnp.float32)
    at_clean = (vocab_ids[None, :] == clean_flat[:, None]).astype(jnp.float32)
    forward_fac = beta / V + (1.0 - beta) * at_noised
    backward_fac = retain * at_clean + spread
    joint = forward_fac * backward_fac
    marginal = retain * probs + spread
    joint_total, cross, model_total, weighted, aligned, clean_logp = lax.psum(
        (
            jnp.sum(joint, axis=1),
            jnp.sum(joint * (jnp.log(backward_fac) - jnp.log(marginal)), axis=1),
            jnp.sum(forward_fac * marginal, axis=1),
            jnp.sum(probs * joint / marginal, axis=1),
            jnp.sum(forward_fac * probs, axis=1),
            jnp.sum(at_clean * log_probs, axis=1),
        ),
        NARROW,
    )
    divergence = cross / joint_total - jnp.log(joint_total) + jnp.log(model_total)
    first_step = step_flat == 1
    losses = jnp.where(first_step, -clean_logp, divergence)
    pull = retain * (
        -(joint / joint_total[:, None]) / marginal + forward_fac / model_total[:, None]
    )
    centre = retain[:, 0] * (-weighted / joint_total + aligned / model_total)
    grad_kl = probs * (pull - centre[:, None])
    grad_recon = probs - at_clean
    grad_logits = (
        (mask / token_total)[:, None] * jnp.where(first_step[:, None], grad_recon, grad_kl)
    ).astype(jnp.bfloat16)
    grad_table_out = jnp.einsum(
        "sd,sv->dv", final_low, grad_logits, preferred_element_type=jnp.float32
    )
    grad_final = back_heads(
        jnp.einsum("sv,dv->sd", grad_logits, table_w[1], preferred_element_type=jnp.float32)
    )
    grad_x, grad_gain_final = rms_backward(grad_final, residual, scale_final, gain_w[2 * layers])
    layer_grads = [None] * layers
    for layer_index in reversed(range(layers)):
        grad_x, produced = layer_backward(
            grad_x,
            kept_layers[layer_index],
            segments,
            query_w[layer_index],
            output_w[layer_index],
            expand_w[layer_index],
            reduce_w[layer_index],
            gain_w[2 * layer_index],
            gain_w[2 * layer_index + 1],
        )
        layer_grads[layer_index] = produced
    grad_look = (math.sqrt(D) * grad_x).astype(jnp.bfloat16)
    grad_table_in = jnp.einsum("sd,sv->dv", grad_look, picks, preferred_element_type=jnp.float32)
    stacked = [jnp.stack([entry[which] for entry in layer_grads]) for which in range(5)]
    gain_layers = stacked[4].reshape(2 * layers, -1)
    grad_tables_all = jnp.stack([grad_table_in, grad_table_out])
    grad_attn_in, grad_attn_out, grad_ffn_in, grad_ffn_out, grad_tables, grad_gains = (
        lax.psum_scatter(stacked[0], WIDE, scatter_dimension=2, tiled=True),
        lax.psum_scatter(stacked[1], WIDE, scatter_dimension=1, tiled=True),
        lax.psum_scatter(stacked[2], WIDE, scatter_dimension=1, tiled=True),
        lax.psum_scatter(stacked[3], WIDE, scatter_dimension=1, tiled=True),
        lax.psum_scatter(grad_tables_all, WIDE, scatter_dimension=1, tiled=True),
        lax.psum_scatter(
            jnp.concatenate([gain_layers, grad_gain_final[None, :]], axis=0),
            WIDE,
            scatter_dimension=1,
            tiled=True,
        ),
    )
    narrow_first = (lax.axis_index(NARROW) == 0).astype(jnp.float32)
    squares = (
        jnp.sum(grad_attn_in * grad_attn_in)
        + jnp.sum(grad_attn_out * grad_attn_out)
        + jnp.sum(grad_ffn_in * grad_ffn_in)
        + jnp.sum(grad_ffn_out * grad_ffn_out)
        + jnp.sum(grad_tables * grad_tables)
        + narrow_first * jnp.sum(grad_gains * grad_gains)
    )
    squares, loss_sum = lax.psum(
        (squares, narrow_first * jnp.sum(mask * losses)), (WIDE, NARROW)
    )
    grad_norm = jnp.sqrt(squares)
    factor = jnp.minimum(1.0, CLIP_NORM / (grad_norm + 1e-06))
    attn_in_next, attn_in_mean_next, attn_in_square_next, attn_in_copy = adam(
        attn_in, factor * grad_attn_in, attn_in_mean, attn_in_square, WEIGHT_DECAY, LEARN_RATE
    )
    attn_out_next, attn_out_mean_next, attn_out_square_next, attn_out_copy = adam(
        attn_out, factor * grad_attn_out, attn_out_mean, attn_out_square, WEIGHT_DECAY, LEARN_RATE
    )
    ffn_in_next, ffn_in_mean_next, ffn_in_square_next, ffn_in_copy = adam(
        ffn_in, factor * grad_ffn_in, ffn_in_mean, ffn_in_square, WEIGHT_DECAY, LEARN_RATE
    )
    ffn_out_next, ffn_out_mean_next, ffn_out_square_next, ffn_out_copy = adam(
        ffn_out, factor * grad_ffn_out, ffn_out_mean, ffn_out_square, WEIGHT_DECAY, LEARN_RATE
    )
    tables_next, tables_mean_next, tables_square_next, tables_copy = adam(
        tables, factor * grad_tables, tables_mean, tables_square, WEIGHT_DECAY, LEARN_RATE
    )
    gains_next, gains_mean_next, gains_square_next, gains_copy = adam(
        gains, factor * grad_gains, gains_mean, gains_square, 0.0, GAIN_RATE
    )
    return (
        loss_sum,
        token_total,
        grad_norm,
        attn_in_next,
        attn_in_mean_next,
        attn_in_square_next,
        attn_in_copy,
        attn_out_next,
        attn_out_mean_next,
        attn_out_square_next,
        attn_out_copy,
        ffn_in_next,
        ffn_in_mean_next,
        ffn_in_square_next,
        ffn_in_copy,
        ffn_out_next,
        ffn_out_mean_next,
        ffn_out_square_next,
        ffn_out_copy,
        tables_next,
        tables_mean_next,
        tables_square_next,
        tables_copy,
        gains_next,
        gains_mean_next,
        gains_square_next,
        gains_copy,
    )


MESH = pl.DeviceIdType.MESH
SLOW, FAST = 1, 2
HBM, KEPT, LOCAL = 1, 2, 3
F32 = jnp.float32
BF16 = jnp.bfloat16
CHUNKS = 8
SPAN = 4
VMEM_LIMIT = 61 * 1024 * 1024
FORWARD_KIND = BF16
BACKWARD_KIND = BF16


def whole_vmem():
    return pl.BlockSpec(memory_space=pltpu.VMEM)


def dot_nn(a, b):
    return lax.dot_general(a, b, (((1,), (0,)), ((), ())), preferred_element_type=F32)


def dot_nt(a, b):
    return lax.dot_general(a, b, (((1,), (1,)), ((), ())), preferred_element_type=F32)


def remote(src, dst, send_sem, recv_sem, device):
    return pltpu.make_async_remote_copy(
        src_ref=src,
        dst_ref=dst,
        send_sem=send_sem,
        recv_sem=recv_sem,
        device_id=device,
        device_id_type=MESH,
    )


def greet(devices):
    barrier = pltpu.get_barrier_semaphore()
    for device in devices:
        pl.semaphore_signal(barrier, inc=1, device_id=device, device_id_type=MESH)
    pl.semaphore_wait(barrier, len(devices))


def group_places(seq_len):
    me = lax.axis_index(NARROW)
    core = lax.rem(me, 2)
    half = seq_len // 2
    mine = pl.multiple_of(core * half, half)
    other = pl.multiple_of((1 - core) * half, half)
    return ({NARROW: me + 1 - 2 * core}, {NARROW: lax.rem(me + 2, 4)}, mine, other)


class Exchange:
    def __init__(self, refs, sems, base, sibling, partner):
        self.near_out, self.near_in, self.far_out, self.far_in = refs
        self.send, self.recv = sems
        self.base, self.sibling, self.partner = base, sibling, partner

    def near(self, j):
        return remote(
            self.near_out.at[j],
            self.near_in.at[j],
            self.send.at[self.base, j],
            self.recv.at[self.base, j],
            self.sibling,
        )

    def far(self, j):
        return remote(
            self.far_out.at[j],
            self.far_in.at[j],
            self.send.at[self.base + 1, j],
            self.recv.at[self.base + 1, j],
            self.partner,
        )

    def give(self, j, value):
        self.near_out[j] = value.astype(self.near_out.dtype)
        self.near(j).start()

    def give_span(self, k, value):
        chunk = self.near_out.shape[1]
        for i in range(SPAN):
            self.give(SPAN * k + i, value[i * chunk : (i + 1) * chunk, :])

    def pass_on_span(self, k, value):
        chunk = self.near_out.shape[1]
        for i in range(SPAN):
            self.pass_on(SPAN * k + i, value[i * chunk : (i + 1) * chunk, :])

    def pass_on(self, j, value):
        self.near(j).wait_recv()
        self.far_out[j] = (value + self.near_in[j].astype(F32)).astype(self.far_out.dtype)
        self.far(j).start()

    def take(self, j):
        self.far(j).wait_recv()
        return self.far_out[j].astype(F32) + self.far_in[j].astype(F32)

    def close(self):
        for j in range(CHUNKS):
            self.near(j).wait_send()
            self.far(j).wait_send()

    @staticmethod
    def scratch(chunk, width, kind):
        return [
            pltpu.VMEM((CHUNKS, chunk, width), BF16),
            pltpu.VMEM((CHUNKS, chunk, width), BF16),
            pltpu.VMEM((CHUNKS, chunk, width), kind),
            pltpu.VMEM((CHUNKS, chunk, width), kind),
        ]


class Share:
    def __init__(self, ref, sems, base, sibling, mine, chunk):
        self.ref, self.base, self.sibling, self.mine, self.chunk = ref, base, sibling, mine, chunk
        self.send, self.recv = sems

    def piece(self, j):
        rows = self.ref.at[pl.ds(pl.multiple_of(self.mine + j * self.chunk, self.chunk), self.chunk)]
        return remote(rows, rows, self.send.at[self.base, j], self.recv.at[self.base, j], self.sibling)

    def put(self, j, value):
        self.ref[pl.ds(pl.multiple_of(self.mine + j * self.chunk, self.chunk), self.chunk), :] = value
        self.piece(j).start()

    def arrived(self, j):
        self.piece(j).wait_recv()

    def close(self):
        for j in range(CHUNKS):
            self.piece(j).wait_send()


def wide_places(count):
    me = lax.axis_index(WIDE)
    fast = lax.rem(me, 2)
    slow = me // 2
    return (me, slow, fast, count // 2)


class Carry:
    def __init__(self, loads, fetches, leaves):
        self.loads, self.fetches, self.leaves = loads, fetches, leaves
        self.left = []

    def fetch(self):
        for copy in self.fetches:
            copy.start()

    def fetched(self):
        for copy in self.fetches:
            copy.wait()

    def leave(self, *which):
        for k in which:
            self.leaves[k].start()
            self.left.append(k)

    def gone(self):
        self.leave(*[k for k in self.leaves if k not in self.left])
        for k in self.left:
            self.leaves[k].wait()

    def peers(self):
        ways = []
        for load in self.loads:
            ways += [way for way in load.ways if way not in ways]
        me, slow, fast, slows = wide_places(self.loads[0].count) if self.loads else (0, 0, 0, 0)
        found = []
        if SLOW in ways:
            found += [{WIDE: 2 * lax.rem(slow + step, slows) + fast} for step in range(1, slows)]
        if FAST in ways:
            found.append({WIDE: me + 1 - 2 * fast})
        return found

    def begin(self, *which):
        for k in which:
            self.loads[k].start()

    def hand_on(self, *which):
        for k in which:
            self.loads[k].relay()

    def end(self, *which):
        for k in which:
            self.loads[k].finish()

    def all(self):
        return range(len(self.loads))


def part_of(weights, index, window):
    shape = weights.shape[1:]
    return shape if window is None else shape[:-1] + (window[1],)


class SlowLoad:
    ways = (SLOW,)

    def __init__(self, weights, index, lead, count, window=None):
        self.index, self.lead, self.count, self.window = index, lead, count, window
        shape, slows = part_of(weights, index, window), count // 2
        self.operands, self.in_specs = [weights], [whole_vmem()]
        self.outs = [jax.ShapeDtypeStruct((slows,) + shape, BF16)]
        self.out_specs = [pl.BlockSpec(memory_space=pl.ANY)]
        self.scratch = [pltpu.VMEM(shape, BF16), pltpu.SemaphoreType.DMA] + [pltpu.SemaphoreType.DMA((slows,))] * 2

    def bind(self, given, out, scratch):
        self.shard, self.out = given[0], out[0]
        self.low, self.local, self.send, self.recv = scratch
        self.me, self.slow, self.fast, self.slows = wide_places(self.count)

    def cast(self):
        if self.window is None:
            self.low[...] = self.shard[self.index].astype(BF16)
        else:
            self.low[...] = self.shard[self.index, :, self.window[0] : self.window[0] + self.window[1]].astype(BF16)

    def target(self):
        return self.out.at[self.slow]

    def slow_copy(self, step):
        return remote(
            self.low, self.target(), self.send.at[step], self.recv.at[step],
            {WIDE: 2 * lax.rem(self.slow + step, self.slows) + self.fast},
        )

    def own_copy(self):
        return pltpu.make_async_copy(self.low, self.target(), self.local)

    def start(self):
        self.cast()
        for step in range(1, self.slows):
            self.slow_copy(step).start()
        self.own_copy().start()

    def finish(self):
        for step in range(1, self.slows):
            self.slow_copy(step).wait()
        self.own_copy().wait()


class FastLoad:
    ways = (FAST,)

    def __init__(self, blocks, lead, count):
        self.lead, self.count = lead, count
        shape, slows = blocks.shape[1:], count // 2
        self.operands, self.in_specs = [blocks], [pl.BlockSpec(memory_space=pl.ANY)]
        self.outs = [jax.ShapeDtypeStruct(shape[:lead] + (count,) + shape[lead:], BF16)]
        self.out_specs = [whole_vmem()]
        self.scratch = [pltpu.SemaphoreType.DMA((slows,))] * 3

    def value(self):
        return self.out[...].reshape((-1, self.out.shape[-1]))

    def bind(self, given, out, scratch):
        self.blocks, self.out = given[0], out[0]
        self.local, self.send, self.recv = scratch
        self.me, self.slow, self.fast, self.slows = wide_places(self.count)

    def copies(self, step):
        target = self.out.at[(slice(None),) * self.lead + (2 * step + self.fast,)]
        return (
            remote(
                self.blocks.at[step], target, self.send.at[step], self.recv.at[step],
                {WIDE: self.me + 1 - 2 * self.fast},
            ),
            pltpu.make_async_copy(self.blocks.at[step], target, self.local.at[step]),
        )

    def start(self):
        for step in range(self.slows):
            for copy in self.copies(step):
                copy.start()

    def finish(self):
        for step in range(self.slows):
            for copy in self.copies(step):
                copy.wait()


class GatherLoad(SlowLoad):
    ways = (SLOW, FAST)

    def __init__(self, weights, index, lead, count, window=None, place=HBM):
        super().__init__(weights, index, lead, count, window)
        shape, slows = part_of(weights, index, window), count // 2
        whole = shape[:lead] + (count,) + shape[lead:]
        self.outs = [jax.ShapeDtypeStruct(whole, BF16)]
        self.scratch = self.scratch + [pltpu.SemaphoreType.DMA((slows,))] * 2
        if place == KEPT:
            self.out_specs = [whole_vmem()]
        self.local_out = place == LOCAL
        if self.local_out:
            self.outs, self.out_specs = [], []
            self.scratch = self.scratch + [pltpu.VMEM(whole, BF16)]

    def bind(self, given, out, scratch):
        if self.local_out:
            out, scratch = scratch[-1:], scratch[:-1]
        super().bind(given, out, scratch[:-2])
        self.fast_send, self.fast_recv = scratch[-2:]

    def value(self, *index):
        found = self.out[index] if index else self.out[...]
        return found.reshape((-1, found.shape[-1]))

    def at(self, owner):
        return self.out.at[(slice(None),) * self.lead + (owner,)]

    def target(self):
        return self.at(self.me)

    def fast_copy(self, step):
        block = self.at(2 * lax.rem(self.slow + self.slows - step, self.slows) + self.fast)
        return remote(
            self.low if step == 0 else block, block, self.fast_send.at[step], self.fast_recv.at[step],
            {WIDE: self.me + 1 - 2 * self.fast},
        )

    def start(self):
        super().start()
        self.fast_copy(0).start()

    def relay(self):
        for step in range(1, self.slows):
            self.slow_copy(step).wait_recv()
            self.fast_copy(step).start()

    def finish(self):
        for step in range(self.slows):
            self.fast_copy(step).wait()
            if step:
                self.slow_copy(step).wait_send()
        self.own_copy().wait()


class PairLoad:
    ways = (FAST,)

    def __init__(self, full, lead, inside=False):
        self.lead, self.count, self.inside = lead, full.shape[lead], inside
        self.shape, self.slows = full.shape[:lead] + full.shape[lead + 1 :], self.count // 2
        self.operands, self.in_specs = ([], []) if inside else ([full], [whole_vmem()])
        self.outs, self.out_specs = [jax.ShapeDtypeStruct((self.slows,) + self.shape, BF16)], [whole_vmem()]
        self.scratch = [pltpu.VMEM((self.slows,) + self.shape, BF16)] + [pltpu.SemaphoreType.DMA((self.slows,))] * 2

    def bind(self, given, out, scratch):
        self.full = None if self.inside else given[0]
        self.out = out[0]
        self.came, self.send, self.recv = scratch
        self.me, self.slow, self.fast, self.slows = wide_places(self.count)

    def block(self, step, fast):
        owner = 2 * lax.rem(self.slow + step, self.slows) + fast
        return self.full.at[(slice(None),) * self.lead + (owner,)]

    def copy(self, step):
        return remote(
            self.block(step, 1 - self.fast), self.came.at[step], self.send.at[step], self.recv.at[step],
            {WIDE: self.me + 1 - 2 * self.fast},
        )

    def start(self):
        for step in list(range(1, self.slows)) + [0]:
            self.copy(step).start()

    def finish(self):
        for step in range(self.slows):
            self.copy(step).wait()
            total = self.block(step, self.fast)[...].astype(F32) + self.came[step].astype(F32)
            self.out[step] = total.astype(BF16)


class ReduceLoad(PairLoad):
    ways = (SLOW, FAST)

    def __init__(self, full, lead, inside=False):
        super().__init__(full, lead, inside)
        self.outs = [jax.ShapeDtypeStruct(self.shape, F32), jax.ShapeDtypeStruct((8, 128), F32)]
        self.out_specs = [whole_vmem()] * 2
        self.scratch = (
            self.scratch
            + [pltpu.VMEM((self.slows - 1,) + self.shape, BF16)]
            + [pltpu.SemaphoreType.DMA((self.slows,))] * 2
        )

    def bind(self, given, out, scratch):
        super().bind(given, out[:1], scratch[:3])
        self.squares = out[1]
        self.landed, self.line_send, self.line_recv = scratch[3:]

    def line_copy(self, step):
        return remote(
            self.came.at[step], self.landed.at[step - 1], self.line_send.at[step], self.line_recv.at[step],
            {WIDE: 2 * lax.rem(self.slow + step, self.slows) + self.fast},
        )

    def relay(self):
        for step in list(range(1, self.slows)) + [0]:
            self.copy(step).wait()
            total = self.block(step, self.fast)[...].astype(F32) + self.came[step].astype(F32)
            self.came[step] = total.astype(BF16)
            if step:
                self.line_copy(step).start()

    def finish(self):
        total = self.came[0].astype(F32)
        for step in range(1, self.slows):
            self.line_copy(step).wait()
            total = total + self.landed[step - 1].astype(F32)
        self.out[...] = total
        self.squares[...] = jnp.full(self.squares.shape, jnp.sum(total * total), F32)


class LineLoad:
    ways = (SLOW,)

    def __init__(self, sums, count):
        self.count = count
        slows = count // 2
        self.operands, self.in_specs = [sums], [whole_vmem()]
        self.outs = [jax.ShapeDtypeStruct(sums.shape[1:], F32), jax.ShapeDtypeStruct((8, 128), F32)]
        self.out_specs = [whole_vmem()] * 2
        self.scratch = [pltpu.VMEM(sums.shape, BF16)] + [pltpu.SemaphoreType.DMA((slows,))] * 2

    def bind(self, given, out, scratch):
        self.sums, (self.out, self.squares) = given[0], out
        self.came, self.send, self.recv = scratch
        self.me, self.slow, self.fast, self.slows = wide_places(self.count)

    def copy(self, step):
        return remote(
            self.sums.at[step], self.came.at[step], self.send.at[step], self.recv.at[step],
            {WIDE: 2 * lax.rem(self.slow + step, self.slows) + self.fast},
        )

    def start(self):
        for step in range(1, self.slows):
            self.copy(step).start()

    def finish(self):
        total = self.sums[0].astype(F32)
        for step in range(1, self.slows):
            self.copy(step).wait()
            total = total + self.came[step].astype(F32)
        self.out[...] = total
        self.squares[...] = jnp.full(self.squares.shape, jnp.sum(total * total), F32)


def run(body, name, operands, outs, scratch, collective_id=None, loads=(), away=(), lazy=(), early=()):
    any_place = pl.BlockSpec(memory_space=pl.ANY)
    given, taken = list(operands), []
    in_specs = [any_place if k in away or k in lazy else whole_vmem() for k in range(len(operands))]
    for load in loads:
        places = []
        for operand, spec in zip(load.operands, load.in_specs):
            known = [k for k, other in enumerate(given) if other is operand]
            if not known:
                known = [len(given)]
                given.append(operand)
                in_specs.append(spec)
            places.append(known[0])
        taken.append(places)
    moved = [operands[k] for k in lazy] + [outs[k] for k in early]
    counts = [len(given), len(outs)] + [len(load.outs) for load in loads]
    counts += [len(scratch)] + [len(load.scratch) for load in loads] + [len(moved), len(moved)]
    parts = 1 + len(loads)

    def kernel(*refs):
        groups, place = [], 0
        for count in counts:
            groups.append(refs[place : place + count])
            place += count
        for k, load in enumerate(loads):
            load.bind([groups[0][p] for p in taken[k]], groups[2 + k], groups[2 + parts + k])
        mine, results = list(groups[0][: len(operands)]), list(groups[1])
        fetches, leaves = [], {}
        for k, buffer, sem in zip(lazy, groups[-2], groups[-1]):
            fetches.append(pltpu.make_async_copy(mine[k], buffer, sem))
            mine[k] = buffer
        for k, buffer, sem in zip(early, groups[-2][len(lazy) :], groups[-1][len(lazy) :]):
            leaves[k] = pltpu.make_async_copy(buffer, results[k], sem)
            results[k] = buffer
        body(*mine, *results, *groups[1 + parts], carry=Carry(list(loads), fetches, leaves))

    results = pl.pallas_call(
        kernel,
        out_shape=tuple(outs) + tuple(out for load in loads for out in load.outs),
        in_specs=in_specs,
        out_specs=tuple(any_place if k in early else whole_vmem() for k in range(len(outs)))
        + tuple(spec for load in loads for spec in load.out_specs),
        scratch_shapes=list(scratch)
        + [s for load in loads for s in load.scratch]
        + [pltpu.VMEM(value.shape, value.dtype) for value in moved]
        + [pltpu.SemaphoreType.DMA] * len(moved),
        compiler_params=pltpu.CompilerParams(
            collective_id=collective_id,
            has_side_effects=collective_id is not None,
            vmem_limit_bytes=VMEM_LIMIT,
        ),
        name=name,
    )(*given)
    return results[: len(outs)], results[len(outs) :]


def sems(kinds):
    return [pltpu.SemaphoreType.DMA((kinds, CHUNKS)), pltpu.SemaphoreType.DMA((kinds, CHUNKS))]


def norm_of(value, gain):
    scale = lax.rsqrt(jnp.mean(value * value, axis=-1, keepdims=True) + NORM_EPS)
    return value * scale * gain


def norm_back(grad, value, gain):
    scale = lax.rsqrt(jnp.mean(value * value, axis=-1, keepdims=True) + NORM_EPS)
    unit = value * scale
    scaled = grad * gain
    back = scale * (scaled - unit * jnp.mean(scaled * unit, axis=-1, keepdims=True))
    return (back, jnp.sum(grad * unit, axis=0, keepdims=True))


GELU_A = math.sqrt(2.0 / math.pi)
GELU_B = 0.044715


def gelu_of(x):
    return 0.5 * x * (1.0 + jnp.tanh(GELU_A * (x + GELU_B * (x * x * x))))


def gelu_slope(x):
    square = x * x
    t = jnp.tanh(GELU_A * (x + GELU_B * (x * square)))
    return 0.5 * (1.0 + t) + 0.5 * x * (1.0 - t * t) * (GELU_A * (1.0 + 3.0 * GELU_B * square))


def rows_at(start, j, chunk):
    return pl.ds(pl.multiple_of(start + j * chunk, chunk), chunk)


LANES = 128
SUB = 64


def spread(row):
    return jnp.transpose(jnp.broadcast_to(row, (LANES, LANES)))


def feature_places(owner, width, share):
    lane = lax.broadcasted_iota(jnp.int32, (LANES, width), 0)
    feature = lax.broadcasted_iota(jnp.int32, (LANES, width), 1)
    return ((feature == lane + owner * share) & (lane < share)).astype(F32).astype(BF16)


def token_parts(ids, first):
    here = ids - first
    high = lax.shift_right_arithmetic(here, 7)
    place = lax.broadcasted_iota(jnp.int32, (LANES, ids.shape[1]), 0)
    return high, jnp.where(place == here - high * LANES, 1.0, 0.0).astype(BF16)


def embed_part(
    ids, counted, gains, steps, rates, table,
    resid, normed, gain_all, count_all, ids_all,
    low, extra, small, near_out, near_in, own, far_out, far_in, wide_out, wide_in, part_out, part_in,
    id_send, id_recv, small_send, small_recv, near_send, near_recv, far_send, far_recv, wide_send, wide_recv,
    part_send, part_recv, send, recv, carry,
):
    seq_len, width = normed.shape
    chunk = seq_len // 2 // CHUNKS
    quarter = seq_len // 4
    share, vocab = table.shape[1:]
    owners = ids_all.shape[0]
    sibling, partner, mine, other = group_places(seq_len)
    place = lax.axis_index(NARROW)
    side = lax.div(place, 2)
    me = lax.axis_index(WIDE)
    first = place * vocab
    around = [lax.rem(me + step, owners) for step in range(owners)]

    def id_copy(step):
        return remote(ids_all.at[me], ids_all.at[me], id_send.at[step], id_recv.at[step], {WIDE: around[step]})

    def small_copy(step):
        return remote(small.at[me], small.at[me], small_send.at[step], small_recv.at[step], {WIDE: around[step]})

    def near_copy(step):
        return remote(near_out.at[step], near_in.at[step], near_send.at[step], near_recv.at[step], sibling)

    def far_copy(step):
        return remote(far_out.at[step], far_in.at[step], far_send.at[step], far_recv.at[step], partner)

    def wide_copy(step):
        return remote(wide_out.at[step], wide_in.at[me], wide_send.at[step], wide_recv.at[step], {WIDE: around[step]})

    def part_copy(piece):
        rows = pl.ds(piece * LANES, LANES)
        return remote(part_out.at[rows], part_in.at[rows], part_send.at[piece], part_recv.at[piece], partner)

    ids_all[me] = ids[...]
    small[me] = jnp.zeros(small.shape[1:], F32)
    small[me, : gains.shape[0], : gains.shape[1]] = gains[...].astype(BF16).astype(F32)
    count = jnp.sum(counted[...].astype(F32), keepdims=True)
    small[me, COUNT_ROW : COUNT_ROW + 1, :] = jnp.broadcast_to(count, (1, small.shape[2]))
    greet([{WIDE: device} for device in around[1:]] + [sibling, partner])
    for step in range(1, owners):
        id_copy(step).start()
    for step in range(1, owners):
        small_copy(step).start()
    carry.begin(0, 1)
    parts = vocab // LANES
    for part in range(parts):
        low[part * share : (part + 1) * share, :] = table[0, :, part * LANES : (part + 1) * LANES].astype(BF16)
    core = lax.rem(place, 2)

    def look_up(step):
        row = lax.rem(me + step, owners)

        def find(which):
            high, picks = token_parts(ids_all[row, pl.ds(which, 1), :], first)
            found = dot_nn(low[...], picks)
            total = jnp.zeros((share, quarter), F32)
            for part in range(parts):
                total = total + jnp.where(high == part, found[part * share : (part + 1) * share, :], 0.0)
            return total.astype(BF16)

        for k in range(2):
            near_out[step, k] = find(2 * (1 - core) + k)
        near_copy(step).start()
        for k in range(2):
            own[step, k] = find(2 * core + k)

    def halve(step):
        near_copy(step).wait_recv()
        own[step] = own[step] + near_in[step]
        far_out[step] = own[step, 1 - side]
        far_copy(step).start()

    def deliver(step):
        far_copy(step).wait_recv()
        total = own[step, side] + far_in[step]
        if step % owners == 0:
            wide_in[me] = total
        else:
            wide_out[step] = total
            wide_copy(step).start()

    order = list(range(1, owners)) + [0]
    for turn in range(owners + 2):
        if turn < owners:
            if order[turn]:
                id_copy(owners - order[turn]).wait_recv()
            look_up(order[turn])
        if 1 <= turn < owners + 1:
            halve(order[turn - 1])
        if turn >= 2:
            deliver(order[turn - 2])
    carry.begin(2, 3)
    carry.hand_on(0, 1)
    for step in range(1, owners):
        small_copy(step).wait_recv()
    total = None
    for owner in range(owners):
        part = dot_nn(small[owner].astype(BF16), feature_places(owner, width, share))
        total = part if total is None else total + part
    gain_all[...] = total
    count_all[...] = jnp.sum(small[...], axis=0)
    half_width = width // 2
    for k in range(seq_len // 2 // LANES):
        when = spread(steps[pl.ds(mine // LANES + k, 1), :].astype(F32))
        for t in range(half_width // LANES):
            columns = slice(t * LANES, (t + 1) * LANES)
            angles = when * rates[:, columns]
            rows = slice(k * LANES, (k + 1) * LANES)
            extra[rows, t * LANES : (t + 1) * LANES] = jnp.sin(angles)
            extra[rows, half_width + t * LANES : half_width + (t + 1) * LANES] = jnp.cos(angles)
    for step in range(1, owners):
        wide_copy(step).wait_recv()
    found = jnp.transpose(wide_in[...].reshape(width, quarter))
    pieces = quarter // LANES
    at_side = pl.multiple_of(side * quarter, quarter)
    at_other = pl.multiple_of((1 - side) * quarter, quarter)
    for piece in range(pieces):
        rows = pl.ds(piece * LANES, LANES)
        part_out[rows, :] = found[piece * LANES : (piece + 1) * LANES, :]
        part_copy(piece).start()

    def finish(start, source, piece):
        rows = rows_at(start, piece, LANES)
        x = math.sqrt(width) * source[pl.ds(piece * LANES, LANES), :].astype(F32) + extra[rows, :]
        resid[rows, :] = x
        here = rows_at(mine + start, piece, LANES)
        normed[here, :] = norm_of(x, gain_all[0:1, :]).astype(BF16)
        give_rows(here, piece if source is part_out else pieces + piece).start()

    def give_rows(here, k):
        return remote(normed.at[here], normed.at[here], send.at[0, k], recv.at[0, k], sibling)

    for piece in range(pieces):
        finish(at_side, part_out, piece)
    for piece in range(pieces):
        part_copy(piece).wait_recv()
        finish(at_other, part_in, piece)
    carry.hand_on(2)
    for k in range(2 * pieces):
        give_rows(rows_at(mine, k % pieces, LANES), k).wait()
    for step in range(owners):
        near_copy(step).wait_send()
        far_copy(step).wait_send()
        if step:
            id_copy(step).wait_send()
            small_copy(step).wait_send()
            wide_copy(step).wait_send()
    for piece in range(pieces):
        part_copy(piece).wait_send()


QUERY_BLOCK = 256


def forward_part(
    layer, weights, points, normed, key_seg, query_seg, resid, gains,
    projected, mixed, middle, normed_two, log_sums, result, normed_next,
    bias, values_t, near_out, near_in, far_out, far_in, near_out2, near_in2, far_out2, far_in2, send, recv,
):
    w_query, w_out, w_in, w_red = weights
    at_half, at_feed, at_sent, at_last = points
    seq_len, width = normed.shape
    chunk = seq_len // 2 // CHUNKS
    block = bias.shape[1]
    heads = mixed.shape[1] // HD
    sibling, partner, mine, other = group_places(seq_len)
    pair = (send, recv)
    first = Exchange((near_out, near_in, far_out, far_in), pair, 0, sibling, partner)
    second = Exchange((near_out2, near_in2, far_out2, far_in2), pair, 2, sibling, partner)
    share = Share(normed_two, pair, 4, sibling, mine, chunk)
    share_next = Share(normed_next, pair, 5, sibling, mine, chunk)

    def ask(i, _):
        rows = rows_at(0, i, block)
        for which in range(3):
            projected[which, rows, :] = dot_nn(normed[rows, :], w_query(which)).astype(BF16)
        return 0

    lax.fori_loop(0, seq_len // block, ask, 0)
    values_t[...] = jnp.transpose(projected[2])

    def attend_rows(start):
        rows = pl.ds(pl.multiple_of(start, block), block)
        bias[...] = jnp.where(key_seg[...] == query_seg[:, rows], 0.0, -1e30)
        asked = projected[0, rows, :] * HD ** (-0.5)
        parts = []
        for head in range(heads):
            scores = dot_nt(projected[1], head_lanes(asked, head, HD)) + bias[...]
            top = jnp.max(scores, axis=0, keepdims=True)
            powers = jnp.exp(scores - top)
            total = jnp.sum(powers, axis=0, keepdims=True)
            log_sums[head : head + 1, rows] = top + jnp.log(total)
            probs = (powers * (1.0 / total)).astype(BF16)
            parts.append(dot_nn(values_t[head * HD : (head + 1) * HD, :], probs))
        mixed[rows, :] = jnp.transpose(jnp.concatenate(parts, axis=0)).astype(BF16)

    def project(start, k):
        return dot_nt(mixed[rows_at(start, k, SPAN * chunk), :], w_out())

    def feed(rows):
        pre = dot_nn(normed_two[rows, :], w_in())
        return dot_nt(gelu_of(pre).astype(BF16), w_red())

    for part in range(CHUNKS // SPAN):

        def both(i, _):
            attend_rows(jnp.where(i == 0, other, mine) + part * block)
            return 0

        lax.fori_loop(0, 2, both, 0)
        first.give_span(part, project(other, part))
        if part == 0:
            at_half()
        first.pass_on_span(part, project(mine, part))
    at_feed()
    for k in range(CHUNKS // SPAN):
        for j in range(SPAN * k, SPAN * (k + 1)):
            rows = rows_at(0, j, chunk)
            mid = resid[rows, :] + first.take(j)
            middle[rows, :] = mid
            share.put(j, norm_of(mid, gains[2 * layer + 1 : 2 * layer + 2, :]).astype(BF16))
        kept = feed(rows_at(mine, k, SPAN * chunk))
        for j in range(SPAN * k, SPAN * (k + 1)):
            share.arrived(j)
        second.give_span(k, feed(rows_at(other, k, SPAN * chunk)))
        second.pass_on_span(k, kept)
    at_sent()
    for j in range(CHUNKS):
        rows = rows_at(0, j, chunk)
        x = middle[rows, :] + second.take(j)
        result[rows, :] = x
        share_next.put(j, norm_of(x, gains[2 * layer + 2 : 2 * layer + 3, :]).astype(BF16))
        if j == CHUNKS - 2:
            at_last()
    for j in range(CHUNKS):
        share_next.arrived(j)
    for part in (first, second, share, share_next):
        part.close()


def layer_outs(seq_len, width, heads_width):
    return [
        jax.ShapeDtypeStruct((3, seq_len, heads_width), BF16),
        jax.ShapeDtypeStruct((seq_len, heads_width), BF16),
        jax.ShapeDtypeStruct((seq_len // 2, width), F32),
        jax.ShapeDtypeStruct((seq_len, width), BF16),
        jax.ShapeDtypeStruct((8, seq_len), F32),
    ]


def layer_scratch(seq_len, width, heads_width):
    half, chunk = seq_len // 2, seq_len // 2 // CHUNKS
    block = SPAN * chunk
    return (
        [pltpu.VMEM((seq_len, block), F32), pltpu.VMEM((heads_width, seq_len), BF16)]
        + Exchange.scratch(chunk, width, FORWARD_KIND)
        + Exchange.scratch(chunk, width, FORWARD_KIND)
        + sems(6)
    )


LAYER_SCRATCH = 12
COUNT_ROW = 5


def front_kernel(
    ids, counted, gains, steps, rates, table, key_seg, query_seg,
    resid, normed, gain_all, count_all, ids_all, projected, mixed, middle, normed_two, log_sums, result, normed_next,
    *scratch, carry,
):
    embed_part(
        ids, counted, gains, steps, rates, table, resid, normed, gain_all, count_all, ids_all,
        *scratch[:-LAYER_SCRATCH], carry,
    )
    carry.end(0, 1)
    later = list(carry.all())[4:]

    def at_half():
        carry.hand_on(3)
        carry.begin(*later[:2])

    def at_feed():
        carry.end(2, 3)
        carry.begin(*later[2:])
        carry.leave(0, 1, 5, 6)

    def at_sent():
        carry.hand_on(*later[:2])
        carry.leave(7, 8)

    forward_part(
        0,
        [carry.loads[0].value] + [load.value for load in carry.loads[1:4]],
        (at_half, at_feed, at_sent, lambda: carry.hand_on(*later[2:3])),
        normed, key_seg, query_seg, resid, gain_all,
        projected, mixed, middle, normed_two, log_sums, result, normed_next, *scratch[-LAYER_SCRATCH:],
    )
    carry.end(*later)
    carry.gone()


def front(ids, counted, gains, steps, rates, tables, key_seg, query_seg, owners, heads_width, collective_id, loads):
    seq_len = ids.size
    share, vocab = tables.shape[1:]
    half, width = seq_len // 2, owners * share
    dma = pltpu.SemaphoreType.DMA
    return run(
        front_kernel,
        "front",
        [ids, counted, gains, steps, rates, tables, key_seg, query_seg],
        [
            jax.ShapeDtypeStruct((half, width), F32),
            jax.ShapeDtypeStruct((seq_len, width), BF16),
            jax.ShapeDtypeStruct((8, width), F32),
            jax.ShapeDtypeStruct((8, LANES), F32),
            jax.ShapeDtypeStruct((owners,) + ids.shape, jnp.int32),
        ]
        + layer_outs(seq_len, width, heads_width)
        + [jax.ShapeDtypeStruct((half, width), F32), jax.ShapeDtypeStruct((seq_len, width), BF16)],
        [
            pltpu.VMEM((vocab // LANES * share, LANES), BF16),
            pltpu.VMEM((half, width), F32),
            pltpu.VMEM((owners, 8, LANES), F32),
        ]
        + [pltpu.VMEM((owners, 2, share, half // 2), BF16)] * 3
        + [pltpu.VMEM((owners, share, half // 2), BF16)] * 4
        + [
            pltpu.VMEM((half // 2, width), BF16),
            pltpu.VMEM((half // 2, width), BF16),
        ]
        + [dma((owners,))] * 10
        + [dma((half // 2 // LANES,))] * 2
        + [dma((1, half // LANES))] * 2
        + layer_scratch(seq_len, width, heads_width),
        collective_id,
        loads,
        early=(0, 1, 5, 6, 7, 8),
    )


TILE = 256


def weight_grad(left_t, right, out):
    columns = right.shape[1]
    tile = TILE if columns % TILE == 0 else columns

    def put(where):
        value = dot_nn(left_t[...], right[:, where]).astype(out.dtype)
        if len(out.shape) == 3:
            out[:, :, where] = value.reshape(out.shape[:2] + (tile,))
        else:
            out[:, where] = value

    def step(i, _):
        put(pl.ds(pl.multiple_of(i * tile, tile), tile))
        return 0

    if tile == columns:
        put(slice(None))
    else:
        lax.fori_loop(0, columns // tile, step, 0)


def head_lanes(value, head, size):
    lanes = lax.broadcasted_iota(jnp.int32, value.shape, 1)
    inside = (lanes >= head * size) & (lanes < (head + 1) * size)
    return jnp.where(inside, value, jnp.zeros_like(value))


def backward_kernel(
    layer, scale, points, grad, branch, w_red, w_in, w_out, normed_two, middle, gains, mixed,
    projected, log_sums, key_seg, query_seg, w_query, resid, normed,
    grad_out, branch_out, d_out, d_query, gain_two, gain_one,
    d_red, d_in, grad_middle, grad_attn, grad_mixed, grad_projected, grad_before, after, turned,
    bias, keys_t, grad_keys, grad_values,
    near_out, near_in, far_out, far_in, far_out2, far_in2, send, recv, loaded, carry, peers=None,
):
    at_start, at_made, at_summed, at_attended, at_sent = points
    seq_len, width = normed_two.shape
    chunk = seq_len // 2 // CHUNKS
    sibling, partner, mine, other = group_places(seq_len)
    carry.fetch()
    greet([sibling, partner] + carry.peers() if peers is None else peers)
    at_start(carry, d_red, d_in)
    pair = (send, recv)
    trade = Exchange((near_out, near_in, far_out, far_in), pair, 0, sibling, partner)
    share = Share(grad_attn, pair, 2, sibling, mine, chunk)

    def ffn_partial(start, k):
        rows = rows_at(start, k, SPAN * chunk)
        pre = dot_nn(normed_two[rows, :], w_in[...])
        after[rows, :] = gelu_of(pre).astype(BF16)
        low = (dot_nn(branch[rows, :], w_red[...]) * gelu_slope(pre)).astype(BF16)
        grad_before[rows, :] = low
        return dot_nt(low, w_in[...])

    for k in range(CHUNKS // SPAN):
        trade.give_span(k, ffn_partial(other, k))
        trade.pass_on_span(k, ffn_partial(mine, k))
    turned[...] = jnp.transpose(branch[...])
    weight_grad(turned, after, d_red)
    turned[...] = jnp.transpose(normed_two[...])
    weight_grad(turned, grad_before, d_in)
    at_made(carry)
    fetch = pltpu.make_async_copy(normed, after, loaded)
    fetch.start()
    carry.fetched()
    total = jnp.zeros((1, width), F32)
    for j in range(CHUNKS):
        rows = rows_at(0, j, chunk)
        back, part = norm_back(trade.take(j), middle[rows, :], gains[2 * layer + 1 : 2 * layer + 2, :])
        total = total + part
        back = back + grad[rows, :]
        grad_middle[rows, :] = back
        share.put(j, back.astype(BF16))
        here = rows_at(mine, j, chunk)
        grad_mixed[here, :] = dot_nn(grad_attn[here, :], w_out[...]).astype(BF16)
    gain_two[...] = total
    for j in range(CHUNKS):
        share.arrived(j)
        here = rows_at(other, j, chunk)
        grad_mixed[here, :] = dot_nn(grad_attn[here, :], w_out[...]).astype(BF16)
    trade.close()
    share.close()
    at_summed(carry)

    block = bias.shape[1]
    heads = grad_mixed.shape[1] // HD
    keys_t[...] = jnp.transpose(projected[1])
    grad_keys[...] = jnp.zeros(grad_keys.shape, F32)
    grad_values[...] = jnp.zeros(grad_values.shape, F32)

    def queries(i, _):
        rows = rows_at(0, i, block)
        bias[...] = jnp.where(key_seg[...] == query_seg[:, rows], 0.0, -1e30)
        asked = projected[0, rows, :] * HD ** (-0.5)
        given = grad_mixed[rows, :]
        parts = []
        for head in range(heads):
            query = head_lanes(asked, head, HD)
            wanted = head_lanes(given, head, HD)
            scores = dot_nt(projected[1], query) + bias[...]
            probs = jnp.exp(scores - log_sums[head : head + 1, rows])
            grad_probs = dot_nt(projected[2], wanted)
            centre = jnp.sum(probs * grad_probs, axis=0, keepdims=True)
            grad_scores = (probs * (grad_probs - centre)).astype(BF16)
            parts.append(dot_nn(keys_t[head * HD : (head + 1) * HD, :], grad_scores))
            grad_keys[...] += dot_nn(grad_scores, query)
            grad_values[...] += dot_nn(probs.astype(BF16), wanted)
        grad_projected[0, rows, :] = (jnp.transpose(jnp.concatenate(parts, axis=0)) * HD ** (-0.5)).astype(BF16)
        return 0

    lax.fori_loop(0, seq_len // block, queries, 0)
    grad_projected[1] = grad_keys[...].astype(BF16)
    grad_projected[2] = grad_values[...].astype(BF16)
    at_attended(carry)

    trade = Exchange((near_out, near_in, far_out2, far_in2), pair, 3, sibling, partner)
    share = Share(branch_out, pair, 5, sibling, mine, chunk)

    def query_partial(start, k):
        rows = rows_at(start, k, SPAN * chunk)
        found = None
        for which in range(3):
            part = dot_nt(grad_projected[which, rows, :], w_query[which])
            found = part if found is None else found + part
        return found

    for k in range(CHUNKS // SPAN):
        trade.give_span(k, query_partial(other, k))
        trade.pass_on_span(k, query_partial(mine, k))
    turned[...] = jnp.transpose(grad_attn[...])
    weight_grad(turned, mixed, d_out)
    fetch.wait()
    turned[...] = jnp.transpose(after[...])
    for which in range(3):
        weight_grad(turned, grad_projected.at[which], d_query.at[which])
    at_sent(carry, d_out, d_query)
    total = jnp.zeros((1, width), F32)
    for j in range(CHUNKS):
        rows = rows_at(0, j, chunk)
        back, part = norm_back(trade.take(j), resid[rows, :], gains[2 * layer : 2 * layer + 1, :])
        total = total + part
        back = back + grad_middle[rows, :]
        grad_out[rows, :] = back
        share.put(j, (back if scale is None else scale * back).astype(BF16))
    gain_one[...] = total
    for j in range(CHUNKS):
        share.arrived(j)
    trade.close()
    share.close()
    if peers is None:
        carry.end(*carry.all())


def backward_scratch(seq_len, width, hidden, heads_width, owners):
    half, chunk = seq_len // 2, seq_len // 2 // CHUNKS
    block = min(QUERY_BLOCK, seq_len)
    far = pltpu.VMEM((CHUNKS, chunk, width), BACKWARD_KIND)
    return (
        [pltpu.VMEM((owners, width // owners, hidden), BF16)] * 2
        + [
            pltpu.VMEM((half, width), F32),
            pltpu.VMEM((seq_len, width), BF16),
            pltpu.VMEM((seq_len, heads_width), BF16),
            pltpu.VMEM((3, seq_len, heads_width), BF16),
            pltpu.VMEM((seq_len, hidden), BF16),
            pltpu.VMEM((seq_len, width), BF16),
            pltpu.VMEM((width, seq_len), BF16),
            pltpu.VMEM((seq_len, block), F32),
            pltpu.VMEM((heads_width, seq_len), BF16),
            pltpu.VMEM((seq_len, heads_width), F32),
            pltpu.VMEM((seq_len, heads_width), F32),
        ]
        + Exchange.scratch(chunk, width, BACKWARD_KIND)
        + [far, far]
        + sems(6)
        + [pltpu.SemaphoreType.DMA]
    )


def backward_outs(seq_len, width, heads_width, owners):
    return [
        jax.ShapeDtypeStruct((seq_len // 2, width), F32),
        jax.ShapeDtypeStruct((seq_len, width), BF16),
        jax.ShapeDtypeStruct((owners, width // owners, heads_width), BF16),
        jax.ShapeDtypeStruct((3, owners, width // owners, heads_width), BF16),
        jax.ShapeDtypeStruct((1, width), F32),
        jax.ShapeDtypeStruct((1, width), F32),
    ]


AWAY, LAZY = (15,), (0, 4, 6, 8, 9, 11, 13, 14)


def backward_block(layer, points, operands, owners, collective_id, loads):
    seq_len, width = operands[5].shape
    hidden, heads_width = operands[3].shape[1], operands[13].shape[2]
    return run(
        functools.partial(backward_kernel, layer, None, points),
        "backward_block",
        operands,
        backward_outs(seq_len, width, heads_width, owners),
        backward_scratch(seq_len, width, hidden, heads_width, owners),
        collective_id,
        loads,
        away=AWAY,
        lazy=LAZY,
    )


def to_rows(columns):
    lanes = lax.broadcasted_iota(jnp.int32, (LANES, LANES), 1)
    total = jnp.zeros((LANES, LANES), F32)
    for k, column in enumerate(columns):
        total = jnp.where(lanes == k, column, total)
    return jnp.transpose(total)[:8, :]


def loss_part(
    row, normed, info, value, gain, table_loads, grad_out, branch, d_gain, losses, d_tables,
    logits, grads, places, turned, stat_out, stat_in, sum_out, sum_in,
    stat_send, stat_recv, sum_send, sum_recv, near_out, near_in, far_out, far_in, send, recv, made,
):
    seq_len, width = normed.shape
    chunk = seq_len // 2 // CHUNKS
    piece_width = table_loads[0].out.shape[-1]
    vocab = piece_width * len(table_loads)
    tiles = vocab // LANES
    blocks = seq_len // LANES
    me = lax.axis_index(NARROW)
    sibling, partner, mine, other = group_places(seq_len)
    peers = [{NARROW: lax.rem(me + k, 4)} for k in range(1, 4)]
    sems = (send, recv)
    trade = Exchange((near_out, near_in, far_out, far_in), sems, 0, sibling, partner)
    share = Share(branch, sems, 2, sibling, mine, chunk)
    first = (me * vocab).astype(F32)
    whole = 4.0 * vocab
    lanes = lax.broadcasted_iota(jnp.int32, (LANES, LANES), 1).astype(F32)

    def stat_copy(b, k):
        return remote(stat_out.at[b], stat_in.at[k, b], stat_send.at[k, b], stat_recv.at[k, b], peers[k])

    def sum_copy(b, k):
        return remote(sum_out.at[b], sum_in.at[k, b], sum_send.at[k, b], sum_recv.at[k, b], peers[k])

    def tile_at(t):
        return pl.ds(pl.multiple_of(t * LANES, LANES), LANES)

    def ask(b, _):
        rows = rows_at(0, b, LANES)
        here = info[:, rows]
        at_noised = spread(here[0:1] - first)
        at_clean = spread(here[1:2] - first)
        places[b, 0] = at_noised
        places[b, 1] = at_clean

        tops, sums = [], [[], [], []]
        for k in range(LANES // SUB):
            part = pl.ds(pl.multiple_of(b * LANES + k * SUB, SUB), SUB)
            subset = slice(k * SUB, (k + 1) * SUB)

            def top_step(t, top):
                return jnp.maximum(top, logits[part, tile_at(t)])

            top = lax.fori_loop(1, tiles, top_step, logits[part, tile_at(0)], unroll=5)
            top = jnp.max(top, axis=1, keepdims=True)
            top_wide = jnp.broadcast_to(top, (SUB, LANES))
            noised_at, clean_at = at_noised[subset], at_clean[subset]

            def sum_step(t, totals):
                powers, noised, clean = totals
                piece = logits[part, tile_at(t)]
                column = lanes[subset] + (t * LANES).astype(F32)
                return (
                    powers + jnp.exp(piece - top_wide),
                    noised + jnp.where(column == noised_at, piece, 0.0),
                    clean + jnp.where(column == clean_at, piece, 0.0),
                )

            zero = jnp.zeros((SUB, LANES), F32)
            totals = lax.fori_loop(0, tiles, sum_step, (zero, zero, zero), unroll=4)
            tops.append(top)
            for found, total in zip(sums, totals):
                found.append(jnp.sum(total, axis=1, keepdims=True))
        stat_out[b] = to_rows([jnp.concatenate(found, axis=0) for found in [tops] + sums])
        for k in range(3):
            stat_copy(b, k).start()
        return 0

    for k, table in enumerate(table_loads):
        if k == len(table_loads) - 1:
            table.finish()

        def product(i, _):
            rows = rows_at(0, i, TILE)
            logits[rows, k * piece_width : (k + 1) * piece_width] = dot_nn(normed[rows, :], table.value())
            return 0

        lax.fori_loop(0, seq_len // TILE, product, 0)
    lax.fori_loop(0, blocks, ask, 0)

    def scalars(b):
        here = info[:, rows_at(0, b, LANES)]
        step = jnp.maximum(here[2:3], 2.0)
        left = STEPS - step + 1.0
        beta = 1.0 / left
        keep = left / STEPS
        rest = (step - 1.0) / (STEPS * whole)
        own = stat_out[b]
        others = [stat_in[k, b] for k in range(3)]
        top = own[0:1]
        for stat in others:
            top = jnp.maximum(top, stat[0:1])
        total = own[1:2] * jnp.exp(own[0:1] - top)
        noised, clean = own[2:3], own[3:4]
        for stat in others:
            total = total + stat[1:2] * jnp.exp(stat[0:1] - top)
            noised, clean = noised + stat[2:3], clean + stat[3:4]
        return here, beta, keep, rest, top + jnp.log(total), noised, clean

    def measure(b, _):
        rows = rows_at(0, b, LANES)
        for k in range(3):
            stat_copy(b, k).wait_recv()
        _, _, keep, rest, log_total, _, _ = scalars(b)
        log_wide = spread(log_total)
        ratio = spread(keep / rest)

        sums = [[], []]
        for k in range(LANES // SUB):
            part = pl.ds(pl.multiple_of(b * LANES + k * SUB, SUB), SUB)
            log_part, ratio_part = log_wide[k * SUB : (k + 1) * SUB], ratio[k * SUB : (k + 1) * SUB]

            def step(t, totals):
                logs, shares = totals
                probs = jnp.exp(logits[part, tile_at(t)] - log_part)
                logits[part, tile_at(t)] = probs
                grown = 1.0 + probs * ratio_part
                return (logs + jnp.log(grown), shares + probs / grown)

            zero = jnp.zeros((SUB, LANES), F32)
            totals = lax.fori_loop(0, tiles, step, (zero, zero), unroll=4)
            for found, total in zip(sums, totals):
                found.append(jnp.sum(total, axis=1, keepdims=True))
        sum_out[b] = to_rows([jnp.concatenate(found, axis=0) for found in sums])
        for k in range(3):
            sum_copy(b, k).start()
        return 0

    lax.fori_loop(0, blocks, measure, 0)

    def pull(b):
        rows = rows_at(0, b, LANES)
        for k in range(3):
            sum_copy(b, k).wait_recv()
        here, beta, keep, rest, log_total, noised, clean = scalars(b)
        sums = sum_out[b] + sum_in[0, b] + sum_in[1, b] + sum_in[2, b]
        log_sum, share_sum = sums[0:1], sums[1:2] / rest
        same = here[0:1] == here[1:2]
        first_step = here[2:3] == 1.0
        base_a, more_a = beta / whole, 1.0 - beta
        base_w = base_a * rest
        joint = whole * base_w + more_a * rest + base_a * keep + jnp.where(same, more_a * keep, 0.0)
        ratio = keep / rest
        prob_n, prob_c = jnp.exp(noised - log_total), jnp.exp(clean - log_total)
        grown_n, grown_c = 1.0 + prob_n * ratio, 1.0 + prob_c * ratio
        marginal_n, marginal_c = rest * grown_n, rest * grown_c
        log_n, log_c = jnp.log(grown_n), jnp.log(grown_c)
        weight_n = jnp.where(same, 0.0, more_a * rest)
        weight_c = jnp.where(same, more_a * rest + base_a * keep + more_a * keep, base_a * keep)
        lift = jnp.log((keep + rest) / rest)
        cross = -base_w * log_sum - weight_n * log_n - weight_c * log_c + (base_w + weight_c) * lift
        model = base_a * (keep + whole * rest) + more_a * marginal_n
        divergence = cross / joint - jnp.log(joint) + jnp.log(model)
        loss = jnp.where(first_step, log_total - clean, divergence)
        losses[:, rows] = here[4:5] * loss
        weighted = base_w * share_sum + weight_n * prob_n / marginal_n + weight_c * prob_c / marginal_c
        aligned = base_a + more_a * prob_n
        centre = keep * (aligned / model - weighted / joint)
        scale = here[3:4]
        zero = jnp.zeros_like(scale)
        even = scale * jnp.where(first_step, 1.0, keep * base_a / model - centre)
        bent = scale * jnp.where(first_step, zero, -keep * base_w / joint / rest)
        at_n = prob_n * keep * (more_a / model - weight_n / joint / marginal_n)
        at_c = -prob_c * keep * (weight_c / joint / marginal_c)
        extra_n = spread(scale * jnp.where(first_step, zero, at_n))
        extra_c = spread(scale * jnp.where(first_step, -1.0, at_c))
        even, bent, ratio = spread(even), spread(bent), spread(ratio)
        at_noised, at_clean = places[b, 0], places[b, 1]

        for k in range(LANES // SUB):
            part = pl.ds(pl.multiple_of(b * LANES + k * SUB, SUB), SUB)
            subset = slice(k * SUB, (k + 1) * SUB)
            even_at, bent_at, ratio_at = even[subset], bent[subset], ratio[subset]
            n_at, c_at, noised_at, clean_at = extra_n[subset], extra_c[subset], at_noised[subset], at_clean[subset]

            def step(t, _):
                probs = logits[part, tile_at(t)]
                column = lanes[subset] + (t * LANES).astype(F32)
                grad = probs * (even_at + bent_at / (1.0 + probs * ratio_at))
                grad = grad + jnp.where(column == noised_at, n_at, 0.0)
                grad = grad + jnp.where(column == clean_at, c_at, 0.0)
                grads[part, tile_at(t)] = grad.astype(BF16)
                return 0

            lax.fori_loop(0, tiles, step, 0, unroll=4)

    def partial(start, k):
        span = SPAN * chunk
        base = start // LANES + k * (span // LANES)
        for b in range(span // LANES):
            pull(base + b)
        total = None
        for k_table, table in enumerate(table_loads):
            part = dot_nt(
                grads[rows_at(start, k, span), k_table * piece_width : (k_table + 1) * piece_width], table.value()
            )
            total = part if total is None else total + part
        return total

    for k in range(CHUNKS // SPAN):
        trade.give_span(k, partial(other, k))
        trade.pass_on_span(k, partial(mine, k))
    turned[...] = jnp.transpose(normed[...])
    for k, d_table in enumerate(d_tables):
        weight_grad(turned, grads.at[:, k * piece_width : (k + 1) * piece_width], d_table)
    made()
    gain_total = jnp.zeros((1, gain.shape[1]), F32)
    for j in range(CHUNKS):
        rows = rows_at(0, j, chunk)
        back, gain_part = norm_back(trade.take(j), value[rows, :], gain[row : row + 1, :])
        gain_total = gain_total + gain_part
        grad_out[rows, :] = back
        share.put(j, back.astype(BF16))
    d_gain[...] = gain_total
    for j in range(CHUNKS):
        share.arrived(j)
    trade.close()
    share.close()

    def finish(b, _):
        for k in range(3):
            stat_copy(b, k).wait_send()
            sum_copy(b, k).wait_send()
        return 0

    lax.fori_loop(0, blocks, finish, 0)


def back_kernel(
    layer, normed, key_seg, query_seg, resid, w_query, w_out, w_in, gains, noised, clean, steps, counted, counts,
    projected, mixed, middle, normed_two, log_sums, grad_out, branch, d_gain, losses, *refs, carry,
):
    pieces = len(carry.loads) - 1
    d_tables, refs = refs[:pieces], refs[pieces:]
    (result, normed_next, info), refs = refs[:3], refs[3:]
    loss_scratch, layer_refs = refs[:-LAYER_SCRATCH], refs[-LAYER_SCRATCH:]
    me = lax.axis_index(NARROW)
    carry.fetch()
    info[...] = jnp.zeros(info.shape, F32)
    mask = counted[...].astype(F32)
    for row, value in enumerate((noised[...], clean[...], steps[...])):
        info[row : row + 1, :] = value.astype(F32)
    info[3:4, :] = mask / counts[COUNT_ROW : COUNT_ROW + 1, 0:1]
    info[4:5, :] = mask
    greet([{NARROW: lax.rem(me + k, 4)} for k in range(1, 4)] + carry.peers())
    carry.begin(0, 1)

    def at_half():
        carry.begin(2)

    def at_feed():
        carry.fetched()
        carry.end(0)
        carry.hand_on(1)
        carry.begin(3)

    def at_sent():
        carry.leave(0, 1, 2, 3)
        carry.hand_on(2)
        carry.begin(4)

    def at_last():
        carry.hand_on(3)

    forward_part(
        layer,
        [lambda which: w_query[which], lambda: w_out[...], lambda: w_in[...], carry.loads[0].value],
        (at_half, at_feed, at_sent, at_last),
        normed, key_seg, query_seg, resid, gains,
        projected, mixed, middle, normed_two, log_sums, result, normed_next, *layer_refs,
    )
    carry.hand_on(4)
    carry.end(1, 2, 3)
    loss_part(
        2 * layer + 2, normed_next, info, result, gains, carry.loads[1:], grad_out, branch, d_gain, losses, d_tables,
        *loss_scratch, *layer_refs[2:6], *layer_refs[-2:], made=lambda: carry.leave(*range(9, 9 + pieces)),
    )
    carry.gone()


def last_and_loss(
    layer, normed, key_seg, query_seg, resid, w_query, w_out, w_in, gains, tokens, counts, vocab, collective_id, loads
):
    seq_len, width = normed.shape
    heads_width = w_query.shape[2]
    half, blocks = seq_len // 2, seq_len // LANES
    pieces = len(loads) - 1
    return run(
        functools.partial(back_kernel, layer),
        "last_and_loss",
        [normed, key_seg, query_seg, resid, w_query, w_out, w_in, gains, *tokens, counts],
        layer_outs(seq_len, width, heads_width)
        + [
            jax.ShapeDtypeStruct((half, width), F32),
            jax.ShapeDtypeStruct((seq_len, width), BF16),
            jax.ShapeDtypeStruct((1, width), F32),
            jax.ShapeDtypeStruct((1, seq_len), F32),
        ]
        + [jax.ShapeDtypeStruct((width, vocab // pieces), BF16)] * pieces,
        [
            pltpu.VMEM((half, width), F32),
            pltpu.VMEM((seq_len, width), BF16),
            pltpu.VMEM((8, seq_len), F32),
            pltpu.VMEM((seq_len, vocab), F32),
            pltpu.VMEM((seq_len, vocab), BF16),
            pltpu.VMEM((blocks, 2, LANES, LANES), F32),
            pltpu.VMEM((width, seq_len), BF16),
            pltpu.VMEM((blocks, 8, LANES), F32),
            pltpu.VMEM((3, blocks, 8, LANES), F32),
            pltpu.VMEM((blocks, 8, LANES), F32),
            pltpu.VMEM((3, blocks, 8, LANES), F32),
        ]
        + [pltpu.SemaphoreType.DMA((3, blocks))] * 4
        + layer_scratch(seq_len, width, heads_width),
        collective_id,
        loads,
        lazy=(3, 6),
        early=(0, 1, 2, 3) + tuple(range(9, 9 + pieces)),
    )


TAIL_SCRATCH = 22


def end_kernel(points, scale, gain_count, *refs, carry):
    operands, refs = refs[:16], refs[16:]
    (ids_all, losses), refs = refs[:2], refs[2:]
    gain_parts, refs = refs[:gain_count], refs[gain_count:]
    count = len(refs) - 3 - 6 - BACK_SCRATCH - TAIL_SCRATCH
    squares, refs = refs[:count], refs[count:]
    (d_table, d_small, scalars), refs = refs[:3], refs[3:]
    made, refs = refs[:6], refs[6:]
    back_refs, tail_refs = refs[:BACK_SCRATCH], refs[BACK_SCRATCH:]
    me, owners, place = lax.axis_index(WIDE), ids_all.shape[0], lax.axis_index(NARROW)
    peers = [{WIDE: lax.rem(me + step, owners)} for step in range(1, owners)]
    peers += [{NARROW: lax.rem(place + step, 4)} for step in range(1, 4)]
    backward_kernel(0, scale, points, *operands, *made, *back_refs, carry, peers=peers)
    tail_body(
        made[1], ids_all, losses, (made[5], made[4], *gain_parts), squares, d_table, d_small, scalars, *tail_refs, carry
    )


BACK_SCRATCH = 22


def tail_body(
    branch, ids_all, losses, gain_parts, squares,
    d_table, d_small, scalars,
    out_blocks, all_in, masked, picks, total, gains_out, gains_in, blocks, block_in, line_out, line_in,
    near, along,
    wide_send, wide_recv, far_send, far_recv, near_send, near_recv, all_send, all_recv,
    sum_sems,
    carry,
):
    seq_len, width = branch.shape
    quarter, half = seq_len // 4, seq_len // 2
    owners = ids_all.shape[0]
    share, vocab = d_table.shape
    sibling, partner, mine, other = group_places(seq_len)
    place = lax.axis_index(NARROW)
    side = lax.div(place, 2)
    me, slow, fast, slows = wide_places(owners)
    beside = {WIDE: me + 1 - 2 * fast}
    group = near.shape[0]
    first = place * vocab
    around = [lax.rem(me + step, owners) for step in range(owners)]
    at_quarter = pl.multiple_of(mine + side * quarter, quarter)
    held = 2 * lax.rem(place, 2) + side

    def along_way(step):
        return {WIDE: 2 * lax.rem(slow + step, slows) + fast}

    def wide_copy(step):
        return remote(
            out_blocks.at[around[step]], all_in.at[me, held],
            wide_send.at[step], wide_recv.at[step], {WIDE: around[step]},
        )

    def far_copy(step):
        rows = all_in.at[around[step], held]
        return remote(rows, rows, far_send.at[step], far_recv.at[step], partner)

    def near_copy(step):
        rows = all_in.at[around[step], pl.ds(2 * lax.rem(place, 2), 2)]
        return remote(rows, rows, near_send.at[step], near_recv.at[step], sibling)

    def gain_near():
        return remote(gains_out, gains_in, sum_sems.at[0, 0], sum_sems.at[1, 0], sibling)

    def gain_pair(step):
        return remote(
            blocks.at[2 * lax.rem(slow + step, slows) + 1 - fast], block_in.at[step],
            sum_sems.at[2, step], sum_sems.at[3, step], beside,
        )

    def gain_line(step):
        return remote(line_out.at[step], line_in.at[step], sum_sems.at[4, step], sum_sems.at[5, step], along_way(step))

    near_ways = [{NARROW: lax.rem(place + step, group)} for step in range(1, group)]
    gains_out[...] = jnp.zeros(gains_out.shape, F32)
    for row, part in enumerate(gain_parts):
        gains_out[row : row + 1, :] = part[...]
    gain_near().start()
    out_blocks[...] = jnp.transpose(branch[pl.ds(at_quarter, quarter), :]).reshape(out_blocks.shape)
    for step in range(1, owners):
        wide_copy(step).start()
    all_in[me, held] = out_blocks[me]
    carry.hand_on(6, 7)
    gain_near().wait_recv()
    both = gains_out[...] + gains_in[...]
    for owner in range(owners):
        blocks[owner] = lax.dot_general(
            both, feature_places(owner, width, share).astype(F32), (((1,), (1,)), ((), ())),
            precision=lax.Precision.HIGHEST, preferred_element_type=F32,
        )
    for step in range(slows):
        gain_pair(step).start()

    def hand_on(step):
        if step:
            wide_copy(owners - step).wait_recv()
        far_copy(step).start()

    def hand_over(step):
        far_copy(step).wait_recv()
        near_copy(step).start()

    def gather_grad(step, first_turn):
        near_copy(step).wait_recv()
        row = around[step]

        for k in range(seq_len // quarter):
            columns = slice(k * quarter, (k + 1) * quarter)
            high, found = token_parts(ids_all[row, k : k + 1, :], first)
            picks[:, columns] = found
            grads = all_in[row, k]
            for part in range(vocab // LANES):
                inside = jnp.where(high == part, 1.0, 0.0).astype(BF16)
                masked[part * share : (part + 1) * share, columns] = grads * inside
        span = 8 * share

        def some(i, _):
            rows = rows_at(0, i, span)
            part = dot_nt(masked[rows, :], picks[...])
            total[rows, :] = part if first_turn else total[rows, :] + part
            return 0

        lax.fori_loop(0, total.shape[0] // span, some, 0)

    order = [0] + list(range(1, owners))
    for turn in range(owners + 2):
        if turn < owners:
            hand_on(order[turn])
        if 1 <= turn < owners + 1:
            hand_over(order[turn - 1])
        if turn == 1:
            for step in list(range(1, slows)) + [0]:
                gain_pair(step).wait_recv()
                line_out[step] = blocks[2 * lax.rem(slow + step, slows) + fast] + block_in[step]
                if step:
                    gain_line(step).start()
        if turn >= 2:
            gather_grad(order[turn - 2], turn == 2)
    for t in range(vocab // LANES):
        d_table[:, t * LANES : (t + 1) * LANES] = total[t * share : (t + 1) * share, :]
    small = line_out[0]
    for step in range(1, slows):
        gain_line(step).wait_recv()
        small = small + line_in[step]
    d_small[...] = small
    carry.end(*carry.all())
    square = jnp.sum(d_table[...] * d_table[...])
    for part in squares:
        square = square + part[0, 0]
    for load in carry.loads:
        square = square + load.squares[0, 0]
    lead = (place == 0).astype(F32)
    square = square + lead * jnp.sum(small * small)
    lanes = lax.broadcasted_iota(jnp.int32, (8, LANES), 1)
    given = jnp.where(lanes == 0, square, jnp.where(lanes == 1, lead * jnp.sum(losses[...]), 0.0))

    def scalar_near(step):
        return remote(near.at[place], near.at[place], sum_sems.at[6, step], sum_sems.at[7, step], near_ways[step - 1])

    def scalar_wide(step):
        return remote(along.at[me], along.at[me], all_send.at[step], all_recv.at[step], {WIDE: around[step]})

    near[place] = given
    for step in range(1, group):
        scalar_near(step).start()
    for step in range(1, group):
        scalar_near(step).wait()
    along[me] = jnp.sum(near[...], axis=0)
    for step in range(1, owners):
        scalar_wide(step).start()
    for step in range(1, owners):
        scalar_wide(step).wait()
    scalars[...] = jnp.sum(along[...], axis=0)
    gain_near().wait_send()
    for step in range(owners):
        far_copy(step).wait_send()
        near_copy(step).wait_send()
        if step:
            wide_copy(step).wait_send()
    for step in range(slows):
        gain_pair(step).wait_send()
        if step:
            gain_line(step).wait_send()


def first_and_tail(
    points, scale, operands, ids_all, losses, gain_parts, squares, share, vocab, group, collective_id, loads
):
    seq_len, width = operands[5].shape
    hidden, heads_width = operands[3].shape[1], operands[13].shape[2]
    owners = ids_all.shape[0]
    slows = owners // 2
    dma = pltpu.SemaphoreType.DMA
    small = (8, LANES)
    made = [pltpu.VMEM(out.shape, out.dtype) for out in backward_outs(seq_len, width, heads_width, owners)]
    tail_scratch = [
        pltpu.VMEM((owners, share, seq_len // 4), BF16),
        pltpu.VMEM((owners, 4, share, seq_len // 4), BF16),
        pltpu.VMEM((vocab // LANES * share, seq_len), BF16),
        pltpu.VMEM((LANES, seq_len), BF16),
        pltpu.VMEM((vocab // LANES * share, LANES), F32),
        pltpu.VMEM((8, width), F32),
        pltpu.VMEM((8, width), F32),
        pltpu.VMEM((owners,) + small, F32),
        pltpu.VMEM((slows,) + small, F32),
        pltpu.VMEM((slows,) + small, F32),
        pltpu.VMEM((slows,) + small, F32),
        pltpu.VMEM((group,) + small, F32),
        pltpu.VMEM((owners,) + small, F32),
    ]
    tail_scratch += [dma((owners,))] * 8 + [dma((12, max(slows, group)))]
    back = backward_scratch(seq_len, width, hidden, heads_width, owners)
    assert len(back) == BACK_SCRATCH and len(tail_scratch) == TAIL_SCRATCH
    return run(
        functools.partial(end_kernel, points, scale, len(gain_parts)),
        "first_and_tail",
        [*operands, ids_all, losses, *gain_parts, *squares],
        [
            jax.ShapeDtypeStruct((share, vocab), F32),
            jax.ShapeDtypeStruct(small, F32),
            jax.ShapeDtypeStruct(small, F32),
        ],
        made + back + tail_scratch,
        collective_id,
        loads,
        away=AWAY,
        lazy=LAZY,
    )


PIECES = 4
TABLE, ATTN_IN, ATTN_OUT, FFN_IN, FFN_OUT = range(5)


def shares_tile(wide, narrow, noised, attn_out, ffn_in, tables):
    rows, seq_len = noised.shape
    return (
        attn_out.shape[0] == 2
        and narrow == 4
        and wide % 2 == 0
        and rows == 1
        and seq_len % (2 * CHUNKS * 16) == 0
        and SPAN * seq_len == 2 * CHUNKS * QUERY_BLOCK
        and tables.shape[1] * wide % 256 == 0
        and attn_out.shape[1] % 16 == 0
        and attn_out.shape[1] <= LANES
        and ffn_in.shape[2] % 128 == 0
        and tables.shape[1] == attn_out.shape[1]
        and tables.shape[2] % (PIECES * TILE) == 0
    )


def per_device(wide, narrow, *arrays):
    noised, attn_out, ffn_in, tables = arrays[0], arrays[6], arrays[7], arrays[9]
    if shares_tile(wide, narrow, noised, attn_out, ffn_in, tables):
        return tiled_device(wide, *arrays)
    return general_device(*arrays)


def tiled_device(
    wide,
    noised,
    clean,
    timesteps,
    segments,
    counted,
    attn_in,
    attn_out,
    ffn_in,
    ffn_out,
    tables,
    gains,
    attn_in_mean,
    attn_out_mean,
    ffn_in_mean,
    ffn_out_mean,
    tables_mean,
    gains_mean,
    attn_in_square,
    attn_out_square,
    ffn_in_square,
    ffn_out_square,
    tables_square,
    gains_square,
):
    layers = attn_in.shape[0]
    gain_rows, gain_cols = gains.shape
    share, vocab = tables.shape[1:]
    leads = (1, 0, 0, 0)
    four = (attn_in, attn_out, ffn_in, ffn_out)

    def joined(value, lead):
        return value.reshape(value.shape[:lead] + (-1,) + value.shape[lead + 2 :])

    ids = noised.reshape(4, -1)
    steps = timesteps.reshape(-1, LANES)
    half_width = D // 2
    rates = jnp.exp(-math.log(10000.0) * jnp.arange(half_width, dtype=F32) / half_width)[None, :]
    quarter = vocab // PIECES
    windows = [(k * quarter, quarter) for k in range(PIECES)]
    key_seg, query_seg = segments.reshape(-1, 1), segments.reshape(1, -1)
    weights = (attn_in, attn_out, ffn_in, ffn_out)
    (residual, normed, gain_w, counts, ids_all, projected, mixed, middle, normed_two, log_sums, result, normed_next), carried = front(
        ids, counted, gains, steps, rates, tables, key_seg, query_seg, wide, attn_out.shape[2], 0,
        [GatherLoad(value, 0, lead, wide, place=KEPT) for value, lead in zip(weights, leads)]
        + [GatherLoad(value, 1, lead, wide) for value, lead in zip(weights[:3], leads)]
        + [SlowLoad(ffn_out, 1, 0, wide)],
    )
    token_total = counts[gain_rows, 0]
    first_w = [joined(value, lead) for value, lead in zip(carried[:4], leads)]
    query_w, output_w, expand_w = [joined(value, lead) for value, lead in zip(carried[4:7], leads)]
    kept = [(residual, normed, projected, mixed, middle, normed_two, log_sums, *first_w)]
    (projected, mixed, middle, normed_two, log_sums, grad, branch, gain_final, losses, *d_last), (reduce_w,) = last_and_loss(
        1, normed_next, key_seg, query_seg, result, query_w, output_w, expand_w, gain_w,
        (noised, clean, timesteps, counted), counts, vocab, 1,
        [FastLoad(carried[7], 0, wide)]
        + [GatherLoad(tables, 1, 0, wide, window, place=LOCAL) for window in windows],
    )
    kept.append(
        (result, normed_next, projected, mixed, middle, normed_two, log_sums)
        + (query_w, output_w, expand_w, joined(reduce_w, 0))
    )
    own, squares = {}, []

    def by_owner(value, lead):
        shape = value.shape
        return value.reshape(shape[:lead] + (wide, shape[lead] // wide) + shape[lead + 1 :])

    def landed(key, results):
        own[key] = results[0]
        squares.append(results[1])
        return results[2:]

    hidden = ffn_in.shape[2]
    made = jax.ShapeDtypeStruct((wide, share, hidden), BF16)
    made_in = jax.ShapeDtypeStruct((3, wide, share, attn_in.shape[3]), BF16)
    made_out = jax.ShapeDtypeStruct((wide, share, attn_out.shape[2]), BF16)

    def start_last(carry, d_red, d_in):
        carry.loads[PIECES].full, carry.loads[PIECES + 1].full = d_red, d_in
        carry.begin(*range(PIECES))

    half_pieces = PIECES // 2
    points = (
        start_last,
        lambda carry: carry.begin(PIECES, PIECES + 1),
        lambda carry: carry.hand_on(*range(half_pieces)),
        lambda carry: carry.hand_on(*range(half_pieces, PIECES)),
        lambda carry, d_out, d_query: None,
    )
    residual, normed, projected, mixed, middle, normed_two, log_sums, *four_w = kept[1]
    query_w, output_w, expand_w, reduce_w = four_w
    (grad, branch, d_out, d_query, gain_two, gain_one), carried = backward_block(
        1, points,
        [grad, branch, reduce_w, expand_w, output_w, normed_two, middle, gain_w, mixed]
        + [projected, log_sums, key_seg, query_seg, query_w, residual, normed],
        wide, 2,
        [ReduceLoad(by_owner(piece, 0), 0) for piece in d_last]
        + [PairLoad(made, 0, True), PairLoad(made, 0, True)],
    )
    for k in range(PIECES):
        carried = landed((TABLE, k), carried)
    red_sums, in_sums = carried

    def start_first(carry, d_red, d_in):
        carry.loads[4].full, carry.loads[5].full = d_red, d_in
        carry.begin(0, 1, 2, 3)

    def sent_first(carry, d_out, d_query):
        carry.hand_on(5)
        carry.loads[6].full, carry.loads[7].full = d_out, d_query
        carry.begin(6, 7)

    points = (
        start_first,
        lambda carry: carry.begin(4, 5),
        lambda carry: carry.hand_on(2, 3),
        lambda carry: carry.hand_on(4),
        sent_first,
    )
    residual, normed, projected, mixed, middle, normed_two, log_sums, *four_w = kept[0]
    query_w, output_w, expand_w, reduce_w = four_w
    (own_first, total_small, scalars), carried = first_and_tail(
        points, math.sqrt(D),
        [grad, branch, reduce_w, expand_w, output_w, normed_two, middle, gain_w, mixed]
        + [projected, log_sums, key_seg, query_seg, query_w, residual, normed],
        ids_all, losses, (gain_one, gain_two, gain_final), squares, share, vocab, 4, 3,
        [LineLoad(red_sums, wide), LineLoad(in_sums, wide), ReduceLoad(d_out, 0), ReduceLoad(d_query, 1)]
        + [ReduceLoad(made, 0, True), ReduceLoad(made, 0, True), ReduceLoad(made_out, 0, True), ReduceLoad(made_in, 1, True)],
    )
    layer_keys = ((FFN_OUT, 1), (FFN_IN, 1), (ATTN_OUT, 1), (ATTN_IN, 1), (FFN_OUT, 0), (FFN_IN, 0), (ATTN_OUT, 0))
    for key in layer_keys + ((ATTN_IN, 0),):
        carried = landed(key, carried)
    grad_attn_in, grad_attn_out, grad_ffn_in, grad_ffn_out = [
        jnp.stack([own[name, index] for index in range(layers)]) for name in (ATTN_IN, ATTN_OUT, FFN_IN, FFN_OUT)
    ]
    grad_tables = jnp.stack([own_first, jnp.concatenate([own[TABLE, k] for k in range(PIECES)], axis=1)])
    grad_gains = total_small[:gain_rows, :gain_cols]
    total_square, loss_sum = scalars[0, 0], scalars[0, 1]
    grad_norm = jnp.sqrt(total_square)
    factor = jnp.minimum(1.0, CLIP_NORM / (grad_norm + 1e-06))
    results = [loss_sum, token_total, grad_norm]
    for weight, gradient, first, second, decay, rate in (
        (attn_in, grad_attn_in, attn_in_mean, attn_in_square, WEIGHT_DECAY, LEARN_RATE),
        (attn_out, grad_attn_out, attn_out_mean, attn_out_square, WEIGHT_DECAY, LEARN_RATE),
        (ffn_in, grad_ffn_in, ffn_in_mean, ffn_in_square, WEIGHT_DECAY, LEARN_RATE),
        (ffn_out, grad_ffn_out, ffn_out_mean, ffn_out_square, WEIGHT_DECAY, LEARN_RATE),
        (tables, grad_tables, tables_mean, tables_square, WEIGHT_DECAY, LEARN_RATE),
        (gains, grad_gains, gains_mean, gains_square, 0.0, GAIN_RATE),
    ):
        results += adam(weight, factor * gradient, first, second, decay, rate)
    return tuple(results)


def solution(mesh):
    wide, narrow = mesh.shape[WIDE], mesh.shape[NARROW]
    placed = (
        P(WIDE, None),
        P(WIDE, None),
        P(WIDE, None),
        P(WIDE, None),
        P(WIDE, None),
        P(None, None, WIDE, NARROW),
        P(None, WIDE, NARROW),
        P(None, WIDE, NARROW),
        P(None, WIDE, NARROW),
        P(None, WIDE, NARROW),
        P(None, WIDE),
        P(None, None, WIDE, NARROW),
        P(None, WIDE, NARROW),
        P(None, WIDE, NARROW),
        P(None, WIDE, NARROW),
        P(None, WIDE, NARROW),
        P(None, WIDE),
        P(None, None, WIDE, NARROW),
        P(None, WIDE, NARROW),
        P(None, WIDE, NARROW),
        P(None, WIDE, NARROW),
        P(None, WIDE, NARROW),
        P(None, WIDE),
    )
    return jax.shard_map(
        functools.partial(per_device, wide, narrow),
        mesh=mesh,
        in_specs=placed,
        out_specs=(
            P(),
            P(),
            P(),
            P(None, None, WIDE, NARROW),
            P(None, None, WIDE, NARROW),
            P(None, None, WIDE, NARROW),
            P(None, None, WIDE, NARROW),
            P(None, WIDE, NARROW),
            P(None, WIDE, NARROW),
            P(None, WIDE, NARROW),
            P(None, WIDE, NARROW),
            P(None, WIDE, NARROW),
            P(None, WIDE, NARROW),
            P(None, WIDE, NARROW),
            P(None, WIDE, NARROW),
            P(None, WIDE, NARROW),
            P(None, WIDE, NARROW),
            P(None, WIDE, NARROW),
            P(None, WIDE, NARROW),
            P(None, WIDE, NARROW),
            P(None, WIDE, NARROW),
            P(None, WIDE, NARROW),
            P(None, WIDE, NARROW),
            P(None, WIDE),
            P(None, WIDE),
            P(None, WIDE),
            P(None, WIDE),
        ),
        check_vma=False,
    )
```

```python
import functools
import math

import jax
import jax.numpy as jnp
from jax import lax
from jax.experimental import pallas as pl
from jax.experimental.pallas import tpu as pltpu
from jax.sharding import PartitionSpec as P

D = 768
HD = 64
V = 8192
STEPS = 1000
ADAM_STEP = 10


NORM_EPS = 1e-05
LEARN_RATE = 0.05
GAIN_RATE = 0.75
FIRST_DECAY = 0.9
SECOND_DECAY = 0.999
ADAM_EPS = 1e-08
WEIGHT_DECAY = 0.01
CLIP_NORM = 0.005
WIDE, NARROW = "wide", "narrow"


def add_heads(partial_value):
    return lax.psum(partial_value, NARROW)


def back_heads(partial_value):
    return lax.psum(partial_value, NARROW)


def rms_forward(value, gain):
    scale_row = lax.rsqrt(jnp.mean(value * value, axis=-1, keepdims=True) + NORM_EPS)
    return (value * scale_row * gain, scale_row)


def rms_backward(grad, value, scale_row, gain):
    unit = value * scale_row
    scaled = grad * gain
    back = scale_row * (scaled - unit * jnp.mean(scaled * unit, axis=-1, keepdims=True))
    return (back, jnp.sum(grad * unit, axis=0))


def time_features(timestep_row):
    half_width = D // 2
    rates = jnp.exp(-math.log(10000.0) * jnp.arange(half_width, dtype=jnp.float32) / half_width)
    angles = timestep_row.astype(jnp.float32)[:, None] * rates[None, :]
    return jnp.concatenate([jnp.sin(angles), jnp.cos(angles)], axis=1)


def masked_scores(queries, key_rows, segment):
    scores = jnp.einsum(
        "qhd,khd->hqk", queries, key_rows, preferred_element_type=jnp.float32
    ) * HD ** (-0.5)
    return jnp.where((segment[:, None] == segment[None, :])[None], scores, -1e30)


def attend(entry):
    queries, key_rows, values, segment = entry
    scores = masked_scores(queries, key_rows, segment)
    row_top = jnp.max(scores, axis=-1, keepdims=True)
    log_total = row_top + jnp.log(jnp.sum(jnp.exp(scores - row_top), axis=-1, keepdims=True))
    probs = jnp.exp(scores - log_total).astype(jnp.bfloat16)
    mixed = jnp.einsum("hqk,khd->qhd", probs, values, preferred_element_type=jnp.float32)
    return (mixed.astype(jnp.bfloat16), log_total)


def attend_back(entry):
    queries, key_rows, values, segment, log_total, grad_mixed = entry
    probs = jnp.exp(masked_scores(queries, key_rows, segment) - log_total)
    grad_probs = jnp.einsum("qhd,khd->hqk", grad_mixed, values, preferred_element_type=jnp.float32)
    grad_scores = (
        probs * (grad_probs - jnp.sum(probs * grad_probs, axis=-1, keepdims=True))
    ).astype(jnp.bfloat16)
    grad_query = jnp.einsum(
        "hqk,khd->qhd", grad_scores, key_rows, preferred_element_type=jnp.float32
    ) * HD ** (-0.5)
    grad_key = jnp.einsum(
        "hqk,qhd->khd", grad_scores, queries, preferred_element_type=jnp.float32
    ) * HD ** (-0.5)
    grad_value = jnp.einsum(
        "hqk,qhd->khd", probs.astype(jnp.bfloat16), grad_mixed, preferred_element_type=jnp.float32
    )
    return (grad_query, grad_key, grad_value)


def layer_forward(residual, segments, query_w, output_w, expand_w, reduce_w, gain_attn, gain_ffn):
    seq_count, seq_len = segments.shape
    normed, scale_one = rms_forward(residual, gain_attn)
    normed = normed.astype(jnp.bfloat16)
    projected = jnp.einsum(
        "sd,cde->cse", normed, query_w, preferred_element_type=jnp.float32
    ).astype(jnp.bfloat16)
    heads = projected.reshape(3, seq_count, seq_len, -1, HD)
    mixed, log_total = lax.map(attend, (heads[0], heads[1], heads[2], segments))
    mixed = mixed.reshape(seq_count * seq_len, -1)
    middle = residual + add_heads(
        jnp.einsum("se,de->sd", mixed, output_w, preferred_element_type=jnp.float32)
    )
    normed_two, scale_two = rms_forward(middle, gain_ffn)
    normed_two = normed_two.astype(jnp.bfloat16)
    before = jnp.dot(normed_two, expand_w, preferred_element_type=jnp.float32)
    after = jax.nn.gelu(before).astype(jnp.bfloat16)
    result = middle + add_heads(
        jnp.einsum("sf,df->sd", after, reduce_w, preferred_element_type=jnp.float32)
    )
    return (
        result,
        (
            residual,
            scale_one,
            normed,
            projected,
            log_total,
            mixed,
            middle,
            scale_two,
            normed_two,
            before,
            after,
        ),
    )


def layer_backward(
    grad, kept, segments, query_w, output_w, expand_w, reduce_w, gain_attn, gain_ffn
):
    (
        residual,
        scale_one,
        normed,
        projected,
        log_total,
        mixed,
        middle,
        scale_two,
        normed_two,
        before,
        after,
    ) = kept
    seq_count, seq_len = segments.shape
    grad_branch = grad.astype(jnp.bfloat16)
    grad_after = jnp.dot(grad_branch, reduce_w, preferred_element_type=jnp.float32)
    grad_reduce = jnp.einsum("sd,sf->df", grad_branch, after, preferred_element_type=jnp.float32)
    _, gelu_pull = jax.vjp(jax.nn.gelu, before)
    grad_before = gelu_pull(grad_after)[0].astype(jnp.bfloat16)
    grad_expand = jnp.einsum(
        "sd,sf->df", normed_two, grad_before, preferred_element_type=jnp.float32
    )
    grad_normed_two = back_heads(
        jnp.einsum("sf,df->sd", grad_before, expand_w, preferred_element_type=jnp.float32)
    )
    grad_middle, grad_gain_ffn = rms_backward(grad_normed_two, middle, scale_two, gain_ffn)
    grad_middle = grad_middle + grad
    grad_attn = grad_middle.astype(jnp.bfloat16)
    grad_mixed = jnp.dot(grad_attn, output_w, preferred_element_type=jnp.float32).astype(
        jnp.bfloat16
    )
    grad_output = jnp.einsum("sd,se->de", grad_attn, mixed, preferred_element_type=jnp.float32)
    heads = projected.reshape(3, seq_count, seq_len, -1, HD)
    grad_query, grad_key, grad_value = lax.map(
        attend_back,
        (
            heads[0],
            heads[1],
            heads[2],
            segments,
            log_total,
            grad_mixed.reshape(seq_count, seq_len, -1, HD),
        ),
    )
    grad_projected = (
        jnp.stack([grad_query, grad_key, grad_value])
        .reshape(3, seq_count * seq_len, -1)
        .astype(jnp.bfloat16)
    )
    grad_query_w = jnp.einsum(
        "sd,cse->cde", normed, grad_projected, preferred_element_type=jnp.float32
    )
    grad_normed = back_heads(
        jnp.einsum("cse,cde->sd", grad_projected, query_w, preferred_element_type=jnp.float32)
    )
    grad_input, grad_gain_attn = rms_backward(grad_normed, residual, scale_one, gain_attn)
    return (
        grad_input + grad_middle,
        (
            grad_query_w,
            grad_output,
            grad_expand,
            grad_reduce,
            jnp.stack([grad_gain_attn, grad_gain_ffn]),
        ),
    )


def adam(weight, grad, first, second, decay, rate):
    first_new = FIRST_DECAY * first + (1.0 - FIRST_DECAY) * grad
    second_new = SECOND_DECAY * second + (1.0 - SECOND_DECAY) * grad * grad
    first_hat = first_new / (1.0 - FIRST_DECAY**ADAM_STEP)
    second_hat = second_new / (1.0 - SECOND_DECAY**ADAM_STEP)
    weight_new = weight - rate * (first_hat / (jnp.sqrt(second_hat) + ADAM_EPS) + decay * weight)
    return (weight_new, first_new, second_new, weight_new.astype(jnp.bfloat16))


def general_device(
    noised,
    clean,
    timesteps,
    segments,
    counted,
    attn_in,
    attn_out,
    ffn_in,
    ffn_out,
    tables,
    gains,
    attn_in_mean,
    attn_out_mean,
    ffn_in_mean,
    ffn_out_mean,
    tables_mean,
    gains_mean,
    attn_in_square,
    attn_out_square,
    ffn_in_square,
    ffn_out_square,
    tables_square,
    gains_square,
):
    layers = attn_in.shape[0]
    mask = counted.reshape(-1).astype(jnp.float32)
    token_total = lax.psum(jnp.sum(mask), WIDE)
    query_w, output_w, expand_w, reduce_w, table_w, gain_low = (
        lax.all_gather(attn_in.astype(jnp.bfloat16), WIDE, axis=2, tiled=True),
        lax.all_gather(attn_out.astype(jnp.bfloat16), WIDE, axis=1, tiled=True),
        lax.all_gather(ffn_in.astype(jnp.bfloat16), WIDE, axis=1, tiled=True),
        lax.all_gather(ffn_out.astype(jnp.bfloat16), WIDE, axis=1, tiled=True),
        lax.all_gather(tables.astype(jnp.bfloat16), WIDE, axis=1, tiled=True),
        lax.all_gather(gains.astype(jnp.bfloat16), WIDE, axis=1, tiled=True),
    )
    gain_w = gain_low.astype(jnp.float32)
    noised_flat = noised.reshape(-1)
    clean_flat = clean.reshape(-1)
    step_flat = timesteps.reshape(-1)
    vocab_local = table_w.shape[2]
    vocab_ids = lax.axis_index(NARROW) * vocab_local + jnp.arange(vocab_local, dtype=jnp.int32)
    picks = (noised_flat[:, None] == vocab_ids[None, :]).astype(jnp.bfloat16)
    looked = add_heads(
        jnp.einsum("sv,dv->sd", picks, table_w[0], preferred_element_type=jnp.float32)
    )
    residual = math.sqrt(D) * looked + time_features(step_flat)
    kept_layers = []
    for layer_index in range(layers):
        residual, kept = layer_forward(
            residual,
            segments,
            query_w[layer_index],
            output_w[layer_index],
            expand_w[layer_index],
            reduce_w[layer_index],
            gain_w[2 * layer_index],
            gain_w[2 * layer_index + 1],
        )
        kept_layers.append(kept)
    final, scale_final = rms_forward(residual, gain_w[2 * layers])
    final_low = final.astype(jnp.bfloat16)
    logits = jnp.dot(final_low, table_w[1], preferred_element_type=jnp.float32)
    local_top = jnp.max(logits, axis=1)
    row_top = lax.pmax(local_top, NARROW)
    row_total = lax.psum(jnp.sum(jnp.exp(logits - row_top[:, None]), axis=1), NARROW)
    log_probs = logits - (row_top + jnp.log(row_total))[:, None]
    probs = jnp.exp(log_probs)
    clamped = jnp.maximum(step_flat, 2).astype(jnp.float32)[:, None]
    beta = 1.0 / (STEPS - clamped + 1.0)
    retain = (STEPS - clamped + 1.0) / STEPS
    spread = (clamped - 1.0) / (STEPS * V)
    at_noised = (vocab_ids[None, :] == noised_flat[:, None]).astype(jnp.float32)
    at_clean = (vocab_ids[None, :] == clean_flat[:, None]).astype(jnp.float32)
    forward_fac = beta / V + (1.0 - beta) * at_noised
    backward_fac = retain * at_clean + spread
    joint = forward_fac * backward_fac
    marginal = retain * probs + spread
    joint_total, cross, model_total, weighted, aligned, clean_logp = lax.psum(
        (
            jnp.sum(joint, axis=1),
            jnp.sum(joint * (jnp.log(backward_fac) - jnp.log(marginal)), axis=1),
            jnp.sum(forward_fac * marginal, axis=1),
            jnp.sum(probs * joint / marginal, axis=1),
            jnp.sum(forward_fac * probs, axis=1),
            jnp.sum(at_clean * log_probs, axis=1),
        ),
        NARROW,
    )
    divergence = cross / joint_total - jnp.log(joint_total) + jnp.log(model_total)
    first_step = step_flat == 1
    losses = jnp.where(first_step, -clean_logp, divergence)
    pull = retain * (
        -(joint / joint_total[:, None]) / marginal + forward_fac / model_total[:, None]
    )
    centre = retain[:, 0] * (-weighted / joint_total + aligned / model_total)
    grad_kl = probs * (pull - centre[:, None])
    grad_recon = probs - at_clean
    grad_logits = (
        (mask / token_total)[:, None] * jnp.where(first_step[:, None], grad_recon, grad_kl)
    ).astype(jnp.bfloat16)
    grad_table_out = jnp.einsum(
        "sd,sv->dv", final_low, grad_logits, preferred_element_type=jnp.float32
    )
    grad_final = back_heads(
        jnp.einsum("sv,dv->sd", grad_logits, table_w[1], preferred_element_type=jnp.float32)
    )
    grad_x, grad_gain_final = rms_backward(grad_final, residual, scale_final, gain_w[2 * layers])
    layer_grads = [None] * layers
    for layer_index in reversed(range(layers)):
        grad_x, produced = layer_backward(
            grad_x,
            kept_layers[layer_index],
            segments,
            query_w[layer_index],
            output_w[layer_index],
            expand_w[layer_index],
            reduce_w[layer_index],
            gain_w[2 * layer_index],
            gain_w[2 * layer_index + 1],
        )
        layer_grads[layer_index] = produced
    grad_look = (math.sqrt(D) * grad_x).astype(jnp.bfloat16)
    grad_table_in = jnp.einsum("sd,sv->dv", grad_look, picks, preferred_element_type=jnp.float32)
    stacked = [jnp.stack([entry[which] for entry in layer_grads]) for which in range(5)]
    gain_layers = stacked[4].reshape(2 * layers, -1)
    grad_tables_all = jnp.stack([grad_table_in, grad_table_out])
    grad_attn_in, grad_attn_out, grad_ffn_in, grad_ffn_out, grad_tables, grad_gains = (
        lax.psum_scatter(stacked[0], WIDE, scatter_dimension=2, tiled=True),
        lax.psum_scatter(stacked[1], WIDE, scatter_dimension=1, tiled=True),
        lax.psum_scatter(stacked[2], WIDE, scatter_dimension=1, tiled=True),
        lax.psum_scatter(stacked[3], WIDE, scatter_dimension=1, tiled=True),
        lax.psum_scatter(grad_tables_all, WIDE, scatter_dimension=1, tiled=True),
        lax.psum_scatter(
            jnp.concatenate([gain_layers, grad_gain_final[None, :]], axis=0),
            WIDE,
            scatter_dimension=1,
            tiled=True,
        ),
    )
    narrow_first = (lax.axis_index(NARROW) == 0).astype(jnp.float32)
    squares = (
        jnp.sum(grad_attn_in * grad_attn_in)
        + jnp.sum(grad_attn_out * grad_attn_out)
        + jnp.sum(grad_ffn_in * grad_ffn_in)
        + jnp.sum(grad_ffn_out * grad_ffn_out)
        + jnp.sum(grad_tables * grad_tables)
        + narrow_first * jnp.sum(grad_gains * grad_gains)
    )
    squares, loss_sum = lax.psum(
        (squares, narrow_first * jnp.sum(mask * losses)), (WIDE, NARROW)
    )
    grad_norm = jnp.sqrt(squares)
    factor = jnp.minimum(1.0, CLIP_NORM / (grad_norm + 1e-06))
    attn_in_next, attn_in_mean_next, attn_in_square_next, attn_in_copy = adam(
        attn_in, factor * grad_attn_in, attn_in_mean, attn_in_square, WEIGHT_DECAY, LEARN_RATE
    )
    attn_out_next, attn_out_mean_next, attn_out_square_next, attn_out_copy = adam(
        attn_out, factor * grad_attn_out, attn_out_mean, attn_out_square, WEIGHT_DECAY, LEARN_RATE
    )
    ffn_in_next, ffn_in_mean_next, ffn_in_square_next, ffn_in_copy = adam(
        ffn_in, factor * grad_ffn_in, ffn_in_mean, ffn_in_square, WEIGHT_DECAY, LEARN_RATE
    )
    ffn_out_next, ffn_out_mean_next, ffn_out_square_next, ffn_out_copy = adam(
        ffn_out, factor * grad_ffn_out, ffn_out_mean, ffn_out_square, WEIGHT_DECAY, LEARN_RATE
    )
    tables_next, tables_mean_next, tables_square_next, tables_copy = adam(
        tables, factor * grad_tables, tables_mean, tables_square, WEIGHT_DECAY, LEARN_RATE
    )
    gains_next, gains_mean_next, gains_square_next, gains_copy = adam(
        gains, factor * grad_gains, gains_mean, gains_square, 0.0, GAIN_RATE
    )
    return (
        loss_sum,
        token_total,
        grad_norm,
        attn_in_next,
        attn_in_mean_next,
        attn_in_square_next,
        attn_in_copy,
        attn_out_next,
        attn_out_mean_next,
        attn_out_square_next,
        attn_out_copy,
        ffn_in_next,
        ffn_in_mean_next,
        ffn_in_square_next,
        ffn_in_copy,
        ffn_out_next,
        ffn_out_mean_next,
        ffn_out_square_next,
        ffn_out_copy,
        tables_next,
        tables_mean_next,
        tables_square_next,
        tables_copy,
        gains_next,
        gains_mean_next,
        gains_square_next,
        gains_copy,
    )


MESH = pl.DeviceIdType.MESH
SLOW, FAST = 1, 2
HBM, KEPT, LOCAL = 1, 2, 3
F32 = jnp.float32
BF16 = jnp.bfloat16
CHUNKS = 8
SPAN = 4
VMEM_LIMIT = 61 * 1024 * 1024
FORWARD_KIND = BF16
BACKWARD_KIND = BF16


def whole_vmem():
    return pl.BlockSpec(memory_space=pltpu.VMEM)


def dot_nn(a, b):
    return lax.dot_general(a, b, (((1,), (0,)), ((), ())), preferred_element_type=F32)


def dot_nt(a, b):
    return lax.dot_general(a, b, (((1,), (1,)), ((), ())), preferred_element_type=F32)


def remote(src, dst, send_sem, recv_sem, device):
    return pltpu.make_async_remote_copy(
        src_ref=src,
        dst_ref=dst,
        send_sem=send_sem,
        recv_sem=recv_sem,
        device_id=device,
        device_id_type=MESH,
    )


def greet(devices):
    barrier = pltpu.get_barrier_semaphore()
    for device in devices:
        pl.semaphore_signal(barrier, inc=1, device_id=device, device_id_type=MESH)
    pl.semaphore_wait(barrier, len(devices))


def group_places(seq_len):
    me = lax.axis_index(NARROW)
    core = lax.rem(me, 2)
    half = seq_len // 2
    mine = pl.multiple_of(core * half, half)
    other = pl.multiple_of((1 - core) * half, half)
    return ({NARROW: me + 1 - 2 * core}, {NARROW: lax.rem(me + 2, 4)}, mine, other)


class Exchange:
    def __init__(self, refs, sems, base, sibling, partner):
        self.near_out, self.near_in, self.far_out, self.far_in = refs
        self.send, self.recv = sems
        self.base, self.sibling, self.partner = base, sibling, partner

    def near(self, j):
        return remote(
            self.near_out.at[j],
            self.near_in.at[j],
            self.send.at[self.base, j],
            self.recv.at[self.base, j],
            self.sibling,
        )

    def far(self, j):
        return remote(
            self.far_out.at[j],
            self.far_in.at[j],
            self.send.at[self.base + 1, j],
            self.recv.at[self.base + 1, j],
            self.partner,
        )

    def give(self, j, value):
        self.near_out[j] = value.astype(self.near_out.dtype)
        self.near(j).start()

    def give_span(self, k, value):
        chunk = self.near_out.shape[1]
        for i in range(SPAN):
            self.give(SPAN * k + i, value[i * chunk : (i + 1) * chunk, :])

    def pass_on_span(self, k, value):
        chunk = self.near_out.shape[1]
        for i in range(SPAN):
            self.pass_on(SPAN * k + i, value[i * chunk : (i + 1) * chunk, :])

    def pass_on(self, j, value):
        self.near(j).wait_recv()
        self.far_out[j] = (value + self.near_in[j].astype(F32)).astype(self.far_out.dtype)
        self.far(j).start()

    def take(self, j):
        self.far(j).wait_recv()
        return self.far_out[j].astype(F32) + self.far_in[j].astype(F32)

    def close(self):
        for j in range(CHUNKS):
            self.near(j).wait_send()
            self.far(j).wait_send()

    @staticmethod
    def scratch(chunk, width, kind):
        return [
            pltpu.VMEM((CHUNKS, chunk, width), BF16),
            pltpu.VMEM((CHUNKS, chunk, width), BF16),
            pltpu.VMEM((CHUNKS, chunk, width), kind),
            pltpu.VMEM((CHUNKS, chunk, width), kind),
        ]


class Share:
    def __init__(self, ref, sems, base, sibling, mine, chunk):
        self.ref, self.base, self.sibling, self.mine, self.chunk = ref, base, sibling, mine, chunk
        self.send, self.recv = sems

    def piece(self, j):
        rows = self.ref.at[pl.ds(pl.multiple_of(self.mine + j * self.chunk, self.chunk), self.chunk)]
        return remote(rows, rows, self.send.at[self.base, j], self.recv.at[self.base, j], self.sibling)

    def put(self, j, value):
        self.ref[pl.ds(pl.multiple_of(self.mine + j * self.chunk, self.chunk), self.chunk), :] = value
        self.piece(j).start()

    def arrived(self, j):
        self.piece(j).wait_recv()

    def close(self):
        for j in range(CHUNKS):
            self.piece(j).wait_send()


def wide_places(count):
    me = lax.axis_index(WIDE)
    fast = lax.rem(me, 2)
    slow = me // 2
    return (me, slow, fast, count // 2)


class Carry:
    def __init__(self, loads, fetches, leaves):
        self.loads, self.fetches, self.leaves = loads, fetches, leaves
        self.left = []

    def fetch(self):
        for copy in self.fetches:
            copy.start()

    def fetched(self):
        for copy in self.fetches:
            copy.wait()

    def leave(self, *which):
        for k in which:
            self.leaves[k].start()
            self.left.append(k)

    def gone(self):
        self.leave(*[k for k in self.leaves if k not in self.left])
        for k in self.left:
            self.leaves[k].wait()

    def peers(self):
        ways = []
        for load in self.loads:
            ways += [way for way in load.ways if way not in ways]
        me, slow, fast, slows = wide_places(self.loads[0].count) if self.loads else (0, 0, 0, 0)
        found = []
        if SLOW in ways:
            found += [{WIDE: 2 * lax.rem(slow + step, slows) + fast} for step in range(1, slows)]
        if FAST in ways:
            found.append({WIDE: me + 1 - 2 * fast})
        return found

    def begin(self, *which):
        for k in which:
            self.loads[k].start()

    def hand_on(self, *which):
        for k in which:
            self.loads[k].relay()

    def end(self, *which):
        for k in which:
            self.loads[k].finish()

    def all(self):
        return range(len(self.loads))


def part_of(weights, index, window):
    shape = weights.shape[1:]
    return shape if window is None else shape[:-1] + (window[1],)


class SlowLoad:
    ways = (SLOW,)

    def __init__(self, weights, index, lead, count, window=None):
        self.index, self.lead, self.count, self.window = index, lead, count, window
        shape, slows = part_of(weights, index, window), count // 2
        self.operands, self.in_specs = [weights], [whole_vmem()]
        self.outs = [jax.ShapeDtypeStruct((slows,) + shape, BF16)]
        self.out_specs = [pl.BlockSpec(memory_space=pl.ANY)]
        self.scratch = [pltpu.VMEM(shape, BF16), pltpu.SemaphoreType.DMA] + [pltpu.SemaphoreType.DMA((slows,))] * 2

    def bind(self, given, out, scratch):
        self.shard, self.out = given[0], out[0]
        self.low, self.local, self.send, self.recv = scratch
        self.me, self.slow, self.fast, self.slows = wide_places(self.count)

    def cast(self):
        if self.window is None:
            self.low[...] = self.shard[self.index].astype(BF16)
        else:
            self.low[...] = self.shard[self.index, :, self.window[0] : self.window[0] + self.window[1]].astype(BF16)

    def target(self):
        return self.out.at[self.slow]

    def slow_copy(self, step):
        return remote(
            self.low, self.target(), self.send.at[step], self.recv.at[step],
            {WIDE: 2 * lax.rem(self.slow + step, self.slows) + self.fast},
        )

    def own_copy(self):
        return pltpu.make_async_copy(self.low, self.target(), self.local)

    def start(self):
        self.cast()
        for step in range(1, self.slows):
            self.slow_copy(step).start()
        self.own_copy().start()

    def finish(self):
        for step in range(1, self.slows):
            self.slow_copy(step).wait()
        self.own_copy().wait()


class FastLoad:
    ways = (FAST,)

    def __init__(self, blocks, lead, count):
        self.lead, self.count = lead, count
        shape, slows = blocks.shape[1:], count // 2
        self.operands, self.in_specs = [blocks], [pl.BlockSpec(memory_space=pl.ANY)]
        self.outs = [jax.ShapeDtypeStruct(shape[:lead] + (count,) + shape[lead:], BF16)]
        self.out_specs = [whole_vmem()]
        self.scratch = [pltpu.SemaphoreType.DMA((slows,))] * 3

    def value(self):
        return self.out[...].reshape((-1, self.out.shape[-1]))

    def bind(self, given, out, scratch):
        self.blocks, self.out = given[0], out[0]
        self.local, self.send, self.recv = scratch
        self.me, self.slow, self.fast, self.slows = wide_places(self.count)

    def copies(self, step):
        target = self.out.at[(slice(None),) * self.lead + (2 * step + self.fast,)]
        return (
            remote(
                self.blocks.at[step], target, self.send.at[step], self.recv.at[step],
                {WIDE: self.me + 1 - 2 * self.fast},
            ),
            pltpu.make_async_copy(self.blocks.at[step], target, self.local.at[step]),
        )

    def start(self):
        for step in range(self.slows):
            for copy in self.copies(step):
                copy.start()

    def finish(self):
        for step in range(self.slows):
            for copy in self.copies(step):
                copy.wait()


class GatherLoad(SlowLoad):
    ways = (SLOW, FAST)

    def __init__(self, weights, index, lead, count, window=None, place=HBM):
        super().__init__(weights, index, lead, count, window)
        shape, slows = part_of(weights, index, window), count // 2
        whole = shape[:lead] + (count,) + shape[lead:]
        self.outs = [jax.ShapeDtypeStruct(whole, BF16)]
        self.scratch = self.scratch + [pltpu.SemaphoreType.DMA((slows,))] * 2
        if place == KEPT:
            self.out_specs = [whole_vmem()]
        self.local_out = place == LOCAL
        if self.local_out:
            self.outs, self.out_specs = [], []
            self.scratch = self.scratch + [pltpu.VMEM(whole, BF16)]

    def bind(self, given, out, scratch):
        if self.local_out:
            out, scratch = scratch[-1:], scratch[:-1]
        super().bind(given, out, scratch[:-2])
        self.fast_send, self.fast_recv = scratch[-2:]

    def value(self, *index):
        found = self.out[index] if index else self.out[...]
        return found.reshape((-1, found.shape[-1]))

    def at(self, owner):
        return self.out.at[(slice(None),) * self.lead + (owner,)]

    def target(self):
        return self.at(self.me)

    def fast_copy(self, step):
        block = self.at(2 * lax.rem(self.slow + self.slows - step, self.slows) + self.fast)
        return remote(
            self.low if step == 0 else block, block, self.fast_send.at[step], self.fast_recv.at[step],
            {WIDE: self.me + 1 - 2 * self.fast},
        )

    def start(self):
        super().start()
        self.fast_copy(0).start()

    def relay(self):
        for step in range(1, self.slows):
            self.slow_copy(step).wait_recv()
            self.fast_copy(step).start()

    def finish(self):
        for step in range(self.slows):
            self.fast_copy(step).wait()
            if step:
                self.slow_copy(step).wait_send()
        self.own_copy().wait()


class PairLoad:
    ways = (FAST,)

    def __init__(self, full, lead, inside=False):
        self.lead, self.count, self.inside = lead, full.shape[lead], inside
        self.shape, self.slows = full.shape[:lead] + full.shape[lead + 1 :], self.count // 2
        self.operands, self.in_specs = ([], []) if inside else ([full], [whole_vmem()])
        self.outs, self.out_specs = [jax.ShapeDtypeStruct((self.slows,) + self.shape, BF16)], [whole_vmem()]
        self.scratch = [pltpu.VMEM((self.slows,) + self.shape, BF16)] + [pltpu.SemaphoreType.DMA((self.slows,))] * 2

    def bind(self, given, out, scratch):
        self.full = None if self.inside else given[0]
        self.out = out[0]
        self.came, self.send, self.recv = scratch
        self.me, self.slow, self.fast, self.slows = wide_places(self.count)

    def block(self, step, fast):
        owner = 2 * lax.rem(self.slow + step, self.slows) + fast
        return self.full.at[(slice(None),) * self.lead + (owner,)]

    def copy(self, step):
        return remote(
            self.block(step, 1 - self.fast), self.came.at[step], self.send.at[step], self.recv.at[step],
            {WIDE: self.me + 1 - 2 * self.fast},
        )

    def start(self):
        for step in list(range(1, self.slows)) + [0]:
            self.copy(step).start()

    def finish(self):
        for step in range(self.slows):
            self.copy(step).wait()
            total = self.block(step, self.fast)[...].astype(F32) + self.came[step].astype(F32)
            self.out[step] = total.astype(BF16)


class ReduceLoad(PairLoad):
    ways = (SLOW, FAST)

    def __init__(self, full, lead, inside=False):
        super().__init__(full, lead, inside)
        self.outs = [jax.ShapeDtypeStruct(self.shape, F32), jax.ShapeDtypeStruct((8, 128), F32)]
        self.out_specs = [whole_vmem()] * 2
        self.scratch = (
            self.scratch
            + [pltpu.VMEM((self.slows - 1,) + self.shape, BF16)]
            + [pltpu.SemaphoreType.DMA((self.slows,))] * 2
        )

    def bind(self, given, out, scratch):
        super().bind(given, out[:1], scratch[:3])
        self.squares = out[1]
        self.landed, self.line_send, self.line_recv = scratch[3:]

    def line_copy(self, step):
        return remote(
            self.came.at[step], self.landed.at[step - 1], self.line_send.at[step], self.line_recv.at[step],
            {WIDE: 2 * lax.rem(self.slow + step, self.slows) + self.fast},
        )

    def relay(self):
        for step in list(range(1, self.slows)) + [0]:
            self.copy(step).wait()
            total = self.block(step, self.fast)[...].astype(F32) + self.came[step].astype(F32)
            self.came[step] = total.astype(BF16)
            if step:
                self.line_copy(step).start()

    def finish(self):
        total = self.came[0].astype(F32)
        for step in range(1, self.slows):
            self.line_copy(step).wait()
            total = total + self.landed[step - 1].astype(F32)
        self.out[...] = total
        self.squares[...] = jnp.full(self.squares.shape, jnp.sum(total * total), F32)


class LineLoad:
    ways = (SLOW,)

    def __init__(self, sums, count):
        self.count = count
        slows = count // 2
        self.operands, self.in_specs = [sums], [whole_vmem()]
        self.outs = [jax.ShapeDtypeStruct(sums.shape[1:], F32), jax.ShapeDtypeStruct((8, 128), F32)]
        self.out_specs = [whole_vmem()] * 2
        self.scratch = [pltpu.VMEM(sums.shape, BF16)] + [pltpu.SemaphoreType.DMA((slows,))] * 2

    def bind(self, given, out, scratch):
        self.sums, (self.out, self.squares) = given[0], out
        self.came, self.send, self.recv = scratch
        self.me, self.slow, self.fast, self.slows = wide_places(self.count)

    def copy(self, step):
        return remote(
            self.sums.at[step], self.came.at[step], self.send.at[step], self.recv.at[step],
            {WIDE: 2 * lax.rem(self.slow + step, self.slows) + self.fast},
        )

    def start(self):
        for step in range(1, self.slows):
            self.copy(step).start()

    def finish(self):
        total = self.sums[0].astype(F32)
        for step in range(1, self.slows):
            self.copy(step).wait()
            total = total + self.came[step].astype(F32)
        self.out[...] = total
        self.squares[...] = jnp.full(self.squares.shape, jnp.sum(total * total), F32)


def run(body, name, operands, outs, scratch, collective_id=None, loads=(), away=(), lazy=(), early=()):
    any_place = pl.BlockSpec(memory_space=pl.ANY)
    given, taken = list(operands), []
    in_specs = [any_place if k in away or k in lazy else whole_vmem() for k in range(len(operands))]
    for load in loads:
        places = []
        for operand, spec in zip(load.operands, load.in_specs):
            known = [k for k, other in enumerate(given) if other is operand]
            if not known:
                known = [len(given)]
                given.append(operand)
                in_specs.append(spec)
            places.append(known[0])
        taken.append(places)
    moved = [operands[k] for k in lazy] + [outs[k] for k in early]
    counts = [len(given), len(outs)] + [len(load.outs) for load in loads]
    counts += [len(scratch)] + [len(load.scratch) for load in loads] + [len(moved), len(moved)]
    parts = 1 + len(loads)

    def kernel(*refs):
        groups, place = [], 0
        for count in counts:
            groups.append(refs[place : place + count])
            place += count
        for k, load in enumerate(loads):
            load.bind([groups[0][p] for p in taken[k]], groups[2 + k], groups[2 + parts + k])
        mine, results = list(groups[0][: len(operands)]), list(groups[1])
        fetches, leaves = [], {}
        for k, buffer, sem in zip(lazy, groups[-2], groups[-1]):
            fetches.append(pltpu.make_async_copy(mine[k], buffer, sem))
            mine[k] = buffer
        for k, buffer, sem in zip(early, groups[-2][len(lazy) :], groups[-1][len(lazy) :]):
            leaves[k] = pltpu.make_async_copy(buffer, results[k], sem)
            results[k] = buffer
        body(*mine, *results, *groups[1 + parts], carry=Carry(list(loads), fetches, leaves))

    results = pl.pallas_call(
        kernel,
        out_shape=tuple(outs) + tuple(out for load in loads for out in load.outs),
        in_specs=in_specs,
        out_specs=tuple(any_place if k in early else whole_vmem() for k in range(len(outs)))
        + tuple(spec for load in loads for spec in load.out_specs),
        scratch_shapes=list(scratch)
        + [s for load in loads for s in load.scratch]
        + [pltpu.VMEM(value.shape, value.dtype) for value in moved]
        + [pltpu.SemaphoreType.DMA] * len(moved),
        compiler_params=pltpu.CompilerParams(
            collective_id=collective_id,
            has_side_effects=collective_id is not None,
            vmem_limit_bytes=VMEM_LIMIT,
        ),
        name=name,
    )(*given)
    return results[: len(outs)], results[len(outs) :]


def sems(kinds):
    return [pltpu.SemaphoreType.DMA((kinds, CHUNKS)), pltpu.SemaphoreType.DMA((kinds, CHUNKS))]


def norm_of(value, gain):
    scale = lax.rsqrt(jnp.mean(value * value, axis=-1, keepdims=True) + NORM_EPS)
    return value * scale * gain


def norm_back(grad, value, gain):
    scale = lax.rsqrt(jnp.mean(value * value, axis=-1, keepdims=True) + NORM_EPS)
    unit = value * scale
    scaled = grad * gain
    back = scale * (scaled - unit * jnp.mean(scaled * unit, axis=-1, keepdims=True))
    return (back, jnp.sum(grad * unit, axis=0, keepdims=True))


GELU_A = math.sqrt(2.0 / math.pi)
GELU_B = 0.044715


def gelu_of(x):
    return 0.5 * x * (1.0 + jnp.tanh(GELU_A * (x + GELU_B * (x * x * x))))


def gelu_slope(x):
    square = x * x
    t = jnp.tanh(GELU_A * (x + GELU_B * (x * square)))
    return 0.5 * (1.0 + t) + 0.5 * x * (1.0 - t * t) * (GELU_A * (1.0 + 3.0 * GELU_B * square))


def rows_at(start, j, chunk):
    return pl.ds(pl.multiple_of(start + j * chunk, chunk), chunk)


LANES = 128
SUB = 64


def spread(row):
    return jnp.transpose(jnp.broadcast_to(row, (LANES, LANES)))


def feature_places(owner, width, share):
    lane = lax.broadcasted_iota(jnp.int32, (LANES, width), 0)
    feature = lax.broadcasted_iota(jnp.int32, (LANES, width), 1)
    return ((feature == lane + owner * share) & (lane < share)).astype(F32).astype(BF16)


def token_parts(ids, first):
    here = ids - first
    high = lax.shift_right_arithmetic(here, 7)
    place = lax.broadcasted_iota(jnp.int32, (LANES, ids.shape[1]), 0)
    return high, jnp.where(place == here - high * LANES, 1.0, 0.0).astype(BF16)


def embed_part(
    ids, counted, gains, steps, rates, table,
    resid, normed, gain_all, count_all, ids_all,
    low, extra, small, near_out, near_in, own, far_out, far_in, wide_out, wide_in, part_out, part_in,
    id_send, id_recv, small_send, small_recv, near_send, near_recv, far_send, far_recv, wide_send, wide_recv,
    part_send, part_recv, send, recv, carry,
):
    seq_len, width = normed.shape
    chunk = seq_len // 2 // CHUNKS
    quarter = seq_len // 4
    share, vocab = table.shape[1:]
    owners = ids_all.shape[0]
    sibling, partner, mine, other = group_places(seq_len)
    place = lax.axis_index(NARROW)
    side = lax.div(place, 2)
    me = lax.axis_index(WIDE)
    first = place * vocab
    around = [lax.rem(me + step, owners) for step in range(owners)]

    def id_copy(step):
        return remote(ids_all.at[me], ids_all.at[me], id_send.at[step], id_recv.at[step], {WIDE: around[step]})

    def small_copy(step):
        return remote(small.at[me], small.at[me], small_send.at[step], small_recv.at[step], {WIDE: around[step]})

    def near_copy(step):
        return remote(near_out.at[step], near_in.at[step], near_send.at[step], near_recv.at[step], sibling)

    def far_copy(step):
        return remote(far_out.at[step], far_in.at[step], far_send.at[step], far_recv.at[step], partner)

    def wide_copy(step):
        return remote(wide_out.at[step], wide_in.at[me], wide_send.at[step], wide_recv.at[step], {WIDE: around[step]})

    def part_copy(piece):
        rows = pl.ds(piece * LANES, LANES)
        return remote(part_out.at[rows], part_in.at[rows], part_send.at[piece], part_recv.at[piece], partner)

    ids_all[me] = ids[...]
    small[me] = jnp.zeros(small.shape[1:], F32)
    small[me, : gains.shape[0], : gains.shape[1]] = gains[...].astype(BF16).astype(F32)
    count = jnp.sum(counted[...].astype(F32), keepdims=True)
    small[me, COUNT_ROW : COUNT_ROW + 1, :] = jnp.broadcast_to(count, (1, small.shape[2]))
    greet([{WIDE: device} for device in around[1:]] + [sibling, partner])
    for step in range(1, owners):
        id_copy(step).start()
    for step in range(1, owners):
        small_copy(step).start()
    carry.begin(0, 1)
    parts = vocab // LANES
    for part in range(parts):
        low[part * share : (part + 1) * share, :] = table[0, :, part * LANES : (part + 1) * LANES].astype(BF16)
    core = lax.rem(place, 2)

    def look_up(step):
        row = lax.rem(me + step, owners)

        def find(which):
            high, picks = token_parts(ids_all[row, pl.ds(which, 1), :], first)
            found = dot_nn(low[...], picks)
            total = jnp.zeros((share, quarter), F32)
            for part in range(parts):
                total = total + jnp.where(high == part, found[part * share : (part + 1) * share, :], 0.0)
            return total.astype(BF16)

        for k in range(2):
            near_out[step, k] = find(2 * (1 - core) + k)
        near_copy(step).start()
        for k in range(2):
            own[step, k] = find(2 * core + k)

    def halve(step):
        near_copy(step).wait_recv()
        own[step] = own[step] + near_in[step]
        far_out[step] = own[step, 1 - side]
        far_copy(step).start()

    def deliver(step):
        far_copy(step).wait_recv()
        total = own[step, side] + far_in[step]
        if step % owners == 0:
            wide_in[me] = total
        else:
            wide_out[step] = total
            wide_copy(step).start()

    order = list(range(1, owners)) + [0]
    for turn in range(owners + 2):
        if turn < owners:
            if order[turn]:
                id_copy(owners - order[turn]).wait_recv()
            look_up(order[turn])
        if 1 <= turn < owners + 1:
            halve(order[turn - 1])
        if turn >= 2:
            deliver(order[turn - 2])
    carry.begin(2, 3)
    carry.hand_on(0, 1)
    for step in range(1, owners):
        small_copy(step).wait_recv()
    total = None
    for owner in range(owners):
        part = dot_nn(small[owner].astype(BF16), feature_places(owner, width, share))
        total = part if total is None else total + part
    gain_all[...] = total
    count_all[...] = jnp.sum(small[...], axis=0)
    half_width = width // 2
    for k in range(seq_len // 2 // LANES):
        when = spread(steps[pl.ds(mine // LANES + k, 1), :].astype(F32))
        for t in range(half_width // LANES):
            columns = slice(t * LANES, (t + 1) * LANES)
            angles = when * rates[:, columns]
            rows = slice(k * LANES, (k + 1) * LANES)
            extra[rows, t * LANES : (t + 1) * LANES] = jnp.sin(angles)
            extra[rows, half_width + t * LANES : half_width + (t + 1) * LANES] = jnp.cos(angles)
    for step in range(1, owners):
        wide_copy(step).wait_recv()
    found = jnp.transpose(wide_in[...].reshape(width, quarter))
    pieces = quarter // LANES
    at_side = pl.multiple_of(side * quarter, quarter)
    at_other = pl.multiple_of((1 - side) * quarter, quarter)
    for piece in range(pieces):
        rows = pl.ds(piece * LANES, LANES)
        part_out[rows, :] = found[piece * LANES : (piece + 1) * LANES, :]
        part_copy(piece).start()

    def finish(start, source, piece):
        rows = rows_at(start, piece, LANES)
        x = math.sqrt(width) * source[pl.ds(piece * LANES, LANES), :].astype(F32) + extra[rows, :]
        resid[rows, :] = x
        here = rows_at(mine + start, piece, LANES)
        normed[here, :] = norm_of(x, gain_all[0:1, :]).astype(BF16)
        give_rows(here, piece if source is part_out else pieces + piece).start()

    def give_rows(here, k):
        return remote(normed.at[here], normed.at[here], send.at[0, k], recv.at[0, k], sibling)

    for piece in range(pieces):
        finish(at_side, part_out, piece)
    for piece in range(pieces):
        part_copy(piece).wait_recv()
        finish(at_other, part_in, piece)
    carry.hand_on(2)
    for k in range(2 * pieces):
        give_rows(rows_at(mine, k % pieces, LANES), k).wait()
    for step in range(owners):
        near_copy(step).wait_send()
        far_copy(step).wait_send()
        if step:
            id_copy(step).wait_send()
            small_copy(step).wait_send()
            wide_copy(step).wait_send()
    for piece in range(pieces):
        part_copy(piece).wait_send()


QUERY_BLOCK = 256


def forward_part(
    layer, weights, points, normed, key_seg, query_seg, resid, gains,
    projected, mixed, middle, normed_two, log_sums, result, normed_next,
    bias, values_t, near_out, near_in, far_out, far_in, near_out2, near_in2, far_out2, far_in2, send, recv,
):
    w_query, w_out, w_in, w_red = weights
    at_half, at_feed, at_sent, at_last = points
    seq_len, width = normed.shape
    chunk = seq_len // 2 // CHUNKS
    block = bias.shape[1]
    heads = mixed.shape[1] // HD
    sibling, partner, mine, other = group_places(seq_len)
    pair = (send, recv)
    first = Exchange((near_out, near_in, far_out, far_in), pair, 0, sibling, partner)
    second = Exchange((near_out2, near_in2, far_out2, far_in2), pair, 2, sibling, partner)
    share = Share(normed_two, pair, 4, sibling, mine, chunk)
    share_next = Share(normed_next, pair, 5, sibling, mine, chunk)

    def ask(i, _):
        rows = rows_at(0, i, block)
        for which in range(3):
            projected[which, rows, :] = dot_nn(normed[rows, :], w_query(which)).astype(BF16)
        return 0

    lax.fori_loop(0, seq_len // block, ask, 0)
    values_t[...] = jnp.transpose(projected[2])

    def attend_rows(start):
        rows = pl.ds(pl.multiple_of(start, block), block)
        bias[...] = jnp.where(key_seg[...] == query_seg[:, rows], 0.0, -1e30)
        asked = projected[0, rows, :] * HD ** (-0.5)
        parts = []
        for head in range(heads):
            scores = dot_nt(projected[1], head_lanes(asked, head, HD)) + bias[...]
            top = jnp.max(scores, axis=0, keepdims=True)
            powers = jnp.exp(scores - top)
            total = jnp.sum(powers, axis=0, keepdims=True)
            log_sums[head : head + 1, rows] = top + jnp.log(total)
            probs = (powers * (1.0 / total)).astype(BF16)
            parts.append(dot_nn(values_t[head * HD : (head + 1) * HD, :], probs))
        mixed[rows, :] = jnp.transpose(jnp.concatenate(parts, axis=0)).astype(BF16)

    def project(start, k):
        return dot_nt(mixed[rows_at(start, k, SPAN * chunk), :], w_out())

    def feed(rows):
        pre = dot_nn(normed_two[rows, :], w_in())
        return dot_nt(gelu_of(pre).astype(BF16), w_red())

    for part in range(CHUNKS // SPAN):

        def both(i, _):
            attend_rows(jnp.where(i == 0, other, mine) + part * block)
            return 0

        lax.fori_loop(0, 2, both, 0)
        first.give_span(part, project(other, part))
        if part == 0:
            at_half()
        first.pass_on_span(part, project(mine, part))
    at_feed()
    for k in range(CHUNKS // SPAN):
        for j in range(SPAN * k, SPAN * (k + 1)):
            rows = rows_at(0, j, chunk)
            mid = resid[rows, :] + first.take(j)
            middle[rows, :] = mid
            share.put(j, norm_of(mid, gains[2 * layer + 1 : 2 * layer + 2, :]).astype(BF16))
        kept = feed(rows_at(mine, k, SPAN * chunk))
        for j in range(SPAN * k, SPAN * (k + 1)):
            share.arrived(j)
        second.give_span(k, feed(rows_at(other, k, SPAN * chunk)))
        second.pass_on_span(k, kept)
    at_sent()
    for j in range(CHUNKS):
        rows = rows_at(0, j, chunk)
        x = middle[rows, :] + second.take(j)
        result[rows, :] = x
        share_next.put(j, norm_of(x, gains[2 * layer + 2 : 2 * layer + 3, :]).astype(BF16))
        if j == CHUNKS // 2 - 1:
            at_last()
    for j in range(CHUNKS):
        share_next.arrived(j)
    for part in (first, second, share, share_next):
        part.close()


def layer_outs(seq_len, width, heads_width):
    return [
        jax.ShapeDtypeStruct((3, seq_len, heads_width), BF16),
        jax.ShapeDtypeStruct((seq_len, heads_width), BF16),
        jax.ShapeDtypeStruct((seq_len // 2, width), F32),
        jax.ShapeDtypeStruct((seq_len, width), BF16),
        jax.ShapeDtypeStruct((8, seq_len), F32),
    ]


def layer_scratch(seq_len, width, heads_width):
    half, chunk = seq_len // 2, seq_len // 2 // CHUNKS
    block = SPAN * chunk
    return (
        [pltpu.VMEM((seq_len, block), F32), pltpu.VMEM((heads_width, seq_len), BF16)]
        + Exchange.scratch(chunk, width, FORWARD_KIND)
        + Exchange.scratch(chunk, width, FORWARD_KIND)
        + sems(6)
    )


LAYER_SCRATCH = 12
COUNT_ROW = 5


def front_kernel(
    ids, counted, gains, steps, rates, table, key_seg, query_seg,
    resid, normed, gain_all, count_all, ids_all, projected, mixed, middle, normed_two, log_sums, result, normed_next,
    *scratch, carry,
):
    embed_part(
        ids, counted, gains, steps, rates, table, resid, normed, gain_all, count_all, ids_all,
        *scratch[:-LAYER_SCRATCH], carry,
    )
    carry.end(0, 1)
    later = list(carry.all())[4:]

    def at_half():
        carry.hand_on(3)
        carry.begin(*later[:2])

    def at_feed():
        carry.end(2, 3)
        carry.begin(*later[2:])
        carry.leave(0, 1, 5, 6)

    def at_sent():
        carry.hand_on(*later[:2])
        carry.leave(7, 8)

    forward_part(
        0,
        [carry.loads[0].value] + [load.value for load in carry.loads[1:4]],
        (at_half, at_feed, at_sent, lambda: carry.hand_on(*later[2:3])),
        normed, key_seg, query_seg, resid, gain_all,
        projected, mixed, middle, normed_two, log_sums, result, normed_next, *scratch[-LAYER_SCRATCH:],
    )
    carry.end(*later)
    carry.gone()


def front(ids, counted, gains, steps, rates, tables, key_seg, query_seg, owners, heads_width, collective_id, loads):
    seq_len = ids.size
    share, vocab = tables.shape[1:]
    half, width = seq_len // 2, owners * share
    dma = pltpu.SemaphoreType.DMA
    return run(
        front_kernel,
        "front",
        [ids, counted, gains, steps, rates, tables, key_seg, query_seg],
        [
            jax.ShapeDtypeStruct((half, width), F32),
            jax.ShapeDtypeStruct((seq_len, width), BF16),
            jax.ShapeDtypeStruct((8, width), F32),
            jax.ShapeDtypeStruct((8, LANES), F32),
            jax.ShapeDtypeStruct((owners,) + ids.shape, jnp.int32),
        ]
        + layer_outs(seq_len, width, heads_width)
        + [jax.ShapeDtypeStruct((half, width), F32), jax.ShapeDtypeStruct((seq_len, width), BF16)],
        [
            pltpu.VMEM((vocab // LANES * share, LANES), BF16),
            pltpu.VMEM((half, width), F32),
            pltpu.VMEM((owners, 8, LANES), F32),
        ]
        + [pltpu.VMEM((owners, 2, share, half // 2), BF16)] * 3
        + [pltpu.VMEM((owners, share, half // 2), BF16)] * 4
        + [
            pltpu.VMEM((half // 2, width), BF16),
            pltpu.VMEM((half // 2, width), BF16),
        ]
        + [dma((owners,))] * 10
        + [dma((half // 2 // LANES,))] * 2
        + [dma((1, half // LANES))] * 2
        + layer_scratch(seq_len, width, heads_width),
        collective_id,
        loads,
        early=(0, 1, 5, 6, 7, 8),
    )


TILE = 256


def weight_grad(left_t, right, out):
    columns = right.shape[1]
    tile = TILE if columns % TILE == 0 else columns

    def put(where):
        value = dot_nn(left_t[...], right[:, where]).astype(out.dtype)
        if len(out.shape) == 3:
            out[:, :, where] = value.reshape(out.shape[:2] + (tile,))
        else:
            out[:, where] = value

    def step(i, _):
        put(pl.ds(pl.multiple_of(i * tile, tile), tile))
        return 0

    if tile == columns:
        put(slice(None))
    else:
        lax.fori_loop(0, columns // tile, step, 0)


def head_lanes(value, head, size):
    lanes = lax.broadcasted_iota(jnp.int32, value.shape, 1)
    inside = (lanes >= head * size) & (lanes < (head + 1) * size)
    return jnp.where(inside, value, jnp.zeros_like(value))


def backward_kernel(
    layer, scale, points, grad, branch, w_red, w_in, w_out, normed_two, middle, gains, mixed,
    projected, log_sums, key_seg, query_seg, w_query, resid, normed,
    grad_out, branch_out, d_out, d_query, gain_two, gain_one,
    d_red, d_in, grad_middle, grad_attn, grad_mixed, grad_projected, grad_before, after, turned,
    bias, keys_t, grad_keys, grad_values,
    near_out, near_in, far_out, far_in, far_out2, far_in2, send, recv, loaded, carry, peers=None,
):
    at_start, at_made, at_summed, at_attended, at_sent = points
    seq_len, width = normed_two.shape
    chunk = seq_len // 2 // CHUNKS
    sibling, partner, mine, other = group_places(seq_len)
    carry.fetch()
    greet([sibling, partner] + carry.peers() if peers is None else peers)
    at_start(carry, d_red, d_in)
    pair = (send, recv)
    trade = Exchange((near_out, near_in, far_out, far_in), pair, 0, sibling, partner)
    share = Share(grad_attn, pair, 2, sibling, mine, chunk)

    def ffn_partial(start, k):
        rows = rows_at(start, k, SPAN * chunk)
        pre = dot_nn(normed_two[rows, :], w_in[...])
        after[rows, :] = gelu_of(pre).astype(BF16)
        low = (dot_nn(branch[rows, :], w_red[...]) * gelu_slope(pre)).astype(BF16)
        grad_before[rows, :] = low
        return dot_nt(low, w_in[...])

    for k in range(CHUNKS // SPAN):
        trade.give_span(k, ffn_partial(other, k))
        trade.pass_on_span(k, ffn_partial(mine, k))
    turned[...] = jnp.transpose(branch[...])
    weight_grad(turned, after, d_red)
    turned[...] = jnp.transpose(normed_two[...])
    weight_grad(turned, grad_before, d_in)
    at_made(carry)
    fetch = pltpu.make_async_copy(normed, after, loaded)
    fetch.start()
    carry.fetched()
    total = jnp.zeros((1, width), F32)
    for j in range(CHUNKS):
        rows = rows_at(0, j, chunk)
        back, part = norm_back(trade.take(j), middle[rows, :], gains[2 * layer + 1 : 2 * layer + 2, :])
        total = total + part
        back = back + grad[rows, :]
        grad_middle[rows, :] = back
        share.put(j, back.astype(BF16))
        here = rows_at(mine, j, chunk)
        grad_mixed[here, :] = dot_nn(grad_attn[here, :], w_out[...]).astype(BF16)
    gain_two[...] = total
    for j in range(CHUNKS):
        share.arrived(j)
        here = rows_at(other, j, chunk)
        grad_mixed[here, :] = dot_nn(grad_attn[here, :], w_out[...]).astype(BF16)
    trade.close()
    share.close()
    at_summed(carry)

    block = bias.shape[1]
    heads = grad_mixed.shape[1] // HD
    keys_t[...] = jnp.transpose(projected[1])
    grad_keys[...] = jnp.zeros(grad_keys.shape, F32)
    grad_values[...] = jnp.zeros(grad_values.shape, F32)

    def queries(i, _):
        rows = rows_at(0, i, block)
        bias[...] = jnp.where(key_seg[...] == query_seg[:, rows], 0.0, -1e30)
        asked = projected[0, rows, :] * HD ** (-0.5)
        given = grad_mixed[rows, :]
        parts = []
        for head in range(heads):
            query = head_lanes(asked, head, HD)
            wanted = head_lanes(given, head, HD)
            scores = dot_nt(projected[1], query) + bias[...]
            probs = jnp.exp(scores - log_sums[head : head + 1, rows])
            grad_probs = dot_nt(projected[2], wanted)
            centre = jnp.sum(probs * grad_probs, axis=0, keepdims=True)
            grad_scores = (probs * (grad_probs - centre)).astype(BF16)
            parts.append(dot_nn(keys_t[head * HD : (head + 1) * HD, :], grad_scores))
            grad_keys[...] += dot_nn(grad_scores, query)
            grad_values[...] += dot_nn(probs.astype(BF16), wanted)
        grad_projected[0, rows, :] = (jnp.transpose(jnp.concatenate(parts, axis=0)) * HD ** (-0.5)).astype(BF16)
        return 0

    lax.fori_loop(0, seq_len // block, queries, 0)
    grad_projected[1] = grad_keys[...].astype(BF16)
    grad_projected[2] = grad_values[...].astype(BF16)
    at_attended(carry)

    trade = Exchange((near_out, near_in, far_out2, far_in2), pair, 3, sibling, partner)
    share = Share(branch_out, pair, 5, sibling, mine, chunk)

    def query_partial(start, k):
        rows = rows_at(start, k, SPAN * chunk)
        found = None
        for which in range(3):
            part = dot_nt(grad_projected[which, rows, :], w_query[which])
            found = part if found is None else found + part
        return found

    for k in range(CHUNKS // SPAN):
        trade.give_span(k, query_partial(other, k))
        trade.pass_on_span(k, query_partial(mine, k))
    turned[...] = jnp.transpose(grad_attn[...])
    weight_grad(turned, mixed, d_out)
    fetch.wait()
    turned[...] = jnp.transpose(after[...])
    for which in range(3):
        weight_grad(turned, grad_projected.at[which], d_query.at[which])
    at_sent(carry, d_out, d_query)
    total = jnp.zeros((1, width), F32)
    for j in range(CHUNKS):
        rows = rows_at(0, j, chunk)
        back, part = norm_back(trade.take(j), resid[rows, :], gains[2 * layer : 2 * layer + 1, :])
        total = total + part
        back = back + grad_middle[rows, :]
        grad_out[rows, :] = back
        share.put(j, (back if scale is None else scale * back).astype(BF16))
    gain_one[...] = total
    for j in range(CHUNKS):
        share.arrived(j)
    trade.close()
    share.close()
    if peers is None:
        carry.end(*carry.all())


def backward_scratch(seq_len, width, hidden, heads_width, owners):
    half, chunk = seq_len // 2, seq_len // 2 // CHUNKS
    block = min(QUERY_BLOCK, seq_len)
    far = pltpu.VMEM((CHUNKS, chunk, width), BACKWARD_KIND)
    return (
        [pltpu.VMEM((owners, width // owners, hidden), BF16)] * 2
        + [
            pltpu.VMEM((half, width), F32),
            pltpu.VMEM((seq_len, width), BF16),
            pltpu.VMEM((seq_len, heads_width), BF16),
            pltpu.VMEM((3, seq_len, heads_width), BF16),
            pltpu.VMEM((seq_len, hidden), BF16),
            pltpu.VMEM((seq_len, width), BF16),
            pltpu.VMEM((width, seq_len), BF16),
            pltpu.VMEM((seq_len, block), F32),
            pltpu.VMEM((heads_width, seq_len), BF16),
            pltpu.VMEM((seq_len, heads_width), F32),
            pltpu.VMEM((seq_len, heads_width), F32),
        ]
        + Exchange.scratch(chunk, width, BACKWARD_KIND)
        + [far, far]
        + sems(6)
        + [pltpu.SemaphoreType.DMA]
    )


def backward_outs(seq_len, width, heads_width, owners):
    return [
        jax.ShapeDtypeStruct((seq_len // 2, width), F32),
        jax.ShapeDtypeStruct((seq_len, width), BF16),
        jax.ShapeDtypeStruct((owners, width // owners, heads_width), BF16),
        jax.ShapeDtypeStruct((3, owners, width // owners, heads_width), BF16),
        jax.ShapeDtypeStruct((1, width), F32),
        jax.ShapeDtypeStruct((1, width), F32),
    ]


AWAY, LAZY = (15,), (0, 4, 6, 8, 9, 11, 13, 14)


def backward_block(layer, points, operands, owners, collective_id, loads):
    seq_len, width = operands[5].shape
    hidden, heads_width = operands[3].shape[1], operands[13].shape[2]
    return run(
        functools.partial(backward_kernel, layer, None, points),
        "backward_block",
        operands,
        backward_outs(seq_len, width, heads_width, owners),
        backward_scratch(seq_len, width, hidden, heads_width, owners),
        collective_id,
        loads,
        away=AWAY,
        lazy=LAZY,
    )


def to_rows(columns):
    lanes = lax.broadcasted_iota(jnp.int32, (LANES, LANES), 1)
    total = jnp.zeros((LANES, LANES), F32)
    for k, column in enumerate(columns):
        total = jnp.where(lanes == k, column, total)
    return jnp.transpose(total)[:8, :]


def loss_part(
    row, normed, info, value, gain, table_loads, grad_out, branch, d_gain, losses, d_tables,
    logits, grads, places, turned, stat_out, stat_in, sum_out, sum_in,
    stat_send, stat_recv, sum_send, sum_recv, near_out, near_in, far_out, far_in, send, recv, made,
):
    seq_len, width = normed.shape
    chunk = seq_len // 2 // CHUNKS
    piece_width = table_loads[0].out.shape[-1]
    vocab = piece_width * len(table_loads)
    tiles = vocab // LANES
    blocks = seq_len // LANES
    me = lax.axis_index(NARROW)
    sibling, partner, mine, other = group_places(seq_len)
    peers = [{NARROW: lax.rem(me + k, 4)} for k in range(1, 4)]
    sems = (send, recv)
    trade = Exchange((near_out, near_in, far_out, far_in), sems, 0, sibling, partner)
    share = Share(branch, sems, 2, sibling, mine, chunk)
    first = (me * vocab).astype(F32)
    whole = 4.0 * vocab
    lanes = lax.broadcasted_iota(jnp.int32, (LANES, LANES), 1).astype(F32)

    def stat_copy(b, k):
        return remote(stat_out.at[b], stat_in.at[k, b], stat_send.at[k, b], stat_recv.at[k, b], peers[k])

    def sum_copy(b, k):
        return remote(sum_out.at[b], sum_in.at[k, b], sum_send.at[k, b], sum_recv.at[k, b], peers[k])

    def tile_at(t):
        return pl.ds(pl.multiple_of(t * LANES, LANES), LANES)

    def ask(b, _):
        rows = rows_at(0, b, LANES)
        here = info[:, rows]
        at_noised = spread(here[0:1] - first)
        at_clean = spread(here[1:2] - first)
        places[b, 0] = at_noised
        places[b, 1] = at_clean

        tops, sums = [], [[], [], []]
        for k in range(LANES // SUB):
            part = pl.ds(pl.multiple_of(b * LANES + k * SUB, SUB), SUB)
            subset = slice(k * SUB, (k + 1) * SUB)

            def top_step(t, top):
                return jnp.maximum(top, logits[part, tile_at(t)])

            top = lax.fori_loop(1, tiles, top_step, logits[part, tile_at(0)], unroll=5)
            top = jnp.max(top, axis=1, keepdims=True)
            top_wide = jnp.broadcast_to(top, (SUB, LANES))
            noised_at, clean_at = at_noised[subset], at_clean[subset]

            def sum_step(t, totals):
                powers, noised, clean = totals
                piece = logits[part, tile_at(t)]
                column = lanes[subset] + (t * LANES).astype(F32)
                return (
                    powers + jnp.exp(piece - top_wide),
                    noised + jnp.where(column == noised_at, piece, 0.0),
                    clean + jnp.where(column == clean_at, piece, 0.0),
                )

            zero = jnp.zeros((SUB, LANES), F32)
            totals = lax.fori_loop(0, tiles, sum_step, (zero, zero, zero), unroll=4)
            tops.append(top)
            for found, total in zip(sums, totals):
                found.append(jnp.sum(total, axis=1, keepdims=True))
        stat_out[b] = to_rows([jnp.concatenate(found, axis=0) for found in [tops] + sums])
        for k in range(3):
            stat_copy(b, k).start()
        return 0

    for k, table in enumerate(table_loads):
        if k == len(table_loads) - 1:
            table.finish()

        def product(i, _):
            rows = rows_at(0, i, TILE)
            logits[rows, k * piece_width : (k + 1) * piece_width] = dot_nn(normed[rows, :], table.value())
            return 0

        lax.fori_loop(0, seq_len // TILE, product, 0)
    lax.fori_loop(0, blocks, ask, 0)

    def scalars(b):
        here = info[:, rows_at(0, b, LANES)]
        step = jnp.maximum(here[2:3], 2.0)
        left = STEPS - step + 1.0
        beta = 1.0 / left
        keep = left / STEPS
        rest = (step - 1.0) / (STEPS * whole)
        own = stat_out[b]
        others = [stat_in[k, b] for k in range(3)]
        top = own[0:1]
        for stat in others:
            top = jnp.maximum(top, stat[0:1])
        total = own[1:2] * jnp.exp(own[0:1] - top)
        noised, clean = own[2:3], own[3:4]
        for stat in others:
            total = total + stat[1:2] * jnp.exp(stat[0:1] - top)
            noised, clean = noised + stat[2:3], clean + stat[3:4]
        return here, beta, keep, rest, top + jnp.log(total), noised, clean

    def measure(b, _):
        rows = rows_at(0, b, LANES)
        for k in range(3):
            stat_copy(b, k).wait_recv()
        _, _, keep, rest, log_total, _, _ = scalars(b)
        log_wide = spread(log_total)
        ratio = spread(keep / rest)

        sums = [[], []]
        for k in range(LANES // SUB):
            part = pl.ds(pl.multiple_of(b * LANES + k * SUB, SUB), SUB)
            log_part, ratio_part = log_wide[k * SUB : (k + 1) * SUB], ratio[k * SUB : (k + 1) * SUB]

            def step(t, totals):
                logs, shares = totals
                probs = jnp.exp(logits[part, tile_at(t)] - log_part)
                logits[part, tile_at(t)] = probs
                grown = 1.0 + probs * ratio_part
                return (logs + jnp.log(grown), shares + probs / grown)

            zero = jnp.zeros((SUB, LANES), F32)
            totals = lax.fori_loop(0, tiles, step, (zero, zero), unroll=4)
            for found, total in zip(sums, totals):
                found.append(jnp.sum(total, axis=1, keepdims=True))
        sum_out[b] = to_rows([jnp.concatenate(found, axis=0) for found in sums])
        for k in range(3):
            sum_copy(b, k).start()
        return 0

    lax.fori_loop(0, blocks, measure, 0)

    def pull(b):
        rows = rows_at(0, b, LANES)
        for k in range(3):
            sum_copy(b, k).wait_recv()
        here, beta, keep, rest, log_total, noised, clean = scalars(b)
        sums = sum_out[b] + sum_in[0, b] + sum_in[1, b] + sum_in[2, b]
        log_sum, share_sum = sums[0:1], sums[1:2] / rest
        same = here[0:1] == here[1:2]
        first_step = here[2:3] == 1.0
        base_a, more_a = beta / whole, 1.0 - beta
        base_w = base_a * rest
        joint = whole * base_w + more_a * rest + base_a * keep + jnp.where(same, more_a * keep, 0.0)
        ratio = keep / rest
        prob_n, prob_c = jnp.exp(noised - log_total), jnp.exp(clean - log_total)
        grown_n, grown_c = 1.0 + prob_n * ratio, 1.0 + prob_c * ratio
        marginal_n, marginal_c = rest * grown_n, rest * grown_c
        log_n, log_c = jnp.log(grown_n), jnp.log(grown_c)
        weight_n = jnp.where(same, 0.0, more_a * rest)
        weight_c = jnp.where(same, more_a * rest + base_a * keep + more_a * keep, base_a * keep)
        lift = jnp.log((keep + rest) / rest)
        cross = -base_w * log_sum - weight_n * log_n - weight_c * log_c + (base_w + weight_c) * lift
        model = base_a * (keep + whole * rest) + more_a * marginal_n
        divergence = cross / joint - jnp.log(joint) + jnp.log(model)
        loss = jnp.where(first_step, log_total - clean, divergence)
        losses[:, rows] = here[4:5] * loss
        weighted = base_w * share_sum + weight_n * prob_n / marginal_n + weight_c * prob_c / marginal_c
        aligned = base_a + more_a * prob_n
        centre = keep * (aligned / model - weighted / joint)
        scale = here[3:4]
        zero = jnp.zeros_like(scale)
        even = scale * jnp.where(first_step, 1.0, keep * base_a / model - centre)
        bent = scale * jnp.where(first_step, zero, -keep * base_w / joint / rest)
        at_n = prob_n * keep * (more_a / model - weight_n / joint / marginal_n)
        at_c = -prob_c * keep * (weight_c / joint / marginal_c)
        extra_n = spread(scale * jnp.where(first_step, zero, at_n))
        extra_c = spread(scale * jnp.where(first_step, -1.0, at_c))
        even, bent, ratio = spread(even), spread(bent), spread(ratio)
        at_noised, at_clean = places[b, 0], places[b, 1]

        for k in range(LANES // SUB):
            part = pl.ds(pl.multiple_of(b * LANES + k * SUB, SUB), SUB)
            subset = slice(k * SUB, (k + 1) * SUB)
            even_at, bent_at, ratio_at = even[subset], bent[subset], ratio[subset]
            n_at, c_at, noised_at, clean_at = extra_n[subset], extra_c[subset], at_noised[subset], at_clean[subset]

            def step(t, _):
                probs = logits[part, tile_at(t)]
                column = lanes[subset] + (t * LANES).astype(F32)
                grad = probs * (even_at + bent_at / (1.0 + probs * ratio_at))
                grad = grad + jnp.where(column == noised_at, n_at, 0.0)
                grad = grad + jnp.where(column == clean_at, c_at, 0.0)
                grads[part, tile_at(t)] = grad.astype(BF16)
                return 0

            lax.fori_loop(0, tiles, step, 0, unroll=4)

    def partial(start, k):
        span = SPAN * chunk
        base = start // LANES + k * (span // LANES)
        for b in range(span // LANES):
            pull(base + b)
        total = None
        for k_table, table in enumerate(table_loads):
            part = dot_nt(
                grads[rows_at(start, k, span), k_table * piece_width : (k_table + 1) * piece_width], table.value()
            )
            total = part if total is None else total + part
        return total

    for k in range(CHUNKS // SPAN):
        trade.give_span(k, partial(other, k))
        trade.pass_on_span(k, partial(mine, k))
    turned[...] = jnp.transpose(normed[...])
    for k, d_table in enumerate(d_tables):
        weight_grad(turned, grads.at[:, k * piece_width : (k + 1) * piece_width], d_table)
    made()
    gain_total = jnp.zeros((1, gain.shape[1]), F32)
    for j in range(CHUNKS):
        rows = rows_at(0, j, chunk)
        back, gain_part = norm_back(trade.take(j), value[rows, :], gain[row : row + 1, :])
        gain_total = gain_total + gain_part
        grad_out[rows, :] = back
        share.put(j, back.astype(BF16))
    d_gain[...] = gain_total
    for j in range(CHUNKS):
        share.arrived(j)
    trade.close()
    share.close()

    def finish(b, _):
        for k in range(3):
            stat_copy(b, k).wait_send()
            sum_copy(b, k).wait_send()
        return 0

    lax.fori_loop(0, blocks, finish, 0)


def back_kernel(
    layer, normed, key_seg, query_seg, resid, w_query, w_out, w_in, gains, noised, clean, steps, counted, counts,
    projected, mixed, middle, normed_two, log_sums, grad_out, branch, d_gain, losses, *refs, carry,
):
    pieces = len(carry.loads) - 1
    d_tables, refs = refs[:pieces], refs[pieces:]
    (result, normed_next, info), refs = refs[:3], refs[3:]
    loss_scratch, layer_refs = refs[:-LAYER_SCRATCH], refs[-LAYER_SCRATCH:]
    me = lax.axis_index(NARROW)
    carry.fetch()
    info[...] = jnp.zeros(info.shape, F32)
    mask = counted[...].astype(F32)
    for row, value in enumerate((noised[...], clean[...], steps[...])):
        info[row : row + 1, :] = value.astype(F32)
    info[3:4, :] = mask / counts[COUNT_ROW : COUNT_ROW + 1, 0:1]
    info[4:5, :] = mask
    greet([{NARROW: lax.rem(me + k, 4)} for k in range(1, 4)] + carry.peers())
    carry.begin(0, 1, 2)

    def at_half():
        carry.begin(3)

    def at_feed():
        carry.fetched()
        carry.end(0)
        carry.hand_on(1, 2)
        carry.begin(4)

    def at_sent():
        carry.leave(0, 1, 2, 3)
        carry.hand_on(3)

    def at_last():
        carry.hand_on(4)

    forward_part(
        layer,
        [lambda which: w_query[which], lambda: w_out[...], lambda: w_in[...], carry.loads[0].value],
        (at_half, at_feed, at_sent, at_last),
        normed, key_seg, query_seg, resid, gains,
        projected, mixed, middle, normed_two, log_sums, result, normed_next, *layer_refs,
    )
    carry.end(1, 2, 3)
    loss_part(
        2 * layer + 2, normed_next, info, result, gains, carry.loads[1:], grad_out, branch, d_gain, losses, d_tables,
        *loss_scratch, *layer_refs[2:6], *layer_refs[-2:], made=lambda: carry.leave(*range(9, 9 + pieces)),
    )
    carry.gone()


def last_and_loss(
    layer, normed, key_seg, query_seg, resid, w_query, w_out, w_in, gains, tokens, counts, vocab, collective_id, loads
):
    seq_len, width = normed.shape
    heads_width = w_query.shape[2]
    half, blocks = seq_len // 2, seq_len // LANES
    pieces = len(loads) - 1
    return run(
        functools.partial(back_kernel, layer),
        "last_and_loss",
        [normed, key_seg, query_seg, resid, w_query, w_out, w_in, gains, *tokens, counts],
        layer_outs(seq_len, width, heads_width)
        + [
            jax.ShapeDtypeStruct((half, width), F32),
            jax.ShapeDtypeStruct((seq_len, width), BF16),
            jax.ShapeDtypeStruct((1, width), F32),
            jax.ShapeDtypeStruct((1, seq_len), F32),
        ]
        + [jax.ShapeDtypeStruct((width, vocab // pieces), BF16)] * pieces,
        [
            pltpu.VMEM((half, width), F32),
            pltpu.VMEM((seq_len, width), BF16),
            pltpu.VMEM((8, seq_len), F32),
            pltpu.VMEM((seq_len, vocab), F32),
            pltpu.VMEM((seq_len, vocab), BF16),
            pltpu.VMEM((blocks, 2, LANES, LANES), F32),
            pltpu.VMEM((width, seq_len), BF16),
            pltpu.VMEM((blocks, 8, LANES), F32),
            pltpu.VMEM((3, blocks, 8, LANES), F32),
            pltpu.VMEM((blocks, 8, LANES), F32),
            pltpu.VMEM((3, blocks, 8, LANES), F32),
        ]
        + [pltpu.SemaphoreType.DMA((3, blocks))] * 4
        + layer_scratch(seq_len, width, heads_width),
        collective_id,
        loads,
        lazy=(3, 6),
        early=(0, 1, 2, 3) + tuple(range(9, 9 + pieces)),
    )


TAIL_SCRATCH = 22


def end_kernel(points, scale, gain_count, *refs, carry):
    operands, refs = refs[:16], refs[16:]
    (ids_all, losses), refs = refs[:2], refs[2:]
    gain_parts, refs = refs[:gain_count], refs[gain_count:]
    count = len(refs) - 3 - 6 - BACK_SCRATCH - TAIL_SCRATCH
    squares, refs = refs[:count], refs[count:]
    (d_table, d_small, scalars), refs = refs[:3], refs[3:]
    made, refs = refs[:6], refs[6:]
    back_refs, tail_refs = refs[:BACK_SCRATCH], refs[BACK_SCRATCH:]
    me, owners, place = lax.axis_index(WIDE), ids_all.shape[0], lax.axis_index(NARROW)
    peers = [{WIDE: lax.rem(me + step, owners)} for step in range(1, owners)]
    peers += [{NARROW: lax.rem(place + step, 4)} for step in range(1, 4)]
    backward_kernel(0, scale, points, *operands, *made, *back_refs, carry, peers=peers)
    tail_body(
        made[1], ids_all, losses, (made[5], made[4], *gain_parts), squares, d_table, d_small, scalars, *tail_refs, carry
    )


BACK_SCRATCH = 22


def tail_body(
    branch, ids_all, losses, gain_parts, squares,
    d_table, d_small, scalars,
    out_blocks, all_in, masked, picks, total, gains_out, gains_in, blocks, block_in, line_out, line_in,
    near, along,
    wide_send, wide_recv, far_send, far_recv, near_send, near_recv, all_send, all_recv,
    sum_sems,
    carry,
):
    seq_len, width = branch.shape
    quarter, half = seq_len // 4, seq_len // 2
    owners = ids_all.shape[0]
    share, vocab = d_table.shape
    sibling, partner, mine, other = group_places(seq_len)
    place = lax.axis_index(NARROW)
    side = lax.div(place, 2)
    me, slow, fast, slows = wide_places(owners)
    beside = {WIDE: me + 1 - 2 * fast}
    group = near.shape[0]
    first = place * vocab
    around = [lax.rem(me + step, owners) for step in range(owners)]
    at_quarter = pl.multiple_of(mine + side * quarter, quarter)
    held = 2 * lax.rem(place, 2) + side

    def along_way(step):
        return {WIDE: 2 * lax.rem(slow + step, slows) + fast}

    def wide_copy(step):
        return remote(
            out_blocks.at[around[step]], all_in.at[me, held],
            wide_send.at[step], wide_recv.at[step], {WIDE: around[step]},
        )

    def far_copy(step):
        rows = all_in.at[around[step], held]
        return remote(rows, rows, far_send.at[step], far_recv.at[step], partner)

    def near_copy(step):
        rows = all_in.at[around[step], pl.ds(2 * lax.rem(place, 2), 2)]
        return remote(rows, rows, near_send.at[step], near_recv.at[step], sibling)

    def gain_near():
        return remote(gains_out, gains_in, sum_sems.at[0, 0], sum_sems.at[1, 0], sibling)

    def gain_pair(step):
        return remote(
            blocks.at[2 * lax.rem(slow + step, slows) + 1 - fast], block_in.at[step],
            sum_sems.at[2, step], sum_sems.at[3, step], beside,
        )

    def gain_line(step):
        return remote(line_out.at[step], line_in.at[step], sum_sems.at[4, step], sum_sems.at[5, step], along_way(step))

    near_ways = [{NARROW: lax.rem(place + step, group)} for step in range(1, group)]
    gains_out[...] = jnp.zeros(gains_out.shape, F32)
    for row, part in enumerate(gain_parts):
        gains_out[row : row + 1, :] = part[...]
    gain_near().start()
    out_blocks[...] = jnp.transpose(branch[pl.ds(at_quarter, quarter), :]).reshape(out_blocks.shape)
    for step in range(1, owners):
        wide_copy(step).start()
    all_in[me, held] = out_blocks[me]
    carry.hand_on(6, 7)
    gain_near().wait_recv()
    both = gains_out[...] + gains_in[...]
    for owner in range(owners):
        blocks[owner] = lax.dot_general(
            both, feature_places(owner, width, share).astype(F32), (((1,), (1,)), ((), ())),
            precision=lax.Precision.HIGHEST, preferred_element_type=F32,
        )
    for step in range(slows):
        gain_pair(step).start()

    def hand_on(step):
        if step:
            wide_copy(owners - step).wait_recv()
        far_copy(step).start()

    def hand_over(step):
        far_copy(step).wait_recv()
        near_copy(step).start()

    def gather_grad(step, first_turn):
        near_copy(step).wait_recv()
        row = around[step]

        for k in range(seq_len // quarter):
            columns = slice(k * quarter, (k + 1) * quarter)
            high, found = token_parts(ids_all[row, k : k + 1, :], first)
            picks[:, columns] = found
            grads = all_in[row, k]
            for part in range(vocab // LANES):
                inside = jnp.where(high == part, 1.0, 0.0).astype(BF16)
                masked[part * share : (part + 1) * share, columns] = grads * inside
        span = 8 * share

        def some(i, _):
            rows = rows_at(0, i, span)
            part = dot_nt(masked[rows, :], picks[...])
            total[rows, :] = part if first_turn else total[rows, :] + part
            return 0

        lax.fori_loop(0, total.shape[0] // span, some, 0)

    order = [0] + list(range(1, owners))
    for turn in range(owners + 2):
        if turn < owners:
            hand_on(order[turn])
        if 1 <= turn < owners + 1:
            hand_over(order[turn - 1])
        if turn == 1:
            for step in list(range(1, slows)) + [0]:
                gain_pair(step).wait_recv()
                line_out[step] = blocks[2 * lax.rem(slow + step, slows) + fast] + block_in[step]
                if step:
                    gain_line(step).start()
        if turn >= 2:
            gather_grad(order[turn - 2], turn == 2)
    for t in range(vocab // LANES):
        d_table[:, t * LANES : (t + 1) * LANES] = total[t * share : (t + 1) * share, :]
    small = line_out[0]
    for step in range(1, slows):
        gain_line(step).wait_recv()
        small = small + line_in[step]
    d_small[...] = small
    carry.end(*carry.all())
    square = jnp.sum(d_table[...] * d_table[...])
    for part in squares:
        square = square + part[0, 0]
    for load in carry.loads:
        square = square + load.squares[0, 0]
    lead = (place == 0).astype(F32)
    square = square + lead * jnp.sum(small * small)
    lanes = lax.broadcasted_iota(jnp.int32, (8, LANES), 1)
    given = jnp.where(lanes == 0, square, jnp.where(lanes == 1, lead * jnp.sum(losses[...]), 0.0))

    def scalar_near(step):
        return remote(near.at[place], near.at[place], sum_sems.at[6, step], sum_sems.at[7, step], near_ways[step - 1])

    def scalar_wide(step):
        return remote(along.at[me], along.at[me], all_send.at[step], all_recv.at[step], {WIDE: around[step]})

    near[place] = given
    for step in range(1, group):
        scalar_near(step).start()
    for step in range(1, group):
        scalar_near(step).wait()
    along[me] = jnp.sum(near[...], axis=0)
    for step in range(1, owners):
        scalar_wide(step).start()
    for step in range(1, owners):
        scalar_wide(step).wait()
    scalars[...] = jnp.sum(along[...], axis=0)
    gain_near().wait_send()
    for step in range(owners):
        far_copy(step).wait_send()
        near_copy(step).wait_send()
        if step:
            wide_copy(step).wait_send()
    for step in range(slows):
        gain_pair(step).wait_send()
        if step:
            gain_line(step).wait_send()


def first_and_tail(
    points, scale, operands, ids_all, losses, gain_parts, squares, share, vocab, group, collective_id, loads
):
    seq_len, width = operands[5].shape
    hidden, heads_width = operands[3].shape[1], operands[13].shape[2]
    owners = ids_all.shape[0]
    slows = owners // 2
    dma = pltpu.SemaphoreType.DMA
    small = (8, LANES)
    made = [pltpu.VMEM(out.shape, out.dtype) for out in backward_outs(seq_len, width, heads_width, owners)]
    tail_scratch = [
        pltpu.VMEM((owners, share, seq_len // 4), BF16),
        pltpu.VMEM((owners, 4, share, seq_len // 4), BF16),
        pltpu.VMEM((vocab // LANES * share, seq_len), BF16),
        pltpu.VMEM((LANES, seq_len), BF16),
        pltpu.VMEM((vocab // LANES * share, LANES), F32),
        pltpu.VMEM((8, width), F32),
        pltpu.VMEM((8, width), F32),
        pltpu.VMEM((owners,) + small, F32),
        pltpu.VMEM((slows,) + small, F32),
        pltpu.VMEM((slows,) + small, F32),
        pltpu.VMEM((slows,) + small, F32),
        pltpu.VMEM((group,) + small, F32),
        pltpu.VMEM((owners,) + small, F32),
    ]
    tail_scratch += [dma((owners,))] * 8 + [dma((12, max(slows, group)))]
    back = backward_scratch(seq_len, width, hidden, heads_width, owners)
    assert len(back) == BACK_SCRATCH and len(tail_scratch) == TAIL_SCRATCH
    return run(
        functools.partial(end_kernel, points, scale, len(gain_parts)),
        "first_and_tail",
        [*operands, ids_all, losses, *gain_parts, *squares],
        [
            jax.ShapeDtypeStruct((share, vocab), F32),
            jax.ShapeDtypeStruct(small, F32),
            jax.ShapeDtypeStruct(small, F32),
        ],
        made + back + tail_scratch,
        collective_id,
        loads,
        away=AWAY,
        lazy=LAZY,
    )


PIECES = 4
TABLE, ATTN_IN, ATTN_OUT, FFN_IN, FFN_OUT = range(5)


def shares_tile(wide, narrow, noised, attn_out, ffn_in, tables):
    rows, seq_len = noised.shape
    return (
        attn_out.shape[0] == 2
        and narrow == 4
        and wide % 2 == 0
        and rows == 1
        and seq_len % (2 * CHUNKS * 16) == 0
        and SPAN * seq_len == 2 * CHUNKS * QUERY_BLOCK
        and tables.shape[1] * wide % 256 == 0
        and attn_out.shape[1] % 16 == 0
        and attn_out.shape[1] <= LANES
        and ffn_in.shape[2] % 128 == 0
        and tables.shape[1] == attn_out.shape[1]
        and tables.shape[2] % (PIECES * TILE) == 0
    )


def per_device(wide, narrow, *arrays):
    noised, attn_out, ffn_in, tables = arrays[0], arrays[6], arrays[7], arrays[9]
    if shares_tile(wide, narrow, noised, attn_out, ffn_in, tables):
        return tiled_device(wide, *arrays)
    return general_device(*arrays)


def tiled_device(
    wide,
    noised,
    clean,
    timesteps,
    segments,
    counted,
    attn_in,
    attn_out,
    ffn_in,
    ffn_out,
    tables,
    gains,
    attn_in_mean,
    attn_out_mean,
    ffn_in_mean,
    ffn_out_mean,
    tables_mean,
    gains_mean,
    attn_in_square,
    attn_out_square,
    ffn_in_square,
    ffn_out_square,
    tables_square,
    gains_square,
):
    layers = attn_in.shape[0]
    gain_rows, gain_cols = gains.shape
    share, vocab = tables.shape[1:]
    leads = (1, 0, 0, 0)
    four = (attn_in, attn_out, ffn_in, ffn_out)

    def joined(value, lead):
        return value.reshape(value.shape[:lead] + (-1,) + value.shape[lead + 2 :])

    ids = noised.reshape(4, -1)
    steps = timesteps.reshape(-1, LANES)
    half_width = D // 2
    rates = jnp.exp(-math.log(10000.0) * jnp.arange(half_width, dtype=F32) / half_width)[None, :]
    quarter = vocab // PIECES
    windows = [(k * quarter, quarter) for k in range(PIECES)]
    key_seg, query_seg = segments.reshape(-1, 1), segments.reshape(1, -1)
    weights = (attn_in, attn_out, ffn_in, ffn_out)
    (residual, normed, gain_w, counts, ids_all, projected, mixed, middle, normed_two, log_sums, result, normed_next), carried = front(
        ids, counted, gains, steps, rates, tables, key_seg, query_seg, wide, attn_out.shape[2], 0,
        [GatherLoad(value, 0, lead, wide, place=KEPT) for value, lead in zip(weights, leads)]
        + [GatherLoad(value, 1, lead, wide) for value, lead in zip(weights[:3], leads)]
        + [SlowLoad(ffn_out, 1, 0, wide)],
    )
    token_total = counts[gain_rows, 0]
    first_w = [joined(value, lead) for value, lead in zip(carried[:4], leads)]
    query_w, output_w, expand_w = [joined(value, lead) for value, lead in zip(carried[4:7], leads)]
    kept = [(residual, normed, projected, mixed, middle, normed_two, log_sums, *first_w)]
    (projected, mixed, middle, normed_two, log_sums, grad, branch, gain_final, losses, *d_last), (reduce_w,) = last_and_loss(
        1, normed_next, key_seg, query_seg, result, query_w, output_w, expand_w, gain_w,
        (noised, clean, timesteps, counted), counts, vocab, 1,
        [FastLoad(carried[7], 0, wide)]
        + [GatherLoad(tables, 1, 0, wide, window, place=LOCAL) for window in windows],
    )
    kept.append(
        (result, normed_next, projected, mixed, middle, normed_two, log_sums)
        + (query_w, output_w, expand_w, joined(reduce_w, 0))
    )
    own, squares = {}, []

    def by_owner(value, lead):
        shape = value.shape
        return value.reshape(shape[:lead] + (wide, shape[lead] // wide) + shape[lead + 1 :])

    def landed(key, results):
        own[key] = results[0]
        squares.append(results[1])
        return results[2:]

    hidden = ffn_in.shape[2]
    made = jax.ShapeDtypeStruct((wide, share, hidden), BF16)
    made_in = jax.ShapeDtypeStruct((3, wide, share, attn_in.shape[3]), BF16)
    made_out = jax.ShapeDtypeStruct((wide, share, attn_out.shape[2]), BF16)

    def start_last(carry, d_red, d_in):
        carry.loads[PIECES].full, carry.loads[PIECES + 1].full = d_red, d_in
        carry.begin(*range(PIECES))

    half_pieces = PIECES // 2
    points = (
        start_last,
        lambda carry: carry.begin(PIECES, PIECES + 1),
        lambda carry: carry.hand_on(*range(half_pieces)),
        lambda carry: carry.hand_on(*range(half_pieces, PIECES)),
        lambda carry, d_out, d_query: None,
    )
    residual, normed, projected, mixed, middle, normed_two, log_sums, *four_w = kept[1]
    query_w, output_w, expand_w, reduce_w = four_w
    (grad, branch, d_out, d_query, gain_two, gain_one), carried = backward_block(
        1, points,
        [grad, branch, reduce_w, expand_w, output_w, normed_two, middle, gain_w, mixed]
        + [projected, log_sums, key_seg, query_seg, query_w, residual, normed],
        wide, 2,
        [ReduceLoad(by_owner(piece, 0), 0) for piece in d_last]
        + [PairLoad(made, 0, True), PairLoad(made, 0, True)],
    )
    for k in range(PIECES):
        carried = landed((TABLE, k), carried)
    red_sums, in_sums = carried

    def start_first(carry, d_red, d_in):
        carry.loads[4].full, carry.loads[5].full = d_red, d_in
        carry.begin(0, 1, 2, 3)

    def sent_first(carry, d_out, d_query):
        carry.hand_on(5)
        carry.loads[6].full, carry.loads[7].full = d_out, d_query
        carry.begin(6, 7)

    points = (
        start_first,
        lambda carry: carry.begin(4, 5),
        lambda carry: carry.hand_on(2, 3),
        lambda carry: carry.hand_on(4),
        sent_first,
    )
    residual, normed, projected, mixed, middle, normed_two, log_sums, *four_w = kept[0]
    query_w, output_w, expand_w, reduce_w = four_w
    (own_first, total_small, scalars), carried = first_and_tail(
        points, math.sqrt(D),
        [grad, branch, reduce_w, expand_w, output_w, normed_two, middle, gain_w, mixed]
        + [projected, log_sums, key_seg, query_seg, query_w, residual, normed],
        ids_all, losses, (gain_one, gain_two, gain_final), squares, share, vocab, 4, 3,
        [LineLoad(red_sums, wide), LineLoad(in_sums, wide), ReduceLoad(d_out, 0), ReduceLoad(d_query, 1)]
        + [ReduceLoad(made, 0, True), ReduceLoad(made, 0, True), ReduceLoad(made_out, 0, True), ReduceLoad(made_in, 1, True)],
    )
    layer_keys = ((FFN_OUT, 1), (FFN_IN, 1), (ATTN_OUT, 1), (ATTN_IN, 1), (FFN_OUT, 0), (FFN_IN, 0), (ATTN_OUT, 0))
    for key in layer_keys + ((ATTN_IN, 0),):
        carried = landed(key, carried)
    grad_attn_in, grad_attn_out, grad_ffn_in, grad_ffn_out = [
        jnp.stack([own[name, index] for index in range(layers)]) for name in (ATTN_IN, ATTN_OUT, FFN_IN, FFN_OUT)
    ]
    grad_tables = jnp.stack([own_first, jnp.concatenate([own[TABLE, k] for k in range(PIECES)], axis=1)])
    grad_gains = total_small[:gain_rows, :gain_cols]
    total_square, loss_sum = scalars[0, 0], scalars[0, 1]
    grad_norm = jnp.sqrt(total_square)
    factor = jnp.minimum(1.0, CLIP_NORM / (grad_norm + 1e-06))
    results = [loss_sum, token_total, grad_norm]
    for weight, gradient, first, second, decay, rate in (
        (attn_in, grad_attn_in, attn_in_mean, attn_in_square, WEIGHT_DECAY, LEARN_RATE),
        (attn_out, grad_attn_out, attn_out_mean, attn_out_square, WEIGHT_DECAY, LEARN_RATE),
        (ffn_in, grad_ffn_in, ffn_in_mean, ffn_in_square, WEIGHT_DECAY, LEARN_RATE),
        (ffn_out, grad_ffn_out, ffn_out_mean, ffn_out_square, WEIGHT_DECAY, LEARN_RATE),
        (tables, grad_tables, tables_mean, tables_square, WEIGHT_DECAY, LEARN_RATE),
        (gains, grad_gains, gains_mean, gains_square, 0.0, GAIN_RATE),
    ):
        results += adam(weight, factor * gradient, first, second, decay, rate)
    return tuple(results)


def solution(mesh):
    wide, narrow = mesh.shape[WIDE], mesh.shape[NARROW]
    placed = (
        P(WIDE, None),
        P(WIDE, None),
        P(WIDE, None),
        P(WIDE, None),
        P(WIDE, None),
        P(None, None, WIDE, NARROW),
        P(None, WIDE, NARROW),
        P(None, WIDE, NARROW),
        P(None, WIDE, NARROW),
        P(None, WIDE, NARROW),
        P(None, WIDE),
        P(None, None, WIDE, NARROW),
        P(None, WIDE, NARROW),
        P(None, WIDE, NARROW),
        P(None, WIDE, NARROW),
        P(None, WIDE, NARROW),
        P(None, WIDE),
        P(None, None, WIDE, NARROW),
        P(None, WIDE, NARROW),
        P(None, WIDE, NARROW),
        P(None, WIDE, NARROW),
        P(None, WIDE, NARROW),
        P(None, WIDE),
    )
    return jax.shard_map(
        functools.partial(per_device, wide, narrow),
        mesh=mesh,
        in_specs=placed,
        out_specs=(
            P(),
            P(),
            P(),
            P(None, None, WIDE, NARROW),
            P(None, None, WIDE, NARROW),
            P(None, None, WIDE, NARROW),
            P(None, None, WIDE, NARROW),
            P(None, WIDE, NARROW),
            P(None, WIDE, NARROW),
            P(None, WIDE, NARROW),
            P(None, WIDE, NARROW),
            P(None, WIDE, NARROW),
            P(None, WIDE, NARROW),
            P(None, WIDE, NARROW),
            P(None, WIDE, NARROW),
            P(None, WIDE, NARROW),
            P(None, WIDE, NARROW),
            P(None, WIDE, NARROW),
            P(None, WIDE, NARROW),
            P(None, WIDE, NARROW),
            P(None, WIDE, NARROW),
            P(None, WIDE, NARROW),
            P(None, WIDE, NARROW),
            P(None, WIDE),
            P(None, WIDE),
            P(None, WIDE),
            P(None, WIDE),
        ),
        check_vma=False,
    )
```
